32 devices in a mesh: grp: 4 (over x, core), blk: 8 (over z, y).
Axes of the slice: x: 2, y: 2, z: 4, core: 2. Of those that a mesh axis runs over, the one named last changes fastest.
Arguments:
- tokens: bfloat16 [8, 1024, 1536], P('grp', 'blk'), may hold values from -6 to 6
- cotangent: bfloat16 [8, 1024, 1536], P('grp', 'blk'), may hold values from -6 to 6
- segment_ids: int32 [8, 1024], P('grp', 'blk'), may hold values from 0 to 7, as said below
- position_ids: int32 [8, 1024], P('grp', 'blk'), may hold values from 0 to 1023, as said below
- w_attend: float32 [1536, 2048], P('blk'), may hold values from -0.15625 to 0.15625
- w_out: float32 [1536, 1536], P('blk'), may hold values from -1.25 to 1.25
- w_gate: float32 [1536, 8960], P('blk'), may hold values from -0.15625 to 0.15625
- w_up: float32 [1536, 8960], P('blk'), may hold values from -0.15625 to 0.15625
- w_down: float32 [8960, 1536], P('blk'), may hold values from -0.0625 to 0.0625
- small_params: float32 [5120], P('blk'), may hold values from -2 to 4, as said below
- first_attend: float32 [1536, 2048], P('blk'), may hold values from -9.1552734e-05 to 9.1552734e-05
- first_out: float32 [1536, 1536], P('blk'), may hold values from -9.1552734e-05 to 9.1552734e-05
- first_gate: float32 [1536, 8960], P('blk'), may hold values from -9.1552734e-05 to 9.1552734e-05
- first_up: float32 [1536, 8960], P('blk'), may hold values from -9.1552734e-05 to 9.1552734e-05
- first_down: float32 [8960, 1536], P('blk'), may hold values from -9.1552734e-05 to 9.1552734e-05
- first_small: float32 [5120], P('blk'), may hold values from -0.00036621094 to 0.00036621094
- second_attend: float32 [1536, 2048], P('blk'), may hold values from 1.1325313e-09 to 4.4873882e-09
- second_out: float32 [1536, 1536], P('blk'), may hold values from 1.1325313e-09 to 4.4873882e-09
- second_gate: float32 [1536, 8960], P('blk'), may hold values from 1.1325313e-09 to 4.4873882e-09
- second_up: float32 [1536, 8960], P('blk'), may hold values from 1.1325313e-09 to 4.4873882e-09
- second_down: float32 [8960, 1536], P('blk'), may hold values from 1.1325313e-09 to 4.4873882e-09
- second_small: float32 [5120], P('blk'), may hold values from 1.7949553e-08 to 7.265295e-08
Outputs:
- out_tokens: bfloat16 [8, 1024, 1536], P('grp', 'blk')
- grad_tokens: bfloat16 [8, 1024, 1536], P('grp', 'blk')
- grad_norm: float32 [], replicated
- new_first_attend: float32 [1536, 2048], P('blk')
- new_second_attend: float32 [1536, 2048], P('blk')
- new_attend: float32 [1536, 2048], P('blk')
- new_first_out: float32 [1536, 1536], P('blk')
- new_second_out: float32 [1536, 1536], P('blk')
- new_out: float32 [1536, 1536], P('blk')
- new_first_gate: float32 [1536, 8960], P('blk')
- new_second_gate: float32 [1536, 8960], P('blk')
- new_gate: float32 [1536, 8960], P('blk')
- new_first_up: float32 [1536, 8960], P('blk')
- new_second_up: float32 [1536, 8960], P('blk')
- new_up: float32 [1536, 8960], P('blk')
- new_first_down: float32 [8960, 1536], P('blk')
- new_second_down: float32 [8960, 1536], P('blk')
- new_down: float32 [8960, 1536], P('blk')
- new_first_small: float32 [5120], P('blk')
- new_second_small: float32 [5120], P('blk')
- new_small: float32 [5120], P('blk')
The draws below stay inside these ranges and needn't reach their ends.
Inputs may be any that keep to these rules, and one draw needn't show every extreme that they name: `segment_ids`: within each row the ids start at 0 and never fall. Of each aligned group of 2 rows exactly one holds a single document; every other row holds exactly 8 documents. `position_ids`: each token's distance from the first token of its document (its run of equal segment ids) in its row. `small_params`: the gains (the first 3072 entries) are positive.
All inputs are finite; a program needn't handle non-finite values.
Results may differ from the reference program's by a relative error of at most 0.028.
Values may be sent and summed in bfloat16 or wider, within the bound.
No kernel may reach another device: no remote copies, remote signals or barrier semaphores. Data moves between devices by JAX's collectives and lax.ppermute only.
A program may use at most 512 MiB of HBM per device.

```python
import math
import jax
import jax.numpy as jnp
from jax import lax

D = 1536
FF = 8960
H = 12
KVH = 2
HD = 128
RG = 2
DOCS = 8
STEP = 10
HQD = 1536
KVD = 256
QKV = 2048
SMALL = 5120
NPARAM = 46797824
LEN = 1024
ROWS = 8
KB = 512


def document_layout(key):
    whole_key, cut_key = jax.random.split(key)
    group_count = ROWS // RG
    whole_pick = jax.random.randint(whole_key, (group_count,), 0, RG)
    row_number = jnp.arange(ROWS, dtype=jnp.int32)
    whole_row = row_number % RG == jnp.repeat(whole_pick, RG)

    def cuts_for(row_key):
        picked = jax.random.permutation(row_key, LEN - 1)[:DOCS - 1] + 1
        return jnp.sort(picked)
    cuts = jax.vmap(cuts_for)(jax.random.split(cut_key, ROWS))
    place = jnp.arange(LEN, dtype=jnp.int32)
    passed = cuts[:, None, :] <= place[None, :, None]
    segment = jnp.sum(passed.astype(jnp.int32), axis=2)
    begin = jnp.max(jnp.where(passed, cuts[:, None, :], 0), axis=2)
    segment = jnp.where(whole_row[:, None], 0, segment)
    begin = jnp.where(whole_row[:, None], 0, begin)
    return (segment.astype(jnp.int32), (place[None, :] - begin).astype(jnp.int32))


def draw_segment_ids(key, part):
    segment, begin_offset = document_layout(key)
    return segment


def draw_position_ids(key, part):
    segment, begin_offset = document_layout(key)
    return begin_offset


def draw_small_params(key, part):
    key = jax.random.fold_in(key, 7)
    gain_key, bias_key = jax.random.split(key)
    gain_keys = jax.random.split(gain_key, 2)
    rise = 3.0
    biases = 0.5 * jnp.clip(jax.random.normal(bias_key, (QKV,), jnp.float32), -4.0, 4.0)
    ramp = jnp.exp((jnp.arange(D, dtype=jnp.float32) / (D - 1) - 0.5) * jnp.log(rise))
    gain_one = ramp * jax.random.uniform(gain_keys[0], (D,), jnp.float32, 0.7, 1.4)
    gain_two = ramp * jax.random.uniform(gain_keys[1], (D,), jnp.float32, 0.7, 1.4)
    return jnp.concatenate([gain_one, gain_two, biases])


def steps_of(stream_key, extent, cuts, least, top_value):
    level, own = 1.0, jax.random.fold_in(stream_key, 6)
    for dim, shards_of in cuts:
        heights = jnp.exp(jax.random.uniform(jax.random.fold_in(own, dim), (shards_of,), jnp.float32, least / len(cuts), top_value / len(cuts)))
        level = level * jnp.repeat(heights, extent[dim] // shards_of).reshape([-1 if axis == dim else 1 for axis in range(len(extent))])
    return level


def gaussian(rng, dims, deviation, limit, shards=(), kind=jnp.bfloat16):
    entries = jax.random.normal(rng, dims, jnp.float32) * deviation
    if len(shards) > 0:
        entries = steps_of(rng, dims, shards, -0.22, 0.18) * entries
    return jnp.clip(entries, min=-limit, max=limit).astype(kind)


def setup_inputs(seed: int = 0) -> dict:
    arg_keys = jax.random.split(jax.random.key(seed), 23)
    return {
        "tokens": gaussian(arg_keys[0], (ROWS, LEN, D), 1.0, 6.0, ((0, 4), (1, 8))),
        "cotangent": gaussian(arg_keys[1], (ROWS, LEN, D), 1.0, 6.0, ((0, 4), (1, 8))),
        "segment_ids": draw_segment_ids(jax.random.fold_in(arg_keys[22], 71), 0),
        "position_ids": draw_position_ids(jax.random.fold_in(arg_keys[22], 71), 0),
        "w_attend": gaussian(arg_keys[4], (D, QKV), D ** -0.5, 0.15625, ((0, 8),), jnp.float32),
        "w_out": gaussian(arg_keys[5], (HQD, D), (HQD // 64) ** -0.5, 1.25, ((0, 8),), jnp.float32),
        "w_gate": gaussian(arg_keys[6], (D, FF), D ** -0.5, 0.15625, ((0, 8),), jnp.float32),
        "w_up": gaussian(arg_keys[7], (D, FF), D ** -0.5, 0.15625, ((0, 8),), jnp.float32),
        "w_down": gaussian(arg_keys[8], (FF, D), FF ** -0.5, 0.0625, ((0, 8),), jnp.float32),
        "small_params": draw_small_params(jax.random.fold_in(arg_keys[22], 71), 0),
        "first_attend": gaussian(arg_keys[10], (D, QKV), (0.11 * NPARAM ** -0.5), 9.1552734375e-05, ((0, 8),), jnp.float32),
        "first_out": gaussian(arg_keys[11], (HQD, D), (0.11 * NPARAM ** -0.5), 9.1552734375e-05, ((0, 8),), jnp.float32),
        "first_gate": gaussian(arg_keys[12], (D, FF), (0.11 * NPARAM ** -0.5), 9.1552734375e-05, ((0, 8),), jnp.float32),
        "first_up": gaussian(arg_keys[13], (D, FF), (0.11 * NPARAM ** -0.5), 9.1552734375e-05, ((0, 8),), jnp.float32),
        "first_down": gaussian(arg_keys[14], (FF, D), (0.11 * NPARAM ** -0.5), 9.1552734375e-05, ((0, 8),), jnp.float32),
        "first_small": gaussian(arg_keys[15], (SMALL,), (0.44 * NPARAM ** -0.5), 0.00036621094, ((0, 8),), jnp.float32),
        "second_attend": jnp.clip(jnp.exp(math.log(4.487388238771928e-09) - 1.37681564 * jax.random.uniform(arg_keys[16], (D, QKV), jnp.float32) ** steps_of(arg_keys[16], (D, QKV), ((0, 8),), -0.2, 0.2)), 1.1325312909704621e-09, 4.487388238771928e-09),
        "second_out": jnp.clip(jnp.exp(math.log(4.487388238771928e-09) - 1.37681564 * jax.random.uniform(arg_keys[17], (HQD, D), jnp.float32) ** steps_of(arg_keys[17], (HQD, D), ((0, 8),), -0.2, 0.2)), 1.1325312909704621e-09, 4.487388238771928e-09),
        "second_gate": jnp.clip(jnp.exp(math.log(4.487388238771928e-09) - 1.37681564 * jax.random.uniform(arg_keys[18], (D, FF), jnp.float32) ** steps_of(arg_keys[18], (D, FF), ((0, 8),), -0.2, 0.2)), 1.1325312909704621e-09, 4.487388238771928e-09),
        "second_up": jnp.clip(jnp.exp(math.log(4.487388238771928e-09) - 1.37681564 * jax.random.uniform(arg_keys[19], (D, FF), jnp.float32) ** steps_of(arg_keys[19], (D, FF), ((0, 8),), -0.2, 0.2)), 1.1325312909704621e-09, 4.487388238771928e-09),
        "second_down": jnp.clip(jnp.exp(math.log(4.487388238771928e-09) - 1.37681564 * jax.random.uniform(arg_keys[20], (FF, D), jnp.float32) ** steps_of(arg_keys[20], (FF, D), ((0, 8),), -0.2, 0.2)), 1.1325312909704621e-09, 4.487388238771928e-09),
        "second_small": jnp.clip(jnp.exp(math.log(7.26529520989061e-08) - 1.39812881 * jax.random.uniform(arg_keys[21], (SMALL,), jnp.float32) ** steps_of(arg_keys[21], (SMALL,), ((0, 8),), -0.2, 0.2)), 1.794955295508771e-08, 7.26529520989061e-08),
    }


NORM_EPS = 1e-06
ROPE_BASE = 10000.0
CLIP_NORM = 1.0
BETA_FIRST = 0.9
BETA_SECOND = 0.95
ADAM_EPS = 1e-08
WEIGHT_DECAY = 0.1
RATE_ATTEND = 0.06
RATE_OUT = 0.5
RATE_GATE = 0.06
RATE_DOWN = 0.03
RATE_VECTOR = 0.5
NEG_LARGE = -1e+30
HIGH_PRECISION = lax.Precision.HIGHEST

@jax.custom_vjp
def low(v):
    return lax.optimization_barrier(v.astype(jnp.bfloat16)).astype(jnp.float32)

@jax.custom_vjp
def low_back(v):
    return v

def low_keep(v):
    return (low(v), None)

def low_pass(kept, grad):
    return (grad,)

def back_keep(v):
    return (v, None)

def back_low(kept, grad):
    return (low(grad),)
low.defvjp(low_keep, low_pass)
low_back.defvjp(back_keep, back_low)

def norm_apply(values, gain):
    return values * lax.rsqrt(lax.optimization_barrier(jnp.mean(values * values, axis=-1, keepdims=True)) + NORM_EPS) * gain

def rotate(values, position):
    half = values.shape[-1] // 2
    freqs = ROPE_BASE ** (-2.0 * jnp.arange(half, dtype=jnp.float32) / values.shape[-1])
    angles = position.astype(jnp.float32)[:, None] * freqs[None, :]
    cosine = jnp.cos(angles)[:, None, :]
    sine = jnp.sin(angles)[:, None, :]
    first_half = values[..., :half]
    second_half = values[..., half:]
    return jnp.concatenate([first_half * cosine - second_half * sine, second_half * cosine + first_half * sine], axis=-1)

def attend_row(query, keys_row, values_row, seg_row):
    head_group = H // KVH
    block_total = LEN // KB
    keys_heads = keys_row.transpose(1, 0, 2)
    values_heads = values_row.transpose(1, 0, 2)
    key_index = jnp.arange(LEN, dtype=jnp.int32)
    query_blocks = query.reshape(block_total, KB, KVH, head_group, HD)
    seg_blocks = seg_row.reshape(block_total, KB)
    index_blocks = key_index.reshape(block_total, KB)

    @jax.checkpoint
    def one_block(parts):
        query_blk, seg_blk, index_blk = parts
        raw_scores = jnp.einsum('qkgd,knd->kgqn', query_blk, keys_heads, precision=HIGH_PRECISION)
        scores = low_back(raw_scores * HD ** (-0.5))
        allowed = jnp.logical_and(key_index[None, :] <= index_blk[:, None], seg_row[None, :] == seg_blk[:, None])
        scores = jnp.where(allowed[None, None], scores, NEG_LARGE)
        row_max = lax.optimization_barrier(jnp.max(scores, axis=-1, keepdims=True))
        weights = jnp.exp(scores - row_max)
        weights = weights / lax.optimization_barrier(jnp.sum(weights, axis=-1, keepdims=True))
        block_out = jnp.einsum('kgqn,knd->qkgd', low(weights), values_heads, precision=HIGH_PRECISION)
        return block_out.reshape(KB, HQD)
    return lax.map(one_block, (query_blocks, seg_blocks, index_blocks)).reshape(LEN, HQD)

def row_forward(params, x_row, seg_row, pos_row):
    attend_used, out_used, gate_used, up_used, down_used, vector_used = [low(param) for param in params]
    gain_one = vector_used[:D]
    gain_two = vector_used[D:2 * D]
    bias = vector_used[2 * D:]
    h_one = low(norm_apply(x_row, gain_one))
    mixed = low_back(jnp.dot(h_one, attend_used, precision=HIGH_PRECISION) + bias)
    query = low(rotate(mixed[:, :HQD].reshape(LEN, H, HD), pos_row))
    key_rot = low(rotate(mixed[:, HQD:HQD + KVD].reshape(LEN, KVH, HD), pos_row))
    value_low = low(mixed[:, HQD + KVD:].reshape(LEN, KVH, HD))
    attended = attend_row(query, key_rot, value_low, seg_row)
    att_in = low(low_back(attended))
    resid = x_row + low_back(jnp.dot(att_in, out_used, precision=HIGH_PRECISION))
    h_two = low(norm_apply(resid, gain_two))
    gate = low_back(jnp.dot(h_two, gate_used, precision=HIGH_PRECISION))
    up_proj = low_back(jnp.dot(h_two, up_used, precision=HIGH_PRECISION))
    hidden = low(jax.nn.silu(gate) * up_proj)
    return resid + jnp.dot(hidden, down_used, precision=HIGH_PRECISION)

def adam_step(weight, grad, first, second, rate, decay):
    first_new = BETA_FIRST * first + (1.0 - BETA_FIRST) * grad
    second_new = BETA_SECOND * second + (1.0 - BETA_SECOND) * grad * grad
    first_hat = first_new / (1.0 - BETA_FIRST ** STEP)
    second_hat = second_new / (1.0 - BETA_SECOND ** STEP)
    weight_new = weight - rate * (first_hat / (jnp.sqrt(second_hat) + ADAM_EPS) + decay * weight)
    return (first_new, second_new, weight_new)

def reference(tokens, cotangent, segment_ids, position_ids, w_attend, w_out, w_gate, w_up, w_down, small_params, first_attend, first_out, first_gate, first_up, first_down, first_small, second_attend, second_out, second_gate, second_up, second_down, second_small):
    params = (w_attend, w_out, w_gate, w_up, w_down, small_params)

    def per_row(totals, row_parts):
        x_row, ct_row, seg_row, pos_row = row_parts

        def forward_here(param_set, x_values):
            return row_forward(param_set, x_values, seg_row, pos_row)
        result, pullback = jax.vjp(forward_here, params, x_row.astype(jnp.float32))
        grad_params, grad_x = pullback(ct_row.astype(jnp.float32))
        totals = tuple((total_now + grad_now for total_now, grad_now in zip(totals, grad_params)))
        return (totals, (result.astype(jnp.bfloat16), grad_x.astype(jnp.bfloat16)))
    zeros_start = tuple((jnp.zeros_like(param) for param in params))
    totals, (out_tokens, grad_tokens) = lax.scan(per_row, zeros_start, (tokens, cotangent, segment_ids, position_ids))
    square_sum = sum((jnp.sum(grad_now * grad_now) for grad_now in totals))
    grad_norm = jnp.sqrt(square_sum)
    factor = jnp.minimum(1.0, CLIP_NORM / (grad_norm + 1e-06))
    grad_attend, grad_out, grad_gate, grad_up, grad_down, grad_vector = [factor * grad_now for grad_now in totals]
    new_first_attend, new_second_attend, new_attend = adam_step(w_attend, grad_attend, first_attend, second_attend, RATE_ATTEND, WEIGHT_DECAY)
    new_first_out, new_second_out, new_out = adam_step(w_out, grad_out, first_out, second_out, RATE_OUT, WEIGHT_DECAY)
    new_first_gate, new_second_gate, new_gate = adam_step(w_gate, grad_gate, first_gate, second_gate, RATE_GATE, WEIGHT_DECAY)
    new_first_up, new_second_up, new_up = adam_step(w_up, grad_up, first_up, second_up, RATE_GATE, WEIGHT_DECAY)
    new_first_down, new_second_down, new_down = adam_step(w_down, grad_down, first_down, second_down, RATE_DOWN, WEIGHT_DECAY)
    new_first_small, new_second_small, new_small = adam_step(small_params, grad_vector, first_small, second_small, RATE_VECTOR, 0.0)
    return (out_tokens, grad_tokens, grad_norm, new_first_attend, new_second_attend, new_attend, new_first_out, new_second_out, new_out, new_first_gate, new_second_gate, new_gate, new_first_up, new_second_up, new_up, new_first_down, new_second_down, new_down, new_first_small, new_second_small, new_small)
```

```python
import jax
import jax.numpy as jnp
from jax import lax
from jax.sharding import PartitionSpec as P

D = 1536
FF = 8960
H = 12
KVH = 2
HD = 128
STEP = 10
HQD = 1536
KVD = 256


NORM_EPS = 1e-06
ROPE_BASE = 10000.0
CLIP_NORM = 1.0
BETA_FIRST = 0.9
BETA_SECOND = 0.95
ADAM_EPS = 1e-08
WEIGHT_DECAY = 0.1
RATE_ATTEND = 0.06
RATE_OUT = 0.5
RATE_GATE = 0.06
RATE_DOWN = 0.03
RATE_VECTOR = 0.5
NEG_LARGE = -1e30


def norm_apply(values, gain):
    return values * lax.rsqrt(jnp.mean(values * values, axis=-1, keepdims=True) + NORM_EPS) * gain


def rotate(values, position):
    half = values.shape[-1] // 2
    freqs = ROPE_BASE ** (-2.0 * jnp.arange(half, dtype=jnp.float32) / values.shape[-1])
    angles = position.astype(jnp.float32)[:, None] * freqs[None, :]
    cosine = jnp.cos(angles)[:, None, :]
    sine = jnp.sin(angles)[:, None, :]
    first_half = values[..., :half]
    second_half = values[..., half:]
    return jnp.concatenate(
        [first_half * cosine - second_half * sine, second_half * cosine + first_half * sine],
        axis=-1,
    )


def swish_product(gate, up_proj):
    return jax.nn.silu(gate) * up_proj


def left_product(left_side, right_side):
    return lax.dot_general(
        left_side, right_side, (((0,), (0,)), ((), ())), preferred_element_type=jnp.float32
    )


def right_transposed(left_side, right_side):
    return lax.dot_general(
        left_side, right_side, (((1,), (1,)), ((), ())), preferred_element_type=jnp.float32
    )


def square_total(arrays):
    return sum((jnp.sum(member * member) for member in arrays))


def unchanged(state_in):
    return state_in


def adam_step(weight, grad, first, second, rate, decay):
    first_new = BETA_FIRST * first + (1.0 - BETA_FIRST) * grad
    second_new = BETA_SECOND * second + (1.0 - BETA_SECOND) * grad * grad
    first_hat = first_new / (1.0 - BETA_FIRST**STEP)
    second_hat = second_new / (1.0 - BETA_SECOND**STEP)
    weight_new = weight - rate * (first_hat / (jnp.sqrt(second_hat) + ADAM_EPS) + decay * weight)
    return (first_new, second_new, weight_new)


CORE = [(0, 1), (1, 0), (2, 3), (3, 2)]
CROSS = [(0, 2), (2, 0), (1, 3), (3, 1)]
DIAG = [(0, 3), (3, 0), (1, 2), (2, 1)]


def low(values):
    return values.astype(jnp.bfloat16)


def wide(values):
    return values.astype(jnp.float32)


def swap_core(values):
    return lax.ppermute(values, "grp", CORE)


def swap_cross(values):
    return lax.ppermute(values, "grp", CROSS)


def swap_diag(values):
    return lax.ppermute(values, "grp", DIAG)


def swap_blk(values, bit):
    count = lax.axis_size("blk")
    return lax.ppermute(values, "blk", [(i, i ^ bit) for i in range(count)])


def blk_bit(bit):
    return (lax.axis_index("blk") & bit) != 0


def bits_of(count):
    out = []
    bit = count // 2
    while bit >= 1:
        out.append(bit)
        bit //= 2
    return out


def gather_bits(values, order):
    done = []
    for bit in order:
        other = swap_blk(values, bit)
        mine = blk_bit(bit)
        axis = sum(1 for d in done if d > bit)
        values = jnp.stack(
            [jnp.where(mine, other, values), jnp.where(mine, values, other)], axis=axis
        )
        done.append(bit)
    return values


def scatter_bits(values, axes, order):
    axes = list(axes)
    for bit in order:
        axis = axes.index(bit)
        mine = blk_bit(bit).astype(jnp.int32)
        keep = lax.dynamic_index_in_dim(values, mine, axis, keepdims=False)
        send = lax.dynamic_index_in_dim(values, 1 - mine, axis, keepdims=False)
        values = low(wide(keep) + wide(swap_blk(send, bit)))
        axes.remove(bit)
    return values


def by_place(parts):
    grp = lax.axis_index("grp")
    core = (grp & 1) != 0
    cross = (grp & 2) != 0
    a, b, c, d = parts
    a, b = jnp.where(core, b, a), jnp.where(core, a, b)
    c, d = jnp.where(core, d, c), jnp.where(core, c, d)
    a, c = jnp.where(cross, c, a), jnp.where(cross, a, c)
    b, d = jnp.where(cross, d, b), jnp.where(cross, b, d)
    return [a, b, c, d]


def gather_near(values):
    cross = swap_cross(values)
    both = swap_core(jnp.stack([values, cross]))
    return [values, both[0], cross, both[1]]


def gather_grp(values):
    return by_place(gather_near(values))


def gather_tokens(values, bit):
    half = values.shape[0] // 2
    cross = swap_cross(values)
    over = swap_blk(values, bit)
    first = swap_blk(cross[:half], bit)
    second = swap_cross(over[half:])
    chip = jnp.concatenate([values, cross, over, first, second])
    return jnp.concatenate([chip, swap_core(chip)])


def scatter_tokens(values, bit):
    half_all = values.shape[0] // 2
    rows = half_all // 4
    half = rows // 2
    chip = wide(values[:half_all]) + wide(swap_core(low(values[half_all:])))
    own, cross, over, far = (chip[rows * i : rows * (i + 1)] for i in range(4))
    far = low(far)
    first = wide(swap_blk(far[:half], bit))
    second = wide(swap_cross(far[half:]))
    cross = low(jnp.concatenate([cross[:half] + first, cross[half:]]))
    over = low(jnp.concatenate([over[:half], over[half:] + second]))
    return own + wide(swap_cross(cross)) + wide(swap_blk(over, bit))


def angles_of(position):
    half = HD // 2
    freqs = ROPE_BASE ** (-2.0 * jnp.arange(half, dtype=jnp.float32) / HD)
    return position.astype(jnp.float32)[:, None] * freqs[None, :]


def rotate_by(values, cosine, sine):
    half = HD // 2
    first_half = values[..., :half]
    second_half = values[..., half:]
    return jnp.concatenate(
        [first_half * cosine - second_half * sine, second_half * cosine + first_half * sine],
        axis=-1,
    )


def on_device(
    tokens,
    cotangent,
    segment_ids,
    position_ids,
    w_attend,
    w_out,
    w_gate,
    w_up,
    w_down,
    small_params,
    first_attend,
    first_out,
    first_gate,
    first_up,
    first_down,
    first_small,
    second_attend,
    second_out,
    second_gate,
    second_up,
    second_down,
    second_small,
):
    rows_here, block_len = tokens.shape[:2]
    blk_count = lax.axis_size("blk")
    seq_len = block_len * blk_count
    token_count = rows_here * block_len
    head_group = H // KVH
    score_scale = HD ** (-0.5)
    grp = lax.axis_index("grp")
    blk = lax.axis_index("blk")
    cross_id, core_id = grp // 2, grp % 2
    strip_heads = H // 4
    strip_q = strip_heads * HD
    bits = bits_of(blk_count)
    team = blk_count // 4
    lows = [bit for bit in bits if bit < team]
    spread = [bits[0]] + lows
    low_shape = (2,) * len(lows)
    in_team = blk_bit(team).astype(jnp.int32)
    weight_rows = w_gate.shape[0]
    ff_block = w_down.shape[0]
    quarter = ff_block // 4
    ff_here = quarter * blk_count // 2

    flat_low = tokens.reshape(token_count, D)
    dy_low = cotangent.reshape(token_count, D)
    positions = position_ids.reshape(token_count)
    vector = wide(gather_bits(low(small_params), bits).reshape(-1))
    gain_one = vector[:D]
    gain_two = vector[D : 2 * D]
    bias = vector[2 * D :]
    kv_at = HQD + HD * cross_id + KVD * core_id
    strip_local = low(
        jnp.concatenate(
            [
                lax.dynamic_slice_in_dim(w_attend, strip_q * grp, strip_q, 1),
                lax.dynamic_slice_in_dim(w_attend, kv_at, HD, 1),
            ],
            axis=1,
        )
    )
    strip_bias = jnp.concatenate(
        [
            lax.dynamic_slice_in_dim(bias, strip_q * grp, strip_q, 0),
            lax.dynamic_slice_in_dim(bias, kv_at, HD, 0),
        ]
    )
    strip = gather_bits(strip_local, bits).reshape(D, strip_q + HD)
    near_tokens = jnp.concatenate(gather_near(flat_low))
    near_positions = jnp.concatenate(gather_near(positions))
    seg_all = gather_bits(segment_ids, bits).reshape((blk_count,) + segment_ids.shape)
    seg_all = seg_all.transpose(1, 0, 2).reshape(rows_here, seq_len)

    near_wide = wide(near_tokens)
    near_one = low(norm_apply(near_wide, gain_one))
    mixed = jnp.dot(near_one, strip, preferred_element_type=jnp.float32) + strip_bias
    angles = angles_of(near_positions)[:, None, :]
    turned = jnp.arange(strip_heads + 1)[None, :, None] < strip_heads + 1 - core_id
    angles = jnp.where(turned, angles, 0.0)
    strip_out = low(
        rotate_by(
            mixed.reshape(4 * token_count, strip_heads + 1, HD), jnp.cos(angles), jnp.sin(angles)
        )
    ).reshape(4, token_count, strip_q + HD)
    strips = by_place(
        [
            strip_out[0],
            swap_core(strip_out[1]),
            swap_cross(strip_out[2]),
            swap_diag(strip_out[3]),
        ]
    )
    query = jnp.concatenate([part[:, :strip_q] for part in strips], axis=1)
    key_value = jnp.concatenate([strips[k][:, strip_q:] for k in (0, 2, 1, 3)], axis=1)
    key_value = key_value.reshape(rows_here, block_len, 2 * KVD)
    query_heads = query.reshape(rows_here, block_len, KVH, head_group, HD).transpose(0, 2, 3, 1, 4)
    kv_all = gather_bits(key_value, bits).reshape((blk_count,) + key_value.shape)
    kv_all = kv_all.transpose(1, 0, 2, 3).reshape(rows_here, seq_len, 2, KVH, HD)
    keys_here = kv_all[:, :, 0]
    values_here = kv_all[:, :, 1]

    query_index = blk * block_len + jnp.arange(block_len, dtype=jnp.int32)
    key_index = jnp.arange(seq_len, dtype=jnp.int32)
    causal = key_index[None, :] <= query_index[:, None]
    same_doc = seg_all[:, None, :] == segment_ids[:, :, None]
    allowed = jnp.logical_and(causal[None, :, :], same_doc)[:, None, None, :, :]

    scores = (
        jnp.einsum("rkgqd,rnkd->rkgqn", query_heads, keys_here, preferred_element_type=jnp.float32)
        * score_scale
    )
    scores = jnp.where(allowed, scores, NEG_LARGE)
    row_max = jnp.max(scores, axis=-1)
    weights = jnp.exp(scores - row_max[..., None])
    row_sum = jnp.sum(weights, axis=-1)
    row_out = jnp.einsum(
        "rkgqn,rnkd->rkgqd", low(weights), values_here, preferred_element_type=jnp.float32
    )
    attended_heads = row_out / row_sum[..., None]
    log_total = row_max + jnp.log(row_sum)
    att_in = low(attended_heads.transpose(0, 3, 1, 2, 4).reshape(token_count, HQD))

    out_local = low(lax.dynamic_slice_in_dim(w_out, strip_q * grp, strip_q, 1))
    out_strip = gather_bits(out_local, bits).reshape(HQD, strip_q)
    out_full = jnp.concatenate(gather_grp(out_strip), axis=1)

    def columns(weight):
        parts = low(weight).reshape(weight_rows, 2, 2, blk_count // 4, 4, quarter)
        parts = lax.dynamic_index_in_dim(parts, grp, 4, keepdims=False)
        keep = lax.dynamic_index_in_dim(parts, in_team, 2, keepdims=False)
        send = lax.dynamic_index_in_dim(parts, 1 - in_team, 2, keepdims=False)
        keep = keep.reshape(weight_rows, ff_here)
        got = swap_blk(send.reshape(weight_rows, ff_here), team)
        mine = blk_bit(team)
        pair = jnp.stack([jnp.where(mine, got, keep), jnp.where(mine, keep, got)])
        done = [team]
        for bit in spread:
            other = swap_blk(pair, bit)
            mine = blk_bit(bit)
            axis = sum(1 for d in done if d > bit)
            pair = jnp.stack(
                [jnp.where(mine, other, pair), jnp.where(mine, pair, other)], axis=axis
            )
            done.append(bit)
        return pair.reshape(D, ff_here)

    gate_here = columns(w_gate)
    up_here = columns(w_up)
    down_local = low(lax.dynamic_slice_in_dim(w_down, quarter * grp, quarter, 0))
    down_here = gather_bits(down_local, spread).reshape(ff_here, D)
    dy_team = gather_tokens(dy_low, team)

    flat = wide(flat_low)
    resid = flat + jnp.dot(att_in, out_full, preferred_element_type=jnp.float32)
    h_two = low(norm_apply(resid, gain_two))
    h_team = gather_tokens(h_two, team)
    gate = jnp.dot(h_team, gate_here, preferred_element_type=jnp.float32)
    up_proj = jnp.dot(h_team, up_here, preferred_element_type=jnp.float32)
    hidden = low(swish_product(gate, up_proj))
    share_down = scatter_bits(
        low(left_product(hidden, dy_team)).reshape((2,) + low_shape + (quarter, D)),
        spread,
        lows[::-1] + [bits[0]],
    )
    d_hidden = right_transposed(dy_team, down_here)
    swish_value, swish_back = jax.vjp(swish_product, gate, up_proj)
    d_gate, d_up = swish_back(d_hidden)
    d_gate = low(d_gate)
    d_up = low(d_up)
    d_htwo = scatter_tokens(
        right_transposed(d_gate, gate_here) + right_transposed(d_up, up_here), team
    )
    out_tokens = low(
        resid
        + scatter_tokens(jnp.dot(hidden, down_here, preferred_element_type=jnp.float32), team)
    )

    def share_columns(grad):
        grad = grad.reshape((2, 2) + low_shape + (weight_rows, ff_here))
        grad = scatter_bits(grad, bits, lows[::-1] + [bits[0]])
        keep = lax.dynamic_index_in_dim(grad, in_team, 0, keepdims=False)
        send = lax.dynamic_index_in_dim(grad, 1 - in_team, 0, keepdims=False)
        got = swap_blk(send, team)
        mine = blk_bit(team)
        return jnp.stack([jnp.where(mine, got, keep), jnp.where(mine, keep, got)])

    share_gate = share_columns(low(left_product(h_team, d_gate)))
    share_up = share_columns(low(left_product(h_team, d_up)))

    norm_value_two, norm_back_two = jax.vjp(norm_apply, resid, gain_two)
    d_resid_norm, grad_gain_two = norm_back_two(d_htwo)
    d_resid = wide(dy_low) + d_resid_norm
    d_att = low(d_resid)

    d_attended = low(right_transposed(d_att, out_full))
    grad_heads = d_attended.reshape(rows_here, block_len, KVH, head_group, HD).transpose(
        0, 2, 3, 1, 4
    )
    row_delta = jnp.sum(wide(grad_heads) * attended_heads, axis=-1)
    scores = (
        jnp.einsum("rkgqd,rnkd->rkgqn", query_heads, keys_here, preferred_element_type=jnp.float32)
        * score_scale
    )
    probs = jnp.where(allowed, jnp.exp(scores - log_total[..., None]), 0.0)
    dprob = jnp.einsum(
        "rkgqd,rnkd->rkgqn", grad_heads, values_here, preferred_element_type=jnp.float32
    )
    dscore = low(probs * (dprob - row_delta[..., None]))
    dq_sum = jnp.einsum(
        "rkgqn,rnkd->rkgqd", dscore, keys_here, preferred_element_type=jnp.float32
    )
    dk_all = jnp.einsum(
        "rkgqn,rkgqd->rnkd", dscore, query_heads, preferred_element_type=jnp.float32
    )
    dv_all = jnp.einsum(
        "rkgqn,rkgqd->rnkd", low(probs), grad_heads, preferred_element_type=jnp.float32
    )
    dkv = low(jnp.stack([dk_all * score_scale, dv_all], axis=2))
    dkv = dkv.reshape(rows_here, blk_count, block_len, 2 * KVD).transpose(1, 0, 2, 3)
    dkv = dkv.reshape((2,) * len(bits) + (rows_here, block_len, 2 * KVD))
    dkv = wide(scatter_bits(dkv, bits, bits[::-1])).reshape(token_count, 2, KVH, HD)
    own_angles = angles_of(positions)[:, None, :]
    cosine, sine = jnp.cos(own_angles), -jnp.sin(own_angles)
    dq_tokens = (dq_sum * score_scale).transpose(0, 3, 1, 2, 4).reshape(token_count, H, HD)
    d_query = low(rotate_by(dq_tokens, cosine, sine)).reshape(token_count, HQD)
    d_key = low(rotate_by(dkv[:, 0], cosine, sine))
    d_value = low(dkv[:, 1])
    d_mixed = jnp.concatenate(
        [d_query, d_key.reshape(token_count, KVD), d_value.reshape(token_count, KVD)], axis=1
    )
    grad_bias = jnp.sum(wide(d_mixed), axis=0)
    parts = by_place(
        [
            jnp.concatenate(
                [
                    d_query[:, strip_q * k : strip_q * (k + 1)],
                    (d_value if k % 2 else d_key)[:, k // 2],
                ],
                axis=1,
            )
            for k in range(4)
        ]
    )
    near_d = jnp.concatenate(
        [parts[0], swap_core(parts[1]), swap_cross(parts[2]), swap_diag(parts[3])]
    )
    share_attend = scatter_bits(
        low(left_product(near_one, near_d)).reshape((2,) * len(bits) + (weight_rows, -1)),
        bits,
        bits[::-1],
    )
    near_hone = right_transposed(near_d, strip)
    near_rms = lax.rsqrt(jnp.mean(near_wide * near_wide, axis=-1, keepdims=True) + NORM_EPS)
    gain_one_part = jnp.sum(near_hone * near_wide * near_rms, axis=0)
    half = low(near_hone[token_count : 2 * token_count]), low(near_hone[3 * token_count :])
    other = wide(swap_core(jnp.concatenate(half)))
    d_hone = near_hone[:token_count] + other[:token_count]
    d_hone = d_hone + wide(
        swap_cross(low(near_hone[2 * token_count : 3 * token_count] + other[token_count:]))
    )
    norm_value_one, norm_back_one = jax.vjp(norm_apply, flat, gain_one)
    d_flat_norm, unused_gain = norm_back_one(d_hone)
    grad_tokens = low(d_resid + d_flat_norm)

    near_att = jnp.concatenate(gather_near(att_in))
    d_parts = by_place([d_att[:, strip_q * k : strip_q * (k + 1)] for k in range(4)])
    near_datt = jnp.concatenate(
        [d_parts[0], swap_core(d_parts[1]), swap_cross(d_parts[2]), swap_diag(d_parts[3])]
    )
    share_out = scatter_bits(
        low(left_product(near_att, near_datt)).reshape((2,) * len(bits) + (weight_rows, -1)),
        bits,
        bits[::-1],
    )

    vector_term = jnp.concatenate([gain_one_part, grad_gain_two, grad_bias])
    vector_term = vector_term + swap_cross(vector_term)
    vector_term = vector_term + swap_core(vector_term)
    vector_term = vector_term.reshape((2,) * len(bits) + (-1,))
    axes = list(bits)
    for bit in bits[::-1]:
        axis = axes.index(bit)
        mine = blk_bit(bit).astype(jnp.int32)
        keep = lax.dynamic_index_in_dim(vector_term, mine, axis, keepdims=False)
        send = lax.dynamic_index_in_dim(vector_term, 1 - mine, axis, keepdims=False)
        vector_term = keep + swap_blk(send, bit)
        axes.remove(bit)
    share_vector = vector_term

    square_sum = square_total(
        [wide(s) for s in (share_attend, share_out, share_gate, share_up, share_down)]
    ) + 0.25 * jnp.sum(share_vector * share_vector)
    square_sum = jnp.full((8, 128), square_sum)
    for bit in bits:
        square_sum = square_sum + swap_blk(square_sum, bit)
    square_sum = square_sum + swap_cross(square_sum)
    square_sum = square_sum + swap_core(square_sum)
    grad_norm = jnp.sqrt(square_sum[0, 0])
    factor = jnp.minimum(1.0, CLIP_NORM / (grad_norm + 1e-06))

    attend_parts = gather_grp(share_attend)
    grad_attend = jnp.concatenate(
        [part[:, :strip_q] for part in attend_parts]
        + [attend_parts[k][:, strip_q:] for k in (0, 2, 1, 3)],
        axis=1,
    )
    grad_out = jnp.concatenate(gather_grp(share_out), axis=1)
    grad_down = jnp.concatenate(gather_grp(share_down), axis=0)

    def whole_columns(share):
        parts = jnp.stack(gather_grp(share))
        parts = parts.reshape(4, 2, weight_rows, 2, blk_count // 4, quarter)
        return parts.transpose(2, 3, 1, 4, 0, 5).reshape(weight_rows, FF)

    grad_gate = whole_columns(share_gate)
    grad_up = whole_columns(share_up)

    new_first_attend, new_second_attend, new_attend = adam_step(
        w_attend, factor * wide(grad_attend), first_attend, second_attend, RATE_ATTEND, WEIGHT_DECAY
    )
    new_first_out, new_second_out, new_out = adam_step(
        w_out, factor * wide(grad_out), first_out, second_out, RATE_OUT, WEIGHT_DECAY
    )
    new_first_gate, new_second_gate, new_gate = adam_step(
        w_gate, factor * wide(grad_gate), first_gate, second_gate, RATE_GATE, WEIGHT_DECAY
    )
    new_first_up, new_second_up, new_up = adam_step(
        w_up, factor * wide(grad_up), first_up, second_up, RATE_GATE, WEIGHT_DECAY
    )
    new_first_down, new_second_down, new_down = adam_step(
        w_down, factor * wide(grad_down), first_down, second_down, RATE_DOWN, WEIGHT_DECAY
    )
    new_first_small, new_second_small, new_small = adam_step(
        small_params, factor * share_vector, first_small, second_small, RATE_VECTOR, 0.0
    )
    return (
        out_tokens.reshape(rows_here, block_len, D),
        grad_tokens.reshape(rows_here, block_len, D),
        grad_norm,
        new_first_attend,
        new_second_attend,
        new_attend,
        new_first_out,
        new_second_out,
        new_out,
        new_first_gate,
        new_second_gate,
        new_gate,
        new_first_up,
        new_second_up,
        new_up,
        new_first_down,
        new_second_down,
        new_down,
        new_first_small,
        new_second_small,
        new_small,
    )


def solution(mesh):
    placed = (
        P("grp", "blk", None),
        P("grp", "blk", None),
        P("grp", "blk"),
        P("grp", "blk"),
        P("blk", None),
        P("blk", None),
        P("blk", None),
        P("blk", None),
        P("blk", None),
        P("blk"),
        P("blk", None),
        P("blk", None),
        P("blk", None),
        P("blk", None),
        P("blk", None),
        P("blk"),
        P("blk", None),
        P("blk", None),
        P("blk", None),
        P("blk", None),
        P("blk", None),
        P("blk"),
    )
    return jax.shard_map(
        on_device,
        mesh=mesh,
        in_specs=placed,
        out_specs=(
            P("grp", "blk", None),
            P("grp", "blk", None),
            P(),
            P("blk", None),
            P("blk", None),
            P("blk", None),
            P("blk", None),
            P("blk", None),
            P("blk", None),
            P("blk", None),
            P("blk", None),
            P("blk", None),
            P("blk", None),
            P("blk", None),
            P("blk", None),
            P("blk", None),
            P("blk", None),
            P("blk", None),
            P("blk"),
            P("blk"),
            P("blk"),
        ),
        check_vma=False,
    )
```

```python
import functools

import jax
import jax.numpy as jnp
from jax import lax
from jax.experimental import pallas as pl
from jax.experimental.pallas import tpu as pltpu
from jax.sharding import PartitionSpec as P

D = 1536
FF = 8960
H = 12
KVH = 2
HD = 128
STEP = 10
HQD = 1536
KVD = 256


NORM_EPS = 1e-06
ROPE_BASE = 10000.0
CLIP_NORM = 1.0
BETA_FIRST = 0.9
BETA_SECOND = 0.95
ADAM_EPS = 1e-08
WEIGHT_DECAY = 0.1
RATE_ATTEND = 0.06
RATE_OUT = 0.5
RATE_GATE = 0.06
RATE_DOWN = 0.03
RATE_VECTOR = 0.5
NEG_LARGE = -1e30
LOG2E = 1.4426950408889634
VMEM = 48 * 1024 * 1024


def norm_apply(values, gain):
    return values * lax.rsqrt(jnp.mean(values * values, axis=-1, keepdims=True) + NORM_EPS) * gain


def swish_product(gate, up_proj):
    return jax.nn.silu(gate) * up_proj


def left_product(left_side, right_side):
    return lax.dot_general(
        left_side, right_side, (((0,), (0,)), ((), ())), preferred_element_type=jnp.float32
    )


def right_transposed(left_side, right_side):
    return lax.dot_general(
        left_side, right_side, (((1,), (1,)), ((), ())), preferred_element_type=jnp.float32
    )


def square_total(arrays):
    return sum((jnp.sum(member * member) for member in arrays))


def adam_step(weight, grad, first, second, rate, decay):
    first_new = BETA_FIRST * first + (1.0 - BETA_FIRST) * grad
    second_new = BETA_SECOND * second + (1.0 - BETA_SECOND) * grad * grad
    first_hat = first_new / (1.0 - BETA_FIRST**STEP)
    second_hat = second_new / (1.0 - BETA_SECOND**STEP)
    weight_new = weight - rate * (first_hat / (jnp.sqrt(second_hat) + ADAM_EPS) + decay * weight)
    return (first_new, second_new, weight_new)


def strip_starts(blk_count, team_bit, grp, quarter):
    per = blk_count // 4
    return [
        (((high * 2 + team_bit) * per + small) * 4 + grp) * quarter
        for high in range(2)
        for small in range(per)
    ]

def pick_body(blk_count, ids, gate_ref, up_ref, gate_out, up_out):
    quarter = FF // blk_count // 4
    for k in range(4):
        @pl.when(ids[0] == k)
        def _(k=k):
            for src, dst in ((gate_ref, gate_out), (up_ref, up_out)):
                for bit in range(2):
                    parts = [src[:, s:s + quarter] for s in strip_starts(blk_count, bit, k, quarter)]
                    dst[ids[1] ^ bit] = jnp.concatenate(parts, axis=1).astype(jnp.bfloat16)

def pick_columns(ids, gate, up, blk_count):
    rows = gate.shape[0]
    step = 48 if rows % 48 == 0 else rows
    wide_here = FF // 8
    spec = pl.BlockSpec((step, FF), lambda i, ids: (i, 0))
    out = pl.BlockSpec((2, step, wide_here), lambda i, ids: (0, i, 0))
    shape = jax.ShapeDtypeStruct((2, rows, wide_here), jnp.bfloat16)
    return pl.pallas_call(
        functools.partial(pick_body, blk_count),
        grid_spec=pltpu.PrefetchScalarGridSpec(
            num_scalar_prefetch=1, grid=(rows // step,), in_specs=[spec, spec], out_specs=[out, out]),
        out_shape=[shape, shape],
        compiler_params=pltpu.CompilerParams(vmem_limit_bytes=VMEM),
        cost_estimate=pl.CostEstimate(flops=0, bytes_accessed=rows * FF * 10, transcendentals=0),
        name="pick_columns",
    )(ids, gate, up)

def near_at(away):
    return (away & 1) * 2 + (away >> 1)


def adam_body(blk_count, rate, decay, ids, factor_ref, grad_ref, w_ref, m_ref, v_ref, m_out, v_out, w_out):
    quarter = FF // blk_count // 4
    per = blk_count // 4
    parts = []
    grads = [[grad_ref[near_at(ids[0] ^ k), bit] for bit in range(2)] for k in range(4)]
    for high in range(2):
        for bit in range(2):
            for small in range(per):
                at = (high * per + small) * quarter
                for k in range(4):
                    parts.append(grads[k][bit][:, at:at + quarter])
    grad = jnp.concatenate(parts, axis=1).astype(jnp.float32) * factor_ref[0]
    m, v, w = adam_step(w_ref[...], grad, m_ref[...], v_ref[...], rate, decay)
    m_out[...] = m
    v_out[...] = v
    w_out[...] = w

def adam_columns(ids, factor, grad, w, m, v, blk_count, rate, decay):
    rows = w.shape[0]
    step = 32 if rows % 32 == 0 else rows
    spec = pl.BlockSpec((step, FF), lambda i, ids: (i, 0))
    shape = jax.ShapeDtypeStruct((rows, FF), jnp.float32)
    return pl.pallas_call(
        functools.partial(adam_body, blk_count, rate, decay),
        grid_spec=pltpu.PrefetchScalarGridSpec(
            num_scalar_prefetch=1, grid=(rows // step,),
            in_specs=[pl.BlockSpec(memory_space=pltpu.SMEM),
                      pl.BlockSpec((4, 2, step, FF // 8), lambda i, ids: (0, 0, i, 0)), spec, spec, spec],
            out_specs=[spec, spec, spec]),
        out_shape=[shape] * 3,
        compiler_params=pltpu.CompilerParams(vmem_limit_bytes=VMEM),
        cost_estimate=pl.CostEstimate(flops=rows * FF * 20, bytes_accessed=rows * FF * 26, transcendentals=rows * FF),
        name="adam_columns",
    )(ids, factor, grad, w, m, v)

def nt(a, b, **kw):
    return lax.dot_general(a, b, (((1,), (1,)), ((), ())), preferred_element_type=jnp.float32, **kw)

def tn(a, b, **kw):
    return lax.dot_general(a, b, (((0,), (0,)), ((), ())), preferred_element_type=jnp.float32, **kw)

def stack_heads(ref, kvh, group):
    return jnp.concatenate([ref[:, HD * (kvh * group + i): HD * (kvh * group + i + 1)] for i in range(group)], axis=0)

def hidden_from(seg_key_ref, seg_query_ref, first, chunk, block_len, blk):
    key = first + lax.broadcasted_iota(jnp.int32, (chunk, block_len), 0)
    query = blk * block_len + lax.broadcasted_iota(jnp.int32, (chunk, block_len), 1)
    seg_key = seg_key_ref[pl.ds(first, chunk), :]
    counts = jnp.logical_and(key <= query, seg_key == seg_query_ref[0:1, :])
    return jnp.where(counts, 0.0, NEG_LARGE)

def attend_body(chunk, ids, q_ref, k_ref, v_ref, seg_key_ref, seg_query_ref, o_ref, lse_ref, m_s, l_s, acc_s):
    block_len = q_ref.shape[0]
    group = H // KVH
    row = pl.program_id(0)
    per = chunk // block_len
    scale = HD ** (-0.5) * LOG2E
    start = ids[1 + row] // per
    stop = ids[0] // per + 1
    for kvh in range(KVH):
        q = stack_heads(q_ref, kvh, group)
        m_s[...] = jnp.full_like(m_s, NEG_LARGE)
        l_s[...] = jnp.zeros_like(l_s)
        acc_s[...] = jnp.zeros_like(acc_s)

        def step(c, carry):
            keys = k_ref[pl.ds(c * per, per), :, HD * kvh: HD * (kvh + 1)].reshape(chunk, HD)
            vals = v_ref[pl.ds(c * per, per), :, HD * kvh: HD * (kvh + 1)].reshape(chunk, HD)
            bias = hidden_from(seg_key_ref, seg_query_ref, c * chunk, chunk, block_len, ids[0])
            s = nt(keys, q) * scale + jnp.concatenate([bias] * group, axis=1)
            old = m_s[0:1, :]
            new = jnp.maximum(old, jnp.max(s, axis=0, keepdims=True))
            p = jnp.exp2(s - new)
            fade = jnp.exp2(old - new)
            l_s[0:1, :] = l_s[0:1, :] * fade + jnp.sum(p, axis=0, keepdims=True)
            acc_s[...] = acc_s[...] * fade + tn(vals, p.astype(jnp.bfloat16))
            m_s[0:1, :] = new
            return carry

        lax.fori_loop(start, stop, step, 0)
        total = l_s[0:1, :]
        out = (acc_s[...] * (1.0 / total)).T
        for i in range(group):
            o_ref[:, HD * (kvh * group + i): HD * (kvh * group + i + 1)] = out[block_len * i: block_len * (i + 1), :].astype(jnp.bfloat16)
        lse_ref[kvh] = jnp.broadcast_to(m_s[0:1, :] + jnp.log2(total), (8, group * block_len))

def attend(ids, q, kv, seg_key, seg_query, block_len):
    blk_count, rows = kv.shape[:2]
    group = H // KVH
    chunk = 2 * block_len
    many = group * block_len
    return pl.pallas_call(
        functools.partial(attend_body, chunk),
        grid_spec=pltpu.PrefetchScalarGridSpec(
            num_scalar_prefetch=1, grid=(rows,),
            in_specs=[
                pl.BlockSpec((block_len, HQD), lambda r, ids: (r, 0)),
                pl.BlockSpec((blk_count, None, block_len, KVD), lambda r, ids: (0, r, 0, 0)),
                pl.BlockSpec((blk_count, None, block_len, KVD), lambda r, ids: (0, r, 0, 1)),
                pl.BlockSpec((None, blk_count * block_len, HD), lambda r, ids: (r, 0, 0)),
                pl.BlockSpec((None, 8, block_len), lambda r, ids: (r, 0, 0)),
            ],
            out_specs=[
                pl.BlockSpec((block_len, HQD), lambda r, ids: (r, 0)),
                pl.BlockSpec((None, KVH, 8, many), lambda r, ids: (r, 0, 0, 0)),
            ],
            scratch_shapes=[pltpu.VMEM((8, many), jnp.float32), pltpu.VMEM((8, many), jnp.float32), pltpu.VMEM((HD, many), jnp.float32)]),
        out_shape=[
            jax.ShapeDtypeStruct((rows * block_len, HQD), jnp.bfloat16),
            jax.ShapeDtypeStruct((rows, KVH, 8, many), jnp.float32),
        ],
        compiler_params=pltpu.CompilerParams(vmem_limit_bytes=VMEM),
        cost_estimate=pl.CostEstimate(flops=4 * rows * H * block_len * blk_count * block_len * HD, bytes_accessed=8 * 2**20, transcendentals=rows * H * block_len * blk_count * block_len),
        name="attend",
    )(ids, q, kv, kv, seg_key, seg_query)

def turn_back(u, cosine, sine):
    lane = lax.broadcasted_iota(jnp.int32, u.shape, 1)
    other = pltpu.roll(u, HD // 2, 1)
    return u * cosine + jnp.where(lane < HD // 2, other, -other) * sine

def attend_back_body(chunk, ids, q_ref, k_ref, v_ref, seg_key_ref, seg_query_ref, o_ref, do_ref, lse_ref, cos_ref, sin_ref, dq_ref, dkv_ref, dq_s):
    block_len = q_ref.shape[0]
    group = H // KVH
    row = pl.program_id(0)
    per = chunk // block_len
    plain = HD ** (-0.5)
    scale = plain * LOG2E
    start = ids[1 + row] // per
    stop = ids[0] // per + 1
    dkv_ref[...] = jnp.zeros_like(dkv_ref)
    for kvh in range(KVH):
        q = stack_heads(q_ref, kvh, group)
        do = stack_heads(do_ref, kvh, group)
        o = stack_heads(o_ref, kvh, group)
        both = do.astype(jnp.float32) * o.astype(jnp.float32)
        delta = nt(jnp.ones((8, HD), jnp.float32), both, precision=lax.Precision.HIGHEST)[0:1, :]
        lse = lse_ref[kvh][0:1, :]
        dq_s[...] = jnp.zeros_like(dq_s)

        def step(c, carry):
            keys = k_ref[pl.ds(c * per, per), :, HD * kvh: HD * (kvh + 1)].reshape(chunk, HD)
            vals = v_ref[pl.ds(c * per, per), :, HD * kvh: HD * (kvh + 1)].reshape(chunk, HD)
            bias = hidden_from(seg_key_ref, seg_query_ref, c * chunk, chunk, block_len, ids[0])
            s = nt(keys, q) * scale + jnp.concatenate([bias] * group, axis=1)
            p = jnp.exp2(s - lse)
            dp = nt(vals, do)
            ds = (p * (dp - delta)).astype(jnp.bfloat16)
            dk = jnp.dot(ds, q, preferred_element_type=jnp.float32) * plain
            dv = jnp.dot(p.astype(jnp.bfloat16), do, preferred_element_type=jnp.float32)
            dkv_ref[pl.ds(c * per, per), :, HD * kvh: HD * (kvh + 1)] = dk.astype(jnp.bfloat16).reshape(per, block_len, HD)
            dkv_ref[pl.ds(c * per, per), :, KVD + HD * kvh: KVD + HD * (kvh + 1)] = dv.astype(jnp.bfloat16).reshape(per, block_len, HD)
            dq_s[...] += tn(ds, keys)
            return carry

        lax.fori_loop(start, stop, step, 0)
        cosine, sine = cos_ref[...], sin_ref[...]
        for i in range(group):
            u = dq_s[block_len * i: block_len * (i + 1), :] * plain
            at = HD * (kvh * group + i)
            dq_ref[:, at: at + HD] = turn_back(u, cosine, sine).astype(jnp.bfloat16)

def attend_back(ids, q, kv, seg_key, seg_query, o, do, lse, cosine, sine, block_len):
    blk_count, rows = kv.shape[:2]
    group = H // KVH
    chunk = 2 * block_len
    many = group * block_len
    per_row = pl.BlockSpec((block_len, HQD), lambda r, ids: (r, 0))
    turn = pl.BlockSpec((block_len, HD), lambda r, ids: (r, 0))
    return pl.pallas_call(
        functools.partial(attend_back_body, chunk),
        grid_spec=pltpu.PrefetchScalarGridSpec(
            num_scalar_prefetch=1, grid=(rows,),
            in_specs=[
                per_row,
                pl.BlockSpec((blk_count, None, block_len, KVD), lambda r, ids: (0, r, 0, 0)),
                pl.BlockSpec((blk_count, None, block_len, KVD), lambda r, ids: (0, r, 0, 1)),
                pl.BlockSpec((None, blk_count * block_len, HD), lambda r, ids: (r, 0, 0)),
                pl.BlockSpec((None, 8, block_len), lambda r, ids: (r, 0, 0)),
                per_row, per_row,
                pl.BlockSpec((None, KVH, 8, many), lambda r, ids: (r, 0, 0, 0)),
                turn, turn,
            ],
            out_specs=[per_row, pl.BlockSpec((blk_count, None, block_len, 2 * KVD), lambda r, ids: (0, r, 0, 0))],
            scratch_shapes=[pltpu.VMEM((many, HD), jnp.float32)]),
        out_shape=[
            jax.ShapeDtypeStruct((rows * block_len, HQD), jnp.bfloat16),
            jax.ShapeDtypeStruct((blk_count, rows, block_len, 2 * KVD), jnp.bfloat16),
        ],
        compiler_params=pltpu.CompilerParams(vmem_limit_bytes=VMEM),
        cost_estimate=pl.CostEstimate(flops=10 * rows * H * block_len * blk_count * block_len * HD, bytes_accessed=12 * 2**20, transcendentals=rows * H * block_len * blk_count * block_len),
        name="attend_back",
    )(ids, q, kv, kv, seg_key, seg_query, o, do, lse, cosine, sine)


CORE = [(0, 1), (1, 0), (2, 3), (3, 2)]
CROSS = [(0, 2), (2, 0), (1, 3), (3, 1)]
DIAG = [(0, 3), (3, 0), (1, 2), (2, 1)]


def low(values):
    return values.astype(jnp.bfloat16)


def wide(values):
    return values.astype(jnp.float32)


def swap_core(values):
    return lax.ppermute(values, "grp", CORE)


def swap_cross(values):
    return lax.ppermute(values, "grp", CROSS)


def swap_diag(values):
    return lax.ppermute(values, "grp", DIAG)


def swap_blk(values, bit):
    count = lax.axis_size("blk")
    return lax.ppermute(values, "blk", [(i, i ^ bit) for i in range(count)])


def blk_bit(bit):
    return (lax.axis_index("blk") & bit) != 0


def bits_of(count):
    out = []
    bit = count // 2
    while bit >= 1:
        out.append(bit)
        bit //= 2
    return out


def gather_bits(values, order):
    done = []
    for bit in order:
        other = swap_blk(values, bit)
        mine = blk_bit(bit)
        axis = sum(1 for d in done if d > bit)
        values = jnp.stack(
            [jnp.where(mine, other, values), jnp.where(mine, values, other)], axis=axis
        )
        done.append(bit)
    return values


def scatter_bits(values, axes, order):
    axes = list(axes)
    for bit in order:
        axis = axes.index(bit)
        mine = blk_bit(bit).astype(jnp.int32)
        keep = lax.dynamic_index_in_dim(values, mine, axis, keepdims=False)
        send = lax.dynamic_index_in_dim(values, 1 - mine, axis, keepdims=False)
        values = low(wide(keep) + wide(swap_blk(send, bit)))
        axes.remove(bit)
    return values


def by_place(parts):
    grp = lax.axis_index("grp")
    core = (grp & 1) != 0
    cross = (grp & 2) != 0
    a, b, c, d = parts
    a, b = jnp.where(core, b, a), jnp.where(core, a, b)
    c, d = jnp.where(core, d, c), jnp.where(core, c, d)
    a, c = jnp.where(cross, c, a), jnp.where(cross, a, c)
    b, d = jnp.where(cross, d, b), jnp.where(cross, b, d)
    return [a, b, c, d]


def gather_near(values):
    cross = swap_cross(values)
    both = swap_core(jnp.stack([values, cross]))
    return [values, both[0], cross, both[1]]


def gather_grp(values):
    return by_place(gather_near(values))


def gather_tokens(values, bit):
    half = values.shape[0] // 2
    cross = swap_cross(values)
    over = swap_blk(values, bit)
    first = swap_blk(cross[:half], bit)
    second = swap_cross(over[half:])
    chip = jnp.concatenate([values, cross, over, first, second])
    return jnp.concatenate([chip, swap_core(chip)])


def scatter_tokens(values, bit):
    half_all = values.shape[0] // 2
    rows = half_all // 4
    half = rows // 2
    chip = wide(values[:half_all]) + wide(swap_core(low(values[half_all:])))
    own, cross, over, far = (chip[rows * i : rows * (i + 1)] for i in range(4))
    far = low(far)
    first = wide(swap_blk(far[:half], bit))
    second = wide(swap_cross(far[half:]))
    cross = low(jnp.concatenate([cross[:half] + first, cross[half:]]))
    over = low(jnp.concatenate([over[:half], over[half:] + second]))
    return own + wide(swap_cross(cross)) + wide(swap_blk(over, bit))


def angles_of(position):
    half = HD // 2
    freqs = ROPE_BASE ** (-2.0 * jnp.arange(half, dtype=jnp.float32) / HD)
    return position.astype(jnp.float32)[:, None] * freqs[None, :]


def rotate_by(values, cosine, sine):
    half = HD // 2
    first_half = values[..., :half]
    second_half = values[..., half:]
    return jnp.concatenate(
        [first_half * cosine - second_half * sine, second_half * cosine + first_half * sine],
        axis=-1,
    )


def after(values, anchor):
    return lax.optimization_barrier((values, anchor))[0]


def gather_step(values, done, bit):
    other = swap_blk(values, bit)
    mine = blk_bit(bit)
    axis = sum(1 for d in done if d > bit)
    return jnp.stack(
        [jnp.where(mine, other, values), jnp.where(mine, values, other)], axis=axis
    )


def gather_two_ways(values, bits, team):
    lows = [bit for bit in bits if bit < team]
    values = gather_step(values, [], bits[0])
    half = values.shape[-1] // 2
    parts = []
    for part, order in (
        (values[..., :half], [team] + lows),
        (values[..., half:], lows + [team]),
    ):
        done = [bits[0]]
        for bit in order:
            part = gather_step(part, done, bit)
            done.append(bit)
        parts.append(part)
    return jnp.concatenate(parts, axis=-1)


def scatter_two_ways(values, bits, team):
    lows = [bit for bit in bits if bit < team][::-1]
    half = values.shape[-1] // 2
    parts = [
        scatter_bits(values[..., :half], bits, lows + [team]),
        scatter_bits(values[..., half:], bits, [team] + lows),
    ]
    return scatter_bits(jnp.concatenate(parts, axis=-1), bits[:1], bits[:1])


def gather_near_stacked(values):
    both = jnp.stack([values, swap_cross(values)])
    return jnp.concatenate([both, swap_core(both)])


def on_device(
    tokens,
    cotangent,
    segment_ids,
    position_ids,
    w_attend,
    w_out,
    w_gate,
    w_up,
    w_down,
    small_params,
    first_attend,
    first_out,
    first_gate,
    first_up,
    first_down,
    first_small,
    second_attend,
    second_out,
    second_gate,
    second_up,
    second_down,
    second_small,
):
    rows_here, block_len = tokens.shape[:2]
    blk_count = lax.axis_size("blk")
    seq_len = block_len * blk_count
    token_count = rows_here * block_len
    grp = lax.axis_index("grp")
    blk = lax.axis_index("blk")
    cross_id, core_id = grp // 2, grp % 2
    strip_heads = H // 4
    strip_q = strip_heads * HD
    bits = bits_of(blk_count)
    team = blk_count // 4
    lows = [bit for bit in bits if bit < team]
    spread = [bits[0]] + lows
    low_shape = (2,) * len(lows)
    in_team = blk_bit(team).astype(jnp.int32)
    weight_rows = w_gate.shape[0]
    ff_block = w_down.shape[0]
    quarter = ff_block // 4
    ff_here = quarter * blk_count // 2

    ids = jnp.stack([grp, in_team])
    flat_low = tokens.reshape(token_count, D)
    dy_low = cotangent.reshape(token_count, D)
    positions = position_ids.reshape(token_count)
    kv_at = HQD + HD * cross_id + KVD * core_id
    strip_local = low(
        jnp.concatenate(
            [
                lax.dynamic_slice_in_dim(w_attend, strip_q * grp, strip_q, 1),
                lax.dynamic_slice_in_dim(w_attend, kv_at, HD, 1),
            ],
            axis=1,
        )
    )
    small_send = jnp.concatenate([low(small_params), low(segment_ids.reshape(token_count))])
    strip_first = gather_step(strip_local, [], bits[0])
    strip_parts = []
    cut = (strip_q + HD) // 2
    for part, order in (
        (strip_first[..., :cut], [team] + lows),
        (strip_first[..., cut:], lows + [team]),
    ):
        done = [bits[0]]
        for bit in order:
            part = gather_step(part, done, bit)
            done.append(bit)
        strip_parts.append(part)
    strip = jnp.concatenate(strip_parts, axis=-1).reshape(D, strip_q + HD)
    near_tokens = jnp.concatenate(gather_near(flat_low))
    near_positions = jnp.concatenate(gather_near(positions))
    small_all = gather_bits(small_send, bits).reshape(blk_count, -1)
    vector = wide(small_all[:, : small_params.shape[0]].reshape(-1))
    gain_one = vector[:D]
    gain_two = vector[D : 2 * D]
    bias = vector[2 * D :]
    strip_bias = jnp.concatenate(
        [
            lax.dynamic_slice_in_dim(bias, strip_q * grp, strip_q, 0),
            lax.dynamic_slice_in_dim(bias, kv_at, HD, 0),
        ]
    )
    seg_all = small_all[:, small_params.shape[0] :].astype(jnp.int32)
    seg_all = seg_all.reshape(blk_count, rows_here, block_len)
    seg_key = jnp.broadcast_to(
        seg_all.transpose(1, 0, 2).reshape(rows_here, seq_len)[:, :, None], (rows_here, seq_len, HD)
    )
    seg_query = jnp.broadcast_to(segment_ids[:, None, :], (rows_here, 8, block_len))
    first_blk = jnp.sum((seg_all[:, :, -1] < segment_ids[None, :, 0]).astype(jnp.int32), axis=0)
    attend_ids = jnp.concatenate([blk[None], first_blk])

    near_wide = wide(near_tokens)
    near_one = low(norm_apply(near_wide, gain_one))
    mixed = jnp.dot(near_one, strip, preferred_element_type=jnp.float32) + strip_bias
    angles = angles_of(near_positions)[:, None, :]
    turned = jnp.arange(strip_heads + 1)[None, :, None] < strip_heads + 1 - core_id
    angles = jnp.where(turned, angles, 0.0)
    strip_out = low(
        rotate_by(
            mixed.reshape(4 * token_count, strip_heads + 1, HD), jnp.cos(angles), jnp.sin(angles)
        )
    ).reshape(4, token_count, strip_q + HD)
    strips = by_place(
        [
            strip_out[0],
            swap_core(strip_out[1]),
            swap_cross(strip_out[2]),
            swap_diag(strip_out[3]),
        ]
    )
    query = jnp.concatenate([part[:, :strip_q] for part in strips], axis=1)
    key_value = jnp.concatenate([strips[k][:, strip_q:] for k in (0, 2, 1, 3)], axis=1)
    key_value = key_value.reshape(rows_here, block_len, 2 * KVD)
    kv_all = gather_two_ways(key_value, bits, team).reshape((blk_count,) + key_value.shape)

    down_local = low(lax.dynamic_slice_in_dim(w_down, quarter * grp, quarter, 0))
    down_first = swap_blk(after(down_local, strip_first), bits[0])
    gate_two, up_two = pick_columns(ids, w_gate, w_up, blk_count)
    mine_team = blk_bit(team)

    def pair_of(two):
        got = swap_blk(two[1], team)
        return jnp.stack([jnp.where(mine_team, got, two[0]), jnp.where(mine_team, two[0], got)])

    gate_pair = pair_of(after(gate_two, strip_parts))
    up_pair = pair_of(after(up_two, strip_parts))

    def place(values, other, done, bit):
        mine = blk_bit(bit)
        axis = sum(1 for d in done if d > bit)
        return jnp.stack(
            [jnp.where(mine, other, values), jnp.where(mine, values, other)], axis=axis
        )

    def finish(values, done):
        for bit in lows:
            values = place(values, swap_blk(values, bit), done, bit)
            done = done + [bit]
        return values

    gate_first = swap_blk(after(gate_pair, strip_out), bits[0])
    down_here = finish(place(down_local, after(down_first, strip_out), [], bits[0]), [bits[0]])
    down_here = down_here.reshape(ff_here, D)
    up_first = swap_blk(after(up_pair, kv_all), bits[0])
    gate_here = finish(place(gate_pair, after(gate_first, kv_all), [team], bits[0]), [team, bits[0]])
    gate_here = gate_here.reshape(D, ff_here)

    out_local = low(lax.dynamic_slice_in_dim(w_out, strip_q * grp, strip_q, 1))
    out_strip = gather_bits(after(out_local, strip_first), bits).reshape(HQD, strip_q)
    out_full = jnp.concatenate(gather_grp(out_strip), axis=1)
    dy_team = gather_tokens(dy_low, team)

    att_in, lse = attend(attend_ids, query, kv_all, seg_key, seg_query, block_len)

    flat = wide(flat_low)
    resid = flat + jnp.dot(att_in, out_full, preferred_element_type=jnp.float32)
    h_two = low(norm_apply(resid, gain_two))
    h_team = gather_tokens(h_two, team)
    up_here = finish(place(up_pair, after(up_first, h_two), [team], bits[0]), [team, bits[0]])
    up_here = up_here.reshape(D, ff_here)
    d_hidden = right_transposed(dy_team, down_here)
    gate = jnp.dot(h_team, gate_here, preferred_element_type=jnp.float32)
    up_proj = jnp.dot(h_team, up_here, preferred_element_type=jnp.float32)
    hidden = low(swish_product(gate, up_proj))
    down_grad = low(left_product(hidden, dy_team)).reshape((2,) + low_shape + (quarter, D))
    swish_value, swish_back = jax.vjp(swish_product, gate, up_proj)
    d_gate, d_up = swish_back(d_hidden)
    d_gate = low(d_gate)
    d_up = low(d_up)
    d_htwo_part = right_transposed(d_gate, gate_here) + right_transposed(d_up, up_here)
    d_htwo = scatter_tokens(d_htwo_part, team)

    def share_start(grad, axes):
        bit = lows[-1]
        axis = axes.index(bit)
        mine = blk_bit(bit).astype(jnp.int32)
        keep = lax.dynamic_index_in_dim(grad, mine, axis, keepdims=False)
        send = lax.dynamic_index_in_dim(grad, 1 - mine, axis, keepdims=False)
        return keep, swap_blk(send, bit)

    def share_mid(keep, got, axes):
        values = low(wide(keep) + wide(got))
        axes = [bit for bit in axes if bit != lows[-1]]
        for bit in lows[-2::-1]:
            values = scatter_bits(values, axes, [bit])
            axes = [b for b in axes if b != bit]
        mine = blk_bit(bits[0]).astype(jnp.int32)
        keep = lax.dynamic_index_in_dim(values, mine, 0, keepdims=False)
        send = lax.dynamic_index_in_dim(values, 1 - mine, 0, keepdims=False)
        return keep, swap_blk(send, bits[0])

    def share_columns(values):
        keep = lax.dynamic_index_in_dim(values, in_team, 0, keepdims=False)
        send = lax.dynamic_index_in_dim(values, 1 - in_team, 0, keepdims=False)
        got = swap_blk(send, team)
        return jnp.stack(
            [jnp.where(mine_team, got, keep), jnp.where(mine_team, keep, got)]
        )

    down_axes = [bits[0]] + lows
    down_keep, down_got = share_start(down_grad, down_axes)
    late_gate, late_up = after((d_gate, d_up), d_htwo_part)
    column_shape = (2, 2) + low_shape + (weight_rows, ff_here)
    gate_grad = low(left_product(h_team, late_gate)).reshape(column_shape)
    gate_keep, gate_got = share_start(gate_grad, bits)
    up_grad = low(left_product(h_team, late_up)).reshape(column_shape)
    up_keep, up_got = share_start(up_grad, bits)
    down_keep, down_got = share_mid(*after((down_keep, down_got), d_gate), down_axes)
    out_part = jnp.dot(after(hidden, up_grad), down_here, preferred_element_type=jnp.float32)

    norm_value_two, norm_back_two = jax.vjp(norm_apply, resid, gain_two)
    d_resid_norm, grad_gain_two = norm_back_two(d_htwo)
    d_resid = wide(dy_low) + d_resid_norm
    d_att = low(d_resid)

    d_attended = low(right_transposed(d_att, out_full))
    own_angles = angles_of(positions)
    cosine, sine = jnp.cos(own_angles), jnp.sin(own_angles)
    d_query, dkv = attend_back(
        attend_ids,
        query,
        kv_all,
        seg_key,
        seg_query,
        att_in,
        d_attended,
        lse,
        jnp.concatenate([cosine, cosine], axis=1),
        jnp.concatenate([sine, sine], axis=1),
        block_len,
    )
    gate_keep, gate_got = share_mid(*after((gate_keep, gate_got), d_attended), bits)
    share_down = low(wide(down_keep) + wide(after(down_got, d_query)))
    dkv = dkv.reshape((2,) * len(bits) + (rows_here, block_len, 2 * KVD))
    dkv = wide(scatter_two_ways(dkv, bits, team)).reshape(token_count, 2, KVH, HD)
    d_key = low(rotate_by(dkv[:, 0], cosine[:, None], -sine[:, None]))
    d_value = low(dkv[:, 1])
    up_keep, up_got = share_mid(*after((up_keep, up_got), d_query), bits)
    out_tokens = low(resid + scatter_tokens(after(out_part, d_query), team))

    def to_strips(parts):
        parts = by_place(parts)
        return jnp.concatenate(
            [parts[0], swap_core(parts[1]), swap_cross(parts[2]), swap_diag(parts[3])]
        )

    near_dq = to_strips([d_query[:, strip_q * k : strip_q * (k + 1)] for k in range(4)])
    block_shape = (2,) * len(bits) + (weight_rows, -1)
    share_query = scatter_bits(
        low(left_product(near_one, near_dq)).reshape(block_shape), bits, bits[::-1]
    )
    near_dkv = to_strips([(d_value if k % 2 else d_key)[:, k // 2] for k in range(4)])
    share_kv = scatter_bits(
        low(left_product(near_one, near_dkv)).reshape(block_shape), bits, bits[::-1]
    )
    grad_bias = jnp.concatenate(
        [
            jnp.sum(wide(part), axis=0)
            for part in (d_query, d_key.reshape(token_count, KVD), d_value.reshape(token_count, KVD))
        ]
    )
    near_hone = right_transposed(near_dq, strip[:, :strip_q]) + right_transposed(
        near_dkv, strip[:, strip_q:]
    )
    near_rms = lax.rsqrt(jnp.mean(near_wide * near_wide, axis=-1, keepdims=True) + NORM_EPS)
    gain_one_part = jnp.sum(near_hone * near_wide * near_rms, axis=0)

    near_att = jnp.concatenate(gather_near(att_in))
    near_datt = to_strips([d_att[:, strip_q * k : strip_q * (k + 1)] for k in range(4)])
    share_out = scatter_bits(
        low(left_product(near_att, after(near_datt, d_query))).reshape(block_shape),
        bits,
        bits[::-1],
    )

    vector_term = jnp.concatenate([gain_one_part, grad_gain_two, grad_bias])
    vector_term = vector_term + swap_cross(vector_term)
    vector_term = vector_term + swap_core(vector_term)
    vector_term = vector_term.reshape((2,) * len(bits) + (-1,))
    axes = list(bits)
    for bit in bits[::-1]:
        axis = axes.index(bit)
        mine = blk_bit(bit).astype(jnp.int32)
        keep = lax.dynamic_index_in_dim(vector_term, mine, axis, keepdims=False)
        send = lax.dynamic_index_in_dim(vector_term, 1 - mine, axis, keepdims=False)
        vector_term = keep + swap_blk(send, bit)
        axes.remove(bit)
    share_vector = vector_term

    share_gate = share_columns(low(wide(gate_keep) + wide(after(gate_got, d_key))))
    near_gate = gather_near_stacked(share_gate)
    share_up = share_columns(low(wide(up_keep) + wide(after(up_got, near_dkv))))
    near_up = gather_near_stacked(share_up)
    grad_down = jnp.concatenate(gather_grp(share_down), axis=0)
    grad_out = jnp.concatenate(gather_grp(share_out), axis=1)
    query_parts = gather_grp(share_query)
    kv_parts = gather_grp(share_kv)
    grad_attend = jnp.concatenate(query_parts + [kv_parts[k] for k in (0, 2, 1, 3)], axis=1)

    square_sum = square_total(
        [
            wide(s)
            for s in (share_query, share_kv, share_out, share_gate, share_up, share_down)
        ]
    ) + 0.25 * jnp.sum(share_vector * share_vector)
    square_sum = jnp.full((8, 128), square_sum)
    for bit in bits:
        square_sum = square_sum + swap_blk(square_sum, bit)
    square_sum = square_sum + swap_cross(square_sum)
    square_sum = square_sum + swap_core(square_sum)
    grad_norm = jnp.sqrt(square_sum[0, 0])
    factor = jnp.minimum(1.0, CLIP_NORM / (grad_norm + 1e-06))

    half = low(near_hone[token_count : 2 * token_count]), low(near_hone[3 * token_count :])
    other = wide(swap_core(jnp.concatenate(half)))
    d_hone = near_hone[:token_count] + other[:token_count]
    d_hone = d_hone + wide(
        swap_cross(low(near_hone[2 * token_count : 3 * token_count] + other[token_count:]))
    )
    norm_value_one, norm_back_one = jax.vjp(norm_apply, flat, gain_one)
    d_flat_norm, unused_gain = norm_back_one(d_hone)
    grad_tokens = low(d_resid + d_flat_norm)

    new_first_gate, new_second_gate, new_gate = adam_columns(
        ids, factor[None], near_gate, w_gate, first_gate, second_gate, blk_count, RATE_GATE, WEIGHT_DECAY
    )
    new_first_up, new_second_up, new_up = adam_columns(
        ids, factor[None], near_up, w_up, first_up, second_up, blk_count, RATE_GATE, WEIGHT_DECAY
    )
    new_first_attend, new_second_attend, new_attend = adam_step(
        w_attend, factor * wide(grad_attend), first_attend, second_attend, RATE_ATTEND, WEIGHT_DECAY
    )
    new_first_out, new_second_out, new_out = adam_step(
        w_out, factor * wide(grad_out), first_out, second_out, RATE_OUT, WEIGHT_DECAY
    )
    new_first_down, new_second_down, new_down = adam_step(
        w_down, factor * wide(grad_down), first_down, second_down, RATE_DOWN, WEIGHT_DECAY
    )
    new_first_small, new_second_small, new_small = adam_step(
        small_params, factor * share_vector, first_small, second_small, RATE_VECTOR, 0.0
    )
    return (
        out_tokens.reshape(rows_here, block_len, D),
        grad_tokens.reshape(rows_here, block_len, D),
        grad_norm,
        new_first_attend,
        new_second_attend,
        new_attend,
        new_first_out,
        new_second_out,
        new_out,
        new_first_gate,
        new_second_gate,
        new_gate,
        new_first_up,
        new_second_up,
        new_up,
        new_first_down,
        new_second_down,
        new_down,
        new_first_small,
        new_second_small,
        new_small,
    )


def solution(mesh):
    placed = (
        P("grp", "blk", None),
        P("grp", "blk", None),
        P("grp", "blk"),
        P("grp", "blk"),
        P("blk", None),
        P("blk", None),
        P("blk", None),
        P("blk", None),
        P("blk", None),
        P("blk"),
        P("blk", None),
        P("blk", None),
        P("blk", None),
        P("blk", None),
        P("blk", None),
        P("blk"),
        P("blk", None),
        P("blk", None),
        P("blk", None),
        P("blk", None),
        P("blk", None),
        P("blk"),
    )
    return jax.shard_map(
        on_device,
        mesh=mesh,
        in_specs=placed,
        out_specs=(
            P("grp", "blk", None),
            P("grp", "blk", None),
            P(),
            P("blk", None),
            P("blk", None),
            P("blk", None),
            P("blk", None),
            P("blk", None),
            P("blk", None),
            P("blk", None),
            P("blk", None),
            P("blk", None),
            P("blk", None),
            P("blk", None),
            P("blk", None),
            P("blk", None),
            P("blk", None),
            P("blk", None),
            P("blk"),
            P("blk"),
            P("blk"),
        ),
        check_vma=False,
    )
```

```python
import functools

import jax
import jax.numpy as jnp
from jax import lax
from jax.experimental import pallas as pl
from jax.experimental.pallas import tpu as pltpu
from jax.sharding import PartitionSpec as P

D = 1536
FF = 8960
H = 12
KVH = 2
HD = 128
STEP = 10
HQD = 1536
KVD = 256


NORM_EPS = 1e-06
ROPE_BASE = 10000.0
CLIP_NORM = 1.0
BETA_FIRST = 0.9
BETA_SECOND = 0.95
ADAM_EPS = 1e-08
WEIGHT_DECAY = 0.1
RATE_ATTEND = 0.06
RATE_OUT = 0.5
RATE_GATE = 0.06
RATE_DOWN = 0.03
RATE_VECTOR = 0.5
NEG_LARGE = -1e30
LOG2E = 1.4426950408889634
VMEM = 48 * 1024 * 1024


def norm_apply(values, gain):
    return values * lax.rsqrt(jnp.mean(values * values, axis=-1, keepdims=True) + NORM_EPS) * gain


def swish_product(gate, up_proj):
    return jax.nn.silu(gate) * up_proj


def left_product(left_side, right_side):
    return lax.dot_general(
        left_side, right_side, (((0,), (0,)), ((), ())), preferred_element_type=jnp.float32
    )


def right_transposed(left_side, right_side):
    return lax.dot_general(
        left_side, right_side, (((1,), (1,)), ((), ())), preferred_element_type=jnp.float32
    )


def square_total(arrays):
    return sum((jnp.sum(member * member) for member in arrays))


def adam_step(weight, grad, first, second, rate, decay):
    first_new = BETA_FIRST * first + (1.0 - BETA_FIRST) * grad
    second_new = BETA_SECOND * second + (1.0 - BETA_SECOND) * grad * grad
    first_hat = first_new / (1.0 - BETA_FIRST**STEP)
    second_hat = second_new / (1.0 - BETA_SECOND**STEP)
    weight_new = weight - rate * (first_hat / (jnp.sqrt(second_hat) + ADAM_EPS) + decay * weight)
    return (first_new, second_new, weight_new)


def strip_starts(blk_count, team_bit, grp, quarter):
    per = blk_count // 4
    return [
        (((high * 2 + team_bit) * per + small) * 4 + grp) * quarter
        for high in range(2)
        for small in range(per)
    ]

def pick_body(blk_count, ids, gate_ref, up_ref, out_ref):
    quarter = FF // blk_count // 4
    for k in range(4):
        @pl.when(ids[0] == k)
        def _(k=k):
            for which, src in enumerate((gate_ref, up_ref)):
                for bit in range(2):
                    parts = [src[:, s:s + quarter] for s in strip_starts(blk_count, bit, k, quarter)]
                    out_ref[ids[1] ^ bit, which] = jnp.concatenate(parts, axis=1).astype(jnp.bfloat16)

def pick_columns(ids, gate, up, blk_count):
    rows = gate.shape[0]
    step = 48 if rows % 48 == 0 else rows
    wide_here = FF // 8
    spec = pl.BlockSpec((step, FF), lambda i, ids: (i, 0))
    out = pl.BlockSpec((2, 2, step, wide_here), lambda i, ids: (0, 0, i, 0))
    shape = jax.ShapeDtypeStruct((2, 2, rows, wide_here), jnp.bfloat16)
    return pl.pallas_call(
        functools.partial(pick_body, blk_count),
        grid_spec=pltpu.PrefetchScalarGridSpec(
            num_scalar_prefetch=1, grid=(rows // step,), in_specs=[spec, spec], out_specs=out),
        out_shape=shape,
        compiler_params=pltpu.CompilerParams(vmem_limit_bytes=VMEM),
        cost_estimate=pl.CostEstimate(flops=0, bytes_accessed=rows * FF * 10, transcendentals=0),
        name="pick_columns",
    )(ids, gate, up)

def near_at(away):
    return (away & 1) * 2 + (away >> 1)


def adam_body(blk_count, rate, decay, ids, factor_ref, grad_ref, w_ref, m_ref, v_ref, m_out, v_out, w_out):
    quarter = FF // blk_count // 4
    per = blk_count // 4
    parts = []
    grads = [[grad_ref[near_at(ids[0] ^ k), bit] for bit in range(2)] for k in range(4)]
    for high in range(2):
        for bit in range(2):
            for small in range(per):
                at = (high * per + small) * quarter
                for k in range(4):
                    parts.append(grads[k][bit][:, at:at + quarter])
    grad = jnp.concatenate(parts, axis=1).astype(jnp.float32) * factor_ref[0]
    m, v, w = adam_step(w_ref[...], grad, m_ref[...], v_ref[...], rate, decay)
    m_out[...] = m
    v_out[...] = v
    w_out[...] = w

def adam_columns(ids, factor, grad, w, m, v, blk_count, rate, decay):
    rows = w.shape[0]
    step = 32 if rows % 32 == 0 else rows
    spec = pl.BlockSpec((step, FF), lambda i, ids: (i, 0))
    shape = jax.ShapeDtypeStruct((rows, FF), jnp.float32)
    return pl.pallas_call(
        functools.partial(adam_body, blk_count, rate, decay),
        grid_spec=pltpu.PrefetchScalarGridSpec(
            num_scalar_prefetch=1, grid=(rows // step,),
            in_specs=[pl.BlockSpec(memory_space=pltpu.SMEM),
                      pl.BlockSpec((4, 2, step, FF // 8), lambda i, ids: (0, 0, i, 0)), spec, spec, spec],
            out_specs=[spec, spec, spec]),
        out_shape=[shape] * 3,
        compiler_params=pltpu.CompilerParams(vmem_limit_bytes=VMEM),
        cost_estimate=pl.CostEstimate(flops=rows * FF * 20, bytes_accessed=rows * FF * 26, transcendentals=rows * FF),
        name="adam_columns",
    )(ids, factor, grad, w, m, v)

def nt(a, b, **kw):
    return lax.dot_general(a, b, (((1,), (1,)), ((), ())), preferred_element_type=jnp.float32, **kw)

def tn(a, b, **kw):
    return lax.dot_general(a, b, (((0,), (0,)), ((), ())), preferred_element_type=jnp.float32, **kw)

def stack_heads(ref, kvh, group):
    return jnp.concatenate([ref[:, HD * (kvh * group + i): HD * (kvh * group + i + 1)] for i in range(group)], axis=0)

def hidden_from(seg_key_ref, seg_query_ref, first, chunk, block_len, blk):
    key = first + lax.broadcasted_iota(jnp.int32, (chunk, block_len), 0)
    query = blk * block_len + lax.broadcasted_iota(jnp.int32, (chunk, block_len), 1)
    seg_key = seg_key_ref[pl.ds(first, chunk), :]
    counts = jnp.logical_and(key <= query, seg_key == seg_query_ref[0:1, :])
    return jnp.where(counts, 0.0, NEG_LARGE)

def attend_body(chunk, ids, q_ref, k_ref, v_ref, seg_key_ref, seg_query_ref, o_ref, lse_ref, m_s, l_s, acc_s):
    block_len = q_ref.shape[0]
    group = H // KVH
    row = pl.program_id(0)
    per = chunk // block_len
    scale = HD ** (-0.5) * LOG2E
    start = ids[1 + row] // per
    stop = ids[0] // per + 1
    for kvh in range(KVH):
        q = stack_heads(q_ref, kvh, group)
        m_s[...] = jnp.full_like(m_s, NEG_LARGE)
        l_s[...] = jnp.zeros_like(l_s)
        acc_s[...] = jnp.zeros_like(acc_s)

        def step(c, carry):
            keys = k_ref[pl.ds(c * per, per), :, HD * kvh: HD * (kvh + 1)].reshape(chunk, HD)
            vals = v_ref[pl.ds(c * per, per), :, HD * kvh: HD * (kvh + 1)].reshape(chunk, HD)
            bias = hidden_from(seg_key_ref, seg_query_ref, c * chunk, chunk, block_len, ids[0])
            s = nt(keys, q) * scale + jnp.concatenate([bias] * group, axis=1)
            old = m_s[0:1, :]
            new = jnp.maximum(old, jnp.max(s, axis=0, keepdims=True))
            p = jnp.exp2(s - new)
            fade = jnp.exp2(old - new)
            l_s[0:1, :] = l_s[0:1, :] * fade + jnp.sum(p, axis=0, keepdims=True)
            acc_s[...] = acc_s[...] * fade + tn(vals, p.astype(jnp.bfloat16))
            m_s[0:1, :] = new
            return carry

        lax.fori_loop(start, stop, step, 0)
        total = l_s[0:1, :]
        out = (acc_s[...] * (1.0 / total)).T
        for i in range(group):
            o_ref[:, HD * (kvh * group + i): HD * (kvh * group + i + 1)] = out[block_len * i: block_len * (i + 1), :].astype(jnp.bfloat16)
        lse_ref[kvh] = jnp.broadcast_to(m_s[0:1, :] + jnp.log2(total), (8, group * block_len))

def attend(ids, q, kv, seg_key, seg_query, block_len):
    blk_count, rows = kv.shape[:2]
    group = H // KVH
    chunk = 2 * block_len
    many = group * block_len
    return pl.pallas_call(
        functools.partial(attend_body, chunk),
        grid_spec=pltpu.PrefetchScalarGridSpec(
            num_scalar_prefetch=1, grid=(rows,),
            in_specs=[
                pl.BlockSpec((block_len, HQD), lambda r, ids: (r, 0)),
                pl.BlockSpec((blk_count, None, block_len, KVD), lambda r, ids: (0, r, 0, 0)),
                pl.BlockSpec((blk_count, None, block_len, KVD), lambda r, ids: (0, r, 0, 1)),
                pl.BlockSpec((None, blk_count * block_len, HD), lambda r, ids: (r, 0, 0)),
                pl.BlockSpec((None, 8, block_len), lambda r, ids: (r, 0, 0)),
            ],
            out_specs=[
                pl.BlockSpec((block_len, HQD), lambda r, ids: (r, 0)),
                pl.BlockSpec((None, KVH, 8, many), lambda r, ids: (r, 0, 0, 0)),
            ],
            scratch_shapes=[pltpu.VMEM((8, many), jnp.float32), pltpu.VMEM((8, many), jnp.float32), pltpu.VMEM((HD, many), jnp.float32)]),
        out_shape=[
            jax.ShapeDtypeStruct((rows * block_len, HQD), jnp.bfloat16),
            jax.ShapeDtypeStruct((rows, KVH, 8, many), jnp.float32),
        ],
        compiler_params=pltpu.CompilerParams(vmem_limit_bytes=VMEM),
        cost_estimate=pl.CostEstimate(flops=4 * rows * H * block_len * blk_count * block_len * HD, bytes_accessed=8 * 2**20, transcendentals=rows * H * block_len * blk_count * block_len),
        name="attend",
    )(ids, q, kv, kv, seg_key, seg_query)

def turn_back(u, cosine, sine):
    lane = lax.broadcasted_iota(jnp.int32, u.shape, 1)
    other = pltpu.roll(u, HD // 2, 1)
    return u * cosine + jnp.where(lane < HD // 2, other, -other) * sine

def attend_back_body(chunk, ids, q_ref, k_ref, v_ref, seg_key_ref, seg_query_ref, o_ref, do_ref, lse_ref, cos_ref, sin_ref, dq_ref, dkv_ref, dq_s):
    block_len = q_ref.shape[0]
    group = H // KVH
    row = pl.program_id(0)
    per = chunk // block_len
    plain = HD ** (-0.5)
    scale = plain * LOG2E
    start = ids[1 + row] // per
    stop = ids[0] // per + 1
    dkv_ref[...] = jnp.zeros_like(dkv_ref)
    for kvh in range(KVH):
        q = stack_heads(q_ref, kvh, group)
        do = stack_heads(do_ref, kvh, group)
        o = stack_heads(o_ref, kvh, group)
        both = do.astype(jnp.float32) * o.astype(jnp.float32)
        delta = nt(jnp.ones((8, HD), jnp.float32), both, precision=lax.Precision.HIGHEST)[0:1, :]
        lse = lse_ref[kvh][0:1, :]
        dq_s[...] = jnp.zeros_like(dq_s)

        def step(c, carry):
            keys = k_ref[pl.ds(c * per, per), :, HD * kvh: HD * (kvh + 1)].reshape(chunk, HD)
            vals = v_ref[pl.ds(c * per, per), :, HD * kvh: HD * (kvh + 1)].reshape(chunk, HD)
            bias = hidden_from(seg_key_ref, seg_query_ref, c * chunk, chunk, block_len, ids[0])
            s = nt(keys, q) * scale + jnp.concatenate([bias] * group, axis=1)
            p = jnp.exp2(s - lse)
            dp = nt(vals, do)
            ds = (p * (dp - delta)).astype(jnp.bfloat16)
            dk = jnp.dot(ds, q, preferred_element_type=jnp.float32) * plain
            dv = jnp.dot(p.astype(jnp.bfloat16), do, preferred_element_type=jnp.float32)
            dkv_ref[pl.ds(c * per, per), :, HD * kvh: HD * (kvh + 1)] = dk.astype(jnp.bfloat16).reshape(per, block_len, HD)
            dkv_ref[pl.ds(c * per, per), :, KVD + HD * kvh: KVD + HD * (kvh + 1)] = dv.astype(jnp.bfloat16).reshape(per, block_len, HD)
            dq_s[...] += tn(ds, keys)
            return carry

        lax.fori_loop(start, stop, step, 0)
        cosine, sine = cos_ref[...], sin_ref[...]
        for i in range(group):
            u = dq_s[block_len * i: block_len * (i + 1), :] * plain
            at = HD * (kvh * group + i)
            dq_ref[:, at: at + HD] = turn_back(u, cosine, sine).astype(jnp.bfloat16)

def attend_back(ids, q, kv, seg_key, seg_query, o, do, lse, cosine, sine, block_len):
    blk_count, rows = kv.shape[:2]
    group = H // KVH
    chunk = 2 * block_len
    many = group * block_len
    per_row = pl.BlockSpec((block_len, HQD), lambda r, ids: (r, 0))
    turn = pl.BlockSpec((block_len, HD), lambda r, ids: (r, 0))
    return pl.pallas_call(
        functools.partial(attend_back_body, chunk),
        grid_spec=pltpu.PrefetchScalarGridSpec(
            num_scalar_prefetch=1, grid=(rows,),
            in_specs=[
                per_row,
                pl.BlockSpec((blk_count, None, block_len, KVD), lambda r, ids: (0, r, 0, 0)),
                pl.BlockSpec((blk_count, None, block_len, KVD), lambda r, ids: (0, r, 0, 1)),
                pl.BlockSpec((None, blk_count * block_len, HD), lambda r, ids: (r, 0, 0)),
                pl.BlockSpec((None, 8, block_len), lambda r, ids: (r, 0, 0)),
                per_row, per_row,
                pl.BlockSpec((None, KVH, 8, many), lambda r, ids: (r, 0, 0, 0)),
                turn, turn,
            ],
            out_specs=[per_row, pl.BlockSpec((blk_count, None, block_len, 2 * KVD), lambda r, ids: (0, r, 0, 0))],
            scratch_shapes=[pltpu.VMEM((many, HD), jnp.float32)]),
        out_shape=[
            jax.ShapeDtypeStruct((rows * block_len, HQD), jnp.bfloat16),
            jax.ShapeDtypeStruct((blk_count, rows, block_len, 2 * KVD), jnp.bfloat16),
        ],
        compiler_params=pltpu.CompilerParams(vmem_limit_bytes=VMEM),
        cost_estimate=pl.CostEstimate(flops=10 * rows * H * block_len * blk_count * block_len * HD, bytes_accessed=12 * 2**20, transcendentals=rows * H * block_len * blk_count * block_len),
        name="attend_back",
    )(ids, q, kv, kv, seg_key, seg_query, o, do, lse, cosine, sine)

def nn(a, b):
    return jnp.dot(a, b, preferred_element_type=jnp.float32)


def middle_body(h_ref, dy_ref, wg_ref, wu_ref, wd_ref, hid_ref, dg_ref, du_ref, dh_ref):
    h = h_ref[...]
    gate = nn(h, wg_ref[...])
    up = nn(h, wu_ref[...])
    sig = 1.0 / (1.0 + jnp.exp(-gate))
    silu = gate * sig
    hid_ref[...] = (silu * up).astype(jnp.bfloat16)
    dhid = nt(dy_ref[...], wd_ref[...])
    dg = (dhid * up * sig * (1.0 + gate * (1.0 - sig))).astype(jnp.bfloat16)
    du = (dhid * silu).astype(jnp.bfloat16)
    dg_ref[...] = dg
    du_ref[...] = du
    dh_ref[...] = (nt(dg, wg_ref[...]) + nt(du, wu_ref[...])).astype(jnp.bfloat16)

def middle(h, dy, wg, wu, wd, step=256):
    T, D = h.shape
    F = wg.shape[1]
    row = pl.BlockSpec((step, D), lambda i: (i, 0))
    rowf = pl.BlockSpec((step, F), lambda i: (i, 0))
    whole = lambda a: pl.BlockSpec(a.shape, lambda i: (0, 0), pipeline_mode=pl.Buffered(1))
    return pl.pallas_call(
        middle_body, grid=(T // step,),
        in_specs=[row, row, whole(wg), whole(wu), whole(wd)],
        out_specs=[rowf, rowf, rowf, row],
        out_shape=[jax.ShapeDtypeStruct((T, F), jnp.bfloat16)] * 3 + [jax.ShapeDtypeStruct((T, D), jnp.bfloat16)],
        compiler_params=pltpu.CompilerParams(vmem_limit_bytes=VMEM),
        cost_estimate=pl.CostEstimate(flops=10 * T * D * F, bytes_accessed=40 * 2**20, transcendentals=T * F),
        name="middle")(h, dy, wg, wu, wd)

def two_grads_body(h_ref, a_ref, b_ref, ga_ref, gb_ref):
    h = h_ref[...]
    ga_ref[...] = tn(h, a_ref[...]).astype(jnp.bfloat16)
    gb_ref[...] = tn(h, b_ref[...]).astype(jnp.bfloat16)

def two_grads(h, a, b, step=256):
    T, D = h.shape
    F = a.shape[1]
    col = pl.BlockSpec((T, step), lambda i: (0, i))
    whole = lambda v: pl.BlockSpec(v.shape, lambda i: (0, 0), pipeline_mode=pl.Buffered(1))
    out = pl.BlockSpec((step, F), lambda i: (i, 0))
    return pl.pallas_call(two_grads_body, grid=(D // step,), in_specs=[col, whole(a), whole(b)], out_specs=[out, out],
        out_shape=[jax.ShapeDtypeStruct((D, F), jnp.bfloat16)] * 2,
        compiler_params=pltpu.CompilerParams(vmem_limit_bytes=VMEM),
        cost_estimate=pl.CostEstimate(flops=4 * T * D * F, bytes_accessed=24 * 2**20, transcendentals=0),
        name="two_grads")(h, a, b)

def down_grad_body(hid_ref, dy_ref, g_ref):
    g_ref[...] = tn(hid_ref[...], dy_ref[...]).astype(jnp.bfloat16)

def down_grad(hid, dy, step=512):
    T, F = hid.shape
    D = dy.shape[1]
    return pl.pallas_call(down_grad_body, grid=(D // step,),
        in_specs=[pl.BlockSpec((T, F), lambda i: (0, 0), pipeline_mode=pl.Buffered(1)), pl.BlockSpec((T, step), lambda i: (0, i))],
        out_specs=pl.BlockSpec((F, step), lambda i: (0, i)),
        out_shape=jax.ShapeDtypeStruct((F, D), jnp.bfloat16),
        compiler_params=pltpu.CompilerParams(vmem_limit_bytes=VMEM),
        cost_estimate=pl.CostEstimate(flops=2 * T * D * F, bytes_accessed=16 * 2**20, transcendentals=0),
        name="down_grad")(hid, dy)

def down_body(hid_ref, wd_ref, o_ref):
    o_ref[...] = nn(hid_ref[...], wd_ref[...]).astype(jnp.bfloat16)

def down(hid, wd, step=256):
    T, F = hid.shape
    D = wd.shape[1]
    return pl.pallas_call(down_body, grid=(T // step,),
        in_specs=[pl.BlockSpec((step, F), lambda i: (i, 0)), pl.BlockSpec((F, D), lambda i: (0, 0), pipeline_mode=pl.Buffered(1))],
        out_specs=pl.BlockSpec((step, D), lambda i: (i, 0)),
        out_shape=jax.ShapeDtypeStruct((T, D), jnp.bfloat16),
        compiler_params=pltpu.CompilerParams(vmem_limit_bytes=VMEM),
        cost_estimate=pl.CostEstimate(flops=2 * T * D * F, bytes_accessed=16 * 2**20, transcendentals=0),
        name="down")(hid, wd)


CORE = [(0, 1), (1, 0), (2, 3), (3, 2)]
CROSS = [(0, 2), (2, 0), (1, 3), (3, 1)]
DIAG = [(0, 3), (3, 0), (1, 2), (2, 1)]


def low(values):
    return values.astype(jnp.bfloat16)


def wide(values):
    return values.astype(jnp.float32)


def swap_core(values):
    return lax.ppermute(values, "grp", CORE)


def swap_cross(values):
    return lax.ppermute(values, "grp", CROSS)


def swap_diag(values):
    return lax.ppermute(values, "grp", DIAG)


def swap_blk(values, bit):
    count = lax.axis_size("blk")
    return lax.ppermute(values, "blk", [(i, i ^ bit) for i in range(count)])


def blk_bit(bit):
    return (lax.axis_index("blk") & bit) != 0


def bits_of(count):
    out = []
    bit = count // 2
    while bit >= 1:
        out.append(bit)
        bit //= 2
    return out


def gather_bits(values, order):
    done = []
    for bit in order:
        other = swap_blk(values, bit)
        mine = blk_bit(bit)
        axis = sum(1 for d in done if d > bit)
        values = jnp.stack(
            [jnp.where(mine, other, values), jnp.where(mine, values, other)], axis=axis
        )
        done.append(bit)
    return values


def scatter_bits(values, axes, order):
    axes = list(axes)
    for bit in order:
        axis = axes.index(bit)
        mine = blk_bit(bit).astype(jnp.int32)
        keep = lax.dynamic_index_in_dim(values, mine, axis, keepdims=False)
        send = lax.dynamic_index_in_dim(values, 1 - mine, axis, keepdims=False)
        values = low(wide(keep) + wide(swap_blk(send, bit)))
        axes.remove(bit)
    return values


def by_place(parts):
    grp = lax.axis_index("grp")
    core = (grp & 1) != 0
    cross = (grp & 2) != 0
    a, b, c, d = parts
    a, b = jnp.where(core, b, a), jnp.where(core, a, b)
    c, d = jnp.where(core, d, c), jnp.where(core, c, d)
    a, c = jnp.where(cross, c, a), jnp.where(cross, a, c)
    b, d = jnp.where(cross, d, b), jnp.where(cross, b, d)
    return [a, b, c, d]


def gather_near(values):
    cross = swap_cross(values)
    both = swap_core(jnp.stack([values, cross]))
    return [values, both[0], cross, both[1]]


def gather_grp(values):
    return by_place(gather_near(values))


def gather_tokens(values, bit):
    half = values.shape[0] // 2
    cross = swap_cross(values)
    over = swap_blk(values, bit)
    first = swap_blk(cross[:half], bit)
    second = swap_cross(over[half:])
    chip = jnp.concatenate([values, cross, over, first, second])
    return jnp.concatenate([chip, swap_core(chip)])


def angles_of(position):
    half = HD // 2
    freqs = ROPE_BASE ** (-2.0 * jnp.arange(half, dtype=jnp.float32) / HD)
    return position.astype(jnp.float32)[:, None] * freqs[None, :]


def rotate_by(values, cosine, sine):
    half = HD // 2
    first_half = values[..., :half]
    second_half = values[..., half:]
    return jnp.concatenate(
        [first_half * cosine - second_half * sine, second_half * cosine + first_half * sine],
        axis=-1,
    )


def after(values, anchor):
    return lax.optimization_barrier((values, anchor))[0]


def gather_step(values, done, bit):
    other = swap_blk(values, bit)
    mine = blk_bit(bit)
    axis = sum(1 for d in done if d > bit)
    return jnp.stack(
        [jnp.where(mine, other, values), jnp.where(mine, values, other)], axis=axis
    )


def gather_two_ways(values, bits, team):
    lows = [bit for bit in bits if bit < team]
    values = gather_step(values, [], bits[0])
    half = values.shape[-1] // 2
    parts = []
    for part, order in (
        (values[..., :half], [team] + lows),
        (values[..., half:], lows + [team]),
    ):
        done = [bits[0]]
        for bit in order:
            part = gather_step(part, done, bit)
            done.append(bit)
        parts.append(part)
    return jnp.concatenate(parts, axis=-1)


def gather_near_stacked(values):
    both = jnp.stack([values, swap_cross(values)])
    return jnp.concatenate([both, swap_core(both)])


def on_device(
    tokens,
    cotangent,
    segment_ids,
    position_ids,
    w_attend,
    w_out,
    w_gate,
    w_up,
    w_down,
    small_params,
    first_attend,
    first_out,
    first_gate,
    first_up,
    first_down,
    first_small,
    second_attend,
    second_out,
    second_gate,
    second_up,
    second_down,
    second_small,
):
    rows_here, block_len = tokens.shape[:2]
    blk_count = lax.axis_size("blk")
    seq_len = block_len * blk_count
    token_count = rows_here * block_len
    grp = lax.axis_index("grp")
    blk = lax.axis_index("blk")
    cross_id, core_id = grp // 2, grp % 2
    strip_heads = H // 4
    strip_q = strip_heads * HD
    bits = bits_of(blk_count)
    team = blk_count // 4
    lows = [bit for bit in bits if bit < team]
    spread = [bits[0]] + lows
    low_shape = (2,) * len(lows)
    in_team = blk_bit(team).astype(jnp.int32)
    weight_rows = w_gate.shape[0]
    ff_block = w_down.shape[0]
    quarter = ff_block // 4
    ff_here = quarter * blk_count // 2

    ids = jnp.stack([grp, in_team])
    flat_low = tokens.reshape(token_count, D)
    dy_low = cotangent.reshape(token_count, D)
    positions = position_ids.reshape(token_count)
    kv_at = HQD + HD * cross_id + KVD * core_id
    strip_local = low(
        jnp.concatenate(
            [
                lax.dynamic_slice_in_dim(w_attend, strip_q * grp, strip_q, 1),
                lax.dynamic_slice_in_dim(w_attend, kv_at, HD, 1),
            ],
            axis=1,
        )
    )
    small_send = jnp.concatenate([low(small_params), low(segment_ids.reshape(token_count))])
    strip_first = gather_step(strip_local, [], bits[0])
    strip_parts = []
    cut = (strip_q + HD) // 2
    for part, order in (
        (strip_first[..., :cut], [team] + lows),
        (strip_first[..., cut:], lows + [team]),
    ):
        done = [bits[0]]
        for bit in order:
            part = gather_step(part, done, bit)
            done.append(bit)
        strip_parts.append(part)
    strip = jnp.concatenate(strip_parts, axis=-1).reshape(D, strip_q + HD)
    near_tokens = jnp.concatenate(gather_near(flat_low))
    near_positions = jnp.concatenate(gather_near(positions))
    small_all = gather_bits(small_send, bits).reshape(blk_count, -1)
    vector = wide(small_all[:, : small_params.shape[0]].reshape(-1))
    gain_one = vector[:D]
    gain_two = vector[D : 2 * D]
    bias = vector[2 * D :]
    strip_bias = jnp.concatenate(
        [
            lax.dynamic_slice_in_dim(bias, strip_q * grp, strip_q, 0),
            lax.dynamic_slice_in_dim(bias, kv_at, HD, 0),
        ]
    )
    seg_all = small_all[:, small_params.shape[0] :].astype(jnp.int32)
    seg_all = seg_all.reshape(blk_count, rows_here, block_len)
    seg_key = jnp.broadcast_to(
        seg_all.transpose(1, 0, 2).reshape(rows_here, seq_len)[:, :, None], (rows_here, seq_len, HD)
    )
    seg_query = jnp.broadcast_to(segment_ids[:, None, :], (rows_here, 8, block_len))
    first_blk = jnp.sum((seg_all[:, :, -1] < segment_ids[None, :, 0]).astype(jnp.int32), axis=0)
    attend_ids = jnp.concatenate([blk[None], first_blk])

    near_wide = wide(near_tokens)
    near_one = low(norm_apply(near_wide, gain_one))
    mixed = jnp.dot(near_one, strip, preferred_element_type=jnp.float32) + strip_bias
    angles = angles_of(near_positions)[:, None, :]
    turned = jnp.arange(strip_heads + 1)[None, :, None] < strip_heads + 1 - core_id
    angles = jnp.where(turned, angles, 0.0)
    strip_out = low(
        rotate_by(
            mixed.reshape(4 * token_count, strip_heads + 1, HD), jnp.cos(angles), jnp.sin(angles)
        )
    ).reshape(4, token_count, strip_q + HD)
    strips = by_place(
        [
            strip_out[0],
            swap_core(strip_out[1]),
            swap_cross(strip_out[2]),
            swap_diag(strip_out[3]),
        ]
    )
    query = jnp.concatenate([part[:, :strip_q] for part in strips], axis=1)
    key_value = jnp.concatenate([strips[k][:, strip_q:] for k in (0, 2, 1, 3)], axis=1)
    key_value = key_value.reshape(rows_here, block_len, 2 * KVD)
    kv_all = gather_two_ways(key_value, bits, team).reshape((blk_count,) + key_value.shape)

    out_piece = weight_rows // 4
    out_local = low(lax.dynamic_slice_in_dim(w_out, out_piece * grp, out_piece, 0))
    out_full = lax.all_gather(out_local, ("blk", "grp"), axis=0, tiled=True)
    down_local = low(lax.dynamic_slice_in_dim(w_down, quarter * grp, quarter, 0))
    down_first = swap_blk(after(down_local, strip_first), bits[0])
    picked = pick_columns(ids, w_gate, w_up, blk_count)
    mine_team = blk_bit(team)
    picked_got = after(swap_blk(picked[1], team), strip_out)
    pair = jnp.stack(
        [jnp.where(mine_team, picked_got, picked[0]), jnp.where(mine_team, picked[0], picked_got)]
    )
    peers = [[i for i in range(blk_count) if (i & team) == t] for t in (0, team)]
    pairs = lax.all_gather(pair, "blk", axis=0, axis_index_groups=peers)
    pairs = pairs.reshape((2, blk_count // 4, 2, 2, weight_rows, ff_here)).transpose(3, 0, 2, 1, 4, 5)
    gate_here = pairs[0].reshape(D, ff_here)
    up_here = pairs[1].reshape(D, ff_here)

    def place(values, other, done, bit):
        mine = blk_bit(bit)
        axis = sum(1 for d in done if d > bit)
        return jnp.stack(
            [jnp.where(mine, other, values), jnp.where(mine, values, other)], axis=axis
        )

    down_here = place(down_local, after(down_first, strip_out), [], bits[0])
    done = [bits[0]]
    for bit in lows:
        other = after(swap_blk(down_here, bit), kv_all)
        down_here = place(down_here, other, done, bit)
        done.append(bit)
    down_here = down_here.reshape(ff_here, D)

    dy_half = token_count // 2
    dy_send = after(dy_low, strip_parts)
    dy_cross, dy_over = after((swap_cross(dy_send), swap_blk(dy_send, team)), strip_out)
    dy_first = swap_blk(dy_cross[:dy_half], team)
    dy_second = swap_cross(dy_over[dy_half:])
    dy_first, dy_second = after((dy_first, dy_second), kv_all)
    dy_chip = jnp.concatenate([dy_low, dy_cross, dy_over, dy_first, dy_second])
    dy_team = jnp.concatenate([dy_chip, swap_core(dy_chip)])

    att_in, lse = attend(attend_ids, query, kv_all, seg_key, seg_query, block_len)

    flat = wide(flat_low)
    resid = flat + jnp.dot(att_in, out_full, preferred_element_type=jnp.float32)
    h_two = low(norm_apply(resid, gain_two))
    h_team = gather_tokens(h_two, team)
    hidden, d_gate, d_up, d_htwo_part = middle(h_team, dy_team, gate_here, up_here, down_here)
    chip_rows = 4 * token_count
    half = token_count // 2

    def chip_sum(values, came):
        return low(wide(values[:chip_rows]) + wide(came))

    def scatter_far(chip):
        far = chip[3 * token_count :]
        return swap_blk(far[:half], team), swap_cross(far[half:])

    def scatter_near(chip, first, second):
        cross, over = (chip[token_count * i : token_count * (i + 1)] for i in (1, 2))
        cross = jnp.concatenate([low(wide(cross[:half]) + wide(first)), cross[half:]])
        over = jnp.concatenate([over[:half], low(wide(over[half:]) + wide(second))])
        return swap_cross(cross), swap_blk(over, team)

    d_came = swap_core(d_htwo_part[chip_rows:])
    down_grad_part = down_grad(hidden, dy_team).reshape((2,) + low_shape + (quarter, D))
    d_chip = chip_sum(d_htwo_part, after(d_came, down_grad_part))
    d_far = scatter_far(d_chip)

    def share_start(grad, axes):
        bit = lows[-1]
        axis = axes.index(bit)
        mine = blk_bit(bit).astype(jnp.int32)
        keep = lax.dynamic_index_in_dim(grad, mine, axis, keepdims=False)
        send = lax.dynamic_index_in_dim(grad, 1 - mine, axis, keepdims=False)
        return keep, swap_blk(send, bit)

    def share_mid(keep, got, axes):
        values = low(wide(keep) + wide(got))
        axes = [bit for bit in axes if bit != lows[-1]]
        for bit in lows[-2::-1]:
            values = scatter_bits(values, axes, [bit])
            axes = [b for b in axes if b != bit]
        mine = blk_bit(bits[0]).astype(jnp.int32)
        keep = lax.dynamic_index_in_dim(values, mine, 0, keepdims=False)
        send = lax.dynamic_index_in_dim(values, 1 - mine, 0, keepdims=False)
        return keep, swap_blk(send, bits[0])

    def share_columns(values):
        keep = lax.dynamic_index_in_dim(values, in_team, 0, keepdims=False)
        send = lax.dynamic_index_in_dim(values, 1 - in_team, 0, keepdims=False)
        got = swap_blk(send, team)
        return jnp.stack(
            [jnp.where(mine_team, got, keep), jnp.where(mine_team, keep, got)]
        )

    down_axes = [bits[0]] + lows
    down_keep, down_got = share_start(down_grad_part, down_axes)
    late_gate, late_up = after((d_gate, d_up), d_chip)
    column_shape = (2, 2) + low_shape + (weight_rows, ff_here)
    gate_grad, up_grad = two_grads(h_team, late_gate, late_up)
    gate_keep, gate_got = share_start(gate_grad.reshape(column_shape), bits)
    d_far = after(d_far, gate_grad)
    d_cross, d_over = scatter_near(d_chip, *d_far)
    out_part = down(after(hidden, d_far), down_here)
    out_came = swap_core(out_part[chip_rows:])
    down_keep, down_got = share_mid(*after((down_keep, down_got), out_part), down_axes)
    d_cross, d_over = after((d_cross, d_over), out_part)
    d_htwo = wide(d_chip[:token_count]) + wide(d_cross) + wide(d_over)

    norm_value_two, norm_back_two = jax.vjp(norm_apply, resid, gain_two)
    d_resid_norm, grad_gain_two = norm_back_two(d_htwo)
    d_resid = wide(dy_low) + d_resid_norm
    d_att = low(d_resid)

    d_attended = low(right_transposed(d_att, out_full))
    own_angles = angles_of(positions)
    cosine, sine = jnp.cos(own_angles), jnp.sin(own_angles)
    d_query, dkv = attend_back(
        attend_ids,
        query,
        kv_all,
        seg_key,
        seg_query,
        att_in,
        d_attended,
        lse,
        jnp.concatenate([cosine, cosine], axis=1),
        jnp.concatenate([sine, sine], axis=1),
        block_len,
    )
    gate_keep, gate_got = share_mid(*after((gate_keep, gate_got), d_query), bits)
    share_down = low(wide(down_keep) + wide(after(down_got, d_query)))
    dkv = dkv.reshape((2,) * len(bits) + (rows_here, block_len, 2 * KVD))
    dkv_first = scatter_bits(dkv[..., :KVD], bits, lows[::-1])
    dkv_second = scatter_bits(dkv[..., KVD:], bits, [team])
    up_keep, up_got = share_start(after(up_grad, dkv_first).reshape(column_shape), bits)
    dkv_first = scatter_bits(dkv_first, bits[:2], [team])
    dkv_second = scatter_bits(dkv_second, [bits[0]] + lows, lows[::-1])
    dkv = jnp.concatenate([dkv_first, dkv_second], axis=-1)
    out_chip = chip_sum(out_part, after(out_came, dkv_first))
    dkv = wide(scatter_bits(dkv, bits[:1], bits[:1])).reshape(token_count, 2, KVH, HD)
    d_key = low(rotate_by(dkv[:, 0], cosine[:, None], -sine[:, None]))
    d_value = low(dkv[:, 1])
    out_far = after(scatter_far(out_chip), d_key)
    out_cross, out_over = scatter_near(out_chip, *out_far)
    up_keep, up_got = share_mid(*after((up_keep, up_got), d_key), bits)

    def to_strips(parts):
        parts = by_place(parts)
        return jnp.concatenate(
            [parts[0], swap_core(parts[1]), swap_cross(parts[2]), swap_diag(parts[3])]
        )

    near_dq = to_strips([d_query[:, strip_q * k : strip_q * (k + 1)] for k in range(4)])
    block_shape = (2,) * len(bits) + (weight_rows, -1)
    share_query = scatter_bits(
        low(left_product(near_one, near_dq)).reshape(block_shape), bits, bits[::-1]
    )
    near_dkv = to_strips([(d_value if k % 2 else d_key)[:, k // 2] for k in range(4)])
    share_kv = scatter_bits(
        low(left_product(near_one, near_dkv)).reshape(block_shape), bits, bits[::-1]
    )
    grad_bias = jnp.concatenate(
        [
            jnp.sum(wide(part), axis=0)
            for part in (d_query, d_key.reshape(token_count, KVD), d_value.reshape(token_count, KVD))
        ]
    )
    out_cross, out_over = after((out_cross, out_over), near_dkv)
    out_tokens = low(resid + wide(out_chip[:token_count]) + wide(out_cross) + wide(out_over))
    near_hone = right_transposed(near_dq, strip[:, :strip_q]) + right_transposed(
        near_dkv, strip[:, strip_q:]
    )
    near_rms = lax.rsqrt(jnp.mean(near_wide * near_wide, axis=-1, keepdims=True) + NORM_EPS)
    gain_one_part = jnp.sum(near_hone * near_wide * near_rms, axis=0)

    near_att = jnp.concatenate(gather_near(att_in))
    near_datt = to_strips([d_att[:, strip_q * k : strip_q * (k + 1)] for k in range(4)])
    share_out = scatter_bits(
        low(left_product(near_att, after(near_datt, d_query))).reshape(block_shape),
        bits,
        bits[::-1],
    )

    vector_term = jnp.concatenate([gain_one_part, grad_gain_two, grad_bias])
    vector_term = vector_term + swap_cross(vector_term)
    vector_term = vector_term + swap_core(vector_term)
    vector_term = vector_term.reshape((2,) * len(bits) + (-1,))
    axes = list(bits)
    for bit in bits[::-1]:
        axis = axes.index(bit)
        mine = blk_bit(bit).astype(jnp.int32)
        keep = lax.dynamic_index_in_dim(vector_term, mine, axis, keepdims=False)
        send = lax.dynamic_index_in_dim(vector_term, 1 - mine, axis, keepdims=False)
        vector_term = keep + swap_blk(send, bit)
        axes.remove(bit)
    share_vector = vector_term

    share_gate = share_columns(low(wide(gate_keep) + wide(after(gate_got, d_key))))
    near_gate = gather_near_stacked(share_gate)
    share_up = share_columns(low(wide(up_keep) + wide(after(up_got, near_dkv))))
    near_up = gather_near_stacked(share_up)
    grad_down = jnp.concatenate(gather_grp(share_down), axis=0)
    grad_out = jnp.concatenate(gather_grp(share_out), axis=1)
    query_parts = gather_grp(share_query)
    kv_parts = gather_grp(share_kv)
    grad_attend = jnp.concatenate(query_parts + [kv_parts[k] for k in (0, 2, 1, 3)], axis=1)

    sides = low(near_hone[token_count : 2 * token_count]), low(near_hone[3 * token_count :])
    other = wide(swap_core(jnp.concatenate(sides)))
    d_hone = near_hone[:token_count] + other[:token_count]
    d_hone_cross = swap_cross(
        low(near_hone[2 * token_count : 3 * token_count] + other[token_count:])
    )
    square_sum = square_total(
        [
            wide(s)
            for s in (share_query, share_kv, share_out, share_gate, share_up, share_down)
        ]
    ) + 0.25 * jnp.sum(share_vector * share_vector)
    square_sum = jnp.full((8, 128), square_sum)
    for bit in bits:
        square_sum = square_sum + swap_blk(square_sum, bit)
    square_sum = square_sum + swap_cross(square_sum)
    square_sum = square_sum + swap_core(square_sum)
    grad_norm = jnp.sqrt(square_sum[0, 0])
    factor = jnp.minimum(1.0, CLIP_NORM / (grad_norm + 1e-06))
    factor = after(factor, out_tokens)

    new_first_gate, new_second_gate, new_gate = adam_columns(
        ids, factor[None], near_gate, w_gate, first_gate, second_gate, blk_count, RATE_GATE, WEIGHT_DECAY
    )
    new_first_up, new_second_up, new_up = adam_columns(
        ids, factor[None], near_up, w_up, first_up, second_up, blk_count, RATE_GATE, WEIGHT_DECAY
    )
    norm_value_one, norm_back_one = jax.vjp(norm_apply, flat, gain_one)
    d_hone = after(d_hone + wide(after(d_hone_cross, new_gate)), new_gate)
    d_flat_norm, unused_gain = norm_back_one(d_hone)
    grad_tokens = low(d_resid + d_flat_norm)

    new_first_attend, new_second_attend, new_attend = adam_step(
        w_attend, factor * wide(grad_attend), first_attend, second_attend, RATE_ATTEND, WEIGHT_DECAY
    )
    new_first_out, new_second_out, new_out = adam_step(
        w_out, factor * wide(grad_out), first_out, second_out, RATE_OUT, WEIGHT_DECAY
    )
    new_first_down, new_second_down, new_down = adam_step(
        w_down, factor * wide(grad_down), first_down, second_down, RATE_DOWN, WEIGHT_DECAY
    )
    new_first_small, new_second_small, new_small = adam_step(
        small_params, factor * share_vector, first_small, second_small, RATE_VECTOR, 0.0
    )
    return (
        out_tokens.reshape(rows_here, block_len, D),
        grad_tokens.reshape(rows_here, block_len, D),
        grad_norm,
        new_first_attend,
        new_second_attend,
        new_attend,
        new_first_out,
        new_second_out,
        new_out,
        new_first_gate,
        new_second_gate,
        new_gate,
        new_first_up,
        new_second_up,
        new_up,
        new_first_down,
        new_second_down,
        new_down,
        new_first_small,
        new_second_small,
        new_small,
    )


def solution(mesh):
    placed = (
        P("grp", "blk", None),
        P("grp", "blk", None),
        P("grp", "blk"),
        P("grp", "blk"),
        P("blk", None),
        P("blk", None),
        P("blk", None),
        P("blk", None),
        P("blk", None),
        P("blk"),
        P("blk", None),
        P("blk", None),
        P("blk", None),
        P("blk", None),
        P("blk", None),
        P("blk"),
        P("blk", None),
        P("blk", None),
        P("blk", None),
        P("blk", None),
        P("blk", None),
        P("blk"),
    )
    return jax.shard_map(
        on_device,
        mesh=mesh,
        in_specs=placed,
        out_specs=(
            P("grp", "blk", None),
            P("grp", "blk", None),
            P(),
            P("blk", None),
            P("blk", None),
            P("blk", None),
            P("blk", None),
            P("blk", None),
            P("blk", None),
            P("blk", None),
            P("blk", None),
            P("blk", None),
            P("blk", None),
            P("blk", None),
            P("blk", None),
            P("blk", None),
            P("blk", None),
            P("blk", None),
            P("blk"),
            P("blk"),
            P("blk"),
        ),
        check_vma=False,
    )
```

```python
import functools

import jax
import jax.numpy as jnp
from jax import lax
from jax.experimental import pallas as pl
from jax.experimental.pallas import tpu as pltpu
from jax.sharding import PartitionSpec as P

D = 1536
FF = 8960
H = 12
KVH = 2
HD = 128
STEP = 10
HQD = 1536
KVD = 256


NORM_EPS = 1e-06
ROPE_BASE = 10000.0
CLIP_NORM = 1.0
BETA_FIRST = 0.9
BETA_SECOND = 0.95
ADAM_EPS = 1e-08
WEIGHT_DECAY = 0.1
RATE_ATTEND = 0.06
RATE_OUT = 0.5
RATE_GATE = 0.06
RATE_DOWN = 0.03
RATE_VECTOR = 0.5
NEG_LARGE = -1e30
LOG2E = 1.4426950408889634
VMEM = 48 * 1024 * 1024


def norm_apply(values, gain):
    return values * lax.rsqrt(jnp.mean(values * values, axis=-1, keepdims=True) + NORM_EPS) * gain


def swish_product(gate, up_proj):
    return jax.nn.silu(gate) * up_proj


def left_product(left_side, right_side):
    return lax.dot_general(
        left_side, right_side, (((0,), (0,)), ((), ())), preferred_element_type=jnp.float32
    )


def right_transposed(left_side, right_side):
    return lax.dot_general(
        left_side, right_side, (((1,), (1,)), ((), ())), preferred_element_type=jnp.float32
    )


def square_total(arrays):
    return sum((jnp.sum(member * member) for member in arrays))


def adam_step(weight, grad, first, second, rate, decay):
    first_new = BETA_FIRST * first + (1.0 - BETA_FIRST) * grad
    second_new = BETA_SECOND * second + (1.0 - BETA_SECOND) * grad * grad
    first_hat = first_new / (1.0 - BETA_FIRST**STEP)
    second_hat = second_new / (1.0 - BETA_SECOND**STEP)
    weight_new = weight - rate * (first_hat / (jnp.sqrt(second_hat) + ADAM_EPS) + decay * weight)
    return (first_new, second_new, weight_new)


def halves_of(quarter):
    first = quarter * 16 // 35
    return ((0, first), (first, quarter - first))


def pick_body(blk_count, ids, gate_ref, up_ref, *out_refs):
    quarter = FF // blk_count // 4
    per = blk_count // 4
    for k in range(4):

        @pl.when(ids[0] == k)
        def _(k=k):
            for (at, size), out_ref in zip(halves_of(quarter), out_refs):
                for which, src in enumerate((gate_ref, up_ref)):
                    for bit in range(2):
                        parts = []
                        for high in range(2):
                            for small in range(per):
                                begin = (((high * 2 + bit) * per + small) * 4 + k) * quarter + at
                                parts.append(src[:, begin : begin + size])
                        out_ref[ids[1] ^ bit, which] = jnp.concatenate(parts, axis=1).astype(
                            jnp.bfloat16
                        )


def pick_columns(ids, gate, up, blk_count):
    rows = gate.shape[0]
    step = 48 if rows % 48 == 0 else rows
    widths = [size * blk_count // 2 for at, size in halves_of(FF // blk_count // 4)]
    spec = pl.BlockSpec((step, FF), lambda i, ids: (i, 0))
    return pl.pallas_call(
        functools.partial(pick_body, blk_count),
        grid_spec=pltpu.PrefetchScalarGridSpec(
            num_scalar_prefetch=1,
            grid=(rows // step,),
            in_specs=[spec, spec],
            out_specs=[pl.BlockSpec((2, 2, step, w), lambda i, ids: (0, 0, i, 0)) for w in widths],
        ),
        out_shape=[jax.ShapeDtypeStruct((2, 2, rows, w), jnp.bfloat16) for w in widths],
        compiler_params=pltpu.CompilerParams(vmem_limit_bytes=VMEM),
        cost_estimate=pl.CostEstimate(flops=0, bytes_accessed=rows * FF * 10, transcendentals=0),
        name="pick_columns",
    )(ids, gate, up)


def adam_body(blk_count, rate, decay, factor_ref, first_ref, second_ref, w_ref, m_ref, v_ref, m_out, v_out, w_out):
    per = blk_count // 4
    sizes = [size for at, size in halves_of(FF // blk_count // 4)]
    grads = [[[ref[k, bit] for bit in range(2)] for k in range(4)] for ref in (first_ref, second_ref)]
    parts = []
    for high in range(2):
        for bit in range(2):
            for small in range(per):
                place = high * per + small
                for k in range(4):
                    for part, size in zip(grads, sizes):
                        parts.append(part[k][bit][:, place * size : (place + 1) * size])
    grad = jnp.concatenate(parts, axis=1).astype(jnp.float32) * factor_ref[0]
    m, v, w = adam_step(w_ref[...], grad, m_ref[...], v_ref[...], rate, decay)
    m_out[...] = m
    v_out[...] = v
    w_out[...] = w


def adam_columns(which, factor, first, second, w, m, v, blk_count, rate, decay):
    rows = w.shape[0]
    step = 32 if rows % 32 == 0 else rows
    spec = pl.BlockSpec((step, FF), lambda i: (i, 0))
    shape = jax.ShapeDtypeStruct((rows, FF), jnp.float32)
    grads = [
        pl.BlockSpec((4, None, 2, step, g.shape[-1]), lambda i: (0, which, 0, i, 0))
        for g in (first, second)
    ]
    return pl.pallas_call(
        functools.partial(adam_body, blk_count, rate, decay),
        grid=(rows // step,),
        in_specs=[pl.BlockSpec(memory_space=pltpu.SMEM)] + grads + [spec, spec, spec],
        out_specs=[spec, spec, spec],
        out_shape=[shape] * 3,
        compiler_params=pltpu.CompilerParams(vmem_limit_bytes=VMEM),
        cost_estimate=pl.CostEstimate(
            flops=rows * FF * 20, bytes_accessed=rows * FF * 26, transcendentals=rows * FF
        ),
        name="adam_columns",
    )(factor, first, second, w, m, v)


def nt(a, b, **kw):
    return lax.dot_general(a, b, (((1,), (1,)), ((), ())), preferred_element_type=jnp.float32, **kw)

def tn(a, b, **kw):
    return lax.dot_general(a, b, (((0,), (0,)), ((), ())), preferred_element_type=jnp.float32, **kw)

def stack_heads(ref, kvh, group):
    return jnp.concatenate([ref[:, HD * (kvh * group + i): HD * (kvh * group + i + 1)] for i in range(group)], axis=0)

def hidden_from(seg_key_ref, seg_query_ref, first, chunk, block_len, blk):
    key = first + lax.broadcasted_iota(jnp.int32, (chunk, block_len), 0)
    query = blk * block_len + lax.broadcasted_iota(jnp.int32, (chunk, block_len), 1)
    seg_key = seg_key_ref[pl.ds(first, chunk), :]
    counts = jnp.logical_and(key <= query, seg_key == seg_query_ref[0:1, :])
    return jnp.where(counts, 0.0, NEG_LARGE)

def attend_body(chunk, ids, q_ref, k_ref, v_ref, seg_key_ref, seg_query_ref, o_ref, lse_ref, m_s, l_s, acc_s):
    block_len = q_ref.shape[0]
    group = H // KVH
    row = pl.program_id(0)
    per = chunk // block_len
    scale = HD ** (-0.5) * LOG2E
    start = ids[1 + row] // per
    stop = ids[0] // per + 1
    for kvh in range(KVH):
        q = stack_heads(q_ref, kvh, group)
        m_s[...] = jnp.full_like(m_s, NEG_LARGE)
        l_s[...] = jnp.zeros_like(l_s)
        acc_s[...] = jnp.zeros_like(acc_s)

        def step(c, carry):
            keys = k_ref[pl.ds(c * per, per), :, HD * kvh: HD * (kvh + 1)].reshape(chunk, HD)
            vals = v_ref[pl.ds(c * per, per), :, HD * kvh: HD * (kvh + 1)].reshape(chunk, HD)
            bias = hidden_from(seg_key_ref, seg_query_ref, c * chunk, chunk, block_len, ids[0])
            s = nt(keys, q) * scale + jnp.concatenate([bias] * group, axis=1)
            old = m_s[0:1, :]
            new = jnp.maximum(old, jnp.max(s, axis=0, keepdims=True))
            p = jnp.exp2(s - new)
            fade = jnp.exp2(old - new)
            l_s[0:1, :] = l_s[0:1, :] * fade + jnp.sum(p, axis=0, keepdims=True)
            acc_s[...] = acc_s[...] * fade + tn(vals, p.astype(jnp.bfloat16))
            m_s[0:1, :] = new
            return carry

        lax.fori_loop(start, stop, step, 0)
        total = l_s[0:1, :]
        out = (acc_s[...] * (1.0 / total)).T
        for i in range(group):
            o_ref[:, HD * (kvh * group + i): HD * (kvh * group + i + 1)] = out[block_len * i: block_len * (i + 1), :].astype(jnp.bfloat16)
        lse_ref[kvh] = jnp.broadcast_to(m_s[0:1, :] + jnp.log2(total), (8, group * block_len))

def attend(ids, q, kv, seg_key, seg_query, block_len):
    blk_count, rows = kv.shape[:2]
    group = H // KVH
    chunk = 2 * block_len
    many = group * block_len
    return pl.pallas_call(
        functools.partial(attend_body, chunk),
        grid_spec=pltpu.PrefetchScalarGridSpec(
            num_scalar_prefetch=1, grid=(rows,),
            in_specs=[
                pl.BlockSpec((block_len, HQD), lambda r, ids: (r, 0)),
                pl.BlockSpec((blk_count, None, block_len, KVD), lambda r, ids: (0, r, 0, 0)),
                pl.BlockSpec((blk_count, None, block_len, KVD), lambda r, ids: (0, r, 0, 1)),
                pl.BlockSpec((None, blk_count * block_len, HD), lambda r, ids: (r, 0, 0)),
                pl.BlockSpec((None, 8, block_len), lambda r, ids: (r, 0, 0)),
            ],
            out_specs=[
                pl.BlockSpec((block_len, HQD), lambda r, ids: (r, 0)),
                pl.BlockSpec((None, KVH, 8, many), lambda r, ids: (r, 0, 0, 0)),
            ],
            scratch_shapes=[pltpu.VMEM((8, many), jnp.float32), pltpu.VMEM((8, many), jnp.float32), pltpu.VMEM((HD, many), jnp.float32)]),
        out_shape=[
            jax.ShapeDtypeStruct((rows * block_len, HQD), jnp.bfloat16),
            jax.ShapeDtypeStruct((rows, KVH, 8, many), jnp.float32),
        ],
        compiler_params=pltpu.CompilerParams(vmem_limit_bytes=VMEM),
        cost_estimate=pl.CostEstimate(flops=4 * rows * H * block_len * blk_count * block_len * HD, bytes_accessed=8 * 2**20, transcendentals=rows * H * block_len * blk_count * block_len),
        name="attend",
    )(ids, q, kv, kv, seg_key, seg_query)

def turn_back(u, cosine, sine):
    lane = lax.broadcasted_iota(jnp.int32, u.shape, 1)
    other = pltpu.roll(u, HD // 2, 1)
    return u * cosine + jnp.where(lane < HD // 2, other, -other) * sine

def attend_back_body(chunk, ids, q_ref, k_ref, v_ref, seg_key_ref, seg_query_ref, o_ref, do_ref, lse_ref, cos_ref, sin_ref, dq_ref, dkv_ref, dq_s):
    block_len = q_ref.shape[0]
    group = H // KVH
    row = pl.program_id(0)
    per = chunk // block_len
    plain = HD ** (-0.5)
    scale = plain * LOG2E
    start = ids[1 + row] // per
    stop = ids[0] // per + 1
    dkv_ref[...] = jnp.zeros_like(dkv_ref)
    for kvh in range(KVH):
        q = stack_heads(q_ref, kvh, group)
        do = stack_heads(do_ref, kvh, group)
        o = stack_heads(o_ref, kvh, group)
        both = do.astype(jnp.float32) * o.astype(jnp.float32)
        delta = nt(jnp.ones((8, HD), jnp.float32), both, precision=lax.Precision.HIGHEST)[0:1, :]
        lse = lse_ref[kvh][0:1, :]
        dq_s[...] = jnp.zeros_like(dq_s)

        def step(c, carry):
            keys = k_ref[pl.ds(c * per, per), :, HD * kvh: HD * (kvh + 1)].reshape(chunk, HD)
            vals = v_ref[pl.ds(c * per, per), :, HD * kvh: HD * (kvh + 1)].reshape(chunk, HD)
            bias = hidden_from(seg_key_ref, seg_query_ref, c * chunk, chunk, block_len, ids[0])
            s = nt(keys, q) * scale + jnp.concatenate([bias] * group, axis=1)
            p = jnp.exp2(s - lse)
            dp = nt(vals, do)
            ds = (p * (dp - delta)).astype(jnp.bfloat16)
            dk = jnp.dot(ds, q, preferred_element_type=jnp.float32) * plain
            dv = jnp.dot(p.astype(jnp.bfloat16), do, preferred_element_type=jnp.float32)
            dkv_ref[pl.ds(c * per, per), :, HD * kvh: HD * (kvh + 1)] = dk.astype(jnp.bfloat16).reshape(per, block_len, HD)
            dkv_ref[pl.ds(c * per, per), :, KVD + HD * kvh: KVD + HD * (kvh + 1)] = dv.astype(jnp.bfloat16).reshape(per, block_len, HD)
            dq_s[...] += tn(ds, keys)
            return carry

        lax.fori_loop(start, stop, step, 0)
        cosine, sine = cos_ref[...], sin_ref[...]
        for i in range(group):
            u = dq_s[block_len * i: block_len * (i + 1), :] * plain
            at = HD * (kvh * group + i)
            dq_ref[:, at: at + HD] = turn_back(u, cosine, sine).astype(jnp.bfloat16)

def attend_back(ids, q, kv, seg_key, seg_query, o, do, lse, cosine, sine, block_len):
    blk_count, rows = kv.shape[:2]
    group = H // KVH
    chunk = 2 * block_len
    many = group * block_len
    per_row = pl.BlockSpec((block_len, HQD), lambda r, ids: (r, 0))
    turn = pl.BlockSpec((block_len, HD), lambda r, ids: (r, 0))
    return pl.pallas_call(
        functools.partial(attend_back_body, chunk),
        grid_spec=pltpu.PrefetchScalarGridSpec(
            num_scalar_prefetch=1, grid=(rows,),
            in_specs=[
                per_row,
                pl.BlockSpec((blk_count, None, block_len, KVD), lambda r, ids: (0, r, 0, 0)),
                pl.BlockSpec((blk_count, None, block_len, KVD), lambda r, ids: (0, r, 0, 1)),
                pl.BlockSpec((None, blk_count * block_len, HD), lambda r, ids: (r, 0, 0)),
                pl.BlockSpec((None, 8, block_len), lambda r, ids: (r, 0, 0)),
                per_row, per_row,
                pl.BlockSpec((None, KVH, 8, many), lambda r, ids: (r, 0, 0, 0)),
                turn, turn,
            ],
            out_specs=[per_row, pl.BlockSpec((blk_count, None, block_len, 2 * KVD), lambda r, ids: (0, r, 0, 0))],
            scratch_shapes=[pltpu.VMEM((many, HD), jnp.float32)]),
        out_shape=[
            jax.ShapeDtypeStruct((rows * block_len, HQD), jnp.bfloat16),
            jax.ShapeDtypeStruct((blk_count, rows, block_len, 2 * KVD), jnp.bfloat16),
        ],
        compiler_params=pltpu.CompilerParams(vmem_limit_bytes=VMEM),
        cost_estimate=pl.CostEstimate(flops=10 * rows * H * block_len * blk_count * block_len * HD, bytes_accessed=12 * 2**20, transcendentals=rows * H * block_len * blk_count * block_len),
        name="attend_back",
    )(ids, q, kv, kv, seg_key, seg_query, o, do, lse, cosine, sine)

def nn(a, b):
    return jnp.dot(a, b, preferred_element_type=jnp.float32)


def middle_body(add, order, h_ref, dy_ref, wg_ref, wu_ref, wd_ref, *refs):
    prev_ref = refs[0] if add else None
    hid_ref, dg_ref, du_ref, dh_ref = refs[-4:]
    h = h_ref[...]
    gate = nn(h, wg_ref[...])
    up = nn(h, wu_ref[...])
    sig = 1.0 / (1.0 + jnp.exp(-gate))
    silu = gate * sig
    hid_ref[...] = (silu * up).astype(jnp.bfloat16)
    dhid = nt(dy_ref[...], wd_ref[...])
    dg = (dhid * up * sig * (1.0 + gate * (1.0 - sig))).astype(jnp.bfloat16)
    du = (dhid * silu).astype(jnp.bfloat16)
    dg_ref[...] = dg
    du_ref[...] = du
    dh = nt(dg, wg_ref[...]) + nt(du, wu_ref[...])
    if add:
        dh = dh + prev_ref[...].astype(jnp.float32)
    dh_ref[...] = dh.astype(jnp.bfloat16)


def middle(order, h, dy, wg, wu, wd, prev=None):
    count = h.shape[0]
    step = count // order.shape[0]
    wide_here = wg.shape[1]
    row = pl.BlockSpec((step, D), lambda i, order: (i, 0))
    placed = pl.BlockSpec((step, D), lambda i, order: (order[i], 0))
    part = pl.BlockSpec((step, wide_here), lambda i, order: (i, 0))
    part_placed = pl.BlockSpec((step, wide_here), lambda i, order: (order[i], 0))

    def whole(array):
        return pl.BlockSpec(array.shape, lambda i, order: (0, 0), pipeline_mode=pl.Buffered(1))

    extra = [] if prev is None else [prev]
    return pl.pallas_call(
        functools.partial(middle_body, prev is not None),
        grid_spec=pltpu.PrefetchScalarGridSpec(
            num_scalar_prefetch=1,
            grid=(count // step,),
            in_specs=[row, placed, whole(wg), whole(wu), whole(wd)] + [row] * len(extra),
            out_specs=[part_placed, part, part, row],
        ),
        out_shape=[jax.ShapeDtypeStruct((count, wide_here), jnp.bfloat16)] * 3
        + [jax.ShapeDtypeStruct((count, D), jnp.bfloat16)],
        compiler_params=pltpu.CompilerParams(vmem_limit_bytes=VMEM),
        cost_estimate=pl.CostEstimate(
            flops=10 * count * D * wide_here, bytes_accessed=30 * 2**20, transcendentals=count * wide_here
        ),
        name="middle",
    )(order, h, dy, wg, wu, wd, *extra)


def two_grads_body(h_ref, a_ref, b_ref, out_ref):
    h = h_ref[...]
    out_ref[0] = tn(h, a_ref[...]).astype(jnp.bfloat16)
    out_ref[1] = tn(h, b_ref[...]).astype(jnp.bfloat16)


def two_grads(h, a, b, step=256):
    count = h.shape[0]
    wide_here = a.shape[1]
    whole = pl.BlockSpec(a.shape, lambda i: (0, 0), pipeline_mode=pl.Buffered(1))
    return pl.pallas_call(
        two_grads_body,
        grid=(D // step,),
        in_specs=[pl.BlockSpec((count, step), lambda i: (0, i)), whole, whole],
        out_specs=pl.BlockSpec((2, step, wide_here), lambda i: (0, i, 0)),
        out_shape=jax.ShapeDtypeStruct((2, D, wide_here), jnp.bfloat16),
        compiler_params=pltpu.CompilerParams(vmem_limit_bytes=VMEM),
        cost_estimate=pl.CostEstimate(
            flops=4 * count * D * wide_here, bytes_accessed=20 * 2**20, transcendentals=0
        ),
        name="two_grads",
    )(h, a, b)


def down_grad_body(hid_ref, dy_ref, g_ref):
    g_ref[...] = tn(hid_ref[...], dy_ref[...]).astype(jnp.bfloat16)

def down_grad(hid, dy, step=512):
    T, F = hid.shape
    D = dy.shape[1]
    return pl.pallas_call(down_grad_body, grid=(D // step,),
        in_specs=[pl.BlockSpec((T, F), lambda i: (0, 0), pipeline_mode=pl.Buffered(1)), pl.BlockSpec((T, step), lambda i: (0, i))],
        out_specs=pl.BlockSpec((F, step), lambda i: (0, i)),
        out_shape=jax.ShapeDtypeStruct((F, D), jnp.bfloat16),
        compiler_params=pltpu.CompilerParams(vmem_limit_bytes=VMEM),
        cost_estimate=pl.CostEstimate(flops=2 * T * D * F, bytes_accessed=16 * 2**20, transcendentals=0),
        name="down_grad")(hid, dy)

def down_body(order, hid_a_ref, hid_b_ref, wd_a_ref, wd_b_ref, o_ref):
    out = nn(hid_a_ref[...], wd_a_ref[...]) + nn(hid_b_ref[...], wd_b_ref[...])
    o_ref[...] = out.astype(jnp.bfloat16)


def down(order, hid_a, hid_b, wd_a, wd_b):
    count = hid_a.shape[0]
    step = count // order.shape[0]

    def placed(array):
        return pl.BlockSpec((step, array.shape[1]), lambda i, order: (order[i], 0))

    def whole(array):
        return pl.BlockSpec(array.shape, lambda i, order: (0, 0), pipeline_mode=pl.Buffered(1))

    return pl.pallas_call(
        down_body,
        grid_spec=pltpu.PrefetchScalarGridSpec(
            num_scalar_prefetch=1,
            grid=(count // step,),
            in_specs=[placed(hid_a), placed(hid_b), whole(wd_a), whole(wd_b)],
            out_specs=pl.BlockSpec((step, D), lambda i, order: (i, 0)),
        ),
        out_shape=jax.ShapeDtypeStruct((count, D), jnp.bfloat16),
        compiler_params=pltpu.CompilerParams(vmem_limit_bytes=VMEM),
        cost_estimate=pl.CostEstimate(
            flops=2 * count * D * (hid_a.shape[1] + hid_b.shape[1]), bytes_accessed=16 * 2**20, transcendentals=0
        ),
        name="down",
    )(order, hid_a, hid_b, wd_a, wd_b)


CORE = [(0, 1), (1, 0), (2, 3), (3, 2)]
CROSS = [(0, 2), (2, 0), (1, 3), (3, 1)]
DIAG = [(0, 3), (3, 0), (1, 2), (2, 1)]


def low(values):
    return values.astype(jnp.bfloat16)


def wide(values):
    return values.astype(jnp.float32)


def swap_core(values):
    return lax.ppermute(values, "grp", CORE)


def swap_cross(values):
    return lax.ppermute(values, "grp", CROSS)


def swap_diag(values):
    return lax.ppermute(values, "grp", DIAG)


def swap_blk(values, bit):
    count = lax.axis_size("blk")
    return lax.ppermute(values, "blk", [(i, i ^ bit) for i in range(count)])


def blk_bit(bit):
    return (lax.axis_index("blk") & bit) != 0


def bits_of(count):
    out = []
    bit = count // 2
    while bit >= 1:
        out.append(bit)
        bit //= 2
    return out


def gather_bits(values, order):
    done = []
    for bit in order:
        other = swap_blk(values, bit)
        mine = blk_bit(bit)
        axis = sum(1 for d in done if d > bit)
        values = jnp.stack(
            [jnp.where(mine, other, values), jnp.where(mine, values, other)], axis=axis
        )
        done.append(bit)
    return values


def scatter_bits(values, axes, order):
    axes = list(axes)
    for bit in order:
        axis = axes.index(bit)
        mine = blk_bit(bit).astype(jnp.int32)
        keep = lax.dynamic_index_in_dim(values, mine, axis, keepdims=False)
        send = lax.dynamic_index_in_dim(values, 1 - mine, axis, keepdims=False)
        values = low(wide(keep) + wide(swap_blk(send, bit)))
        axes.remove(bit)
    return values


def by_place(parts):
    grp = lax.axis_index("grp")
    core = (grp & 1) != 0
    cross = (grp & 2) != 0
    a, b, c, d = parts
    a, b = jnp.where(core, b, a), jnp.where(core, a, b)
    c, d = jnp.where(core, d, c), jnp.where(core, c, d)
    a, c = jnp.where(cross, c, a), jnp.where(cross, a, c)
    b, d = jnp.where(cross, d, b), jnp.where(cross, b, d)
    return [a, b, c, d]


def gather_near(values):
    cross = swap_cross(values)
    both = swap_core(jnp.stack([values, cross]))
    return [values, both[0], cross, both[1]]


def gather_grp(values):
    return by_place(gather_near(values))


def gather_tokens(values, bit):
    half = values.shape[0] // 2
    cross = swap_cross(values)
    over = swap_blk(values, bit)
    first = swap_blk(cross[:half], bit)
    second = swap_cross(over[half:])
    chip = jnp.concatenate([values, cross, over, first, second])
    return jnp.concatenate([chip, swap_core(chip)])


def angles_of(position):
    half = HD // 2
    freqs = ROPE_BASE ** (-2.0 * jnp.arange(half, dtype=jnp.float32) / HD)
    return position.astype(jnp.float32)[:, None] * freqs[None, :]


def rotate_by(values, cosine, sine):
    half = HD // 2
    first_half = values[..., :half]
    second_half = values[..., half:]
    return jnp.concatenate(
        [first_half * cosine - second_half * sine, second_half * cosine + first_half * sine],
        axis=-1,
    )


def after(values, anchor):
    return lax.optimization_barrier((values, anchor))[0]


def gather_step(values, done, bit):
    other = swap_blk(values, bit)
    mine = blk_bit(bit)
    axis = sum(1 for d in done if d > bit)
    return jnp.stack(
        [jnp.where(mine, other, values), jnp.where(mine, values, other)], axis=axis
    )


def on_device(
    tokens,
    cotangent,
    segment_ids,
    position_ids,
    w_attend,
    w_out,
    w_gate,
    w_up,
    w_down,
    small_params,
    first_attend,
    first_out,
    first_gate,
    first_up,
    first_down,
    first_small,
    second_attend,
    second_out,
    second_gate,
    second_up,
    second_down,
    second_small,
):
    rows_here, block_len = tokens.shape[:2]
    blk_count = lax.axis_size("blk")
    seq_len = block_len * blk_count
    token_count = rows_here * block_len
    grp = lax.axis_index("grp")
    blk = lax.axis_index("blk")
    cross_id, core_id = grp // 2, grp % 2
    strip_heads = H // 4
    strip_q = strip_heads * HD
    bits = bits_of(blk_count)
    team = blk_count // 4
    lows = [bit for bit in bits if bit < team]
    spread = [bits[0]] + lows
    low_shape = (2,) * len(lows)
    in_team = blk_bit(team).astype(jnp.int32)
    weight_rows = w_gate.shape[0]
    ff_block = w_down.shape[0]
    quarter = ff_block // 4
    widths = [size * blk_count // 2 for at, size in halves_of(quarter)]
    chip_rows = 4 * token_count
    half = token_count // 2

    ids = jnp.stack([grp, in_team])
    flat_low = tokens.reshape(token_count, D)
    dy_low = cotangent.reshape(token_count, D)
    positions = position_ids.reshape(token_count)
    kv_at = HQD + HD * cross_id + KVD * core_id
    strip_local = low(
        jnp.concatenate(
            [
                lax.dynamic_slice_in_dim(w_attend, strip_q * grp, strip_q, 1),
                lax.dynamic_slice_in_dim(w_attend, kv_at, HD, 1),
            ],
            axis=1,
        )
    )
    small_count = small_params.shape[0]
    small_send = jnp.concatenate([low(small_params), low(segment_ids.reshape(token_count))])
    strip_wide = strip_q + HD
    small_send = jnp.pad(small_send, (0, -small_send.shape[0] % strip_wide))
    strip_local = jnp.concatenate([strip_local, small_send.reshape(-1, strip_wide)])
    strip_first = gather_step(strip_local, [], bits[0])
    strip_parts = []
    cut = strip_wide // 2
    for part, order in (
        (strip_first[..., :cut], [team] + lows),
        (strip_first[..., cut:], lows + [team]),
    ):
        done = [bits[0]]
        for bit in order:
            part = gather_step(part, done, bit)
            done.append(bit)
        strip_parts.append(part)
    strip_all = jnp.concatenate(strip_parts, axis=-1).reshape(blk_count, -1, strip_wide)
    strip = strip_all[:, :weight_rows].reshape(D, strip_wide)
    small_all = strip_all[:, weight_rows:].reshape(blk_count, -1)
    digits = low(jnp.stack([positions // 64, positions % 64], axis=1))
    digits = jnp.pad(digits, ((0, 0), (0, HD - 2)))
    near_all = jnp.concatenate(gather_near(jnp.concatenate([flat_low, digits], axis=1)))
    near_tokens = near_all[:, :D]
    near_positions = 64.0 * wide(near_all[:, D]) + wide(near_all[:, D + 1])
    vector = wide(small_all[:, :small_count].reshape(-1))
    gain_one = vector[:D]
    gain_two = vector[D : 2 * D]
    bias = vector[2 * D :]
    strip_bias = jnp.concatenate(
        [
            lax.dynamic_slice_in_dim(bias, strip_q * grp, strip_q, 0),
            lax.dynamic_slice_in_dim(bias, kv_at, HD, 0),
        ]
    )
    seg_all = small_all[:, small_count : small_count + token_count].astype(jnp.int32)
    seg_all = seg_all.reshape(blk_count, rows_here, block_len)
    seg_key = jnp.broadcast_to(
        seg_all.transpose(1, 0, 2).reshape(rows_here, seq_len)[:, :, None], (rows_here, seq_len, HD)
    )
    seg_query = jnp.broadcast_to(segment_ids[:, None, :], (rows_here, 8, block_len))
    first_blk = jnp.sum((seg_all[:, :, -1] < segment_ids[None, :, 0]).astype(jnp.int32), axis=0)
    attend_ids = jnp.concatenate([blk[None], first_blk])

    near_wide = wide(near_tokens)
    near_one = low(norm_apply(near_wide, gain_one))
    mixed = jnp.dot(near_one, strip, preferred_element_type=jnp.float32) + strip_bias
    angles = angles_of(near_positions)[:, None, :]
    turned = jnp.arange(strip_heads + 1)[None, :, None] < strip_heads + 1 - core_id
    angles = jnp.where(turned, angles, 0.0)
    strip_out = low(
        rotate_by(
            mixed.reshape(4 * token_count, strip_heads + 1, HD), jnp.cos(angles), jnp.sin(angles)
        )
    ).reshape(4, token_count, strip_q + HD)
    strips = by_place(
        [
            strip_out[0],
            swap_core(strip_out[1]),
            swap_cross(strip_out[2]),
            swap_diag(strip_out[3]),
        ]
    )
    query = jnp.concatenate([part[:, :strip_q] for part in strips], axis=1)
    key_value = jnp.concatenate([strips[k][:, strip_q:] for k in (0, 2, 1, 3)], axis=1)
    key_value = key_value.reshape(rows_here, block_len, 2 * KVD)
    kv_first = gather_step(key_value, [], bits[0])
    kv_parts = []
    for part, order in (
        (kv_first[..., :KVD], [team] + lows),
        (kv_first[..., KVD:], lows + [team]),
    ):
        done = [bits[0]]
        for bit in order:
            part = gather_step(part, done, bit)
            done.append(bit)
        kv_parts.append(part)
    kv_all = jnp.concatenate(kv_parts, axis=-1).reshape((blk_count,) + key_value.shape)

    teams = [
        [g * blk_count + (i | t) for g in range(4) for t in (0, team)]
        for i in range(blk_count)
        if not i & team
    ]
    dy_team = lax.all_gather(dy_low, ("grp", "blk"), axis=0, tiled=True, axis_index_groups=teams)
    order = jnp.stack(
        [
            (grp ^ (2 * (i & 1) + (i >> 2))) * 2 + (in_team ^ ((i >> 1) & 1))
            for i in range(8)
        ]
    )

    mine_team = blk_bit(team)
    peers = [[i for i in range(blk_count) if (i & team) == t] for t in (0, team)]
    (low_first, size_first), (low_second, size_second) = halves_of(quarter)

    def place(values, other, done, bit):
        mine = blk_bit(bit)
        axis = sum(1 for d in done if d > bit)
        return jnp.stack(
            [jnp.where(mine, other, values), jnp.where(mine, values, other)], axis=axis
        )

    def lows_of(values, done, anchor):
        for bit in lows:
            values = place(values, after(swap_blk(values, bit), anchor), done, bit)
            done = done + [bit]
        return values

    def team_pair(mine, got):
        return jnp.stack([jnp.where(mine_team, got, mine), jnp.where(mine_team, mine, got)])

    def whole_weights(pair):
        pairs = lax.all_gather(pair, "blk", axis=0, axis_index_groups=peers)
        pairs = pairs.reshape((2, blk_count // 4) + pair.shape).transpose(3, 0, 2, 1, 4, 5)
        return pairs[0].reshape(D, -1), pairs[1].reshape(D, -1)

    picked_a, picked_b = pick_columns(ids, w_gate, w_up, blk_count)
    got_a = swap_blk(after(picked_a[1], strip_parts), team)
    gate_a, up_a = whole_weights(team_pair(picked_a[0], after(got_a, strips)))
    got_b = swap_blk(after(picked_b[1], strip_out), team)
    gate_b, up_b = whole_weights(team_pair(picked_b[0], after(got_b, kv_all)))

    down_at = quarter * grp
    down_a = low(lax.dynamic_slice_in_dim(w_down, down_at, size_first, 0))
    down_got = swap_blk(after(down_a, strip_first), bits[0])
    down_a = place(down_a, after(down_got, strip_out), [], bits[0])
    down_a = lows_of(down_a, [bits[0]], kv_all).reshape(widths[0], D)

    out_strip = low(lax.dynamic_slice_in_dim(w_out, strip_q * grp, strip_q, 1))
    out_got = swap_blk(after(out_strip, strip_first), bits[0])
    out_strip = place(out_strip, after(out_got, strip_parts), [], bits[0])
    out_got = swap_blk(out_strip, team)
    out_strip = place(out_strip, after(out_got, strip_out), [bits[0]], team)
    out_strip = lows_of(out_strip, [bits[0], team], kv_first).reshape(HQD, strip_q)
    out_cross = after(swap_cross(out_strip), kv_all)
    out_both = jnp.stack([out_strip, out_cross])
    out_core = swap_core(out_both)
    out_full = jnp.concatenate(by_place([out_strip, out_core[0], out_cross, out_core[1]]), axis=1)

    down_b = low(lax.dynamic_slice_in_dim(w_down, down_at + size_first, size_second, 0))
    down_got_b = swap_blk(after(down_b, kv_all), bits[0])

    att_in, lse = attend(attend_ids, query, kv_all, seg_key, seg_query, block_len)
    down_b = place(down_b, after(down_got_b, att_in), [], bits[0])

    flat = wide(flat_low)
    resid = flat + jnp.dot(att_in, out_full, preferred_element_type=jnp.float32)
    h_two = low(norm_apply(resid, gain_two))
    h_team = gather_tokens(h_two, team)
    hidden_a, d_gate_a, d_up_a, part_a = middle(order, h_team, dy_team, gate_a, up_a, down_a)
    down_b = lows_of(down_b, [bits[0]], hidden_a).reshape(widths[1], D)
    down_share_a = lax.psum_scatter(
        down_grad(hidden_a, dy_team), "blk", scatter_dimension=0, axis_index_groups=peers, tiled=True
    )
    column_grad_a = two_grads(h_team, d_gate_a, d_up_a)

    def part_sent(values, axis, bit):
        mine = blk_bit(bit).astype(jnp.int32)
        keep = lax.dynamic_index_in_dim(values, mine, axis, keepdims=False)
        send = lax.dynamic_index_in_dim(values, 1 - mine, axis, keepdims=False)
        return keep, swap_blk(send, bit)

    def part_sum(keep, got):
        return low(wide(keep) + wide(got))

    def columns_first(grad):
        grad = grad.reshape((2, 2, 2) + low_shape + (weight_rows, -1))
        return part_sent(grad, 2 + len(lows), lows[-1])

    def columns_second(keep, got):
        values = part_sum(keep, got)
        for i in range(len(lows) - 2, -1, -1):
            values = part_sum(*part_sent(values, 3 + i, lows[i]))
        return part_sent(values, 1, bits[0])

    def columns_third(keep, got):
        values = part_sum(keep, got)
        mine = lax.dynamic_index_in_dim(values, in_team, 1, keepdims=False)
        send = lax.dynamic_index_in_dim(values, 1 - in_team, 1, keepdims=False)
        return mine, swap_blk(send, team)

    def columns_last(mine, got):
        return jnp.stack(
            [jnp.where(mine_team, got, mine), jnp.where(mine_team, mine, got)], axis=1
        )

    first_a = columns_first(column_grad_a)
    hidden_b, d_gate_b, d_up_b, d_htwo_part = middle(
        order, after(h_team, column_grad_a), dy_team, gate_b, up_b, down_b, part_a
    )

    def chip_sum(values, came):
        return low(wide(values[:chip_rows]) + wide(came))

    def scatter_far(chip):
        far = chip[3 * token_count :]
        return swap_blk(far[:half], team), swap_cross(far[half:])

    def scatter_near(chip, first, second):
        cross, over = (chip[token_count * i : token_count * (i + 1)] for i in (1, 2))
        cross = jnp.concatenate([low(wide(cross[:half]) + wide(first)), cross[half:]])
        over = jnp.concatenate([over[:half], low(wide(over[half:]) + wide(second))])
        return swap_cross(cross), swap_blk(over, team)

    d_came = swap_core(d_htwo_part[chip_rows:])
    down_grad_b = down_grad(hidden_b, dy_team)
    down_share_b = lax.psum_scatter(
        down_grad_b, "blk", scatter_dimension=0, axis_index_groups=peers, tiled=True
    )
    d_chip = chip_sum(d_htwo_part, after(d_came, down_grad_b))
    d_far = scatter_far(d_chip)
    column_grad_b = two_grads(h_team, *after((d_gate_b, d_up_b), d_chip))
    first_b = columns_first(column_grad_b)
    d_far = after(d_far, column_grad_b)
    d_cross, d_over = scatter_near(d_chip, *d_far)
    out_part = down(order, *after((hidden_a, hidden_b), d_far), down_a, down_b)
    out_came = swap_core(out_part[chip_rows:])
    second_a = columns_second(*after(first_a, out_part))
    d_cross, d_over = after((d_cross, d_over), out_part)
    d_htwo = wide(d_chip[:token_count]) + wide(d_cross) + wide(d_over)

    norm_value_two, norm_back_two = jax.vjp(norm_apply, resid, gain_two)
    d_resid_norm, grad_gain_two = norm_back_two(d_htwo)
    d_resid = wide(dy_low) + d_resid_norm
    d_att = low(d_resid)

    d_attended = low(right_transposed(d_att, out_full))
    own_angles = angles_of(positions)
    cosine, sine = jnp.cos(own_angles), jnp.sin(own_angles)
    d_query, dkv = attend_back(
        attend_ids,
        query,
        kv_all,
        seg_key,
        seg_query,
        att_in,
        d_attended,
        lse,
        jnp.concatenate([cosine, cosine], axis=1),
        jnp.concatenate([sine, sine], axis=1),
        block_len,
    )
    second_b = columns_second(*after(first_b, d_query))
    third_a = columns_third(*after(second_a, d_query))
    dkv = dkv.reshape((2,) * len(bits) + (rows_here, block_len, 2 * KVD))
    dkv_first = scatter_bits(dkv[..., :KVD], bits, lows[::-1])
    dkv_second = scatter_bits(dkv[..., KVD:], bits, [team])
    dkv_first = scatter_bits(dkv_first, bits[:2], [team])
    dkv_second = scatter_bits(dkv_second, [bits[0]] + lows, lows[::-1])
    dkv = jnp.concatenate([dkv_first, dkv_second], axis=-1)
    dkv_mid = dkv
    out_chip = chip_sum(out_part, after(out_came, dkv_mid))
    dkv = wide(scatter_bits(dkv, bits[:1], bits[:1])).reshape(token_count, 2, KVH, HD)
    d_key = low(rotate_by(dkv[:, 0], cosine[:, None], -sine[:, None]))
    d_value = low(dkv[:, 1])
    out_far = after(scatter_far(out_chip), d_key)
    out_cross, out_over = scatter_near(out_chip, *out_far)
    third_b = columns_third(*after(second_b, d_key))
    share_a = columns_last(*after(third_a, dkv_mid))
    all_a = lax.all_gather(share_a, "grp", axis=0)
    share_down = jnp.concatenate([down_share_a, down_share_b])
    grad_down = lax.all_gather(share_down, "grp", axis=0, tiled=True)

    def to_strips(parts):
        parts = by_place(parts)
        return jnp.concatenate(
            [parts[0], swap_core(parts[1]), swap_cross(parts[2]), swap_diag(parts[3])]
        )

    near_dq = to_strips([d_query[:, strip_q * k : strip_q * (k + 1)] for k in range(4)])
    block_shape = (2,) * len(bits) + (weight_rows, -1)
    query_grad = low(left_product(near_one, near_dq)).reshape(block_shape)
    steps_query = part_sent(after(query_grad, dkv_mid), len(bits) - 1, bits[-1])
    near_dkv = to_strips([(d_value if k % 2 else d_key)[:, k // 2] for k in range(4)])
    kv_grad = low(left_product(near_one, near_dkv)).reshape(block_shape)
    steps_kv = part_sent(kv_grad, len(bits) - 1, bits[-1])
    for i in range(len(bits) - 2, -1, -1):
        steps_query = part_sent(part_sum(*after(steps_query, kv_grad)), i, bits[i])
        kv_sum = part_sum(*steps_kv)
        kv_grad = kv_sum
        steps_kv = part_sent(kv_sum, i, bits[i])
    share_kv = part_sum(*steps_kv)
    share_query = part_sum(*after(steps_query, share_kv))
    grad_bias = jnp.concatenate(
        [
            jnp.sum(wide(part), axis=0)
            for part in (d_query, d_key.reshape(token_count, KVD), d_value.reshape(token_count, KVD))
        ]
    )
    out_cross, out_over = after((out_cross, out_over), near_dkv)
    out_tokens = low(resid + wide(out_chip[:token_count]) + wide(out_cross) + wide(out_over))
    near_hone = right_transposed(near_dq, strip[:, :strip_q]) + right_transposed(
        near_dkv, strip[:, strip_q:]
    )
    near_rms = lax.rsqrt(jnp.mean(near_wide * near_wide, axis=-1, keepdims=True) + NORM_EPS)
    gain_one_part = jnp.sum(near_hone * near_wide * near_rms, axis=0)

    near_att = jnp.concatenate(gather_near(att_in))
    near_datt = to_strips([d_att[:, strip_q * k : strip_q * (k + 1)] for k in range(4)])
    out_grad = low(left_product(near_att, after(near_datt, d_attended))).reshape(block_shape)
    steps_out = part_sent(out_grad, len(bits) - 1, bits[-1])
    anchors = [dkv_mid, near_dkv]
    for i in range(len(bits) - 2, -1, -1):
        anchor = anchors[min(len(bits) - 2 - i, 1)]
        steps_out = part_sent(part_sum(*after(steps_out, anchor)), i, bits[i])
    share_out = part_sum(*after(steps_out, kv_grad))

    vector_term = jnp.concatenate([gain_one_part, grad_gain_two, grad_bias])
    vector_term = vector_term + swap_cross(vector_term)
    vector_term = vector_term + swap_core(vector_term)
    vector_term = vector_term.reshape((2,) * len(bits) + (-1,))
    axes = list(bits)
    for bit in bits[::-1]:
        axis = axes.index(bit)
        mine = blk_bit(bit).astype(jnp.int32)
        keep = lax.dynamic_index_in_dim(vector_term, mine, axis, keepdims=False)
        send = lax.dynamic_index_in_dim(vector_term, 1 - mine, axis, keepdims=False)
        vector_term = keep + swap_blk(send, bit)
        axes.remove(bit)
    share_vector = vector_term

    share_b = columns_last(*after(third_b, near_dkv))
    all_b = lax.all_gather(share_b, "grp", axis=0)
    grad_out = jnp.concatenate(gather_grp(share_out), axis=1)
    query_parts = gather_grp(share_query)
    key_parts = gather_grp(share_kv)
    grad_attend = jnp.concatenate(query_parts + [key_parts[k] for k in (0, 2, 1, 3)], axis=1)

    sides = low(near_hone[token_count : 2 * token_count]), low(near_hone[3 * token_count :])
    other = wide(swap_core(jnp.concatenate(sides)))
    d_hone = near_hone[:token_count] + other[:token_count]
    d_hone_cross = swap_cross(
        low(near_hone[2 * token_count : 3 * token_count] + other[token_count:])
    )
    square_sum = square_total(
        [
            wide(s)
            for s in (share_query, share_kv, share_out, share_a, share_b, share_down)
        ]
    ) + 0.25 * jnp.sum(share_vector * share_vector)
    square_sum = jnp.full((8, 128), square_sum)
    for bit in bits:
        square_sum = square_sum + swap_blk(square_sum, bit)
    square_sum = square_sum + swap_cross(square_sum)
    square_sum = square_sum + swap_core(square_sum)
    grad_norm = jnp.sqrt(square_sum[0, 0])
    factor = jnp.minimum(1.0, CLIP_NORM / (grad_norm + 1e-06))
    factor = after(factor, out_tokens)

    new_first_gate, new_second_gate, new_gate = adam_columns(
        0, factor[None], all_a, all_b, w_gate, first_gate, second_gate, blk_count, RATE_GATE, WEIGHT_DECAY
    )
    new_first_up, new_second_up, new_up = adam_columns(
        1, factor[None], all_a, all_b, w_up, first_up, second_up, blk_count, RATE_GATE, WEIGHT_DECAY
    )
    norm_value_one, norm_back_one = jax.vjp(norm_apply, flat, gain_one)
    d_hone = after(d_hone + wide(after(d_hone_cross, new_gate)), new_gate)
    d_flat_norm, unused_gain = norm_back_one(d_hone)
    grad_tokens = low(d_resid + d_flat_norm)

    new_first_attend, new_second_attend, new_attend = adam_step(
        w_attend, factor * wide(grad_attend), first_attend, second_attend, RATE_ATTEND, WEIGHT_DECAY
    )
    new_first_out, new_second_out, new_out = adam_step(
        w_out, factor * wide(grad_out), first_out, second_out, RATE_OUT, WEIGHT_DECAY
    )
    new_first_down, new_second_down, new_down = adam_step(
        w_down, factor * wide(grad_down), first_down, second_down, RATE_DOWN, WEIGHT_DECAY
    )
    new_first_small, new_second_small, new_small = adam_step(
        small_params, factor * share_vector, first_small, second_small, RATE_VECTOR, 0.0
    )
    return (
        out_tokens.reshape(rows_here, block_len, D),
        grad_tokens.reshape(rows_here, block_len, D),
        grad_norm,
        new_first_attend,
        new_second_attend,
        new_attend,
        new_first_out,
        new_second_out,
        new_out,
        new_first_gate,
        new_second_gate,
        new_gate,
        new_first_up,
        new_second_up,
        new_up,
        new_first_down,
        new_second_down,
        new_down,
        new_first_small,
        new_second_small,
        new_small,
    )


def solution(mesh):
    placed = (
        P("grp", "blk", None),
        P("grp", "blk", None),
        P("grp", "blk"),
        P("grp", "blk"),
        P("blk", None),
        P("blk", None),
        P("blk", None),
        P("blk", None),
        P("blk", None),
        P("blk"),
        P("blk", None),
        P("blk", None),
        P("blk", None),
        P("blk", None),
        P("blk", None),
        P("blk"),
        P("blk", None),
        P("blk", None),
        P("blk", None),
        P("blk", None),
        P("blk", None),
        P("blk"),
    )
    return jax.shard_map(
        on_device,
        mesh=mesh,
        in_specs=placed,
        out_specs=(
            P("grp", "blk", None),
            P("grp", "blk", None),
            P(),
            P("blk", None),
            P("blk", None),
            P("blk", None),
            P("blk", None),
            P("blk", None),
            P("blk", None),
            P("blk", None),
            P("blk", None),
            P("blk", None),
            P("blk", None),
            P("blk", None),
            P("blk", None),
            P("blk", None),
            P("blk", None),
            P("blk", None),
            P("blk"),
            P("blk"),
            P("blk"),
        ),
        check_vma=False,
    )
```

```python
import functools

import jax
import jax.numpy as jnp
from jax import lax
from jax.experimental import pallas as pl
from jax.experimental.pallas import tpu as pltpu
from jax.sharding import PartitionSpec as P

D = 1536
FF = 8960
H = 12
KVH = 2
HD = 128
STEP = 10
HQD = 1536
KVD = 256


NORM_EPS = 1e-06
ROPE_BASE = 10000.0
CLIP_NORM = 1.0
BETA_FIRST = 0.9
BETA_SECOND = 0.95
ADAM_EPS = 1e-08
WEIGHT_DECAY = 0.1
RATE_ATTEND = 0.06
RATE_OUT = 0.5
RATE_GATE = 0.06
RATE_DOWN = 0.03
RATE_VECTOR = 0.5
NEG_LARGE = -1e30
LOG2E = 1.4426950408889634
VMEM = 48 * 1024 * 1024


def norm_apply(values, gain):
    return values * lax.rsqrt(jnp.mean(values * values, axis=-1, keepdims=True) + NORM_EPS) * gain


def swish_product(gate, up_proj):
    return jax.nn.silu(gate) * up_proj


def left_product(left_side, right_side):
    return lax.dot_general(
        left_side, right_side, (((0,), (0,)), ((), ())), preferred_element_type=jnp.float32
    )


def right_transposed(left_side, right_side):
    return lax.dot_general(
        left_side, right_side, (((1,), (1,)), ((), ())), preferred_element_type=jnp.float32
    )


def square_total(arrays):
    return sum((jnp.sum(member * member) for member in arrays))


def adam_step(weight, grad, first, second, rate, decay):
    first_new = BETA_FIRST * first + (1.0 - BETA_FIRST) * grad
    second_new = BETA_SECOND * second + (1.0 - BETA_SECOND) * grad * grad
    first_hat = first_new / (1.0 - BETA_FIRST**STEP)
    second_hat = second_new / (1.0 - BETA_SECOND**STEP)
    weight_new = weight - rate * (first_hat / (jnp.sqrt(second_hat) + ADAM_EPS) + decay * weight)
    return (first_new, second_new, weight_new)


def halves_of(quarter):
    first = quarter * 16 // 35
    return ((0, first), (first, quarter - first))


def pick_body(blk_count, ids, gate_ref, up_ref, *out_refs):
    quarter = FF // blk_count // 4
    per = blk_count // 4
    for k in range(4):

        @pl.when(ids[0] == k)
        def _(k=k):
            for (at, size), out_ref in zip(halves_of(quarter), out_refs):
                for which, src in enumerate((gate_ref, up_ref)):
                    for bit in range(2):
                        parts = []
                        for high in range(2):
                            for small in range(per):
                                begin = (((high * 2 + bit) * per + small) * 4 + k) * quarter + at
                                parts.append(src[:, begin : begin + size])
                        out_ref[ids[1] ^ bit, which] = jnp.concatenate(parts, axis=1).astype(
                            jnp.bfloat16
                        )


def pick_columns(ids, gate, up, blk_count):
    rows = gate.shape[0]
    step = 48 if rows % 48 == 0 else rows
    widths = [size * blk_count // 2 for at, size in halves_of(FF // blk_count // 4)]
    spec = pl.BlockSpec((step, FF), lambda i, ids: (i, 0))
    return pl.pallas_call(
        functools.partial(pick_body, blk_count),
        grid_spec=pltpu.PrefetchScalarGridSpec(
            num_scalar_prefetch=1,
            grid=(rows // step,),
            in_specs=[spec, spec],
            out_specs=[pl.BlockSpec((2, 2, step, w), lambda i, ids: (0, 0, i, 0)) for w in widths],
        ),
        out_shape=[jax.ShapeDtypeStruct((2, 2, rows, w), jnp.bfloat16) for w in widths],
        compiler_params=pltpu.CompilerParams(vmem_limit_bytes=VMEM),
        cost_estimate=pl.CostEstimate(flops=0, bytes_accessed=rows * FF * 10, transcendentals=0),
        name="pick_columns",
    )(ids, gate, up)


def near_at(away):
    return (away & 1) * 2 + (away >> 1)


def adam_body(blk_count, rate, decay, ids, factor_ref, first_ref, second_ref, w_ref, m_ref, v_ref, m_out, v_out, w_out):
    per = blk_count // 4
    sizes = [size for at, size in halves_of(FF // blk_count // 4)]
    grads = [
        [[ref[near_at(ids[0] ^ k), bit] for bit in range(2)] for k in range(4)]
        for ref in (first_ref, second_ref)
    ]
    parts = []
    for high in range(2):
        for bit in range(2):
            for small in range(per):
                place = high * per + small
                for k in range(4):
                    for part, size in zip(grads, sizes):
                        parts.append(part[k][bit][:, place * size : (place + 1) * size])
    grad = jnp.concatenate(parts, axis=1).astype(jnp.float32) * factor_ref[0]
    m, v, w = adam_step(w_ref[...], grad, m_ref[...], v_ref[...], rate, decay)
    m_out[...] = m
    v_out[...] = v
    w_out[...] = w


def adam_columns(which, ids, factor, first, second, w, m, v, blk_count, rate, decay):
    rows = w.shape[0]
    step = 32 if rows % 32 == 0 else rows
    spec = pl.BlockSpec((step, FF), lambda i, ids: (i, 0))
    shape = jax.ShapeDtypeStruct((rows, FF), jnp.float32)
    grads = [
        pl.BlockSpec((4, None, 2, step, g.shape[-1]), lambda i, ids: (0, which, 0, i, 0))
        for g in (first, second)
    ]
    return pl.pallas_call(
        functools.partial(adam_body, blk_count, rate, decay),
        grid_spec=pltpu.PrefetchScalarGridSpec(
            num_scalar_prefetch=1,
            grid=(rows // step,),
            in_specs=[pl.BlockSpec(memory_space=pltpu.SMEM)] + grads + [spec, spec, spec],
            out_specs=[spec, spec, spec],
        ),
        out_shape=[shape] * 3,
        compiler_params=pltpu.CompilerParams(vmem_limit_bytes=VMEM),
        cost_estimate=pl.CostEstimate(
            flops=rows * FF * 20, bytes_accessed=rows * FF * 26, transcendentals=rows * FF
        ),
        name="adam_columns",
    )(ids, factor, first, second, w, m, v)


def nt(a, b, **kw):
    return lax.dot_general(a, b, (((1,), (1,)), ((), ())), preferred_element_type=jnp.float32, **kw)

def tn(a, b, **kw):
    return lax.dot_general(a, b, (((0,), (0,)), ((), ())), preferred_element_type=jnp.float32, **kw)

def stack_heads(ref, kvh, group):
    return jnp.concatenate([ref[:, HD * (kvh * group + i): HD * (kvh * group + i + 1)] for i in range(group)], axis=0)

def hidden_from(seg_key_ref, seg_query_ref, first, chunk, block_len, blk):
    key = first + lax.broadcasted_iota(jnp.int32, (chunk, block_len), 0)
    query = blk * block_len + lax.broadcasted_iota(jnp.int32, (chunk, block_len), 1)
    seg_key = seg_key_ref[pl.ds(first, chunk), :]
    counts = jnp.logical_and(key <= query, seg_key == seg_query_ref[0:1, :])
    return jnp.where(counts, 0.0, NEG_LARGE)

def attend_body(chunk, ids, q_ref, k_ref, v_ref, seg_key_ref, seg_query_ref, o_ref, lse_ref, m_s, l_s, acc_s):
    block_len = q_ref.shape[0]
    group = H // KVH
    row = pl.program_id(0)
    per = chunk // block_len
    scale = HD ** (-0.5) * LOG2E
    start = ids[1 + row] // per
    stop = ids[0] // per + 1
    for kvh in range(KVH):
        q = stack_heads(q_ref, kvh, group)
        m_s[...] = jnp.full_like(m_s, NEG_LARGE)
        l_s[...] = jnp.zeros_like(l_s)
        acc_s[...] = jnp.zeros_like(acc_s)

        def step(c, carry):
            keys = k_ref[pl.ds(c * per, per), :, HD * kvh: HD * (kvh + 1)].reshape(chunk, HD)
            vals = v_ref[pl.ds(c * per, per), :, HD * kvh: HD * (kvh + 1)].reshape(chunk, HD)
            bias = hidden_from(seg_key_ref, seg_query_ref, c * chunk, chunk, block_len, ids[0])
            s = nt(keys, q) * scale + jnp.concatenate([bias] * group, axis=1)
            old = m_s[0:1, :]
            new = jnp.maximum(old, jnp.max(s, axis=0, keepdims=True))
            p = jnp.exp2(s - new)
            fade = jnp.exp2(old - new)
            l_s[0:1, :] = l_s[0:1, :] * fade + jnp.sum(p, axis=0, keepdims=True)
            acc_s[...] = acc_s[...] * fade + tn(vals, p.astype(jnp.bfloat16))
            m_s[0:1, :] = new
            return carry

        lax.fori_loop(start, stop, step, 0)
        total = l_s[0:1, :]
        out = (acc_s[...] * (1.0 / total)).T
        for i in range(group):
            o_ref[:, HD * (kvh * group + i): HD * (kvh * group + i + 1)] = out[block_len * i: block_len * (i + 1), :].astype(jnp.bfloat16)
        lse_ref[kvh] = jnp.broadcast_to(m_s[0:1, :] + jnp.log2(total), (8, group * block_len))

def attend(ids, q, kv, seg_key, seg_query, block_len):
    blk_count, rows = kv.shape[:2]
    group = H // KVH
    chunk = 2 * block_len
    many = group * block_len
    return pl.pallas_call(
        functools.partial(attend_body, chunk),
        grid_spec=pltpu.PrefetchScalarGridSpec(
            num_scalar_prefetch=1, grid=(rows,),
            in_specs=[
                pl.BlockSpec((block_len, HQD), lambda r, ids: (r, 0)),
                pl.BlockSpec((blk_count, None, block_len, KVD), lambda r, ids: (0, r, 0, 0)),
                pl.BlockSpec((blk_count, None, block_len, KVD), lambda r, ids: (0, r, 0, 1)),
                pl.BlockSpec((None, blk_count * block_len, HD), lambda r, ids: (r, 0, 0)),
                pl.BlockSpec((None, 8, block_len), lambda r, ids: (r, 0, 0)),
            ],
            out_specs=[
                pl.BlockSpec((block_len, HQD), lambda r, ids: (r, 0)),
                pl.BlockSpec((None, KVH, 8, many), lambda r, ids: (r, 0, 0, 0)),
            ],
            scratch_shapes=[pltpu.VMEM((8, many), jnp.float32), pltpu.VMEM((8, many), jnp.float32), pltpu.VMEM((HD, many), jnp.float32)]),
        out_shape=[
            jax.ShapeDtypeStruct((rows * block_len, HQD), jnp.bfloat16),
            jax.ShapeDtypeStruct((rows, KVH, 8, many), jnp.float32),
        ],
        compiler_params=pltpu.CompilerParams(vmem_limit_bytes=VMEM),
        cost_estimate=pl.CostEstimate(flops=4 * rows * H * block_len * blk_count * block_len * HD, bytes_accessed=8 * 2**20, transcendentals=rows * H * block_len * blk_count * block_len),
        name="attend",
    )(ids, q, kv, kv, seg_key, seg_query)

def turn_back(u, cosine, sine):
    lane = lax.broadcasted_iota(jnp.int32, u.shape, 1)
    other = pltpu.roll(u, HD // 2, 1)
    return u * cosine + jnp.where(lane < HD // 2, other, -other) * sine

def attend_back_body(chunk, ids, q_ref, k_ref, v_ref, seg_key_ref, seg_query_ref, o_ref, do_ref, lse_ref, cos_ref, sin_ref, dq_ref, dkv_ref, dq_s):
    block_len = q_ref.shape[0]
    group = H // KVH
    row = pl.program_id(0)
    per = chunk // block_len
    plain = HD ** (-0.5)
    scale = plain * LOG2E
    start = ids[1 + row] // per
    stop = ids[0] // per + 1
    dkv_ref[...] = jnp.zeros_like(dkv_ref)
    for kvh in range(KVH):
        q = stack_heads(q_ref, kvh, group)
        do = stack_heads(do_ref, kvh, group)
        o = stack_heads(o_ref, kvh, group)
        both = do.astype(jnp.float32) * o.astype(jnp.float32)
        delta = nt(jnp.ones((8, HD), jnp.float32), both, precision=lax.Precision.HIGHEST)[0:1, :]
        lse = lse_ref[kvh][0:1, :]
        dq_s[...] = jnp.zeros_like(dq_s)

        def step(c, carry):
            keys = k_ref[pl.ds(c * per, per), :, HD * kvh: HD * (kvh + 1)].reshape(chunk, HD)
            vals = v_ref[pl.ds(c * per, per), :, HD * kvh: HD * (kvh + 1)].reshape(chunk, HD)
            bias = hidden_from(seg_key_ref, seg_query_ref, c * chunk, chunk, block_len, ids[0])
            s = nt(keys, q) * scale + jnp.concatenate([bias] * group, axis=1)
            p = jnp.exp2(s - lse)
            dp = nt(vals, do)
            ds = (p * (dp - delta)).astype(jnp.bfloat16)
            dk = jnp.dot(ds, q, preferred_element_type=jnp.float32) * plain
            dv = jnp.dot(p.astype(jnp.bfloat16), do, preferred_element_type=jnp.float32)
            dkv_ref[pl.ds(c * per, per), :, HD * kvh: HD * (kvh + 1)] = dk.astype(jnp.bfloat16).reshape(per, block_len, HD)
            dkv_ref[pl.ds(c * per, per), :, KVD + HD * kvh: KVD + HD * (kvh + 1)] = dv.astype(jnp.bfloat16).reshape(per, block_len, HD)
            dq_s[...] += tn(ds, keys)
            return carry

        lax.fori_loop(start, stop, step, 0)
        cosine, sine = cos_ref[...], sin_ref[...]
        for i in range(group):
            u = dq_s[block_len * i: block_len * (i + 1), :] * plain
            at = HD * (kvh * group + i)
            dq_ref[:, at: at + HD] = turn_back(u, cosine, sine).astype(jnp.bfloat16)

def attend_back(ids, q, kv, seg_key, seg_query, o, do, lse, cosine, sine, block_len):
    blk_count, rows = kv.shape[:2]
    group = H // KVH
    chunk = 2 * block_len
    many = group * block_len
    per_row = pl.BlockSpec((block_len, HQD), lambda r, ids: (r, 0))
    turn = pl.BlockSpec((block_len, HD), lambda r, ids: (r, 0))
    return pl.pallas_call(
        functools.partial(attend_back_body, chunk),
        grid_spec=pltpu.PrefetchScalarGridSpec(
            num_scalar_prefetch=1, grid=(rows,),
            in_specs=[
                per_row,
                pl.BlockSpec((blk_count, None, block_len, KVD), lambda r, ids: (0, r, 0, 0)),
                pl.BlockSpec((blk_count, None, block_len, KVD), lambda r, ids: (0, r, 0, 1)),
                pl.BlockSpec((None, blk_count * block_len, HD), lambda r, ids: (r, 0, 0)),
                pl.BlockSpec((None, 8, block_len), lambda r, ids: (r, 0, 0)),
                per_row, per_row,
                pl.BlockSpec((None, KVH, 8, many), lambda r, ids: (r, 0, 0, 0)),
                turn, turn,
            ],
            out_specs=[per_row, pl.BlockSpec((blk_count, None, block_len, 2 * KVD), lambda r, ids: (0, r, 0, 0))],
            scratch_shapes=[pltpu.VMEM((many, HD), jnp.float32)]),
        out_shape=[
            jax.ShapeDtypeStruct((rows * block_len, HQD), jnp.bfloat16),
            jax.ShapeDtypeStruct((blk_count, rows, block_len, 2 * KVD), jnp.bfloat16),
        ],
        compiler_params=pltpu.CompilerParams(vmem_limit_bytes=VMEM),
        cost_estimate=pl.CostEstimate(flops=10 * rows * H * block_len * blk_count * block_len * HD, bytes_accessed=12 * 2**20, transcendentals=rows * H * block_len * blk_count * block_len),
        name="attend_back",
    )(ids, q, kv, kv, seg_key, seg_query, o, do, lse, cosine, sine)

def nn(a, b):
    return jnp.dot(a, b, preferred_element_type=jnp.float32)


def middle_body(add, order, h_ref, dy_ref, wg_ref, wu_ref, wd_ref, *refs):
    prev_ref = refs[0] if add else None
    hid_ref, dg_ref, du_ref, dh_ref = refs[-4:]
    h = h_ref[...]
    gate = nn(h, wg_ref[...])
    up = nn(h, wu_ref[...])
    sig = 1.0 / (1.0 + jnp.exp(-gate))
    silu = gate * sig
    hid_ref[...] = (silu * up).astype(jnp.bfloat16)
    dhid = nt(dy_ref[...], wd_ref[...])
    dg = (dhid * up * sig * (1.0 + gate * (1.0 - sig))).astype(jnp.bfloat16)
    du = (dhid * silu).astype(jnp.bfloat16)
    dg_ref[...] = dg
    du_ref[...] = du
    dh = nt(dg, wg_ref[...]) + nt(du, wu_ref[...])
    if add:
        dh = dh + prev_ref[...].astype(jnp.float32)
    dh_ref[...] = dh.astype(jnp.bfloat16)


def middle(order, h, dy, gate_up, wd, prev=None):
    count = h.shape[0]
    step = count // order.shape[0]
    wide_here = wd.shape[0]
    row = pl.BlockSpec((step, D), lambda i, order: (i, 0))
    placed = pl.BlockSpec((step, D), lambda i, order: (order[i], 0))
    part = pl.BlockSpec((step, wide_here), lambda i, order: (i, 0))
    part_placed = pl.BlockSpec((step, wide_here), lambda i, order: (order[i], 0))
    once = pl.Buffered(1)
    extra = [] if prev is None else [prev]
    return pl.pallas_call(
        functools.partial(middle_body, prev is not None),
        grid_spec=pltpu.PrefetchScalarGridSpec(
            num_scalar_prefetch=1,
            grid=(count // step,),
            in_specs=[
                placed,
                row,
                pl.BlockSpec((None, D, wide_here), lambda i, order: (0, 0, 0), pipeline_mode=once),
                pl.BlockSpec((None, D, wide_here), lambda i, order: (1, 0, 0), pipeline_mode=once),
                pl.BlockSpec((wide_here, D), lambda i, order: (0, 0), pipeline_mode=once),
            ]
            + [row] * len(extra),
            out_specs=[part, part_placed, part_placed, row],
        ),
        out_shape=[jax.ShapeDtypeStruct((count, wide_here), jnp.bfloat16)] * 3
        + [jax.ShapeDtypeStruct((count, D), jnp.bfloat16)],
        compiler_params=pltpu.CompilerParams(vmem_limit_bytes=VMEM),
        cost_estimate=pl.CostEstimate(
            flops=10 * count * D * wide_here, bytes_accessed=30 * 2**20, transcendentals=count * wide_here
        ),
        name="middle",
    )(order, h, dy, gate_up, gate_up, wd, *extra)


def two_grads_body(h_ref, a_ref, b_ref, out_ref):
    h = h_ref[...]
    out_ref[0] = tn(h, a_ref[...]).astype(jnp.bfloat16)
    out_ref[1] = tn(h, b_ref[...]).astype(jnp.bfloat16)


def two_grads(h, a, b, step=256):
    count = h.shape[0]
    wide_here = a.shape[1]
    whole = pl.BlockSpec(a.shape, lambda i: (0, 0), pipeline_mode=pl.Buffered(1))
    return pl.pallas_call(
        two_grads_body,
        grid=(D // step,),
        in_specs=[pl.BlockSpec((count, step), lambda i: (0, i)), whole, whole],
        out_specs=pl.BlockSpec((2, step, wide_here), lambda i: (0, i, 0)),
        out_shape=jax.ShapeDtypeStruct((2, D, wide_here), jnp.bfloat16),
        compiler_params=pltpu.CompilerParams(vmem_limit_bytes=VMEM),
        cost_estimate=pl.CostEstimate(
            flops=4 * count * D * wide_here, bytes_accessed=20 * 2**20, transcendentals=0
        ),
        name="two_grads",
    )(h, a, b)


def down_grad_body(hid_ref, dy_ref, g_ref):
    g_ref[...] = tn(hid_ref[...], dy_ref[...]).astype(jnp.bfloat16)

def down_grad(hid, dy, step=512):
    T, F = hid.shape
    D = dy.shape[1]
    return pl.pallas_call(down_grad_body, grid=(D // step,),
        in_specs=[pl.BlockSpec((T, F), lambda i: (0, 0), pipeline_mode=pl.Buffered(1)), pl.BlockSpec((T, step), lambda i: (0, i))],
        out_specs=pl.BlockSpec((F, step), lambda i: (0, i)),
        out_shape=jax.ShapeDtypeStruct((F, D), jnp.bfloat16),
        compiler_params=pltpu.CompilerParams(vmem_limit_bytes=VMEM),
        cost_estimate=pl.CostEstimate(flops=2 * T * D * F, bytes_accessed=16 * 2**20, transcendentals=0),
        name="down_grad")(hid, dy)

def down_body(hid_a_ref, hid_b_ref, wd_a_ref, wd_b_ref, o_ref):
    out = nn(hid_a_ref[...], wd_a_ref[...]) + nn(hid_b_ref[...], wd_b_ref[...])
    o_ref[...] = out.astype(jnp.bfloat16)


def down(hid_a, hid_b, wd_a, wd_b, step):
    count = hid_a.shape[0]

    def rows(array):
        return pl.BlockSpec((step, array.shape[1]), lambda i: (i, 0))

    def whole(array):
        return pl.BlockSpec(array.shape, lambda i: (0, 0), pipeline_mode=pl.Buffered(1))

    return pl.pallas_call(
        down_body,
        grid=(count // step,),
        in_specs=[rows(hid_a), rows(hid_b), whole(wd_a), whole(wd_b)],
        out_specs=pl.BlockSpec((step, D), lambda i: (i, 0)),
        out_shape=jax.ShapeDtypeStruct((count, D), jnp.bfloat16),
        compiler_params=pltpu.CompilerParams(vmem_limit_bytes=VMEM),
        cost_estimate=pl.CostEstimate(
            flops=2 * count * D * (hid_a.shape[1] + hid_b.shape[1]), bytes_accessed=16 * 2**20, transcendentals=0
        ),
        name="down",
    )(hid_a, hid_b, wd_a, wd_b)


CORE = [(0, 1), (1, 0), (2, 3), (3, 2)]
CROSS = [(0, 2), (2, 0), (1, 3), (3, 1)]
DIAG = [(0, 3), (3, 0), (1, 2), (2, 1)]


def low(values):
    return values.astype(jnp.bfloat16)


def wide(values):
    return values.astype(jnp.float32)


def swap_core(values):
    return lax.ppermute(values, "grp", CORE)


def swap_cross(values):
    return lax.ppermute(values, "grp", CROSS)


def swap_diag(values):
    return lax.ppermute(values, "grp", DIAG)


def swap_blk(values, bit):
    count = lax.axis_size("blk")
    return lax.ppermute(values, "blk", [(i, i ^ bit) for i in range(count)])


def blk_bit(bit):
    return (lax.axis_index("blk") & bit) != 0


def bits_of(count):
    out = []
    bit = count // 2
    while bit >= 1:
        out.append(bit)
        bit //= 2
    return out


def gather_bits(values, order):
    done = []
    for bit in order:
        other = swap_blk(values, bit)
        mine = blk_bit(bit)
        axis = sum(1 for d in done if d > bit)
        values = jnp.stack(
            [jnp.where(mine, other, values), jnp.where(mine, values, other)], axis=axis
        )
        done.append(bit)
    return values


def scatter_bits(values, axes, order):
    axes = list(axes)
    for bit in order:
        axis = axes.index(bit)
        mine = blk_bit(bit).astype(jnp.int32)
        keep = lax.dynamic_index_in_dim(values, mine, axis, keepdims=False)
        send = lax.dynamic_index_in_dim(values, 1 - mine, axis, keepdims=False)
        values = low(wide(keep) + wide(swap_blk(send, bit)))
        axes.remove(bit)
    return values


def by_place(parts):
    grp = lax.axis_index("grp")
    core = (grp & 1) != 0
    cross = (grp & 2) != 0
    a, b, c, d = parts
    a, b = jnp.where(core, b, a), jnp.where(core, a, b)
    c, d = jnp.where(core, d, c), jnp.where(core, c, d)
    a, c = jnp.where(cross, c, a), jnp.where(cross, a, c)
    b, d = jnp.where(cross, d, b), jnp.where(cross, b, d)
    return [a, b, c, d]


def gather_near(values):
    cross = swap_cross(values)
    both = swap_core(jnp.stack([values, cross]))
    return [values, both[0], cross, both[1]]


def gather_grp(values):
    return by_place(gather_near(values))


def gather_tokens(values, bit):
    half = values.shape[0] // 2
    cross = swap_cross(values)
    over = swap_blk(values, bit)
    first = swap_blk(cross[:half], bit)
    second = swap_cross(over[half:])
    chip = jnp.concatenate([values, cross, over, first, second])
    return jnp.concatenate([chip, swap_core(chip)])


def angles_of(position):
    half = HD // 2
    freqs = ROPE_BASE ** (-2.0 * jnp.arange(half, dtype=jnp.float32) / HD)
    return position.astype(jnp.float32)[:, None] * freqs[None, :]


def rotate_by(values, cosine, sine):
    half = HD // 2
    first_half = values[..., :half]
    second_half = values[..., half:]
    return jnp.concatenate(
        [first_half * cosine - second_half * sine, second_half * cosine + first_half * sine],
        axis=-1,
    )


def after(values, anchor):
    return lax.optimization_barrier((values, anchor))[0]


def gather_step(values, done, bit):
    other = swap_blk(values, bit)
    mine = blk_bit(bit)
    axis = sum(1 for d in done if d > bit)
    return jnp.stack(
        [jnp.where(mine, other, values), jnp.where(mine, values, other)], axis=axis
    )


def gather_near_stacked(values):
    both = jnp.stack([values, swap_cross(values)])
    return jnp.concatenate([both, swap_core(both)])


def ring_order(count):
    return list(range(0, count, 2)) + list(range(count - 1, 0, -2))


def ring_groups(count):
    return [[g * count + b for b in ring_order(count)] for g in range(4)]


def gather_ring(values):
    count = lax.axis_size("blk")
    parts = lax.all_gather(values, ("grp", "blk"), axis=0, axis_index_groups=ring_groups(count))
    ring = ring_order(count)
    return [parts[ring.index(b)] for b in range(count)]


def on_device(
    tokens,
    cotangent,
    segment_ids,
    position_ids,
    w_attend,
    w_out,
    w_gate,
    w_up,
    w_down,
    small_params,
    first_attend,
    first_out,
    first_gate,
    first_up,
    first_down,
    first_small,
    second_attend,
    second_out,
    second_gate,
    second_up,
    second_down,
    second_small,
):
    rows_here, block_len = tokens.shape[:2]
    blk_count = lax.axis_size("blk")
    seq_len = block_len * blk_count
    token_count = rows_here * block_len
    grp = lax.axis_index("grp")
    blk = lax.axis_index("blk")
    cross_id, core_id = grp // 2, grp % 2
    strip_heads = H // 4
    strip_q = strip_heads * HD
    bits = bits_of(blk_count)
    team = blk_count // 4
    lows = [bit for bit in bits if bit < team]
    spread = [bits[0]] + lows
    low_shape = (2,) * len(lows)
    in_team = blk_bit(team).astype(jnp.int32)
    weight_rows = w_gate.shape[0]
    ff_block = w_down.shape[0]
    quarter = ff_block // 4
    widths = [size * blk_count // 2 for at, size in halves_of(quarter)]
    chip_rows = 4 * token_count
    half = token_count // 2

    ids = jnp.stack([grp, in_team])
    flat_low = tokens.reshape(token_count, D)
    dy_low = cotangent.reshape(token_count, D)
    positions = position_ids.reshape(token_count)
    kv_at = HQD + HD * cross_id + KVD * core_id
    strip_local = low(
        jnp.concatenate(
            [
                lax.dynamic_slice_in_dim(w_attend, strip_q * grp, strip_q, 1),
                lax.dynamic_slice_in_dim(w_attend, kv_at, HD, 1),
            ],
            axis=1,
        )
    )
    small_count = small_params.shape[0]
    small_send = jnp.concatenate([low(small_params), low(segment_ids.reshape(token_count))])
    strip_wide = strip_q + HD
    small_send = jnp.pad(small_send, (0, -small_send.shape[0] % strip_wide))
    strip_local = jnp.concatenate([strip_local, small_send.reshape(-1, strip_wide)])
    strip_list = gather_ring(strip_local)
    strip = jnp.concatenate([part[:weight_rows] for part in strip_list])
    small_all = jnp.stack([part[weight_rows:] for part in strip_list]).reshape(blk_count, -1)
    digits = low(jnp.stack([positions // 64, positions % 64], axis=1))
    digits = jnp.pad(digits, ((0, 0), (0, HD - 2)))
    token_send = jnp.concatenate([flat_low, digits], axis=1)
    token_cross = swap_cross(token_send)
    dy_over = swap_blk(dy_low, team)
    dy_cross = swap_cross(after(dy_low, token_cross))

    def place(values, other, done, bit, lead=0):
        mine = blk_bit(bit)
        axis = lead + sum(1 for d in done if d > bit)
        return jnp.stack(
            [jnp.where(mine, other, values), jnp.where(mine, values, other)], axis=axis
        )

    out_strip = low(lax.dynamic_slice_in_dim(w_out, strip_q * grp, strip_q, 1))
    out_zero = swap_blk(out_strip, bits[0])
    out_strip = place(out_strip, out_zero, [], bits[0])
    out_one = swap_blk(out_strip, team)
    out_strip = place(out_strip, out_one, [bits[0]], team)
    token_core = swap_core(jnp.stack([token_send, token_cross]))
    near_all = jnp.concatenate([token_send, token_core[0], token_cross, token_core[1]])
    near_all = after(near_all, out_strip)
    near_tokens = near_all[:, :D]
    near_positions = 64.0 * wide(near_all[:, D]) + wide(near_all[:, D + 1])
    vector = wide(small_all[:, :small_count].reshape(-1))
    gain_one = vector[:D]
    gain_two = vector[D : 2 * D]
    bias = vector[2 * D :]
    strip_bias = jnp.concatenate(
        [
            lax.dynamic_slice_in_dim(bias, strip_q * grp, strip_q, 0),
            lax.dynamic_slice_in_dim(bias, kv_at, HD, 0),
        ]
    )
    seg_all = small_all[:, small_count : small_count + token_count].astype(jnp.int32)
    seg_all = seg_all.reshape(blk_count, rows_here, block_len)
    seg_key = jnp.broadcast_to(
        seg_all.transpose(1, 0, 2).reshape(rows_here, seq_len)[:, :, None], (rows_here, seq_len, HD)
    )
    seg_query = jnp.broadcast_to(segment_ids[:, None, :], (rows_here, 8, block_len))
    first_blk = jnp.sum((seg_all[:, :, -1] < segment_ids[None, :, 0]).astype(jnp.int32), axis=0)
    attend_ids = jnp.concatenate([blk[None], first_blk])

    near_wide = wide(near_tokens)
    near_one = low(norm_apply(near_wide, gain_one))
    mixed = jnp.dot(near_one, strip, preferred_element_type=jnp.float32) + strip_bias
    angles = angles_of(near_positions)[:, None, :]
    turned = jnp.arange(strip_heads + 1)[None, :, None] < strip_heads + 1 - core_id
    angles = jnp.where(turned, angles, 0.0)
    strip_out = low(
        rotate_by(
            mixed.reshape(4 * token_count, strip_heads + 1, HD), jnp.cos(angles), jnp.sin(angles)
        )
    ).reshape(4, token_count, strip_q + HD)
    strips = by_place(
        [
            strip_out[0],
            swap_core(strip_out[1]),
            swap_cross(strip_out[2]),
            swap_diag(strip_out[3]),
        ]
    )
    query = jnp.concatenate([part[:, :strip_q] for part in strips], axis=1)
    key_value = jnp.concatenate([strips[k][:, strip_q:] for k in (0, 2, 1, 3)], axis=1)
    key_value = key_value.reshape(rows_here, block_len, 2 * KVD)
    kv_all = jnp.stack(gather_ring(key_value))

    teams = [
        [g * blk_count + (i | t) for g in range(4) for t in (0, team)]
        for i in range(blk_count)
        if not i & team
    ]
    order = jnp.stack(
        [
            (grp ^ (2 * (i & 1) + (i >> 2))) * 2 + (in_team ^ ((i >> 1) & 1))
            for i in range(8)
        ]
    )

    mine_team = blk_bit(team)
    peers = [[i for i in range(blk_count) if (i & team) == t] for t in (0, team)]
    (low_first, size_first), (low_second, size_second) = halves_of(quarter)

    def team_pair(mine, got):
        return jnp.stack(
            [jnp.where(mine_team, got, mine), jnp.where(mine_team, mine, got)], axis=1
        )

    def lows_of(values, done, anchor, lead=0):
        for bit in lows:
            values = place(values, after(swap_blk(values, bit), anchor), done, bit, lead)
            done = done + [bit]
        return values

    picked_a, picked_b = pick_columns(ids, w_gate, w_up, blk_count)
    got_a = swap_blk(after(picked_a[1], out_one), team)
    got_b = swap_blk(after(picked_b[1], strip_out), team)
    pair_a = after(team_pair(picked_a[0], after(got_a, strip_out)), key_value)
    pair_a_got = swap_blk(pair_a, bits[0])

    down_at = quarter * grp
    down_a = low(lax.dynamic_slice_in_dim(w_down, down_at, size_first, 0))
    down_got = swap_blk(after(down_a, out_zero), bits[0])
    down_a = after(place(down_a, after(down_got, strip_out), [], bits[0]), key_value)
    down_a = lows_of(down_a, [bits[0]], kv_all).reshape(widths[0], D)

    out_strip = lows_of(out_strip, [bits[0], team], strip_out).reshape(HQD, strip_q)
    out_cross = swap_cross(after(out_strip, key_value))
    out_core = swap_core(jnp.stack([out_strip, out_cross]))
    out_full = jnp.concatenate(by_place([out_strip, out_core[0], out_cross, out_core[1]]), axis=1)
    kv_all = after(kv_all, out_full)

    pair_a = place(pair_a, after(pair_a_got, kv_all), [team], bits[0], 1)
    gate_up_a = lows_of(pair_a, [bits[0], team], kv_all, 1).reshape(2, D, -1)
    down_b = low(lax.dynamic_slice_in_dim(w_down, down_at + size_first, size_second, 0))
    down_got_b = swap_blk(after(down_b, kv_all), bits[0])
    pair_b = team_pair(picked_b[0], after(got_b, kv_all))
    pair_b_got = swap_blk(pair_b, bits[0])
    dy_cross, dy_over = after((dy_cross, dy_over), kv_all)
    dy_first = swap_blk(dy_cross[:half], team)
    dy_second = swap_cross(dy_over[half:])

    att_in, lse = attend(attend_ids, query, kv_all, seg_key, seg_query, block_len)

    flat = wide(flat_low)
    resid = flat + jnp.dot(att_in, out_full, preferred_element_type=jnp.float32)
    h_two = low(norm_apply(resid, gain_two))
    h_team = lax.all_gather(h_two, ("grp", "blk"), axis=0, tiled=True, axis_index_groups=teams)
    dy_first, dy_second, down_got_b, pair_b_got = after(
        (dy_first, dy_second, down_got_b, pair_b_got), h_two
    )
    dy_chip = jnp.concatenate([dy_low, dy_cross, dy_over, dy_first, dy_second])
    dy_team = jnp.concatenate([dy_chip, swap_core(dy_chip)])
    down_b = place(down_b, down_got_b, [], bits[0])
    pair_b = place(pair_b, pair_b_got, [team], bits[0], 1)
    h_team = after(h_team, (dy_team, down_b, pair_b))
    hidden_a, d_gate_a, d_up_a, part_a = middle(order, h_team, dy_team, gate_up_a, down_a)
    down_b = lows_of(down_b, [bits[0]], hidden_a).reshape(widths[1], D)
    gate_up_b = lows_of(pair_b, [bits[0], team], hidden_a, 1).reshape(2, D, -1)
    down_share_a = lax.psum_scatter(
        down_grad(hidden_a, dy_team), "blk", scatter_dimension=0, axis_index_groups=peers, tiled=True
    )
    column_grad_a = two_grads(h_team, d_gate_a, d_up_a)

    def part_sent(values, axis, bit):
        mine = blk_bit(bit).astype(jnp.int32)
        keep = lax.dynamic_index_in_dim(values, mine, axis, keepdims=False)
        send = lax.dynamic_index_in_dim(values, 1 - mine, axis, keepdims=False)
        return keep, swap_blk(send, bit)

    def part_sum(keep, got):
        return low(wide(keep) + wide(got))

    def columns_first(grad):
        grad = grad.reshape((2, 2, 2) + low_shape + (weight_rows, -1))
        return part_sent(grad, 2 + len(lows), lows[-1])

    def columns_second(keep, got):
        values = part_sum(keep, got)
        for i in range(len(lows) - 2, -1, -1):
            values = part_sum(*part_sent(values, 3 + i, lows[i]))
        return part_sent(values, 1, bits[0])

    def columns_third(keep, got):
        values = part_sum(keep, got)
        mine = lax.dynamic_index_in_dim(values, in_team, 1, keepdims=False)
        send = lax.dynamic_index_in_dim(values, 1 - in_team, 1, keepdims=False)
        return values, (mine, swap_blk(send, team))

    def rows_second(keep, got):
        values = part_sum(keep, got)
        for i in range(len(lows) - 2, -1, -1):
            values = part_sum(*part_sent(values, 1 + i, lows[i]))
        return part_sent(values, 0, bits[0])

    def columns_last(mine, got):
        return jnp.stack(
            [jnp.where(mine_team, got, mine), jnp.where(mine_team, mine, got)], axis=1
        )

    first_a = columns_first(column_grad_a)
    hidden_b, d_gate_b, d_up_b, d_htwo_part = middle(
        order, after(h_team, column_grad_a), dy_team, gate_up_b, down_b, part_a
    )

    def chip_sum(values, came):
        return low(wide(values[:chip_rows]) + wide(came))

    def scatter_far(chip):
        far = chip[3 * token_count :]
        return swap_blk(far[:half], team), swap_cross(far[half:])

    def scatter_near(chip, first, second):
        cross, over = (chip[token_count * i : token_count * (i + 1)] for i in (1, 2))
        cross = jnp.concatenate([low(wide(cross[:half]) + wide(first)), cross[half:]])
        over = jnp.concatenate([over[:half], low(wide(over[half:]) + wide(second))])
        return swap_cross(cross), swap_blk(over, team)

    d_came = swap_core(d_htwo_part[chip_rows:])
    down_grad_b = down_grad(hidden_b, dy_team)
    rows_b = part_sent(
        down_grad_b.reshape((2,) + low_shape + (size_second, D)), len(lows), lows[-1]
    )
    d_chip = chip_sum(d_htwo_part, after(d_came, down_grad_b))
    d_far = scatter_far(d_chip)
    column_grad_b = two_grads(h_team, *after((d_gate_b, d_up_b), d_chip))
    first_b = columns_first(column_grad_b)
    d_far = after(d_far, column_grad_b)
    d_cross, d_over = scatter_near(d_chip, *d_far)
    out_part = down(*after((hidden_a, hidden_b), d_far), down_a, down_b, token_count)
    out_came = swap_core(out_part[chip_rows:])
    d_cross, d_over = after((d_cross, d_over), out_part)
    d_htwo = wide(d_chip[:token_count]) + wide(d_cross) + wide(d_over)

    norm_value_two, norm_back_two = jax.vjp(norm_apply, resid, gain_two)
    d_resid_norm, grad_gain_two = norm_back_two(d_htwo)
    d_resid = wide(dy_low) + d_resid_norm
    d_att = low(d_resid)
    second_a = columns_second(*after(first_a, d_att))
    rows_b = rows_second(*after(rows_b, d_att))
    out_chip = chip_sum(out_part, after(out_came, d_att))
    out_far = scatter_far(out_chip)

    d_attended = low(right_transposed(d_att, out_full))
    own_angles = angles_of(positions)
    cosine, sine = jnp.cos(own_angles), jnp.sin(own_angles)
    d_query, dkv = attend_back(
        attend_ids,
        query,
        kv_all,
        seg_key,
        seg_query,
        att_in,
        d_attended,
        lse,
        jnp.concatenate([cosine, cosine], axis=1),
        jnp.concatenate([sine, sine], axis=1),
        block_len,
    )
    second_b = columns_second(*after(first_b, d_query))
    dkv = jnp.concatenate([dkv[b] for b in ring_order(blk_count)])
    dkv = lax.psum_scatter(
        dkv.reshape(blk_count * token_count, 2 * KVD),
        ("grp", "blk"),
        scatter_dimension=0,
        axis_index_groups=ring_groups(blk_count),
        tiled=True,
    )
    sum_a, third_a = columns_third(*after(second_a, d_query))
    down_share_b = part_sum(*after(rows_b, d_query))
    out_cross, out_over = scatter_near(out_chip, *after(out_far, d_query))
    share_down = jnp.concatenate([down_share_a, down_share_b])
    grad_down = lax.all_gather(share_down, "grp", axis=0, tiled=True)
    def to_strips(parts):
        parts = by_place(parts)
        return jnp.concatenate(
            [parts[0], swap_core(parts[1]), swap_cross(parts[2]), swap_diag(parts[3])]
        )

    near_dq = to_strips([d_query[:, strip_q * k : strip_q * (k + 1)] for k in range(4)])
    block_shape = (2,) * len(bits) + (weight_rows, -1)
    query_grad = low(left_product(near_one, near_dq)).reshape(block_shape)
    steps_query = part_sent(query_grad, len(bits) - 1, bits[-1])
    dkv = wide(after(dkv, (sum_a, share_down, query_grad))).reshape(token_count, 2, KVH, HD)
    d_key = low(rotate_by(dkv[:, 0], cosine[:, None], -sine[:, None]))
    d_value = low(dkv[:, 1])
    near_dkv = to_strips([(d_value if k % 2 else d_key)[:, k // 2] for k in range(4)])
    kv_grad = low(left_product(near_one, near_dkv)).reshape(block_shape)
    steps_kv = part_sent(kv_grad, len(bits) - 1, bits[-1])
    sum_b, third_b = columns_third(*after(second_b, d_key))
    near_a = gather_near_stacked(columns_last(*after(third_a, d_key)))
    for i in range(len(bits) - 2, -1, -1):
        steps_query = part_sent(part_sum(*after(steps_query, d_key)), i, bits[i])
        kv_sum = part_sum(*steps_kv)
        kv_grad = kv_sum
        steps_kv = part_sent(kv_sum, i, bits[i])
    share_kv = part_sum(*steps_kv)
    share_query = part_sum(*after(steps_query, kv_grad))
    grad_bias = jnp.concatenate(
        [
            jnp.sum(wide(part), axis=0)
            for part in (d_query, d_key.reshape(token_count, KVD), d_value.reshape(token_count, KVD))
        ]
    )
    out_cross, out_over = after((out_cross, out_over), near_dkv)
    out_tokens = low(resid + wide(out_chip[:token_count]) + wide(out_cross) + wide(out_over))
    near_hone = right_transposed(near_dq, strip[:, :strip_q]) + right_transposed(
        near_dkv, strip[:, strip_q:]
    )
    near_rms = lax.rsqrt(jnp.mean(near_wide * near_wide, axis=-1, keepdims=True) + NORM_EPS)
    gain_one_part = jnp.sum(near_hone * near_wide * near_rms, axis=0)

    near_att = jnp.concatenate(gather_near(after(att_in, hidden_a)))
    near_datt = to_strips([d_att[:, strip_q * k : strip_q * (k + 1)] for k in range(4)])
    out_grad = low(left_product(near_att, after(near_datt, d_attended))).reshape(block_shape)
    steps_out = part_sent(out_grad, len(bits) - 1, bits[-1])
    anchors = [d_query, d_key]
    for i in range(len(bits) - 2, -1, -1):
        anchor = anchors[min(len(bits) - 2 - i, 1)]
        steps_out = part_sent(part_sum(*after(steps_out, anchor)), i, bits[i])
    share_out = part_sum(*after(steps_out, kv_grad))

    vector_term = jnp.concatenate([gain_one_part, grad_gain_two, grad_bias])
    vector_term = vector_term + swap_cross(vector_term)
    vector_term = vector_term + swap_core(vector_term)
    vector_term = vector_term.reshape((2,) * len(bits) + (-1,))
    axes = list(bits)
    for bit in bits[::-1]:
        axis = axes.index(bit)
        mine = blk_bit(bit).astype(jnp.int32)
        keep = lax.dynamic_index_in_dim(vector_term, mine, axis, keepdims=False)
        send = lax.dynamic_index_in_dim(vector_term, 1 - mine, axis, keepdims=False)
        vector_term = keep + swap_blk(send, bit)
        axes.remove(bit)
    share_vector = vector_term

    near_b = gather_near_stacked(columns_last(*after(third_b, kv_grad)))
    grad_out = jnp.concatenate(gather_grp(share_out), axis=1)
    query_parts = gather_grp(share_query)
    key_parts = gather_grp(share_kv)
    grad_attend = jnp.concatenate(query_parts + [key_parts[k] for k in (0, 2, 1, 3)], axis=1)

    sides = low(near_hone[token_count : 2 * token_count]), low(near_hone[3 * token_count :])
    other = wide(swap_core(jnp.concatenate(sides)))
    d_hone = near_hone[:token_count] + other[:token_count]
    d_hone_cross = swap_cross(
        low(near_hone[2 * token_count : 3 * token_count] + other[token_count:])
    )
    square_sum = square_total(
        [
            wide(s)
            for s in (share_query, share_kv, share_out, sum_a, sum_b, share_down)
        ]
    ) + 0.25 * jnp.sum(share_vector * share_vector)
    square_sum = jnp.full((8, 128), square_sum)
    for bit in bits:
        square_sum = square_sum + swap_blk(square_sum, bit)
    square_sum = square_sum + swap_cross(square_sum)
    square_sum = square_sum + swap_core(square_sum)
    grad_norm = jnp.sqrt(square_sum[0, 0])
    factor = jnp.minimum(1.0, CLIP_NORM / (grad_norm + 1e-06))
    factor = after(factor, out_tokens)

    new_first_gate, new_second_gate, new_gate = adam_columns(
        0, ids, factor[None], near_a, near_b, w_gate, first_gate, second_gate, blk_count, RATE_GATE, WEIGHT_DECAY
    )
    new_first_up, new_second_up, new_up = adam_columns(
        1, ids, factor[None], near_a, near_b, w_up, first_up, second_up, blk_count, RATE_GATE, WEIGHT_DECAY
    )
    norm_value_one, norm_back_one = jax.vjp(norm_apply, flat, gain_one)
    d_hone = after(d_hone + wide(after(d_hone_cross, new_gate)), new_gate)
    d_flat_norm, unused_gain = norm_back_one(d_hone)
    grad_tokens = low(d_resid + d_flat_norm)

    new_first_attend, new_second_attend, new_attend = adam_step(
        w_attend, factor * wide(grad_attend), first_attend, second_attend, RATE_ATTEND, WEIGHT_DECAY
    )
    new_first_out, new_second_out, new_out = adam_step(
        w_out, factor * wide(grad_out), first_out, second_out, RATE_OUT, WEIGHT_DECAY
    )
    new_first_down, new_second_down, new_down = adam_step(
        w_down, factor * wide(grad_down), first_down, second_down, RATE_DOWN, WEIGHT_DECAY
    )
    new_first_small, new_second_small, new_small = adam_step(
        small_params, factor * share_vector, first_small, second_small, RATE_VECTOR, 0.0
    )
    return (
        out_tokens.reshape(rows_here, block_len, D),
        grad_tokens.reshape(rows_here, block_len, D),
        grad_norm,
        new_first_attend,
        new_second_attend,
        new_attend,
        new_first_out,
        new_second_out,
        new_out,
        new_first_gate,
        new_second_gate,
        new_gate,
        new_first_up,
        new_second_up,
        new_up,
        new_first_down,
        new_second_down,
        new_down,
        new_first_small,
        new_second_small,
        new_small,
    )


def solution(mesh):
    placed = (
        P("grp", "blk", None),
        P("grp", "blk", None),
        P("grp", "blk"),
        P("grp", "blk"),
        P("blk", None),
        P("blk", None),
        P("blk", None),
        P("blk", None),
        P("blk", None),
        P("blk"),
        P("blk", None),
        P("blk", None),
        P("blk", None),
        P("blk", None),
        P("blk", None),
        P("blk"),
        P("blk", None),
        P("blk", None),
        P("blk", None),
        P("blk", None),
        P("blk", None),
        P("blk"),
    )
    return jax.shard_map(
        on_device,
        mesh=mesh,
        in_specs=placed,
        out_specs=(
            P("grp", "blk", None),
            P("grp", "blk", None),
            P(),
            P("blk", None),
            P("blk", None),
            P("blk", None),
            P("blk", None),
            P("blk", None),
            P("blk", None),
            P("blk", None),
            P("blk", None),
            P("blk", None),
            P("blk", None),
            P("blk", None),
            P("blk", None),
            P("blk", None),
            P("blk", None),
            P("blk", None),
            P("blk"),
            P("blk"),
            P("blk"),
        ),
        check_vma=False,
    )
```

```python
import functools

import jax
import jax.numpy as jnp
from jax import lax
from jax.experimental import pallas as pl
from jax.experimental.pallas import tpu as pltpu
from jax.sharding import PartitionSpec as P

D = 1536
FF = 8960
H = 12
KVH = 2
HD = 128
STEP = 10
HQD = 1536
KVD = 256


NORM_EPS = 1e-06
ROPE_BASE = 10000.0
CLIP_NORM = 1.0
BETA_FIRST = 0.9
BETA_SECOND = 0.95
ADAM_EPS = 1e-08
WEIGHT_DECAY = 0.1
RATE_ATTEND = 0.06
RATE_OUT = 0.5
RATE_GATE = 0.06
RATE_DOWN = 0.03
RATE_VECTOR = 0.5
NEG_LARGE = -1e30
LOG2E = 1.4426950408889634
VMEM = 48 * 1024 * 1024
SMALL_COST = pl.CostEstimate(flops=1000, bytes_accessed=1000, transcendentals=0)


def norm_apply(values, gain):
    return values * lax.rsqrt(jnp.mean(values * values, axis=-1, keepdims=True) + NORM_EPS) * gain


def swish_product(gate, up_proj):
    return jax.nn.silu(gate) * up_proj


def left_product(left_side, right_side):
    return lax.dot_general(
        left_side, right_side, (((0,), (0,)), ((), ())), preferred_element_type=jnp.float32
    )


def right_transposed(left_side, right_side):
    return lax.dot_general(
        left_side, right_side, (((1,), (1,)), ((), ())), preferred_element_type=jnp.float32
    )


def square_total(arrays):
    return sum((jnp.sum(member * member) for member in arrays))


def adam_step(weight, grad, first, second, rate, decay):
    first_new = BETA_FIRST * first + (1.0 - BETA_FIRST) * grad
    second_new = BETA_SECOND * second + (1.0 - BETA_SECOND) * grad * grad
    first_hat = first_new / (1.0 - BETA_FIRST**STEP)
    second_hat = second_new / (1.0 - BETA_SECOND**STEP)
    weight_new = weight - rate * (first_hat / (jnp.sqrt(second_hat) + ADAM_EPS) + decay * weight)
    return (first_new, second_new, weight_new)


def halves_of(quarter):
    first = quarter * 16 // 35
    return ((0, first), (first, quarter - first))


def pick_body(blk_count, ids, gate_ref, up_ref, *out_refs):
    quarter = FF // blk_count // 4
    per = blk_count // 4
    for k in range(4):

        @pl.when(ids[0] == k)
        def _(k=k):
            for (at, size), out_ref in zip(halves_of(quarter), out_refs):
                for which, src in enumerate((gate_ref, up_ref)):
                    for bit in range(2):
                        parts = []
                        for high in range(2):
                            for small in range(per):
                                begin = (((high * 2 + bit) * per + small) * 4 + k) * quarter + at
                                parts.append(src[:, begin : begin + size])
                        out_ref[ids[1] ^ bit, which] = jnp.concatenate(parts, axis=1).astype(
                            jnp.bfloat16
                        )


def pick_columns(ids, gate, up, blk_count):
    rows = gate.shape[0]
    step = 48 if rows % 48 == 0 else rows
    widths = [size * blk_count // 2 for at, size in halves_of(FF // blk_count // 4)]
    spec = pl.BlockSpec((step, FF), lambda i, ids: (i, 0))
    return pl.pallas_call(
        functools.partial(pick_body, blk_count),
        grid_spec=pltpu.PrefetchScalarGridSpec(
            num_scalar_prefetch=1,
            grid=(rows // step,),
            in_specs=[spec, spec],
            out_specs=[pl.BlockSpec((2, 2, step, w), lambda i, ids: (0, 0, i, 0)) for w in widths],
        ),
        out_shape=[jax.ShapeDtypeStruct((2, 2, rows, w), jnp.bfloat16) for w in widths],
        compiler_params=pltpu.CompilerParams(vmem_limit_bytes=VMEM),
        cost_estimate=SMALL_COST,
        name="pick_columns",
    )(ids, gate, up)


def near_at(away):
    return (away & 1) * 2 + (away >> 1)


def adam_body(blk_count, rate, decay, ids, factor_ref, first_ref, second_ref, w_ref, m_ref, v_ref, m_out, v_out, w_out):
    per = blk_count // 4
    sizes = [size for at, size in halves_of(FF // blk_count // 4)]
    grads = [
        [[ref[near_at(ids[0] ^ k), bit] for bit in range(2)] for k in range(4)]
        for ref in (first_ref, second_ref)
    ]
    parts = []
    for high in range(2):
        for bit in range(2):
            for small in range(per):
                place = high * per + small
                for k in range(4):
                    for part, size in zip(grads, sizes):
                        parts.append(part[k][bit][:, place * size : (place + 1) * size])
    grad = jnp.concatenate(parts, axis=1).astype(jnp.float32) * factor_ref[0]
    m, v, w = adam_step(w_ref[...], grad, m_ref[...], v_ref[...], rate, decay)
    m_out[...] = m
    v_out[...] = v
    w_out[...] = w


def adam_columns(which, ids, factor, first, second, w, m, v, blk_count, rate, decay):
    rows = w.shape[0]
    step = 32 if rows % 32 == 0 else rows
    spec = pl.BlockSpec((step, FF), lambda i, ids: (i, 0))
    shape = jax.ShapeDtypeStruct((rows, FF), jnp.float32)
    grads = [
        pl.BlockSpec((4, None, 2, step, g.shape[-1]), lambda i, ids: (0, which, 0, i, 0))
        for g in (first, second)
    ]
    return pl.pallas_call(
        functools.partial(adam_body, blk_count, rate, decay),
        grid_spec=pltpu.PrefetchScalarGridSpec(
            num_scalar_prefetch=1,
            grid=(rows // step,),
            in_specs=[pl.BlockSpec(memory_space=pltpu.SMEM)] + grads + [spec, spec, spec],
            out_specs=[spec, spec, spec],
        ),
        out_shape=[shape] * 3,
        compiler_params=pltpu.CompilerParams(vmem_limit_bytes=VMEM),
        cost_estimate=SMALL_COST,
        name="adam_columns",
    )(ids, factor, first, second, w, m, v)


def nt(a, b, **kw):
    return lax.dot_general(a, b, (((1,), (1,)), ((), ())), preferred_element_type=jnp.float32, **kw)

def tn(a, b, **kw):
    return lax.dot_general(a, b, (((0,), (0,)), ((), ())), preferred_element_type=jnp.float32, **kw)

def stack_heads(ref, kvh, group):
    return jnp.concatenate([ref[:, HD * (kvh * group + i): HD * (kvh * group + i + 1)] for i in range(group)], axis=0)

def hidden_from(seg_key_ref, seg_query_ref, first, chunk, block_len, blk):
    key = first + lax.broadcasted_iota(jnp.int32, (chunk, block_len), 0)
    query = blk * block_len + lax.broadcasted_iota(jnp.int32, (chunk, block_len), 1)
    seg_key = seg_key_ref[pl.ds(first, chunk), :]
    counts = jnp.logical_and(key <= query, seg_key == seg_query_ref[0:1, :])
    return jnp.where(counts, 0.0, NEG_LARGE)

def ring_pair(ref, c, at):
    return jnp.concatenate(
        [ref[c, :, at : at + HD], ref[ref.shape[0] - 1 - c, :, at : at + HD]], axis=0
    )


def attend_body(chunk, ids, q_ref, k_ref, v_ref, seg_key_ref, seg_query_ref, o_ref, lse_ref, m_s, l_s, acc_s):
    block_len = q_ref.shape[0]
    group = H // KVH
    row = pl.program_id(0)
    per = chunk // block_len
    scale = HD ** (-0.5) * LOG2E
    start = ids[1 + row] // per
    stop = ids[0] // per + 1
    for kvh in range(KVH):
        q = stack_heads(q_ref, kvh, group)
        m_s[...] = jnp.full_like(m_s, NEG_LARGE)
        l_s[...] = jnp.zeros_like(l_s)
        acc_s[...] = jnp.zeros_like(acc_s)

        def step(c, carry):
            keys = ring_pair(k_ref, c, HD * kvh)
            vals = ring_pair(v_ref, c, HD * kvh)
            bias = hidden_from(seg_key_ref, seg_query_ref, c * chunk, chunk, block_len, ids[0])
            s = nt(keys, q) * scale + jnp.concatenate([bias] * group, axis=1)
            old = m_s[0:1, :]
            new = jnp.maximum(old, jnp.max(s, axis=0, keepdims=True))
            p = jnp.exp2(s - new)
            fade = jnp.exp2(old - new)
            l_s[0:1, :] = l_s[0:1, :] * fade + jnp.sum(p, axis=0, keepdims=True)
            acc_s[...] = acc_s[...] * fade + tn(vals, p.astype(jnp.bfloat16))
            m_s[0:1, :] = new
            return carry

        lax.fori_loop(start, stop, step, 0)
        total = l_s[0:1, :]
        out = (acc_s[...] * (1.0 / total)).T
        for i in range(group):
            o_ref[:, HD * (kvh * group + i): HD * (kvh * group + i + 1)] = out[block_len * i: block_len * (i + 1), :].astype(jnp.bfloat16)
        lse_ref[kvh] = jnp.broadcast_to(m_s[0:1, :] + jnp.log2(total), (8, group * block_len))

def attend(ids, q, kv, seg_key, seg_query, block_len):
    blk_count, rows = kv.shape[:2]
    group = H // KVH
    chunk = 2 * block_len
    many = group * block_len
    return pl.pallas_call(
        functools.partial(attend_body, chunk),
        grid_spec=pltpu.PrefetchScalarGridSpec(
            num_scalar_prefetch=1, grid=(rows,),
            in_specs=[
                pl.BlockSpec((block_len, HQD), lambda r, ids: (r, 0)),
                pl.BlockSpec((blk_count, None, block_len, KVD), lambda r, ids: (0, r, 0, 0)),
                pl.BlockSpec((blk_count, None, block_len, KVD), lambda r, ids: (0, r, 0, 1)),
                pl.BlockSpec((None, blk_count * block_len, HD), lambda r, ids: (r, 0, 0)),
                pl.BlockSpec((None, 8, block_len), lambda r, ids: (r, 0, 0)),
            ],
            out_specs=[
                pl.BlockSpec((block_len, HQD), lambda r, ids: (r, 0)),
                pl.BlockSpec((None, KVH, 8, many), lambda r, ids: (r, 0, 0, 0)),
            ],
            scratch_shapes=[pltpu.VMEM((8, many), jnp.float32), pltpu.VMEM((8, many), jnp.float32), pltpu.VMEM((HD, many), jnp.float32)]),
        out_shape=[
            jax.ShapeDtypeStruct((rows * block_len, HQD), jnp.bfloat16),
            jax.ShapeDtypeStruct((rows, KVH, 8, many), jnp.float32),
        ],
        compiler_params=pltpu.CompilerParams(vmem_limit_bytes=VMEM),
        cost_estimate=SMALL_COST,
        name="attend",
    )(ids, q, kv, kv, seg_key, seg_query)

def turn_back(u, cosine, sine):
    lane = lax.broadcasted_iota(jnp.int32, u.shape, 1)
    other = pltpu.roll(u, HD // 2, 1)
    return u * cosine + jnp.where(lane < HD // 2, other, -other) * sine

def attend_back_body(chunk, ids, q_ref, k_ref, v_ref, seg_key_ref, seg_query_ref, o_ref, do_ref, lse_ref, cos_ref, sin_ref, dq_ref, dkv_ref, dq_s):
    block_len = q_ref.shape[0]
    group = H // KVH
    row = pl.program_id(0)
    per = chunk // block_len
    plain = HD ** (-0.5)
    scale = plain * LOG2E
    start = ids[1 + row] // per
    stop = ids[0] // per + 1
    dkv_ref[...] = jnp.zeros_like(dkv_ref)
    for kvh in range(KVH):
        q = stack_heads(q_ref, kvh, group)
        do = stack_heads(do_ref, kvh, group)
        o = stack_heads(o_ref, kvh, group)
        both = do.astype(jnp.float32) * o.astype(jnp.float32)
        delta = nt(jnp.ones((8, HD), jnp.float32), both, precision=lax.Precision.HIGHEST)[0:1, :]
        lse = lse_ref[kvh][0:1, :]
        dq_s[...] = jnp.zeros_like(dq_s)

        def step(c, carry):
            keys = ring_pair(k_ref, c, HD * kvh)
            vals = ring_pair(v_ref, c, HD * kvh)
            bias = hidden_from(seg_key_ref, seg_query_ref, c * chunk, chunk, block_len, ids[0])
            s = nt(keys, q) * scale + jnp.concatenate([bias] * group, axis=1)
            p = jnp.exp2(s - lse)
            dp = nt(vals, do)
            ds = (p * (dp - delta)).astype(jnp.bfloat16)
            dk = jnp.dot(ds, q, preferred_element_type=jnp.float32) * plain
            dv = jnp.dot(p.astype(jnp.bfloat16), do, preferred_element_type=jnp.float32)
            for at, part in ((HD * kvh, dk.astype(jnp.bfloat16)), (KVD + HD * kvh, dv.astype(jnp.bfloat16))):
                dkv_ref[c, :, at : at + HD] = part[:block_len]
                dkv_ref[dkv_ref.shape[0] - 1 - c, :, at : at + HD] = part[block_len:]
            dq_s[...] += tn(ds, keys)
            return carry

        lax.fori_loop(start, stop, step, 0)
        cosine, sine = cos_ref[...], sin_ref[...]
        for i in range(group):
            u = dq_s[block_len * i: block_len * (i + 1), :] * plain
            at = HD * (kvh * group + i)
            dq_ref[:, at: at + HD] = turn_back(u, cosine, sine).astype(jnp.bfloat16)

def attend_back(ids, q, kv, seg_key, seg_query, o, do, lse, cosine, sine, block_len):
    blk_count, rows = kv.shape[:2]
    group = H // KVH
    chunk = 2 * block_len
    many = group * block_len
    per_row = pl.BlockSpec((block_len, HQD), lambda r, ids: (r, 0))
    turn = pl.BlockSpec((block_len, HD), lambda r, ids: (r, 0))
    return pl.pallas_call(
        functools.partial(attend_back_body, chunk),
        grid_spec=pltpu.PrefetchScalarGridSpec(
            num_scalar_prefetch=1, grid=(rows,),
            in_specs=[
                per_row,
                pl.BlockSpec((blk_count, None, block_len, KVD), lambda r, ids: (0, r, 0, 0)),
                pl.BlockSpec((blk_count, None, block_len, KVD), lambda r, ids: (0, r, 0, 1)),
                pl.BlockSpec((None, blk_count * block_len, HD), lambda r, ids: (r, 0, 0)),
                pl.BlockSpec((None, 8, block_len), lambda r, ids: (r, 0, 0)),
                per_row, per_row,
                pl.BlockSpec((None, KVH, 8, many), lambda r, ids: (r, 0, 0, 0)),
                turn, turn,
            ],
            out_specs=[per_row, pl.BlockSpec((blk_count, None, block_len, 2 * KVD), lambda r, ids: (0, r, 0, 0))],
            scratch_shapes=[pltpu.VMEM((many, HD), jnp.float32)]),
        out_shape=[
            jax.ShapeDtypeStruct((rows * block_len, HQD), jnp.bfloat16),
            jax.ShapeDtypeStruct((blk_count, rows, block_len, 2 * KVD), jnp.bfloat16),
        ],
        compiler_params=pltpu.CompilerParams(vmem_limit_bytes=VMEM),
        cost_estimate=SMALL_COST,
        name="attend_back",
    )(ids, q, kv, kv, seg_key, seg_query, o, do, lse, cosine, sine)

def nn(a, b):
    return jnp.dot(a, b, preferred_element_type=jnp.float32)


def middle_body(add, order, h_ref, dy_ref, wg_ref, wu_ref, wd_ref, *refs):
    prev_ref = refs[0] if add else None
    hid_ref, dg_ref, du_ref, dh_ref = refs[-4:]
    h = h_ref[...]
    gate = nn(h, wg_ref[...])
    up = nn(h, wu_ref[...])
    sig = 1.0 / (1.0 + jnp.exp(-gate))
    silu = gate * sig
    hid_ref[...] = (silu * up).astype(jnp.bfloat16)
    dhid = nt(dy_ref[...], wd_ref[...])
    dg = (dhid * up * sig * (1.0 + gate * (1.0 - sig))).astype(jnp.bfloat16)
    du = (dhid * silu).astype(jnp.bfloat16)
    dg_ref[...] = dg
    du_ref[...] = du
    dh = nt(dg, wg_ref[...]) + nt(du, wu_ref[...])
    if add:
        dh = dh + prev_ref[...].astype(jnp.float32)
    dh_ref[...] = dh.astype(jnp.bfloat16)


def middle(order, h, dy, gate_up, wd, prev=None):
    count = h.shape[0]
    step = count // order.shape[0]
    wide_here = wd.shape[0]
    row = pl.BlockSpec((step, D), lambda i, order: (i, 0))
    placed = pl.BlockSpec((step, D), lambda i, order: (order[i], 0))
    part = pl.BlockSpec((step, wide_here), lambda i, order: (i, 0))
    part_placed = pl.BlockSpec((step, wide_here), lambda i, order: (order[i], 0))
    once = pl.Buffered(1)
    extra = [] if prev is None else [prev]
    return pl.pallas_call(
        functools.partial(middle_body, prev is not None),
        grid_spec=pltpu.PrefetchScalarGridSpec(
            num_scalar_prefetch=1,
            grid=(count // step,),
            in_specs=[
                placed,
                row,
                pl.BlockSpec((None, D, wide_here), lambda i, order: (0, 0, 0), pipeline_mode=once),
                pl.BlockSpec((None, D, wide_here), lambda i, order: (1, 0, 0), pipeline_mode=once),
                pl.BlockSpec((wide_here, D), lambda i, order: (0, 0), pipeline_mode=once),
            ]
            + [row] * len(extra),
            out_specs=[part, part_placed, part_placed, row],
        ),
        out_shape=[jax.ShapeDtypeStruct((count, wide_here), jnp.bfloat16)] * 3
        + [jax.ShapeDtypeStruct((count, D), jnp.bfloat16)],
        compiler_params=pltpu.CompilerParams(vmem_limit_bytes=VMEM),
        cost_estimate=SMALL_COST,
        name="middle",
    )(order, h, dy, gate_up, gate_up, wd, *extra)


def two_grads_body(h_ref, a_ref, b_ref, out_ref):
    h = h_ref[...]
    out_ref[0] = tn(h, a_ref[...]).astype(jnp.bfloat16)
    out_ref[1] = tn(h, b_ref[...]).astype(jnp.bfloat16)


def two_grads(h, a, b, step=256):
    count = h.shape[0]
    wide_here = a.shape[1]
    whole = pl.BlockSpec(a.shape, lambda i: (0, 0), pipeline_mode=pl.Buffered(1))
    return pl.pallas_call(
        two_grads_body,
        grid=(D // step,),
        in_specs=[pl.BlockSpec((count, step), lambda i: (0, i)), whole, whole],
        out_specs=pl.BlockSpec((2, step, wide_here), lambda i: (0, i, 0)),
        out_shape=jax.ShapeDtypeStruct((2, D, wide_here), jnp.bfloat16),
        compiler_params=pltpu.CompilerParams(vmem_limit_bytes=VMEM),
        cost_estimate=SMALL_COST,
        name="two_grads",
    )(h, a, b)


def down_grad_body(hid_ref, dy_ref, g_ref):
    g_ref[...] = tn(hid_ref[...], dy_ref[...]).astype(jnp.bfloat16)

def down_grad(hid, dy, step=512):
    T, F = hid.shape
    D = dy.shape[1]
    return pl.pallas_call(down_grad_body, grid=(D // step,),
        in_specs=[pl.BlockSpec((T, F), lambda i: (0, 0), pipeline_mode=pl.Buffered(1)), pl.BlockSpec((T, step), lambda i: (0, i))],
        out_specs=pl.BlockSpec((F, step), lambda i: (0, i)),
        out_shape=jax.ShapeDtypeStruct((F, D), jnp.bfloat16),
        compiler_params=pltpu.CompilerParams(vmem_limit_bytes=VMEM),
        cost_estimate=SMALL_COST,
        name="down_grad")(hid, dy)

def down_body(hid_a_ref, hid_b_ref, wd_a_ref, wd_b_ref, o_ref):
    out = nn(hid_a_ref[...], wd_a_ref[...]) + nn(hid_b_ref[...], wd_b_ref[...])
    o_ref[...] = out.astype(jnp.bfloat16)


def down(hid_a, hid_b, wd_a, wd_b, step):
    count = hid_a.shape[0]

    def rows(array):
        return pl.BlockSpec((step, array.shape[1]), lambda i: (i, 0))

    def whole(array):
        return pl.BlockSpec(array.shape, lambda i: (0, 0), pipeline_mode=pl.Buffered(1))

    return pl.pallas_call(
        down_body,
        grid=(count // step,),
        in_specs=[rows(hid_a), rows(hid_b), whole(wd_a), whole(wd_b)],
        out_specs=pl.BlockSpec((step, D), lambda i: (i, 0)),
        out_shape=jax.ShapeDtypeStruct((count, D), jnp.bfloat16),
        compiler_params=pltpu.CompilerParams(vmem_limit_bytes=VMEM),
        cost_estimate=SMALL_COST,
        name="down",
    )(hid_a, hid_b, wd_a, wd_b)


CORE = [(0, 1), (1, 0), (2, 3), (3, 2)]
CROSS = [(0, 2), (2, 0), (1, 3), (3, 1)]
DIAG = [(0, 3), (3, 0), (1, 2), (2, 1)]


def low(values):
    return values.astype(jnp.bfloat16)


def wide(values):
    return values.astype(jnp.float32)


def swap_core(values):
    return lax.ppermute(values, "grp", CORE)


def swap_cross(values):
    return lax.ppermute(values, "grp", CROSS)


def swap_diag(values):
    return lax.ppermute(values, "grp", DIAG)


def swap_blk(values, bit):
    count = lax.axis_size("blk")
    return lax.ppermute(values, "blk", [(i, i ^ bit) for i in range(count)])


def blk_bit(bit):
    return (lax.axis_index("blk") & bit) != 0


def bits_of(count):
    out = []
    bit = count // 2
    while bit >= 1:
        out.append(bit)
        bit //= 2
    return out


def gather_bits(values, order):
    done = []
    for bit in order:
        other = swap_blk(values, bit)
        mine = blk_bit(bit)
        axis = sum(1 for d in done if d > bit)
        values = jnp.stack(
            [jnp.where(mine, other, values), jnp.where(mine, values, other)], axis=axis
        )
        done.append(bit)
    return values


def scatter_bits(values, axes, order):
    axes = list(axes)
    for bit in order:
        axis = axes.index(bit)
        mine = blk_bit(bit).astype(jnp.int32)
        keep = lax.dynamic_index_in_dim(values, mine, axis, keepdims=False)
        send = lax.dynamic_index_in_dim(values, 1 - mine, axis, keepdims=False)
        values = low(wide(keep) + wide(swap_blk(send, bit)))
        axes.remove(bit)
    return values


def by_place(parts):
    grp = lax.axis_index("grp")
    core = (grp & 1) != 0
    cross = (grp & 2) != 0
    a, b, c, d = parts
    a, b = jnp.where(core, b, a), jnp.where(core, a, b)
    c, d = jnp.where(core, d, c), jnp.where(core, c, d)
    a, c = jnp.where(cross, c, a), jnp.where(cross, a, c)
    b, d = jnp.where(cross, d, b), jnp.where(cross, b, d)
    return [a, b, c, d]


def gather_near(values):
    cross = swap_cross(values)
    both = swap_core(jnp.stack([values, cross]))
    return [values, both[0], cross, both[1]]


def gather_grp(values):
    return by_place(gather_near(values))


def gather_tokens(values, bit):
    half = values.shape[0] // 2
    cross = swap_cross(values)
    over = swap_blk(values, bit)
    first = swap_blk(cross[:half], bit)
    second = swap_cross(over[half:])
    chip = jnp.concatenate([values, cross, over, first, second])
    return jnp.concatenate([chip, swap_core(chip)])


def angles_of(position):
    half = HD // 2
    freqs = ROPE_BASE ** (-2.0 * jnp.arange(half, dtype=jnp.float32) / HD)
    return position.astype(jnp.float32)[:, None] * freqs[None, :]


def rotate_by(values, cosine, sine):
    half = HD // 2
    first_half = values[..., :half]
    second_half = values[..., half:]
    return jnp.concatenate(
        [first_half * cosine - second_half * sine, second_half * cosine + first_half * sine],
        axis=-1,
    )


def after(values, anchor):
    return lax.optimization_barrier((values, anchor))[0]


def gather_step(values, done, bit):
    other = swap_blk(values, bit)
    mine = blk_bit(bit)
    axis = sum(1 for d in done if d > bit)
    return jnp.stack(
        [jnp.where(mine, other, values), jnp.where(mine, values, other)], axis=axis
    )


def gather_near_stacked(values):
    both = jnp.stack([values, swap_cross(values)])
    return jnp.concatenate([both, swap_core(both)])


def ring_order(count):
    return list(range(0, count, 2)) + list(range(count - 1, 0, -2))


def ring_groups(count):
    return [[g * count + b for b in ring_order(count)] for g in range(4)]


def gather_ring(values):
    count = lax.axis_size("blk")
    return lax.all_gather(values, ("grp", "blk"), axis=0, axis_index_groups=ring_groups(count))


def exchange_near(parts):
    cross = swap_cross(jnp.stack([parts[2], parts[3]]))
    core = swap_core(jnp.stack([parts[1], cross[1]]))
    return [parts[0], core[0], cross[0], core[1]]


def on_device(
    tokens,
    cotangent,
    segment_ids,
    position_ids,
    w_attend,
    w_out,
    w_gate,
    w_up,
    w_down,
    small_params,
    first_attend,
    first_out,
    first_gate,
    first_up,
    first_down,
    first_small,
    second_attend,
    second_out,
    second_gate,
    second_up,
    second_down,
    second_small,
):
    rows_here, block_len = tokens.shape[:2]
    blk_count = lax.axis_size("blk")
    seq_len = block_len * blk_count
    token_count = rows_here * block_len
    grp = lax.axis_index("grp")
    blk = lax.axis_index("blk")
    cross_id, core_id = grp // 2, grp % 2
    strip_heads = H // 4
    strip_q = strip_heads * HD
    bits = bits_of(blk_count)
    team = blk_count // 4
    lows = [bit for bit in bits if bit < team]
    spread = [bits[0]] + lows
    low_shape = (2,) * len(lows)
    in_team = blk_bit(team).astype(jnp.int32)
    weight_rows = w_gate.shape[0]
    ff_block = w_down.shape[0]
    quarter = ff_block // 4
    widths = [size * blk_count // 2 for at, size in halves_of(quarter)]
    chip_rows = 4 * token_count
    half = token_count // 2

    ids = jnp.stack([grp, in_team])
    flat_low = tokens.reshape(token_count, D)
    dy_low = cotangent.reshape(token_count, D)
    positions = position_ids.reshape(token_count)
    kv_at = HQD + HD * cross_id + KVD * core_id
    strip_local = low(
        jnp.concatenate(
            [
                lax.dynamic_slice_in_dim(w_attend, strip_q * grp, strip_q, 1),
                lax.dynamic_slice_in_dim(w_attend, kv_at, HD, 1),
            ],
            axis=1,
        )
    )
    small_count = small_params.shape[0]
    small_send = jnp.concatenate([low(small_params), low(segment_ids.reshape(token_count))])
    strip_wide = strip_q + HD
    small_send = jnp.pad(small_send, (0, -small_send.shape[0] % (16 * strip_wide)))
    strip_local = jnp.concatenate([strip_local, small_send.reshape(-1, strip_wide)])
    ring = ring_order(blk_count)
    strip_ring = gather_ring(strip_local)
    strip = jnp.concatenate([strip_ring[ring.index(b), :weight_rows] for b in range(blk_count)])
    small_all = jnp.stack([strip_ring[ring.index(b), weight_rows:] for b in range(blk_count)])
    small_all = small_all.reshape(blk_count, -1)
    digits = low(jnp.stack([positions // 64, positions % 64], axis=1))
    digits = jnp.pad(digits, ((0, 0), (0, HD - 2)))
    token_send = jnp.concatenate([flat_low, digits], axis=1)
    token_cross = swap_cross(token_send)
    dy_over = swap_blk(dy_low, team)
    dy_cross = swap_cross(after(dy_low, token_cross))

    def place(values, other, done, bit, lead=0):
        mine = blk_bit(bit)
        axis = lead + sum(1 for d in done if d > bit)
        return jnp.stack(
            [jnp.where(mine, other, values), jnp.where(mine, values, other)], axis=axis
        )

    mine_team = blk_bit(team)
    (low_first, size_first), (low_second, size_second) = halves_of(quarter)

    def team_pair(mine, got):
        return jnp.stack(
            [jnp.where(mine_team, got, mine), jnp.where(mine_team, mine, got)], axis=1
        )

    out_local = low(lax.dynamic_slice_in_dim(w_out, strip_q * grp, strip_q, 1))
    out_ring = gather_ring(after(out_local, strip_ring))
    picked_a, picked_b = pick_columns(ids, w_gate, w_up, blk_count)
    got_a = swap_blk(picked_a[1], team)
    down_here = low(lax.dynamic_slice_in_dim(w_down, quarter * grp, quarter, 0))
    down_got = swap_blk(after(down_here, token_cross), bits[0])
    down_here = place(down_here, down_got, [], bits[0])
    pair_a = team_pair(picked_a[0], got_a)
    token_core = swap_core(jnp.stack([token_send, token_cross]))
    near_all = jnp.concatenate([token_send, token_core[0], token_cross, token_core[1]])
    near_all = after(near_all, (pair_a, down_here, dy_cross, dy_over))
    dy_first = swap_blk(dy_cross[:half], team)
    dy_second = swap_cross(dy_over[half:])
    near_tokens = near_all[:, :D]
    near_positions = 64.0 * wide(near_all[:, D]) + wide(near_all[:, D + 1])
    vector = wide(small_all[:, :small_count].reshape(-1))
    gain_one = vector[:D]
    gain_two = vector[D : 2 * D]
    bias = vector[2 * D :]
    strip_bias = jnp.concatenate(
        [
            lax.dynamic_slice_in_dim(bias, strip_q * grp, strip_q, 0),
            lax.dynamic_slice_in_dim(bias, kv_at, HD, 0),
        ]
    )
    seg_all = small_all[:, small_count : small_count + token_count].astype(jnp.int32)
    seg_all = seg_all.reshape(blk_count, rows_here, block_len)
    seg_key = jnp.broadcast_to(
        seg_all.transpose(1, 0, 2).reshape(rows_here, seq_len)[:, :, None], (rows_here, seq_len, HD)
    )
    seg_query = jnp.broadcast_to(segment_ids[:, None, :], (rows_here, 8, block_len))
    first_blk = jnp.sum((seg_all[:, :, -1] < segment_ids[None, :, 0]).astype(jnp.int32), axis=0)
    attend_ids = jnp.concatenate([blk[None], first_blk])

    near_wide = wide(near_tokens)
    near_one = low(norm_apply(near_wide, gain_one))
    mixed = jnp.dot(near_one, strip, preferred_element_type=jnp.float32) + strip_bias
    angles = angles_of(near_positions)[:, None, :]
    turned = jnp.arange(strip_heads + 1)[None, :, None] < strip_heads + 1 - core_id
    angles = jnp.where(turned, angles, 0.0)
    strip_out = low(
        rotate_by(
            mixed.reshape(4 * token_count, strip_heads + 1, HD), jnp.cos(angles), jnp.sin(angles)
        )
    ).reshape(4, token_count, strip_q + HD)
    strips = by_place(exchange_near(strip_out))
    query = jnp.concatenate([part[:, :strip_q] for part in strips], axis=1)
    key_value = jnp.concatenate([strips[k][:, strip_q:] for k in (0, 2, 1, 3)], axis=1)
    key_value = key_value.reshape(rows_here, block_len, 2 * KVD)
    key_value = after(key_value, (dy_first, dy_second))
    kv_all = gather_ring(key_value)
    dy_chip = jnp.concatenate([dy_low, dy_cross, dy_over, dy_first, dy_second])
    dy_team = jnp.concatenate([dy_chip, swap_core(dy_chip)])

    teams = [
        [g * blk_count + (i | t) for g in range(4) for t in (0, team)]
        for i in range(blk_count)
        if not i & team
    ]
    order = jnp.stack(
        [
            (grp ^ (2 * (i & 1) + (i >> 2))) * 2 + (in_team ^ ((i >> 1) & 1))
            for i in range(8)
        ]
    )

    peers = [[i for i in range(blk_count) if (i & team) == t] for t in (0, team)]

    def lows_of(values, done, lead=0, anchor=None):
        for bit in lows:
            got = swap_blk(values, bit)
            if anchor is not None:
                got = after(got, anchor)
            values = place(values, got, done, bit, lead)
            done = done + [bit]
        return values

    pair_a_got = swap_blk(pair_a, bits[0])
    down_here = lows_of(down_here, [bits[0]]).reshape(2 * blk_count // 4, quarter, D)
    got_b = swap_blk(after(picked_b[1], strip_out), team)
    pair_a = place(pair_a, after(pair_a_got, key_value), [team], bits[0], 1)
    pair_b = team_pair(picked_b[0], after(got_b, key_value))
    kv_all = after(kv_all, (pair_a, pair_b, down_here, dy_team))

    gate_up_a = lows_of(after(pair_a, kv_all), [bits[0], team], 1).reshape(2, D, -1)
    pair_b = after(pair_b, kv_all)
    pair_b_got = swap_blk(pair_b, bits[0])
    down_a = down_here[:, :size_first].reshape(widths[0], D)
    down_b = down_here[:, size_first:].reshape(widths[1], D)

    out_ring = after(out_ring, key_value)
    out_strip = jnp.concatenate([out_ring[ring.index(b)] for b in range(blk_count)])
    out_cross = swap_cross(out_strip)
    out_core = swap_core(jnp.stack([out_strip, after(out_cross, kv_all)]))
    out_full = jnp.concatenate(by_place([out_strip, out_core[0], out_cross, out_core[1]]), axis=1)

    att_in, lse = attend(attend_ids, query, kv_all, seg_key, seg_query, block_len)

    flat = wide(flat_low)
    resid = flat + jnp.dot(att_in, out_full, preferred_element_type=jnp.float32)
    h_two = low(norm_apply(resid, gain_two))
    h_team = lax.all_gather(h_two, ("grp", "blk"), axis=0, tiled=True, axis_index_groups=teams)
    pair_b_got = after(pair_b_got, (h_two, gate_up_a))
    pair_b = place(pair_b, pair_b_got, [team], bits[0], 1)
    h_team = after(h_team, (gate_up_a, pair_b))
    hidden_a, d_gate_a, d_up_a, part_a = middle(order, h_team, dy_team, gate_up_a, down_a)
    gate_up_b = lows_of(pair_b, [bits[0], team], 1, hidden_a).reshape(2, D, -1)
    down_grad_a = down_grad(hidden_a, dy_team)
    down_share_a = lax.psum_scatter(
        down_grad_a, "blk", scatter_dimension=0, axis_index_groups=peers, tiled=True
    )
    column_grad_a = two_grads(h_team, d_gate_a, d_up_a)

    def part_sent(values, axis, bit):
        mine = blk_bit(bit).astype(jnp.int32)
        keep = lax.dynamic_index_in_dim(values, mine, axis, keepdims=False)
        send = lax.dynamic_index_in_dim(values, 1 - mine, axis, keepdims=False)
        return keep, swap_blk(send, bit)

    def part_sum(keep, got):
        return low(wide(keep) + wide(got))

    def columns_first(grad):
        grad = grad.reshape((2, 2, 2) + low_shape + (weight_rows, -1))
        return part_sent(grad, 2 + len(lows), lows[-1])

    def columns_mid(keep, got):
        values = part_sum(keep, got)
        for i in range(len(lows) - 2, -1, -1):
            values = part_sum(*part_sent(values, 3 + i, lows[i]))
        return values

    def columns_third(keep, got):
        values = part_sum(keep, got)
        mine = lax.dynamic_index_in_dim(values, in_team, 1, keepdims=False)
        send = lax.dynamic_index_in_dim(values, 1 - in_team, 1, keepdims=False)
        return values, (mine, swap_blk(send, team))

    def rows_second(keep, got):
        values = part_sum(keep, got)
        for i in range(len(lows) - 2, -1, -1):
            values = part_sum(*part_sent(values, 1 + i, lows[i]))
        return part_sent(values, 0, bits[0])

    def columns_last(mine, got):
        return jnp.stack(
            [jnp.where(mine_team, got, mine), jnp.where(mine_team, mine, got)], axis=1
        )

    first_a = columns_first(column_grad_a)
    hidden_b, d_gate_b, d_up_b, d_htwo_part = middle(
        order, after(h_team, (column_grad_a, down_grad_a)), dy_team, gate_up_b, down_b, part_a
    )

    def chip_sum(values, came):
        return low(wide(values[:chip_rows]) + wide(came))

    def scatter_far(chip):
        far = chip[3 * token_count :]
        return swap_blk(far[:half], team), swap_cross(far[half:])

    def scatter_near(chip, first, second):
        cross, over = (chip[token_count * i : token_count * (i + 1)] for i in (1, 2))
        cross = jnp.concatenate([low(wide(cross[:half]) + wide(first)), cross[half:]])
        over = jnp.concatenate([over[:half], low(wide(over[half:]) + wide(second))])
        return swap_cross(cross), swap_blk(over, team)

    d_came = swap_core(d_htwo_part[chip_rows:])
    down_grad_b = down_grad(hidden_b, dy_team)
    rows_b = part_sent(
        down_grad_b.reshape((2,) + low_shape + (size_second, D)), len(lows), lows[-1]
    )
    d_chip = chip_sum(d_htwo_part, after(d_came, down_grad_b))
    d_far = scatter_far(d_chip)
    column_grad_b = two_grads(h_team, *after((d_gate_b, d_up_b), d_chip))
    first_b = columns_first(column_grad_b)
    d_far = after(d_far, column_grad_b)
    d_cross, d_over = scatter_near(d_chip, *d_far)
    out_part = down(*after((hidden_a, hidden_b), d_far), down_a, down_b, token_count)
    out_came = swap_core(out_part[chip_rows:])
    mid_a = columns_mid(*after(first_a, out_part))
    second_a = part_sent(mid_a, 1, bits[0])
    d_cross, d_over = after((d_cross, d_over), out_part)
    d_htwo = wide(d_chip[:token_count]) + wide(d_cross) + wide(d_over)

    norm_value_two, norm_back_two = jax.vjp(norm_apply, resid, gain_two)
    d_resid_norm, grad_gain_two = norm_back_two(d_htwo)
    d_resid = wide(dy_low) + d_resid_norm
    d_att = after(low(d_resid), down_share_a)
    rows_b = rows_second(*after(rows_b, d_att))

    d_attended = low(right_transposed(d_att, out_full))
    own_angles = angles_of(positions)
    cosine, sine = jnp.cos(own_angles), jnp.sin(own_angles)
    d_query, dkv = attend_back(
        attend_ids,
        query,
        kv_all,
        seg_key,
        seg_query,
        att_in,
        d_attended,
        lse,
        jnp.concatenate([cosine, cosine], axis=1),
        jnp.concatenate([sine, sine], axis=1),
        block_len,
    )
    dkv = lax.psum_scatter(
        dkv.reshape(blk_count * token_count, 2 * KVD),
        ("grp", "blk"),
        scatter_dimension=0,
        axis_index_groups=ring_groups(blk_count),
        tiled=True,
    )
    down_share_b = part_sum(*after(rows_b, d_query))
    sum_a, third_a = columns_third(*after(second_a, d_query))

    def to_strips(parts):
        return jnp.concatenate(exchange_near(by_place(parts)))

    near_dq = to_strips([d_query[:, strip_q * k : strip_q * (k + 1)] for k in range(4)])
    block_shape = (2,) * len(bits) + (weight_rows, -1)
    query_grad = low(left_product(near_one, near_dq)).reshape(block_shape)
    steps_query = part_sent(query_grad, len(bits) - 1, bits[-1])
    near_a = gather_near_stacked(columns_last(*after(third_a, d_query)))
    dkv = wide(after(dkv, (query_grad, down_share_b))).reshape(token_count, 2, KVH, HD)
    d_key = low(rotate_by(dkv[:, 0], cosine[:, None], -sine[:, None]))
    d_value = low(dkv[:, 1])
    near_dkv = to_strips([(d_value if k % 2 else d_key)[:, k // 2] for k in range(4)])
    near_dkv = after(near_dkv, near_a)
    kv_grad = low(left_product(near_one, near_dkv)).reshape(block_shape)
    grad_bias = jnp.concatenate(
        [
            jnp.sum(wide(part), axis=0)
            for part in (d_query, d_key.reshape(token_count, KVD), d_value.reshape(token_count, KVD))
        ]
    )
    near_hone = right_transposed(near_dq, strip[:, :strip_q]) + right_transposed(
        near_dkv, strip[:, strip_q:]
    )
    near_rms = lax.rsqrt(jnp.mean(near_wide * near_wide, axis=-1, keepdims=True) + NORM_EPS)
    gain_one_part = jnp.sum(near_hone * near_wide * near_rms, axis=0)
    vector_rows = -(-small_count // HD)
    vector_term = jnp.concatenate([gain_one_part, grad_gain_two, grad_bias])
    vector_term = vector_term.reshape(blk_count, small_count)
    vector_term = jnp.pad(vector_term, ((0, 0), (0, vector_rows * HD - small_count)))
    vector_term = low(vector_term).reshape((2,) * len(bits) + (vector_rows, HD))
    kv_grad = jnp.concatenate([kv_grad, vector_term], axis=-2)
    kv_pad = -kv_grad.shape[-2] % 16
    kv_grad = jnp.pad(kv_grad, ((0, 0),) * (len(bits)) + ((0, kv_pad), (0, 0)))
    steps_kv = part_sent(kv_grad, len(bits) - 1, bits[-1])
    second_b = part_sent(columns_mid(*after(first_b, dkv)), 1, bits[0])
    share_down = after(jnp.concatenate([down_share_a, down_share_b]), dkv)
    grad_down = lax.all_gather(share_down, "grp", axis=0, tiled=True)
    for i in range(len(bits) - 2, -1, -1):
        steps_query = part_sent(part_sum(*after(steps_query, d_key)), i, bits[i])
        kv_sum = part_sum(*steps_kv)
        kv_grad = kv_sum
        steps_kv = part_sent(kv_sum, i, bits[i])
    share_kv_all = wide(steps_kv[0]) + wide(steps_kv[1])
    share_kv = low(share_kv_all[:weight_rows])
    vector_part = share_kv_all[weight_rows : weight_rows + vector_rows]
    sum_b, third_b = columns_third(*after(second_b, kv_grad))
    share_query = part_sum(*after(steps_query, kv_grad))
    near_att = jnp.concatenate(gather_near(after(att_in, hidden_a)))
    near_datt = to_strips([d_att[:, strip_q * k : strip_q * (k + 1)] for k in range(4)])
    out_grad = low(left_product(near_att, after(near_datt, d_attended))).reshape(block_shape)
    steps_out = part_sent(out_grad, len(bits) - 1, bits[-1])
    anchors = [d_query, d_key]
    for i in range(len(bits) - 2, -1, -1):
        anchor = anchors[min(len(bits) - 2 - i, 1)]
        steps_out = part_sent(part_sum(*after(steps_out, anchor)), i, bits[i])
    share_out = part_sum(*after(steps_out, kv_grad))

    near_b = gather_near_stacked(columns_last(*third_b))
    grad_out = jnp.concatenate(gather_grp(share_out), axis=1)
    query_parts = gather_grp(share_query)
    key_parts = gather_grp(share_kv)
    grad_attend = jnp.concatenate(query_parts + [key_parts[k] for k in (0, 2, 1, 3)], axis=1)

    sides = low(near_hone[token_count : 2 * token_count]), low(near_hone[3 * token_count :])
    other = wide(swap_core(jnp.concatenate(sides)))
    d_hone = near_hone[:token_count] + other[:token_count]
    d_hone_cross = swap_cross(
        low(near_hone[2 * token_count : 3 * token_count] + other[token_count:])
    )
    square_sum = square_total(
        [
            wide(s)
            for s in (share_query, share_kv, share_out, sum_a, sum_b, share_down)
        ]
    )
    packed = jnp.concatenate([vector_part, jnp.full((8, HD), square_sum)])
    packed = packed + swap_cross(packed)
    packed = packed + swap_core(packed)
    share_vector = packed[:vector_rows].reshape(-1)[:small_count]
    square_sum = packed[vector_rows:] + jnp.sum(share_vector * share_vector)
    for bit in bits:
        square_sum = square_sum + swap_blk(square_sum, bit)
    grad_norm = jnp.sqrt(square_sum[0, 0])
    factor = jnp.minimum(1.0, CLIP_NORM / (grad_norm + 1e-06))
    out_chip = chip_sum(out_part, after(out_came, kv_grad))
    out_far = scatter_far(out_chip)
    factor = after(factor, out_chip)

    new_first_gate, new_second_gate, new_gate = adam_columns(
        0, ids, factor[None], near_a, near_b, w_gate, first_gate, second_gate, blk_count, RATE_GATE, WEIGHT_DECAY
    )
    new_first_up, new_second_up, new_up = adam_columns(
        1, ids, factor[None], near_a, near_b, w_up, first_up, second_up, blk_count, RATE_GATE, WEIGHT_DECAY
    )
    norm_value_one, norm_back_one = jax.vjp(norm_apply, flat, gain_one)
    d_hone = after(d_hone + wide(after(d_hone_cross, new_gate)), new_gate)
    d_flat_norm, unused_gain = norm_back_one(d_hone)
    grad_tokens = low(d_resid + d_flat_norm)

    new_first_attend, new_second_attend, new_attend = adam_step(
        w_attend, factor * wide(grad_attend), first_attend, second_attend, RATE_ATTEND, WEIGHT_DECAY
    )
    new_first_out, new_second_out, new_out = adam_step(
        w_out, factor * wide(grad_out), first_out, second_out, RATE_OUT, WEIGHT_DECAY
    )
    new_first_down, new_second_down, new_down = adam_step(
        w_down, factor * wide(grad_down), first_down, second_down, RATE_DOWN, WEIGHT_DECAY
    )
    new_first_small, new_second_small, new_small = adam_step(
        small_params, factor * share_vector, first_small, second_small, RATE_VECTOR, 0.0
    )

    out_far = after(out_far, new_down)
    out_near = after(scatter_near(out_chip, *out_far), (new_gate, new_up))
    out_tokens = low(resid + wide(out_chip[:token_count]) + wide(out_near[0]) + wide(out_near[1]))
    return (
        out_tokens.reshape(rows_here, block_len, D),
        grad_tokens.reshape(rows_here, block_len, D),
        grad_norm,
        new_first_attend,
        new_second_attend,
        new_attend,
        new_first_out,
        new_second_out,
        new_out,
        new_first_gate,
        new_second_gate,
        new_gate,
        new_first_up,
        new_second_up,
        new_up,
        new_first_down,
        new_second_down,
        new_down,
        new_first_small,
        new_second_small,
        new_small,
    )


def solution(mesh):
    placed = (
        P("grp", "blk", None),
        P("grp", "blk", None),
        P("grp", "blk"),
        P("grp", "blk"),
        P("blk", None),
        P("blk", None),
        P("blk", None),
        P("blk", None),
        P("blk", None),
        P("blk"),
        P("blk", None),
        P("blk", None),
        P("blk", None),
        P("blk", None),
        P("blk", None),
        P("blk"),
        P("blk", None),
        P("blk", None),
        P("blk", None),
        P("blk", None),
        P("blk", None),
        P("blk"),
    )
    return jax.shard_map(
        on_device,
        mesh=mesh,
        in_specs=placed,
        out_specs=(
            P("grp", "blk", None),
            P("grp", "blk", None),
            P(),
            P("blk", None),
            P("blk", None),
            P("blk", None),
            P("blk", None),
            P("blk", None),
            P("blk", None),
            P("blk", None),
            P("blk", None),
            P("blk", None),
            P("blk", None),
            P("blk", None),
            P("blk", None),
            P("blk", None),
            P("blk", None),
            P("blk", None),
            P("blk"),
            P("blk"),
            P("blk"),
        ),
        check_vma=False,
    )
```

```python
import functools

import jax
import jax.numpy as jnp
from jax import lax
from jax.experimental import pallas as pl
from jax.experimental.pallas import tpu as pltpu
from jax.sharding import PartitionSpec as P

D = 1536
FF = 8960
H = 12
KVH = 2
HD = 128
STEP = 10
HQD = 1536
KVD = 256


NORM_EPS = 1e-06
ROPE_BASE = 10000.0
CLIP_NORM = 1.0
BETA_FIRST = 0.9
BETA_SECOND = 0.95
ADAM_EPS = 1e-08
WEIGHT_DECAY = 0.1
RATE_ATTEND = 0.06
RATE_OUT = 0.5
RATE_GATE = 0.06
RATE_DOWN = 0.03
RATE_VECTOR = 0.5
NEG_LARGE = -1e30
LOG2E = 1.4426950408889634
VMEM = 48 * 1024 * 1024
SMALL_COST = pl.CostEstimate(flops=1000, bytes_accessed=1000, transcendentals=0)


def norm_apply(values, gain):
    return values * lax.rsqrt(jnp.mean(values * values, axis=-1, keepdims=True) + NORM_EPS) * gain


def swish_product(gate, up_proj):
    return jax.nn.silu(gate) * up_proj


def left_product(left_side, right_side):
    return lax.dot_general(
        left_side, right_side, (((0,), (0,)), ((), ())), preferred_element_type=jnp.float32
    )


def right_transposed(left_side, right_side):
    return lax.dot_general(
        left_side, right_side, (((1,), (1,)), ((), ())), preferred_element_type=jnp.float32
    )


def square_total(arrays):
    return sum((jnp.sum(member * member) for member in arrays))


def adam_step(weight, grad, first, second, rate, decay):
    first_new = BETA_FIRST * first + (1.0 - BETA_FIRST) * grad
    second_new = BETA_SECOND * second + (1.0 - BETA_SECOND) * grad * grad
    first_hat = first_new / (1.0 - BETA_FIRST**STEP)
    second_hat = second_new / (1.0 - BETA_SECOND**STEP)
    weight_new = weight - rate * (first_hat / (jnp.sqrt(second_hat) + ADAM_EPS) + decay * weight)
    return (first_new, second_new, weight_new)


def ring_order(count):
    return list(range(0, count, 2)) + list(range(count - 1, 0, -2))


def halves_of(quarter):
    first = quarter * 16 // 35
    return ((0, first), (first, quarter - first))


def pick_body(blk_count, ids, gate_ref, up_ref, *out_refs):
    quarter = FF // blk_count // 4
    per = blk_count // 4
    for k in range(4):

        @pl.when(ids[0] == k)
        def _(k=k):
            for (at, size), out_ref in zip(halves_of(quarter), out_refs):
                for which, src in enumerate((gate_ref, up_ref)):
                    for bit in range(2):
                        parts = []
                        for high in range(2):
                            for small in range(per):
                                begin = (((high * 2 + bit) * per + small) * 4 + k) * quarter + at
                                parts.append(src[:, begin : begin + size])
                        out_ref[ids[1] ^ bit, which] = jnp.concatenate(parts, axis=1).astype(
                            jnp.bfloat16
                        )


def pick_columns(ids, gate, up, blk_count):
    rows = gate.shape[0]
    step = 48 if rows % 48 == 0 else rows
    widths = [size * blk_count // 2 for at, size in halves_of(FF // blk_count // 4)]
    spec = pl.BlockSpec((step, FF), lambda i, ids: (i, 0))
    return pl.pallas_call(
        functools.partial(pick_body, blk_count),
        grid_spec=pltpu.PrefetchScalarGridSpec(
            num_scalar_prefetch=1,
            grid=(rows // step,),
            in_specs=[spec, spec],
            out_specs=[pl.BlockSpec((2, 2, step, w), lambda i, ids: (0, 0, i, 0)) for w in widths],
        ),
        out_shape=[jax.ShapeDtypeStruct((2, 2, rows, w), jnp.bfloat16) for w in widths],
        compiler_params=pltpu.CompilerParams(vmem_limit_bytes=VMEM),
        cost_estimate=SMALL_COST,
        name="pick_columns",
    )(ids, gate, up)


def near_at(away):
    return (away & 1) * 2 + (away >> 1)


def adam_body(blk_count, rate, decay, ids, factor_ref, first_ref, second_ref, w_ref, m_ref, v_ref, m_out, v_out, w_out):
    per = blk_count // 4
    sizes = [size for at, size in halves_of(FF // blk_count // 4)]
    grads = [
        [[ref[near_at(ids[0] ^ k), bit] for bit in range(2)] for k in range(4)]
        for ref in (first_ref, second_ref)
    ]
    parts = []
    for high in range(2):
        for bit in range(2):
            for small in range(per):
                place = high * per + small
                for k in range(4):
                    for part, size in zip(grads, sizes):
                        parts.append(part[k][bit][:, place * size : (place + 1) * size])
    grad = jnp.concatenate(parts, axis=1).astype(jnp.float32) * factor_ref[0]
    m, v, w = adam_step(w_ref[...], grad, m_ref[...], v_ref[...], rate, decay)
    m_out[...] = m
    v_out[...] = v
    w_out[...] = w


def adam_columns(which, ids, factor, first, second, w, m, v, blk_count, rate, decay):
    rows = w.shape[0]
    step = 32 if rows % 32 == 0 else rows
    spec = pl.BlockSpec((step, FF), lambda i, ids: (i, 0))
    shape = jax.ShapeDtypeStruct((rows, FF), jnp.float32)
    grads = [
        pl.BlockSpec((4, None, 2, step, g.shape[-1]), lambda i, ids: (0, which, 0, i, 0))
        for g in (first, second)
    ]
    return pl.pallas_call(
        functools.partial(adam_body, blk_count, rate, decay),
        grid_spec=pltpu.PrefetchScalarGridSpec(
            num_scalar_prefetch=1,
            grid=(rows // step,),
            in_specs=[pl.BlockSpec(memory_space=pltpu.SMEM)] + grads + [spec, spec, spec],
            out_specs=[spec, spec, spec],
        ),
        out_shape=[shape] * 3,
        compiler_params=pltpu.CompilerParams(vmem_limit_bytes=VMEM),
        cost_estimate=SMALL_COST,
        name="adam_columns",
    )(ids, factor, first, second, w, m, v)


def nt(a, b, **kw):
    return lax.dot_general(a, b, (((1,), (1,)), ((), ())), preferred_element_type=jnp.float32, **kw)

def tn(a, b, **kw):
    return lax.dot_general(a, b, (((0,), (0,)), ((), ())), preferred_element_type=jnp.float32, **kw)

def stack_heads(ref, kvh, group):
    return jnp.concatenate([ref[:, HD * (kvh * group + i): HD * (kvh * group + i + 1)] for i in range(group)], axis=0)

def hidden_from(seg_key_ref, seg_query_ref, first, chunk, block_len, blk):
    key = first + lax.broadcasted_iota(jnp.int32, (chunk, block_len), 0)
    query = blk * block_len + lax.broadcasted_iota(jnp.int32, (chunk, block_len), 1)
    seg_key = seg_key_ref[pl.ds(first, chunk), :]
    counts = jnp.logical_and(key <= query, seg_key == seg_query_ref[0:1, :])
    return jnp.where(counts, 0.0, NEG_LARGE)

def ring_pair(ref, c, at):
    return jnp.concatenate(
        [ref[c, :, at : at + HD], ref[ref.shape[0] - 1 - c, :, at : at + HD]], axis=0
    )


def attend_body(chunk, ids, q_ref, k_ref, v_ref, seg_key_ref, seg_query_ref, o_ref, lse_ref, m_s, l_s, acc_s):
    block_len = q_ref.shape[0]
    group = H // KVH
    row = pl.program_id(0)
    per = chunk // block_len
    scale = HD ** (-0.5) * LOG2E
    start = ids[1 + row] // per
    stop = ids[0] // per + 1
    for kvh in range(KVH):
        q = stack_heads(q_ref, kvh, group)
        m_s[...] = jnp.full_like(m_s, NEG_LARGE)
        l_s[...] = jnp.zeros_like(l_s)
        acc_s[...] = jnp.zeros_like(acc_s)

        def step(c, carry):
            keys = ring_pair(k_ref, c, HD * kvh)
            vals = ring_pair(v_ref, c, HD * kvh)
            bias = hidden_from(seg_key_ref, seg_query_ref, c * chunk, chunk, block_len, ids[0])
            s = nt(keys, q) * scale + jnp.concatenate([bias] * group, axis=1)
            old = m_s[0:1, :]
            new = jnp.maximum(old, jnp.max(s, axis=0, keepdims=True))
            p = jnp.exp2(s - new)
            fade = jnp.exp2(old - new)
            l_s[0:1, :] = l_s[0:1, :] * fade + jnp.sum(p, axis=0, keepdims=True)
            acc_s[...] = acc_s[...] * fade + tn(vals, p.astype(jnp.bfloat16))
            m_s[0:1, :] = new
            return carry

        lax.fori_loop(start, stop, step, 0)
        total = l_s[0:1, :]
        out = (acc_s[...] * (1.0 / total)).T
        for i in range(group):
            o_ref[:, HD * (kvh * group + i): HD * (kvh * group + i + 1)] = out[block_len * i: block_len * (i + 1), :].astype(jnp.bfloat16)
        lse_ref[kvh] = jnp.broadcast_to(m_s[0:1, :] + jnp.log2(total), (8, group * block_len))

def attend(ids, q, kv, seg_key, seg_query, block_len):
    blk_count, rows = kv.shape[:2]
    group = H // KVH
    chunk = 2 * block_len
    many = group * block_len
    return pl.pallas_call(
        functools.partial(attend_body, chunk),
        grid_spec=pltpu.PrefetchScalarGridSpec(
            num_scalar_prefetch=1, grid=(rows,),
            in_specs=[
                pl.BlockSpec((block_len, HQD), lambda r, ids: (r, 0)),
                pl.BlockSpec((blk_count, None, block_len, KVD), lambda r, ids: (0, r, 0, 0)),
                pl.BlockSpec((blk_count, None, block_len, KVD), lambda r, ids: (0, r, 0, 1)),
                pl.BlockSpec((None, blk_count * block_len, HD), lambda r, ids: (r, 0, 0)),
                pl.BlockSpec((None, 8, block_len), lambda r, ids: (r, 0, 0)),
            ],
            out_specs=[
                pl.BlockSpec((block_len, HQD), lambda r, ids: (r, 0)),
                pl.BlockSpec((None, KVH, 8, many), lambda r, ids: (r, 0, 0, 0)),
            ],
            scratch_shapes=[pltpu.VMEM((8, many), jnp.float32), pltpu.VMEM((8, many), jnp.float32), pltpu.VMEM((HD, many), jnp.float32)]),
        out_shape=[
            jax.ShapeDtypeStruct((rows * block_len, HQD), jnp.bfloat16),
            jax.ShapeDtypeStruct((rows, KVH, 8, many), jnp.float32),
        ],
        compiler_params=pltpu.CompilerParams(vmem_limit_bytes=VMEM),
        cost_estimate=SMALL_COST,
        name="attend",
    )(ids, q, kv, kv, seg_key, seg_query)

def turn_back(u, cosine, sine):
    lane = lax.broadcasted_iota(jnp.int32, u.shape, 1)
    other = pltpu.roll(u, HD // 2, 1)
    return u * cosine + jnp.where(lane < HD // 2, other, -other) * sine

def attend_back_body(chunk, ids, q_ref, k_ref, v_ref, seg_key_ref, seg_query_ref, o_ref, do_ref, lse_ref, cos_ref, sin_ref, dq_ref, dkv_ref, dq_s):
    block_len = q_ref.shape[0]
    group = H // KVH
    row = pl.program_id(0)
    per = chunk // block_len
    plain = HD ** (-0.5)
    scale = plain * LOG2E
    start = ids[1 + row] // per
    stop = ids[0] // per + 1
    dkv_ref[...] = jnp.zeros_like(dkv_ref)
    for kvh in range(KVH):
        q = stack_heads(q_ref, kvh, group)
        do = stack_heads(do_ref, kvh, group)
        o = stack_heads(o_ref, kvh, group)
        both = do.astype(jnp.float32) * o.astype(jnp.float32)
        delta = nt(jnp.ones((8, HD), jnp.float32), both, precision=lax.Precision.HIGHEST)[0:1, :]
        lse = lse_ref[kvh][0:1, :]
        dq_s[...] = jnp.zeros_like(dq_s)

        def step(c, carry):
            keys = ring_pair(k_ref, c, HD * kvh)
            vals = ring_pair(v_ref, c, HD * kvh)
            bias = hidden_from(seg_key_ref, seg_query_ref, c * chunk, chunk, block_len, ids[0])
            s = nt(keys, q) * scale + jnp.concatenate([bias] * group, axis=1)
            p = jnp.exp2(s - lse)
            dp = nt(vals, do)
            ds = (p * (dp - delta)).astype(jnp.bfloat16)
            dk = jnp.dot(ds, q, preferred_element_type=jnp.float32) * plain
            dv = jnp.dot(p.astype(jnp.bfloat16), do, preferred_element_type=jnp.float32)
            for at, part in ((HD * kvh, dk.astype(jnp.bfloat16)), (KVD + HD * kvh, dv.astype(jnp.bfloat16))):
                dkv_ref[c, :, at : at + HD] = part[:block_len]
                dkv_ref[dkv_ref.shape[0] - 1 - c, :, at : at + HD] = part[block_len:]
            dq_s[...] += tn(ds, keys)
            return carry

        lax.fori_loop(start, stop, step, 0)
        cosine, sine = cos_ref[...], sin_ref[...]
        for i in range(group):
            u = dq_s[block_len * i: block_len * (i + 1), :] * plain
            at = HD * (kvh * group + i)
            dq_ref[:, at: at + HD] = turn_back(u, cosine, sine).astype(jnp.bfloat16)

def attend_back(ids, q, kv, seg_key, seg_query, o, do, lse, cosine, sine, block_len):
    blk_count, rows = kv.shape[:2]
    group = H // KVH
    chunk = 2 * block_len
    many = group * block_len
    per_row = pl.BlockSpec((block_len, HQD), lambda r, ids: (r, 0))
    turn = pl.BlockSpec((block_len, HD), lambda r, ids: (r, 0))
    return pl.pallas_call(
        functools.partial(attend_back_body, chunk),
        grid_spec=pltpu.PrefetchScalarGridSpec(
            num_scalar_prefetch=1, grid=(rows,),
            in_specs=[
                per_row,
                pl.BlockSpec((blk_count, None, block_len, KVD), lambda r, ids: (0, r, 0, 0)),
                pl.BlockSpec((blk_count, None, block_len, KVD), lambda r, ids: (0, r, 0, 1)),
                pl.BlockSpec((None, blk_count * block_len, HD), lambda r, ids: (r, 0, 0)),
                pl.BlockSpec((None, 8, block_len), lambda r, ids: (r, 0, 0)),
                per_row, per_row,
                pl.BlockSpec((None, KVH, 8, many), lambda r, ids: (r, 0, 0, 0)),
                turn, turn,
            ],
            out_specs=[per_row, pl.BlockSpec((blk_count, None, block_len, 2 * KVD), lambda r, ids: (0, r, 0, 0))],
            scratch_shapes=[pltpu.VMEM((many, HD), jnp.float32)]),
        out_shape=[
            jax.ShapeDtypeStruct((rows * block_len, HQD), jnp.bfloat16),
            jax.ShapeDtypeStruct((blk_count, rows, block_len, 2 * KVD), jnp.bfloat16),
        ],
        compiler_params=pltpu.CompilerParams(vmem_limit_bytes=VMEM),
        cost_estimate=SMALL_COST,
        name="attend_back",
    )(ids, q, kv, kv, seg_key, seg_query, o, do, lse, cosine, sine)

def nn(a, b):
    return jnp.dot(a, b, preferred_element_type=jnp.float32)


def middle_body(add, order, h_ref, dy_ref, wg_ref, wu_ref, wd_ref, *refs):
    prev_ref = refs[0] if add else None
    hid_ref, dg_ref, du_ref, dh_ref = refs[-4:]
    h = h_ref[...]
    gate = nn(h, wg_ref[...])
    up = nn(h, wu_ref[...])
    sig = 1.0 / (1.0 + jnp.exp(-gate))
    silu = gate * sig
    hid_ref[...] = (silu * up).astype(jnp.bfloat16)
    dhid = nt(dy_ref[...], wd_ref[...])
    dg = (dhid * up * sig * (1.0 + gate * (1.0 - sig))).astype(jnp.bfloat16)
    du = (dhid * silu).astype(jnp.bfloat16)
    dg_ref[...] = dg
    du_ref[...] = du
    dh = nt(dg, wg_ref[...]) + nt(du, wu_ref[...])
    if add:
        dh = dh + prev_ref[...].astype(jnp.float32)
    dh_ref[...] = dh.astype(jnp.bfloat16)


def middle(order, h, dy, gate_up, wd, prev=None):
    count = h.shape[0]
    step = count // order.shape[0]
    wide_here = wd.shape[0]
    row = pl.BlockSpec((step, D), lambda i, order: (i, 0))
    placed = pl.BlockSpec((step, D), lambda i, order: (order[i], 0))
    part = pl.BlockSpec((step, wide_here), lambda i, order: (i, 0))
    part_placed = pl.BlockSpec((step, wide_here), lambda i, order: (order[i], 0))
    once = pl.Buffered(1)
    extra = [] if prev is None else [prev]
    return pl.pallas_call(
        functools.partial(middle_body, prev is not None),
        grid_spec=pltpu.PrefetchScalarGridSpec(
            num_scalar_prefetch=1,
            grid=(count // step,),
            in_specs=[
                placed,
                row,
                pl.BlockSpec((None, D, wide_here), lambda i, order: (0, 0, 0), pipeline_mode=once),
                pl.BlockSpec((None, D, wide_here), lambda i, order: (1, 0, 0), pipeline_mode=once),
                pl.BlockSpec((wide_here, D), lambda i, order: (0, 0), pipeline_mode=once),
            ]
            + [row] * len(extra),
            out_specs=[part, part_placed, part_placed, row],
        ),
        out_shape=[jax.ShapeDtypeStruct((count, wide_here), jnp.bfloat16)] * 3
        + [jax.ShapeDtypeStruct((count, D), jnp.bfloat16)],
        compiler_params=pltpu.CompilerParams(vmem_limit_bytes=VMEM),
        cost_estimate=SMALL_COST,
        name="middle",
    )(order, h, dy, gate_up, gate_up, wd, *extra)


def two_grads_body(h_ref, a_ref, b_ref, out_ref):
    h = h_ref[...]
    out_ref[0] = tn(h, a_ref[...]).astype(jnp.bfloat16)
    out_ref[1] = tn(h, b_ref[...]).astype(jnp.bfloat16)


def two_grads(h, a, b, step=256):
    count = h.shape[0]
    wide_here = a.shape[1]
    whole = pl.BlockSpec(a.shape, lambda i: (0, 0), pipeline_mode=pl.Buffered(1))
    return pl.pallas_call(
        two_grads_body,
        grid=(D // step,),
        in_specs=[pl.BlockSpec((count, step), lambda i: (0, i)), whole, whole],
        out_specs=pl.BlockSpec((2, step, wide_here), lambda i: (0, i, 0)),
        out_shape=jax.ShapeDtypeStruct((2, D, wide_here), jnp.bfloat16),
        compiler_params=pltpu.CompilerParams(vmem_limit_bytes=VMEM),
        cost_estimate=SMALL_COST,
        name="two_grads",
    )(h, a, b)


def down_grad_body(hid_ref, dy_ref, g_ref):
    g_ref[...] = tn(hid_ref[...], dy_ref[...]).astype(jnp.bfloat16)

def down_grad(hid, dy, step=512):
    T, F = hid.shape
    D = dy.shape[1]
    return pl.pallas_call(down_grad_body, grid=(D // step,),
        in_specs=[pl.BlockSpec((T, F), lambda i: (0, 0), pipeline_mode=pl.Buffered(1)), pl.BlockSpec((T, step), lambda i: (0, i))],
        out_specs=pl.BlockSpec((F, step), lambda i: (0, i)),
        out_shape=jax.ShapeDtypeStruct((F, D), jnp.bfloat16),
        compiler_params=pltpu.CompilerParams(vmem_limit_bytes=VMEM),
        cost_estimate=SMALL_COST,
        name="down_grad")(hid, dy)

def down_body(hid_a_ref, hid_b_ref, wd_a_ref, wd_b_ref, o_ref):
    out = nn(hid_a_ref[...], wd_a_ref[...]) + nn(hid_b_ref[...], wd_b_ref[...])
    o_ref[...] = out.astype(jnp.bfloat16)


def down(hid_a, hid_b, wd_a, wd_b, step):
    count = hid_a.shape[0]

    def rows(array):
        return pl.BlockSpec((step, array.shape[1]), lambda i: (i, 0))

    def whole(array):
        return pl.BlockSpec(array.shape, lambda i: (0, 0), pipeline_mode=pl.Buffered(1))

    return pl.pallas_call(
        down_body,
        grid=(count // step,),
        in_specs=[rows(hid_a), rows(hid_b), whole(wd_a), whole(wd_b)],
        out_specs=pl.BlockSpec((step, D), lambda i: (i, 0)),
        out_shape=jax.ShapeDtypeStruct((count, D), jnp.bfloat16),
        compiler_params=pltpu.CompilerParams(vmem_limit_bytes=VMEM),
        cost_estimate=SMALL_COST,
        name="down",
    )(hid_a, hid_b, wd_a, wd_b)


def turn(u, cosine, sine):
    lane = lax.broadcasted_iota(jnp.int32, u.shape, 1)
    other = pltpu.roll(u, HD // 2, 1)
    return u * cosine + jnp.where(lane < HD // 2, -other, other) * sine


def mix_body(
    blk_count, rows, small_count, ids, own_ref, cross_ref, core_ref, ring_ref, freq_ref,
    self_ref, near_ref, far_ref, one_ref, strip_ref, vector_ref,
):
    ring = ring_order(blk_count)
    wide_here = ring_ref.shape[-1]
    pieces = []
    for b in range(blk_count):
        at = ring.index(b)
        strip_ref[rows * b : rows * (b + 1)] = ring_ref[at, :rows]
        left = small_count
        line = rows
        while left > 0:
            size = min(left, wide_here)
            pieces.append(ring_ref[at, line : line + 1, :size].astype(jnp.float32))
            left -= size
            line += 1
    vector = jnp.concatenate(pieces, axis=1)
    vector_ref[...] = vector
    gain = vector[:, :D]
    grp = ids[0]
    strip_q = wide_here - HD
    bias = jnp.zeros((1, wide_here), jnp.float32)
    for k in range(4):
        kv_at = 2 * D + HQD + HD * (k // 2) + KVD * (k % 2)
        part = jnp.concatenate(
            [
                vector[:, 2 * D + strip_q * k : 2 * D + strip_q * (k + 1)],
                vector[:, kv_at : kv_at + HD],
            ],
            axis=1,
        )
        bias = bias + jnp.where(grp == k, part, 0.0)
    count = own_ref.shape[0]
    strip = strip_ref[...]
    for d in range(4):
        source = (own_ref[...], core_ref[0], cross_ref[...], core_ref[1])[d]
        x = source[:, :D].astype(jnp.float32)
        root = lax.rsqrt(jnp.mean(x * x, axis=1, keepdims=True) + NORM_EPS)
        one = (x * root * gain).astype(jnp.bfloat16)
        one_ref[count * d : count * (d + 1)] = one
        mixed = nn(one, strip) + bias
        digits = source[:, D : D + HD].astype(jnp.float32)
        position = 64.0 * digits[:, 0:1] + digits[:, 1:2]
        angles = position * freq_ref[...]
        cosine, sine = jnp.cos(angles), jnp.sin(angles)
        for i in range(wide_here // HD):
            c, s = cosine, sine
            if i == wide_here // HD - 1:
                c = jnp.where(grp % 2 == 1, 1.0, c)
                s = jnp.where(grp % 2 == 1, 0.0, s)
            at = HD * i
            out = turn(mixed[:, at : at + HD], c, s).astype(jnp.bfloat16)
            if d == 0:
                self_ref[:, at : at + HD] = out
            elif d == 1:
                near_ref[:, at : at + HD] = out
            else:
                far_ref[d - 2, :, at : at + HD] = out


def mix(ids, own, cross, core, ring, freq, blk_count, rows, small_count):
    count = own.shape[0]
    wide_here = ring.shape[-1]
    low16 = jnp.bfloat16
    return pl.pallas_call(
        functools.partial(mix_body, blk_count, rows, small_count),
        in_specs=[pl.BlockSpec(memory_space=pltpu.SMEM)] + [pl.BlockSpec(memory_space=pltpu.VMEM)] * 5,
        out_specs=[pl.BlockSpec(memory_space=pltpu.VMEM)] * 6,
        out_shape=[
            jax.ShapeDtypeStruct((count, wide_here), low16),
            jax.ShapeDtypeStruct((count, wide_here), low16),
            jax.ShapeDtypeStruct((2, count, wide_here), low16),
            jax.ShapeDtypeStruct((4 * count, D), low16),
            jax.ShapeDtypeStruct((D, wide_here), low16),
            jax.ShapeDtypeStruct((1, blk_count * small_count), jnp.float32),
        ],
        compiler_params=pltpu.CompilerParams(vmem_limit_bytes=VMEM),
        cost_estimate=SMALL_COST,
        name="mix",
    )(ids, own, cross, core, ring, freq)


def pack_body(ids, self_ref, cross_ref, core_ref, q_ref, kv_ref):
    strip_q = self_ref.shape[1] - HD
    for g in range(4):

        @pl.when(ids[0] == g)
        def _(g=g):
            for k in range(4):
                part = (self_ref[...], core_ref[0], cross_ref[0], core_ref[1])[g ^ k]
                q_ref[:, strip_q * k : strip_q * (k + 1)] = part[:, :strip_q]
                at = (k % 2) * KVD + (k // 2) * HD
                kv_ref[:, at : at + HD] = part[:, strip_q:]


def pack(ids, own, cross, core):
    count = own.shape[0]
    return pl.pallas_call(
        pack_body,
        in_specs=[pl.BlockSpec(memory_space=pltpu.SMEM)] + [pl.BlockSpec(memory_space=pltpu.VMEM)] * 3,
        out_specs=[pl.BlockSpec(memory_space=pltpu.VMEM)] * 2,
        out_shape=[
            jax.ShapeDtypeStruct((count, HQD), jnp.bfloat16),
            jax.ShapeDtypeStruct((count, 2 * KVD), jnp.bfloat16),
        ],
        compiler_params=pltpu.CompilerParams(vmem_limit_bytes=VMEM),
        cost_estimate=SMALL_COST,
        name="pack",
    )(ids, own, cross, core)


def turn_dkv_body(ids, dkv_ref, cos_ref, sin_ref, self_ref, near_ref, far_ref, sum_ref):
    items = []
    sums = [None] * 4
    for k in range(4):
        at = (k % 2) * KVD + (k // 2) * HD
        part = dkv_ref[:, at : at + HD]
        if k % 2 == 0:
            part = turn_back(part.astype(jnp.float32), cos_ref[...], sin_ref[...]).astype(jnp.bfloat16)
        items.append(part)
        sums[(k % 2) * 2 + k // 2] = jnp.sum(part.astype(jnp.float32), axis=0, keepdims=True)
    sum_ref[...] = jnp.concatenate(sums, axis=1)
    for g in range(4):

        @pl.when(ids[0] == g)
        def _(g=g):
            self_ref[...] = items[g]
            near_ref[...] = items[g ^ 1]
            far_ref[0] = items[g ^ 2]
            far_ref[1] = items[g ^ 3]


def turn_dkv(ids, dkv, cosine, sine):
    count = dkv.shape[0]
    return pl.pallas_call(
        turn_dkv_body,
        in_specs=[pl.BlockSpec(memory_space=pltpu.SMEM)] + [pl.BlockSpec(memory_space=pltpu.VMEM)] * 3,
        out_specs=[pl.BlockSpec(memory_space=pltpu.VMEM)] * 4,
        out_shape=[
            jax.ShapeDtypeStruct((count, HD), jnp.bfloat16),
            jax.ShapeDtypeStruct((count, HD), jnp.bfloat16),
            jax.ShapeDtypeStruct((2, count, HD), jnp.bfloat16),
            jax.ShapeDtypeStruct((1, 2 * KVD), jnp.float32),
        ],
        compiler_params=pltpu.CompilerParams(vmem_limit_bytes=VMEM),
        cost_estimate=SMALL_COST,
        name="turn_dkv",
    )(ids, dkv, cosine, sine)


def kv_grad_body(
    blk_count, rows, small_count, self_ref, cross_ref, core_ref, dq_ref, one_ref, own_ref, near_x_ref,
    core_x_ref, strip_ref, gain_two_ref, bias_q_ref, bias_kv_ref, grad_ref, here_ref, there_ref,
):
    count = self_ref.shape[0]
    strip_q = strip_ref.shape[1] - HD
    parts = (self_ref[...], core_ref[0], cross_ref[0], core_ref[1])
    near = jnp.concatenate(parts, axis=0)
    grad = tn(one_ref[...], near)
    gain_one = jnp.zeros((1, D), jnp.float32)
    for d in range(4):
        x = (own_ref[...], core_x_ref[0], near_x_ref[...], core_x_ref[1])[d][:, :D].astype(jnp.float32)
        root = lax.rsqrt(jnp.mean(x * x, axis=1, keepdims=True) + NORM_EPS)
        hone = nt(dq_ref[count * d : count * (d + 1)], strip_ref[:, :strip_q])
        hone = hone + nt(parts[d], strip_ref[:, strip_q:])
        gain_one = gain_one + jnp.sum(hone * x * root, axis=0, keepdims=True)
        out_ref = (here_ref, there_ref)[d % 2]
        out_ref[count * (d // 2) : count * (d // 2 + 1)] = hone.astype(jnp.bfloat16)
    vector = jnp.concatenate([gain_one, gain_two_ref[...], bias_q_ref[...], bias_kv_ref[...]], axis=1)
    extra = grad_ref.shape[1] - rows
    for b in range(blk_count):
        grad_ref[b, :rows] = grad[rows * b : rows * (b + 1)].astype(jnp.bfloat16)
        lines = []
        for line in range(extra):
            size = min(HD, max(small_count - line * HD, 0))
            begin = small_count * b + line * HD
            pieces = [vector[:, begin : begin + size]] if size > 0 else []
            if size < HD:
                pieces.append(jnp.zeros((1, HD - size), jnp.float32))
            lines.append(pieces[0] if len(pieces) == 1 else jnp.concatenate(pieces, axis=1))
        grad_ref[b, rows:] = jnp.concatenate(lines, axis=0).astype(jnp.bfloat16)


def kv_grad_rows(rows, small_count):
    needed = rows + -(-small_count // HD)
    return needed + -needed % 16


def make_kv_grad(blk_count, rows, small_count, own, cross, core, dq, one, x_own, x_cross, x_core, strip, gain_two, bias_q, bias_kv):
    count = own.shape[0]
    height = kv_grad_rows(rows, small_count)
    return pl.pallas_call(
        functools.partial(kv_grad_body, blk_count, rows, small_count),
        in_specs=[pl.BlockSpec(memory_space=pltpu.VMEM)] * 12,
        out_specs=[pl.BlockSpec(memory_space=pltpu.VMEM)] * 3,
        out_shape=[
            jax.ShapeDtypeStruct((blk_count, height, HD), jnp.bfloat16),
            jax.ShapeDtypeStruct((2 * count, D), jnp.bfloat16),
            jax.ShapeDtypeStruct((2 * count, D), jnp.bfloat16),
        ],
        compiler_params=pltpu.CompilerParams(vmem_limit_bytes=VMEM),
        cost_estimate=SMALL_COST,
        name="kv_grad",
    )(own, cross, core, dq, one, x_own, x_cross, x_core, strip, gain_two, bias_q, bias_kv)


CORE = [(0, 1), (1, 0), (2, 3), (3, 2)]
CROSS = [(0, 2), (2, 0), (1, 3), (3, 1)]
DIAG = [(0, 3), (3, 0), (1, 2), (2, 1)]


def low(values):
    return values.astype(jnp.bfloat16)


def wide(values):
    return values.astype(jnp.float32)


def swap_core(values):
    return lax.ppermute(values, "grp", CORE)


def swap_cross(values):
    return lax.ppermute(values, "grp", CROSS)


def swap_diag(values):
    return lax.ppermute(values, "grp", DIAG)


def swap_blk(values, bit):
    count = lax.axis_size("blk")
    return lax.ppermute(values, "blk", [(i, i ^ bit) for i in range(count)])


def blk_bit(bit):
    return (lax.axis_index("blk") & bit) != 0


def bits_of(count):
    out = []
    bit = count // 2
    while bit >= 1:
        out.append(bit)
        bit //= 2
    return out


def gather_bits(values, order):
    done = []
    for bit in order:
        other = swap_blk(values, bit)
        mine = blk_bit(bit)
        axis = sum(1 for d in done if d > bit)
        values = jnp.stack(
            [jnp.where(mine, other, values), jnp.where(mine, values, other)], axis=axis
        )
        done.append(bit)
    return values


def scatter_bits(values, axes, order):
    axes = list(axes)
    for bit in order:
        axis = axes.index(bit)
        mine = blk_bit(bit).astype(jnp.int32)
        keep = lax.dynamic_index_in_dim(values, mine, axis, keepdims=False)
        send = lax.dynamic_index_in_dim(values, 1 - mine, axis, keepdims=False)
        values = low(wide(keep) + wide(swap_blk(send, bit)))
        axes.remove(bit)
    return values


def by_place(parts):
    grp = lax.axis_index("grp")
    core = (grp & 1) != 0
    cross = (grp & 2) != 0
    a, b, c, d = parts
    a, b = jnp.where(core, b, a), jnp.where(core, a, b)
    c, d = jnp.where(core, d, c), jnp.where(core, c, d)
    a, c = jnp.where(cross, c, a), jnp.where(cross, a, c)
    b, d = jnp.where(cross, d, b), jnp.where(cross, b, d)
    return [a, b, c, d]


def gather_near(values):
    cross = swap_cross(values)
    both = swap_core(jnp.stack([values, cross]))
    return [values, both[0], cross, both[1]]


def gather_grp(values):
    return by_place(gather_near(values))


def gather_tokens(values, bit):
    half = values.shape[0] // 2
    cross = swap_cross(values)
    over = swap_blk(values, bit)
    first = swap_blk(cross[:half], bit)
    second = swap_cross(over[half:])
    chip = jnp.concatenate([values, cross, over, first, second])
    return jnp.concatenate([chip, swap_core(chip)])


def angles_of(position):
    half = HD // 2
    freqs = ROPE_BASE ** (-2.0 * jnp.arange(half, dtype=jnp.float32) / HD)
    return position.astype(jnp.float32)[:, None] * freqs[None, :]


def rotate_by(values, cosine, sine):
    half = HD // 2
    first_half = values[..., :half]
    second_half = values[..., half:]
    return jnp.concatenate(
        [first_half * cosine - second_half * sine, second_half * cosine + first_half * sine],
        axis=-1,
    )


def after(values, anchor):
    return lax.optimization_barrier((values, anchor))[0]


def gather_step(values, done, bit):
    other = swap_blk(values, bit)
    mine = blk_bit(bit)
    axis = sum(1 for d in done if d > bit)
    return jnp.stack(
        [jnp.where(mine, other, values), jnp.where(mine, values, other)], axis=axis
    )


def gather_near_stacked(values):
    both = jnp.stack([values, swap_cross(values)])
    return jnp.concatenate([both, swap_core(both)])


def ring_groups(count):
    return [[g * count + b for b in ring_order(count)] for g in range(4)]


def gather_ring(values):
    count = lax.axis_size("blk")
    return lax.all_gather(values, ("grp", "blk"), axis=0, axis_index_groups=ring_groups(count))


def exchange_near(parts):
    cross = swap_cross(jnp.stack([parts[2], parts[3]]))
    core = swap_core(jnp.stack([parts[1], cross[1]]))
    return [parts[0], core[0], cross[0], core[1]]


def on_device(
    tokens,
    cotangent,
    segment_ids,
    position_ids,
    w_attend,
    w_out,
    w_gate,
    w_up,
    w_down,
    small_params,
    first_attend,
    first_out,
    first_gate,
    first_up,
    first_down,
    first_small,
    second_attend,
    second_out,
    second_gate,
    second_up,
    second_down,
    second_small,
):
    rows_here, block_len = tokens.shape[:2]
    blk_count = lax.axis_size("blk")
    seq_len = block_len * blk_count
    token_count = rows_here * block_len
    grp = lax.axis_index("grp")
    blk = lax.axis_index("blk")
    cross_id, core_id = grp // 2, grp % 2
    strip_heads = H // 4
    strip_q = strip_heads * HD
    bits = bits_of(blk_count)
    team = blk_count // 4
    lows = [bit for bit in bits if bit < team]
    spread = [bits[0]] + lows
    low_shape = (2,) * len(lows)
    in_team = blk_bit(team).astype(jnp.int32)
    weight_rows = w_gate.shape[0]
    ff_block = w_down.shape[0]
    quarter = ff_block // 4
    widths = [size * blk_count // 2 for at, size in halves_of(quarter)]
    chip_rows = 4 * token_count
    half = token_count // 2

    ids = jnp.stack([grp, in_team])
    flat_low = tokens.reshape(token_count, D)
    dy_low = cotangent.reshape(token_count, D)
    positions = position_ids.reshape(token_count)
    kv_at = HQD + HD * cross_id + KVD * core_id
    strip_local = low(
        jnp.concatenate(
            [
                lax.dynamic_slice_in_dim(w_attend, strip_q * grp, strip_q, 1),
                lax.dynamic_slice_in_dim(w_attend, kv_at, HD, 1),
            ],
            axis=1,
        )
    )
    small_count = small_params.shape[0]
    small_send = jnp.concatenate([low(small_params), low(segment_ids.reshape(token_count))])
    strip_wide = strip_q + HD
    small_send = jnp.pad(small_send, (0, -small_send.shape[0] % (16 * strip_wide)))
    strip_local = jnp.concatenate([strip_local, small_send.reshape(-1, strip_wide)])
    ring = ring_order(blk_count)
    strip_ring = gather_ring(strip_local)
    small_ring = strip_ring[:, weight_rows:].reshape(blk_count, -1)[:, small_count : small_count + token_count]
    small_all = jnp.stack([small_ring[ring.index(b)] for b in range(blk_count)])
    digits = low(jnp.stack([positions // 64, positions % 64], axis=1))
    digits = jnp.pad(digits, ((0, 0), (0, HD - 2)))
    token_send = jnp.concatenate([flat_low, digits], axis=1)
    token_cross = swap_cross(token_send)
    dy_over = swap_blk(dy_low, team)
    dy_cross = swap_cross(after(dy_low, token_cross))

    def place(values, other, done, bit, lead=0):
        mine = blk_bit(bit)
        axis = lead + sum(1 for d in done if d > bit)
        return jnp.stack(
            [jnp.where(mine, other, values), jnp.where(mine, values, other)], axis=axis
        )

    mine_team = blk_bit(team)
    (low_first, size_first), (low_second, size_second) = halves_of(quarter)

    def team_pair(mine, got):
        return jnp.stack(
            [jnp.where(mine_team, got, mine), jnp.where(mine_team, mine, got)], axis=1
        )

    out_local = low(lax.dynamic_slice_in_dim(w_out, strip_q * grp, strip_q, 1))
    out_ring = gather_ring(after(out_local, strip_ring))
    picked_a, picked_b = pick_columns(ids, w_gate, w_up, blk_count)
    got_a = swap_blk(picked_a[1], team)
    down_here = low(lax.dynamic_slice_in_dim(w_down, quarter * grp, quarter, 0))
    down_got = swap_blk(after(down_here, strip_ring), bits[0])
    pair_a = team_pair(picked_a[0], got_a)
    token_core = swap_core(jnp.stack([token_send, token_cross]))
    token_core = after(token_core, (pair_a, dy_cross, dy_over))
    freqs = ROPE_BASE ** (-2.0 * jnp.arange(HD // 2, dtype=jnp.float32) / HD)
    freqs = jnp.concatenate([freqs, freqs])[None]
    mixed_own, mixed_core, mixed_far, near_one, strip, vector = mix(
        ids, token_send, token_cross, token_core, strip_ring, freqs, blk_count, weight_rows, small_count
    )
    dy_first = swap_blk(after(dy_cross, mixed_own)[:half], team)
    dy_second = swap_cross(after(dy_over, mixed_own)[half:])
    vector = vector[0]
    gain_one = vector[:D]
    gain_two = vector[D : 2 * D]
    seg_all = small_all.astype(jnp.int32)
    seg_all = seg_all.reshape(blk_count, rows_here, block_len)
    seg_key = jnp.broadcast_to(
        seg_all.transpose(1, 0, 2).reshape(rows_here, seq_len)[:, :, None], (rows_here, seq_len, HD)
    )
    seg_query = jnp.broadcast_to(segment_ids[:, None, :], (rows_here, 8, block_len))
    first_blk = jnp.sum((seg_all[:, :, -1] < segment_ids[None, :, 0]).astype(jnp.int32), axis=0)
    attend_ids = jnp.concatenate([blk[None], first_blk])

    mixed_cross = swap_cross(mixed_far)
    mixed_core = swap_core(jnp.stack([mixed_core, mixed_cross[1]]))
    query, packed_kv = pack(ids, mixed_own, mixed_cross, mixed_core)
    key_value = packed_kv.reshape(rows_here, block_len, 2 * KVD)
    kv_all = gather_ring(key_value)
    dy_chip = jnp.concatenate([dy_low, dy_cross, dy_over, dy_first, dy_second])
    dy_team = jnp.concatenate([dy_chip, swap_core(dy_chip)])

    teams = [
        [g * blk_count + (i | t) for g in range(4) for t in (0, team)]
        for i in range(blk_count)
        if not i & team
    ]
    order = jnp.stack(
        [
            (grp ^ (2 * (i & 1) + (i >> 2))) * 2 + (in_team ^ ((i >> 1) & 1))
            for i in range(8)
        ]
    )

    peers = [[i for i in range(blk_count) if (i & team) == t] for t in (0, team)]

    def lows_of(values, done, lead=0, anchor=None):
        for bit in lows:
            got = swap_blk(values, bit)
            if anchor is not None:
                got = after(got, anchor)
            values = place(values, got, done, bit, lead)
            done = done + [bit]
        return values

    pair_a_got = swap_blk(after(pair_a, mixed_own), bits[0])
    down_here = place(down_here, after(down_got, mixed_own), [], bits[0])
    down_here = lows_of(down_here, [bits[0]]).reshape(2 * blk_count // 4, quarter, D)
    got_b = swap_blk(after(picked_b[1], mixed_own), team)
    pair_a_got, got_b = after((pair_a_got, got_b), kv_all)
    kv_all = after(kv_all, (pair_a_got, got_b, down_here))
    pair_a = place(pair_a, pair_a_got, [team], bits[0], 1)
    gate_up_a = lows_of(pair_a, [bits[0], team], 1).reshape(2, D, -1)
    pair_b = team_pair(picked_b[0], got_b)
    pair_b_got = swap_blk(pair_b, bits[0])
    down_a = down_here[:, :size_first].reshape(widths[0], D)
    down_b = down_here[:, size_first:].reshape(widths[1], D)

    out_ring = after(out_ring, packed_kv)
    out_strip = jnp.concatenate([out_ring[ring.index(b)] for b in range(blk_count)])
    out_cross = swap_cross(out_strip)
    out_core = swap_core(jnp.stack([out_strip, after(out_cross, kv_all)]))
    out_full = jnp.concatenate(by_place([out_strip, out_core[0], out_cross, out_core[1]]), axis=1)

    att_in, lse = attend(attend_ids, query, kv_all, seg_key, seg_query, block_len)

    flat = wide(flat_low)
    resid = flat + jnp.dot(att_in, out_full, preferred_element_type=jnp.float32)
    h_two = low(norm_apply(resid, gain_two))
    h_team = lax.all_gather(h_two, ("grp", "blk"), axis=0, tiled=True, axis_index_groups=teams)
    pair_b_got = after(pair_b_got, (h_two, gate_up_a))
    pair_b = place(pair_b, pair_b_got, [team], bits[0], 1)
    h_team = after(h_team, (gate_up_a, pair_b, dy_team))
    hidden_a, d_gate_a, d_up_a, part_a = middle(order, h_team, dy_team, gate_up_a, down_a)
    gate_up_b = lows_of(pair_b, [bits[0], team], 1, hidden_a).reshape(2, D, -1)
    down_grad_a = down_grad(hidden_a, dy_team)
    down_share_a = lax.psum_scatter(
        down_grad_a, "blk", scatter_dimension=0, axis_index_groups=peers, tiled=True
    )
    column_grad_a = two_grads(h_team, d_gate_a, d_up_a)

    def part_sent(values, axis, bit):
        mine = blk_bit(bit).astype(jnp.int32)
        keep = lax.dynamic_index_in_dim(values, mine, axis, keepdims=False)
        send = lax.dynamic_index_in_dim(values, 1 - mine, axis, keepdims=False)
        return keep, swap_blk(send, bit)

    def part_sum(keep, got):
        return low(wide(keep) + wide(got))

    def columns_first(grad):
        grad = grad.reshape((2, 2, 2) + low_shape + (weight_rows, -1))
        return part_sent(grad, 2 + len(lows), lows[-1])

    def columns_mid(keep, got):
        values = part_sum(keep, got)
        for i in range(len(lows) - 2, -1, -1):
            values = part_sum(*part_sent(values, 3 + i, lows[i]))
        return values

    def columns_third(keep, got):
        values = part_sum(keep, got)
        mine = lax.dynamic_index_in_dim(values, in_team, 1, keepdims=False)
        send = lax.dynamic_index_in_dim(values, 1 - in_team, 1, keepdims=False)
        return values, (mine, swap_blk(send, team))

    def rows_second(keep, got):
        values = part_sum(keep, got)
        for i in range(len(lows) - 2, -1, -1):
            values = part_sum(*part_sent(values, 1 + i, lows[i]))
        return part_sent(values, 0, bits[0])

    def columns_last(mine, got):
        return jnp.stack(
            [jnp.where(mine_team, got, mine), jnp.where(mine_team, mine, got)], axis=1
        )

    first_a = columns_first(column_grad_a)
    hidden_b, d_gate_b, d_up_b, d_htwo_part = middle(
        order, after(h_team, (column_grad_a, down_grad_a)), dy_team, gate_up_b, down_b, part_a
    )

    def chip_sum(values, came):
        return low(wide(values[:chip_rows]) + wide(came))

    def scatter_far(chip):
        far = chip[3 * token_count :]
        return swap_blk(far[:half], team), swap_cross(far[half:])

    def scatter_near(chip, first, second):
        cross, over = (chip[token_count * i : token_count * (i + 1)] for i in (1, 2))
        cross = jnp.concatenate([low(wide(cross[:half]) + wide(first)), cross[half:]])
        over = jnp.concatenate([over[:half], low(wide(over[half:]) + wide(second))])
        return swap_cross(cross), swap_blk(over, team)

    near_att_cross = swap_cross(after(att_in, hidden_a))
    d_htwo_part = after(d_htwo_part, (first_a[1], down_share_a, near_att_cross))
    d_came = swap_core(d_htwo_part[chip_rows:])
    down_grad_b = down_grad(hidden_b, dy_team)
    rows_b = part_sent(
        down_grad_b.reshape((2,) + low_shape + (size_second, D)), len(lows), lows[-1]
    )
    d_chip = chip_sum(d_htwo_part, after(d_came, down_grad_b))
    d_far = scatter_far(d_chip)
    column_grad_b = two_grads(h_team, *after((d_gate_b, d_up_b), d_chip))
    first_b = columns_first(column_grad_b)
    d_far = after(d_far, column_grad_b)
    d_cross, d_over = scatter_near(d_chip, *d_far)
    out_part = down(*after((hidden_a, hidden_b), d_far), down_a, down_b, token_count)
    out_came = swap_core(out_part[chip_rows:])
    mid_a = columns_mid(*after(first_a, d_far))
    second_a = part_sent(mid_a, 1, bits[0])
    d_cross, d_over = after((d_cross, d_over), out_part)
    d_htwo = wide(d_chip[:token_count]) + wide(d_cross) + wide(d_over)

    norm_value_two, norm_back_two = jax.vjp(norm_apply, resid, gain_two)
    d_resid_norm, grad_gain_two = norm_back_two(d_htwo)
    d_resid = wide(dy_low) + d_resid_norm
    d_att = low(d_resid)
    rows_b = rows_second(*after(rows_b, d_att))

    d_attended = low(right_transposed(d_att, out_full))
    own_angles = angles_of(positions)
    cosine, sine = jnp.cos(own_angles), jnp.sin(own_angles)
    d_query, dkv = attend_back(
        attend_ids,
        query,
        kv_all,
        seg_key,
        seg_query,
        att_in,
        d_attended,
        lse,
        jnp.concatenate([cosine, cosine], axis=1),
        jnp.concatenate([sine, sine], axis=1),
        block_len,
    )
    dkv = lax.psum_scatter(
        dkv.reshape(blk_count * token_count, 2 * KVD),
        ("grp", "blk"),
        scatter_dimension=0,
        axis_index_groups=ring_groups(blk_count),
        tiled=True,
    )
    down_share_b = part_sum(*after(rows_b, d_query))
    sum_a, third_a = columns_third(*after(second_a, d_query))

    def to_strips(parts):
        return jnp.concatenate(exchange_near(by_place(parts)))

    near_dq = to_strips([d_query[:, strip_q * k : strip_q * (k + 1)] for k in range(4)])
    block_shape = (2,) * len(bits) + (weight_rows, -1)
    query_grad = low(left_product(near_one, near_dq)).reshape(block_shape)
    steps_query = part_sent(query_grad, len(bits) - 1, bits[-1])
    near_a = gather_near_stacked(columns_last(*after(third_a, d_query)))
    dkv = after(dkv, (query_grad, down_share_b))
    own_part, core_part, far_part, bias_kv = turn_dkv(
        ids, dkv, jnp.concatenate([cosine, cosine], axis=1), jnp.concatenate([sine, sine], axis=1)
    )
    bias_q = jnp.sum(wide(d_query), axis=0)
    d_key = own_part
    cross_part = swap_cross(far_part)
    core_part = swap_core(jnp.stack([core_part, cross_part[1]]))
    kv_grad, hone_here, hone_there = make_kv_grad(
        blk_count,
        weight_rows,
        small_count,
        own_part,
        cross_part,
        core_part,
        near_dq,
        near_one,
        token_send,
        token_cross,
        token_core,
        strip,
        grad_gain_two[None],
        bias_q[None],
        bias_kv,
    )
    vector_rows = -(-small_count // HD)
    kv_grad = kv_grad.reshape((2,) * len(bits) + kv_grad.shape[1:])
    steps_kv = part_sent(kv_grad, len(bits) - 1, bits[-1])
    second_b = part_sent(columns_mid(*after(first_b, d_query)), 1, bits[0])
    share_down = after(jnp.concatenate([down_share_a, down_share_b]), dkv)
    grad_down = lax.all_gather(share_down, "grp", axis=0, tiled=True)
    for i in range(len(bits) - 2, -1, -1):
        steps_query = part_sent(part_sum(*after(steps_query, d_key)), i, bits[i])
        kv_sum = part_sum(*steps_kv)
        kv_grad = kv_sum
        steps_kv = part_sent(kv_sum, i, bits[i])
    share_kv_all = wide(steps_kv[0]) + wide(after(steps_kv[1], near_a))
    share_kv = low(share_kv_all[:weight_rows])
    vector_part = share_kv_all[weight_rows : weight_rows + vector_rows]
    sum_b, third_b = columns_third(*after(second_b, kv_grad))
    share_query = part_sum(*after(steps_query, kv_grad))
    near_att = swap_core(jnp.stack([att_in, near_att_cross]))
    near_att = jnp.concatenate([att_in, near_att[0], near_att_cross, near_att[1]])
    near_datt = to_strips([d_att[:, strip_q * k : strip_q * (k + 1)] for k in range(4)])
    out_grad = low(left_product(near_att, after(near_datt, d_attended))).reshape(block_shape)
    steps_out = part_sent(out_grad, len(bits) - 1, bits[-1])
    anchors = [near_dq, near_dq]
    for i in range(len(bits) - 2, -1, -1):
        anchor = anchors[min(len(bits) - 2 - i, 1)]
        steps_out = part_sent(part_sum(*after(steps_out, anchor)), i, bits[i])
    share_out = part_sum(*after(steps_out, own_part))

    own_b = columns_last(*after(third_b, share_kv_all))
    cross_b = swap_cross(own_b)
    near_b = jnp.stack([own_b, cross_b])
    near_b = jnp.concatenate([near_b, swap_core(near_b)])
    grad_out = jnp.concatenate(gather_grp(share_out), axis=1)
    query_parts = gather_grp(share_query)
    key_parts = gather_grp(share_kv)
    grad_attend = jnp.concatenate(query_parts + [key_parts[k] for k in (0, 2, 1, 3)], axis=1)

    other = wide(swap_core(hone_there))
    d_hone = wide(hone_here[:token_count]) + other[:token_count]
    d_hone_cross = swap_cross(low(wide(hone_here[token_count:]) + other[token_count:]))
    square_sum = square_total(
        [
            wide(s)
            for s in (share_query, share_kv, share_out, sum_a, sum_b, share_down)
        ]
    )
    packed = jnp.concatenate([vector_part, jnp.full((8, HD), square_sum)])
    packed = packed + swap_cross(packed)
    packed = packed + swap_core(packed)
    share_vector = packed[:vector_rows].reshape(-1)[:small_count]
    square_sum = packed[vector_rows:] + jnp.sum(share_vector * share_vector)
    for bit in bits:
        square_sum = square_sum + swap_blk(square_sum, bit)
    grad_norm = jnp.sqrt(square_sum[0, 0])
    factor = jnp.minimum(1.0, CLIP_NORM / (grad_norm + 1e-06))
    out_chip = chip_sum(out_part, after(out_came, kv_grad))
    out_far = scatter_far(out_chip)
    factor = after(factor, (out_chip, cross_b))

    new_first_gate, new_second_gate, new_gate = adam_columns(
        0, ids, factor[None], near_a, near_b, w_gate, first_gate, second_gate, blk_count, RATE_GATE, WEIGHT_DECAY
    )
    new_first_up, new_second_up, new_up = adam_columns(
        1, ids, factor[None], near_a, near_b, w_up, first_up, second_up, blk_count, RATE_GATE, WEIGHT_DECAY
    )
    norm_value_one, norm_back_one = jax.vjp(norm_apply, flat, gain_one)
    d_hone = after(d_hone + wide(after(d_hone_cross, new_gate)), new_gate)
    d_flat_norm, unused_gain = norm_back_one(d_hone)
    grad_tokens = low(d_resid + d_flat_norm)

    new_first_attend, new_second_attend, new_attend = adam_step(
        w_attend, factor * wide(grad_attend), first_attend, second_attend, RATE_ATTEND, WEIGHT_DECAY
    )
    new_first_out, new_second_out, new_out = adam_step(
        w_out, factor * wide(grad_out), first_out, second_out, RATE_OUT, WEIGHT_DECAY
    )
    new_first_down, new_second_down, new_down = adam_step(
        w_down, factor * wide(grad_down), first_down, second_down, RATE_DOWN, WEIGHT_DECAY
    )
    new_first_small, new_second_small, new_small = adam_step(
        small_params, factor * share_vector, first_small, second_small, RATE_VECTOR, 0.0
    )

    out_far = after(out_far, new_down)
    out_near = after(scatter_near(out_chip, *out_far), (new_gate, new_up))
    out_tokens = low(resid + wide(out_chip[:token_count]) + wide(out_near[0]) + wide(out_near[1]))
    return (
        out_tokens.reshape(rows_here, block_len, D),
        grad_tokens.reshape(rows_here, block_len, D),
        grad_norm,
        new_first_attend,
        new_second_attend,
        new_attend,
        new_first_out,
        new_second_out,
        new_out,
        new_first_gate,
        new_second_gate,
        new_gate,
        new_first_up,
        new_second_up,
        new_up,
        new_first_down,
        new_second_down,
        new_down,
        new_first_small,
        new_second_small,
        new_small,
    )


def solution(mesh):
    placed = (
        P("grp", "blk", None),
        P("grp", "blk", None),
        P("grp", "blk"),
        P("grp", "blk"),
        P("blk", None),
        P("blk", None),
        P("blk", None),
        P("blk", None),
        P("blk", None),
        P("blk"),
        P("blk", None),
        P("blk", None),
        P("blk", None),
        P("blk", None),
        P("blk", None),
        P("blk"),
        P("blk", None),
        P("blk", None),
        P("blk", None),
        P("blk", None),
        P("blk", None),
        P("blk"),
    )
    return jax.shard_map(
        on_device,
        mesh=mesh,
        in_specs=placed,
        out_specs=(
            P("grp", "blk", None),
            P("grp", "blk", None),
            P(),
            P("blk", None),
            P("blk", None),
            P("blk", None),
            P("blk", None),
            P("blk", None),
            P("blk", None),
            P("blk", None),
            P("blk", None),
            P("blk", None),
            P("blk", None),
            P("blk", None),
            P("blk", None),
            P("blk", None),
            P("blk", None),
            P("blk", None),
            P("blk"),
            P("blk"),
            P("blk"),
        ),
        check_vma=False,
    )
```

```python
import functools

import jax
import jax.numpy as jnp
from jax import lax
from jax.experimental import pallas as pl
from jax.experimental.pallas import tpu as pltpu
from jax.sharding import PartitionSpec as P

D = 1536
FF = 8960
H = 12
KVH = 2
HD = 128
STEP = 10
HQD = 1536
KVD = 256


NORM_EPS = 1e-06
ROPE_BASE = 10000.0
CLIP_NORM = 1.0
BETA_FIRST = 0.9
BETA_SECOND = 0.95
ADAM_EPS = 1e-08
WEIGHT_DECAY = 0.1
RATE_ATTEND = 0.06
RATE_OUT = 0.5
RATE_GATE = 0.06
RATE_DOWN = 0.03
RATE_VECTOR = 0.5
NEG_LARGE = -1e30
LOG2E = 1.4426950408889634
VMEM = 48 * 1024 * 1024
SMALL_COST = pl.CostEstimate(flops=1000, bytes_accessed=1000, transcendentals=0)


def norm_apply(values, gain):
    return values * lax.rsqrt(jnp.mean(values * values, axis=-1, keepdims=True) + NORM_EPS) * gain


def swish_product(gate, up_proj):
    return jax.nn.silu(gate) * up_proj


def left_product(left_side, right_side):
    return lax.dot_general(
        left_side, right_side, (((0,), (0,)), ((), ())), preferred_element_type=jnp.float32
    )


def right_transposed(left_side, right_side):
    return lax.dot_general(
        left_side, right_side, (((1,), (1,)), ((), ())), preferred_element_type=jnp.float32
    )


def square_total(arrays):
    return sum((jnp.sum(member * member) for member in arrays))


def adam_step(weight, grad, first, second, rate, decay):
    first_new = BETA_FIRST * first + (1.0 - BETA_FIRST) * grad
    second_new = BETA_SECOND * second + (1.0 - BETA_SECOND) * grad * grad
    first_hat = first_new / (1.0 - BETA_FIRST**STEP)
    second_hat = second_new / (1.0 - BETA_SECOND**STEP)
    weight_new = weight - rate * (first_hat / (jnp.sqrt(second_hat) + ADAM_EPS) + decay * weight)
    return (first_new, second_new, weight_new)


def ring_order(count):
    return list(range(0, count, 2)) + list(range(count - 1, 0, -2))


def halves_of(quarter):
    first = quarter * 16 // 35
    return ((0, first), (first, quarter - first))


def pick_body(blk_count, ids, gate_ref, up_ref, *out_refs):
    quarter = FF // blk_count // 4
    per = blk_count // 4
    for k in range(4):

        @pl.when(ids[0] == k)
        def _(k=k):
            for (at, size), out_ref in zip(halves_of(quarter), out_refs):
                for which, src in enumerate((gate_ref, up_ref)):
                    for bit in range(2):
                        parts = []
                        for high in range(2):
                            for small in range(per):
                                begin = (((high * 2 + bit) * per + small) * 4 + k) * quarter + at
                                parts.append(src[:, begin : begin + size])
                        out_ref[ids[1] ^ bit, which] = jnp.concatenate(parts, axis=1).astype(
                            jnp.bfloat16
                        )


def pick_columns(ids, gate, up, blk_count):
    rows = gate.shape[0]
    step = 48 if rows % 48 == 0 else rows
    widths = [size * blk_count // 2 for at, size in halves_of(FF // blk_count // 4)]
    spec = pl.BlockSpec((step, FF), lambda i, ids: (i, 0))
    return pl.pallas_call(
        functools.partial(pick_body, blk_count),
        grid_spec=pltpu.PrefetchScalarGridSpec(
            num_scalar_prefetch=1,
            grid=(rows // step,),
            in_specs=[spec, spec],
            out_specs=[pl.BlockSpec((2, 2, step, w), lambda i, ids: (0, 0, i, 0)) for w in widths],
        ),
        out_shape=[jax.ShapeDtypeStruct((2, 2, rows, w), jnp.bfloat16) for w in widths],
        compiler_params=pltpu.CompilerParams(vmem_limit_bytes=VMEM),
        cost_estimate=SMALL_COST,
        name="pick_columns",
    )(ids, gate, up)


def near_at(away):
    return (away & 1) * 2 + (away >> 1)


def adam_body(blk_count, rate, decay, ids, factor_ref, first_ref, second_ref, w_ref, m_ref, v_ref, m_out, v_out, w_out):
    per = blk_count // 4
    sizes = [size for at, size in halves_of(FF // blk_count // 4)]
    grads = [
        [[ref[near_at(ids[0] ^ k), bit] for bit in range(2)] for k in range(4)]
        for ref in (first_ref, second_ref)
    ]
    parts = []
    for high in range(2):
        for bit in range(2):
            for small in range(per):
                place = high * per + small
                for k in range(4):
                    for part, size in zip(grads, sizes):
                        parts.append(part[k][bit][:, place * size : (place + 1) * size])
    grad = jnp.concatenate(parts, axis=1).astype(jnp.float32) * factor_ref[0]
    m, v, w = adam_step(w_ref[...], grad, m_ref[...], v_ref[...], rate, decay)
    m_out[...] = m
    v_out[...] = v
    w_out[...] = w


def adam_columns(which, ids, factor, first, second, w, m, v, blk_count, rate, decay):
    rows = w.shape[0]
    step = 32 if rows % 32 == 0 else rows
    spec = pl.BlockSpec((step, FF), lambda i, ids: (i, 0))
    shape = jax.ShapeDtypeStruct((rows, FF), jnp.float32)
    grads = [
        pl.BlockSpec((4, None, 2, step, g.shape[-1]), lambda i, ids: (0, which, 0, i, 0))
        for g in (first, second)
    ]
    return pl.pallas_call(
        functools.partial(adam_body, blk_count, rate, decay),
        grid_spec=pltpu.PrefetchScalarGridSpec(
            num_scalar_prefetch=1,
            grid=(rows // step,),
            in_specs=[pl.BlockSpec(memory_space=pltpu.SMEM)] + grads + [spec, spec, spec],
            out_specs=[spec, spec, spec],
        ),
        out_shape=[shape] * 3,
        compiler_params=pltpu.CompilerParams(vmem_limit_bytes=VMEM),
        cost_estimate=SMALL_COST,
        name="adam_columns",
    )(ids, factor, first, second, w, m, v)


def nt(a, b, **kw):
    return lax.dot_general(a, b, (((1,), (1,)), ((), ())), preferred_element_type=jnp.float32, **kw)

def tn(a, b, **kw):
    return lax.dot_general(a, b, (((0,), (0,)), ((), ())), preferred_element_type=jnp.float32, **kw)

def stack_heads(ref, kvh, group):
    return jnp.concatenate([ref[:, HD * (kvh * group + i): HD * (kvh * group + i + 1)] for i in range(group)], axis=0)

def hidden_from(seg_key_ref, seg_query_ref, first, chunk, block_len, blk):
    key = first + lax.broadcasted_iota(jnp.int32, (chunk, block_len), 0)
    query = blk * block_len + lax.broadcasted_iota(jnp.int32, (chunk, block_len), 1)
    seg_key = seg_key_ref[pl.ds(first, chunk), :]
    counts = jnp.logical_and(key <= query, seg_key == seg_query_ref[0:1, :])
    return jnp.where(counts, 0.0, NEG_LARGE)

def ring_pair(ref, c, at):
    return jnp.concatenate(
        [ref[c, :, at : at + HD], ref[ref.shape[0] - 1 - c, :, at : at + HD]], axis=0
    )


def attend_body(chunk, ids, q_ref, k_ref, v_ref, seg_key_ref, seg_query_ref, o_ref, lse_ref, m_s, l_s, acc_s):
    block_len = q_ref.shape[0]
    group = H // KVH
    row = pl.program_id(0)
    per = chunk // block_len
    scale = HD ** (-0.5) * LOG2E
    start = ids[1 + row] // per
    stop = ids[0] // per + 1
    for kvh in range(KVH):
        q = stack_heads(q_ref, kvh, group)
        m_s[...] = jnp.full_like(m_s, NEG_LARGE)
        l_s[...] = jnp.zeros_like(l_s)
        acc_s[...] = jnp.zeros_like(acc_s)

        def step(c, carry):
            keys = ring_pair(k_ref, c, HD * kvh)
            vals = ring_pair(v_ref, c, HD * kvh)
            bias = hidden_from(seg_key_ref, seg_query_ref, c * chunk, chunk, block_len, ids[0])
            s = nt(keys, q) * scale + jnp.concatenate([bias] * group, axis=1)
            old = m_s[0:1, :]
            new = jnp.maximum(old, jnp.max(s, axis=0, keepdims=True))
            p = jnp.exp2(s - new)
            fade = jnp.exp2(old - new)
            l_s[0:1, :] = l_s[0:1, :] * fade + jnp.sum(p, axis=0, keepdims=True)
            acc_s[...] = acc_s[...] * fade + tn(vals, p.astype(jnp.bfloat16))
            m_s[0:1, :] = new
            return carry

        lax.fori_loop(start, stop, step, 0)
        total = l_s[0:1, :]
        out = (acc_s[...] * (1.0 / total)).T
        for i in range(group):
            o_ref[:, HD * (kvh * group + i): HD * (kvh * group + i + 1)] = out[block_len * i: block_len * (i + 1), :].astype(jnp.bfloat16)
        lse_ref[kvh] = jnp.broadcast_to(m_s[0:1, :] + jnp.log2(total), (8, group * block_len))

def attend(ids, q, kv, seg_key, seg_query, block_len):
    blk_count, rows = kv.shape[:2]
    group = H // KVH
    chunk = 2 * block_len
    many = group * block_len
    return pl.pallas_call(
        functools.partial(attend_body, chunk),
        grid_spec=pltpu.PrefetchScalarGridSpec(
            num_scalar_prefetch=1, grid=(rows,),
            in_specs=[
                pl.BlockSpec((block_len, HQD), lambda r, ids: (r, 0)),
                pl.BlockSpec((blk_count, None, block_len, KVD), lambda r, ids: (0, r, 0, 0)),
                pl.BlockSpec((blk_count, None, block_len, KVD), lambda r, ids: (0, r, 0, 1)),
                pl.BlockSpec((None, blk_count * block_len, HD), lambda r, ids: (r, 0, 0)),
                pl.BlockSpec((None, 8, block_len), lambda r, ids: (r, 0, 0)),
            ],
            out_specs=[
                pl.BlockSpec((block_len, HQD), lambda r, ids: (r, 0)),
                pl.BlockSpec((None, KVH, 8, many), lambda r, ids: (r, 0, 0, 0)),
            ],
            scratch_shapes=[pltpu.VMEM((8, many), jnp.float32), pltpu.VMEM((8, many), jnp.float32), pltpu.VMEM((HD, many), jnp.float32)]),
        out_shape=[
            jax.ShapeDtypeStruct((rows * block_len, HQD), jnp.bfloat16),
            jax.ShapeDtypeStruct((rows, KVH, 8, many), jnp.float32),
        ],
        compiler_params=pltpu.CompilerParams(vmem_limit_bytes=VMEM),
        cost_estimate=SMALL_COST,
        name="attend",
    )(ids, q, kv, kv, seg_key, seg_query)

def turn_back(u, cosine, sine):
    lane = lax.broadcasted_iota(jnp.int32, u.shape, 1)
    other = pltpu.roll(u, HD // 2, 1)
    return u * cosine + jnp.where(lane < HD // 2, other, -other) * sine

def attend_back_body(chunk, ids, q_ref, k_ref, v_ref, seg_key_ref, seg_query_ref, o_ref, do_ref, lse_ref, cos_ref, sin_ref, dq_ref, dkv_ref, dq_s):
    block_len = q_ref.shape[0]
    group = H // KVH
    row = pl.program_id(0)
    per = chunk // block_len
    plain = HD ** (-0.5)
    scale = plain * LOG2E
    start = ids[1 + row] // per
    stop = ids[0] // per + 1
    dkv_ref[...] = jnp.zeros_like(dkv_ref)
    for kvh in range(KVH):
        q = stack_heads(q_ref, kvh, group)
        do = stack_heads(do_ref, kvh, group)
        o = stack_heads(o_ref, kvh, group)
        both = do.astype(jnp.float32) * o.astype(jnp.float32)
        delta = nt(jnp.ones((8, HD), jnp.float32), both, precision=lax.Precision.HIGHEST)[0:1, :]
        lse = lse_ref[kvh][0:1, :]
        dq_s[...] = jnp.zeros_like(dq_s)

        def step(c, carry):
            keys = ring_pair(k_ref, c, HD * kvh)
            vals = ring_pair(v_ref, c, HD * kvh)
            bias = hidden_from(seg_key_ref, seg_query_ref, c * chunk, chunk, block_len, ids[0])
            s = nt(keys, q) * scale + jnp.concatenate([bias] * group, axis=1)
            p = jnp.exp2(s - lse)
            dp = nt(vals, do)
            ds = (p * (dp - delta)).astype(jnp.bfloat16)
            dk = jnp.dot(ds, q, preferred_element_type=jnp.float32) * plain
            dv = jnp.dot(p.astype(jnp.bfloat16), do, preferred_element_type=jnp.float32)
            for at, part in ((HD * kvh, dk.astype(jnp.bfloat16)), (KVD + HD * kvh, dv.astype(jnp.bfloat16))):
                dkv_ref[c, :, at : at + HD] = part[:block_len]
                dkv_ref[dkv_ref.shape[0] - 1 - c, :, at : at + HD] = part[block_len:]
            dq_s[...] += tn(ds, keys)
            return carry

        lax.fori_loop(start, stop, step, 0)
        cosine, sine = cos_ref[...], sin_ref[...]
        for i in range(group):
            u = dq_s[block_len * i: block_len * (i + 1), :] * plain
            at = HD * (kvh * group + i)
            dq_ref[:, at: at + HD] = turn_back(u, cosine, sine).astype(jnp.bfloat16)

def attend_back(ids, q, kv, seg_key, seg_query, o, do, lse, cosine, sine, block_len):
    blk_count, rows = kv.shape[:2]
    group = H // KVH
    chunk = 2 * block_len
    many = group * block_len
    per_row = pl.BlockSpec((block_len, HQD), lambda r, ids: (r, 0))
    turn = pl.BlockSpec((block_len, HD), lambda r, ids: (r, 0))
    return pl.pallas_call(
        functools.partial(attend_back_body, chunk),
        grid_spec=pltpu.PrefetchScalarGridSpec(
            num_scalar_prefetch=1, grid=(rows,),
            in_specs=[
                per_row,
                pl.BlockSpec((blk_count, None, block_len, KVD), lambda r, ids: (0, r, 0, 0)),
                pl.BlockSpec((blk_count, None, block_len, KVD), lambda r, ids: (0, r, 0, 1)),
                pl.BlockSpec((None, blk_count * block_len, HD), lambda r, ids: (r, 0, 0)),
                pl.BlockSpec((None, 8, block_len), lambda r, ids: (r, 0, 0)),
                per_row, per_row,
                pl.BlockSpec((None, KVH, 8, many), lambda r, ids: (r, 0, 0, 0)),
                turn, turn,
            ],
            out_specs=[per_row, pl.BlockSpec((blk_count, None, block_len, 2 * KVD), lambda r, ids: (0, r, 0, 0))],
            scratch_shapes=[pltpu.VMEM((many, HD), jnp.float32)]),
        out_shape=[
            jax.ShapeDtypeStruct((rows * block_len, HQD), jnp.bfloat16),
            jax.ShapeDtypeStruct((blk_count, rows, block_len, 2 * KVD), jnp.bfloat16),
        ],
        compiler_params=pltpu.CompilerParams(vmem_limit_bytes=VMEM),
        cost_estimate=SMALL_COST,
        name="attend_back",
    )(ids, q, kv, kv, seg_key, seg_query, o, do, lse, cosine, sine)

def nn(a, b):
    return jnp.dot(a, b, preferred_element_type=jnp.float32)


def middle_body(add, order, h_ref, dy_ref, wg_ref, wu_ref, wd_ref, *refs):
    prev_ref = refs[0] if add else None
    hid_ref, dg_ref, du_ref, dh_ref = refs[-4:]
    h = h_ref[...]
    gate = nn(h, wg_ref[...])
    up = nn(h, wu_ref[...])
    sig = 1.0 / (1.0 + jnp.exp(-gate))
    silu = gate * sig
    hid_ref[...] = (silu * up).astype(jnp.bfloat16)
    dhid = nt(dy_ref[...], wd_ref[...])
    dg = (dhid * up * sig * (1.0 + gate * (1.0 - sig))).astype(jnp.bfloat16)
    du = (dhid * silu).astype(jnp.bfloat16)
    dg_ref[...] = dg
    du_ref[...] = du
    dh = nt(dg, wg_ref[...]) + nt(du, wu_ref[...])
    if add:
        dh = dh + prev_ref[...].astype(jnp.float32)
    dh_ref[...] = dh.astype(jnp.bfloat16)


def middle(order, h, dy, gate_up, wd, prev=None):
    count = h.shape[0]
    step = count // order.shape[0]
    wide_here = wd.shape[0]
    row = pl.BlockSpec((step, D), lambda i, order: (i, 0))
    placed = pl.BlockSpec((step, D), lambda i, order: (order[i], 0))
    part = pl.BlockSpec((step, wide_here), lambda i, order: (i, 0))
    part_placed = pl.BlockSpec((step, wide_here), lambda i, order: (order[i], 0))
    once = pl.Buffered(1)
    extra = [] if prev is None else [prev]
    return pl.pallas_call(
        functools.partial(middle_body, prev is not None),
        grid_spec=pltpu.PrefetchScalarGridSpec(
            num_scalar_prefetch=1,
            grid=(count // step,),
            in_specs=[
                placed,
                row,
                pl.BlockSpec((None, D, wide_here), lambda i, order: (0, 0, 0), pipeline_mode=once),
                pl.BlockSpec((None, D, wide_here), lambda i, order: (1, 0, 0), pipeline_mode=once),
                pl.BlockSpec((wide_here, D), lambda i, order: (0, 0), pipeline_mode=once),
            ]
            + [row] * len(extra),
            out_specs=[part, part_placed, part_placed, row],
        ),
        out_shape=[jax.ShapeDtypeStruct((count, wide_here), jnp.bfloat16)] * 3
        + [jax.ShapeDtypeStruct((count, D), jnp.bfloat16)],
        compiler_params=pltpu.CompilerParams(vmem_limit_bytes=VMEM),
        cost_estimate=SMALL_COST,
        name="middle",
    )(order, h, dy, gate_up, gate_up, wd, *extra)


def two_grads_body(h_ref, a_ref, b_ref, out_ref):
    h = h_ref[...]
    out_ref[0] = tn(h, a_ref[...]).astype(jnp.bfloat16)
    out_ref[1] = tn(h, b_ref[...]).astype(jnp.bfloat16)


def two_grads(h, a, b, step=256):
    count = h.shape[0]
    wide_here = a.shape[1]
    whole = pl.BlockSpec(a.shape, lambda i: (0, 0), pipeline_mode=pl.Buffered(1))
    return pl.pallas_call(
        two_grads_body,
        grid=(D // step,),
        in_specs=[pl.BlockSpec((count, step), lambda i: (0, i)), whole, whole],
        out_specs=pl.BlockSpec((2, step, wide_here), lambda i: (0, i, 0)),
        out_shape=jax.ShapeDtypeStruct((2, D, wide_here), jnp.bfloat16),
        compiler_params=pltpu.CompilerParams(vmem_limit_bytes=VMEM),
        cost_estimate=SMALL_COST,
        name="two_grads",
    )(h, a, b)


def down_grad_body(hid_ref, dy_ref, g_ref):
    g_ref[...] = tn(hid_ref[...], dy_ref[...]).astype(jnp.bfloat16)

def down_grad(hid, dy, step=512):
    T, F = hid.shape
    D = dy.shape[1]
    return pl.pallas_call(down_grad_body, grid=(D // step,),
        in_specs=[pl.BlockSpec((T, F), lambda i: (0, 0), pipeline_mode=pl.Buffered(1)), pl.BlockSpec((T, step), lambda i: (0, i))],
        out_specs=pl.BlockSpec((F, step), lambda i: (0, i)),
        out_shape=jax.ShapeDtypeStruct((F, D), jnp.bfloat16),
        compiler_params=pltpu.CompilerParams(vmem_limit_bytes=VMEM),
        cost_estimate=SMALL_COST,
        name="down_grad")(hid, dy)

def down_body(hid_a_ref, hid_b_ref, wd_a_ref, wd_b_ref, o_ref):
    out = nn(hid_a_ref[...], wd_a_ref[...]) + nn(hid_b_ref[...], wd_b_ref[...])
    o_ref[...] = out.astype(jnp.bfloat16)


def down(hid_a, hid_b, wd_a, wd_b, step):
    count = hid_a.shape[0]

    def rows(array):
        return pl.BlockSpec((step, array.shape[1]), lambda i: (i, 0))

    def whole(array):
        return pl.BlockSpec(array.shape, lambda i: (0, 0), pipeline_mode=pl.Buffered(1))

    return pl.pallas_call(
        down_body,
        grid=(count // step,),
        in_specs=[rows(hid_a), rows(hid_b), whole(wd_a), whole(wd_b)],
        out_specs=pl.BlockSpec((step, D), lambda i: (i, 0)),
        out_shape=jax.ShapeDtypeStruct((count, D), jnp.bfloat16),
        compiler_params=pltpu.CompilerParams(vmem_limit_bytes=VMEM),
        cost_estimate=SMALL_COST,
        name="down",
    )(hid_a, hid_b, wd_a, wd_b)


def turn(u, cosine, sine):
    lane = lax.broadcasted_iota(jnp.int32, u.shape, 1)
    other = pltpu.roll(u, HD // 2, 1)
    return u * cosine + jnp.where(lane < HD // 2, -other, other) * sine


def mix_body(
    blk_count, rows, small_count, ids, own_ref, cross_ref, core_ref, ring_ref, freq_ref,
    self_ref, near_ref, far_ref, one_ref, strip_ref, vector_ref,
):
    ring = ring_order(blk_count)
    wide_here = ring_ref.shape[-1]
    pieces = []
    for b in range(blk_count):
        at = ring.index(b)
        strip_ref[rows * b : rows * (b + 1)] = ring_ref[at, :rows]
        left = small_count
        line = rows
        while left > 0:
            size = min(left, wide_here)
            pieces.append(ring_ref[at, line : line + 1, :size].astype(jnp.float32))
            left -= size
            line += 1
    vector = jnp.concatenate(pieces, axis=1)
    vector_ref[...] = vector
    gain = vector[:, :D]
    grp = ids[0]
    strip_q = wide_here - HD
    bias = jnp.zeros((1, wide_here), jnp.float32)
    for k in range(4):
        kv_at = 2 * D + HQD + HD * (k // 2) + KVD * (k % 2)
        part = jnp.concatenate(
            [
                vector[:, 2 * D + strip_q * k : 2 * D + strip_q * (k + 1)],
                vector[:, kv_at : kv_at + HD],
            ],
            axis=1,
        )
        bias = bias + jnp.where(grp == k, part, 0.0)
    count = own_ref.shape[0]
    strip = strip_ref[...]
    for d in range(4):
        source = (own_ref[...], core_ref[0], cross_ref[...], core_ref[1])[d]
        x = source[:, :D].astype(jnp.float32)
        root = lax.rsqrt(jnp.mean(x * x, axis=1, keepdims=True) + NORM_EPS)
        one = (x * root * gain).astype(jnp.bfloat16)
        one_ref[count * d : count * (d + 1)] = one
        mixed = nn(one, strip) + bias
        digits = source[:, D : D + HD].astype(jnp.float32)
        position = 64.0 * digits[:, 0:1] + digits[:, 1:2]
        angles = position * freq_ref[...]
        cosine, sine = jnp.cos(angles), jnp.sin(angles)
        for i in range(wide_here // HD):
            c, s = cosine, sine
            if i == wide_here // HD - 1:
                c = jnp.where(grp % 2 == 1, 1.0, c)
                s = jnp.where(grp % 2 == 1, 0.0, s)
            at = HD * i
            out = turn(mixed[:, at : at + HD], c, s).astype(jnp.bfloat16)
            if d == 0:
                self_ref[:, at : at + HD] = out
            elif d == 1:
                near_ref[:, at : at + HD] = out
            else:
                far_ref[d - 2, :, at : at + HD] = out


def mix(ids, own, cross, core, ring, freq, blk_count, rows, small_count):
    count = own.shape[0]
    wide_here = ring.shape[-1]
    low16 = jnp.bfloat16
    return pl.pallas_call(
        functools.partial(mix_body, blk_count, rows, small_count),
        in_specs=[pl.BlockSpec(memory_space=pltpu.SMEM)] + [pl.BlockSpec(memory_space=pltpu.VMEM)] * 5,
        out_specs=[pl.BlockSpec(memory_space=pltpu.VMEM)] * 6,
        out_shape=[
            jax.ShapeDtypeStruct((count, wide_here), low16),
            jax.ShapeDtypeStruct((count, wide_here), low16),
            jax.ShapeDtypeStruct((2, count, wide_here), low16),
            jax.ShapeDtypeStruct((4 * count, D), low16),
            jax.ShapeDtypeStruct((D, wide_here), low16),
            jax.ShapeDtypeStruct((1, blk_count * small_count), jnp.float32),
        ],
        compiler_params=pltpu.CompilerParams(vmem_limit_bytes=VMEM),
        cost_estimate=SMALL_COST,
        name="mix",
    )(ids, own, cross, core, ring, freq)


def pack_body(ids, self_ref, cross_ref, core_ref, q_ref, kv_ref):
    strip_q = self_ref.shape[1] - HD
    for g in range(4):

        @pl.when(ids[0] == g)
        def _(g=g):
            for k in range(4):
                part = (self_ref[...], core_ref[0], cross_ref[0], core_ref[1])[g ^ k]
                q_ref[:, strip_q * k : strip_q * (k + 1)] = part[:, :strip_q]
                at = (k % 2) * KVD + (k // 2) * HD
                kv_ref[:, at : at + HD] = part[:, strip_q:]


def pack(ids, own, cross, core):
    count = own.shape[0]
    return pl.pallas_call(
        pack_body,
        in_specs=[pl.BlockSpec(memory_space=pltpu.SMEM)] + [pl.BlockSpec(memory_space=pltpu.VMEM)] * 3,
        out_specs=[pl.BlockSpec(memory_space=pltpu.VMEM)] * 2,
        out_shape=[
            jax.ShapeDtypeStruct((count, HQD), jnp.bfloat16),
            jax.ShapeDtypeStruct((count, 2 * KVD), jnp.bfloat16),
        ],
        compiler_params=pltpu.CompilerParams(vmem_limit_bytes=VMEM),
        cost_estimate=SMALL_COST,
        name="pack",
    )(ids, own, cross, core)


def turn_dkv_body(ids, dkv_ref, cos_ref, sin_ref, self_ref, near_ref, far_ref, sum_ref):
    items = []
    sums = [None] * 4
    for k in range(4):
        at = (k % 2) * KVD + (k // 2) * HD
        part = dkv_ref[:, at : at + HD]
        if k % 2 == 0:
            part = turn_back(part.astype(jnp.float32), cos_ref[...], sin_ref[...]).astype(jnp.bfloat16)
        items.append(part)
        sums[(k % 2) * 2 + k // 2] = jnp.sum(part.astype(jnp.float32), axis=0, keepdims=True)
    sum_ref[...] = jnp.concatenate(sums, axis=1)
    for g in range(4):

        @pl.when(ids[0] == g)
        def _(g=g):
            self_ref[...] = items[g]
            near_ref[...] = items[g ^ 1]
            far_ref[0] = items[g ^ 2]
            far_ref[1] = items[g ^ 3]


def turn_dkv(ids, dkv, cosine, sine):
    count = dkv.shape[0]
    return pl.pallas_call(
        turn_dkv_body,
        in_specs=[pl.BlockSpec(memory_space=pltpu.SMEM)] + [pl.BlockSpec(memory_space=pltpu.VMEM)] * 3,
        out_specs=[pl.BlockSpec(memory_space=pltpu.VMEM)] * 4,
        out_shape=[
            jax.ShapeDtypeStruct((count, HD), jnp.bfloat16),
            jax.ShapeDtypeStruct((count, HD), jnp.bfloat16),
            jax.ShapeDtypeStruct((2, count, HD), jnp.bfloat16),
            jax.ShapeDtypeStruct((1, 2 * KVD), jnp.float32),
        ],
        compiler_params=pltpu.CompilerParams(vmem_limit_bytes=VMEM),
        cost_estimate=SMALL_COST,
        name="turn_dkv",
    )(ids, dkv, cosine, sine)


def kv_grad_body(
    blk_count, rows, small_count, self_ref, cross_ref, core_ref, dq_ref, one_ref, own_ref, near_x_ref,
    core_x_ref, strip_ref, gain_two_ref, bias_q_ref, bias_kv_ref, grad_ref, here_ref, there_ref,
):
    count = self_ref.shape[0]
    strip_q = strip_ref.shape[1] - HD
    parts = (self_ref[...], core_ref[0], cross_ref[0], core_ref[1])
    near = jnp.concatenate(parts, axis=0)
    grad = tn(one_ref[...], near)
    gain_one = jnp.zeros((1, D), jnp.float32)
    for d in range(4):
        x = (own_ref[...], core_x_ref[0], near_x_ref[...], core_x_ref[1])[d][:, :D].astype(jnp.float32)
        root = lax.rsqrt(jnp.mean(x * x, axis=1, keepdims=True) + NORM_EPS)
        hone = nt(dq_ref[count * d : count * (d + 1)], strip_ref[:, :strip_q])
        hone = hone + nt(parts[d], strip_ref[:, strip_q:])
        gain_one = gain_one + jnp.sum(hone * x * root, axis=0, keepdims=True)
        out_ref = (here_ref, there_ref)[d % 2]
        out_ref[count * (d // 2) : count * (d // 2 + 1)] = hone.astype(jnp.bfloat16)
    vector = jnp.concatenate([gain_one, gain_two_ref[...], bias_q_ref[...], bias_kv_ref[...]], axis=1)
    extra = grad_ref.shape[1] - rows
    for b in range(blk_count):
        grad_ref[b, :rows] = grad[rows * b : rows * (b + 1)].astype(jnp.bfloat16)
        lines = []
        for line in range(extra):
            size = min(HD, max(small_count - line * HD, 0))
            begin = small_count * b + line * HD
            pieces = [vector[:, begin : begin + size]] if size > 0 else []
            if size < HD:
                pieces.append(jnp.zeros((1, HD - size), jnp.float32))
            lines.append(pieces[0] if len(pieces) == 1 else jnp.concatenate(pieces, axis=1))
        grad_ref[b, rows:] = jnp.concatenate(lines, axis=0).astype(jnp.bfloat16)


def kv_grad_rows(rows, small_count):
    needed = rows + -(-small_count // HD)
    return needed + -needed % 16


def make_kv_grad(blk_count, rows, small_count, own, cross, core, dq, one, x_own, x_cross, x_core, strip, gain_two, bias_q, bias_kv):
    count = own.shape[0]
    height = kv_grad_rows(rows, small_count)
    return pl.pallas_call(
        functools.partial(kv_grad_body, blk_count, rows, small_count),
        in_specs=[pl.BlockSpec(memory_space=pltpu.VMEM)] * 12,
        out_specs=[pl.BlockSpec(memory_space=pltpu.VMEM)] * 3,
        out_shape=[
            jax.ShapeDtypeStruct((blk_count, height, HD), jnp.bfloat16),
            jax.ShapeDtypeStruct((2 * count, D), jnp.bfloat16),
            jax.ShapeDtypeStruct((2 * count, D), jnp.bfloat16),
        ],
        compiler_params=pltpu.CompilerParams(vmem_limit_bytes=VMEM),
        cost_estimate=SMALL_COST,
        name="kv_grad",
    )(own, cross, core, dq, one, x_own, x_cross, x_core, strip, gain_two, bias_q, bias_kv)


CORE = [(0, 1), (1, 0), (2, 3), (3, 2)]
CROSS = [(0, 2), (2, 0), (1, 3), (3, 1)]
DIAG = [(0, 3), (3, 0), (1, 2), (2, 1)]


def low(values):
    return values.astype(jnp.bfloat16)


def wide(values):
    return values.astype(jnp.float32)


def swap_core(values):
    return lax.ppermute(values, "grp", CORE)


def swap_cross(values):
    return lax.ppermute(values, "grp", CROSS)


def swap_diag(values):
    return lax.ppermute(values, "grp", DIAG)


def swap_blk(values, bit):
    count = lax.axis_size("blk")
    return lax.ppermute(values, "blk", [(i, i ^ bit) for i in range(count)])


def blk_bit(bit):
    return (lax.axis_index("blk") & bit) != 0


def bits_of(count):
    out = []
    bit = count // 2
    while bit >= 1:
        out.append(bit)
        bit //= 2
    return out


def gather_bits(values, order):
    done = []
    for bit in order:
        other = swap_blk(values, bit)
        mine = blk_bit(bit)
        axis = sum(1 for d in done if d > bit)
        values = jnp.stack(
            [jnp.where(mine, other, values), jnp.where(mine, values, other)], axis=axis
        )
        done.append(bit)
    return values


def scatter_bits(values, axes, order):
    axes = list(axes)
    for bit in order:
        axis = axes.index(bit)
        mine = blk_bit(bit).astype(jnp.int32)
        keep = lax.dynamic_index_in_dim(values, mine, axis, keepdims=False)
        send = lax.dynamic_index_in_dim(values, 1 - mine, axis, keepdims=False)
        values = low(wide(keep) + wide(swap_blk(send, bit)))
        axes.remove(bit)
    return values


def by_place(parts):
    grp = lax.axis_index("grp")
    core = (grp & 1) != 0
    cross = (grp & 2) != 0
    a, b, c, d = parts
    a, b = jnp.where(core, b, a), jnp.where(core, a, b)
    c, d = jnp.where(core, d, c), jnp.where(core, c, d)
    a, c = jnp.where(cross, c, a), jnp.where(cross, a, c)
    b, d = jnp.where(cross, d, b), jnp.where(cross, b, d)
    return [a, b, c, d]


def gather_near(values):
    cross = swap_cross(values)
    both = swap_core(jnp.stack([values, cross]))
    return [values, both[0], cross, both[1]]


def gather_grp(values):
    return by_place(gather_near(values))


def gather_tokens(values, bit):
    half = values.shape[0] // 2
    cross = swap_cross(values)
    over = swap_blk(values, bit)
    first = swap_blk(cross[:half], bit)
    second = swap_cross(over[half:])
    chip = jnp.concatenate([values, cross, over, first, second])
    return jnp.concatenate([chip, swap_core(chip)])


def angles_of(position):
    half = HD // 2
    freqs = ROPE_BASE ** (-2.0 * jnp.arange(half, dtype=jnp.float32) / HD)
    return position.astype(jnp.float32)[:, None] * freqs[None, :]


def rotate_by(values, cosine, sine):
    half = HD // 2
    first_half = values[..., :half]
    second_half = values[..., half:]
    return jnp.concatenate(
        [first_half * cosine - second_half * sine, second_half * cosine + first_half * sine],
        axis=-1,
    )


def after(values, anchor):
    return lax.optimization_barrier((values, anchor))[0]


def gather_step(values, done, bit):
    other = swap_blk(values, bit)
    mine = blk_bit(bit)
    axis = sum(1 for d in done if d > bit)
    return jnp.stack(
        [jnp.where(mine, other, values), jnp.where(mine, values, other)], axis=axis
    )


def gather_near_stacked(values):
    both = jnp.stack([values, swap_cross(values)])
    return jnp.concatenate([both, swap_core(both)])


def ring_groups(count):
    return [[g * count + b for b in ring_order(count)] for g in range(4)]


def gather_ring(values):
    count = lax.axis_size("blk")
    return lax.all_gather(values, ("grp", "blk"), axis=0, axis_index_groups=ring_groups(count))


def exchange_near(parts):
    cross = swap_cross(jnp.stack([parts[2], parts[3]]))
    core = swap_core(jnp.stack([parts[1], cross[1]]))
    return [parts[0], core[0], cross[0], core[1]]


def on_device(
    tokens,
    cotangent,
    segment_ids,
    position_ids,
    w_attend,
    w_out,
    w_gate,
    w_up,
    w_down,
    small_params,
    first_attend,
    first_out,
    first_gate,
    first_up,
    first_down,
    first_small,
    second_attend,
    second_out,
    second_gate,
    second_up,
    second_down,
    second_small,
):
    rows_here, block_len = tokens.shape[:2]
    blk_count = lax.axis_size("blk")
    seq_len = block_len * blk_count
    token_count = rows_here * block_len
    grp = lax.axis_index("grp")
    blk = lax.axis_index("blk")
    cross_id, core_id = grp // 2, grp % 2
    strip_heads = H // 4
    strip_q = strip_heads * HD
    bits = bits_of(blk_count)
    team = blk_count // 4
    lows = [bit for bit in bits if bit < team]
    spread = [bits[0]] + lows
    low_shape = (2,) * len(lows)
    in_team = blk_bit(team).astype(jnp.int32)
    weight_rows = w_gate.shape[0]
    ff_block = w_down.shape[0]
    quarter = ff_block // 4
    widths = [size * blk_count // 2 for at, size in halves_of(quarter)]
    chip_rows = 4 * token_count
    half = token_count // 2

    ids = jnp.stack([grp, in_team])
    flat_low = tokens.reshape(token_count, D)
    dy_low = cotangent.reshape(token_count, D)
    positions = position_ids.reshape(token_count)
    kv_at = HQD + HD * cross_id + KVD * core_id
    strip_local = low(
        jnp.concatenate(
            [
                lax.dynamic_slice_in_dim(w_attend, strip_q * grp, strip_q, 1),
                lax.dynamic_slice_in_dim(w_attend, kv_at, HD, 1),
            ],
            axis=1,
        )
    )
    small_count = small_params.shape[0]
    small_send = jnp.concatenate([low(small_params), low(segment_ids.reshape(token_count))])
    strip_wide = strip_q + HD
    small_send = jnp.pad(small_send, (0, -small_send.shape[0] % (16 * strip_wide)))
    strip_local = jnp.concatenate([strip_local, small_send.reshape(-1, strip_wide)])
    ring = ring_order(blk_count)
    strip_ring = gather_ring(strip_local)
    small_ring = strip_ring[:, weight_rows:].reshape(blk_count, -1)[:, small_count : small_count + token_count]
    small_all = jnp.stack([small_ring[ring.index(b)] for b in range(blk_count)])
    digits = low(jnp.stack([positions // 64, positions % 64], axis=1))
    digits = jnp.pad(digits, ((0, 0), (0, HD - 2)))
    token_send = jnp.concatenate([flat_low, digits], axis=1)
    picked_a, picked_b = pick_columns(ids, w_gate, w_up, blk_count)
    token_cross = after(swap_cross(token_send), (picked_a, strip_ring))
    dy_over = swap_blk(after(dy_low, token_cross), team)
    dy_cross = swap_cross(after(dy_low, token_cross))

    def place(values, other, done, bit, lead=0):
        mine = blk_bit(bit)
        axis = lead + sum(1 for d in done if d > bit)
        return jnp.stack(
            [jnp.where(mine, other, values), jnp.where(mine, values, other)], axis=axis
        )

    mine_team = blk_bit(team)
    (low_first, size_first), (low_second, size_second) = halves_of(quarter)

    def team_pair(mine, got):
        return jnp.stack(
            [jnp.where(mine_team, got, mine), jnp.where(mine_team, mine, got)], axis=1
        )

    out_local = low(lax.dynamic_slice_in_dim(w_out, strip_q * grp, strip_q, 1))
    out_ring = gather_ring(after(out_local, strip_ring))
    got_a = swap_blk(picked_a[1], team)
    down_here = low(lax.dynamic_slice_in_dim(w_down, quarter * grp, quarter, 0))
    down_got = swap_blk(after(down_here, strip_ring), bits[0])
    token_core = swap_core(jnp.stack([token_send, token_cross]))
    freqs = ROPE_BASE ** (-2.0 * jnp.arange(HD // 2, dtype=jnp.float32) / HD)
    freqs = jnp.concatenate([freqs, freqs])[None]
    mixed_own, mixed_core, mixed_far, near_one, strip, vector = mix(
        ids, token_send, token_cross, token_core, strip_ring, freqs, blk_count, weight_rows, small_count
    )
    vector = vector[0]
    gain_one = vector[:D]
    gain_two = vector[D : 2 * D]
    seg_all = small_all.astype(jnp.int32)
    seg_all = seg_all.reshape(blk_count, rows_here, block_len)
    seg_key = jnp.broadcast_to(
        seg_all.transpose(1, 0, 2).reshape(rows_here, seq_len)[:, :, None], (rows_here, seq_len, HD)
    )
    seg_query = jnp.broadcast_to(segment_ids[:, None, :], (rows_here, 8, block_len))
    first_blk = jnp.sum((seg_all[:, :, -1] < segment_ids[None, :, 0]).astype(jnp.int32), axis=0)
    attend_ids = jnp.concatenate([blk[None], first_blk])

    mixed_cross = swap_cross(mixed_far)
    mixed_core = swap_core(jnp.stack([mixed_core, mixed_cross[1]]))
    query, packed_kv = pack(ids, mixed_own, mixed_cross, mixed_core)
    key_value = packed_kv.reshape(rows_here, block_len, 2 * KVD)
    kv_all = gather_ring(key_value)

    teams = [
        [g * blk_count + (i | t) for g in range(4) for t in (0, team)]
        for i in range(blk_count)
        if not i & team
    ]
    order = jnp.stack(
        [
            (grp ^ (2 * (i & 1) + (i >> 2))) * 2 + (in_team ^ ((i >> 1) & 1))
            for i in range(8)
        ]
    )

    peers = [[i for i in range(blk_count) if (i & team) == t] for t in (0, team)]

    def lows_of(values, done, lead=0, anchor=None):
        for bit in lows:
            got = swap_blk(values, bit)
            if anchor is not None:
                got = after(got, anchor)
            values = place(values, got, done, bit, lead)
            done = done + [bit]
        return values

    got_b = swap_blk(after(picked_b[1], mixed_own), team)
    down_got, dy_cross, dy_over = after((down_got, dy_cross, dy_over), packed_kv)
    pair_a = team_pair(picked_a[0], after(got_a, packed_kv))
    kv_all = after(kv_all, (got_b, down_got, dy_cross, dy_over))
    pair_a = after(pair_a, kv_all)
    pair_a_got = swap_blk(pair_a, bits[0])
    down_here = place(down_here, down_got, [], bits[0])
    dy_first = swap_blk(dy_cross[:half], team)
    dy_second = swap_cross(dy_over[half:])
    dy_chip = jnp.concatenate([dy_low, dy_cross, dy_over, dy_first, dy_second])
    dy_team = jnp.concatenate([dy_chip, swap_core(dy_chip)])
    pair_a = place(pair_a, pair_a_got, [team], bits[0], 1)
    gate_up_a = lows_of(pair_a, [bits[0], team], 1).reshape(2, D, -1)
    pair_b = team_pair(picked_b[0], got_b)
    pair_b_got = swap_blk(after(pair_b, pair_a_got), bits[0])
    out_ring = after(out_ring, packed_kv)
    out_strip = jnp.concatenate([out_ring[ring.index(b)] for b in range(blk_count)])
    out_cross = swap_cross(out_strip)
    out_core = swap_core(jnp.stack([out_strip, after(out_cross, kv_all)]))
    out_full = jnp.concatenate(by_place([out_strip, out_core[0], out_cross, out_core[1]]), axis=1)

    att_in, lse = attend(attend_ids, query, kv_all, seg_key, seg_query, block_len)
    down_here = lows_of(down_here, [bits[0]], 0, att_in).reshape(2 * blk_count // 4, quarter, D)
    down_a = down_here[:, :size_first].reshape(widths[0], D)
    down_b = down_here[:, size_first:].reshape(widths[1], D)


    flat = wide(flat_low)
    resid = flat + jnp.dot(att_in, out_full, preferred_element_type=jnp.float32)
    h_two = low(norm_apply(resid, gain_two))
    h_two = after(h_two, (pair_a_got, down_here))
    h_team = lax.all_gather(h_two, ("grp", "blk"), axis=0, tiled=True, axis_index_groups=teams)
    pair_b_got = after(pair_b_got, (h_two, gate_up_a))
    pair_b = place(pair_b, pair_b_got, [team], bits[0], 1)
    h_team = after(h_team, (gate_up_a, pair_b, dy_team))
    hidden_a, d_gate_a, d_up_a, part_a = middle(order, h_team, dy_team, gate_up_a, down_a)
    gate_up_b = lows_of(pair_b, [bits[0], team], 1, hidden_a).reshape(2, D, -1)
    down_grad_a = down_grad(hidden_a, dy_team)
    down_share_a = lax.psum_scatter(
        down_grad_a, "blk", scatter_dimension=0, axis_index_groups=peers, tiled=True
    )
    column_grad_a = two_grads(h_team, d_gate_a, d_up_a)

    def part_sent(values, axis, bit):
        mine = blk_bit(bit).astype(jnp.int32)
        keep = lax.dynamic_index_in_dim(values, mine, axis, keepdims=False)
        send = lax.dynamic_index_in_dim(values, 1 - mine, axis, keepdims=False)
        return keep, swap_blk(send, bit)

    def part_sum(keep, got):
        return low(wide(keep) + wide(got))

    def columns_first(grad):
        grad = grad.reshape((2, 2, 2) + low_shape + (weight_rows, -1))
        return part_sent(grad, 2 + len(lows), lows[-1])

    def columns_mid(keep, got):
        values = part_sum(keep, got)
        for i in range(len(lows) - 2, -1, -1):
            values = part_sum(*part_sent(values, 3 + i, lows[i]))
        return values

    def columns_third(keep, got):
        values = part_sum(keep, got)
        mine = lax.dynamic_index_in_dim(values, in_team, 1, keepdims=False)
        send = lax.dynamic_index_in_dim(values, 1 - in_team, 1, keepdims=False)
        return values, (mine, swap_blk(send, team))

    def rows_second(keep, got):
        values = part_sum(keep, got)
        for i in range(len(lows) - 2, -1, -1):
            values = part_sum(*part_sent(values, 1 + i, lows[i]))
        return part_sent(values, 0, bits[0])

    def columns_last(mine, got):
        return jnp.stack(
            [jnp.where(mine_team, got, mine), jnp.where(mine_team, mine, got)], axis=1
        )

    first_a = columns_first(column_grad_a)
    hidden_b, d_gate_b, d_up_b, d_htwo_part = middle(
        order, after(h_team, (column_grad_a, down_grad_a)), dy_team, gate_up_b, down_b, part_a
    )

    def chip_sum(values, came):
        return low(wide(values[:chip_rows]) + wide(came))

    def scatter_far(chip):
        far = chip[3 * token_count :]
        return swap_blk(far[:half], team), swap_cross(far[half:])

    def scatter_near(chip, first, second):
        cross, over = (chip[token_count * i : token_count * (i + 1)] for i in (1, 2))
        cross = jnp.concatenate([low(wide(cross[:half]) + wide(first)), cross[half:]])
        over = jnp.concatenate([over[:half], low(wide(over[half:]) + wide(second))])
        return swap_cross(cross), swap_blk(over, team)

    near_att_cross = swap_cross(after(att_in, hidden_a))
    d_htwo_part = after(d_htwo_part, (first_a[1], down_share_a, near_att_cross))
    d_came = swap_core(d_htwo_part[chip_rows:])
    down_grad_b = down_grad(hidden_b, dy_team)
    rows_b = part_sent(
        down_grad_b.reshape((2,) + low_shape + (size_second, D)), len(lows), lows[-1]
    )
    d_chip = chip_sum(d_htwo_part, after(d_came, down_grad_b))
    d_far = scatter_far(d_chip)
    column_grad_b = two_grads(h_team, *after((d_gate_b, d_up_b), d_chip))
    first_b = columns_first(column_grad_b)
    d_far = after(d_far, column_grad_b)
    d_cross, d_over = scatter_near(d_chip, *d_far)
    out_part = down(*after((hidden_a, hidden_b), d_far), down_a, down_b, token_count)
    out_came = swap_core(out_part[chip_rows:])
    mid_a = columns_mid(*after(first_a, d_far))
    second_a = part_sent(mid_a, 1, bits[0])
    d_cross, d_over = after((d_cross, d_over), out_part)
    d_htwo = wide(d_chip[:token_count]) + wide(d_cross) + wide(d_over)

    norm_value_two, norm_back_two = jax.vjp(norm_apply, resid, gain_two)
    d_resid_norm, grad_gain_two = norm_back_two(d_htwo)
    d_resid = wide(dy_low) + d_resid_norm
    d_att = low(d_resid)
    rows_b = rows_second(*after(rows_b, d_att))

    d_attended = low(right_transposed(d_att, out_full))
    own_angles = angles_of(positions)
    cosine, sine = jnp.cos(own_angles), jnp.sin(own_angles)
    d_query, dkv = attend_back(
        attend_ids,
        query,
        kv_all,
        seg_key,
        seg_query,
        att_in,
        d_attended,
        lse,
        jnp.concatenate([cosine, cosine], axis=1),
        jnp.concatenate([sine, sine], axis=1),
        block_len,
    )
    dkv = lax.psum_scatter(
        dkv.reshape(blk_count * token_count, 2 * KVD),
        ("grp", "blk"),
        scatter_dimension=0,
        axis_index_groups=ring_groups(blk_count),
        tiled=True,
    )
    down_share_b = part_sum(*after(rows_b, d_query))
    sum_a, third_a = columns_third(*after(second_a, d_query))

    def to_strips(parts):
        return jnp.concatenate(exchange_near(by_place(parts)))

    near_dq = to_strips([d_query[:, strip_q * k : strip_q * (k + 1)] for k in range(4)])
    block_shape = (2,) * len(bits) + (weight_rows, -1)
    query_grad = low(left_product(near_one, near_dq)).reshape(block_shape)
    steps_query = part_sent(query_grad, len(bits) - 1, bits[-1])
    near_a = gather_near_stacked(columns_last(*after(third_a, d_query)))
    second_b = part_sent(columns_mid(*after(first_b, d_query)), 1, bits[0])
    dkv = after(dkv, (query_grad, down_share_b))
    own_part, core_part, far_part, bias_kv = turn_dkv(
        ids, dkv, jnp.concatenate([cosine, cosine], axis=1), jnp.concatenate([sine, sine], axis=1)
    )
    bias_q = jnp.sum(wide(d_query), axis=0)
    d_key = own_part
    cross_part = swap_cross(far_part)
    core_part = swap_core(jnp.stack([core_part, cross_part[1]]))
    kv_grad, hone_here, hone_there = make_kv_grad(
        blk_count,
        weight_rows,
        small_count,
        own_part,
        cross_part,
        core_part,
        near_dq,
        near_one,
        token_send,
        token_cross,
        token_core,
        strip,
        grad_gain_two[None],
        bias_q[None],
        bias_kv,
    )
    vector_rows = -(-small_count // HD)
    kv_grad = kv_grad.reshape((2,) * len(bits) + kv_grad.shape[1:])
    steps_kv = part_sent(kv_grad, len(bits) - 1, bits[-1])
    share_down = after(jnp.concatenate([down_share_a, down_share_b]), dkv)
    grad_down = lax.all_gather(share_down, "grp", axis=0, tiled=True)
    for i in range(len(bits) - 2, -1, -1):
        steps_query = part_sent(part_sum(*after(steps_query, d_key)), i, bits[i])
        kv_sum = part_sum(*steps_kv)
        kv_grad = kv_sum
        steps_kv = part_sent(kv_sum, i, bits[i])
    sum_b, third_b = columns_third(*after(second_b, kv_grad))
    share_kv_all = wide(steps_kv[0]) + wide(after(steps_kv[1], (near_a, third_b[1])))
    share_kv = low(share_kv_all[:weight_rows])
    vector_part = share_kv_all[weight_rows : weight_rows + vector_rows]
    share_query = part_sum(*after(steps_query, kv_grad))
    near_att = swap_core(jnp.stack([att_in, near_att_cross]))
    near_att = jnp.concatenate([att_in, near_att[0], near_att_cross, near_att[1]])
    near_datt = to_strips([d_att[:, strip_q * k : strip_q * (k + 1)] for k in range(4)])
    out_grad = low(left_product(near_att, after(near_datt, d_attended))).reshape(block_shape)
    steps_out = part_sent(out_grad, len(bits) - 1, bits[-1])
    anchors = [near_dq, near_dq]
    for i in range(len(bits) - 2, -1, -1):
        anchor = anchors[min(len(bits) - 2 - i, 1)]
        steps_out = part_sent(part_sum(*after(steps_out, anchor)), i, bits[i])
    share_out = part_sum(*after(steps_out, kv_grad))

    own_b = columns_last(*third_b)
    cross_b = swap_cross(own_b)
    near_b = jnp.stack([own_b, cross_b])
    near_b = jnp.concatenate([near_b, swap_core(near_b)])
    grad_out = jnp.concatenate(gather_grp(share_out), axis=1)
    query_parts = gather_grp(share_query)
    key_parts = gather_grp(share_kv)
    grad_attend = jnp.concatenate(query_parts + [key_parts[k] for k in (0, 2, 1, 3)], axis=1)

    other = wide(swap_core(hone_there))
    d_hone = wide(hone_here[:token_count]) + other[:token_count]
    d_hone_cross = swap_cross(low(wide(hone_here[token_count:]) + other[token_count:]))
    square_sum = square_total(
        [
            wide(s)
            for s in (share_query, share_kv, share_out, sum_a, sum_b, share_down)
        ]
    )
    packed = jnp.concatenate([vector_part, jnp.full((8, HD), square_sum)])
    packed = packed + swap_cross(packed)
    packed = packed + swap_core(packed)
    share_vector = packed[:vector_rows].reshape(-1)[:small_count]
    square_sum = packed[vector_rows:] + jnp.sum(share_vector * share_vector)
    for bit in bits:
        square_sum = square_sum + swap_blk(square_sum, bit)
    grad_norm = jnp.sqrt(square_sum[0, 0])
    factor = jnp.minimum(1.0, CLIP_NORM / (grad_norm + 1e-06))
    out_chip = chip_sum(out_part, after(out_came, kv_grad))
    out_far = scatter_far(out_chip)
    factor = after(factor, (out_chip, cross_b))

    new_first_gate, new_second_gate, new_gate = adam_columns(
        0, ids, factor[None], near_a, near_b, w_gate, first_gate, second_gate, blk_count, RATE_GATE, WEIGHT_DECAY
    )
    new_first_up, new_second_up, new_up = adam_columns(
        1, ids, factor[None], near_a, near_b, w_up, first_up, second_up, blk_count, RATE_GATE, WEIGHT_DECAY
    )
    norm_value_one, norm_back_one = jax.vjp(norm_apply, flat, gain_one)
    d_hone = after(d_hone + wide(after(d_hone_cross, new_gate)), new_gate)
    d_flat_norm, unused_gain = norm_back_one(d_hone)
    grad_tokens = low(d_resid + d_flat_norm)

    new_first_attend, new_second_attend, new_attend = adam_step(
        w_attend, factor * wide(grad_attend), first_attend, second_attend, RATE_ATTEND, WEIGHT_DECAY
    )
    new_first_out, new_second_out, new_out = adam_step(
        w_out, factor * wide(grad_out), first_out, second_out, RATE_OUT, WEIGHT_DECAY
    )
    new_first_down, new_second_down, new_down = adam_step(
        w_down, factor * wide(grad_down), first_down, second_down, RATE_DOWN, WEIGHT_DECAY
    )
    new_first_small, new_second_small, new_small = adam_step(
        small_params, factor * share_vector, first_small, second_small, RATE_VECTOR, 0.0
    )

    out_near = after(scatter_near(out_chip, *after(out_far, factor)), (new_gate, new_up))
    out_tokens = low(resid + wide(out_chip[:token_count]) + wide(out_near[0]) + wide(out_near[1]))
    return (
        out_tokens.reshape(rows_here, block_len, D),
        grad_tokens.reshape(rows_here, block_len, D),
        grad_norm,
        new_first_attend,
        new_second_attend,
        new_attend,
        new_first_out,
        new_second_out,
        new_out,
        new_first_gate,
        new_second_gate,
        new_gate,
        new_first_up,
        new_second_up,
        new_up,
        new_first_down,
        new_second_down,
        new_down,
        new_first_small,
        new_second_small,
        new_small,
    )


def solution(mesh):
    placed = (
        P("grp", "blk", None),
        P("grp", "blk", None),
        P("grp", "blk"),
        P("grp", "blk"),
        P("blk", None),
        P("blk", None),
        P("blk", None),
        P("blk", None),
        P("blk", None),
        P("blk"),
        P("blk", None),
        P("blk", None),
        P("blk", None),
        P("blk", None),
        P("blk", None),
        P("blk"),
        P("blk", None),
        P("blk", None),
        P("blk", None),
        P("blk", None),
        P("blk", None),
        P("blk"),
    )
    return jax.shard_map(
        on_device,
        mesh=mesh,
        in_specs=placed,
        out_specs=(
            P("grp", "blk", None),
            P("grp", "blk", None),
            P(),
            P("blk", None),
            P("blk", None),
            P("blk", None),
            P("blk", None),
            P("blk", None),
            P("blk", None),
            P("blk", None),
            P("blk", None),
            P("blk", None),
            P("blk", None),
            P("blk", None),
            P("blk", None),
            P("blk", None),
            P("blk", None),
            P("blk", None),
            P("blk"),
            P("blk"),
            P("blk"),
        ),
        check_vma=False,
    )
```

```python
import functools

import jax
import jax.numpy as jnp
from jax import lax
from jax.experimental import pallas as pl
from jax.experimental.pallas import tpu as pltpu
from jax.sharding import PartitionSpec as P

D = 1536
FF = 8960
H = 12
KVH = 2
HD = 128
STEP = 10
HQD = 1536
KVD = 256


NORM_EPS = 1e-06
ROPE_BASE = 10000.0
CLIP_NORM = 1.0
BETA_FIRST = 0.9
BETA_SECOND = 0.95
ADAM_EPS = 1e-08
WEIGHT_DECAY = 0.1
RATE_ATTEND = 0.06
RATE_OUT = 0.5
RATE_GATE = 0.06
RATE_DOWN = 0.03
RATE_VECTOR = 0.5
NEG_LARGE = -1e30
LOG2E = 1.4426950408889634
VMEM = 48 * 1024 * 1024
SMALL_COST = pl.CostEstimate(flops=1000, bytes_accessed=1000, transcendentals=0)


def norm_apply(values, gain):
    return values * lax.rsqrt(jnp.mean(values * values, axis=-1, keepdims=True) + NORM_EPS) * gain


def swish_product(gate, up_proj):
    return jax.nn.silu(gate) * up_proj


def left_product(left_side, right_side):
    return lax.dot_general(
        left_side, right_side, (((0,), (0,)), ((), ())), preferred_element_type=jnp.float32
    )


def right_transposed(left_side, right_side):
    return lax.dot_general(
        left_side, right_side, (((1,), (1,)), ((), ())), preferred_element_type=jnp.float32
    )


def square_total(arrays):
    return sum((jnp.sum(member * member) for member in arrays))


def adam_step(weight, grad, first, second, rate, decay):
    first_new = BETA_FIRST * first + (1.0 - BETA_FIRST) * grad
    second_new = BETA_SECOND * second + (1.0 - BETA_SECOND) * grad * grad
    first_hat = first_new / (1.0 - BETA_FIRST**STEP)
    second_hat = second_new / (1.0 - BETA_SECOND**STEP)
    weight_new = weight - rate * (first_hat / (jnp.sqrt(second_hat) + ADAM_EPS) + decay * weight)
    return (first_new, second_new, weight_new)


def ring_order(count):
    return list(range(0, count, 2)) + list(range(count - 1, 0, -2))


def halves_of(quarter):
    first = quarter * 16 // 35
    return ((0, first), (first, quarter - first))


def pick_body(blk_count, ids, gate_ref, up_ref, *out_refs):
    quarter = FF // blk_count // 4
    per = blk_count // 4
    for k in range(4):

        @pl.when(ids[0] == k)
        def _(k=k):
            for (at, size), out_ref in zip(halves_of(quarter), out_refs):
                for which, src in enumerate((gate_ref, up_ref)):
                    for bit in range(2):
                        parts = []
                        for high in range(2):
                            for small in range(per):
                                begin = (((high * 2 + bit) * per + small) * 4 + k) * quarter + at
                                parts.append(src[:, begin : begin + size])
                        out_ref[ids[1] ^ bit, which] = jnp.concatenate(parts, axis=1).astype(
                            jnp.bfloat16
                        )


def pick_columns(ids, gate, up, blk_count):
    rows = gate.shape[0]
    step = 48 if rows % 48 == 0 else rows
    widths = [size * blk_count // 2 for at, size in halves_of(FF // blk_count // 4)]
    spec = pl.BlockSpec((step, FF), lambda i, ids: (i, 0))
    return pl.pallas_call(
        functools.partial(pick_body, blk_count),
        grid_spec=pltpu.PrefetchScalarGridSpec(
            num_scalar_prefetch=1,
            grid=(rows // step,),
            in_specs=[spec, spec],
            out_specs=[pl.BlockSpec((2, 2, step, w), lambda i, ids: (0, 0, i, 0)) for w in widths],
        ),
        out_shape=[jax.ShapeDtypeStruct((2, 2, rows, w), jnp.bfloat16) for w in widths],
        compiler_params=pltpu.CompilerParams(vmem_limit_bytes=VMEM),
        cost_estimate=SMALL_COST,
        name="pick_columns",
    )(ids, gate, up)


def near_at(away):
    return (away & 1) * 2 + (away >> 1)


def adam_body(blk_count, rate, decay, ids, factor_ref, first_ref, second_ref, w_ref, m_ref, v_ref, m_out, v_out, w_out):
    per = blk_count // 4
    sizes = [size for at, size in halves_of(FF // blk_count // 4)]
    grads = [
        [[ref[near_at(ids[0] ^ k), bit] for bit in range(2)] for k in range(4)]
        for ref in (first_ref, second_ref)
    ]
    parts = []
    for high in range(2):
        for bit in range(2):
            for small in range(per):
                place = high * per + small
                for k in range(4):
                    for part, size in zip(grads, sizes):
                        parts.append(part[k][bit][:, place * size : (place + 1) * size])
    grad = jnp.concatenate(parts, axis=1).astype(jnp.float32) * factor_ref[0]
    m, v, w = adam_step(w_ref[...], grad, m_ref[...], v_ref[...], rate, decay)
    m_out[...] = m
    v_out[...] = v
    w_out[...] = w


def adam_columns(which, ids, factor, first, second, w, m, v, blk_count, rate, decay):
    rows = w.shape[0]
    step = 32 if rows % 32 == 0 else rows
    spec = pl.BlockSpec((step, FF), lambda i, ids: (i, 0))
    shape = jax.ShapeDtypeStruct((rows, FF), jnp.float32)
    grads = [
        pl.BlockSpec((4, None, 2, step, g.shape[-1]), lambda i, ids: (0, which, 0, i, 0))
        for g in (first, second)
    ]
    return pl.pallas_call(
        functools.partial(adam_body, blk_count, rate, decay),
        grid_spec=pltpu.PrefetchScalarGridSpec(
            num_scalar_prefetch=1,
            grid=(rows // step,),
            in_specs=[pl.BlockSpec(memory_space=pltpu.SMEM)] + grads + [spec, spec, spec],
            out_specs=[spec, spec, spec],
        ),
        out_shape=[shape] * 3,
        compiler_params=pltpu.CompilerParams(vmem_limit_bytes=VMEM),
        cost_estimate=SMALL_COST,
        name="adam_columns",
    )(ids, factor, first, second, w, m, v)


def nt(a, b, **kw):
    return lax.dot_general(a, b, (((1,), (1,)), ((), ())), preferred_element_type=jnp.float32, **kw)

def tn(a, b, **kw):
    return lax.dot_general(a, b, (((0,), (0,)), ((), ())), preferred_element_type=jnp.float32, **kw)

def stack_heads(ref, kvh, group):
    return jnp.concatenate([ref[:, HD * (kvh * group + i): HD * (kvh * group + i + 1)] for i in range(group)], axis=0)

def hidden_from(seg_key_ref, seg_query_ref, first, chunk, block_len, blk):
    key = first + lax.broadcasted_iota(jnp.int32, (chunk, block_len), 0)
    query = blk * block_len + lax.broadcasted_iota(jnp.int32, (chunk, block_len), 1)
    seg_key = seg_key_ref[pl.ds(first, chunk), :]
    counts = jnp.logical_and(key <= query, seg_key == seg_query_ref[0:1, :])
    return jnp.where(counts, 0.0, NEG_LARGE)

def ring_pair(ref, c, at):
    return jnp.concatenate(
        [ref[c, :, at : at + HD], ref[ref.shape[0] - 1 - c, :, at : at + HD]], axis=0
    )


def attend_body(chunk, ids, q_ref, k_ref, v_ref, seg_key_ref, seg_query_ref, o_ref, lse_ref, m_s, l_s, acc_s):
    block_len = q_ref.shape[0]
    group = H // KVH
    row = pl.program_id(0)
    per = chunk // block_len
    scale = HD ** (-0.5) * LOG2E
    start = ids[1 + row] // per
    stop = ids[0] // per + 1
    for kvh in range(KVH):
        q = stack_heads(q_ref, kvh, group)
        m_s[...] = jnp.full_like(m_s, NEG_LARGE)
        l_s[...] = jnp.zeros_like(l_s)
        acc_s[...] = jnp.zeros_like(acc_s)

        def step(c, carry):
            keys = ring_pair(k_ref, c, HD * kvh)
            vals = ring_pair(v_ref, c, HD * kvh)
            bias = hidden_from(seg_key_ref, seg_query_ref, c * chunk, chunk, block_len, ids[0])
            s = nt(keys, q) * scale + jnp.concatenate([bias] * group, axis=1)
            old = m_s[0:1, :]
            new = jnp.maximum(old, jnp.max(s, axis=0, keepdims=True))
            p = jnp.exp2(s - new)
            fade = jnp.exp2(old - new)
            l_s[0:1, :] = l_s[0:1, :] * fade + jnp.sum(p, axis=0, keepdims=True)
            acc_s[...] = acc_s[...] * fade + tn(vals, p.astype(jnp.bfloat16))
            m_s[0:1, :] = new
            return carry

        lax.fori_loop(start, stop, step, 0)
        total = l_s[0:1, :]
        out = (acc_s[...] * (1.0 / total)).T
        for i in range(group):
            o_ref[:, HD * (kvh * group + i): HD * (kvh * group + i + 1)] = out[block_len * i: block_len * (i + 1), :].astype(jnp.bfloat16)
        lse_ref[kvh] = jnp.broadcast_to(m_s[0:1, :] + jnp.log2(total), (8, group * block_len))

def attend(ids, q, kv, seg_key, seg_query, block_len):
    blk_count, rows = kv.shape[:2]
    group = H // KVH
    chunk = 2 * block_len
    many = group * block_len
    return pl.pallas_call(
        functools.partial(attend_body, chunk),
        grid_spec=pltpu.PrefetchScalarGridSpec(
            num_scalar_prefetch=1, grid=(rows,),
            in_specs=[
                pl.BlockSpec((block_len, HQD), lambda r, ids: (r, 0)),
                pl.BlockSpec((blk_count, None, block_len, KVD), lambda r, ids: (0, r, 0, 0)),
                pl.BlockSpec((blk_count, None, block_len, KVD), lambda r, ids: (0, r, 0, 1)),
                pl.BlockSpec((None, blk_count * block_len, HD), lambda r, ids: (r, 0, 0)),
                pl.BlockSpec((None, 8, block_len), lambda r, ids: (r, 0, 0)),
            ],
            out_specs=[
                pl.BlockSpec((block_len, HQD), lambda r, ids: (r, 0)),
                pl.BlockSpec((None, KVH, 8, many), lambda r, ids: (r, 0, 0, 0)),
            ],
            scratch_shapes=[pltpu.VMEM((8, many), jnp.float32), pltpu.VMEM((8, many), jnp.float32), pltpu.VMEM((HD, many), jnp.float32)]),
        out_shape=[
            jax.ShapeDtypeStruct((rows * block_len, HQD), jnp.bfloat16),
            jax.ShapeDtypeStruct((rows, KVH, 8, many), jnp.float32),
        ],
        compiler_params=pltpu.CompilerParams(vmem_limit_bytes=VMEM),
        cost_estimate=SMALL_COST,
        name="attend",
    )(ids, q, kv, kv, seg_key, seg_query)

def turn_back(u, cosine, sine):
    lane = lax.broadcasted_iota(jnp.int32, u.shape, 1)
    other = pltpu.roll(u, HD // 2, 1)
    return u * cosine + jnp.where(lane < HD // 2, other, -other) * sine

def attend_back_body(chunk, ids, q_ref, k_ref, v_ref, seg_key_ref, seg_query_ref, o_ref, do_ref, lse_ref, cos_ref, sin_ref, dq_ref, dkv_ref, dq_s):
    block_len = q_ref.shape[0]
    group = H // KVH
    row = pl.program_id(0)
    per = chunk // block_len
    plain = HD ** (-0.5)
    scale = plain * LOG2E
    start = ids[1 + row] // per
    stop = ids[0] // per + 1
    dkv_ref[...] = jnp.zeros_like(dkv_ref)
    for kvh in range(KVH):
        q = stack_heads(q_ref, kvh, group)
        do = stack_heads(do_ref, kvh, group)
        o = stack_heads(o_ref, kvh, group)
        both = do.astype(jnp.float32) * o.astype(jnp.float32)
        delta = nt(jnp.ones((8, HD), jnp.float32), both, precision=lax.Precision.HIGHEST)[0:1, :]
        lse = lse_ref[kvh][0:1, :]
        dq_s[...] = jnp.zeros_like(dq_s)

        def step(c, carry):
            keys = ring_pair(k_ref, c, HD * kvh)
            vals = ring_pair(v_ref, c, HD * kvh)
            bias = hidden_from(seg_key_ref, seg_query_ref, c * chunk, chunk, block_len, ids[0])
            s = nt(keys, q) * scale + jnp.concatenate([bias] * group, axis=1)
            p = jnp.exp2(s - lse)
            dp = nt(vals, do)
            ds = (p * (dp - delta)).astype(jnp.bfloat16)
            dk = jnp.dot(ds, q, preferred_element_type=jnp.float32) * plain
            dv = jnp.dot(p.astype(jnp.bfloat16), do, preferred_element_type=jnp.float32)
            for at, part in ((HD * kvh, dk.astype(jnp.bfloat16)), (KVD + HD * kvh, dv.astype(jnp.bfloat16))):
                dkv_ref[c, :, at : at + HD] = part[:block_len]
                dkv_ref[dkv_ref.shape[0] - 1 - c, :, at : at + HD] = part[block_len:]
            dq_s[...] += tn(ds, keys)
            return carry

        lax.fori_loop(start, stop, step, 0)
        cosine, sine = cos_ref[...], sin_ref[...]
        for i in range(group):
            u = dq_s[block_len * i: block_len * (i + 1), :] * plain
            at = HD * (kvh * group + i)
            dq_ref[:, at: at + HD] = turn_back(u, cosine, sine).astype(jnp.bfloat16)

def attend_back(ids, q, kv, seg_key, seg_query, o, do, lse, cosine, sine, block_len):
    blk_count, rows = kv.shape[:2]
    group = H // KVH
    chunk = 2 * block_len
    many = group * block_len
    per_row = pl.BlockSpec((block_len, HQD), lambda r, ids: (r, 0))
    turn = pl.BlockSpec((block_len, HD), lambda r, ids: (r, 0))
    return pl.pallas_call(
        functools.partial(attend_back_body, chunk),
        grid_spec=pltpu.PrefetchScalarGridSpec(
            num_scalar_prefetch=1, grid=(rows,),
            in_specs=[
                per_row,
                pl.BlockSpec((blk_count, None, block_len, KVD), lambda r, ids: (0, r, 0, 0)),
                pl.BlockSpec((blk_count, None, block_len, KVD), lambda r, ids: (0, r, 0, 1)),
                pl.BlockSpec((None, blk_count * block_len, HD), lambda r, ids: (r, 0, 0)),
                pl.BlockSpec((None, 8, block_len), lambda r, ids: (r, 0, 0)),
                per_row, per_row,
                pl.BlockSpec((None, KVH, 8, many), lambda r, ids: (r, 0, 0, 0)),
                turn, turn,
            ],
            out_specs=[per_row, pl.BlockSpec((blk_count, None, block_len, 2 * KVD), lambda r, ids: (0, r, 0, 0))],
            scratch_shapes=[pltpu.VMEM((many, HD), jnp.float32)]),
        out_shape=[
            jax.ShapeDtypeStruct((rows * block_len, HQD), jnp.bfloat16),
            jax.ShapeDtypeStruct((blk_count, rows, block_len, 2 * KVD), jnp.bfloat16),
        ],
        compiler_params=pltpu.CompilerParams(vmem_limit_bytes=VMEM),
        cost_estimate=SMALL_COST,
        name="attend_back",
    )(ids, q, kv, kv, seg_key, seg_query, o, do, lse, cosine, sine)

def nn(a, b):
    return jnp.dot(a, b, preferred_element_type=jnp.float32)


def middle_body(add, order, h_ref, dy_ref, wg_ref, wu_ref, wd_ref, *refs):
    prev_ref = refs[0] if add else None
    hid_ref, dg_ref, du_ref, dh_ref = refs[-4:]
    h = h_ref[...]
    gate = nn(h, wg_ref[...])
    up = nn(h, wu_ref[...])
    sig = 1.0 / (1.0 + jnp.exp(-gate))
    silu = gate * sig
    hid_ref[...] = (silu * up).astype(jnp.bfloat16)
    dhid = nt(dy_ref[...], wd_ref[...])
    dg = (dhid * up * sig * (1.0 + gate * (1.0 - sig))).astype(jnp.bfloat16)
    du = (dhid * silu).astype(jnp.bfloat16)
    dg_ref[...] = dg
    du_ref[...] = du
    dh = nt(dg, wg_ref[...]) + nt(du, wu_ref[...])
    if add:
        dh = dh + prev_ref[...].astype(jnp.float32)
    dh_ref[...] = dh.astype(jnp.bfloat16)


def middle(order, h, dy, gate_up, wd, prev=None):
    count = h.shape[0]
    step = count // order.shape[0]
    wide_here = wd.shape[0]
    row = pl.BlockSpec((step, D), lambda i, order: (i, 0))
    placed = pl.BlockSpec((step, D), lambda i, order: (order[i], 0))
    part = pl.BlockSpec((step, wide_here), lambda i, order: (i, 0))
    part_placed = pl.BlockSpec((step, wide_here), lambda i, order: (order[i], 0))
    once = pl.Buffered(1)
    extra = [] if prev is None else [prev]
    return pl.pallas_call(
        functools.partial(middle_body, prev is not None),
        grid_spec=pltpu.PrefetchScalarGridSpec(
            num_scalar_prefetch=1,
            grid=(count // step,),
            in_specs=[
                placed,
                row,
                pl.BlockSpec((None, D, wide_here), lambda i, order: (0, 0, 0), pipeline_mode=once),
                pl.BlockSpec((None, D, wide_here), lambda i, order: (1, 0, 0), pipeline_mode=once),
                pl.BlockSpec((wide_here, D), lambda i, order: (0, 0), pipeline_mode=once),
            ]
            + [row] * len(extra),
            out_specs=[part, part_placed, part_placed, row],
        ),
        out_shape=[jax.ShapeDtypeStruct((count, wide_here), jnp.bfloat16)] * 3
        + [jax.ShapeDtypeStruct((count, D), jnp.bfloat16)],
        compiler_params=pltpu.CompilerParams(vmem_limit_bytes=VMEM),
        cost_estimate=SMALL_COST,
        name="middle",
    )(order, h, dy, gate_up, gate_up, wd, *extra)


def two_grads_body(h_ref, a_ref, b_ref, out_ref):
    h = h_ref[...]
    out_ref[0] = tn(h, a_ref[...]).astype(jnp.bfloat16)
    out_ref[1] = tn(h, b_ref[...]).astype(jnp.bfloat16)


def two_grads(h, a, b, step=256):
    count = h.shape[0]
    wide_here = a.shape[1]
    whole = pl.BlockSpec(a.shape, lambda i: (0, 0), pipeline_mode=pl.Buffered(1))
    return pl.pallas_call(
        two_grads_body,
        grid=(D // step,),
        in_specs=[pl.BlockSpec((count, step), lambda i: (0, i)), whole, whole],
        out_specs=pl.BlockSpec((2, step, wide_here), lambda i: (0, i, 0)),
        out_shape=jax.ShapeDtypeStruct((2, D, wide_here), jnp.bfloat16),
        compiler_params=pltpu.CompilerParams(vmem_limit_bytes=VMEM),
        cost_estimate=SMALL_COST,
        name="two_grads",
    )(h, a, b)


def down_grad_body(hid_ref, dy_ref, g_ref):
    g_ref[...] = tn(hid_ref[...], dy_ref[...]).astype(jnp.bfloat16)

def down_grad(hid, dy, step=512):
    T, F = hid.shape
    D = dy.shape[1]
    return pl.pallas_call(down_grad_body, grid=(D // step,),
        in_specs=[pl.BlockSpec((T, F), lambda i: (0, 0), pipeline_mode=pl.Buffered(1)), pl.BlockSpec((T, step), lambda i: (0, i))],
        out_specs=pl.BlockSpec((F, step), lambda i: (0, i)),
        out_shape=jax.ShapeDtypeStruct((F, D), jnp.bfloat16),
        compiler_params=pltpu.CompilerParams(vmem_limit_bytes=VMEM),
        cost_estimate=SMALL_COST,
        name="down_grad")(hid, dy)

def down_body(hid_a_ref, hid_b_ref, wd_a_ref, wd_b_ref, o_ref):
    out = nn(hid_a_ref[...], wd_a_ref[...]) + nn(hid_b_ref[...], wd_b_ref[...])
    o_ref[...] = out.astype(jnp.bfloat16)


def down(hid_a, hid_b, wd_a, wd_b, step):
    count = hid_a.shape[0]

    def rows(array):
        return pl.BlockSpec((step, array.shape[1]), lambda i: (i, 0))

    def whole(array):
        return pl.BlockSpec(array.shape, lambda i: (0, 0), pipeline_mode=pl.Buffered(1))

    return pl.pallas_call(
        down_body,
        grid=(count // step,),
        in_specs=[rows(hid_a), rows(hid_b), whole(wd_a), whole(wd_b)],
        out_specs=pl.BlockSpec((step, D), lambda i: (i, 0)),
        out_shape=jax.ShapeDtypeStruct((count, D), jnp.bfloat16),
        compiler_params=pltpu.CompilerParams(vmem_limit_bytes=VMEM),
        cost_estimate=SMALL_COST,
        name="down",
    )(hid_a, hid_b, wd_a, wd_b)


def turn(u, cosine, sine):
    lane = lax.broadcasted_iota(jnp.int32, u.shape, 1)
    other = pltpu.roll(u, HD // 2, 1)
    return u * cosine + jnp.where(lane < HD // 2, -other, other) * sine


def mix_body(
    blk_count, rows, small_count, ids, own_ref, cross_ref, core_ref, ring_ref, freq_ref,
    self_ref, near_ref, far_ref, one_ref, strip_ref, vector_ref,
):
    ring = ring_order(blk_count)
    wide_here = ring_ref.shape[-1]
    pieces = []
    for b in range(blk_count):
        at = ring.index(b)
        strip_ref[rows * b : rows * (b + 1)] = ring_ref[at, :rows]
        left = small_count
        line = rows
        while left > 0:
            size = min(left, wide_here)
            pieces.append(ring_ref[at, line : line + 1, :size].astype(jnp.float32))
            left -= size
            line += 1
    vector = jnp.concatenate(pieces, axis=1)
    vector_ref[...] = vector
    gain = vector[:, :D]
    grp = ids[0]
    strip_q = wide_here - HD
    bias = jnp.zeros((1, wide_here), jnp.float32)
    for k in range(4):
        kv_at = 2 * D + HQD + HD * (k // 2) + KVD * (k % 2)
        part = jnp.concatenate(
            [
                vector[:, 2 * D + strip_q * k : 2 * D + strip_q * (k + 1)],
                vector[:, kv_at : kv_at + HD],
            ],
            axis=1,
        )
        bias = bias + jnp.where(grp == k, part, 0.0)
    count = own_ref.shape[0]
    strip = strip_ref[...]
    for d in range(4):
        source = (own_ref[...], core_ref[0], cross_ref[...], core_ref[1])[d]
        x = source[:, :D].astype(jnp.float32)
        root = lax.rsqrt(jnp.mean(x * x, axis=1, keepdims=True) + NORM_EPS)
        one = (x * root * gain).astype(jnp.bfloat16)
        one_ref[count * d : count * (d + 1)] = one
        mixed = nn(one, strip) + bias
        digits = source[:, D : D + HD].astype(jnp.float32)
        position = 64.0 * digits[:, 0:1] + digits[:, 1:2]
        angles = position * freq_ref[...]
        cosine, sine = jnp.cos(angles), jnp.sin(angles)
        for i in range(wide_here // HD):
            c, s = cosine, sine
            if i == wide_here // HD - 1:
                c = jnp.where(grp % 2 == 1, 1.0, c)
                s = jnp.where(grp % 2 == 1, 0.0, s)
            at = HD * i
            out = turn(mixed[:, at : at + HD], c, s).astype(jnp.bfloat16)
            if d == 0:
                self_ref[:, at : at + HD] = out
            elif d == 1:
                near_ref[:, at : at + HD] = out
            else:
                far_ref[d - 2, :, at : at + HD] = out


def mix(ids, own, cross, core, ring, freq, blk_count, rows, small_count):
    count = own.shape[0]
    wide_here = ring.shape[-1]
    low16 = jnp.bfloat16
    return pl.pallas_call(
        functools.partial(mix_body, blk_count, rows, small_count),
        in_specs=[pl.BlockSpec(memory_space=pltpu.SMEM)] + [pl.BlockSpec(memory_space=pltpu.VMEM)] * 5,
        out_specs=[pl.BlockSpec(memory_space=pltpu.VMEM)] * 6,
        out_shape=[
            jax.ShapeDtypeStruct((count, wide_here), low16),
            jax.ShapeDtypeStruct((count, wide_here), low16),
            jax.ShapeDtypeStruct((2, count, wide_here), low16),
            jax.ShapeDtypeStruct((4 * count, D), low16),
            jax.ShapeDtypeStruct((D, wide_here), low16),
            jax.ShapeDtypeStruct((1, blk_count * small_count), jnp.float32),
        ],
        compiler_params=pltpu.CompilerParams(vmem_limit_bytes=VMEM),
        cost_estimate=SMALL_COST,
        name="mix",
    )(ids, own, cross, core, ring, freq)


def pack_body(ids, self_ref, cross_ref, core_ref, q_ref, kv_ref):
    strip_q = self_ref.shape[1] - HD
    for g in range(4):

        @pl.when(ids[0] == g)
        def _(g=g):
            for k in range(4):
                part = (self_ref[...], core_ref[0], cross_ref[0], core_ref[1])[g ^ k]
                q_ref[:, strip_q * k : strip_q * (k + 1)] = part[:, :strip_q]
                at = (k % 2) * KVD + (k // 2) * HD
                kv_ref[:, at : at + HD] = part[:, strip_q:]


def pack(ids, own, cross, core):
    count = own.shape[0]
    return pl.pallas_call(
        pack_body,
        in_specs=[pl.BlockSpec(memory_space=pltpu.SMEM)] + [pl.BlockSpec(memory_space=pltpu.VMEM)] * 3,
        out_specs=[pl.BlockSpec(memory_space=pltpu.VMEM)] * 2,
        out_shape=[
            jax.ShapeDtypeStruct((count, HQD), jnp.bfloat16),
            jax.ShapeDtypeStruct((count, 2 * KVD), jnp.bfloat16),
        ],
        compiler_params=pltpu.CompilerParams(vmem_limit_bytes=VMEM),
        cost_estimate=SMALL_COST,
        name="pack",
    )(ids, own, cross, core)


def turn_dkv_body(ids, dkv_ref, cos_ref, sin_ref, self_ref, near_ref, far_ref, sum_ref):
    items = []
    sums = [None] * 4
    for k in range(4):
        at = (k % 2) * KVD + (k // 2) * HD
        part = dkv_ref[:, at : at + HD]
        if k % 2 == 0:
            part = turn_back(part.astype(jnp.float32), cos_ref[...], sin_ref[...]).astype(jnp.bfloat16)
        items.append(part)
        sums[(k % 2) * 2 + k // 2] = jnp.sum(part.astype(jnp.float32), axis=0, keepdims=True)
    sum_ref[...] = jnp.concatenate(sums, axis=1)
    for g in range(4):

        @pl.when(ids[0] == g)
        def _(g=g):
            self_ref[...] = items[g]
            near_ref[...] = items[g ^ 1]
            far_ref[0] = items[g ^ 2]
            far_ref[1] = items[g ^ 3]


def turn_dkv(ids, dkv, cosine, sine):
    count = dkv.shape[0]
    return pl.pallas_call(
        turn_dkv_body,
        in_specs=[pl.BlockSpec(memory_space=pltpu.SMEM)] + [pl.BlockSpec(memory_space=pltpu.VMEM)] * 3,
        out_specs=[pl.BlockSpec(memory_space=pltpu.VMEM)] * 4,
        out_shape=[
            jax.ShapeDtypeStruct((count, HD), jnp.bfloat16),
            jax.ShapeDtypeStruct((count, HD), jnp.bfloat16),
            jax.ShapeDtypeStruct((2, count, HD), jnp.bfloat16),
            jax.ShapeDtypeStruct((1, 2 * KVD), jnp.float32),
        ],
        compiler_params=pltpu.CompilerParams(vmem_limit_bytes=VMEM),
        cost_estimate=SMALL_COST,
        name="turn_dkv",
    )(ids, dkv, cosine, sine)


def kv_grad_body(
    blk_count, rows, small_count, self_ref, cross_ref, core_ref, dq_ref, one_ref, own_ref, near_x_ref,
    core_x_ref, strip_ref, gain_two_ref, bias_q_ref, bias_kv_ref, grad_ref, here_ref, there_ref,
):
    count = self_ref.shape[0]
    strip_q = strip_ref.shape[1] - HD
    parts = (self_ref[...], core_ref[0], cross_ref[0], core_ref[1])
    near = jnp.concatenate(parts, axis=0)
    grad = tn(one_ref[...], near)
    gain_one = jnp.zeros((1, D), jnp.float32)
    for d in range(4):
        x = (own_ref[...], core_x_ref[0], near_x_ref[...], core_x_ref[1])[d][:, :D].astype(jnp.float32)
        root = lax.rsqrt(jnp.mean(x * x, axis=1, keepdims=True) + NORM_EPS)
        hone = nt(dq_ref[count * d : count * (d + 1)], strip_ref[:, :strip_q])
        hone = hone + nt(parts[d], strip_ref[:, strip_q:])
        gain_one = gain_one + jnp.sum(hone * x * root, axis=0, keepdims=True)
        out_ref = (here_ref, there_ref)[d % 2]
        out_ref[count * (d // 2) : count * (d // 2 + 1)] = hone.astype(jnp.bfloat16)
    vector = jnp.concatenate([gain_one, gain_two_ref[...], bias_q_ref[...], bias_kv_ref[...]], axis=1)
    extra = grad_ref.shape[1] - rows
    for b in range(blk_count):
        grad_ref[b, :rows] = grad[rows * b : rows * (b + 1)].astype(jnp.bfloat16)
        lines = []
        for line in range(extra):
            size = min(HD, max(small_count - line * HD, 0))
            begin = small_count * b + line * HD
            pieces = [vector[:, begin : begin + size]] if size > 0 else []
            if size < HD:
                pieces.append(jnp.zeros((1, HD - size), jnp.float32))
            lines.append(pieces[0] if len(pieces) == 1 else jnp.concatenate(pieces, axis=1))
        grad_ref[b, rows:] = jnp.concatenate(lines, axis=0).astype(jnp.bfloat16)


def kv_grad_rows(rows, small_count):
    needed = rows + -(-small_count // HD)
    return needed + -needed % 16


def make_kv_grad(blk_count, rows, small_count, own, cross, core, dq, one, x_own, x_cross, x_core, strip, gain_two, bias_q, bias_kv):
    count = own.shape[0]
    height = kv_grad_rows(rows, small_count)
    return pl.pallas_call(
        functools.partial(kv_grad_body, blk_count, rows, small_count),
        in_specs=[pl.BlockSpec(memory_space=pltpu.VMEM)] * 12,
        out_specs=[pl.BlockSpec(memory_space=pltpu.VMEM)] * 3,
        out_shape=[
            jax.ShapeDtypeStruct((blk_count, height, HD), jnp.bfloat16),
            jax.ShapeDtypeStruct((2 * count, D), jnp.bfloat16),
            jax.ShapeDtypeStruct((2 * count, D), jnp.bfloat16),
        ],
        compiler_params=pltpu.CompilerParams(vmem_limit_bytes=VMEM),
        cost_estimate=SMALL_COST,
        name="kv_grad",
    )(own, cross, core, dq, one, x_own, x_cross, x_core, strip, gain_two, bias_q, bias_kv)


CORE = [(0, 1), (1, 0), (2, 3), (3, 2)]
CROSS = [(0, 2), (2, 0), (1, 3), (3, 1)]
DIAG = [(0, 3), (3, 0), (1, 2), (2, 1)]


def low(values):
    return values.astype(jnp.bfloat16)


def wide(values):
    return values.astype(jnp.float32)


def swap_core(values):
    return lax.ppermute(values, "grp", CORE)


def swap_cross(values):
    return lax.ppermute(values, "grp", CROSS)


def swap_diag(values):
    return lax.ppermute(values, "grp", DIAG)


def swap_blk(values, bit):
    count = lax.axis_size("blk")
    return lax.ppermute(values, "blk", [(i, i ^ bit) for i in range(count)])


def blk_bit(bit):
    return (lax.axis_index("blk") & bit) != 0


def bits_of(count):
    out = []
    bit = count // 2
    while bit >= 1:
        out.append(bit)
        bit //= 2
    return out


def gather_bits(values, order):
    done = []
    for bit in order:
        other = swap_blk(values, bit)
        mine = blk_bit(bit)
        axis = sum(1 for d in done if d > bit)
        values = jnp.stack(
            [jnp.where(mine, other, values), jnp.where(mine, values, other)], axis=axis
        )
        done.append(bit)
    return values


def scatter_bits(values, axes, order):
    axes = list(axes)
    for bit in order:
        axis = axes.index(bit)
        mine = blk_bit(bit).astype(jnp.int32)
        keep = lax.dynamic_index_in_dim(values, mine, axis, keepdims=False)
        send = lax.dynamic_index_in_dim(values, 1 - mine, axis, keepdims=False)
        values = low(wide(keep) + wide(swap_blk(send, bit)))
        axes.remove(bit)
    return values


def by_place(parts):
    grp = lax.axis_index("grp")
    core = (grp & 1) != 0
    cross = (grp & 2) != 0
    a, b, c, d = parts
    a, b = jnp.where(core, b, a), jnp.where(core, a, b)
    c, d = jnp.where(core, d, c), jnp.where(core, c, d)
    a, c = jnp.where(cross, c, a), jnp.where(cross, a, c)
    b, d = jnp.where(cross, d, b), jnp.where(cross, b, d)
    return [a, b, c, d]


def gather_near(values):
    cross = swap_cross(values)
    both = swap_core(jnp.stack([values, cross]))
    return [values, both[0], cross, both[1]]


def gather_grp(values):
    return by_place(gather_near(values))


def gather_tokens(values, bit):
    half = values.shape[0] // 2
    cross = swap_cross(values)
    over = swap_blk(values, bit)
    first = swap_blk(cross[:half], bit)
    second = swap_cross(over[half:])
    chip = jnp.concatenate([values, cross, over, first, second])
    return jnp.concatenate([chip, swap_core(chip)])


def angles_of(position):
    half = HD // 2
    freqs = ROPE_BASE ** (-2.0 * jnp.arange(half, dtype=jnp.float32) / HD)
    return position.astype(jnp.float32)[:, None] * freqs[None, :]


def rotate_by(values, cosine, sine):
    half = HD // 2
    first_half = values[..., :half]
    second_half = values[..., half:]
    return jnp.concatenate(
        [first_half * cosine - second_half * sine, second_half * cosine + first_half * sine],
        axis=-1,
    )


def after(values, anchor):
    return lax.optimization_barrier((values, anchor))[0]


def gather_step(values, done, bit):
    other = swap_blk(values, bit)
    mine = blk_bit(bit)
    axis = sum(1 for d in done if d > bit)
    return jnp.stack(
        [jnp.where(mine, other, values), jnp.where(mine, values, other)], axis=axis
    )


def gather_near_stacked(values):
    both = jnp.stack([values, swap_cross(values)])
    return jnp.concatenate([both, swap_core(both)])


def ring_groups(count):
    return [[g * count + b for b in ring_order(count)] for g in range(4)]


def gather_ring(values):
    count = lax.axis_size("blk")
    return lax.all_gather(values, ("grp", "blk"), axis=0, axis_index_groups=ring_groups(count))


def exchange_near(parts):
    cross = swap_cross(jnp.stack([parts[2], parts[3]]))
    core = swap_core(jnp.stack([parts[1], cross[1]]))
    return [parts[0], core[0], cross[0], core[1]]


def on_device(
    tokens,
    cotangent,
    segment_ids,
    position_ids,
    w_attend,
    w_out,
    w_gate,
    w_up,
    w_down,
    small_params,
    first_attend,
    first_out,
    first_gate,
    first_up,
    first_down,
    first_small,
    second_attend,
    second_out,
    second_gate,
    second_up,
    second_down,
    second_small,
):
    rows_here, block_len = tokens.shape[:2]
    blk_count = lax.axis_size("blk")
    seq_len = block_len * blk_count
    token_count = rows_here * block_len
    grp = lax.axis_index("grp")
    blk = lax.axis_index("blk")
    cross_id, core_id = grp // 2, grp % 2
    strip_heads = H // 4
    strip_q = strip_heads * HD
    bits = bits_of(blk_count)
    team = blk_count // 4
    lows = [bit for bit in bits if bit < team]
    spread = [bits[0]] + lows
    low_shape = (2,) * len(lows)
    in_team = blk_bit(team).astype(jnp.int32)
    weight_rows = w_gate.shape[0]
    ff_block = w_down.shape[0]
    quarter = ff_block // 4
    widths = [size * blk_count // 2 for at, size in halves_of(quarter)]
    chip_rows = 4 * token_count
    half = token_count // 2

    ids = jnp.stack([grp, in_team])
    flat_low = tokens.reshape(token_count, D)
    dy_low = cotangent.reshape(token_count, D)
    positions = position_ids.reshape(token_count)
    kv_at = HQD + HD * cross_id + KVD * core_id
    strip_local = low(
        jnp.concatenate(
            [
                lax.dynamic_slice_in_dim(w_attend, strip_q * grp, strip_q, 1),
                lax.dynamic_slice_in_dim(w_attend, kv_at, HD, 1),
            ],
            axis=1,
        )
    )
    small_count = small_params.shape[0]
    small_send = jnp.concatenate([low(small_params), low(segment_ids.reshape(token_count))])
    strip_wide = strip_q + HD
    small_send = jnp.pad(small_send, (0, -small_send.shape[0] % (16 * strip_wide)))
    strip_local = jnp.concatenate([strip_local, small_send.reshape(-1, strip_wide)])
    ring = ring_order(blk_count)
    strip_ring = gather_ring(strip_local)
    small_ring = strip_ring[:, weight_rows:].reshape(blk_count, -1)[:, small_count : small_count + token_count]
    small_all = jnp.stack([small_ring[ring.index(b)] for b in range(blk_count)])
    digits = low(jnp.stack([positions // 64, positions % 64], axis=1))
    digits = jnp.pad(digits, ((0, 0), (0, HD - 2)))
    token_send = jnp.concatenate([flat_low, digits], axis=1)
    picked_a, picked_b = pick_columns(ids, w_gate, w_up, blk_count)
    token_cross = after(swap_cross(token_send), (picked_a, strip_ring))
    dy_over = swap_blk(after(dy_low, token_cross), team)
    dy_cross = swap_cross(after(dy_low, token_cross))

    def place(values, other, done, bit, lead=0):
        mine = blk_bit(bit)
        axis = lead + sum(1 for d in done if d > bit)
        return jnp.stack(
            [jnp.where(mine, other, values), jnp.where(mine, values, other)], axis=axis
        )

    mine_team = blk_bit(team)
    (low_first, size_first), (low_second, size_second) = halves_of(quarter)

    def team_pair(mine, got):
        return jnp.stack(
            [jnp.where(mine_team, got, mine), jnp.where(mine_team, mine, got)], axis=1
        )

    out_local = low(lax.dynamic_slice_in_dim(w_out, strip_q * grp, strip_q, 1))
    out_ring = gather_ring(after(out_local, strip_ring))
    down_here = low(lax.dynamic_slice_in_dim(w_down, quarter * grp, quarter, 0))
    token_core = swap_core(jnp.stack([token_send, token_cross]))
    freqs = ROPE_BASE ** (-2.0 * jnp.arange(HD // 2, dtype=jnp.float32) / HD)
    freqs = jnp.concatenate([freqs, freqs])[None]
    mixed_own, mixed_core, mixed_far, near_one, strip, vector = mix(
        ids, token_send, token_cross, token_core, strip_ring, freqs, blk_count, weight_rows, small_count
    )
    vector = vector[0]
    gain_one = vector[:D]
    gain_two = vector[D : 2 * D]
    seg_all = small_all.astype(jnp.int32)
    seg_all = seg_all.reshape(blk_count, rows_here, block_len)
    seg_key = jnp.broadcast_to(
        seg_all.transpose(1, 0, 2).reshape(rows_here, seq_len)[:, :, None], (rows_here, seq_len, HD)
    )
    seg_query = jnp.broadcast_to(segment_ids[:, None, :], (rows_here, 8, block_len))
    first_blk = jnp.sum((seg_all[:, :, -1] < segment_ids[None, :, 0]).astype(jnp.int32), axis=0)
    attend_ids = jnp.concatenate([blk[None], first_blk])

    mixed_cross = swap_cross(mixed_far)
    mixed_core = swap_core(jnp.stack([mixed_core, mixed_cross[1]]))
    got_a = swap_blk(picked_a[1], team)
    mixed_core = after(mixed_core, got_a)
    query, packed_kv = pack(ids, mixed_own, mixed_cross, mixed_core)
    key_value = packed_kv.reshape(rows_here, block_len, 2 * KVD)
    kv_all = gather_ring(key_value)

    teams = [
        [g * blk_count + (i | t) for g in range(4) for t in (0, team)]
        for i in range(blk_count)
        if not i & team
    ]
    order = jnp.stack(
        [
            (grp ^ (2 * (i & 1) + (i >> 2))) * 2 + (in_team ^ ((i >> 1) & 1))
            for i in range(8)
        ]
    )

    peers = [[i for i in range(blk_count) if (i & team) == t] for t in (0, team)]

    def lows_of(values, done, lead=0, anchor=None):
        for bit in lows:
            got = swap_blk(values, bit)
            if anchor is not None:
                got = after(got, anchor)
            values = place(values, got, done, bit, lead)
            done = done + [bit]
        return values

    got_b = swap_blk(after(picked_b[1], mixed_own), team)
    dy_cross, dy_over = after((dy_cross, dy_over), packed_kv)
    pair_a = team_pair(picked_a[0], after(got_a, packed_kv))
    kv_all = after(kv_all, (got_b, dy_cross, dy_over))
    pair_a = after(pair_a, kv_all)
    pair_a_got = swap_blk(pair_a, bits[0])
    dy_first = swap_blk(dy_cross[:half], team)
    dy_second = swap_cross(dy_over[half:])
    dy_chip = jnp.concatenate([dy_low, dy_cross, dy_over, dy_first, dy_second])
    dy_team = jnp.concatenate([dy_chip, swap_core(dy_chip)])
    pair_a = place(pair_a, pair_a_got, [team], bits[0], 1)
    gate_up_a = lows_of(pair_a, [bits[0], team], 1).reshape(2, D, -1)
    pair_b = team_pair(picked_b[0], got_b)
    pair_b_got = swap_blk(after(pair_b, pair_a_got), bits[0])
    out_ring = after(out_ring, packed_kv)
    out_strip = jnp.concatenate([out_ring[ring.index(b)] for b in range(blk_count)])
    out_cross = swap_cross(out_strip)
    out_core = swap_core(jnp.stack([out_strip, after(out_cross, kv_all)]))
    out_full = jnp.concatenate(by_place([out_strip, out_core[0], out_cross, out_core[1]]), axis=1)

    att_in, lse = attend(attend_ids, query, kv_all, seg_key, seg_query, block_len)
    flat = wide(flat_low)
    resid = flat + jnp.dot(att_in, out_full, preferred_element_type=jnp.float32)
    h_two = low(norm_apply(resid, gain_two))
    h_two = after(h_two, pair_a_got)
    down_got = after(swap_blk(after(down_here, kv_all), bits[0]), h_two)
    down_here = place(down_here, down_got, [], bits[0])
    down_here = lows_of(down_here, [bits[0]]).reshape(2 * blk_count // 4, quarter, D)
    down_a = down_here[:, :size_first].reshape(widths[0], D)
    down_b = down_here[:, size_first:].reshape(widths[1], D)
    h_team = lax.all_gather(h_two, ("grp", "blk"), axis=0, tiled=True, axis_index_groups=teams)
    pair_b_got = after(pair_b_got, (h_two, gate_up_a))
    pair_b = place(pair_b, pair_b_got, [team], bits[0], 1)
    h_team = after(h_team, (gate_up_a, pair_b, dy_team))
    hidden_a, d_gate_a, d_up_a, part_a = middle(order, h_team, dy_team, gate_up_a, down_a)
    gate_up_b = lows_of(pair_b, [bits[0], team], 1, hidden_a).reshape(2, D, -1)
    down_grad_a = down_grad(after(hidden_a, gate_up_b), dy_team)
    down_share_a = lax.psum_scatter(
        down_grad_a, "blk", scatter_dimension=0, axis_index_groups=peers, tiled=True
    )
    column_grad_a = two_grads(h_team, d_gate_a, d_up_a)

    def part_sent(values, axis, bit):
        mine = blk_bit(bit).astype(jnp.int32)
        keep = lax.dynamic_index_in_dim(values, mine, axis, keepdims=False)
        send = lax.dynamic_index_in_dim(values, 1 - mine, axis, keepdims=False)
        return keep, swap_blk(send, bit)

    def part_sum(keep, got):
        return low(wide(keep) + wide(got))

    def columns_first(grad):
        grad = grad.reshape((2, 2, 2) + low_shape + (weight_rows, -1))
        return part_sent(grad, 2 + len(lows), lows[-1])

    def columns_mid(keep, got):
        values = part_sum(keep, got)
        for i in range(len(lows) - 2, -1, -1):
            values = part_sum(*part_sent(values, 3 + i, lows[i]))
        return values

    def columns_third(keep, got):
        values = part_sum(keep, got)
        mine = lax.dynamic_index_in_dim(values, in_team, 1, keepdims=False)
        send = lax.dynamic_index_in_dim(values, 1 - in_team, 1, keepdims=False)
        return values, (mine, swap_blk(send, team))

    def rows_second(keep, got):
        values = part_sum(keep, got)
        for i in range(len(lows) - 2, -1, -1):
            values = part_sum(*part_sent(values, 1 + i, lows[i]))
        return part_sent(values, 0, bits[0])

    def columns_last(mine, got):
        return jnp.stack(
            [jnp.where(mine_team, got, mine), jnp.where(mine_team, mine, got)], axis=1
        )

    first_a = columns_first(column_grad_a)
    hidden_b, d_gate_b, d_up_b, d_htwo_part = middle(
        order, after(h_team, (column_grad_a, down_grad_a)), dy_team, gate_up_b, down_b, part_a
    )

    def chip_sum(values, came):
        return low(wide(values[:chip_rows]) + wide(came))

    def scatter_far(chip):
        far = chip[3 * token_count :]
        return swap_blk(far[:half], team), swap_cross(far[half:])

    def scatter_near(chip, first, second):
        cross, over = (chip[token_count * i : token_count * (i + 1)] for i in (1, 2))
        cross = jnp.concatenate([low(wide(cross[:half]) + wide(first)), cross[half:]])
        over = jnp.concatenate([over[:half], low(wide(over[half:]) + wide(second))])
        return swap_cross(cross), swap_blk(over, team)

    near_att_cross = swap_cross(after(att_in, hidden_a))
    d_htwo_part = after(d_htwo_part, (first_a[1], down_share_a, near_att_cross))
    d_came = swap_core(d_htwo_part[chip_rows:])
    down_grad_b = down_grad(hidden_b, dy_team)
    rows_b = part_sent(
        down_grad_b.reshape((2,) + low_shape + (size_second, D)), len(lows), lows[-1]
    )
    mid_a = columns_mid(*after(first_a, d_came))
    second_a = part_sent(mid_a, 1, bits[0])
    d_chip = chip_sum(d_htwo_part, after(d_came, down_grad_b))
    d_far = scatter_far(d_chip)
    column_grad_b = two_grads(h_team, *after((d_gate_b, d_up_b), d_chip))
    first_b = columns_first(column_grad_b)
    d_far = after(d_far, column_grad_b)
    d_cross, d_over = scatter_near(d_chip, *d_far)
    out_part = down(*after((hidden_a, hidden_b), d_far), down_a, down_b, token_count)
    out_came = swap_core(out_part[chip_rows:])
    d_cross, d_over = after((d_cross, d_over), out_part)
    d_htwo = wide(d_chip[:token_count]) + wide(d_cross) + wide(d_over)

    norm_value_two, norm_back_two = jax.vjp(norm_apply, resid, gain_two)
    d_resid_norm, grad_gain_two = norm_back_two(d_htwo)
    d_resid = wide(dy_low) + d_resid_norm
    d_att = low(d_resid)
    rows_b = rows_second(*after(rows_b, d_att))

    d_attended = low(right_transposed(d_att, out_full))
    own_angles = angles_of(positions)
    cosine, sine = jnp.cos(own_angles), jnp.sin(own_angles)
    d_query, dkv = attend_back(
        attend_ids,
        query,
        kv_all,
        seg_key,
        seg_query,
        att_in,
        d_attended,
        lse,
        jnp.concatenate([cosine, cosine], axis=1),
        jnp.concatenate([sine, sine], axis=1),
        block_len,
    )
    dkv = lax.psum_scatter(
        dkv.reshape(blk_count * token_count, 2 * KVD),
        ("grp", "blk"),
        scatter_dimension=0,
        axis_index_groups=ring_groups(blk_count),
        tiled=True,
    )
    down_share_b = part_sum(*after(rows_b, d_query))
    sum_a, third_a = columns_third(*after(second_a, d_att))

    def to_strips(parts):
        return jnp.concatenate(exchange_near(by_place(parts)))

    near_dq = to_strips([d_query[:, strip_q * k : strip_q * (k + 1)] for k in range(4)])
    block_shape = (2,) * len(bits) + (weight_rows, -1)
    query_grad = low(left_product(near_one, near_dq)).reshape(block_shape)
    steps_query = part_sent(query_grad, len(bits) - 1, bits[-1])
    near_a = gather_near_stacked(columns_last(*after(third_a, d_query)))
    second_b = part_sent(columns_mid(*after(first_b, d_query)), 1, bits[0])
    dkv = after(dkv, (query_grad, down_share_b))
    own_part, core_part, far_part, bias_kv = turn_dkv(
        ids, dkv, jnp.concatenate([cosine, cosine], axis=1), jnp.concatenate([sine, sine], axis=1)
    )
    bias_q = jnp.sum(wide(d_query), axis=0)
    d_key = own_part
    cross_part = swap_cross(far_part)
    core_part = swap_core(jnp.stack([core_part, cross_part[1]]))
    kv_grad, hone_here, hone_there = make_kv_grad(
        blk_count,
        weight_rows,
        small_count,
        own_part,
        cross_part,
        core_part,
        near_dq,
        near_one,
        token_send,
        token_cross,
        token_core,
        strip,
        grad_gain_two[None],
        bias_q[None],
        bias_kv,
    )
    vector_rows = -(-small_count // HD)
    kv_grad = kv_grad.reshape((2,) * len(bits) + kv_grad.shape[1:])
    steps_kv = part_sent(kv_grad, len(bits) - 1, bits[-1])
    share_down = after(jnp.concatenate([down_share_a, down_share_b]), dkv)
    grad_down = lax.all_gather(share_down, "grp", axis=0, tiled=True)
    for i in range(len(bits) - 2, -1, -1):
        steps_query = part_sent(part_sum(*after(steps_query, d_key)), i, bits[i])
        kv_sum = part_sum(*steps_kv)
        kv_grad = kv_sum
        steps_kv = part_sent(kv_sum, i, bits[i])
    sum_b, third_b = columns_third(*after(second_b, kv_grad))
    share_kv_all = wide(steps_kv[0]) + wide(after(steps_kv[1], (near_a, third_b[1])))
    share_kv = low(share_kv_all[:weight_rows])
    vector_part = share_kv_all[weight_rows : weight_rows + vector_rows]
    share_query = part_sum(*after(steps_query, kv_grad))
    near_att = swap_core(jnp.stack([att_in, near_att_cross]))
    near_att = jnp.concatenate([att_in, near_att[0], near_att_cross, near_att[1]])
    near_datt = to_strips([d_att[:, strip_q * k : strip_q * (k + 1)] for k in range(4)])
    out_grad = low(left_product(near_att, after(near_datt, d_attended))).reshape(block_shape)
    steps_out = part_sent(out_grad, len(bits) - 1, bits[-1])
    anchors = [near_dq, near_dq]
    for i in range(len(bits) - 2, -1, -1):
        anchor = anchors[min(len(bits) - 2 - i, 1)]
        steps_out = part_sent(part_sum(*after(steps_out, anchor)), i, bits[i])
    share_out = part_sum(*after(steps_out, kv_grad))

    own_b = columns_last(*third_b)
    cross_b = swap_cross(own_b)
    near_b = jnp.stack([own_b, cross_b])
    near_b = jnp.concatenate([near_b, swap_core(near_b)])
    grad_out = jnp.concatenate(gather_grp(share_out), axis=1)
    query_parts = gather_grp(share_query)
    key_parts = gather_grp(share_kv)
    grad_attend = jnp.concatenate(query_parts + [key_parts[k] for k in (0, 2, 1, 3)], axis=1)

    other = wide(swap_core(hone_there))
    d_hone = wide(hone_here[:token_count]) + other[:token_count]
    d_hone_cross = swap_cross(low(wide(hone_here[token_count:]) + other[token_count:]))
    square_sum = square_total(
        [
            wide(s)
            for s in (share_query, share_kv, share_out, sum_a, sum_b, share_down)
        ]
    )
    packed = jnp.concatenate([vector_part, jnp.full((8, HD), square_sum)])
    packed = packed + swap_cross(packed)
    packed = packed + swap_core(packed)
    share_vector = packed[:vector_rows].reshape(-1)[:small_count]
    square_sum = packed[vector_rows:] + jnp.sum(share_vector * share_vector)
    for bit in bits:
        square_sum = square_sum + swap_blk(square_sum, bit)
    grad_norm = jnp.sqrt(square_sum[0, 0])
    factor = jnp.minimum(1.0, CLIP_NORM / (grad_norm + 1e-06))
    out_chip = chip_sum(out_part, after(out_came, kv_grad))
    out_far = scatter_far(out_chip)
    factor = after(factor, (out_chip, cross_b))

    new_first_gate, new_second_gate, new_gate = adam_columns(
        0, ids, factor[None], near_a, near_b, w_gate, first_gate, second_gate, blk_count, RATE_GATE, WEIGHT_DECAY
    )
    new_first_up, new_second_up, new_up = adam_columns(
        1, ids, factor[None], near_a, near_b, w_up, first_up, second_up, blk_count, RATE_GATE, WEIGHT_DECAY
    )
    norm_value_one, norm_back_one = jax.vjp(norm_apply, flat, gain_one)
    d_hone = after(d_hone + wide(after(d_hone_cross, new_gate)), new_gate)
    d_flat_norm, unused_gain = norm_back_one(d_hone)
    grad_tokens = low(d_resid + d_flat_norm)

    new_first_attend, new_second_attend, new_attend = adam_step(
        w_attend, factor * wide(grad_attend), first_attend, second_attend, RATE_ATTEND, WEIGHT_DECAY
    )
    new_first_out, new_second_out, new_out = adam_step(
        w_out, factor * wide(grad_out), first_out, second_out, RATE_OUT, WEIGHT_DECAY
    )
    new_first_down, new_second_down, new_down = adam_step(
        w_down, factor * wide(grad_down), first_down, second_down, RATE_DOWN, WEIGHT_DECAY
    )
    new_first_small, new_second_small, new_small = adam_step(
        small_params, factor * share_vector, first_small, second_small, RATE_VECTOR, 0.0
    )

    out_near = after(scatter_near(out_chip, *after(out_far, factor)), (new_gate, new_up))
    out_tokens = low(resid + wide(out_chip[:token_count]) + wide(out_near[0]) + wide(out_near[1]))
    return (
        out_tokens.reshape(rows_here, block_len, D),
        grad_tokens.reshape(rows_here, block_len, D),
        grad_norm,
        new_first_attend,
        new_second_attend,
        new_attend,
        new_first_out,
        new_second_out,
        new_out,
        new_first_gate,
        new_second_gate,
        new_gate,
        new_first_up,
        new_second_up,
        new_up,
        new_first_down,
        new_second_down,
        new_down,
        new_first_small,
        new_second_small,
        new_small,
    )


def solution(mesh):
    placed = (
        P("grp", "blk", None),
        P("grp", "blk", None),
        P("grp", "blk"),
        P("grp", "blk"),
        P("blk", None),
        P("blk", None),
        P("blk", None),
        P("blk", None),
        P("blk", None),
        P("blk"),
        P("blk", None),
        P("blk", None),
        P("blk", None),
        P("blk", None),
        P("blk", None),
        P("blk"),
        P("blk", None),
        P("blk", None),
        P("blk", None),
        P("blk", None),
        P("blk", None),
        P("blk"),
    )
    return jax.shard_map(
        on_device,
        mesh=mesh,
        in_specs=placed,
        out_specs=(
            P("grp", "blk", None),
            P("grp", "blk", None),
            P(),
            P("blk", None),
            P("blk", None),
            P("blk", None),
            P("blk", None),
            P("blk", None),
            P("blk", None),
            P("blk", None),
            P("blk", None),
            P("blk", None),
            P("blk", None),
            P("blk", None),
            P("blk", None),
            P("blk", None),
            P("blk", None),
            P("blk", None),
            P("blk"),
            P("blk"),
            P("blk"),
        ),
        check_vma=False,
    )
```

```python
import functools

import jax
import jax.numpy as jnp
from jax import lax
from jax.experimental import pallas as pl
from jax.experimental.pallas import tpu as pltpu
from jax.sharding import PartitionSpec as P

D = 1536
FF = 8960
H = 12
KVH = 2
HD = 128
STEP = 10
HQD = 1536
KVD = 256


NORM_EPS = 1e-06
ROPE_BASE = 10000.0
CLIP_NORM = 1.0
BETA_FIRST = 0.9
BETA_SECOND = 0.95
ADAM_EPS = 1e-08
WEIGHT_DECAY = 0.1
RATE_ATTEND = 0.06
RATE_OUT = 0.5
RATE_GATE = 0.06
RATE_DOWN = 0.03
RATE_VECTOR = 0.5
NEG_LARGE = -1e30
LOG2E = 1.4426950408889634
VMEM = 48 * 1024 * 1024
SMALL_COST = pl.CostEstimate(flops=1000, bytes_accessed=1000, transcendentals=0)


def norm_apply(values, gain):
    return values * lax.rsqrt(jnp.mean(values * values, axis=-1, keepdims=True) + NORM_EPS) * gain


def swish_product(gate, up_proj):
    return jax.nn.silu(gate) * up_proj


def left_product(left_side, right_side):
    return lax.dot_general(
        left_side, right_side, (((0,), (0,)), ((), ())), preferred_element_type=jnp.float32
    )


def right_transposed(left_side, right_side):
    return lax.dot_general(
        left_side, right_side, (((1,), (1,)), ((), ())), preferred_element_type=jnp.float32
    )


def square_total(arrays):
    return sum((jnp.sum(member * member) for member in arrays))


def adam_step(weight, grad, first, second, rate, decay):
    first_new = BETA_FIRST * first + (1.0 - BETA_FIRST) * grad
    second_new = BETA_SECOND * second + (1.0 - BETA_SECOND) * grad * grad
    first_hat = first_new / (1.0 - BETA_FIRST**STEP)
    second_hat = second_new / (1.0 - BETA_SECOND**STEP)
    weight_new = weight - rate * (first_hat / (jnp.sqrt(second_hat) + ADAM_EPS) + decay * weight)
    return (first_new, second_new, weight_new)


def ring_order(count):
    return list(range(0, count, 2)) + list(range(count - 1, 0, -2))


def halves_of(quarter):
    first = quarter * 16 // 35
    return ((0, first), (first, quarter - first))


def pick_body(blk_count, ids, gate_ref, up_ref, *out_refs):
    quarter = FF // blk_count // 4
    per = blk_count // 4
    for k in range(4):

        @pl.when(ids[0] == k)
        def _(k=k):
            for (at, size), out_ref in zip(halves_of(quarter), out_refs):
                for which, src in enumerate((gate_ref, up_ref)):
                    for bit in range(2):
                        parts = []
                        for high in range(2):
                            for small in range(per):
                                begin = (((high * 2 + bit) * per + small) * 4 + k) * quarter + at
                                parts.append(src[:, begin : begin + size])
                        out_ref[ids[1] ^ bit, which] = jnp.concatenate(parts, axis=1).astype(
                            jnp.bfloat16
                        )


def pick_columns(ids, gate, up, blk_count):
    rows = gate.shape[0]
    step = 48 if rows % 48 == 0 else rows
    widths = [size * blk_count // 2 for at, size in halves_of(FF // blk_count // 4)]
    spec = pl.BlockSpec((step, FF), lambda i, ids: (i, 0))
    return pl.pallas_call(
        functools.partial(pick_body, blk_count),
        grid_spec=pltpu.PrefetchScalarGridSpec(
            num_scalar_prefetch=1,
            grid=(rows // step,),
            in_specs=[spec, spec],
            out_specs=[pl.BlockSpec((2, 2, step, w), lambda i, ids: (0, 0, i, 0)) for w in widths],
        ),
        out_shape=[jax.ShapeDtypeStruct((2, 2, rows, w), jnp.bfloat16) for w in widths],
        compiler_params=pltpu.CompilerParams(vmem_limit_bytes=VMEM),
        cost_estimate=SMALL_COST,
        name="pick_columns",
    )(ids, gate, up)


def near_at(away):
    return (away & 1) * 2 + (away >> 1)


def adam_body(blk_count, rate, decay, ids, factor_ref, first_ref, second_ref, w_ref, m_ref, v_ref, m_out, v_out, w_out):
    per = blk_count // 4
    sizes = [size for at, size in halves_of(FF // blk_count // 4)]
    grads = [
        [[ref[near_at(ids[0] ^ k), bit] for bit in range(2)] for k in range(4)]
        for ref in (first_ref, second_ref)
    ]
    parts = []
    for high in range(2):
        for bit in range(2):
            for small in range(per):
                place = high * per + small
                for k in range(4):
                    for part, size in zip(grads, sizes):
                        parts.append(part[k][bit][:, place * size : (place + 1) * size])
    grad = jnp.concatenate(parts, axis=1).astype(jnp.float32) * factor_ref[0]
    m, v, w = adam_step(w_ref[...], grad, m_ref[...], v_ref[...], rate, decay)
    m_out[...] = m
    v_out[...] = v
    w_out[...] = w


def adam_columns(which, ids, factor, first, second, w, m, v, blk_count, rate, decay):
    rows = w.shape[0]
    step = 32 if rows % 32 == 0 else rows
    spec = pl.BlockSpec((step, FF), lambda i, ids: (i, 0))
    shape = jax.ShapeDtypeStruct((rows, FF), jnp.float32)
    grads = [
        pl.BlockSpec((4, None, 2, step, g.shape[-1]), lambda i, ids: (0, which, 0, i, 0))
        for g in (first, second)
    ]
    return pl.pallas_call(
        functools.partial(adam_body, blk_count, rate, decay),
        grid_spec=pltpu.PrefetchScalarGridSpec(
            num_scalar_prefetch=1,
            grid=(rows // step,),
            in_specs=[pl.BlockSpec(memory_space=pltpu.SMEM)] + grads + [spec, spec, spec],
            out_specs=[spec, spec, spec],
        ),
        out_shape=[shape] * 3,
        compiler_params=pltpu.CompilerParams(vmem_limit_bytes=VMEM),
        cost_estimate=SMALL_COST,
        name="adam_columns",
    )(ids, factor, first, second, w, m, v)


def nt(a, b, **kw):
    return lax.dot_general(a, b, (((1,), (1,)), ((), ())), preferred_element_type=jnp.float32, **kw)

def tn(a, b, **kw):
    return lax.dot_general(a, b, (((0,), (0,)), ((), ())), preferred_element_type=jnp.float32, **kw)

def stack_heads(ref, kvh, group):
    return jnp.concatenate([ref[:, HD * (kvh * group + i): HD * (kvh * group + i + 1)] for i in range(group)], axis=0)

def hidden_from(seg_key_ref, seg_query_ref, first, chunk, block_len, blk):
    key = first + lax.broadcasted_iota(jnp.int32, (chunk, block_len), 0)
    query = blk * block_len + lax.broadcasted_iota(jnp.int32, (chunk, block_len), 1)
    seg_key = seg_key_ref[pl.ds(first, chunk), :]
    counts = jnp.logical_and(key <= query, seg_key == seg_query_ref[0:1, :])
    return jnp.where(counts, 0.0, NEG_LARGE)

def ring_pair(ref, c, at):
    return jnp.concatenate(
        [ref[c, :, at : at + HD], ref[ref.shape[0] - 1 - c, :, at : at + HD]], axis=0
    )


def attend_body(chunk, ids, q_ref, k_ref, v_ref, seg_key_ref, seg_query_ref, o_ref, lse_ref, m_s, l_s, acc_s):
    block_len = q_ref.shape[0]
    group = H // KVH
    row = pl.program_id(0)
    per = chunk // block_len
    scale = HD ** (-0.5) * LOG2E
    start = ids[1 + row] // per
    stop = ids[0] // per + 1
    for kvh in range(KVH):
        q = stack_heads(q_ref, kvh, group)
        m_s[...] = jnp.full_like(m_s, NEG_LARGE)
        l_s[...] = jnp.zeros_like(l_s)
        acc_s[...] = jnp.zeros_like(acc_s)

        def step(c, carry):
            keys = ring_pair(k_ref, c, HD * kvh)
            vals = ring_pair(v_ref, c, HD * kvh)
            bias = hidden_from(seg_key_ref, seg_query_ref, c * chunk, chunk, block_len, ids[0])
            s = nt(keys, q) * scale + jnp.concatenate([bias] * group, axis=1)
            old = m_s[0:1, :]
            new = jnp.maximum(old, jnp.max(s, axis=0, keepdims=True))
            p = jnp.exp2(s - new)
            fade = jnp.exp2(old - new)
            l_s[0:1, :] = l_s[0:1, :] * fade + jnp.sum(p, axis=0, keepdims=True)
            acc_s[...] = acc_s[...] * fade + tn(vals, p.astype(jnp.bfloat16))
            m_s[0:1, :] = new
            return carry

        lax.fori_loop(start, stop, step, 0)
        total = l_s[0:1, :]
        out = (acc_s[...] * (1.0 / total)).T
        for i in range(group):
            o_ref[:, HD * (kvh * group + i): HD * (kvh * group + i + 1)] = out[block_len * i: block_len * (i + 1), :].astype(jnp.bfloat16)
        lse_ref[kvh] = jnp.broadcast_to(m_s[0:1, :] + jnp.log2(total), (8, group * block_len))

def attend(ids, q, kv, seg_key, seg_query, block_len):
    blk_count, rows = kv.shape[:2]
    group = H // KVH
    chunk = 2 * block_len
    many = group * block_len
    return pl.pallas_call(
        functools.partial(attend_body, chunk),
        grid_spec=pltpu.PrefetchScalarGridSpec(
            num_scalar_prefetch=1, grid=(rows,),
            in_specs=[
                pl.BlockSpec((block_len, HQD), lambda r, ids: (r, 0)),
                pl.BlockSpec((blk_count, None, block_len, KVD), lambda r, ids: (0, r, 0, 0)),
                pl.BlockSpec((blk_count, None, block_len, KVD), lambda r, ids: (0, r, 0, 1)),
                pl.BlockSpec((None, blk_count * block_len, HD), lambda r, ids: (r, 0, 0)),
                pl.BlockSpec((None, 8, block_len), lambda r, ids: (r, 0, 0)),
            ],
            out_specs=[
                pl.BlockSpec((block_len, HQD), lambda r, ids: (r, 0)),
                pl.BlockSpec((None, KVH, 8, many), lambda r, ids: (r, 0, 0, 0)),
            ],
            scratch_shapes=[pltpu.VMEM((8, many), jnp.float32), pltpu.VMEM((8, many), jnp.float32), pltpu.VMEM((HD, many), jnp.float32)]),
        out_shape=[
            jax.ShapeDtypeStruct((rows * block_len, HQD), jnp.bfloat16),
            jax.ShapeDtypeStruct((rows, KVH, 8, many), jnp.float32),
        ],
        compiler_params=pltpu.CompilerParams(vmem_limit_bytes=VMEM),
        cost_estimate=SMALL_COST,
        name="attend",
    )(ids, q, kv, kv, seg_key, seg_query)

def turn_back(u, cosine, sine):
    lane = lax.broadcasted_iota(jnp.int32, u.shape, 1)
    other = pltpu.roll(u, HD // 2, 1)
    return u * cosine + jnp.where(lane < HD // 2, other, -other) * sine

def attend_back_body(chunk, ids, q_ref, k_ref, v_ref, seg_key_ref, seg_query_ref, o_ref, do_ref, lse_ref, cos_ref, sin_ref, dq_ref, dkv_ref, dq_s):
    block_len = q_ref.shape[0]
    group = H // KVH
    row = pl.program_id(0)
    per = chunk // block_len
    plain = HD ** (-0.5)
    scale = plain * LOG2E
    start = ids[1 + row] // per
    stop = ids[0] // per + 1
    dkv_ref[...] = jnp.zeros_like(dkv_ref)
    for kvh in range(KVH):
        q = stack_heads(q_ref, kvh, group)
        do = stack_heads(do_ref, kvh, group)
        o = stack_heads(o_ref, kvh, group)
        both = do.astype(jnp.float32) * o.astype(jnp.float32)
        delta = nt(jnp.ones((8, HD), jnp.float32), both, precision=lax.Precision.HIGHEST)[0:1, :]
        lse = lse_ref[kvh][0:1, :]
        dq_s[...] = jnp.zeros_like(dq_s)

        def step(c, carry):
            keys = ring_pair(k_ref, c, HD * kvh)
            vals = ring_pair(v_ref, c, HD * kvh)
            bias = hidden_from(seg_key_ref, seg_query_ref, c * chunk, chunk, block_len, ids[0])
            s = nt(keys, q) * scale + jnp.concatenate([bias] * group, axis=1)
            p = jnp.exp2(s - lse)
            dp = nt(vals, do)
            ds = (p * (dp - delta)).astype(jnp.bfloat16)
            dk = jnp.dot(ds, q, preferred_element_type=jnp.float32) * plain
            dv = jnp.dot(p.astype(jnp.bfloat16), do, preferred_element_type=jnp.float32)
            for at, part in ((HD * kvh, dk.astype(jnp.bfloat16)), (KVD + HD * kvh, dv.astype(jnp.bfloat16))):
                dkv_ref[c, :, at : at + HD] = part[:block_len]
                dkv_ref[dkv_ref.shape[0] - 1 - c, :, at : at + HD] = part[block_len:]
            dq_s[...] += tn(ds, keys)
            return carry

        lax.fori_loop(start, stop, step, 0)
        cosine, sine = cos_ref[...], sin_ref[...]
        for i in range(group):
            u = dq_s[block_len * i: block_len * (i + 1), :] * plain
            at = HD * (kvh * group + i)
            dq_ref[:, at: at + HD] = turn_back(u, cosine, sine).astype(jnp.bfloat16)

def attend_back(ids, q, kv, seg_key, seg_query, o, do, lse, cosine, sine, block_len):
    blk_count, rows = kv.shape[:2]
    group = H // KVH
    chunk = 2 * block_len
    many = group * block_len
    per_row = pl.BlockSpec((block_len, HQD), lambda r, ids: (r, 0))
    turn = pl.BlockSpec((block_len, HD), lambda r, ids: (r, 0))
    return pl.pallas_call(
        functools.partial(attend_back_body, chunk),
        grid_spec=pltpu.PrefetchScalarGridSpec(
            num_scalar_prefetch=1, grid=(rows,),
            in_specs=[
                per_row,
                pl.BlockSpec((blk_count, None, block_len, KVD), lambda r, ids: (0, r, 0, 0)),
                pl.BlockSpec((blk_count, None, block_len, KVD), lambda r, ids: (0, r, 0, 1)),
                pl.BlockSpec((None, blk_count * block_len, HD), lambda r, ids: (r, 0, 0)),
                pl.BlockSpec((None, 8, block_len), lambda r, ids: (r, 0, 0)),
                per_row, per_row,
                pl.BlockSpec((None, KVH, 8, many), lambda r, ids: (r, 0, 0, 0)),
                turn, turn,
            ],
            out_specs=[per_row, pl.BlockSpec((blk_count, None, block_len, 2 * KVD), lambda r, ids: (0, r, 0, 0))],
            scratch_shapes=[pltpu.VMEM((many, HD), jnp.float32)]),
        out_shape=[
            jax.ShapeDtypeStruct((rows * block_len, HQD), jnp.bfloat16),
            jax.ShapeDtypeStruct((blk_count, rows, block_len, 2 * KVD), jnp.bfloat16),
        ],
        compiler_params=pltpu.CompilerParams(vmem_limit_bytes=VMEM),
        cost_estimate=SMALL_COST,
        name="attend_back",
    )(ids, q, kv, kv, seg_key, seg_query, o, do, lse, cosine, sine)

def nn(a, b):
    return jnp.dot(a, b, preferred_element_type=jnp.float32)


def middle_body(add, order, h_ref, dy_ref, wg_ref, wu_ref, wd_ref, *refs):
    prev_ref = refs[0] if add else None
    hid_ref, dg_ref, du_ref, dh_ref = refs[-4:]
    h = h_ref[...]
    gate = nn(h, wg_ref[...])
    up = nn(h, wu_ref[...])
    sig = 1.0 / (1.0 + jnp.exp(-gate))
    silu = gate * sig
    hid_ref[...] = (silu * up).astype(jnp.bfloat16)
    dhid = nt(dy_ref[...], wd_ref[...])
    dg = (dhid * up * sig * (1.0 + gate * (1.0 - sig))).astype(jnp.bfloat16)
    du = (dhid * silu).astype(jnp.bfloat16)
    dg_ref[...] = dg
    du_ref[...] = du
    dh = nt(dg, wg_ref[...]) + nt(du, wu_ref[...])
    if add:
        dh = dh + prev_ref[...].astype(jnp.float32)
    dh_ref[...] = dh.astype(jnp.bfloat16)


def middle(order, h, dy, gate_up, wd, prev=None):
    count = h.shape[0]
    step = count // order.shape[0]
    wide_here = wd.shape[0]
    row = pl.BlockSpec((step, D), lambda i, order: (i, 0))
    placed = pl.BlockSpec((step, D), lambda i, order: (order[i], 0))
    part = pl.BlockSpec((step, wide_here), lambda i, order: (i, 0))
    part_placed = pl.BlockSpec((step, wide_here), lambda i, order: (order[i], 0))
    once = pl.Buffered(1)
    extra = [] if prev is None else [prev]
    return pl.pallas_call(
        functools.partial(middle_body, prev is not None),
        grid_spec=pltpu.PrefetchScalarGridSpec(
            num_scalar_prefetch=1,
            grid=(count // step,),
            in_specs=[
                placed,
                row,
                pl.BlockSpec((None, D, wide_here), lambda i, order: (0, 0, 0), pipeline_mode=once),
                pl.BlockSpec((None, D, wide_here), lambda i, order: (1, 0, 0), pipeline_mode=once),
                pl.BlockSpec((wide_here, D), lambda i, order: (0, 0), pipeline_mode=once),
            ]
            + [row] * len(extra),
            out_specs=[part, part_placed, part_placed, row],
        ),
        out_shape=[jax.ShapeDtypeStruct((count, wide_here), jnp.bfloat16)] * 3
        + [jax.ShapeDtypeStruct((count, D), jnp.bfloat16)],
        compiler_params=pltpu.CompilerParams(vmem_limit_bytes=VMEM),
        cost_estimate=SMALL_COST,
        name="middle",
    )(order, h, dy, gate_up, gate_up, wd, *extra)


def two_grads_body(h_ref, a_ref, b_ref, out_ref):
    h = h_ref[...]
    out_ref[0] = tn(h, a_ref[...]).astype(jnp.bfloat16)
    out_ref[1] = tn(h, b_ref[...]).astype(jnp.bfloat16)


def two_grads(h, a, b, step=256):
    count = h.shape[0]
    wide_here = a.shape[1]
    whole = pl.BlockSpec(a.shape, lambda i: (0, 0), pipeline_mode=pl.Buffered(1))
    return pl.pallas_call(
        two_grads_body,
        grid=(D // step,),
        in_specs=[pl.BlockSpec((count, step), lambda i: (0, i)), whole, whole],
        out_specs=pl.BlockSpec((2, step, wide_here), lambda i: (0, i, 0)),
        out_shape=jax.ShapeDtypeStruct((2, D, wide_here), jnp.bfloat16),
        compiler_params=pltpu.CompilerParams(vmem_limit_bytes=VMEM),
        cost_estimate=SMALL_COST,
        name="two_grads",
    )(h, a, b)


def down_grad_body(hid_ref, dy_ref, g_ref):
    g_ref[...] = tn(hid_ref[...], dy_ref[...]).astype(jnp.bfloat16)

def down_grad(hid, dy, step=512):
    T, F = hid.shape
    D = dy.shape[1]
    return pl.pallas_call(down_grad_body, grid=(D // step,),
        in_specs=[pl.BlockSpec((T, F), lambda i: (0, 0), pipeline_mode=pl.Buffered(1)), pl.BlockSpec((T, step), lambda i: (0, i))],
        out_specs=pl.BlockSpec((F, step), lambda i: (0, i)),
        out_shape=jax.ShapeDtypeStruct((F, D), jnp.bfloat16),
        compiler_params=pltpu.CompilerParams(vmem_limit_bytes=VMEM),
        cost_estimate=SMALL_COST,
        name="down_grad")(hid, dy)

def down_body(hid_a_ref, hid_b_ref, wd_a_ref, wd_b_ref, o_ref):
    out = nn(hid_a_ref[...], wd_a_ref[...]) + nn(hid_b_ref[...], wd_b_ref[...])
    o_ref[...] = out.astype(jnp.bfloat16)


def down(hid_a, hid_b, wd_a, wd_b, step):
    count = hid_a.shape[0]

    def rows(array):
        return pl.BlockSpec((step, array.shape[1]), lambda i: (i, 0))

    def whole(array):
        return pl.BlockSpec(array.shape, lambda i: (0, 0), pipeline_mode=pl.Buffered(1))

    return pl.pallas_call(
        down_body,
        grid=(count // step,),
        in_specs=[rows(hid_a), rows(hid_b), whole(wd_a), whole(wd_b)],
        out_specs=pl.BlockSpec((step, D), lambda i: (i, 0)),
        out_shape=jax.ShapeDtypeStruct((count, D), jnp.bfloat16),
        compiler_params=pltpu.CompilerParams(vmem_limit_bytes=VMEM),
        cost_estimate=SMALL_COST,
        name="down",
    )(hid_a, hid_b, wd_a, wd_b)


def turn(u, cosine, sine):
    lane = lax.broadcasted_iota(jnp.int32, u.shape, 1)
    other = pltpu.roll(u, HD // 2, 1)
    return u * cosine + jnp.where(lane < HD // 2, -other, other) * sine


def mix_body(
    blk_count, rows, small_count, ids, own_ref, cross_ref, core_ref, ring_ref, freq_ref,
    self_ref, near_ref, far_ref, one_ref, strip_ref, vector_ref,
):
    ring = ring_order(blk_count)
    wide_here = ring_ref.shape[-1]
    pieces = []
    for b in range(blk_count):
        at = ring.index(b)
        strip_ref[rows * b : rows * (b + 1)] = ring_ref[at, :rows]
        left = small_count
        line = rows
        while left > 0:
            size = min(left, wide_here)
            pieces.append(ring_ref[at, line : line + 1, :size].astype(jnp.float32))
            left -= size
            line += 1
    vector = jnp.concatenate(pieces, axis=1)
    vector_ref[...] = vector
    gain = vector[:, :D]
    grp = ids[0]
    strip_q = wide_here - HD
    bias = jnp.zeros((1, wide_here), jnp.float32)
    for k in range(4):
        kv_at = 2 * D + HQD + HD * (k // 2) + KVD * (k % 2)
        part = jnp.concatenate(
            [
                vector[:, 2 * D + strip_q * k : 2 * D + strip_q * (k + 1)],
                vector[:, kv_at : kv_at + HD],
            ],
            axis=1,
        )
        bias = bias + jnp.where(grp == k, part, 0.0)
    count = own_ref.shape[0]
    strip = strip_ref[...]
    for d in range(4):
        source = (own_ref[...], core_ref[0], cross_ref[...], core_ref[1])[d]
        x = source[:, :D].astype(jnp.float32)
        root = lax.rsqrt(jnp.mean(x * x, axis=1, keepdims=True) + NORM_EPS)
        one = (x * root * gain).astype(jnp.bfloat16)
        one_ref[count * d : count * (d + 1)] = one
        mixed = nn(one, strip) + bias
        digits = source[:, D : D + HD].astype(jnp.float32)
        position = 64.0 * digits[:, 0:1] + digits[:, 1:2]
        angles = position * freq_ref[...]
        cosine, sine = jnp.cos(angles), jnp.sin(angles)
        for i in range(wide_here // HD):
            c, s = cosine, sine
            if i == wide_here // HD - 1:
                c = jnp.where(grp % 2 == 1, 1.0, c)
                s = jnp.where(grp % 2 == 1, 0.0, s)
            at = HD * i
            out = turn(mixed[:, at : at + HD], c, s).astype(jnp.bfloat16)
            if d == 0:
                self_ref[:, at : at + HD] = out
            elif d == 1:
                near_ref[:, at : at + HD] = out
            else:
                far_ref[d - 2, :, at : at + HD] = out


def mix(ids, own, cross, core, ring, freq, blk_count, rows, small_count):
    count = own.shape[0]
    wide_here = ring.shape[-1]
    low16 = jnp.bfloat16
    return pl.pallas_call(
        functools.partial(mix_body, blk_count, rows, small_count),
        in_specs=[pl.BlockSpec(memory_space=pltpu.SMEM)] + [pl.BlockSpec(memory_space=pltpu.VMEM)] * 5,
        out_specs=[pl.BlockSpec(memory_space=pltpu.VMEM)] * 6,
        out_shape=[
            jax.ShapeDtypeStruct((count, wide_here), low16),
            jax.ShapeDtypeStruct((count, wide_here), low16),
            jax.ShapeDtypeStruct((2, count, wide_here), low16),
            jax.ShapeDtypeStruct((4 * count, D), low16),
            jax.ShapeDtypeStruct((D, wide_here), low16),
            jax.ShapeDtypeStruct((1, blk_count * small_count), jnp.float32),
        ],
        compiler_params=pltpu.CompilerParams(vmem_limit_bytes=VMEM),
        cost_estimate=SMALL_COST,
        name="mix",
    )(ids, own, cross, core, ring, freq)


def pack_body(ids, self_ref, cross_ref, core_ref, q_ref, kv_ref):
    strip_q = self_ref.shape[1] - HD
    for g in range(4):

        @pl.when(ids[0] == g)
        def _(g=g):
            for k in range(4):
                part = (self_ref[...], core_ref[0], cross_ref[0], core_ref[1])[g ^ k]
                q_ref[:, strip_q * k : strip_q * (k + 1)] = part[:, :strip_q]
                at = (k % 2) * KVD + (k // 2) * HD
                kv_ref[:, at : at + HD] = part[:, strip_q:]


def pack(ids, own, cross, core):
    count = own.shape[0]
    return pl.pallas_call(
        pack_body,
        in_specs=[pl.BlockSpec(memory_space=pltpu.SMEM)] + [pl.BlockSpec(memory_space=pltpu.VMEM)] * 3,
        out_specs=[pl.BlockSpec(memory_space=pltpu.VMEM)] * 2,
        out_shape=[
            jax.ShapeDtypeStruct((count, HQD), jnp.bfloat16),
            jax.ShapeDtypeStruct((count, 2 * KVD), jnp.bfloat16),
        ],
        compiler_params=pltpu.CompilerParams(vmem_limit_bytes=VMEM),
        cost_estimate=SMALL_COST,
        name="pack",
    )(ids, own, cross, core)


def turn_dkv_body(ids, dkv_ref, cos_ref, sin_ref, self_ref, near_ref, far_ref, sum_ref):
    items = []
    sums = [None] * 4
    for k in range(4):
        at = (k % 2) * KVD + (k // 2) * HD
        part = dkv_ref[:, at : at + HD]
        if k % 2 == 0:
            part = turn_back(part.astype(jnp.float32), cos_ref[...], sin_ref[...]).astype(jnp.bfloat16)
        items.append(part)
        sums[(k % 2) * 2 + k // 2] = jnp.sum(part.astype(jnp.float32), axis=0, keepdims=True)
    sum_ref[...] = jnp.concatenate(sums, axis=1)
    for g in range(4):

        @pl.when(ids[0] == g)
        def _(g=g):
            self_ref[...] = items[g]
            near_ref[...] = items[g ^ 1]
            far_ref[0] = items[g ^ 2]
            far_ref[1] = items[g ^ 3]


def turn_dkv(ids, dkv, cosine, sine):
    count = dkv.shape[0]
    return pl.pallas_call(
        turn_dkv_body,
        in_specs=[pl.BlockSpec(memory_space=pltpu.SMEM)] + [pl.BlockSpec(memory_space=pltpu.VMEM)] * 3,
        out_specs=[pl.BlockSpec(memory_space=pltpu.VMEM)] * 4,
        out_shape=[
            jax.ShapeDtypeStruct((count, HD), jnp.bfloat16),
            jax.ShapeDtypeStruct((count, HD), jnp.bfloat16),
            jax.ShapeDtypeStruct((2, count, HD), jnp.bfloat16),
            jax.ShapeDtypeStruct((1, 2 * KVD), jnp.float32),
        ],
        compiler_params=pltpu.CompilerParams(vmem_limit_bytes=VMEM),
        cost_estimate=SMALL_COST,
        name="turn_dkv",
    )(ids, dkv, cosine, sine)


def kv_grad_body(
    blk_count, rows, small_count, self_ref, cross_ref, core_ref, dq_ref, one_ref, own_ref, near_x_ref,
    core_x_ref, strip_ref, gain_two_ref, bias_q_ref, bias_kv_ref, grad_ref, here_ref, there_ref,
):
    count = self_ref.shape[0]
    strip_q = strip_ref.shape[1] - HD
    parts = (self_ref[...], core_ref[0], cross_ref[0], core_ref[1])
    near = jnp.concatenate(parts, axis=0)
    grad = tn(one_ref[...], near)
    gain_one = jnp.zeros((1, D), jnp.float32)
    for d in range(4):
        x = (own_ref[...], core_x_ref[0], near_x_ref[...], core_x_ref[1])[d][:, :D].astype(jnp.float32)
        root = lax.rsqrt(jnp.mean(x * x, axis=1, keepdims=True) + NORM_EPS)
        hone = nt(dq_ref[count * d : count * (d + 1)], strip_ref[:, :strip_q])
        hone = hone + nt(parts[d], strip_ref[:, strip_q:])
        gain_one = gain_one + jnp.sum(hone * x * root, axis=0, keepdims=True)
        out_ref = (here_ref, there_ref)[d % 2]
        out_ref[count * (d // 2) : count * (d // 2 + 1)] = hone.astype(jnp.bfloat16)
    vector = jnp.concatenate([gain_one, gain_two_ref[...], bias_q_ref[...], bias_kv_ref[...]], axis=1)
    extra = grad_ref.shape[1] - rows
    for b in range(blk_count):
        grad_ref[b, :rows] = grad[rows * b : rows * (b + 1)].astype(jnp.bfloat16)
        lines = []
        for line in range(extra):
            size = min(HD, max(small_count - line * HD, 0))
            begin = small_count * b + line * HD
            pieces = [vector[:, begin : begin + size]] if size > 0 else []
            if size < HD:
                pieces.append(jnp.zeros((1, HD - size), jnp.float32))
            lines.append(pieces[0] if len(pieces) == 1 else jnp.concatenate(pieces, axis=1))
        grad_ref[b, rows:] = jnp.concatenate(lines, axis=0).astype(jnp.bfloat16)


def kv_grad_rows(rows, small_count):
    needed = rows + -(-small_count // HD)
    return needed + -needed % 16


def make_kv_grad(blk_count, rows, small_count, own, cross, core, dq, one, x_own, x_cross, x_core, strip, gain_two, bias_q, bias_kv):
    count = own.shape[0]
    height = kv_grad_rows(rows, small_count)
    return pl.pallas_call(
        functools.partial(kv_grad_body, blk_count, rows, small_count),
        in_specs=[pl.BlockSpec(memory_space=pltpu.VMEM)] * 12,
        out_specs=[pl.BlockSpec(memory_space=pltpu.VMEM)] * 3,
        out_shape=[
            jax.ShapeDtypeStruct((blk_count, height, HD), jnp.bfloat16),
            jax.ShapeDtypeStruct((2 * count, D), jnp.bfloat16),
            jax.ShapeDtypeStruct((2 * count, D), jnp.bfloat16),
        ],
        compiler_params=pltpu.CompilerParams(vmem_limit_bytes=VMEM),
        cost_estimate=SMALL_COST,
        name="kv_grad",
    )(own, cross, core, dq, one, x_own, x_cross, x_core, strip, gain_two, bias_q, bias_kv)


CORE = [(0, 1), (1, 0), (2, 3), (3, 2)]
CROSS = [(0, 2), (2, 0), (1, 3), (3, 1)]
DIAG = [(0, 3), (3, 0), (1, 2), (2, 1)]


def low(values):
    return values.astype(jnp.bfloat16)


def wide(values):
    return values.astype(jnp.float32)


def swap_core(values):
    return lax.ppermute(values, "grp", CORE)


def swap_cross(values):
    return lax.ppermute(values, "grp", CROSS)


def swap_diag(values):
    return lax.ppermute(values, "grp", DIAG)


def swap_blk(values, bit):
    count = lax.axis_size("blk")
    return lax.ppermute(values, "blk", [(i, i ^ bit) for i in range(count)])


def blk_bit(bit):
    return (lax.axis_index("blk") & bit) != 0


def bits_of(count):
    out = []
    bit = count // 2
    while bit >= 1:
        out.append(bit)
        bit //= 2
    return out


def gather_bits(values, order):
    done = []
    for bit in order:
        other = swap_blk(values, bit)
        mine = blk_bit(bit)
        axis = sum(1 for d in done if d > bit)
        values = jnp.stack(
            [jnp.where(mine, other, values), jnp.where(mine, values, other)], axis=axis
        )
        done.append(bit)
    return values


def scatter_bits(values, axes, order):
    axes = list(axes)
    for bit in order:
        axis = axes.index(bit)
        mine = blk_bit(bit).astype(jnp.int32)
        keep = lax.dynamic_index_in_dim(values, mine, axis, keepdims=False)
        send = lax.dynamic_index_in_dim(values, 1 - mine, axis, keepdims=False)
        values = low(wide(keep) + wide(swap_blk(send, bit)))
        axes.remove(bit)
    return values


def by_place(parts):
    grp = lax.axis_index("grp")
    core = (grp & 1) != 0
    cross = (grp & 2) != 0
    a, b, c, d = parts
    a, b = jnp.where(core, b, a), jnp.where(core, a, b)
    c, d = jnp.where(core, d, c), jnp.where(core, c, d)
    a, c = jnp.where(cross, c, a), jnp.where(cross, a, c)
    b, d = jnp.where(cross, d, b), jnp.where(cross, b, d)
    return [a, b, c, d]


def gather_near(values):
    cross = swap_cross(values)
    both = swap_core(jnp.stack([values, cross]))
    return [values, both[0], cross, both[1]]


def gather_grp(values):
    return by_place(gather_near(values))


def gather_tokens(values, bit):
    half = values.shape[0] // 2
    cross = swap_cross(values)
    over = swap_blk(values, bit)
    first = swap_blk(cross[:half], bit)
    second = swap_cross(over[half:])
    chip = jnp.concatenate([values, cross, over, first, second])
    return jnp.concatenate([chip, swap_core(chip)])


def angles_of(position):
    half = HD // 2
    freqs = ROPE_BASE ** (-2.0 * jnp.arange(half, dtype=jnp.float32) / HD)
    return position.astype(jnp.float32)[:, None] * freqs[None, :]


def rotate_by(values, cosine, sine):
    half = HD // 2
    first_half = values[..., :half]
    second_half = values[..., half:]
    return jnp.concatenate(
        [first_half * cosine - second_half * sine, second_half * cosine + first_half * sine],
        axis=-1,
    )


def after(values, anchor):
    return lax.optimization_barrier((values, anchor))[0]


def gather_step(values, done, bit):
    other = swap_blk(values, bit)
    mine = blk_bit(bit)
    axis = sum(1 for d in done if d > bit)
    return jnp.stack(
        [jnp.where(mine, other, values), jnp.where(mine, values, other)], axis=axis
    )


def gather_near_stacked(values):
    both = jnp.stack([values, swap_cross(values)])
    return jnp.concatenate([both, swap_core(both)])


def ring_groups(count):
    return [[g * count + b for b in ring_order(count)] for g in range(4)]


def gather_ring(values):
    count = lax.axis_size("blk")
    return lax.all_gather(values, ("grp", "blk"), axis=0, axis_index_groups=ring_groups(count))


def exchange_near(parts):
    cross = swap_cross(jnp.stack([parts[2], parts[3]]))
    core = swap_core(jnp.stack([parts[1], cross[1]]))
    return [parts[0], core[0], cross[0], core[1]]


def on_device(
    tokens,
    cotangent,
    segment_ids,
    position_ids,
    w_attend,
    w_out,
    w_gate,
    w_up,
    w_down,
    small_params,
    first_attend,
    first_out,
    first_gate,
    first_up,
    first_down,
    first_small,
    second_attend,
    second_out,
    second_gate,
    second_up,
    second_down,
    second_small,
):
    rows_here, block_len = tokens.shape[:2]
    blk_count = lax.axis_size("blk")
    seq_len = block_len * blk_count
    token_count = rows_here * block_len
    grp = lax.axis_index("grp")
    blk = lax.axis_index("blk")
    cross_id, core_id = grp // 2, grp % 2
    strip_heads = H // 4
    strip_q = strip_heads * HD
    bits = bits_of(blk_count)
    team = blk_count // 4
    lows = [bit for bit in bits if bit < team]
    spread = [bits[0]] + lows
    low_shape = (2,) * len(lows)
    in_team = blk_bit(team).astype(jnp.int32)
    weight_rows = w_gate.shape[0]
    ff_block = w_down.shape[0]
    quarter = ff_block // 4
    widths = [size * blk_count // 2 for at, size in halves_of(quarter)]
    chip_rows = 4 * token_count
    half = token_count // 2

    ids = jnp.stack([grp, in_team])
    flat_low = tokens.reshape(token_count, D)
    dy_low = cotangent.reshape(token_count, D)
    positions = position_ids.reshape(token_count)
    kv_at = HQD + HD * cross_id + KVD * core_id
    strip_local = low(
        jnp.concatenate(
            [
                lax.dynamic_slice_in_dim(w_attend, strip_q * grp, strip_q, 1),
                lax.dynamic_slice_in_dim(w_attend, kv_at, HD, 1),
            ],
            axis=1,
        )
    )
    small_count = small_params.shape[0]
    small_send = jnp.concatenate([low(small_params), low(segment_ids.reshape(token_count))])
    strip_wide = strip_q + HD
    small_send = jnp.pad(small_send, (0, -small_send.shape[0] % (16 * strip_wide)))
    strip_local = jnp.concatenate([strip_local, small_send.reshape(-1, strip_wide)])
    ring = ring_order(blk_count)
    strip_ring = gather_ring(strip_local)
    small_ring = strip_ring[:, weight_rows:].reshape(blk_count, -1)[:, small_count : small_count + token_count]
    small_all = jnp.stack([small_ring[ring.index(b)] for b in range(blk_count)])
    digits = low(jnp.stack([positions // 64, positions % 64], axis=1))
    digits = jnp.pad(digits, ((0, 0), (0, HD - 2)))
    token_send = jnp.concatenate([flat_low, digits], axis=1)
    picked_a, picked_b = pick_columns(ids, w_gate, w_up, blk_count)
    got_a = swap_blk(picked_a[1], team)
    dy_cross = swap_cross(after(dy_low, picked_a))
    dy_over = swap_blk(after(dy_low, strip_ring), team)
    token_cross = after(swap_cross(token_send), (picked_a, strip_ring, got_a, dy_cross))

    def place(values, other, done, bit, lead=0):
        mine = blk_bit(bit)
        axis = lead + sum(1 for d in done if d > bit)
        return jnp.stack(
            [jnp.where(mine, other, values), jnp.where(mine, values, other)], axis=axis
        )

    mine_team = blk_bit(team)
    (low_first, size_first), (low_second, size_second) = halves_of(quarter)

    def team_pair(mine, got):
        return jnp.stack(
            [jnp.where(mine_team, got, mine), jnp.where(mine_team, mine, got)], axis=1
        )

    out_local = low(lax.dynamic_slice_in_dim(w_out, strip_q * grp, strip_q, 1))
    out_ring = gather_ring(after(out_local, strip_ring))
    down_here = low(lax.dynamic_slice_in_dim(w_down, quarter * grp, quarter, 0))
    token_core = swap_core(jnp.stack([token_send, token_cross]))
    freqs = ROPE_BASE ** (-2.0 * jnp.arange(HD // 2, dtype=jnp.float32) / HD)
    freqs = jnp.concatenate([freqs, freqs])[None]
    mixed_own, mixed_core, mixed_far, near_one, strip, vector = mix(
        ids, token_send, token_cross, token_core, strip_ring, freqs, blk_count, weight_rows, small_count
    )
    vector = vector[0]
    gain_one = vector[:D]
    gain_two = vector[D : 2 * D]
    seg_all = small_all.astype(jnp.int32)
    seg_all = seg_all.reshape(blk_count, rows_here, block_len)
    seg_key = jnp.broadcast_to(
        seg_all.transpose(1, 0, 2).reshape(rows_here, seq_len)[:, :, None], (rows_here, seq_len, HD)
    )
    seg_query = jnp.broadcast_to(segment_ids[:, None, :], (rows_here, 8, block_len))
    first_blk = jnp.sum((seg_all[:, :, -1] < segment_ids[None, :, 0]).astype(jnp.int32), axis=0)
    attend_ids = jnp.concatenate([blk[None], first_blk])

    dy_first = swap_blk(dy_cross[:half], team)
    dy_second = swap_cross(dy_over[half:])
    mixed_cross = swap_cross(mixed_far)
    mixed_core = swap_core(jnp.stack([mixed_core, mixed_cross[1]]))
    mixed_core = after(mixed_core, dy_over)
    query, packed_kv = pack(ids, mixed_own, mixed_cross, mixed_core)
    key_value = packed_kv.reshape(rows_here, block_len, 2 * KVD)
    kv_all = gather_ring(key_value)

    teams = [
        [g * blk_count + (i | t) for g in range(4) for t in (0, team)]
        for i in range(blk_count)
        if not i & team
    ]
    order = jnp.stack(
        [
            (grp ^ (2 * (i & 1) + (i >> 2))) * 2 + (in_team ^ ((i >> 1) & 1))
            for i in range(8)
        ]
    )

    peers = [[i for i in range(blk_count) if (i & team) == t] for t in (0, team)]

    def lows_of(values, done, lead=0, anchor=None):
        for bit in lows:
            got = swap_blk(values, bit)
            if anchor is not None:
                got = after(got, anchor)
            values = place(values, got, done, bit, lead)
            done = done + [bit]
        return values

    got_b = swap_blk(after(picked_b[1], mixed_own), team)
    pair_a = team_pair(picked_a[0], after(got_a, mixed_own))
    pair_a_got = swap_blk(pair_a, bits[0])
    pair_a_got, got_b = after((pair_a_got, got_b), kv_all)
    kv_all = after(kv_all, (pair_a_got, got_b, dy_first, dy_second))
    down_got = swap_blk(after(down_here, kv_all), bits[0])
    dy_chip = jnp.concatenate([dy_low, dy_cross, dy_over, dy_first, dy_second])
    dy_team = jnp.concatenate([dy_chip, swap_core(dy_chip)])
    pair_a = place(pair_a, pair_a_got, [team], bits[0], 1)
    gate_up_a = lows_of(pair_a, [bits[0], team], 1).reshape(2, D, -1)
    pair_b = team_pair(picked_b[0], got_b)
    pair_b_got = swap_blk(after(pair_b, pair_a_got), bits[0])
    out_ring = after(out_ring, packed_kv)
    out_strip = jnp.concatenate([out_ring[ring.index(b)] for b in range(blk_count)])
    out_cross = swap_cross(out_strip)
    out_core = swap_core(jnp.stack([out_strip, after(out_cross, kv_all)]))
    out_full = jnp.concatenate(by_place([out_strip, out_core[0], out_cross, out_core[1]]), axis=1)

    att_in, lse = attend(attend_ids, query, kv_all, seg_key, seg_query, block_len)
    flat = wide(flat_low)
    resid = flat + jnp.dot(att_in, out_full, preferred_element_type=jnp.float32)
    h_two = low(norm_apply(resid, gain_two))
    down_here = place(down_here, down_got, [], bits[0])
    down_here = lows_of(down_here, [bits[0]]).reshape(2 * blk_count // 4, quarter, D)
    down_a = down_here[:, :size_first].reshape(widths[0], D)
    down_b = down_here[:, size_first:].reshape(widths[1], D)
    h_team = lax.all_gather(h_two, ("grp", "blk"), axis=0, tiled=True, axis_index_groups=teams)
    pair_b_got = after(pair_b_got, (h_two, gate_up_a))
    pair_b = place(pair_b, pair_b_got, [team], bits[0], 1)
    h_team = after(h_team, (gate_up_a, pair_b, dy_team))
    hidden_a, d_gate_a, d_up_a, part_a = middle(order, h_team, dy_team, gate_up_a, down_a)
    gate_up_b = lows_of(pair_b, [bits[0], team], 1, hidden_a).reshape(2, D, -1)
    down_grad_a = down_grad(after(hidden_a, gate_up_b), dy_team)
    down_share_a = lax.psum_scatter(
        down_grad_a, "blk", scatter_dimension=0, axis_index_groups=peers, tiled=True
    )
    column_grad_a = two_grads(h_team, d_gate_a, d_up_a)

    def part_sent(values, axis, bit):
        mine = blk_bit(bit).astype(jnp.int32)
        keep = lax.dynamic_index_in_dim(values, mine, axis, keepdims=False)
        send = lax.dynamic_index_in_dim(values, 1 - mine, axis, keepdims=False)
        return keep, swap_blk(send, bit)

    def part_sum(keep, got):
        return low(wide(keep) + wide(got))

    def columns_first(grad):
        grad = grad.reshape((2, 2, 2) + low_shape + (weight_rows, -1))
        return part_sent(grad, 2 + len(lows), lows[-1])

    def columns_mid(keep, got):
        values = part_sum(keep, got)
        for i in range(len(lows) - 2, -1, -1):
            values = part_sum(*part_sent(values, 3 + i, lows[i]))
        return values

    def columns_third(keep, got):
        values = part_sum(keep, got)
        mine = lax.dynamic_index_in_dim(values, in_team, 1, keepdims=False)
        send = lax.dynamic_index_in_dim(values, 1 - in_team, 1, keepdims=False)
        return values, (mine, swap_blk(send, team))

    def rows_second(keep, got):
        values = part_sum(keep, got)
        for i in range(len(lows) - 2, -1, -1):
            values = part_sum(*part_sent(values, 1 + i, lows[i]))
        return part_sent(values, 0, bits[0])

    def columns_last(mine, got):
        return jnp.stack(
            [jnp.where(mine_team, got, mine), jnp.where(mine_team, mine, got)], axis=1
        )

    first_a = columns_first(column_grad_a)
    hidden_b, d_gate_b, d_up_b, d_htwo_part = middle(
        order, after(h_team, (column_grad_a, down_grad_a)), dy_team, gate_up_b, down_b, part_a
    )

    def chip_sum(values, came):
        return low(wide(values[:chip_rows]) + wide(came))

    def scatter_far(chip):
        far = chip[3 * token_count :]
        return swap_blk(far[:half], team), swap_cross(far[half:])

    def scatter_near(chip, first, second):
        cross, over = (chip[token_count * i : token_count * (i + 1)] for i in (1, 2))
        cross = jnp.concatenate([low(wide(cross[:half]) + wide(first)), cross[half:]])
        over = jnp.concatenate([over[:half], low(wide(over[half:]) + wide(second))])
        return swap_cross(cross), swap_blk(over, team)

    near_att_cross = swap_cross(after(att_in, hidden_a))
    d_htwo_part = after(d_htwo_part, (first_a[1], down_share_a, near_att_cross))
    d_came = swap_core(d_htwo_part[chip_rows:])
    down_grad_b = down_grad(hidden_b, dy_team)
    rows_b = part_sent(
        down_grad_b.reshape((2,) + low_shape + (size_second, D)), len(lows), lows[-1]
    )
    mid_a = columns_mid(*after(first_a, d_came))
    second_a = part_sent(mid_a, 1, bits[0])
    d_chip = chip_sum(d_htwo_part, after(d_came, down_grad_b))
    d_far = scatter_far(d_chip)
    column_grad_b = two_grads(h_team, *after((d_gate_b, d_up_b), d_chip))
    first_b = columns_first(column_grad_b)
    d_far = after(d_far, column_grad_b)
    d_cross, d_over = scatter_near(d_chip, *d_far)
    out_part = down(*after((hidden_a, hidden_b), d_far), down_a, down_b, token_count)
    out_came = swap_core(out_part[chip_rows:])
    d_cross, d_over = after((d_cross, d_over), out_part)
    d_htwo = wide(d_chip[:token_count]) + wide(d_cross) + wide(d_over)

    norm_value_two, norm_back_two = jax.vjp(norm_apply, resid, gain_two)
    d_resid_norm, grad_gain_two = norm_back_two(d_htwo)
    d_resid = wide(dy_low) + d_resid_norm
    d_att = low(d_resid)
    rows_b = rows_second(*after(rows_b, d_att))

    d_attended = low(right_transposed(d_att, out_full))
    own_angles = angles_of(positions)
    cosine, sine = jnp.cos(own_angles), jnp.sin(own_angles)
    d_query, dkv = attend_back(
        attend_ids,
        query,
        kv_all,
        seg_key,
        seg_query,
        att_in,
        d_attended,
        lse,
        jnp.concatenate([cosine, cosine], axis=1),
        jnp.concatenate([sine, sine], axis=1),
        block_len,
    )
    dkv = lax.psum_scatter(
        dkv.reshape(blk_count * token_count, 2 * KVD),
        ("grp", "blk"),
        scatter_dimension=0,
        axis_index_groups=ring_groups(blk_count),
        tiled=True,
    )
    down_share_b = part_sum(*after(rows_b, d_query))
    sum_a, third_a = columns_third(*after(second_a, d_att))

    def to_strips(parts):
        return jnp.concatenate(exchange_near(by_place(parts)))

    near_dq = to_strips([d_query[:, strip_q * k : strip_q * (k + 1)] for k in range(4)])
    block_shape = (2,) * len(bits) + (weight_rows, -1)
    query_grad = low(left_product(near_one, near_dq)).reshape(block_shape)
    steps_query = part_sent(query_grad, len(bits) - 1, bits[-1])
    second_b = part_sent(columns_mid(*after(first_b, d_query)), 1, bits[0])
    dkv = after(dkv, down_share_b)
    own_part, core_part, far_part, bias_kv = turn_dkv(
        ids, dkv, jnp.concatenate([cosine, cosine], axis=1), jnp.concatenate([sine, sine], axis=1)
    )
    bias_q = jnp.sum(wide(d_query), axis=0)
    d_key = own_part
    cross_part = swap_cross(far_part)
    near_a = gather_near_stacked(columns_last(*after(third_a, own_part)))
    core_part = swap_core(jnp.stack([core_part, cross_part[1]]))
    kv_grad, hone_here, hone_there = make_kv_grad(
        blk_count,
        weight_rows,
        small_count,
        own_part,
        cross_part,
        core_part,
        near_dq,
        near_one,
        token_send,
        token_cross,
        token_core,
        strip,
        grad_gain_two[None],
        bias_q[None],
        bias_kv,
    )
    vector_rows = -(-small_count // HD)
    kv_grad = kv_grad.reshape((2,) * len(bits) + kv_grad.shape[1:])
    steps_kv = part_sent(kv_grad, len(bits) - 1, bits[-1])
    share_down = after(jnp.concatenate([down_share_a, down_share_b]), dkv)
    grad_down = lax.all_gather(share_down, "grp", axis=0, tiled=True)
    for i in range(len(bits) - 2, -1, -1):
        steps_query = part_sent(part_sum(*after(steps_query, d_key)), i, bits[i])
        kv_sum = part_sum(*steps_kv)
        kv_grad = kv_sum
        steps_kv = part_sent(kv_sum, i, bits[i])
    sum_b, third_b = columns_third(*after(second_b, kv_grad))
    share_kv_all = wide(steps_kv[0]) + wide(after(steps_kv[1], third_b[1]))
    share_kv = low(share_kv_all[:weight_rows])
    vector_part = share_kv_all[weight_rows : weight_rows + vector_rows]
    share_query = part_sum(*after(steps_query, kv_grad))
    near_att = swap_core(jnp.stack([att_in, near_att_cross]))
    near_att = jnp.concatenate([att_in, near_att[0], near_att_cross, near_att[1]])
    near_datt = to_strips([d_att[:, strip_q * k : strip_q * (k + 1)] for k in range(4)])
    out_grad = low(left_product(near_att, after(near_datt, d_attended))).reshape(block_shape)
    steps_out = part_sent(out_grad, len(bits) - 1, bits[-1])
    anchors = [near_dq, near_dq]
    for i in range(len(bits) - 2, -1, -1):
        anchor = anchors[min(len(bits) - 2 - i, 1)]
        steps_out = part_sent(part_sum(*after(steps_out, anchor)), i, bits[i])
    share_out = part_sum(*after(steps_out, kv_grad))

    own_b = columns_last(*third_b)
    cross_b = swap_cross(own_b)
    near_b = jnp.stack([own_b, cross_b])
    near_b = jnp.concatenate([near_b, swap_core(near_b)])
    grad_out = jnp.concatenate(gather_grp(share_out), axis=1)
    query_parts = gather_grp(share_query)
    key_parts = gather_grp(share_kv)
    grad_attend = jnp.concatenate(query_parts + [key_parts[k] for k in (0, 2, 1, 3)], axis=1)

    other = wide(swap_core(hone_there))
    d_hone = wide(hone_here[:token_count]) + other[:token_count]
    d_hone_cross = swap_cross(low(wide(hone_here[token_count:]) + other[token_count:]))
    square_sum = square_total(
        [
            wide(s)
            for s in (share_query, share_kv, share_out, sum_a, sum_b, share_down)
        ]
    )
    packed = jnp.concatenate([vector_part, jnp.full((8, HD), square_sum)])
    packed = packed + swap_cross(packed)
    packed = packed + swap_core(packed)
    share_vector = packed[:vector_rows].reshape(-1)[:small_count]
    square_sum = packed[vector_rows:] + jnp.sum(share_vector * share_vector)
    for bit in bits:
        square_sum = square_sum + swap_blk(square_sum, bit)
    grad_norm = jnp.sqrt(square_sum[0, 0])
    factor = jnp.minimum(1.0, CLIP_NORM / (grad_norm + 1e-06))
    out_chip = chip_sum(out_part, after(out_came, kv_grad))
    out_far = scatter_far(out_chip)
    factor = after(factor, (out_chip, cross_b, near_a))

    new_first_gate, new_second_gate, new_gate = adam_columns(
        0, ids, factor[None], near_a, near_b, w_gate, first_gate, second_gate, blk_count, RATE_GATE, WEIGHT_DECAY
    )
    new_first_up, new_second_up, new_up = adam_columns(
        1, ids, factor[None], near_a, near_b, w_up, first_up, second_up, blk_count, RATE_GATE, WEIGHT_DECAY
    )
    norm_value_one, norm_back_one = jax.vjp(norm_apply, flat, gain_one)
    d_hone = after(d_hone + wide(after(d_hone_cross, new_gate)), new_gate)
    d_flat_norm, unused_gain = norm_back_one(d_hone)
    grad_tokens = low(d_resid + d_flat_norm)

    new_first_attend, new_second_attend, new_attend = adam_step(
        w_attend, factor * wide(grad_attend), first_attend, second_attend, RATE_ATTEND, WEIGHT_DECAY
    )
    new_first_out, new_second_out, new_out = adam_step(
        w_out, factor * wide(grad_out), first_out, second_out, RATE_OUT, WEIGHT_DECAY
    )
    new_first_down, new_second_down, new_down = adam_step(
        w_down, factor * wide(grad_down), first_down, second_down, RATE_DOWN, WEIGHT_DECAY
    )
    new_first_small, new_second_small, new_small = adam_step(
        small_params, factor * share_vector, first_small, second_small, RATE_VECTOR, 0.0
    )

    out_near = after(scatter_near(out_chip, *after(out_far, factor)), (new_gate, new_up))
    out_tokens = low(resid + wide(out_chip[:token_count]) + wide(out_near[0]) + wide(out_near[1]))
    return (
        out_tokens.reshape(rows_here, block_len, D),
        grad_tokens.reshape(rows_here, block_len, D),
        grad_norm,
        new_first_attend,
        new_second_attend,
        new_attend,
        new_first_out,
        new_second_out,
        new_out,
        new_first_gate,
        new_second_gate,
        new_gate,
        new_first_up,
        new_second_up,
        new_up,
        new_first_down,
        new_second_down,
        new_down,
        new_first_small,
        new_second_small,
        new_small,
    )


def solution(mesh):
    placed = (
        P("grp", "blk", None),
        P("grp", "blk", None),
        P("grp", "blk"),
        P("grp", "blk"),
        P("blk", None),
        P("blk", None),
        P("blk", None),
        P("blk", None),
        P("blk", None),
        P("blk"),
        P("blk", None),
        P("blk", None),
        P("blk", None),
        P("blk", None),
        P("blk", None),
        P("blk"),
        P("blk", None),
        P("blk", None),
        P("blk", None),
        P("blk", None),
        P("blk", None),
        P("blk"),
    )
    return jax.shard_map(
        on_device,
        mesh=mesh,
        in_specs=placed,
        out_specs=(
            P("grp", "blk", None),
            P("grp", "blk", None),
            P(),
            P("blk", None),
            P("blk", None),
            P("blk", None),
            P("blk", None),
            P("blk", None),
            P("blk", None),
            P("blk", None),
            P("blk", None),
            P("blk", None),
            P("blk", None),
            P("blk", None),
            P("blk", None),
            P("blk", None),
            P("blk", None),
            P("blk", None),
            P("blk"),
            P("blk"),
            P("blk"),
        ),
        check_vma=False,
    )
```

```python
import functools

import jax
import jax.numpy as jnp
from jax import lax
from jax.experimental import pallas as pl
from jax.experimental.pallas import tpu as pltpu
from jax.sharding import PartitionSpec as P

D = 1536
FF = 8960
H = 12
KVH = 2
HD = 128
STEP = 10
HQD = 1536
KVD = 256


NORM_EPS = 1e-06
ROPE_BASE = 10000.0
CLIP_NORM = 1.0
BETA_FIRST = 0.9
BETA_SECOND = 0.95
ADAM_EPS = 1e-08
WEIGHT_DECAY = 0.1
RATE_ATTEND = 0.06
RATE_OUT = 0.5
RATE_GATE = 0.06
RATE_DOWN = 0.03
RATE_VECTOR = 0.5
NEG_LARGE = -1e30
LOG2E = 1.4426950408889634
VMEM = 48 * 1024 * 1024
SMALL_COST = pl.CostEstimate(flops=1000, bytes_accessed=1000, transcendentals=0)


def norm_apply(values, gain):
    return values * lax.rsqrt(jnp.mean(values * values, axis=-1, keepdims=True) + NORM_EPS) * gain


def swish_product(gate, up_proj):
    return jax.nn.silu(gate) * up_proj


def left_product(left_side, right_side):
    return lax.dot_general(
        left_side, right_side, (((0,), (0,)), ((), ())), preferred_element_type=jnp.float32
    )


def right_transposed(left_side, right_side):
    return lax.dot_general(
        left_side, right_side, (((1,), (1,)), ((), ())), preferred_element_type=jnp.float32
    )


def square_total(arrays):
    return sum((jnp.sum(member * member) for member in arrays))


def adam_step(weight, grad, first, second, rate, decay):
    first_new = BETA_FIRST * first + (1.0 - BETA_FIRST) * grad
    second_new = BETA_SECOND * second + (1.0 - BETA_SECOND) * grad * grad
    first_hat = first_new / (1.0 - BETA_FIRST**STEP)
    second_hat = second_new / (1.0 - BETA_SECOND**STEP)
    weight_new = weight - rate * (first_hat / (jnp.sqrt(second_hat) + ADAM_EPS) + decay * weight)
    return (first_new, second_new, weight_new)


def ring_order(count):
    return list(range(0, count, 2)) + list(range(count - 1, 0, -2))


def halves_of(quarter):
    first = quarter * 16 // 35
    return ((0, first), (first, quarter - first))


def pick_body(blk_count, ids, gate_ref, up_ref, *out_refs):
    quarter = FF // blk_count // 4
    per = blk_count // 4
    for k in range(4):

        @pl.when(ids[0] == k)
        def _(k=k):
            for (at, size), out_ref in zip(halves_of(quarter), out_refs):
                for which, src in enumerate((gate_ref, up_ref)):
                    for bit in range(2):
                        parts = []
                        for high in range(2):
                            for small in range(per):
                                begin = (((high * 2 + bit) * per + small) * 4 + k) * quarter + at
                                parts.append(src[:, begin : begin + size])
                        out_ref[ids[1] ^ bit, which] = jnp.concatenate(parts, axis=1).astype(
                            jnp.bfloat16
                        )


def pick_columns(ids, gate, up, blk_count):
    rows = gate.shape[0]
    step = 48 if rows % 48 == 0 else rows
    widths = [size * blk_count // 2 for at, size in halves_of(FF // blk_count // 4)]
    spec = pl.BlockSpec((step, FF), lambda i, ids: (i, 0))
    return pl.pallas_call(
        functools.partial(pick_body, blk_count),
        grid_spec=pltpu.PrefetchScalarGridSpec(
            num_scalar_prefetch=1,
            grid=(rows // step,),
            in_specs=[spec, spec],
            out_specs=[pl.BlockSpec((2, 2, step, w), lambda i, ids: (0, 0, i, 0)) for w in widths],
        ),
        out_shape=[jax.ShapeDtypeStruct((2, 2, rows, w), jnp.bfloat16) for w in widths],
        compiler_params=pltpu.CompilerParams(vmem_limit_bytes=VMEM),
        cost_estimate=SMALL_COST,
        name="pick_columns",
    )(ids, gate, up)


def near_at(away):
    return (away & 1) * 2 + (away >> 1)


def adam_body(blk_count, rate, decay, ids, factor_ref, first_ref, second_ref, w_ref, m_ref, v_ref, m_out, v_out, w_out):
    per = blk_count // 4
    sizes = [size for at, size in halves_of(FF // blk_count // 4)]
    grads = [
        [[ref[near_at(ids[0] ^ k), bit] for bit in range(2)] for k in range(4)]
        for ref in (first_ref, second_ref)
    ]
    parts = []
    for high in range(2):
        for bit in range(2):
            for small in range(per):
                place = high * per + small
                for k in range(4):
                    for part, size in zip(grads, sizes):
                        parts.append(part[k][bit][:, place * size : (place + 1) * size])
    grad = jnp.concatenate(parts, axis=1).astype(jnp.float32) * factor_ref[0]
    m, v, w = adam_step(w_ref[...], grad, m_ref[...], v_ref[...], rate, decay)
    m_out[...] = m
    v_out[...] = v
    w_out[...] = w


def adam_columns(which, ids, factor, first, second, w, m, v, blk_count, rate, decay):
    rows = w.shape[0]
    step = 32 if rows % 32 == 0 else rows
    spec = pl.BlockSpec((step, FF), lambda i, ids: (i, 0))
    shape = jax.ShapeDtypeStruct((rows, FF), jnp.float32)
    grads = [
        pl.BlockSpec((4, None, 2, step, g.shape[-1]), lambda i, ids: (0, which, 0, i, 0))
        for g in (first, second)
    ]
    return pl.pallas_call(
        functools.partial(adam_body, blk_count, rate, decay),
        grid_spec=pltpu.PrefetchScalarGridSpec(
            num_scalar_prefetch=1,
            grid=(rows // step,),
            in_specs=[pl.BlockSpec(memory_space=pltpu.SMEM)] + grads + [spec, spec, spec],
            out_specs=[spec, spec, spec],
        ),
        out_shape=[shape] * 3,
        compiler_params=pltpu.CompilerParams(vmem_limit_bytes=VMEM),
        cost_estimate=SMALL_COST,
        name="adam_columns",
    )(ids, factor, first, second, w, m, v)


def nt(a, b, **kw):
    return lax.dot_general(a, b, (((1,), (1,)), ((), ())), preferred_element_type=jnp.float32, **kw)

def tn(a, b, **kw):
    return lax.dot_general(a, b, (((0,), (0,)), ((), ())), preferred_element_type=jnp.float32, **kw)

def stack_heads(ref, kvh, group):
    return jnp.concatenate([ref[:, HD * (kvh * group + i): HD * (kvh * group + i + 1)] for i in range(group)], axis=0)

def hidden_from(seg_key_ref, seg_query_ref, first, chunk, block_len, blk):
    key = first + lax.broadcasted_iota(jnp.int32, (chunk, block_len), 0)
    query = blk * block_len + lax.broadcasted_iota(jnp.int32, (chunk, block_len), 1)
    seg_key = seg_key_ref[pl.ds(first, chunk), :]
    counts = jnp.logical_and(key <= query, seg_key == seg_query_ref[0:1, :])
    return jnp.where(counts, 0.0, NEG_LARGE)

def ring_pair(ref, c, at):
    return jnp.concatenate(
        [ref[c, :, at : at + HD], ref[ref.shape[0] - 1 - c, :, at : at + HD]], axis=0
    )


def attend_body(chunk, ids, q_ref, k_ref, v_ref, seg_key_ref, seg_query_ref, o_ref, lse_ref, m_s, l_s, acc_s):
    block_len = q_ref.shape[0]
    group = H // KVH
    row = pl.program_id(0)
    per = chunk // block_len
    scale = HD ** (-0.5) * LOG2E
    start = ids[1 + row] // per
    stop = ids[0] // per + 1
    for kvh in range(KVH):
        q = stack_heads(q_ref, kvh, group)
        m_s[...] = jnp.full_like(m_s, NEG_LARGE)
        l_s[...] = jnp.zeros_like(l_s)
        acc_s[...] = jnp.zeros_like(acc_s)

        def step(c, carry):
            keys = ring_pair(k_ref, c, HD * kvh)
            vals = ring_pair(v_ref, c, HD * kvh)
            bias = hidden_from(seg_key_ref, seg_query_ref, c * chunk, chunk, block_len, ids[0])
            s = nt(keys, q) * scale + jnp.concatenate([bias] * group, axis=1)
            old = m_s[0:1, :]
            new = jnp.maximum(old, jnp.max(s, axis=0, keepdims=True))
            p = jnp.exp2(s - new)
            fade = jnp.exp2(old - new)
            l_s[0:1, :] = l_s[0:1, :] * fade + jnp.sum(p, axis=0, keepdims=True)
            acc_s[...] = acc_s[...] * fade + tn(vals, p.astype(jnp.bfloat16))
            m_s[0:1, :] = new
            return carry

        lax.fori_loop(start, stop, step, 0)
        total = l_s[0:1, :]
        out = (acc_s[...] * (1.0 / total)).T
        for i in range(group):
            o_ref[:, HD * (kvh * group + i): HD * (kvh * group + i + 1)] = out[block_len * i: block_len * (i + 1), :].astype(jnp.bfloat16)
        lse_ref[kvh] = jnp.broadcast_to(m_s[0:1, :] + jnp.log2(total), (8, group * block_len))

def attend(ids, q, kv, seg_key, seg_query, block_len):
    blk_count, rows = kv.shape[:2]
    group = H // KVH
    chunk = 2 * block_len
    many = group * block_len
    return pl.pallas_call(
        functools.partial(attend_body, chunk),
        grid_spec=pltpu.PrefetchScalarGridSpec(
            num_scalar_prefetch=1, grid=(rows,),
            in_specs=[
                pl.BlockSpec((block_len, HQD), lambda r, ids: (r, 0)),
                pl.BlockSpec((blk_count, None, block_len, KVD), lambda r, ids: (0, r, 0, 0)),
                pl.BlockSpec((blk_count, None, block_len, KVD), lambda r, ids: (0, r, 0, 1)),
                pl.BlockSpec((None, blk_count * block_len, HD), lambda r, ids: (r, 0, 0)),
                pl.BlockSpec((None, 8, block_len), lambda r, ids: (r, 0, 0)),
            ],
            out_specs=[
                pl.BlockSpec((block_len, HQD), lambda r, ids: (r, 0)),
                pl.BlockSpec((None, KVH, 8, many), lambda r, ids: (r, 0, 0, 0)),
            ],
            scratch_shapes=[pltpu.VMEM((8, many), jnp.float32), pltpu.VMEM((8, many), jnp.float32), pltpu.VMEM((HD, many), jnp.float32)]),
        out_shape=[
            jax.ShapeDtypeStruct((rows * block_len, HQD), jnp.bfloat16),
            jax.ShapeDtypeStruct((rows, KVH, 8, many), jnp.float32),
        ],
        compiler_params=pltpu.CompilerParams(vmem_limit_bytes=VMEM),
        cost_estimate=SMALL_COST,
        name="attend",
    )(ids, q, kv, kv, seg_key, seg_query)

def turn_back(u, cosine, sine):
    lane = lax.broadcasted_iota(jnp.int32, u.shape, 1)
    other = pltpu.roll(u, HD // 2, 1)
    return u * cosine + jnp.where(lane < HD // 2, other, -other) * sine

def attend_back_body(chunk, ids, q_ref, k_ref, v_ref, seg_key_ref, seg_query_ref, o_ref, do_ref, lse_ref, cos_ref, sin_ref, dq_ref, dkv_ref, dq_s):
    block_len = q_ref.shape[0]
    group = H // KVH
    row = pl.program_id(0)
    per = chunk // block_len
    plain = HD ** (-0.5)
    scale = plain * LOG2E
    start = ids[1 + row] // per
    stop = ids[0] // per + 1
    dkv_ref[...] = jnp.zeros_like(dkv_ref)
    for kvh in range(KVH):
        q = stack_heads(q_ref, kvh, group)
        do = stack_heads(do_ref, kvh, group)
        o = stack_heads(o_ref, kvh, group)
        both = do.astype(jnp.float32) * o.astype(jnp.float32)
        delta = nt(jnp.ones((8, HD), jnp.float32), both, precision=lax.Precision.HIGHEST)[0:1, :]
        lse = lse_ref[kvh][0:1, :]
        dq_s[...] = jnp.zeros_like(dq_s)

        def step(c, carry):
            keys = ring_pair(k_ref, c, HD * kvh)
            vals = ring_pair(v_ref, c, HD * kvh)
            bias = hidden_from(seg_key_ref, seg_query_ref, c * chunk, chunk, block_len, ids[0])
            s = nt(keys, q) * scale + jnp.concatenate([bias] * group, axis=1)
            p = jnp.exp2(s - lse)
            dp = nt(vals, do)
            ds = (p * (dp - delta)).astype(jnp.bfloat16)
            dk = jnp.dot(ds, q, preferred_element_type=jnp.float32) * plain
            dv = jnp.dot(p.astype(jnp.bfloat16), do, preferred_element_type=jnp.float32)
            for at, part in ((HD * kvh, dk.astype(jnp.bfloat16)), (KVD + HD * kvh, dv.astype(jnp.bfloat16))):
                dkv_ref[c, :, at : at + HD] = part[:block_len]
                dkv_ref[dkv_ref.shape[0] - 1 - c, :, at : at + HD] = part[block_len:]
            dq_s[...] += tn(ds, keys)
            return carry

        lax.fori_loop(start, stop, step, 0)
        cosine, sine = cos_ref[...], sin_ref[...]
        for i in range(group):
            u = dq_s[block_len * i: block_len * (i + 1), :] * plain
            at = HD * (kvh * group + i)
            dq_ref[:, at: at + HD] = turn_back(u, cosine, sine).astype(jnp.bfloat16)

def attend_back(ids, q, kv, seg_key, seg_query, o, do, lse, cosine, sine, block_len):
    blk_count, rows = kv.shape[:2]
    group = H // KVH
    chunk = 2 * block_len
    many = group * block_len
    per_row = pl.BlockSpec((block_len, HQD), lambda r, ids: (r, 0))
    turn = pl.BlockSpec((block_len, HD), lambda r, ids: (r, 0))
    return pl.pallas_call(
        functools.partial(attend_back_body, chunk),
        grid_spec=pltpu.PrefetchScalarGridSpec(
            num_scalar_prefetch=1, grid=(rows,),
            in_specs=[
                per_row,
                pl.BlockSpec((blk_count, None, block_len, KVD), lambda r, ids: (0, r, 0, 0)),
                pl.BlockSpec((blk_count, None, block_len, KVD), lambda r, ids: (0, r, 0, 1)),
                pl.BlockSpec((None, blk_count * block_len, HD), lambda r, ids: (r, 0, 0)),
                pl.BlockSpec((None, 8, block_len), lambda r, ids: (r, 0, 0)),
                per_row, per_row,
                pl.BlockSpec((None, KVH, 8, many), lambda r, ids: (r, 0, 0, 0)),
                turn, turn,
            ],
            out_specs=[per_row, pl.BlockSpec((blk_count, None, block_len, 2 * KVD), lambda r, ids: (0, r, 0, 0))],
            scratch_shapes=[pltpu.VMEM((many, HD), jnp.float32)]),
        out_shape=[
            jax.ShapeDtypeStruct((rows * block_len, HQD), jnp.bfloat16),
            jax.ShapeDtypeStruct((blk_count, rows, block_len, 2 * KVD), jnp.bfloat16),
        ],
        compiler_params=pltpu.CompilerParams(vmem_limit_bytes=VMEM),
        cost_estimate=SMALL_COST,
        name="attend_back",
    )(ids, q, kv, kv, seg_key, seg_query, o, do, lse, cosine, sine)

def nn(a, b):
    return jnp.dot(a, b, preferred_element_type=jnp.float32)


def middle_body(add, order, h_ref, dy_ref, wg_ref, wu_ref, wd_ref, *refs):
    prev_ref = refs[0] if add else None
    hid_ref, dg_ref, du_ref, dh_ref = refs[-4:]
    h = h_ref[...]
    gate = nn(h, wg_ref[...])
    up = nn(h, wu_ref[...])
    sig = 1.0 / (1.0 + jnp.exp(-gate))
    silu = gate * sig
    hid_ref[...] = (silu * up).astype(jnp.bfloat16)
    dhid = nt(dy_ref[...], wd_ref[...])
    dg = (dhid * up * sig * (1.0 + gate * (1.0 - sig))).astype(jnp.bfloat16)
    du = (dhid * silu).astype(jnp.bfloat16)
    dg_ref[...] = dg
    du_ref[...] = du
    dh = nt(dg, wg_ref[...]) + nt(du, wu_ref[...])
    if add:
        dh = dh + prev_ref[...].astype(jnp.float32)
    dh_ref[...] = dh.astype(jnp.bfloat16)


def middle(order, h, dy, gate_up, wd, prev=None):
    count = h.shape[0]
    step = count // order.shape[0]
    wide_here = wd.shape[0]
    row = pl.BlockSpec((step, D), lambda i, order: (i, 0))
    placed = pl.BlockSpec((step, D), lambda i, order: (order[i], 0))
    part = pl.BlockSpec((step, wide_here), lambda i, order: (i, 0))
    part_placed = pl.BlockSpec((step, wide_here), lambda i, order: (order[i], 0))
    once = pl.Buffered(1)
    extra = [] if prev is None else [prev]
    return pl.pallas_call(
        functools.partial(middle_body, prev is not None),
        grid_spec=pltpu.PrefetchScalarGridSpec(
            num_scalar_prefetch=1,
            grid=(count // step,),
            in_specs=[
                placed,
                row,
                pl.BlockSpec((None, D, wide_here), lambda i, order: (0, 0, 0), pipeline_mode=once),
                pl.BlockSpec((None, D, wide_here), lambda i, order: (1, 0, 0), pipeline_mode=once),
                pl.BlockSpec((wide_here, D), lambda i, order: (0, 0), pipeline_mode=once),
            ]
            + [row] * len(extra),
            out_specs=[part, part_placed, part_placed, row],
        ),
        out_shape=[jax.ShapeDtypeStruct((count, wide_here), jnp.bfloat16)] * 3
        + [jax.ShapeDtypeStruct((count, D), jnp.bfloat16)],
        compiler_params=pltpu.CompilerParams(vmem_limit_bytes=VMEM),
        cost_estimate=SMALL_COST,
        name="middle",
    )(order, h, dy, gate_up, gate_up, wd, *extra)


def two_grads_body(h_ref, a_ref, b_ref, out_ref):
    h = h_ref[...]
    out_ref[0] = tn(h, a_ref[...]).astype(jnp.bfloat16)
    out_ref[1] = tn(h, b_ref[...]).astype(jnp.bfloat16)


def two_grads(h, a, b, step=256):
    count = h.shape[0]
    wide_here = a.shape[1]
    whole = pl.BlockSpec(a.shape, lambda i: (0, 0), pipeline_mode=pl.Buffered(1))
    return pl.pallas_call(
        two_grads_body,
        grid=(D // step,),
        in_specs=[pl.BlockSpec((count, step), lambda i: (0, i)), whole, whole],
        out_specs=pl.BlockSpec((2, step, wide_here), lambda i: (0, i, 0)),
        out_shape=jax.ShapeDtypeStruct((2, D, wide_here), jnp.bfloat16),
        compiler_params=pltpu.CompilerParams(vmem_limit_bytes=VMEM),
        cost_estimate=SMALL_COST,
        name="two_grads",
    )(h, a, b)


def down_grad_body(hid_ref, dy_ref, g_ref):
    g_ref[...] = tn(hid_ref[...], dy_ref[...]).astype(jnp.bfloat16)

def down_grad(hid, dy, step=512):
    T, F = hid.shape
    D = dy.shape[1]
    return pl.pallas_call(down_grad_body, grid=(D // step,),
        in_specs=[pl.BlockSpec((T, F), lambda i: (0, 0), pipeline_mode=pl.Buffered(1)), pl.BlockSpec((T, step), lambda i: (0, i))],
        out_specs=pl.BlockSpec((F, step), lambda i: (0, i)),
        out_shape=jax.ShapeDtypeStruct((F, D), jnp.bfloat16),
        compiler_params=pltpu.CompilerParams(vmem_limit_bytes=VMEM),
        cost_estimate=SMALL_COST,
        name="down_grad")(hid, dy)

def down_body(hid_a_ref, hid_b_ref, wd_a_ref, wd_b_ref, o_ref):
    out = nn(hid_a_ref[...], wd_a_ref[...]) + nn(hid_b_ref[...], wd_b_ref[...])
    o_ref[...] = out.astype(jnp.bfloat16)


def down(hid_a, hid_b, wd_a, wd_b, step):
    count = hid_a.shape[0]

    def rows(array):
        return pl.BlockSpec((step, array.shape[1]), lambda i: (i, 0))

    def whole(array):
        return pl.BlockSpec(array.shape, lambda i: (0, 0), pipeline_mode=pl.Buffered(1))

    return pl.pallas_call(
        down_body,
        grid=(count // step,),
        in_specs=[rows(hid_a), rows(hid_b), whole(wd_a), whole(wd_b)],
        out_specs=pl.BlockSpec((step, D), lambda i: (i, 0)),
        out_shape=jax.ShapeDtypeStruct((count, D), jnp.bfloat16),
        compiler_params=pltpu.CompilerParams(vmem_limit_bytes=VMEM),
        cost_estimate=SMALL_COST,
        name="down",
    )(hid_a, hid_b, wd_a, wd_b)


def turn(u, cosine, sine):
    lane = lax.broadcasted_iota(jnp.int32, u.shape, 1)
    other = pltpu.roll(u, HD // 2, 1)
    return u * cosine + jnp.where(lane < HD // 2, -other, other) * sine


def mix_body(
    blk_count, rows, small_count, ids, own_ref, cross_ref, core_ref, ring_ref, freq_ref,
    self_ref, near_ref, far_ref, one_ref, strip_ref, vector_ref,
):
    ring = ring_order(blk_count)
    wide_here = ring_ref.shape[-1]
    pieces = []
    for b in range(blk_count):
        at = ring.index(b)
        strip_ref[rows * b : rows * (b + 1)] = ring_ref[at, :rows]
        left = small_count
        line = rows
        while left > 0:
            size = min(left, wide_here)
            pieces.append(ring_ref[at, line : line + 1, :size].astype(jnp.float32))
            left -= size
            line += 1
    vector = jnp.concatenate(pieces, axis=1)
    vector_ref[...] = vector
    gain = vector[:, :D]
    grp = ids[0]
    strip_q = wide_here - HD
    bias = jnp.zeros((1, wide_here), jnp.float32)
    for k in range(4):
        kv_at = 2 * D + HQD + HD * (k // 2) + KVD * (k % 2)
        part = jnp.concatenate(
            [
                vector[:, 2 * D + strip_q * k : 2 * D + strip_q * (k + 1)],
                vector[:, kv_at : kv_at + HD],
            ],
            axis=1,
        )
        bias = bias + jnp.where(grp == k, part, 0.0)
    count = own_ref.shape[0]
    strip = strip_ref[...]
    for d in range(4):
        source = (own_ref[...], core_ref[0], cross_ref[...], core_ref[1])[d]
        x = source[:, :D].astype(jnp.float32)
        root = lax.rsqrt(jnp.mean(x * x, axis=1, keepdims=True) + NORM_EPS)
        one = (x * root * gain).astype(jnp.bfloat16)
        one_ref[count * d : count * (d + 1)] = one
        mixed = nn(one, strip) + bias
        digits = source[:, D : D + HD].astype(jnp.float32)
        position = 64.0 * digits[:, 0:1] + digits[:, 1:2]
        angles = position * freq_ref[...]
        cosine, sine = jnp.cos(angles), jnp.sin(angles)
        for i in range(wide_here // HD):
            c, s = cosine, sine
            if i == wide_here // HD - 1:
                c = jnp.where(grp % 2 == 1, 1.0, c)
                s = jnp.where(grp % 2 == 1, 0.0, s)
            at = HD * i
            out = turn(mixed[:, at : at + HD], c, s).astype(jnp.bfloat16)
            if d == 0:
                self_ref[:, at : at + HD] = out
            elif d == 1:
                near_ref[:, at : at + HD] = out
            else:
                far_ref[d - 2, :, at : at + HD] = out


def mix(ids, own, cross, core, ring, freq, blk_count, rows, small_count):
    count = own.shape[0]
    wide_here = ring.shape[-1]
    low16 = jnp.bfloat16
    return pl.pallas_call(
        functools.partial(mix_body, blk_count, rows, small_count),
        in_specs=[pl.BlockSpec(memory_space=pltpu.SMEM)] + [pl.BlockSpec(memory_space=pltpu.VMEM)] * 5,
        out_specs=[pl.BlockSpec(memory_space=pltpu.VMEM)] * 6,
        out_shape=[
            jax.ShapeDtypeStruct((count, wide_here), low16),
            jax.ShapeDtypeStruct((count, wide_here), low16),
            jax.ShapeDtypeStruct((2, count, wide_here), low16),
            jax.ShapeDtypeStruct((4 * count, D), low16),
            jax.ShapeDtypeStruct((D, wide_here), low16),
            jax.ShapeDtypeStruct((1, blk_count * small_count), jnp.float32),
        ],
        compiler_params=pltpu.CompilerParams(vmem_limit_bytes=VMEM),
        cost_estimate=SMALL_COST,
        name="mix",
    )(ids, own, cross, core, ring, freq)


def pack_body(ids, self_ref, cross_ref, core_ref, q_ref, kv_ref):
    strip_q = self_ref.shape[1] - HD
    for g in range(4):

        @pl.when(ids[0] == g)
        def _(g=g):
            for k in range(4):
                part = (self_ref[...], core_ref[0], cross_ref[0], core_ref[1])[g ^ k]
                q_ref[:, strip_q * k : strip_q * (k + 1)] = part[:, :strip_q]
                at = (k % 2) * KVD + (k // 2) * HD
                kv_ref[:, at : at + HD] = part[:, strip_q:]


def pack(ids, own, cross, core):
    count = own.shape[0]
    return pl.pallas_call(
        pack_body,
        in_specs=[pl.BlockSpec(memory_space=pltpu.SMEM)] + [pl.BlockSpec(memory_space=pltpu.VMEM)] * 3,
        out_specs=[pl.BlockSpec(memory_space=pltpu.VMEM)] * 2,
        out_shape=[
            jax.ShapeDtypeStruct((count, HQD), jnp.bfloat16),
            jax.ShapeDtypeStruct((count, 2 * KVD), jnp.bfloat16),
        ],
        compiler_params=pltpu.CompilerParams(vmem_limit_bytes=VMEM),
        cost_estimate=SMALL_COST,
        name="pack",
    )(ids, own, cross, core)


def turn_dkv_body(ids, dkv_ref, cos_ref, sin_ref, self_ref, near_ref, far_ref, sum_ref):
    items = []
    sums = [None] * 4
    for k in range(4):
        at = (k % 2) * KVD + (k // 2) * HD
        part = dkv_ref[:, at : at + HD]
        if k % 2 == 0:
            part = turn_back(part.astype(jnp.float32), cos_ref[...], sin_ref[...]).astype(jnp.bfloat16)
        items.append(part)
        sums[(k % 2) * 2 + k // 2] = jnp.sum(part.astype(jnp.float32), axis=0, keepdims=True)
    sum_ref[...] = jnp.concatenate(sums, axis=1)
    for g in range(4):

        @pl.when(ids[0] == g)
        def _(g=g):
            self_ref[...] = items[g]
            near_ref[...] = items[g ^ 1]
            far_ref[0] = items[g ^ 2]
            far_ref[1] = items[g ^ 3]


def turn_dkv(ids, dkv, cosine, sine):
    count = dkv.shape[0]
    return pl.pallas_call(
        turn_dkv_body,
        in_specs=[pl.BlockSpec(memory_space=pltpu.SMEM)] + [pl.BlockSpec(memory_space=pltpu.VMEM)] * 3,
        out_specs=[pl.BlockSpec(memory_space=pltpu.VMEM)] * 4,
        out_shape=[
            jax.ShapeDtypeStruct((count, HD), jnp.bfloat16),
            jax.ShapeDtypeStruct((count, HD), jnp.bfloat16),
            jax.ShapeDtypeStruct((2, count, HD), jnp.bfloat16),
            jax.ShapeDtypeStruct((1, 2 * KVD), jnp.float32),
        ],
        compiler_params=pltpu.CompilerParams(vmem_limit_bytes=VMEM),
        cost_estimate=SMALL_COST,
        name="turn_dkv",
    )(ids, dkv, cosine, sine)


def kv_grad_body(
    blk_count, rows, small_count, self_ref, cross_ref, core_ref, dq_ref, one_ref, own_ref, near_x_ref,
    core_x_ref, strip_ref, gain_two_ref, bias_q_ref, bias_kv_ref, grad_ref, here_ref, there_ref,
):
    count = self_ref.shape[0]
    strip_q = strip_ref.shape[1] - HD
    parts = (self_ref[...], core_ref[0], cross_ref[0], core_ref[1])
    near = jnp.concatenate(parts, axis=0)
    grad = tn(one_ref[...], near)
    gain_one = jnp.zeros((1, D), jnp.float32)
    for d in range(4):
        x = (own_ref[...], core_x_ref[0], near_x_ref[...], core_x_ref[1])[d][:, :D].astype(jnp.float32)
        root = lax.rsqrt(jnp.mean(x * x, axis=1, keepdims=True) + NORM_EPS)
        hone = nt(dq_ref[count * d : count * (d + 1)], strip_ref[:, :strip_q])
        hone = hone + nt(parts[d], strip_ref[:, strip_q:])
        gain_one = gain_one + jnp.sum(hone * x * root, axis=0, keepdims=True)
        out_ref = (here_ref, there_ref)[d % 2]
        out_ref[count * (d // 2) : count * (d // 2 + 1)] = hone.astype(jnp.bfloat16)
    vector = jnp.concatenate([gain_one, gain_two_ref[...], bias_q_ref[...], bias_kv_ref[...]], axis=1)
    extra = grad_ref.shape[1] - rows
    for b in range(blk_count):
        grad_ref[b, :rows] = grad[rows * b : rows * (b + 1)].astype(jnp.bfloat16)
        lines = []
        for line in range(extra):
            size = min(HD, max(small_count - line * HD, 0))
            begin = small_count * b + line * HD
            pieces = [vector[:, begin : begin + size]] if size > 0 else []
            if size < HD:
                pieces.append(jnp.zeros((1, HD - size), jnp.float32))
            lines.append(pieces[0] if len(pieces) == 1 else jnp.concatenate(pieces, axis=1))
        grad_ref[b, rows:] = jnp.concatenate(lines, axis=0).astype(jnp.bfloat16)


def kv_grad_rows(rows, small_count):
    needed = rows + -(-small_count // HD)
    return needed + -needed % 16


def make_kv_grad(blk_count, rows, small_count, own, cross, core, dq, one, x_own, x_cross, x_core, strip, gain_two, bias_q, bias_kv):
    count = own.shape[0]
    height = kv_grad_rows(rows, small_count)
    return pl.pallas_call(
        functools.partial(kv_grad_body, blk_count, rows, small_count),
        in_specs=[pl.BlockSpec(memory_space=pltpu.VMEM)] * 12,
        out_specs=[pl.BlockSpec(memory_space=pltpu.VMEM)] * 3,
        out_shape=[
            jax.ShapeDtypeStruct((blk_count, height, HD), jnp.bfloat16),
            jax.ShapeDtypeStruct((2 * count, D), jnp.bfloat16),
            jax.ShapeDtypeStruct((2 * count, D), jnp.bfloat16),
        ],
        compiler_params=pltpu.CompilerParams(vmem_limit_bytes=VMEM),
        cost_estimate=SMALL_COST,
        name="kv_grad",
    )(own, cross, core, dq, one, x_own, x_cross, x_core, strip, gain_two, bias_q, bias_kv)


CORE = [(0, 1), (1, 0), (2, 3), (3, 2)]
CROSS = [(0, 2), (2, 0), (1, 3), (3, 1)]
DIAG = [(0, 3), (3, 0), (1, 2), (2, 1)]


def low(values):
    return values.astype(jnp.bfloat16)


def wide(values):
    return values.astype(jnp.float32)


def swap_core(values):
    return lax.ppermute(values, "grp", CORE)


def swap_cross(values):
    return lax.ppermute(values, "grp", CROSS)


def swap_diag(values):
    return lax.ppermute(values, "grp", DIAG)


def swap_blk(values, bit):
    count = lax.axis_size("blk")
    return lax.ppermute(values, "blk", [(i, i ^ bit) for i in range(count)])


def blk_bit(bit):
    return (lax.axis_index("blk") & bit) != 0


def bits_of(count):
    out = []
    bit = count // 2
    while bit >= 1:
        out.append(bit)
        bit //= 2
    return out


def gather_bits(values, order):
    done = []
    for bit in order:
        other = swap_blk(values, bit)
        mine = blk_bit(bit)
        axis = sum(1 for d in done if d > bit)
        values = jnp.stack(
            [jnp.where(mine, other, values), jnp.where(mine, values, other)], axis=axis
        )
        done.append(bit)
    return values


def scatter_bits(values, axes, order):
    axes = list(axes)
    for bit in order:
        axis = axes.index(bit)
        mine = blk_bit(bit).astype(jnp.int32)
        keep = lax.dynamic_index_in_dim(values, mine, axis, keepdims=False)
        send = lax.dynamic_index_in_dim(values, 1 - mine, axis, keepdims=False)
        values = low(wide(keep) + wide(swap_blk(send, bit)))
        axes.remove(bit)
    return values


def by_place(parts):
    grp = lax.axis_index("grp")
    core = (grp & 1) != 0
    cross = (grp & 2) != 0
    a, b, c, d = parts
    a, b = jnp.where(core, b, a), jnp.where(core, a, b)
    c, d = jnp.where(core, d, c), jnp.where(core, c, d)
    a, c = jnp.where(cross, c, a), jnp.where(cross, a, c)
    b, d = jnp.where(cross, d, b), jnp.where(cross, b, d)
    return [a, b, c, d]


def gather_near(values):
    cross = swap_cross(values)
    both = swap_core(jnp.stack([values, cross]))
    return [values, both[0], cross, both[1]]


def gather_grp(values):
    return by_place(gather_near(values))


def gather_tokens(values, bit):
    half = values.shape[0] // 2
    cross = swap_cross(values)
    over = swap_blk(values, bit)
    first = swap_blk(cross[:half], bit)
    second = swap_cross(over[half:])
    chip = jnp.concatenate([values, cross, over, first, second])
    return jnp.concatenate([chip, swap_core(chip)])


def angles_of(position):
    half = HD // 2
    freqs = ROPE_BASE ** (-2.0 * jnp.arange(half, dtype=jnp.float32) / HD)
    return position.astype(jnp.float32)[:, None] * freqs[None, :]


def rotate_by(values, cosine, sine):
    half = HD // 2
    first_half = values[..., :half]
    second_half = values[..., half:]
    return jnp.concatenate(
        [first_half * cosine - second_half * sine, second_half * cosine + first_half * sine],
        axis=-1,
    )


def after(values, anchor):
    return lax.optimization_barrier((values, anchor))[0]


def gather_step(values, done, bit):
    other = swap_blk(values, bit)
    mine = blk_bit(bit)
    axis = sum(1 for d in done if d > bit)
    return jnp.stack(
        [jnp.where(mine, other, values), jnp.where(mine, values, other)], axis=axis
    )


def gather_near_stacked(values):
    both = jnp.stack([values, swap_cross(values)])
    return jnp.concatenate([both, swap_core(both)])


def ring_groups(count):
    return [[g * count + b for b in ring_order(count)] for g in range(4)]


def gather_ring(values):
    count = lax.axis_size("blk")
    return lax.all_gather(values, ("grp", "blk"), axis=0, axis_index_groups=ring_groups(count))


def exchange_near(parts):
    cross = swap_cross(jnp.stack([parts[2], parts[3]]))
    core = swap_core(jnp.stack([parts[1], cross[1]]))
    return [parts[0], core[0], cross[0], core[1]]


def on_device(
    tokens,
    cotangent,
    segment_ids,
    position_ids,
    w_attend,
    w_out,
    w_gate,
    w_up,
    w_down,
    small_params,
    first_attend,
    first_out,
    first_gate,
    first_up,
    first_down,
    first_small,
    second_attend,
    second_out,
    second_gate,
    second_up,
    second_down,
    second_small,
):
    rows_here, block_len = tokens.shape[:2]
    blk_count = lax.axis_size("blk")
    seq_len = block_len * blk_count
    token_count = rows_here * block_len
    grp = lax.axis_index("grp")
    blk = lax.axis_index("blk")
    cross_id, core_id = grp // 2, grp % 2
    strip_heads = H // 4
    strip_q = strip_heads * HD
    bits = bits_of(blk_count)
    team = blk_count // 4
    lows = [bit for bit in bits if bit < team]
    spread = [bits[0]] + lows
    low_shape = (2,) * len(lows)
    in_team = blk_bit(team).astype(jnp.int32)
    weight_rows = w_gate.shape[0]
    ff_block = w_down.shape[0]
    quarter = ff_block // 4
    widths = [size * blk_count // 2 for at, size in halves_of(quarter)]
    chip_rows = 4 * token_count
    half = token_count // 2

    ids = jnp.stack([grp, in_team])
    flat_low = tokens.reshape(token_count, D)
    dy_low = cotangent.reshape(token_count, D)
    positions = position_ids.reshape(token_count)
    kv_at = HQD + HD * cross_id + KVD * core_id
    strip_local = low(
        jnp.concatenate(
            [
                lax.dynamic_slice_in_dim(w_attend, strip_q * grp, strip_q, 1),
                lax.dynamic_slice_in_dim(w_attend, kv_at, HD, 1),
            ],
            axis=1,
        )
    )
    small_count = small_params.shape[0]
    small_send = jnp.concatenate([low(small_params), low(segment_ids.reshape(token_count))])
    strip_wide = strip_q + HD
    small_send = jnp.pad(small_send, (0, -small_send.shape[0] % (16 * strip_wide)))
    strip_local = jnp.concatenate([strip_local, small_send.reshape(-1, strip_wide)])
    ring = ring_order(blk_count)
    strip_ring = gather_ring(strip_local)
    small_ring = strip_ring[:, weight_rows:].reshape(blk_count, -1)[:, small_count : small_count + token_count]
    small_all = jnp.stack([small_ring[ring.index(b)] for b in range(blk_count)])
    digits = low(jnp.stack([positions // 64, positions % 64], axis=1))
    digits = jnp.pad(digits, ((0, 0), (0, HD - 2)))
    token_send = jnp.concatenate([flat_low, digits], axis=1)
    picked_a, picked_b = pick_columns(ids, w_gate, w_up, blk_count)
    got_a = swap_blk(picked_a[1], team)
    dy_cross = swap_cross(after(dy_low, picked_a))
    dy_over = swap_blk(after(dy_low, strip_ring), team)
    token_cross = after(swap_cross(token_send), (picked_a, strip_ring, got_a, dy_cross))

    def place(values, other, done, bit, lead=0):
        mine = blk_bit(bit)
        axis = lead + sum(1 for d in done if d > bit)
        return jnp.stack(
            [jnp.where(mine, other, values), jnp.where(mine, values, other)], axis=axis
        )

    mine_team = blk_bit(team)
    (low_first, size_first), (low_second, size_second) = halves_of(quarter)

    def team_pair(mine, got):
        return jnp.stack(
            [jnp.where(mine_team, got, mine), jnp.where(mine_team, mine, got)], axis=1
        )

    out_local = low(lax.dynamic_slice_in_dim(w_out, strip_q * grp, strip_q, 1))
    out_ring = gather_ring(after(out_local, strip_ring))
    down_here = low(lax.dynamic_slice_in_dim(w_down, quarter * grp, quarter, 0))
    token_core = swap_core(jnp.stack([token_send, token_cross]))
    freqs = ROPE_BASE ** (-2.0 * jnp.arange(HD // 2, dtype=jnp.float32) / HD)
    freqs = jnp.concatenate([freqs, freqs])[None]
    mixed_own, mixed_core, mixed_far, near_one, strip, vector = mix(
        ids, token_send, token_cross, token_core, strip_ring, freqs, blk_count, weight_rows, small_count
    )
    vector = vector[0]
    gain_one = vector[:D]
    gain_two = vector[D : 2 * D]
    seg_all = small_all.astype(jnp.int32)
    seg_all = seg_all.reshape(blk_count, rows_here, block_len)
    seg_key = jnp.broadcast_to(
        seg_all.transpose(1, 0, 2).reshape(rows_here, seq_len)[:, :, None], (rows_here, seq_len, HD)
    )
    seg_query = jnp.broadcast_to(segment_ids[:, None, :], (rows_here, 8, block_len))
    first_blk = jnp.sum((seg_all[:, :, -1] < segment_ids[None, :, 0]).astype(jnp.int32), axis=0)
    attend_ids = jnp.concatenate([blk[None], first_blk])

    dy_first = swap_blk(dy_cross[:half], team)
    dy_second = swap_cross(dy_over[half:])
    mixed_cross = swap_cross(mixed_far)
    mixed_core = swap_core(jnp.stack([mixed_core, mixed_cross[1]]))
    pair_a = team_pair(picked_a[0], after(got_a, mixed_own))
    pair_a_got = swap_blk(pair_a, bits[0])
    mixed_core = after(mixed_core, (dy_over, pair_a_got))
    query, packed_kv = pack(ids, mixed_own, mixed_cross, mixed_core)
    key_value = packed_kv.reshape(rows_here, block_len, 2 * KVD)
    kv_all = gather_ring(key_value)

    teams = [
        [g * blk_count + (i | t) for g in range(4) for t in (0, team)]
        for i in range(blk_count)
        if not i & team
    ]
    order = jnp.stack(
        [
            (grp ^ (2 * (i & 1) + (i >> 2))) * 2 + (in_team ^ ((i >> 1) & 1))
            for i in range(8)
        ]
    )

    peers = [[i for i in range(blk_count) if (i & team) == t] for t in (0, team)]

    def lows_of(values, done, lead=0, anchor=None):
        for bit in lows:
            got = swap_blk(values, bit)
            if anchor is not None:
                got = after(got, anchor)
            values = place(values, got, done, bit, lead)
            done = done + [bit]
        return values

    got_b = swap_blk(after(picked_b[1], mixed_own), team)
    pair_a = place(pair_a, after(pair_a_got, packed_kv), [team], bits[0], 1)
    gate_up_a = lows_of(pair_a, [bits[0], team], 1).reshape(2, D, -1)
    got_b = after(got_b, kv_all)
    kv_all = after(kv_all, (gate_up_a, got_b, dy_first, dy_second))
    down_got = swap_blk(after(down_here, kv_all), bits[0])
    dy_chip = jnp.concatenate([dy_low, dy_cross, dy_over, dy_first, dy_second])
    dy_team = jnp.concatenate([dy_chip, swap_core(dy_chip)])
    pair_b = team_pair(picked_b[0], got_b)
    pair_b_got = swap_blk(after(pair_b, down_got), bits[0])
    out_ring = after(out_ring, packed_kv)
    out_strip = jnp.concatenate([out_ring[ring.index(b)] for b in range(blk_count)])
    out_cross = swap_cross(out_strip)
    out_core = swap_core(jnp.stack([out_strip, after(out_cross, kv_all)]))
    out_full = jnp.concatenate(by_place([out_strip, out_core[0], out_cross, out_core[1]]), axis=1)

    att_in, lse = attend(attend_ids, query, kv_all, seg_key, seg_query, block_len)
    flat = wide(flat_low)
    resid = flat + jnp.dot(att_in, out_full, preferred_element_type=jnp.float32)
    h_two = low(norm_apply(resid, gain_two))
    h_two = after(h_two, down_got)
    down_here = place(down_here, down_got, [], bits[0])
    down_here = lows_of(down_here, [bits[0]]).reshape(2 * blk_count // 4, quarter, D)
    down_a = down_here[:, :size_first].reshape(widths[0], D)
    down_b = down_here[:, size_first:].reshape(widths[1], D)
    h_team = lax.all_gather(h_two, ("grp", "blk"), axis=0, tiled=True, axis_index_groups=teams)
    pair_b_got = after(pair_b_got, (h_two, gate_up_a))
    pair_b = place(pair_b, pair_b_got, [team], bits[0], 1)
    h_team = after(h_team, (gate_up_a, pair_b, dy_team))
    hidden_a, d_gate_a, d_up_a, part_a = middle(order, h_team, dy_team, gate_up_a, down_a)
    gate_up_b = lows_of(pair_b, [bits[0], team], 1, hidden_a).reshape(2, D, -1)
    down_grad_a = down_grad(after(hidden_a, gate_up_b), dy_team)
    down_share_a = lax.psum_scatter(
        down_grad_a, "blk", scatter_dimension=0, axis_index_groups=peers, tiled=True
    )
    column_grad_a = two_grads(h_team, d_gate_a, d_up_a)

    def part_sent(values, axis, bit):
        mine = blk_bit(bit).astype(jnp.int32)
        keep = lax.dynamic_index_in_dim(values, mine, axis, keepdims=False)
        send = lax.dynamic_index_in_dim(values, 1 - mine, axis, keepdims=False)
        return keep, swap_blk(send, bit)

    def part_sum(keep, got):
        return low(wide(keep) + wide(got))

    def columns_first(grad):
        grad = grad.reshape((2, 2, 2) + low_shape + (weight_rows, -1))
        return part_sent(grad, 2 + len(lows), lows[-1])

    def columns_mid(keep, got):
        values = part_sum(keep, got)
        for i in range(len(lows) - 2, -1, -1):
            values = part_sum(*part_sent(values, 3 + i, lows[i]))
        return values

    def columns_third(keep, got):
        values = part_sum(keep, got)
        mine = lax.dynamic_index_in_dim(values, in_team, 1, keepdims=False)
        send = lax.dynamic_index_in_dim(values, 1 - in_team, 1, keepdims=False)
        return values, (mine, swap_blk(send, team))

    def rows_second(keep, got):
        values = part_sum(keep, got)
        for i in range(len(lows) - 2, -1, -1):
            values = part_sum(*part_sent(values, 1 + i, lows[i]))
        return part_sent(values, 0, bits[0])

    def columns_last(mine, got):
        return jnp.stack(
            [jnp.where(mine_team, got, mine), jnp.where(mine_team, mine, got)], axis=1
        )

    first_a = columns_first(column_grad_a)
    hidden_b, d_gate_b, d_up_b, d_htwo_part = middle(
        order, after(h_team, (column_grad_a, down_grad_a)), dy_team, gate_up_b, down_b, part_a
    )

    def chip_sum(values, came):
        return low(wide(values[:chip_rows]) + wide(came))

    def scatter_far(chip):
        far = chip[3 * token_count :]
        return swap_blk(far[:half], team), swap_cross(far[half:])

    def scatter_near(chip, first, second):
        cross, over = (chip[token_count * i : token_count * (i + 1)] for i in (1, 2))
        cross = jnp.concatenate([low(wide(cross[:half]) + wide(first)), cross[half:]])
        over = jnp.concatenate([over[:half], low(wide(over[half:]) + wide(second))])
        return swap_cross(cross), swap_blk(over, team)

    near_att_cross = swap_cross(after(att_in, hidden_a))
    d_htwo_part = after(d_htwo_part, (first_a[1], down_share_a, near_att_cross))
    d_came = swap_core(d_htwo_part[chip_rows:])
    down_grad_b = down_grad(hidden_b, dy_team)
    rows_b = part_sent(
        down_grad_b.reshape((2,) + low_shape + (size_second, D)), len(lows), lows[-1]
    )
    mid_a = columns_mid(*after(first_a, d_came))
    second_a = part_sent(mid_a, 1, bits[0])
    d_chip = chip_sum(d_htwo_part, after(d_came, down_grad_b))
    d_far = scatter_far(d_chip)
    column_grad_b = two_grads(h_team, *after((d_gate_b, d_up_b), d_chip))
    first_b = columns_first(column_grad_b)
    d_far = after(d_far, column_grad_b)
    d_cross, d_over = scatter_near(d_chip, *d_far)
    out_part = down(*after((hidden_a, hidden_b), d_far), down_a, down_b, token_count)
    out_came = swap_core(out_part[chip_rows:])
    d_cross, d_over = after((d_cross, d_over), out_part)
    d_htwo = wide(d_chip[:token_count]) + wide(d_cross) + wide(d_over)

    norm_value_two, norm_back_two = jax.vjp(norm_apply, resid, gain_two)
    d_resid_norm, grad_gain_two = norm_back_two(d_htwo)
    d_resid = wide(dy_low) + d_resid_norm
    d_att = low(d_resid)
    rows_b = rows_second(*after(rows_b, d_att))

    d_attended = low(right_transposed(d_att, out_full))
    own_angles = angles_of(positions)
    cosine, sine = jnp.cos(own_angles), jnp.sin(own_angles)
    d_query, dkv = attend_back(
        attend_ids,
        query,
        kv_all,
        seg_key,
        seg_query,
        att_in,
        d_attended,
        lse,
        jnp.concatenate([cosine, cosine], axis=1),
        jnp.concatenate([sine, sine], axis=1),
        block_len,
    )
    dkv = lax.psum_scatter(
        dkv.reshape(blk_count * token_count, 2 * KVD),
        ("grp", "blk"),
        scatter_dimension=0,
        axis_index_groups=ring_groups(blk_count),
        tiled=True,
    )
    down_share_b = part_sum(*after(rows_b, d_query))
    sum_a, third_a = columns_third(*after(second_a, d_att))

    def to_strips(parts):
        return jnp.concatenate(exchange_near(by_place(parts)))

    near_dq = to_strips([d_query[:, strip_q * k : strip_q * (k + 1)] for k in range(4)])
    block_shape = (2,) * len(bits) + (weight_rows, -1)
    query_grad = low(left_product(near_one, near_dq)).reshape(block_shape)
    steps_query = part_sent(query_grad, len(bits) - 1, bits[-1])
    second_b = part_sent(columns_mid(*after(first_b, d_query)), 1, bits[0])
    dkv = after(dkv, down_share_b)
    own_part, core_part, far_part, bias_kv = turn_dkv(
        ids, dkv, jnp.concatenate([cosine, cosine], axis=1), jnp.concatenate([sine, sine], axis=1)
    )
    bias_q = jnp.sum(wide(d_query), axis=0)
    d_key = own_part
    cross_part = swap_cross(far_part)
    near_a = gather_near_stacked(columns_last(*after(third_a, own_part)))
    core_part = swap_core(jnp.stack([core_part, cross_part[1]]))
    kv_grad, hone_here, hone_there = make_kv_grad(
        blk_count,
        weight_rows,
        small_count,
        own_part,
        cross_part,
        core_part,
        near_dq,
        near_one,
        token_send,
        token_cross,
        token_core,
        strip,
        grad_gain_two[None],
        bias_q[None],
        bias_kv,
    )
    vector_rows = -(-small_count // HD)
    kv_grad = kv_grad.reshape((2,) * len(bits) + kv_grad.shape[1:])
    steps_kv = part_sent(kv_grad, len(bits) - 1, bits[-1])
    share_down = after(jnp.concatenate([down_share_a, down_share_b]), dkv)
    grad_down = lax.all_gather(share_down, "grp", axis=0, tiled=True)
    for i in range(len(bits) - 2, -1, -1):
        steps_query = part_sent(part_sum(*after(steps_query, d_key)), i, bits[i])
        kv_sum = part_sum(*steps_kv)
        kv_grad = kv_sum
        steps_kv = part_sent(kv_sum, i, bits[i])
    sum_b, third_b = columns_third(*after(second_b, kv_grad))
    share_kv_all = wide(steps_kv[0]) + wide(after(steps_kv[1], third_b[1]))
    share_kv = low(share_kv_all[:weight_rows])
    vector_part = share_kv_all[weight_rows : weight_rows + vector_rows]
    share_query = part_sum(*after(steps_query, kv_grad))
    near_att = swap_core(jnp.stack([att_in, near_att_cross]))
    near_att = jnp.concatenate([att_in, near_att[0], near_att_cross, near_att[1]])
    near_datt = to_strips([d_att[:, strip_q * k : strip_q * (k + 1)] for k in range(4)])
    out_grad = low(left_product(near_att, after(near_datt, d_attended))).reshape(block_shape)
    steps_out = part_sent(out_grad, len(bits) - 1, bits[-1])
    anchors = [near_dq, near_dq]
    for i in range(len(bits) - 2, -1, -1):
        anchor = anchors[min(len(bits) - 2 - i, 1)]
        steps_out = part_sent(part_sum(*after(steps_out, anchor)), i, bits[i])
    share_out = part_sum(*after(steps_out, kv_grad))

    grad_out = jnp.concatenate(gather_grp(share_out), axis=1)
    query_parts = gather_grp(share_query)
    key_parts = gather_grp(share_kv)
    grad_attend = jnp.concatenate(query_parts + [key_parts[k] for k in (0, 2, 1, 3)], axis=1)

    other = wide(swap_core(hone_there))
    d_hone = wide(hone_here[:token_count]) + other[:token_count]
    d_hone_cross = swap_cross(low(wide(hone_here[token_count:]) + other[token_count:]))
    square_sum = square_total(
        [
            wide(s)
            for s in (share_query, share_kv, share_out, sum_a, sum_b, share_down)
        ]
    )
    packed = jnp.concatenate([vector_part, jnp.full((8, HD), square_sum)])
    packed = packed + swap_cross(packed)
    packed = packed + swap_core(packed)
    share_vector = packed[:vector_rows].reshape(-1)[:small_count]
    square_sum = packed[vector_rows:] + jnp.sum(share_vector * share_vector)
    for bit in bits:
        square_sum = square_sum + swap_blk(square_sum, bit)
    grad_norm = jnp.sqrt(square_sum[0, 0])
    factor = jnp.minimum(1.0, CLIP_NORM / (grad_norm + 1e-06))
    out_chip = chip_sum(out_part, after(out_came, kv_grad))
    out_far = scatter_far(out_chip)
    factor = after(factor, (out_chip, near_a))

    new_first_attend, new_second_attend, new_attend = adam_step(
        w_attend, factor * wide(grad_attend), first_attend, second_attend, RATE_ATTEND, WEIGHT_DECAY
    )
    new_first_out, new_second_out, new_out = adam_step(
        w_out, factor * wide(grad_out), first_out, second_out, RATE_OUT, WEIGHT_DECAY
    )
    new_first_down, new_second_down, new_down = adam_step(
        w_down, factor * wide(grad_down), first_down, second_down, RATE_DOWN, WEIGHT_DECAY
    )
    own_b = columns_last(*third_b)
    cross_b = after(swap_cross(own_b), new_down)
    near_b = jnp.stack([own_b, cross_b])
    near_b = jnp.concatenate([near_b, swap_core(near_b)])
    new_first_gate, new_second_gate, new_gate = adam_columns(
        0, ids, factor[None], near_a, near_b, w_gate, first_gate, second_gate, blk_count, RATE_GATE, WEIGHT_DECAY
    )
    new_first_up, new_second_up, new_up = adam_columns(
        1, ids, factor[None], near_a, near_b, w_up, first_up, second_up, blk_count, RATE_GATE, WEIGHT_DECAY
    )
    norm_value_one, norm_back_one = jax.vjp(norm_apply, flat, gain_one)
    d_hone = after(d_hone + wide(after(d_hone_cross, new_gate)), new_gate)
    d_flat_norm, unused_gain = norm_back_one(d_hone)
    grad_tokens = low(d_resid + d_flat_norm)

    new_first_small, new_second_small, new_small = adam_step(
        small_params, factor * share_vector, first_small, second_small, RATE_VECTOR, 0.0
    )

    out_near = after(scatter_near(out_chip, *after(out_far, factor)), (new_gate, new_up))
    out_tokens = low(resid + wide(out_chip[:token_count]) + wide(out_near[0]) + wide(out_near[1]))
    return (
        out_tokens.reshape(rows_here, block_len, D),
        grad_tokens.reshape(rows_here, block_len, D),
        grad_norm,
        new_first_attend,
        new_second_attend,
        new_attend,
        new_first_out,
        new_second_out,
        new_out,
        new_first_gate,
        new_second_gate,
        new_gate,
        new_first_up,
        new_second_up,
        new_up,
        new_first_down,
        new_second_down,
        new_down,
        new_first_small,
        new_second_small,
        new_small,
    )


def solution(mesh):
    placed = (
        P("grp", "blk", None),
        P("grp", "blk", None),
        P("grp", "blk"),
        P("grp", "blk"),
        P("blk", None),
        P("blk", None),
        P("blk", None),
        P("blk", None),
        P("blk", None),
        P("blk"),
        P("blk", None),
        P("blk", None),
        P("blk", None),
        P("blk", None),
        P("blk", None),
        P("blk"),
        P("blk", None),
        P("blk", None),
        P("blk", None),
        P("blk", None),
        P("blk", None),
        P("blk"),
    )
    return jax.shard_map(
        on_device,
        mesh=mesh,
        in_specs=placed,
        out_specs=(
            P("grp", "blk", None),
            P("grp", "blk", None),
            P(),
            P("blk", None),
            P("blk", None),
            P("blk", None),
            P("blk", None),
            P("blk", None),
            P("blk", None),
            P("blk", None),
            P("blk", None),
            P("blk", None),
            P("blk", None),
            P("blk", None),
            P("blk", None),
            P("blk", None),
            P("blk", None),
            P("blk", None),
            P("blk"),
            P("blk"),
            P("blk"),
        ),
        check_vma=False,
    )
```

```python
import functools

import jax
import jax.numpy as jnp
from jax import lax
from jax.experimental import pallas as pl
from jax.experimental.pallas import tpu as pltpu
from jax.sharding import PartitionSpec as P

D = 1536
FF = 8960
H = 12
KVH = 2
HD = 128
STEP = 10
HQD = 1536
KVD = 256


NORM_EPS = 1e-06
ROPE_BASE = 10000.0
CLIP_NORM = 1.0
BETA_FIRST = 0.9
BETA_SECOND = 0.95
ADAM_EPS = 1e-08
WEIGHT_DECAY = 0.1
RATE_ATTEND = 0.06
RATE_OUT = 0.5
RATE_GATE = 0.06
RATE_DOWN = 0.03
RATE_VECTOR = 0.5
NEG_LARGE = -1e30
LOG2E = 1.4426950408889634
VMEM = 48 * 1024 * 1024
SMALL_COST = pl.CostEstimate(flops=1000, bytes_accessed=1000, transcendentals=0)


def norm_apply(values, gain):
    return values * lax.rsqrt(jnp.mean(values * values, axis=-1, keepdims=True) + NORM_EPS) * gain


def swish_product(gate, up_proj):
    return jax.nn.silu(gate) * up_proj


def left_product(left_side, right_side):
    return lax.dot_general(
        left_side, right_side, (((0,), (0,)), ((), ())), preferred_element_type=jnp.float32
    )


def right_transposed(left_side, right_side):
    return lax.dot_general(
        left_side, right_side, (((1,), (1,)), ((), ())), preferred_element_type=jnp.float32
    )


def square_total(arrays):
    return sum((jnp.sum(member * member) for member in arrays))


def adam_step(weight, grad, first, second, rate, decay):
    first_new = BETA_FIRST * first + (1.0 - BETA_FIRST) * grad
    second_new = BETA_SECOND * second + (1.0 - BETA_SECOND) * grad * grad
    first_hat = first_new / (1.0 - BETA_FIRST**STEP)
    second_hat = second_new / (1.0 - BETA_SECOND**STEP)
    weight_new = weight - rate * (first_hat / (jnp.sqrt(second_hat) + ADAM_EPS) + decay * weight)
    return (first_new, second_new, weight_new)


def ring_order(count):
    return list(range(0, count, 2)) + list(range(count - 1, 0, -2))


def halves_of(quarter):
    first = quarter * 16 // 35
    return ((0, first), (first, quarter - first))


def pick_body(blk_count, ids, gate_ref, up_ref, *out_refs):
    quarter = FF // blk_count // 4
    per = blk_count // 4
    for k in range(4):

        @pl.when(ids[0] == k)
        def _(k=k):
            for (at, size), out_ref in zip(halves_of(quarter), out_refs):
                for which, src in enumerate((gate_ref, up_ref)):
                    for bit in range(2):
                        parts = []
                        for high in range(2):
                            for small in range(per):
                                begin = (((high * 2 + bit) * per + small) * 4 + k) * quarter + at
                                parts.append(src[:, begin : begin + size])
                        out_ref[ids[1] ^ bit, which] = jnp.concatenate(parts, axis=1).astype(
                            jnp.bfloat16
                        )


def pick_columns(ids, gate, up, blk_count):
    rows = gate.shape[0]
    step = 48 if rows % 48 == 0 else rows
    widths = [size * blk_count // 2 for at, size in halves_of(FF // blk_count // 4)]
    spec = pl.BlockSpec((step, FF), lambda i, ids: (i, 0))
    return pl.pallas_call(
        functools.partial(pick_body, blk_count),
        grid_spec=pltpu.PrefetchScalarGridSpec(
            num_scalar_prefetch=1,
            grid=(rows // step,),
            in_specs=[spec, spec],
            out_specs=[pl.BlockSpec((2, 2, step, w), lambda i, ids: (0, 0, i, 0)) for w in widths],
        ),
        out_shape=[jax.ShapeDtypeStruct((2, 2, rows, w), jnp.bfloat16) for w in widths],
        compiler_params=pltpu.CompilerParams(vmem_limit_bytes=VMEM),
        cost_estimate=SMALL_COST,
        name="pick_columns",
    )(ids, gate, up)


def adam_body(blk_count, rate, decay, ids, factor_ref, first_ref, first_far_ref, second_ref, second_far_ref, w_ref, m_ref, v_ref, m_out, v_out, w_out):
    per = blk_count // 4
    sizes = [size for at, size in halves_of(FF // blk_count // 4)]
    grads = []
    for near_ref, far_ref in ((first_ref, first_far_ref), (second_ref, second_far_ref)):
        by_grp = []
        for k in range(4):
            away = ids[0] ^ k
            bits_of_k = []
            for bit in range(2):
                near = near_ref[away >> 1, bit].astype(jnp.float32)
                far = far_ref[away >> 1, bit].astype(jnp.float32)
                bits_of_k.append(jnp.where((away & 1) == 1, far, near))
            by_grp.append(bits_of_k)
        grads.append(by_grp)
    parts = []
    for high in range(2):
        for bit in range(2):
            for small in range(per):
                place = high * per + small
                for k in range(4):
                    for part, size in zip(grads, sizes):
                        parts.append(part[k][bit][:, place * size : (place + 1) * size])
    grad = jnp.concatenate(parts, axis=1) * factor_ref[0]
    m, v, w = adam_step(w_ref[...], grad, m_ref[...], v_ref[...], rate, decay)
    m_out[...] = m
    v_out[...] = v
    w_out[...] = w


def adam_columns(which, ids, factor, first, second, w, m, v, blk_count, rate, decay):
    rows = w.shape[0]
    step = 32 if rows % 32 == 0 else rows
    spec = pl.BlockSpec((step, FF), lambda i, ids: (i, 0))
    shape = jax.ShapeDtypeStruct((rows, FF), jnp.float32)
    grads = [
        pl.BlockSpec((2, None, 2, step, g.shape[-1]), lambda i, ids: (0, which, 0, i, 0))
        for g in first + second
    ]
    return pl.pallas_call(
        functools.partial(adam_body, blk_count, rate, decay),
        grid_spec=pltpu.PrefetchScalarGridSpec(
            num_scalar_prefetch=1,
            grid=(rows // step,),
            in_specs=[pl.BlockSpec(memory_space=pltpu.SMEM)] + grads + [spec, spec, spec],
            out_specs=[spec, spec, spec],
        ),
        out_shape=[shape] * 3,
        compiler_params=pltpu.CompilerParams(vmem_limit_bytes=VMEM),
        cost_estimate=SMALL_COST,
        name="adam_columns",
    )(ids, factor, *first, *second, w, m, v)


def nt(a, b, **kw):
    return lax.dot_general(a, b, (((1,), (1,)), ((), ())), preferred_element_type=jnp.float32, **kw)

def tn(a, b, **kw):
    return lax.dot_general(a, b, (((0,), (0,)), ((), ())), preferred_element_type=jnp.float32, **kw)

def stack_heads(ref, kvh, group):
    return jnp.concatenate([ref[:, HD * (kvh * group + i): HD * (kvh * group + i + 1)] for i in range(group)], axis=0)

def hidden_from(seg_key_ref, seg_query_ref, first, chunk, block_len, blk):
    key = first + lax.broadcasted_iota(jnp.int32, (chunk, block_len), 0)
    query = blk * block_len + lax.broadcasted_iota(jnp.int32, (chunk, block_len), 1)
    seg_key = seg_key_ref[pl.ds(first, chunk), :]
    counts = jnp.logical_and(key <= query, seg_key == seg_query_ref[0:1, :])
    return jnp.where(counts, 0.0, NEG_LARGE)

def ring_pair(ref, c, at):
    return jnp.concatenate(
        [ref[c, :, at : at + HD], ref[ref.shape[0] - 1 - c, :, at : at + HD]], axis=0
    )


def attend_body(chunk, ids, q_ref, k_ref, v_ref, seg_key_ref, seg_query_ref, o_ref, lse_ref, m_s, l_s, acc_s):
    block_len = q_ref.shape[0]
    group = H // KVH
    row = pl.program_id(0)
    per = chunk // block_len
    scale = HD ** (-0.5) * LOG2E
    start = ids[1 + row] // per
    stop = ids[0] // per + 1
    for kvh in range(KVH):
        q = stack_heads(q_ref, kvh, group)
        m_s[...] = jnp.full_like(m_s, NEG_LARGE)
        l_s[...] = jnp.zeros_like(l_s)
        acc_s[...] = jnp.zeros_like(acc_s)

        def step(c, carry):
            keys = ring_pair(k_ref, c, HD * kvh)
            vals = ring_pair(v_ref, c, HD * kvh)
            bias = hidden_from(seg_key_ref, seg_query_ref, c * chunk, chunk, block_len, ids[0])
            s = nt(keys, q) * scale + jnp.concatenate([bias] * group, axis=1)
            old = m_s[0:1, :]
            new = jnp.maximum(old, jnp.max(s, axis=0, keepdims=True))
            p = jnp.exp2(s - new)
            fade = jnp.exp2(old - new)
            l_s[0:1, :] = l_s[0:1, :] * fade + jnp.sum(p, axis=0, keepdims=True)
            acc_s[...] = acc_s[...] * fade + tn(vals, p.astype(jnp.bfloat16))
            m_s[0:1, :] = new
            return carry

        lax.fori_loop(start, stop, step, 0)
        total = l_s[0:1, :]
        out = (acc_s[...] * (1.0 / total)).T
        for i in range(group):
            o_ref[:, HD * (kvh * group + i): HD * (kvh * group + i + 1)] = out[block_len * i: block_len * (i + 1), :].astype(jnp.bfloat16)
        lse_ref[kvh] = jnp.broadcast_to(m_s[0:1, :] + jnp.log2(total), (8, group * block_len))

def attend(ids, q, kv, seg_key, seg_query, block_len):
    blk_count, rows = kv.shape[:2]
    group = H // KVH
    chunk = 2 * block_len
    many = group * block_len
    return pl.pallas_call(
        functools.partial(attend_body, chunk),
        grid_spec=pltpu.PrefetchScalarGridSpec(
            num_scalar_prefetch=1, grid=(rows,),
            in_specs=[
                pl.BlockSpec((block_len, HQD), lambda r, ids: (r, 0)),
                pl.BlockSpec((blk_count, None, block_len, KVD), lambda r, ids: (0, r, 0, 0)),
                pl.BlockSpec((blk_count, None, block_len, KVD), lambda r, ids: (0, r, 0, 1)),
                pl.BlockSpec((None, blk_count * block_len, HD), lambda r, ids: (r, 0, 0)),
                pl.BlockSpec((None, 8, block_len), lambda r, ids: (r, 0, 0)),
            ],
            out_specs=[
                pl.BlockSpec((block_len, HQD), lambda r, ids: (r, 0)),
                pl.BlockSpec((None, KVH, 8, many), lambda r, ids: (r, 0, 0, 0)),
            ],
            scratch_shapes=[pltpu.VMEM((8, many), jnp.float32), pltpu.VMEM((8, many), jnp.float32), pltpu.VMEM((HD, many), jnp.float32)]),
        out_shape=[
            jax.ShapeDtypeStruct((rows * block_len, HQD), jnp.bfloat16),
            jax.ShapeDtypeStruct((rows, KVH, 8, many), jnp.float32),
        ],
        compiler_params=pltpu.CompilerParams(vmem_limit_bytes=VMEM),
        cost_estimate=SMALL_COST,
        name="attend",
    )(ids, q, kv, kv, seg_key, seg_query)

def turn_back(u, cosine, sine):
    lane = lax.broadcasted_iota(jnp.int32, u.shape, 1)
    other = pltpu.roll(u, HD // 2, 1)
    return u * cosine + jnp.where(lane < HD // 2, other, -other) * sine

def attend_back_body(chunk, ids, q_ref, k_ref, v_ref, seg_key_ref, seg_query_ref, o_ref, do_ref, lse_ref, cos_ref, sin_ref, dq_ref, dkv_ref, dq_s):
    block_len = q_ref.shape[0]
    group = H // KVH
    row = pl.program_id(0)
    per = chunk // block_len
    plain = HD ** (-0.5)
    scale = plain * LOG2E
    start = ids[1 + row] // per
    stop = ids[0] // per + 1
    dkv_ref[...] = jnp.zeros_like(dkv_ref)
    for kvh in range(KVH):
        q = stack_heads(q_ref, kvh, group)
        do = stack_heads(do_ref, kvh, group)
        o = stack_heads(o_ref, kvh, group)
        both = do.astype(jnp.float32) * o.astype(jnp.float32)
        delta = nt(jnp.ones((8, HD), jnp.float32), both, precision=lax.Precision.HIGHEST)[0:1, :]
        lse = lse_ref[kvh][0:1, :]
        dq_s[...] = jnp.zeros_like(dq_s)

        def step(c, carry):
            keys = ring_pair(k_ref, c, HD * kvh)
            vals = ring_pair(v_ref, c, HD * kvh)
            bias = hidden_from(seg_key_ref, seg_query_ref, c * chunk, chunk, block_len, ids[0])
            s = nt(keys, q) * scale + jnp.concatenate([bias] * group, axis=1)
            p = jnp.exp2(s - lse)
            dp = nt(vals, do)
            ds = (p * (dp - delta)).astype(jnp.bfloat16)
            dk = jnp.dot(ds, q, preferred_element_type=jnp.float32) * plain
            dv = jnp.dot(p.astype(jnp.bfloat16), do, preferred_element_type=jnp.float32)
            for at, part in ((HD * kvh, dk.astype(jnp.bfloat16)), (KVD + HD * kvh, dv.astype(jnp.bfloat16))):
                dkv_ref[c, :, at : at + HD] = part[:block_len]
                dkv_ref[dkv_ref.shape[0] - 1 - c, :, at : at + HD] = part[block_len:]
            dq_s[...] += tn(ds, keys)
            return carry

        lax.fori_loop(start, stop, step, 0)
        cosine, sine = cos_ref[...], sin_ref[...]
        for i in range(group):
            u = dq_s[block_len * i: block_len * (i + 1), :] * plain
            at = HD * (kvh * group + i)
            dq_ref[:, at: at + HD] = turn_back(u, cosine, sine).astype(jnp.bfloat16)

def attend_back(ids, q, kv, seg_key, seg_query, o, do, lse, cosine, sine, block_len):
    blk_count, rows = kv.shape[:2]
    group = H // KVH
    chunk = 2 * block_len
    many = group * block_len
    per_row = pl.BlockSpec((block_len, HQD), lambda r, ids: (r, 0))
    turn = pl.BlockSpec((block_len, HD), lambda r, ids: (r, 0))
    return pl.pallas_call(
        functools.partial(attend_back_body, chunk),
        grid_spec=pltpu.PrefetchScalarGridSpec(
            num_scalar_prefetch=1, grid=(rows,),
            in_specs=[
                per_row,
                pl.BlockSpec((blk_count, None, block_len, KVD), lambda r, ids: (0, r, 0, 0)),
                pl.BlockSpec((blk_count, None, block_len, KVD), lambda r, ids: (0, r, 0, 1)),
                pl.BlockSpec((None, blk_count * block_len, HD), lambda r, ids: (r, 0, 0)),
                pl.BlockSpec((None, 8, block_len), lambda r, ids: (r, 0, 0)),
                per_row, per_row,
                pl.BlockSpec((None, KVH, 8, many), lambda r, ids: (r, 0, 0, 0)),
                turn, turn,
            ],
            out_specs=[per_row, pl.BlockSpec((blk_count, None, block_len, 2 * KVD), lambda r, ids: (0, r, 0, 0))],
            scratch_shapes=[pltpu.VMEM((many, HD), jnp.float32)]),
        out_shape=[
            jax.ShapeDtypeStruct((rows * block_len, HQD), jnp.bfloat16),
            jax.ShapeDtypeStruct((blk_count, rows, block_len, 2 * KVD), jnp.bfloat16),
        ],
        compiler_params=pltpu.CompilerParams(vmem_limit_bytes=VMEM),
        cost_estimate=SMALL_COST,
        name="attend_back",
    )(ids, q, kv, kv, seg_key, seg_query, o, do, lse, cosine, sine)

def nn(a, b):
    return jnp.dot(a, b, preferred_element_type=jnp.float32)


def middle_body(add, order, h_ref, dy_ref, wg_ref, wu_ref, wd_ref, *refs):
    prev_refs = refs[:2] if add else None
    hid_ref, dg_ref, du_ref, dh_ref, dh_far_ref = refs[-5:]
    here = pl.program_id(0) < 4
    h = h_ref[...]
    gate = nn(h, wg_ref[...])
    up = nn(h, wu_ref[...])
    sig = 1.0 / (1.0 + jnp.exp(-gate))
    silu = gate * sig
    hid_ref[...] = (silu * up).astype(jnp.bfloat16)
    dhid = nt(dy_ref[...], wd_ref[...])
    dg = (dhid * up * sig * (1.0 + gate * (1.0 - sig))).astype(jnp.bfloat16)
    du = (dhid * silu).astype(jnp.bfloat16)
    dg_ref[...] = dg
    du_ref[...] = du
    dh = nt(dg, wg_ref[...]) + nt(du, wu_ref[...])
    if add:
        prev = jnp.where(here, prev_refs[0][...].astype(jnp.float32), prev_refs[1][...].astype(jnp.float32))
        dh = dh + prev
    dh = dh.astype(jnp.bfloat16)

    @pl.when(here)
    def _():
        dh_ref[...] = dh

    @pl.when(jnp.logical_not(here))
    def _():
        dh_far_ref[...] = dh


def middle(order, h, dy, gate_up, wd, prev=None):
    count = h.shape[0]
    step = count // order.shape[0]
    wide_here = wd.shape[0]
    row = pl.BlockSpec((step, D), lambda i, order: (i, 0))
    placed = pl.BlockSpec((step, D), lambda i, order: (order[i], 0))
    part = pl.BlockSpec((step, wide_here), lambda i, order: (i, 0))
    part_placed = pl.BlockSpec((step, wide_here), lambda i, order: (order[i], 0))
    once = pl.Buffered(1)
    extra = [] if prev is None else list(prev)
    near = pl.BlockSpec((step, D), lambda i, order: (jnp.minimum(i, 3), 0))
    far = pl.BlockSpec((step, D), lambda i, order: (jnp.maximum(i - 4, 0), 0))
    return pl.pallas_call(
        functools.partial(middle_body, prev is not None),
        grid_spec=pltpu.PrefetchScalarGridSpec(
            num_scalar_prefetch=1,
            grid=(count // step,),
            in_specs=[
                placed,
                row,
                pl.BlockSpec((None, D, wide_here), lambda i, order: (0, 0, 0), pipeline_mode=once),
                pl.BlockSpec((None, D, wide_here), lambda i, order: (1, 0, 0), pipeline_mode=once),
                pl.BlockSpec((wide_here, D), lambda i, order: (0, 0), pipeline_mode=once),
            ]
            + [near, far][: len(extra)],
            out_specs=[part, part_placed, part_placed, near, far],
        ),
        out_shape=[jax.ShapeDtypeStruct((count, wide_here), jnp.bfloat16)] * 3
        + [jax.ShapeDtypeStruct((count // 2, D), jnp.bfloat16)] * 2,
        compiler_params=pltpu.CompilerParams(vmem_limit_bytes=VMEM),
        cost_estimate=SMALL_COST,
        name="middle",
    )(order, h, dy, gate_up, gate_up, wd, *extra)


def two_grads_body(h_ref, a_ref, b_ref, out_ref):
    h = h_ref[...]
    out_ref[0] = tn(h, a_ref[...]).astype(jnp.bfloat16)
    out_ref[1] = tn(h, b_ref[...]).astype(jnp.bfloat16)


def two_grads(h, a, b, step=256):
    count = h.shape[0]
    wide_here = a.shape[1]
    whole = pl.BlockSpec(a.shape, lambda i: (0, 0), pipeline_mode=pl.Buffered(1))
    return pl.pallas_call(
        two_grads_body,
        grid=(D // step,),
        in_specs=[pl.BlockSpec((count, step), lambda i: (0, i)), whole, whole],
        out_specs=pl.BlockSpec((2, step, wide_here), lambda i: (0, i, 0)),
        out_shape=jax.ShapeDtypeStruct((2, D, wide_here), jnp.bfloat16),
        compiler_params=pltpu.CompilerParams(vmem_limit_bytes=VMEM),
        cost_estimate=SMALL_COST,
        name="two_grads",
    )(h, a, b)


def down_grad_body(hid_ref, dy_ref, g_ref):
    g_ref[...] = tn(hid_ref[...], dy_ref[...]).astype(jnp.bfloat16)

def down_grad(hid, dy, step=512):
    T, F = hid.shape
    D = dy.shape[1]
    return pl.pallas_call(down_grad_body, grid=(D // step,),
        in_specs=[pl.BlockSpec((T, F), lambda i: (0, 0), pipeline_mode=pl.Buffered(1)), pl.BlockSpec((T, step), lambda i: (0, i))],
        out_specs=pl.BlockSpec((F, step), lambda i: (0, i)),
        out_shape=jax.ShapeDtypeStruct((F, D), jnp.bfloat16),
        compiler_params=pltpu.CompilerParams(vmem_limit_bytes=VMEM),
        cost_estimate=SMALL_COST,
        name="down_grad")(hid, dy)

def down_body(hid_a_ref, hid_b_ref, wd_a_ref, wd_b_ref, o_ref, o_far_ref):
    out = nn(hid_a_ref[...], wd_a_ref[...]) + nn(hid_b_ref[...], wd_b_ref[...])
    out = out.astype(jnp.bfloat16)
    here = pl.program_id(0) < 4

    @pl.when(here)
    def _():
        o_ref[...] = out

    @pl.when(jnp.logical_not(here))
    def _():
        o_far_ref[...] = out


def down(hid_a, hid_b, wd_a, wd_b, step):
    count = hid_a.shape[0]

    def rows(array):
        return pl.BlockSpec((step, array.shape[1]), lambda i: (i, 0))

    def whole(array):
        return pl.BlockSpec(array.shape, lambda i: (0, 0), pipeline_mode=pl.Buffered(1))

    return pl.pallas_call(
        down_body,
        grid=(count // step,),
        in_specs=[rows(hid_a), rows(hid_b), whole(wd_a), whole(wd_b)],
        out_specs=[
            pl.BlockSpec((step, D), lambda i: (jnp.minimum(i, 3), 0)),
            pl.BlockSpec((step, D), lambda i: (jnp.maximum(i - 4, 0), 0)),
        ],
        out_shape=[jax.ShapeDtypeStruct((count // 2, D), jnp.bfloat16)] * 2,
        compiler_params=pltpu.CompilerParams(vmem_limit_bytes=VMEM),
        cost_estimate=SMALL_COST,
        name="down",
    )(hid_a, hid_b, wd_a, wd_b)


def turn(u, cosine, sine):
    lane = lax.broadcasted_iota(jnp.int32, u.shape, 1)
    other = pltpu.roll(u, HD // 2, 1)
    return u * cosine + jnp.where(lane < HD // 2, -other, other) * sine


def mix_body(
    blk_count, rows, small_count, ids, own_ref, cross_ref, core_ref, ring_ref, freq_ref,
    self_ref, near_ref, far_ref, one_ref, strip_ref, vector_ref,
):
    ring = ring_order(blk_count)
    wide_here = ring_ref.shape[-1]
    pieces = []
    for b in range(blk_count):
        at = ring.index(b)
        strip_ref[rows * b : rows * (b + 1)] = ring_ref[at, :rows]
        left = small_count
        line = rows
        while left > 0:
            size = min(left, wide_here)
            pieces.append(ring_ref[at, line : line + 1, :size].astype(jnp.float32))
            left -= size
            line += 1
    vector = jnp.concatenate(pieces, axis=1)
    vector_ref[...] = vector
    gain = vector[:, :D]
    grp = ids[0]
    strip_q = wide_here - HD
    bias = jnp.zeros((1, wide_here), jnp.float32)
    for k in range(4):
        kv_at = 2 * D + HQD + HD * (k // 2) + KVD * (k % 2)
        part = jnp.concatenate(
            [
                vector[:, 2 * D + strip_q * k : 2 * D + strip_q * (k + 1)],
                vector[:, kv_at : kv_at + HD],
            ],
            axis=1,
        )
        bias = bias + jnp.where(grp == k, part, 0.0)
    count = own_ref.shape[0]
    strip = strip_ref[...]
    for d in range(4):
        source = (own_ref[...], core_ref[0], cross_ref[...], core_ref[1])[d]
        x = source[:, :D].astype(jnp.float32)
        root = lax.rsqrt(jnp.mean(x * x, axis=1, keepdims=True) + NORM_EPS)
        one = (x * root * gain).astype(jnp.bfloat16)
        one_ref[count * d : count * (d + 1)] = one
        mixed = nn(one, strip) + bias
        digits = source[:, D : D + HD].astype(jnp.float32)
        position = 64.0 * digits[:, 0:1] + digits[:, 1:2]
        angles = position * freq_ref[...]
        cosine, sine = jnp.cos(angles), jnp.sin(angles)
        for i in range(wide_here // HD):
            c, s = cosine, sine
            if i == wide_here // HD - 1:
                c = jnp.where(grp % 2 == 1, 1.0, c)
                s = jnp.where(grp % 2 == 1, 0.0, s)
            at = HD * i
            out = turn(mixed[:, at : at + HD], c, s).astype(jnp.bfloat16)
            if d == 0:
                self_ref[:, at : at + HD] = out
            elif d == 1:
                near_ref[:, at : at + HD] = out
            else:
                far_ref[d - 2, :, at : at + HD] = out


def mix(ids, own, cross, core, ring, freq, blk_count, rows, small_count):
    count = own.shape[0]
    wide_here = ring.shape[-1]
    low16 = jnp.bfloat16
    return pl.pallas_call(
        functools.partial(mix_body, blk_count, rows, small_count),
        in_specs=[pl.BlockSpec(memory_space=pltpu.SMEM)] + [pl.BlockSpec(memory_space=pltpu.VMEM)] * 5,
        out_specs=[pl.BlockSpec(memory_space=pltpu.VMEM)] * 6,
        out_shape=[
            jax.ShapeDtypeStruct((count, wide_here), low16),
            jax.ShapeDtypeStruct((count, wide_here), low16),
            jax.ShapeDtypeStruct((2, count, wide_here), low16),
            jax.ShapeDtypeStruct((4 * count, D), low16),
            jax.ShapeDtypeStruct((D, wide_here), low16),
            jax.ShapeDtypeStruct((1, blk_count * small_count), jnp.float32),
        ],
        compiler_params=pltpu.CompilerParams(vmem_limit_bytes=VMEM),
        cost_estimate=SMALL_COST,
        name="mix",
    )(ids, own, cross, core, ring, freq)


def pack_body(ids, self_ref, cross_ref, core_ref, q_ref, kv_ref):
    strip_q = self_ref.shape[1] - HD
    for g in range(4):

        @pl.when(ids[0] == g)
        def _(g=g):
            for k in range(4):
                part = (self_ref[...], core_ref[0], cross_ref[0], core_ref[1])[g ^ k]
                q_ref[:, strip_q * k : strip_q * (k + 1)] = part[:, :strip_q]
                at = (k % 2) * KVD + (k // 2) * HD
                kv_ref[:, at : at + HD] = part[:, strip_q:]


def pack(ids, own, cross, core):
    count = own.shape[0]
    return pl.pallas_call(
        pack_body,
        in_specs=[pl.BlockSpec(memory_space=pltpu.SMEM)] + [pl.BlockSpec(memory_space=pltpu.VMEM)] * 3,
        out_specs=[pl.BlockSpec(memory_space=pltpu.VMEM)] * 2,
        out_shape=[
            jax.ShapeDtypeStruct((count, HQD), jnp.bfloat16),
            jax.ShapeDtypeStruct((count, 2 * KVD), jnp.bfloat16),
        ],
        compiler_params=pltpu.CompilerParams(vmem_limit_bytes=VMEM),
        cost_estimate=SMALL_COST,
        name="pack",
    )(ids, own, cross, core)


def turn_dkv_body(ids, dkv_ref, cos_ref, sin_ref, self_ref, near_ref, far_ref, sum_ref):
    items = []
    sums = [None] * 4
    for k in range(4):
        at = (k % 2) * KVD + (k // 2) * HD
        part = dkv_ref[:, at : at + HD]
        if k % 2 == 0:
            part = turn_back(part.astype(jnp.float32), cos_ref[...], sin_ref[...]).astype(jnp.bfloat16)
        items.append(part)
        sums[(k % 2) * 2 + k // 2] = jnp.sum(part.astype(jnp.float32), axis=0, keepdims=True)
    sum_ref[...] = jnp.concatenate(sums, axis=1)
    for g in range(4):

        @pl.when(ids[0] == g)
        def _(g=g):
            self_ref[...] = items[g]
            near_ref[...] = items[g ^ 1]
            far_ref[0] = items[g ^ 2]
            far_ref[1] = items[g ^ 3]


def turn_dkv(ids, dkv, cosine, sine):
    count = dkv.shape[0]
    return pl.pallas_call(
        turn_dkv_body,
        in_specs=[pl.BlockSpec(memory_space=pltpu.SMEM)] + [pl.BlockSpec(memory_space=pltpu.VMEM)] * 3,
        out_specs=[pl.BlockSpec(memory_space=pltpu.VMEM)] * 4,
        out_shape=[
            jax.ShapeDtypeStruct((count, HD), jnp.bfloat16),
            jax.ShapeDtypeStruct((count, HD), jnp.bfloat16),
            jax.ShapeDtypeStruct((2, count, HD), jnp.bfloat16),
            jax.ShapeDtypeStruct((1, 2 * KVD), jnp.float32),
        ],
        compiler_params=pltpu.CompilerParams(vmem_limit_bytes=VMEM),
        cost_estimate=SMALL_COST,
        name="turn_dkv",
    )(ids, dkv, cosine, sine)


def kv_grad_body(
    blk_count, rows, small_count, self_ref, cross_ref, core_ref, dq_ref, one_ref, own_ref, near_x_ref,
    core_x_ref, strip_ref, gain_two_ref, bias_q_ref, bias_kv_ref, grad_ref, here_ref, there_ref,
):
    count = self_ref.shape[0]
    strip_q = strip_ref.shape[1] - HD
    parts = (self_ref[...], core_ref[0], cross_ref[0], core_ref[1])
    near = jnp.concatenate(parts, axis=0)
    grad = tn(one_ref[...], near)
    gain_one = jnp.zeros((1, D), jnp.float32)
    for d in range(4):
        x = (own_ref[...], core_x_ref[0], near_x_ref[...], core_x_ref[1])[d][:, :D].astype(jnp.float32)
        root = lax.rsqrt(jnp.mean(x * x, axis=1, keepdims=True) + NORM_EPS)
        hone = nt(dq_ref[count * d : count * (d + 1)], strip_ref[:, :strip_q])
        hone = hone + nt(parts[d], strip_ref[:, strip_q:])
        gain_one = gain_one + jnp.sum(hone * x * root, axis=0, keepdims=True)
        out_ref = (here_ref, there_ref)[d % 2]
        out_ref[count * (d // 2) : count * (d // 2 + 1)] = hone.astype(jnp.bfloat16)
    vector = jnp.concatenate([gain_one, gain_two_ref[...], bias_q_ref[...], bias_kv_ref[...]], axis=1)
    extra = grad_ref.shape[1] - rows
    for b in range(blk_count):
        grad_ref[b, :rows] = grad[rows * b : rows * (b + 1)].astype(jnp.bfloat16)
        lines = []
        for line in range(extra):
            size = min(HD, max(small_count - line * HD, 0))
            begin = small_count * b + line * HD
            pieces = [vector[:, begin : begin + size]] if size > 0 else []
            if size < HD:
                pieces.append(jnp.zeros((1, HD - size), jnp.float32))
            lines.append(pieces[0] if len(pieces) == 1 else jnp.concatenate(pieces, axis=1))
        grad_ref[b, rows:] = jnp.concatenate(lines, axis=0).astype(jnp.bfloat16)


def kv_grad_rows(rows, small_count):
    needed = rows + -(-small_count // HD)
    return needed + -needed % 16


def make_kv_grad(blk_count, rows, small_count, own, cross, core, dq, one, x_own, x_cross, x_core, strip, gain_two, bias_q, bias_kv):
    count = own.shape[0]
    height = kv_grad_rows(rows, small_count)
    return pl.pallas_call(
        functools.partial(kv_grad_body, blk_count, rows, small_count),
        in_specs=[pl.BlockSpec(memory_space=pltpu.VMEM)] * 12,
        out_specs=[pl.BlockSpec(memory_space=pltpu.VMEM)] * 3,
        out_shape=[
            jax.ShapeDtypeStruct((blk_count, height, HD), jnp.bfloat16),
            jax.ShapeDtypeStruct((2 * count, D), jnp.bfloat16),
            jax.ShapeDtypeStruct((2 * count, D), jnp.bfloat16),
        ],
        compiler_params=pltpu.CompilerParams(vmem_limit_bytes=VMEM),
        cost_estimate=SMALL_COST,
        name="kv_grad",
    )(own, cross, core, dq, one, x_own, x_cross, x_core, strip, gain_two, bias_q, bias_kv)


CORE = [(0, 1), (1, 0), (2, 3), (3, 2)]
CROSS = [(0, 2), (2, 0), (1, 3), (3, 1)]
DIAG = [(0, 3), (3, 0), (1, 2), (2, 1)]


def low(values):
    return values.astype(jnp.bfloat16)


def wide(values):
    return values.astype(jnp.float32)


def swap_core(values):
    return lax.ppermute(values, "grp", CORE)


def swap_cross(values):
    return lax.ppermute(values, "grp", CROSS)


def swap_diag(values):
    return lax.ppermute(values, "grp", DIAG)


def swap_blk(values, bit):
    count = lax.axis_size("blk")
    return lax.ppermute(values, "blk", [(i, i ^ bit) for i in range(count)])


def blk_bit(bit):
    return (lax.axis_index("blk") & bit) != 0


def bits_of(count):
    out = []
    bit = count // 2
    while bit >= 1:
        out.append(bit)
        bit //= 2
    return out


def gather_bits(values, order):
    done = []
    for bit in order:
        other = swap_blk(values, bit)
        mine = blk_bit(bit)
        axis = sum(1 for d in done if d > bit)
        values = jnp.stack(
            [jnp.where(mine, other, values), jnp.where(mine, values, other)], axis=axis
        )
        done.append(bit)
    return values


def scatter_bits(values, axes, order):
    axes = list(axes)
    for bit in order:
        axis = axes.index(bit)
        mine = blk_bit(bit).astype(jnp.int32)
        keep = lax.dynamic_index_in_dim(values, mine, axis, keepdims=False)
        send = lax.dynamic_index_in_dim(values, 1 - mine, axis, keepdims=False)
        values = low(wide(keep) + wide(swap_blk(send, bit)))
        axes.remove(bit)
    return values


def by_place(parts):
    grp = lax.axis_index("grp")
    core = (grp & 1) != 0
    cross = (grp & 2) != 0
    a, b, c, d = parts
    a, b = jnp.where(core, b, a), jnp.where(core, a, b)
    c, d = jnp.where(core, d, c), jnp.where(core, c, d)
    a, c = jnp.where(cross, c, a), jnp.where(cross, a, c)
    b, d = jnp.where(cross, d, b), jnp.where(cross, b, d)
    return [a, b, c, d]


def gather_near(values):
    cross = swap_cross(values)
    both = swap_core(jnp.stack([values, cross]))
    return [values, both[0], cross, both[1]]


def gather_grp(values):
    return by_place(gather_near(values))


def gather_tokens(values, bit):
    half = values.shape[0] // 2
    cross = swap_cross(values)
    over = swap_blk(values, bit)
    first = swap_blk(cross[:half], bit)
    second = swap_cross(over[half:])
    chip = jnp.concatenate([values, cross, over, first, second])
    return jnp.concatenate([chip, swap_core(chip)])


def angles_of(position):
    half = HD // 2
    freqs = ROPE_BASE ** (-2.0 * jnp.arange(half, dtype=jnp.float32) / HD)
    return position.astype(jnp.float32)[:, None] * freqs[None, :]


def rotate_by(values, cosine, sine):
    half = HD // 2
    first_half = values[..., :half]
    second_half = values[..., half:]
    return jnp.concatenate(
        [first_half * cosine - second_half * sine, second_half * cosine + first_half * sine],
        axis=-1,
    )


def after(values, anchor):
    return lax.optimization_barrier((values, anchor))[0]


def gather_step(values, done, bit):
    other = swap_blk(values, bit)
    mine = blk_bit(bit)
    axis = sum(1 for d in done if d > bit)
    return jnp.stack(
        [jnp.where(mine, other, values), jnp.where(mine, values, other)], axis=axis
    )


def gather_near_stacked(values):
    both = jnp.stack([values, swap_cross(values)])
    return [both, swap_core(both)]


def ring_groups(count):
    return [[g * count + b for b in ring_order(count)] for g in range(4)]


def gather_ring(values):
    count = lax.axis_size("blk")
    return lax.all_gather(values, ("grp", "blk"), axis=0, axis_index_groups=ring_groups(count))


def exchange_near(parts):
    cross = swap_cross(jnp.stack([parts[2], parts[3]]))
    core = swap_core(jnp.stack([parts[1], cross[1]]))
    return [parts[0], core[0], cross[0], core[1]]


def on_device(
    tokens,
    cotangent,
    segment_ids,
    position_ids,
    w_attend,
    w_out,
    w_gate,
    w_up,
    w_down,
    small_params,
    first_attend,
    first_out,
    first_gate,
    first_up,
    first_down,
    first_small,
    second_attend,
    second_out,
    second_gate,
    second_up,
    second_down,
    second_small,
):
    rows_here, block_len = tokens.shape[:2]
    blk_count = lax.axis_size("blk")
    seq_len = block_len * blk_count
    token_count = rows_here * block_len
    grp = lax.axis_index("grp")
    blk = lax.axis_index("blk")
    cross_id, core_id = grp // 2, grp % 2
    strip_heads = H // 4
    strip_q = strip_heads * HD
    bits = bits_of(blk_count)
    team = blk_count // 4
    lows = [bit for bit in bits if bit < team]
    spread = [bits[0]] + lows
    low_shape = (2,) * len(lows)
    in_team = blk_bit(team).astype(jnp.int32)
    weight_rows = w_gate.shape[0]
    ff_block = w_down.shape[0]
    quarter = ff_block // 4
    widths = [size * blk_count // 2 for at, size in halves_of(quarter)]
    chip_rows = 4 * token_count
    half = token_count // 2

    ids = jnp.stack([grp, in_team])
    flat_low = tokens.reshape(token_count, D)
    dy_low = cotangent.reshape(token_count, D)
    positions = position_ids.reshape(token_count)
    kv_at = HQD + HD * cross_id + KVD * core_id
    strip_local = low(
        jnp.concatenate(
            [
                lax.dynamic_slice_in_dim(w_attend, strip_q * grp, strip_q, 1),
                lax.dynamic_slice_in_dim(w_attend, kv_at, HD, 1),
            ],
            axis=1,
        )
    )
    small_count = small_params.shape[0]
    small_send = jnp.concatenate([low(small_params), low(segment_ids.reshape(token_count))])
    strip_wide = strip_q + HD
    small_send = jnp.pad(small_send, (0, -small_send.shape[0] % (16 * strip_wide)))
    strip_local = jnp.concatenate([strip_local, small_send.reshape(-1, strip_wide)])
    ring = ring_order(blk_count)
    strip_ring = gather_ring(strip_local)
    small_ring = strip_ring[:, weight_rows:].reshape(blk_count, -1)[:, small_count : small_count + token_count]
    small_all = jnp.stack([small_ring[ring.index(b)] for b in range(blk_count)])
    digits = low(jnp.stack([positions // 64, positions % 64], axis=1))
    digits = jnp.pad(digits, ((0, 0), (0, HD - 2)))
    token_send = jnp.concatenate([flat_low, digits], axis=1)
    picked_a, picked_b = pick_columns(ids, w_gate, w_up, blk_count)
    got_a = swap_blk(picked_a[1], team)
    dy_cross = swap_cross(after(dy_low, picked_a))
    token_cross = after(swap_cross(token_send), (picked_a, strip_ring, got_a, dy_cross))

    def place(values, other, done, bit, lead=0):
        mine = blk_bit(bit)
        axis = lead + sum(1 for d in done if d > bit)
        return jnp.stack(
            [jnp.where(mine, other, values), jnp.where(mine, values, other)], axis=axis
        )

    mine_team = blk_bit(team)
    (low_first, size_first), (low_second, size_second) = halves_of(quarter)

    def team_pair(mine, got):
        return jnp.stack(
            [jnp.where(mine_team, got, mine), jnp.where(mine_team, mine, got)], axis=1
        )

    out_local = low(lax.dynamic_slice_in_dim(w_out, strip_q * grp, strip_q, 1))
    out_ring = gather_ring(after(out_local, strip_ring))
    down_here = low(lax.dynamic_slice_in_dim(w_down, quarter * grp, quarter, 0))
    token_core = swap_core(jnp.stack([token_send, token_cross]))
    freqs = ROPE_BASE ** (-2.0 * jnp.arange(HD // 2, dtype=jnp.float32) / HD)
    freqs = jnp.concatenate([freqs, freqs])[None]
    mixed_own, mixed_core, mixed_far, near_one, strip, vector = mix(
        ids, token_send, token_cross, token_core, strip_ring, freqs, blk_count, weight_rows, small_count
    )
    vector = vector[0]
    gain_one = vector[:D]
    gain_two = vector[D : 2 * D]
    seg_all = small_all.astype(jnp.int32)
    seg_all = seg_all.reshape(blk_count, rows_here, block_len)
    seg_key = jnp.broadcast_to(
        seg_all.transpose(1, 0, 2).reshape(rows_here, seq_len)[:, :, None], (rows_here, seq_len, HD)
    )
    seg_query = jnp.broadcast_to(segment_ids[:, None, :], (rows_here, 8, block_len))
    first_blk = jnp.sum((seg_all[:, :, -1] < segment_ids[None, :, 0]).astype(jnp.int32), axis=0)
    attend_ids = jnp.concatenate([blk[None], first_blk])

    mixed_cross = swap_cross(mixed_far)
    mixed_core = swap_core(jnp.stack([mixed_core, mixed_cross[1]]))
    pair_a = team_pair(picked_a[0], after(got_a, mixed_own))
    pair_a_got = swap_blk(pair_a, bits[0])
    mixed_core = after(mixed_core, pair_a_got)
    down_got = swap_blk(after(down_here, mixed_own), bits[0])
    query, packed_kv = pack(ids, mixed_own, mixed_cross, mixed_core)
    key_value = packed_kv.reshape(rows_here, block_len, 2 * KVD)
    kv_all = gather_ring(key_value)

    teams = [
        [g * blk_count + (i | t) for g in range(4) for t in (0, team)]
        for i in range(blk_count)
        if not i & team
    ]
    order = jnp.stack(
        [
            (grp ^ (2 * (i & 1) + (i >> 2))) * 2 + (in_team ^ ((i >> 1) & 1))
            for i in range(8)
        ]
    )

    peers = [[i for i in range(blk_count) if (i & team) == t] for t in (0, team)]

    def lows_of(values, done, lead=0, anchor=None):
        for bit in lows:
            got = swap_blk(values, bit)
            if anchor is not None:
                got = after(got, anchor)
            values = place(values, got, done, bit, lead)
            done = done + [bit]
        return values

    got_b = swap_blk(after(picked_b[1], mixed_own), team)
    dy_over = swap_blk(after(dy_low, packed_kv), team)
    pair_a = place(pair_a, after(pair_a_got, packed_kv), [team], bits[0], 1)
    got_b, down_got, dy_over = after((got_b, down_got, dy_over), kv_all)
    kv_all = after(kv_all, (got_b, down_got, dy_over, pair_a))
    pair_a_got = swap_blk(pair_a, lows[0])
    down_here = place(down_here, down_got, [], bits[0])
    down_here = lows_of(down_here, [bits[0]]).reshape(2 * blk_count // 4, quarter, D)
    dy_first = swap_blk(dy_cross[:half], team)
    dy_second = swap_cross(dy_over[half:])
    dy_chip = jnp.concatenate([dy_low, dy_cross, dy_over, dy_first, dy_second])
    dy_team = jnp.concatenate([dy_chip, swap_core(dy_chip)])
    pair_b = team_pair(picked_b[0], got_b)
    pair_b_got = swap_blk(pair_b, bits[0])
    out_ring = after(out_ring, packed_kv)
    out_strip = jnp.concatenate([out_ring[ring.index(b)] for b in range(blk_count)])
    out_cross = swap_cross(out_strip)
    out_core = swap_core(jnp.stack([out_strip, after(out_cross, kv_all)]))
    out_full = jnp.concatenate(by_place([out_strip, out_core[0], out_cross, out_core[1]]), axis=1)

    att_in, lse = attend(attend_ids, query, kv_all, seg_key, seg_query, block_len)
    flat = wide(flat_low)
    resid = flat + jnp.dot(att_in, out_full, preferred_element_type=jnp.float32)
    h_two = low(norm_apply(resid, gain_two))
    h_two = after(h_two, pair_a_got)
    pair_a_got = after(pair_a_got, h_two)
    pair_a = place(pair_a, pair_a_got, [bits[0], team], lows[0], 1)
    for i in range(1, len(lows)):
        done = [bits[0], team] + lows[:i]
        pair_a = place(pair_a, swap_blk(pair_a, lows[i]), done, lows[i], 1)
    gate_up_a = pair_a.reshape(2, D, -1)
    pair_b_got = after(pair_b_got, h_two)
    down_a = down_here[:, :size_first].reshape(widths[0], D)
    down_b = down_here[:, size_first:].reshape(widths[1], D)
    h_team = lax.all_gather(h_two, ("grp", "blk"), axis=0, tiled=True, axis_index_groups=teams)
    pair_b_got = after(pair_b_got, (h_two, gate_up_a))
    pair_b = place(pair_b, pair_b_got, [team], bits[0], 1)
    h_team = after(h_team, (gate_up_a, pair_b, dy_team))
    hidden_a, d_gate_a, d_up_a, *part_a = middle(order, h_team, dy_team, gate_up_a, down_a)
    gate_up_b = lows_of(pair_b, [bits[0], team], 1, hidden_a).reshape(2, D, -1)
    down_grad_a = down_grad(after(hidden_a, gate_up_b), dy_team)
    down_share_a = lax.psum_scatter(
        down_grad_a, "blk", scatter_dimension=0, axis_index_groups=peers, tiled=True
    )
    column_grad_a = two_grads(h_team, d_gate_a, d_up_a)

    def part_sent(values, axis, bit):
        mine = blk_bit(bit).astype(jnp.int32)
        keep = lax.dynamic_index_in_dim(values, mine, axis, keepdims=False)
        send = lax.dynamic_index_in_dim(values, 1 - mine, axis, keepdims=False)
        return keep, swap_blk(send, bit)

    def part_sum(keep, got):
        return low(wide(keep) + wide(got))

    def columns_first(grad):
        grad = grad.reshape((2, 2, 2) + low_shape + (weight_rows, -1))
        return part_sent(grad, 2 + len(lows), lows[-1])

    def columns_mid(keep, got):
        values = part_sum(keep, got)
        for i in range(len(lows) - 2, -1, -1):
            values = part_sum(*part_sent(values, 3 + i, lows[i]))
        return values

    def columns_third(keep, got):
        values = part_sum(keep, got)
        mine = lax.dynamic_index_in_dim(values, in_team, 1, keepdims=False)
        send = lax.dynamic_index_in_dim(values, 1 - in_team, 1, keepdims=False)
        return values, (mine, swap_blk(send, team))

    def rows_second(keep, got):
        values = part_sum(keep, got)
        for i in range(len(lows) - 2, -1, -1):
            values = part_sum(*part_sent(values, 1 + i, lows[i]))
        return part_sent(values, 0, bits[0])

    def columns_last(mine, got):
        return jnp.stack(
            [jnp.where(mine_team, got, mine), jnp.where(mine_team, mine, got)], axis=1
        )

    first_a = columns_first(column_grad_a)
    hidden_b, d_gate_b, d_up_b, d_here, d_there = middle(
        order, after(h_team, (column_grad_a, down_grad_a)), dy_team, gate_up_b, down_b, part_a
    )

    def chip_sum(values, came):
        return low(wide(values) + wide(came))

    def scatter_far(chip):
        far = chip[3 * token_count :]
        return swap_blk(far[:half], team), swap_cross(far[half:])

    def scatter_near(chip, first, second):
        cross, over = (chip[token_count * i : token_count * (i + 1)] for i in (1, 2))
        cross = jnp.concatenate([low(wide(cross[:half]) + wide(first)), cross[half:]])
        over = jnp.concatenate([over[:half], low(wide(over[half:]) + wide(second))])
        return swap_cross(cross), swap_blk(over, team)

    near_att_cross = swap_cross(after(att_in, hidden_a))
    d_there = after(d_there, (first_a[1], down_share_a, near_att_cross))
    d_came = swap_core(d_there)
    down_grad_b = down_grad(hidden_b, dy_team)
    rows_b = part_sent(
        down_grad_b.reshape((2,) + low_shape + (size_second, D)), len(lows), lows[-1]
    )
    mid_a = columns_mid(*after(first_a, d_came))
    second_a = part_sent(mid_a, 1, bits[0])
    d_chip = chip_sum(d_here, after(d_came, down_grad_b))
    d_far = scatter_far(d_chip)
    column_grad_b = two_grads(h_team, *after((d_gate_b, d_up_b), d_chip))
    first_b = columns_first(column_grad_b)
    d_far = after(d_far, column_grad_b)
    d_cross, d_over = scatter_near(d_chip, *d_far)
    out_part, out_there = down(*after((hidden_a, hidden_b), d_far), down_a, down_b, token_count)
    out_came = swap_core(out_there)
    d_cross, d_over = after((d_cross, d_over), out_part)
    d_htwo = wide(d_chip[:token_count]) + wide(d_cross) + wide(d_over)

    norm_value_two, norm_back_two = jax.vjp(norm_apply, resid, gain_two)
    d_resid_norm, grad_gain_two = norm_back_two(d_htwo)
    d_resid = wide(dy_low) + d_resid_norm
    d_att = low(d_resid)
    rows_b = rows_second(*after(rows_b, d_att))

    d_attended = low(right_transposed(d_att, out_full))
    own_angles = angles_of(positions)
    cosine, sine = jnp.cos(own_angles), jnp.sin(own_angles)
    d_query, dkv = attend_back(
        attend_ids,
        query,
        kv_all,
        seg_key,
        seg_query,
        att_in,
        d_attended,
        lse,
        jnp.concatenate([cosine, cosine], axis=1),
        jnp.concatenate([sine, sine], axis=1),
        block_len,
    )
    dkv = lax.psum_scatter(
        dkv.reshape(blk_count * token_count, 2 * KVD),
        ("grp", "blk"),
        scatter_dimension=0,
        axis_index_groups=ring_groups(blk_count),
        tiled=True,
    )
    down_share_b = part_sum(*after(rows_b, d_query))
    sum_a, third_a = columns_third(*after(second_a, d_att))

    def to_strips(parts):
        return jnp.concatenate(exchange_near(by_place(parts)))

    near_dq = to_strips([d_query[:, strip_q * k : strip_q * (k + 1)] for k in range(4)])
    block_shape = (2,) * len(bits) + (weight_rows, -1)
    query_grad = low(left_product(near_one, near_dq)).reshape(block_shape)
    steps_query = part_sent(query_grad, len(bits) - 1, bits[-1])
    second_b = part_sent(columns_mid(*after(first_b, d_query)), 1, bits[0])
    dkv = after(dkv, down_share_b)
    own_part, core_part, far_part, bias_kv = turn_dkv(
        ids, dkv, jnp.concatenate([cosine, cosine], axis=1), jnp.concatenate([sine, sine], axis=1)
    )
    bias_q = jnp.sum(wide(d_query), axis=0)
    d_key = own_part
    cross_part = swap_cross(far_part)
    near_a = gather_near_stacked(columns_last(*after(third_a, own_part)))
    core_part = swap_core(jnp.stack([core_part, cross_part[1]]))
    kv_grad, hone_here, hone_there = make_kv_grad(
        blk_count,
        weight_rows,
        small_count,
        own_part,
        cross_part,
        core_part,
        near_dq,
        near_one,
        token_send,
        token_cross,
        token_core,
        strip,
        grad_gain_two[None],
        bias_q[None],
        bias_kv,
    )
    vector_rows = -(-small_count // HD)
    kv_grad = kv_grad.reshape((2,) * len(bits) + kv_grad.shape[1:])
    steps_kv = part_sent(kv_grad, len(bits) - 1, bits[-1])
    share_down = after(jnp.concatenate([down_share_a, down_share_b]), dkv)
    grad_down = lax.all_gather(share_down, "grp", axis=0, tiled=True)
    for i in range(len(bits) - 2, -1, -1):
        steps_query = part_sent(part_sum(*after(steps_query, d_key)), i, bits[i])
        kv_sum = part_sum(*steps_kv)
        kv_grad = kv_sum
        steps_kv = part_sent(kv_sum, i, bits[i])
    sum_b, third_b = columns_third(*after(second_b, kv_grad))
    share_kv_all = wide(steps_kv[0]) + wide(after(steps_kv[1], third_b[1]))
    share_kv = low(share_kv_all[:weight_rows])
    vector_part = share_kv_all[weight_rows : weight_rows + vector_rows]
    share_query = part_sum(*after(steps_query, kv_grad))
    near_att = swap_core(jnp.stack([att_in, near_att_cross]))
    near_att = jnp.concatenate([att_in, near_att[0], near_att_cross, near_att[1]])
    near_datt = to_strips([d_att[:, strip_q * k : strip_q * (k + 1)] for k in range(4)])
    out_grad = low(left_product(near_att, after(near_datt, d_attended))).reshape(block_shape)
    steps_out = part_sent(out_grad, len(bits) - 1, bits[-1])
    anchors = [own_part, kv_grad]
    for i in range(len(bits) - 2, -1, -1):
        anchor = anchors[min(len(bits) - 2 - i, 1)]
        steps_out = part_sent(part_sum(*after(steps_out, anchor)), i, bits[i])
    share_out = part_sum(*after(steps_out, kv_grad))

    grad_out = jnp.concatenate(gather_grp(share_out), axis=1)
    query_parts = gather_grp(share_query)
    key_parts = gather_grp(share_kv)
    grad_attend = jnp.concatenate(query_parts + [key_parts[k] for k in (0, 2, 1, 3)], axis=1)

    other = wide(swap_core(hone_there))
    d_hone = wide(hone_here[:token_count]) + other[:token_count]
    d_hone_cross = swap_cross(low(wide(hone_here[token_count:]) + other[token_count:]))
    square_sum = square_total(
        [
            wide(s)
            for s in (share_query, share_kv, share_out, sum_a, sum_b, share_down)
        ]
    )
    packed = jnp.concatenate([vector_part, jnp.full((8, HD), square_sum)])
    packed = packed + swap_cross(packed)
    packed = packed + swap_core(packed)
    share_vector = packed[:vector_rows].reshape(-1)[:small_count]
    square_sum = packed[vector_rows:] + jnp.sum(share_vector * share_vector)
    for bit in bits:
        square_sum = square_sum + swap_blk(square_sum, bit)
    grad_norm = jnp.sqrt(square_sum[0, 0])
    factor = jnp.minimum(1.0, CLIP_NORM / (grad_norm + 1e-06))
    out_chip = chip_sum(out_part, after(out_came, kv_grad))
    out_far = scatter_far(out_chip)
    factor = after(factor, (out_chip, near_a))

    new_first_attend, new_second_attend, new_attend = adam_step(
        w_attend, factor * wide(grad_attend), first_attend, second_attend, RATE_ATTEND, WEIGHT_DECAY
    )
    new_first_out, new_second_out, new_out = adam_step(
        w_out, factor * wide(grad_out), first_out, second_out, RATE_OUT, WEIGHT_DECAY
    )
    new_first_down, new_second_down, new_down = adam_step(
        w_down, factor * wide(grad_down), first_down, second_down, RATE_DOWN, WEIGHT_DECAY
    )
    own_b = columns_last(*third_b)
    cross_b = after(swap_cross(own_b), new_down)
    near_b = jnp.stack([own_b, cross_b])
    near_b = [near_b, swap_core(near_b)]
    new_first_gate, new_second_gate, new_gate = adam_columns(
        0, ids, factor[None], near_a, near_b, w_gate, first_gate, second_gate, blk_count, RATE_GATE, WEIGHT_DECAY
    )
    new_first_up, new_second_up, new_up = adam_columns(
        1, ids, factor[None], near_a, near_b, w_up, first_up, second_up, blk_count, RATE_GATE, WEIGHT_DECAY
    )
    norm_value_one, norm_back_one = jax.vjp(norm_apply, flat, gain_one)
    d_hone = after(d_hone + wide(after(d_hone_cross, new_gate)), new_gate)
    d_flat_norm, unused_gain = norm_back_one(d_hone)
    grad_tokens = low(d_resid + d_flat_norm)

    new_first_small, new_second_small, new_small = adam_step(
        small_params, factor * share_vector, first_small, second_small, RATE_VECTOR, 0.0
    )

    out_near = after(scatter_near(out_chip, *after(out_far, factor)), (new_gate, new_up))
    out_tokens = low(resid + wide(out_chip[:token_count]) + wide(out_near[0]) + wide(out_near[1]))
    return (
        out_tokens.reshape(rows_here, block_len, D),
        grad_tokens.reshape(rows_here, block_len, D),
        grad_norm,
        new_first_attend,
        new_second_attend,
        new_attend,
        new_first_out,
        new_second_out,
        new_out,
        new_first_gate,
        new_second_gate,
        new_gate,
        new_first_up,
        new_second_up,
        new_up,
        new_first_down,
        new_second_down,
        new_down,
        new_first_small,
        new_second_small,
        new_small,
    )


def solution(mesh):
    placed = (
        P("grp", "blk", None),
        P("grp", "blk", None),
        P("grp", "blk"),
        P("grp", "blk"),
        P("blk", None),
        P("blk", None),
        P("blk", None),
        P("blk", None),
        P("blk", None),
        P("blk"),
        P("blk", None),
        P("blk", None),
        P("blk", None),
        P("blk", None),
        P("blk", None),
        P("blk"),
        P("blk", None),
        P("blk", None),
        P("blk", None),
        P("blk", None),
        P("blk", None),
        P("blk"),
    )
    return jax.shard_map(
        on_device,
        mesh=mesh,
        in_specs=placed,
        out_specs=(
            P("grp", "blk", None),
            P("grp", "blk", None),
            P(),
            P("blk", None),
            P("blk", None),
            P("blk", None),
            P("blk", None),
            P("blk", None),
            P("blk", None),
            P("blk", None),
            P("blk", None),
            P("blk", None),
            P("blk", None),
            P("blk", None),
            P("blk", None),
            P("blk", None),
            P("blk", None),
            P("blk", None),
            P("blk"),
            P("blk"),
            P("blk"),
        ),
        check_vma=False,
    )
```

```python
import functools

import jax
import jax.numpy as jnp
from jax import lax
from jax.experimental import pallas as pl
from jax.experimental.pallas import tpu as pltpu
from jax.sharding import PartitionSpec as P

D = 1536
FF = 8960
H = 12
KVH = 2
HD = 128
STEP = 10
HQD = 1536
KVD = 256


NORM_EPS = 1e-06
ROPE_BASE = 10000.0
CLIP_NORM = 1.0
BETA_FIRST = 0.9
BETA_SECOND = 0.95
ADAM_EPS = 1e-08
WEIGHT_DECAY = 0.1
RATE_ATTEND = 0.06
RATE_OUT = 0.5
RATE_GATE = 0.06
RATE_DOWN = 0.03
RATE_VECTOR = 0.5
NEG_LARGE = -1e30
LOG2E = 1.4426950408889634
VMEM = 48 * 1024 * 1024
SMALL_COST = pl.CostEstimate(flops=1000, bytes_accessed=1000, transcendentals=0)


def norm_apply(values, gain):
    return values * lax.rsqrt(jnp.mean(values * values, axis=-1, keepdims=True) + NORM_EPS) * gain


def swish_product(gate, up_proj):
    return jax.nn.silu(gate) * up_proj


def left_product(left_side, right_side):
    return lax.dot_general(
        left_side, right_side, (((0,), (0,)), ((), ())), preferred_element_type=jnp.float32
    )


def right_transposed(left_side, right_side):
    return lax.dot_general(
        left_side, right_side, (((1,), (1,)), ((), ())), preferred_element_type=jnp.float32
    )


def square_total(arrays):
    return sum((jnp.sum(member * member) for member in arrays))


def adam_step(weight, grad, first, second, rate, decay):
    first_new = BETA_FIRST * first + (1.0 - BETA_FIRST) * grad
    second_new = BETA_SECOND * second + (1.0 - BETA_SECOND) * grad * grad
    first_hat = first_new / (1.0 - BETA_FIRST**STEP)
    second_hat = second_new / (1.0 - BETA_SECOND**STEP)
    weight_new = weight - rate * (first_hat / (jnp.sqrt(second_hat) + ADAM_EPS) + decay * weight)
    return (first_new, second_new, weight_new)


def ring_order(count):
    return list(range(0, count, 2)) + list(range(count - 1, 0, -2))


def halves_of(quarter):
    first = quarter * 16 // 35
    return ((0, first), (first, quarter - first))


def pick_body(blk_count, ids, gate_ref, up_ref, *out_refs):
    quarter = FF // blk_count // 4
    per = blk_count // 4
    for k in range(4):

        @pl.when(ids[0] == k)
        def _(k=k):
            for (at, size), out_ref in zip(halves_of(quarter), out_refs):
                for which, src in enumerate((gate_ref, up_ref)):
                    for bit in range(2):
                        parts = []
                        for high in range(2):
                            for small in range(per):
                                begin = (((high * 2 + bit) * per + small) * 4 + k) * quarter + at
                                parts.append(src[:, begin : begin + size])
                        out_ref[ids[1] ^ bit, which] = jnp.concatenate(parts, axis=1).astype(
                            jnp.bfloat16
                        )


def pick_columns(ids, gate, up, blk_count):
    rows = gate.shape[0]
    step = 48 if rows % 48 == 0 else rows
    widths = [size * blk_count // 2 for at, size in halves_of(FF // blk_count // 4)]
    spec = pl.BlockSpec((step, FF), lambda i, ids: (i, 0))
    return pl.pallas_call(
        functools.partial(pick_body, blk_count),
        grid_spec=pltpu.PrefetchScalarGridSpec(
            num_scalar_prefetch=1,
            grid=(rows // step,),
            in_specs=[spec, spec],
            out_specs=[pl.BlockSpec((2, 2, step, w), lambda i, ids: (0, 0, i, 0)) for w in widths],
        ),
        out_shape=[jax.ShapeDtypeStruct((2, 2, rows, w), jnp.bfloat16) for w in widths],
        compiler_params=pltpu.CompilerParams(vmem_limit_bytes=VMEM),
        cost_estimate=SMALL_COST,
        name="pick_columns",
    )(ids, gate, up)


def adam_body(blk_count, rate, decay, ids, factor_ref, first_ref, first_far_ref, second_ref, second_far_ref, w_ref, m_ref, v_ref, m_out, v_out, w_out):
    per = blk_count // 4
    sizes = [size for at, size in halves_of(FF // blk_count // 4)]
    grads = []
    for near_ref, far_ref in ((first_ref, first_far_ref), (second_ref, second_far_ref)):
        by_grp = []
        for k in range(4):
            away = ids[0] ^ k
            bits_of_k = []
            for bit in range(2):
                near = near_ref[away >> 1, bit].astype(jnp.float32)
                far = far_ref[away >> 1, bit].astype(jnp.float32)
                bits_of_k.append(jnp.where((away & 1) == 1, far, near))
            by_grp.append(bits_of_k)
        grads.append(by_grp)
    parts = []
    for high in range(2):
        for bit in range(2):
            for small in range(per):
                place = high * per + small
                for k in range(4):
                    for part, size in zip(grads, sizes):
                        parts.append(part[k][bit][:, place * size : (place + 1) * size])
    grad = jnp.concatenate(parts, axis=1) * factor_ref[0]
    m, v, w = adam_step(w_ref[...], grad, m_ref[...], v_ref[...], rate, decay)
    m_out[...] = m
    v_out[...] = v
    w_out[...] = w


def adam_columns(which, ids, factor, first, second, w, m, v, blk_count, rate, decay):
    rows = w.shape[0]
    step = 32 if rows % 32 == 0 else rows
    spec = pl.BlockSpec((step, FF), lambda i, ids: (i, 0))
    shape = jax.ShapeDtypeStruct((rows, FF), jnp.float32)
    grads = [
        pl.BlockSpec((2, None, 2, step, g.shape[-1]), lambda i, ids: (0, which, 0, i, 0))
        for g in first + second
    ]
    return pl.pallas_call(
        functools.partial(adam_body, blk_count, rate, decay),
        grid_spec=pltpu.PrefetchScalarGridSpec(
            num_scalar_prefetch=1,
            grid=(rows // step,),
            in_specs=[pl.BlockSpec(memory_space=pltpu.SMEM)] + grads + [spec, spec, spec],
            out_specs=[spec, spec, spec],
        ),
        out_shape=[shape] * 3,
        compiler_params=pltpu.CompilerParams(vmem_limit_bytes=VMEM),
        cost_estimate=SMALL_COST,
        name="adam_columns",
    )(ids, factor, *first, *second, w, m, v)


def nt(a, b, **kw):
    return lax.dot_general(a, b, (((1,), (1,)), ((), ())), preferred_element_type=jnp.float32, **kw)

def tn(a, b, **kw):
    return lax.dot_general(a, b, (((0,), (0,)), ((), ())), preferred_element_type=jnp.float32, **kw)

def stack_heads(ref, kvh, group):
    return jnp.concatenate([ref[:, HD * (kvh * group + i): HD * (kvh * group + i + 1)] for i in range(group)], axis=0)

def hidden_from(seg_key_ref, seg_query_ref, first, chunk, block_len, blk):
    key = first + lax.broadcasted_iota(jnp.int32, (chunk, block_len), 0)
    query = blk * block_len + lax.broadcasted_iota(jnp.int32, (chunk, block_len), 1)
    seg_key = seg_key_ref[pl.ds(first, chunk), :]
    counts = jnp.logical_and(key <= query, seg_key == seg_query_ref[0:1, :])
    return jnp.where(counts, 0.0, NEG_LARGE)

def ring_pair(ref, c, at):
    return jnp.concatenate(
        [ref[c, :, at : at + HD], ref[ref.shape[0] - 1 - c, :, at : at + HD]], axis=0
    )


def attend_body(chunk, ids, q_ref, k_ref, v_ref, seg_key_ref, seg_query_ref, o_ref, lse_ref, m_s, l_s, acc_s):
    block_len = q_ref.shape[0]
    group = H // KVH
    row = pl.program_id(0)
    per = chunk // block_len
    scale = HD ** (-0.5) * LOG2E
    start = ids[1 + row] // per
    stop = ids[0] // per + 1
    for kvh in range(KVH):
        q = stack_heads(q_ref, kvh, group)
        m_s[...] = jnp.full_like(m_s, NEG_LARGE)
        l_s[...] = jnp.zeros_like(l_s)
        acc_s[...] = jnp.zeros_like(acc_s)

        def step(c, carry):
            keys = ring_pair(k_ref, c, HD * kvh)
            vals = ring_pair(v_ref, c, HD * kvh)
            bias = hidden_from(seg_key_ref, seg_query_ref, c * chunk, chunk, block_len, ids[0])
            s = nt(keys, q) * scale + jnp.concatenate([bias] * group, axis=1)
            old = m_s[0:1, :]
            new = jnp.maximum(old, jnp.max(s, axis=0, keepdims=True))
            p = jnp.exp2(s - new)
            fade = jnp.exp2(old - new)
            l_s[0:1, :] = l_s[0:1, :] * fade + jnp.sum(p, axis=0, keepdims=True)
            acc_s[...] = acc_s[...] * fade + tn(vals, p.astype(jnp.bfloat16))
            m_s[0:1, :] = new
            return carry

        lax.fori_loop(start, stop, step, 0)
        total = l_s[0:1, :]
        out = (acc_s[...] * (1.0 / total)).T
        for i in range(group):
            o_ref[:, HD * (kvh * group + i): HD * (kvh * group + i + 1)] = out[block_len * i: block_len * (i + 1), :].astype(jnp.bfloat16)
        lse_ref[kvh] = jnp.broadcast_to(m_s[0:1, :] + jnp.log2(total), (8, group * block_len))

def attend(ids, q, kv, seg_key, seg_query, block_len):
    blk_count, rows = kv.shape[:2]
    group = H // KVH
    chunk = 2 * block_len
    many = group * block_len
    return pl.pallas_call(
        functools.partial(attend_body, chunk),
        grid_spec=pltpu.PrefetchScalarGridSpec(
            num_scalar_prefetch=1, grid=(rows,),
            in_specs=[
                pl.BlockSpec((block_len, HQD), lambda r, ids: (r, 0)),
                pl.BlockSpec((blk_count, None, block_len, KVD), lambda r, ids: (0, r, 0, 0)),
                pl.BlockSpec((blk_count, None, block_len, KVD), lambda r, ids: (0, r, 0, 1)),
                pl.BlockSpec((None, blk_count * block_len, HD), lambda r, ids: (r, 0, 0)),
                pl.BlockSpec((None, 8, block_len), lambda r, ids: (r, 0, 0)),
            ],
            out_specs=[
                pl.BlockSpec((block_len, HQD), lambda r, ids: (r, 0)),
                pl.BlockSpec((None, KVH, 8, many), lambda r, ids: (r, 0, 0, 0)),
            ],
            scratch_shapes=[pltpu.VMEM((8, many), jnp.float32), pltpu.VMEM((8, many), jnp.float32), pltpu.VMEM((HD, many), jnp.float32)]),
        out_shape=[
            jax.ShapeDtypeStruct((rows * block_len, HQD), jnp.bfloat16),
            jax.ShapeDtypeStruct((rows, KVH, 8, many), jnp.float32),
        ],
        compiler_params=pltpu.CompilerParams(vmem_limit_bytes=VMEM),
        cost_estimate=SMALL_COST,
        name="attend",
    )(ids, q, kv, kv, seg_key, seg_query)

def turn_back(u, cosine, sine):
    lane = lax.broadcasted_iota(jnp.int32, u.shape, 1)
    other = pltpu.roll(u, HD // 2, 1)
    return u * cosine + jnp.where(lane < HD // 2, other, -other) * sine

def attend_back_body(chunk, ids, q_ref, k_ref, v_ref, seg_key_ref, seg_query_ref, o_ref, do_ref, lse_ref, cos_ref, sin_ref, dq_ref, dkv_ref, dq_s):
    block_len = q_ref.shape[0]
    group = H // KVH
    row = pl.program_id(0)
    per = chunk // block_len
    plain = HD ** (-0.5)
    scale = plain * LOG2E
    start = ids[1 + row] // per
    stop = ids[0] // per + 1
    dkv_ref[...] = jnp.zeros_like(dkv_ref)
    for kvh in range(KVH):
        q = stack_heads(q_ref, kvh, group)
        do = stack_heads(do_ref, kvh, group)
        o = stack_heads(o_ref, kvh, group)
        both = do.astype(jnp.float32) * o.astype(jnp.float32)
        delta = nt(jnp.ones((8, HD), jnp.float32), both, precision=lax.Precision.HIGHEST)[0:1, :]
        lse = lse_ref[kvh][0:1, :]
        dq_s[...] = jnp.zeros_like(dq_s)

        def step(c, carry):
            keys = ring_pair(k_ref, c, HD * kvh)
            vals = ring_pair(v_ref, c, HD * kvh)
            bias = hidden_from(seg_key_ref, seg_query_ref, c * chunk, chunk, block_len, ids[0])
            s = nt(keys, q) * scale + jnp.concatenate([bias] * group, axis=1)
            p = jnp.exp2(s - lse)
            dp = nt(vals, do)
            ds = (p * (dp - delta)).astype(jnp.bfloat16)
            dk = jnp.dot(ds, q, preferred_element_type=jnp.float32) * plain
            dv = jnp.dot(p.astype(jnp.bfloat16), do, preferred_element_type=jnp.float32)
            for at, part in ((HD * kvh, dk.astype(jnp.bfloat16)), (KVD + HD * kvh, dv.astype(jnp.bfloat16))):
                dkv_ref[c, :, at : at + HD] = part[:block_len]
                dkv_ref[dkv_ref.shape[0] - 1 - c, :, at : at + HD] = part[block_len:]
            dq_s[...] += tn(ds, keys)
            return carry

        lax.fori_loop(start, stop, step, 0)
        cosine, sine = cos_ref[...], sin_ref[...]
        for i in range(group):
            u = dq_s[block_len * i: block_len * (i + 1), :] * plain
            at = HD * (kvh * group + i)
            dq_ref[:, at: at + HD] = turn_back(u, cosine, sine).astype(jnp.bfloat16)

def attend_back(ids, q, kv, seg_key, seg_query, o, do, lse, cosine, sine, block_len):
    blk_count, rows = kv.shape[:2]
    group = H // KVH
    chunk = 2 * block_len
    many = group * block_len
    per_row = pl.BlockSpec((block_len, HQD), lambda r, ids: (r, 0))
    turn = pl.BlockSpec((block_len, HD), lambda r, ids: (r, 0))
    return pl.pallas_call(
        functools.partial(attend_back_body, chunk),
        grid_spec=pltpu.PrefetchScalarGridSpec(
            num_scalar_prefetch=1, grid=(rows,),
            in_specs=[
                per_row,
                pl.BlockSpec((blk_count, None, block_len, KVD), lambda r, ids: (0, r, 0, 0)),
                pl.BlockSpec((blk_count, None, block_len, KVD), lambda r, ids: (0, r, 0, 1)),
                pl.BlockSpec((None, blk_count * block_len, HD), lambda r, ids: (r, 0, 0)),
                pl.BlockSpec((None, 8, block_len), lambda r, ids: (r, 0, 0)),
                per_row, per_row,
                pl.BlockSpec((None, KVH, 8, many), lambda r, ids: (r, 0, 0, 0)),
                turn, turn,
            ],
            out_specs=[per_row, pl.BlockSpec((blk_count, None, block_len, 2 * KVD), lambda r, ids: (0, r, 0, 0))],
            scratch_shapes=[pltpu.VMEM((many, HD), jnp.float32)]),
        out_shape=[
            jax.ShapeDtypeStruct((rows * block_len, HQD), jnp.bfloat16),
            jax.ShapeDtypeStruct((blk_count, rows, block_len, 2 * KVD), jnp.bfloat16),
        ],
        compiler_params=pltpu.CompilerParams(vmem_limit_bytes=VMEM),
        cost_estimate=SMALL_COST,
        name="attend_back",
    )(ids, q, kv, kv, seg_key, seg_query, o, do, lse, cosine, sine)

def nn(a, b):
    return jnp.dot(a, b, preferred_element_type=jnp.float32)


def middle_body(add, order, h_ref, dy_ref, wg_ref, wu_ref, wd_ref, *refs):
    prev_refs = refs[:2] if add else None
    hid_ref, dg_ref, du_ref, dh_ref, dh_far_ref = refs[-5:]
    here = pl.program_id(0) < 4
    h = h_ref[...]
    gate = nn(h, wg_ref[...])
    up = nn(h, wu_ref[...])
    sig = 1.0 / (1.0 + jnp.exp(-gate))
    silu = gate * sig
    hid_ref[...] = (silu * up).astype(jnp.bfloat16)
    dhid = nt(dy_ref[...], wd_ref[...])
    dg = (dhid * up * sig * (1.0 + gate * (1.0 - sig))).astype(jnp.bfloat16)
    du = (dhid * silu).astype(jnp.bfloat16)
    dg_ref[...] = dg
    du_ref[...] = du
    dh = nt(dg, wg_ref[...]) + nt(du, wu_ref[...])
    if add:
        prev = jnp.where(here, prev_refs[0][...].astype(jnp.float32), prev_refs[1][...].astype(jnp.float32))
        dh = dh + prev
    dh = dh.astype(jnp.bfloat16)

    @pl.when(here)
    def _():
        dh_ref[...] = dh

    @pl.when(jnp.logical_not(here))
    def _():
        dh_far_ref[...] = dh


def middle(order, h, dy, gate_up, wd, prev=None):
    count = h.shape[0]
    step = count // order.shape[0]
    wide_here = wd.shape[0]
    row = pl.BlockSpec((step, D), lambda i, order: (i, 0))
    placed = pl.BlockSpec((step, D), lambda i, order: (order[i], 0))
    part = pl.BlockSpec((step, wide_here), lambda i, order: (i, 0))
    part_placed = pl.BlockSpec((step, wide_here), lambda i, order: (order[i], 0))
    once = pl.Buffered(1)
    extra = [] if prev is None else list(prev)
    near = pl.BlockSpec((step, D), lambda i, order: (jnp.minimum(i, 3), 0))
    far = pl.BlockSpec((step, D), lambda i, order: (jnp.maximum(i - 4, 0), 0))
    return pl.pallas_call(
        functools.partial(middle_body, prev is not None),
        grid_spec=pltpu.PrefetchScalarGridSpec(
            num_scalar_prefetch=1,
            grid=(count // step,),
            in_specs=[
                placed,
                row,
                pl.BlockSpec((None, D, wide_here), lambda i, order: (0, 0, 0), pipeline_mode=once),
                pl.BlockSpec((None, D, wide_here), lambda i, order: (1, 0, 0), pipeline_mode=once),
                pl.BlockSpec((wide_here, D), lambda i, order: (0, 0), pipeline_mode=once),
            ]
            + [near, far][: len(extra)],
            out_specs=[part, part_placed, part_placed, near, far],
        ),
        out_shape=[jax.ShapeDtypeStruct((count, wide_here), jnp.bfloat16)] * 3
        + [jax.ShapeDtypeStruct((count // 2, D), jnp.bfloat16)] * 2,
        compiler_params=pltpu.CompilerParams(vmem_limit_bytes=VMEM),
        cost_estimate=SMALL_COST,
        name="middle",
    )(order, h, dy, gate_up, gate_up, wd, *extra)


def two_grads_body(h_ref, a_ref, b_ref, out_ref):
    h = h_ref[...]
    out_ref[0] = tn(h, a_ref[...]).astype(jnp.bfloat16)
    out_ref[1] = tn(h, b_ref[...]).astype(jnp.bfloat16)


def two_grads(h, a, b, step=256):
    count = h.shape[0]
    wide_here = a.shape[1]
    whole = pl.BlockSpec(a.shape, lambda i: (0, 0), pipeline_mode=pl.Buffered(1))
    return pl.pallas_call(
        two_grads_body,
        grid=(D // step,),
        in_specs=[pl.BlockSpec((count, step), lambda i: (0, i)), whole, whole],
        out_specs=pl.BlockSpec((2, step, wide_here), lambda i: (0, i, 0)),
        out_shape=jax.ShapeDtypeStruct((2, D, wide_here), jnp.bfloat16),
        compiler_params=pltpu.CompilerParams(vmem_limit_bytes=VMEM),
        cost_estimate=SMALL_COST,
        name="two_grads",
    )(h, a, b)


def down_grad_body(hid_ref, dy_ref, g_ref):
    g_ref[...] = tn(hid_ref[...], dy_ref[...]).astype(jnp.bfloat16)

def down_grad(hid, dy, step=512):
    T, F = hid.shape
    D = dy.shape[1]
    return pl.pallas_call(down_grad_body, grid=(D // step,),
        in_specs=[pl.BlockSpec((T, F), lambda i: (0, 0), pipeline_mode=pl.Buffered(1)), pl.BlockSpec((T, step), lambda i: (0, i))],
        out_specs=pl.BlockSpec((F, step), lambda i: (0, i)),
        out_shape=jax.ShapeDtypeStruct((F, D), jnp.bfloat16),
        compiler_params=pltpu.CompilerParams(vmem_limit_bytes=VMEM),
        cost_estimate=SMALL_COST,
        name="down_grad")(hid, dy)

def down_body(hid_a_ref, hid_b_ref, wd_a_ref, wd_b_ref, o_ref, o_far_ref):
    out = nn(hid_a_ref[...], wd_a_ref[...]) + nn(hid_b_ref[...], wd_b_ref[...])
    out = out.astype(jnp.bfloat16)
    here = pl.program_id(0) < 4

    @pl.when(here)
    def _():
        o_ref[...] = out

    @pl.when(jnp.logical_not(here))
    def _():
        o_far_ref[...] = out


def down(hid_a, hid_b, wd_a, wd_b, step):
    count = hid_a.shape[0]

    def rows(array):
        return pl.BlockSpec((step, array.shape[1]), lambda i: (i, 0))

    def whole(array):
        return pl.BlockSpec(array.shape, lambda i: (0, 0), pipeline_mode=pl.Buffered(1))

    return pl.pallas_call(
        down_body,
        grid=(count // step,),
        in_specs=[rows(hid_a), rows(hid_b), whole(wd_a), whole(wd_b)],
        out_specs=[
            pl.BlockSpec((step, D), lambda i: (jnp.minimum(i, 3), 0)),
            pl.BlockSpec((step, D), lambda i: (jnp.maximum(i - 4, 0), 0)),
        ],
        out_shape=[jax.ShapeDtypeStruct((count // 2, D), jnp.bfloat16)] * 2,
        compiler_params=pltpu.CompilerParams(vmem_limit_bytes=VMEM),
        cost_estimate=SMALL_COST,
        name="down",
    )(hid_a, hid_b, wd_a, wd_b)


def turn(u, cosine, sine):
    lane = lax.broadcasted_iota(jnp.int32, u.shape, 1)
    other = pltpu.roll(u, HD // 2, 1)
    return u * cosine + jnp.where(lane < HD // 2, -other, other) * sine


def mix_body(
    blk_count, rows, small_count, ids, own_ref, cross_ref, core_ref, ring_ref, freq_ref,
    self_ref, near_ref, far_ref, one_ref, strip_ref, vector_ref,
):
    ring = ring_order(blk_count)
    wide_here = ring_ref.shape[-1]
    pieces = []
    for b in range(blk_count):
        at = ring.index(b)
        strip_ref[rows * b : rows * (b + 1)] = ring_ref[at, :rows]
        left = small_count
        line = rows
        while left > 0:
            size = min(left, wide_here)
            pieces.append(ring_ref[at, line : line + 1, :size].astype(jnp.float32))
            left -= size
            line += 1
    vector = jnp.concatenate(pieces, axis=1)
    vector_ref[...] = vector
    gain = vector[:, :D]
    grp = ids[0]
    strip_q = wide_here - HD
    bias = jnp.zeros((1, wide_here), jnp.float32)
    for k in range(4):
        kv_at = 2 * D + HQD + HD * (k // 2) + KVD * (k % 2)
        part = jnp.concatenate(
            [
                vector[:, 2 * D + strip_q * k : 2 * D + strip_q * (k + 1)],
                vector[:, kv_at : kv_at + HD],
            ],
            axis=1,
        )
        bias = bias + jnp.where(grp == k, part, 0.0)
    count = own_ref.shape[0]
    strip = strip_ref[...]
    for d in range(4):
        source = (own_ref[...], core_ref[0], cross_ref[...], core_ref[1])[d]
        x = source[:, :D].astype(jnp.float32)
        root = lax.rsqrt(jnp.mean(x * x, axis=1, keepdims=True) + NORM_EPS)
        one = (x * root * gain).astype(jnp.bfloat16)
        one_ref[count * d : count * (d + 1)] = one
        mixed = nn(one, strip) + bias
        digits = source[:, D : D + HD].astype(jnp.float32)
        position = 64.0 * digits[:, 0:1] + digits[:, 1:2]
        angles = position * freq_ref[...]
        cosine, sine = jnp.cos(angles), jnp.sin(angles)
        for i in range(wide_here // HD):
            c, s = cosine, sine
            if i == wide_here // HD - 1:
                c = jnp.where(grp % 2 == 1, 1.0, c)
                s = jnp.where(grp % 2 == 1, 0.0, s)
            at = HD * i
            out = turn(mixed[:, at : at + HD], c, s).astype(jnp.bfloat16)
            if d == 0:
                self_ref[:, at : at + HD] = out
            elif d == 1:
                near_ref[:, at : at + HD] = out
            else:
                far_ref[d - 2, :, at : at + HD] = out


def mix(ids, own, cross, core, ring, freq, blk_count, rows, small_count):
    count = own.shape[0]
    wide_here = ring.shape[-1]
    low16 = jnp.bfloat16
    return pl.pallas_call(
        functools.partial(mix_body, blk_count, rows, small_count),
        in_specs=[pl.BlockSpec(memory_space=pltpu.SMEM)] + [pl.BlockSpec(memory_space=pltpu.VMEM)] * 5,
        out_specs=[pl.BlockSpec(memory_space=pltpu.VMEM)] * 6,
        out_shape=[
            jax.ShapeDtypeStruct((count, wide_here), low16),
            jax.ShapeDtypeStruct((count, wide_here), low16),
            jax.ShapeDtypeStruct((2, count, wide_here), low16),
            jax.ShapeDtypeStruct((4 * count, D), low16),
            jax.ShapeDtypeStruct((D, wide_here), low16),
            jax.ShapeDtypeStruct((1, blk_count * small_count), jnp.float32),
        ],
        compiler_params=pltpu.CompilerParams(vmem_limit_bytes=VMEM),
        cost_estimate=SMALL_COST,
        name="mix",
    )(ids, own, cross, core, ring, freq)


def pack_body(ids, self_ref, cross_ref, core_ref, q_ref, kv_ref):
    strip_q = self_ref.shape[1] - HD
    for g in range(4):

        @pl.when(ids[0] == g)
        def _(g=g):
            for k in range(4):
                part = (self_ref[...], core_ref[0], cross_ref[0], core_ref[1])[g ^ k]
                q_ref[:, strip_q * k : strip_q * (k + 1)] = part[:, :strip_q]
                at = (k % 2) * KVD + (k // 2) * HD
                kv_ref[:, at : at + HD] = part[:, strip_q:]


def pack(ids, own, cross, core):
    count = own.shape[0]
    return pl.pallas_call(
        pack_body,
        in_specs=[pl.BlockSpec(memory_space=pltpu.SMEM)] + [pl.BlockSpec(memory_space=pltpu.VMEM)] * 3,
        out_specs=[pl.BlockSpec(memory_space=pltpu.VMEM)] * 2,
        out_shape=[
            jax.ShapeDtypeStruct((count, HQD), jnp.bfloat16),
            jax.ShapeDtypeStruct((count, 2 * KVD), jnp.bfloat16),
        ],
        compiler_params=pltpu.CompilerParams(vmem_limit_bytes=VMEM),
        cost_estimate=SMALL_COST,
        name="pack",
    )(ids, own, cross, core)


def turn_dkv_body(ids, dkv_ref, cos_ref, sin_ref, self_ref, near_ref, far_ref, sum_ref):
    items = []
    sums = [None] * 4
    for k in range(4):
        at = (k % 2) * KVD + (k // 2) * HD
        part = dkv_ref[:, at : at + HD]
        if k % 2 == 0:
            part = turn_back(part.astype(jnp.float32), cos_ref[...], sin_ref[...]).astype(jnp.bfloat16)
        items.append(part)
        sums[(k % 2) * 2 + k // 2] = jnp.sum(part.astype(jnp.float32), axis=0, keepdims=True)
    sum_ref[...] = jnp.concatenate(sums, axis=1)
    for g in range(4):

        @pl.when(ids[0] == g)
        def _(g=g):
            self_ref[...] = items[g]
            near_ref[...] = items[g ^ 1]
            far_ref[0] = items[g ^ 2]
            far_ref[1] = items[g ^ 3]


def turn_dkv(ids, dkv, cosine, sine):
    count = dkv.shape[0]
    return pl.pallas_call(
        turn_dkv_body,
        in_specs=[pl.BlockSpec(memory_space=pltpu.SMEM)] + [pl.BlockSpec(memory_space=pltpu.VMEM)] * 3,
        out_specs=[pl.BlockSpec(memory_space=pltpu.VMEM)] * 4,
        out_shape=[
            jax.ShapeDtypeStruct((count, HD), jnp.bfloat16),
            jax.ShapeDtypeStruct((count, HD), jnp.bfloat16),
            jax.ShapeDtypeStruct((2, count, HD), jnp.bfloat16),
            jax.ShapeDtypeStruct((1, 2 * KVD), jnp.float32),
        ],
        compiler_params=pltpu.CompilerParams(vmem_limit_bytes=VMEM),
        cost_estimate=SMALL_COST,
        name="turn_dkv",
    )(ids, dkv, cosine, sine)


def kv_grad_body(
    blk_count, rows, small_count, self_ref, cross_ref, core_ref, dq_ref, one_ref, own_ref, near_x_ref,
    core_x_ref, strip_ref, gain_two_ref, bias_q_ref, bias_kv_ref, grad_ref, here_ref, there_ref,
):
    count = self_ref.shape[0]
    strip_q = strip_ref.shape[1] - HD
    parts = (self_ref[...], core_ref[0], cross_ref[0], core_ref[1])
    near = jnp.concatenate(parts, axis=0)
    grad = tn(one_ref[...], near)
    gain_one = jnp.zeros((1, D), jnp.float32)
    for d in range(4):
        x = (own_ref[...], core_x_ref[0], near_x_ref[...], core_x_ref[1])[d][:, :D].astype(jnp.float32)
        root = lax.rsqrt(jnp.mean(x * x, axis=1, keepdims=True) + NORM_EPS)
        hone = nt(dq_ref[count * d : count * (d + 1)], strip_ref[:, :strip_q])
        hone = hone + nt(parts[d], strip_ref[:, strip_q:])
        gain_one = gain_one + jnp.sum(hone * x * root, axis=0, keepdims=True)
        out_ref = (here_ref, there_ref)[d % 2]
        out_ref[count * (d // 2) : count * (d // 2 + 1)] = hone.astype(jnp.bfloat16)
    vector = jnp.concatenate([gain_one, gain_two_ref[...], bias_q_ref[...], bias_kv_ref[...]], axis=1)
    extra = grad_ref.shape[1] - rows
    for b in range(blk_count):
        grad_ref[b, :rows] = grad[rows * b : rows * (b + 1)].astype(jnp.bfloat16)
        lines = []
        for line in range(extra):
            size = min(HD, max(small_count - line * HD, 0))
            begin = small_count * b + line * HD
            pieces = [vector[:, begin : begin + size]] if size > 0 else []
            if size < HD:
                pieces.append(jnp.zeros((1, HD - size), jnp.float32))
            lines.append(pieces[0] if len(pieces) == 1 else jnp.concatenate(pieces, axis=1))
        grad_ref[b, rows:] = jnp.concatenate(lines, axis=0).astype(jnp.bfloat16)


def kv_grad_rows(rows, small_count):
    needed = rows + -(-small_count // HD)
    return needed + -needed % 16


def make_kv_grad(blk_count, rows, small_count, own, cross, core, dq, one, x_own, x_cross, x_core, strip, gain_two, bias_q, bias_kv):
    count = own.shape[0]
    height = kv_grad_rows(rows, small_count)
    return pl.pallas_call(
        functools.partial(kv_grad_body, blk_count, rows, small_count),
        in_specs=[pl.BlockSpec(memory_space=pltpu.VMEM)] * 12,
        out_specs=[pl.BlockSpec(memory_space=pltpu.VMEM)] * 3,
        out_shape=[
            jax.ShapeDtypeStruct((blk_count, height, HD), jnp.bfloat16),
            jax.ShapeDtypeStruct((2 * count, D), jnp.bfloat16),
            jax.ShapeDtypeStruct((2 * count, D), jnp.bfloat16),
        ],
        compiler_params=pltpu.CompilerParams(vmem_limit_bytes=VMEM),
        cost_estimate=SMALL_COST,
        name="kv_grad",
    )(own, cross, core, dq, one, x_own, x_cross, x_core, strip, gain_two, bias_q, bias_kv)


CORE = [(0, 1), (1, 0), (2, 3), (3, 2)]
CROSS = [(0, 2), (2, 0), (1, 3), (3, 1)]
DIAG = [(0, 3), (3, 0), (1, 2), (2, 1)]


def low(values):
    return values.astype(jnp.bfloat16)


def wide(values):
    return values.astype(jnp.float32)


def swap_core(values):
    return lax.ppermute(values, "grp", CORE)


def swap_cross(values):
    return lax.ppermute(values, "grp", CROSS)


def swap_diag(values):
    return lax.ppermute(values, "grp", DIAG)


def swap_blk(values, bit):
    count = lax.axis_size("blk")
    return lax.ppermute(values, "blk", [(i, i ^ bit) for i in range(count)])


def blk_bit(bit):
    return (lax.axis_index("blk") & bit) != 0


def bits_of(count):
    out = []
    bit = count // 2
    while bit >= 1:
        out.append(bit)
        bit //= 2
    return out


def gather_bits(values, order):
    done = []
    for bit in order:
        other = swap_blk(values, bit)
        mine = blk_bit(bit)
        axis = sum(1 for d in done if d > bit)
        values = jnp.stack(
            [jnp.where(mine, other, values), jnp.where(mine, values, other)], axis=axis
        )
        done.append(bit)
    return values


def scatter_bits(values, axes, order):
    axes = list(axes)
    for bit in order:
        axis = axes.index(bit)
        mine = blk_bit(bit).astype(jnp.int32)
        keep = lax.dynamic_index_in_dim(values, mine, axis, keepdims=False)
        send = lax.dynamic_index_in_dim(values, 1 - mine, axis, keepdims=False)
        values = low(wide(keep) + wide(swap_blk(send, bit)))
        axes.remove(bit)
    return values


def by_place(parts):
    grp = lax.axis_index("grp")
    core = (grp & 1) != 0
    cross = (grp & 2) != 0
    a, b, c, d = parts
    a, b = jnp.where(core, b, a), jnp.where(core, a, b)
    c, d = jnp.where(core, d, c), jnp.where(core, c, d)
    a, c = jnp.where(cross, c, a), jnp.where(cross, a, c)
    b, d = jnp.where(cross, d, b), jnp.where(cross, b, d)
    return [a, b, c, d]


def gather_near(values):
    cross = swap_cross(values)
    both = swap_core(jnp.stack([values, cross]))
    return [values, both[0], cross, both[1]]


def gather_grp(values):
    return by_place(gather_near(values))


def gather_tokens(values, bit):
    half = values.shape[0] // 2
    cross = swap_cross(values)
    over = swap_blk(values, bit)
    first = swap_blk(cross[:half], bit)
    second = swap_cross(over[half:])
    chip = jnp.concatenate([values, cross, over, first, second])
    return jnp.concatenate([chip, swap_core(chip)])


def angles_of(position):
    half = HD // 2
    freqs = ROPE_BASE ** (-2.0 * jnp.arange(half, dtype=jnp.float32) / HD)
    return position.astype(jnp.float32)[:, None] * freqs[None, :]


def rotate_by(values, cosine, sine):
    half = HD // 2
    first_half = values[..., :half]
    second_half = values[..., half:]
    return jnp.concatenate(
        [first_half * cosine - second_half * sine, second_half * cosine + first_half * sine],
        axis=-1,
    )


def after(values, anchor):
    return lax.optimization_barrier((values, anchor))[0]


def gather_step(values, done, bit):
    other = swap_blk(values, bit)
    mine = blk_bit(bit)
    axis = sum(1 for d in done if d > bit)
    return jnp.stack(
        [jnp.where(mine, other, values), jnp.where(mine, values, other)], axis=axis
    )


def gather_near_stacked(values):
    both = jnp.stack([values, swap_cross(values)])
    return [both, swap_core(both)]


def ring_groups(count):
    return [[g * count + b for b in ring_order(count)] for g in range(4)]


def gather_ring(values):
    count = lax.axis_size("blk")
    return lax.all_gather(values, ("grp", "blk"), axis=0, axis_index_groups=ring_groups(count))


def exchange_near(parts):
    cross = swap_cross(jnp.stack([parts[2], parts[3]]))
    core = swap_core(jnp.stack([parts[1], cross[1]]))
    return [parts[0], core[0], cross[0], core[1]]


def on_device(
    tokens,
    cotangent,
    segment_ids,
    position_ids,
    w_attend,
    w_out,
    w_gate,
    w_up,
    w_down,
    small_params,
    first_attend,
    first_out,
    first_gate,
    first_up,
    first_down,
    first_small,
    second_attend,
    second_out,
    second_gate,
    second_up,
    second_down,
    second_small,
):
    rows_here, block_len = tokens.shape[:2]
    blk_count = lax.axis_size("blk")
    seq_len = block_len * blk_count
    token_count = rows_here * block_len
    grp = lax.axis_index("grp")
    blk = lax.axis_index("blk")
    cross_id, core_id = grp // 2, grp % 2
    strip_heads = H // 4
    strip_q = strip_heads * HD
    bits = bits_of(blk_count)
    team = blk_count // 4
    lows = [bit for bit in bits if bit < team]
    spread = [bits[0]] + lows
    low_shape = (2,) * len(lows)
    in_team = blk_bit(team).astype(jnp.int32)
    weight_rows = w_gate.shape[0]
    ff_block = w_down.shape[0]
    quarter = ff_block // 4
    widths = [size * blk_count // 2 for at, size in halves_of(quarter)]
    chip_rows = 4 * token_count
    half = token_count // 2

    ids = jnp.stack([grp, in_team])
    flat_low = tokens.reshape(token_count, D)
    dy_low = cotangent.reshape(token_count, D)
    positions = position_ids.reshape(token_count)
    kv_at = HQD + HD * cross_id + KVD * core_id
    strip_local = low(
        jnp.concatenate(
            [
                lax.dynamic_slice_in_dim(w_attend, strip_q * grp, strip_q, 1),
                lax.dynamic_slice_in_dim(w_attend, kv_at, HD, 1),
            ],
            axis=1,
        )
    )
    small_count = small_params.shape[0]
    small_send = jnp.concatenate([low(small_params), low(segment_ids.reshape(token_count))])
    strip_wide = strip_q + HD
    small_send = jnp.pad(small_send, (0, -small_send.shape[0] % (16 * strip_wide)))
    strip_local = jnp.concatenate([strip_local, small_send.reshape(-1, strip_wide)])
    ring = ring_order(blk_count)
    strip_ring = gather_ring(strip_local)
    small_ring = strip_ring[:, weight_rows:].reshape(blk_count, -1)[:, small_count : small_count + token_count]
    small_all = jnp.stack([small_ring[ring.index(b)] for b in range(blk_count)])
    digits = low(jnp.stack([positions // 64, positions % 64], axis=1))
    digits = jnp.pad(digits, ((0, 0), (0, HD - 2)))
    token_send = jnp.concatenate([flat_low, digits], axis=1)
    picked_a, picked_b = pick_columns(ids, w_gate, w_up, blk_count)
    got_a = swap_blk(picked_a[1], team)
    dy_cross = swap_cross(after(dy_low, picked_a))
    dy_over = swap_blk(after(dy_low, strip_ring), team)
    token_cross = after(swap_cross(token_send), (picked_a, strip_ring, got_a, dy_cross))

    def place(values, other, done, bit, lead=0):
        mine = blk_bit(bit)
        axis = lead + sum(1 for d in done if d > bit)
        return jnp.stack(
            [jnp.where(mine, other, values), jnp.where(mine, values, other)], axis=axis
        )

    mine_team = blk_bit(team)
    (low_first, size_first), (low_second, size_second) = halves_of(quarter)

    def team_pair(mine, got):
        return jnp.stack(
            [jnp.where(mine_team, got, mine), jnp.where(mine_team, mine, got)], axis=1
        )

    out_local = low(lax.dynamic_slice_in_dim(w_out, strip_q * grp, strip_q, 1))
    out_ring = gather_ring(after(out_local, strip_ring))
    down_here = low(lax.dynamic_slice_in_dim(w_down, quarter * grp, quarter, 0))
    token_core = swap_core(jnp.stack([token_send, token_cross]))
    freqs = ROPE_BASE ** (-2.0 * jnp.arange(HD // 2, dtype=jnp.float32) / HD)
    freqs = jnp.concatenate([freqs, freqs])[None]
    mixed_own, mixed_core, mixed_far, near_one, strip, vector = mix(
        ids, token_send, token_cross, token_core, strip_ring, freqs, blk_count, weight_rows, small_count
    )
    vector = vector[0]
    gain_one = vector[:D]
    gain_two = vector[D : 2 * D]
    seg_all = small_all.astype(jnp.int32)
    seg_all = seg_all.reshape(blk_count, rows_here, block_len)
    seg_key = jnp.broadcast_to(
        seg_all.transpose(1, 0, 2).reshape(rows_here, seq_len)[:, :, None], (rows_here, seq_len, HD)
    )
    seg_query = jnp.broadcast_to(segment_ids[:, None, :], (rows_here, 8, block_len))
    first_blk = jnp.sum((seg_all[:, :, -1] < segment_ids[None, :, 0]).astype(jnp.int32), axis=0)
    attend_ids = jnp.concatenate([blk[None], first_blk])

    mixed_cross = swap_cross(mixed_far)
    mixed_core = swap_core(jnp.stack([mixed_core, mixed_cross[1]]))
    pair_a = team_pair(picked_a[0], after(got_a, mixed_own))
    pair_a_got = swap_blk(pair_a, bits[0])
    mixed_core = after(mixed_core, (pair_a_got, dy_over))
    down_got = swap_blk(after(down_here, mixed_own), bits[0])
    query, packed_kv = pack(ids, mixed_own, mixed_cross, mixed_core)
    key_value = packed_kv.reshape(rows_here, block_len, 2 * KVD)
    kv_all = gather_ring(key_value)

    teams = [
        [g * blk_count + (i | t) for g in range(4) for t in (0, team)]
        for i in range(blk_count)
        if not i & team
    ]
    order = jnp.stack(
        [
            (grp ^ (2 * (i & 1) + (i >> 2))) * 2 + (in_team ^ ((i >> 1) & 1))
            for i in range(8)
        ]
    )

    peers = [[i for i in range(blk_count) if (i & team) == t] for t in (0, team)]

    def lows_of(values, done, lead=0, anchor=None):
        for bit in lows:
            got = swap_blk(values, bit)
            if anchor is not None:
                got = after(got, anchor)
            values = place(values, got, done, bit, lead)
            done = done + [bit]
        return values

    got_b = swap_blk(after(picked_b[1], mixed_own), team)
    pair_a = place(pair_a, after(pair_a_got, packed_kv), [team], bits[0], 1)
    pair_y_got = swap_blk(pair_a, lows[0])
    got_b, down_got = after((got_b, down_got), kv_all)
    kv_all = after(kv_all, (got_b, down_got, pair_y_got))
    down_here = place(down_here, down_got, [], bits[0])
    down_here = lows_of(down_here, [bits[0]]).reshape(2 * blk_count // 4, quarter, D)
    dy_first = swap_blk(dy_cross[:half], team)
    dy_second = swap_cross(dy_over[half:])
    dy_chip = jnp.concatenate([dy_low, dy_cross, dy_over, dy_first, dy_second])
    dy_team = jnp.concatenate([dy_chip, swap_core(dy_chip)])
    pair_b = team_pair(picked_b[0], after(got_b, kv_all))
    pair_b_got = swap_blk(pair_b, bits[0])
    out_ring = after(out_ring, packed_kv)
    out_strip = jnp.concatenate([out_ring[ring.index(b)] for b in range(blk_count)])
    out_cross = swap_cross(out_strip)
    out_core = swap_core(jnp.stack([out_strip, after(out_cross, kv_all)]))
    out_full = jnp.concatenate(by_place([out_strip, out_core[0], out_cross, out_core[1]]), axis=1)

    att_in, lse = attend(attend_ids, query, kv_all, seg_key, seg_query, block_len)
    flat = wide(flat_low)
    resid = flat + jnp.dot(att_in, out_full, preferred_element_type=jnp.float32)
    h_two = low(norm_apply(resid, gain_two))
    pair_a = place(pair_a, after(pair_y_got, h_two), [bits[0], team], lows[0], 1)
    for i in range(1, len(lows)):
        done = [bits[0], team] + lows[:i]
        pair_a = place(pair_a, swap_blk(pair_a, lows[i]), done, lows[i], 1)
    gate_up_a = pair_a.reshape(2, D, -1)
    pair_b_got = after(pair_b_got, h_two)
    down_a = down_here[:, :size_first].reshape(widths[0], D)
    down_b = down_here[:, size_first:].reshape(widths[1], D)
    h_team = lax.all_gather(h_two, ("grp", "blk"), axis=0, tiled=True, axis_index_groups=teams)
    pair_b_got = after(pair_b_got, (h_two, gate_up_a))
    pair_b = place(pair_b, pair_b_got, [team], bits[0], 1)
    h_team = after(h_team, (gate_up_a, pair_b, dy_team))
    hidden_a, d_gate_a, d_up_a, *part_a = middle(order, h_team, dy_team, gate_up_a, down_a)
    gate_up_b = lows_of(pair_b, [bits[0], team], 1, hidden_a).reshape(2, D, -1)
    down_grad_a = down_grad(after(hidden_a, gate_up_b), dy_team)
    down_share_a = lax.psum_scatter(
        down_grad_a, "blk", scatter_dimension=0, axis_index_groups=peers, tiled=True
    )
    column_grad_a = two_grads(h_team, d_gate_a, d_up_a)

    def part_sent(values, axis, bit):
        mine = blk_bit(bit).astype(jnp.int32)
        keep = lax.dynamic_index_in_dim(values, mine, axis, keepdims=False)
        send = lax.dynamic_index_in_dim(values, 1 - mine, axis, keepdims=False)
        return keep, swap_blk(send, bit)

    def part_sum(keep, got):
        return low(wide(keep) + wide(got))

    def columns_first(grad):
        grad = grad.reshape((2, 2, 2) + low_shape + (weight_rows, -1))
        return part_sent(grad, 2 + len(lows), lows[-1])

    def columns_mid(keep, got):
        values = part_sum(keep, got)
        for i in range(len(lows) - 2, -1, -1):
            values = part_sum(*part_sent(values, 3 + i, lows[i]))
        return values

    def columns_third(keep, got):
        values = part_sum(keep, got)
        mine = lax.dynamic_index_in_dim(values, in_team, 1, keepdims=False)
        send = lax.dynamic_index_in_dim(values, 1 - in_team, 1, keepdims=False)
        return values, (mine, swap_blk(send, team))

    def rows_second(keep, got):
        values = part_sum(keep, got)
        for i in range(len(lows) - 2, -1, -1):
            values = part_sum(*part_sent(values, 1 + i, lows[i]))
        return part_sent(values, 0, bits[0])

    def columns_last(mine, got):
        return jnp.stack(
            [jnp.where(mine_team, got, mine), jnp.where(mine_team, mine, got)], axis=1
        )

    first_a = columns_first(column_grad_a)
    hidden_b, d_gate_b, d_up_b, d_here, d_there = middle(
        order, after(h_team, (column_grad_a, down_grad_a)), dy_team, gate_up_b, down_b, part_a
    )

    def chip_sum(values, came):
        return low(wide(values) + wide(came))

    def scatter_far(chip):
        far = chip[3 * token_count :]
        return swap_blk(far[:half], team), swap_cross(far[half:])

    def scatter_near(chip, first, second):
        cross, over = (chip[token_count * i : token_count * (i + 1)] for i in (1, 2))
        cross = jnp.concatenate([low(wide(cross[:half]) + wide(first)), cross[half:]])
        over = jnp.concatenate([over[:half], low(wide(over[half:]) + wide(second))])
        return swap_cross(cross), swap_blk(over, team)

    near_att_cross = swap_cross(after(att_in, hidden_a))
    d_there = after(d_there, (first_a[1], down_share_a, near_att_cross))
    d_came = swap_core(d_there)
    down_grad_b = down_grad(hidden_b, dy_team)
    rows_b = part_sent(
        down_grad_b.reshape((2,) + low_shape + (size_second, D)), len(lows), lows[-1]
    )
    mid_a = columns_mid(*after(first_a, d_came))
    second_a = part_sent(mid_a, 1, bits[0])
    d_chip = chip_sum(d_here, after(d_came, down_grad_b))
    d_far = scatter_far(d_chip)
    column_grad_b = two_grads(h_team, *after((d_gate_b, d_up_b), d_chip))
    first_b = columns_first(column_grad_b)
    d_far = after(d_far, column_grad_b)
    d_cross, d_over = scatter_near(d_chip, *d_far)
    out_part, out_there = down(*after((hidden_a, hidden_b), d_far), down_a, down_b, token_count)
    out_came = swap_core(out_there)
    d_cross, d_over = after((d_cross, d_over), out_part)
    d_htwo = wide(d_chip[:token_count]) + wide(d_cross) + wide(d_over)

    norm_value_two, norm_back_two = jax.vjp(norm_apply, resid, gain_two)
    d_resid_norm, grad_gain_two = norm_back_two(d_htwo)
    d_resid = wide(dy_low) + d_resid_norm
    d_att = low(d_resid)
    rows_b = rows_second(*after(rows_b, d_att))

    d_attended = low(right_transposed(d_att, out_full))
    own_angles = angles_of(positions)
    cosine, sine = jnp.cos(own_angles), jnp.sin(own_angles)
    d_query, dkv = attend_back(
        attend_ids,
        query,
        kv_all,
        seg_key,
        seg_query,
        att_in,
        d_attended,
        lse,
        jnp.concatenate([cosine, cosine], axis=1),
        jnp.concatenate([sine, sine], axis=1),
        block_len,
    )
    dkv = lax.psum_scatter(
        dkv.reshape(blk_count * token_count, 2 * KVD),
        ("grp", "blk"),
        scatter_dimension=0,
        axis_index_groups=ring_groups(blk_count),
        tiled=True,
    )
    down_share_b = part_sum(*after(rows_b, d_query))
    sum_a, third_a = columns_third(*after(second_a, d_att))

    def to_strips(parts):
        return jnp.concatenate(exchange_near(by_place(parts)))

    near_dq = to_strips([d_query[:, strip_q * k : strip_q * (k + 1)] for k in range(4)])
    block_shape = (2,) * len(bits) + (weight_rows, -1)
    query_grad = low(left_product(near_one, near_dq)).reshape(block_shape)
    steps_query = part_sent(query_grad, len(bits) - 1, bits[-1])
    second_b = part_sent(columns_mid(*after(first_b, d_query)), 1, bits[0])
    dkv = after(dkv, down_share_b)
    own_part, core_part, far_part, bias_kv = turn_dkv(
        ids, dkv, jnp.concatenate([cosine, cosine], axis=1), jnp.concatenate([sine, sine], axis=1)
    )
    bias_q = jnp.sum(wide(d_query), axis=0)
    d_key = own_part
    cross_part = swap_cross(far_part)
    near_a = gather_near_stacked(columns_last(*after(third_a, own_part)))
    core_part = swap_core(jnp.stack([core_part, cross_part[1]]))
    kv_grad, hone_here, hone_there = make_kv_grad(
        blk_count,
        weight_rows,
        small_count,
        own_part,
        cross_part,
        core_part,
        near_dq,
        near_one,
        token_send,
        token_cross,
        token_core,
        strip,
        grad_gain_two[None],
        bias_q[None],
        bias_kv,
    )
    vector_rows = -(-small_count // HD)
    kv_grad = kv_grad.reshape((2,) * len(bits) + kv_grad.shape[1:])
    steps_kv = part_sent(kv_grad, len(bits) - 1, bits[-1])
    share_down = after(jnp.concatenate([down_share_a, down_share_b]), dkv)
    grad_down = lax.all_gather(share_down, "grp", axis=0, tiled=True)
    for i in range(len(bits) - 2, -1, -1):
        steps_query = part_sent(part_sum(*after(steps_query, d_key)), i, bits[i])
        kv_sum = part_sum(*steps_kv)
        kv_grad = kv_sum
        steps_kv = part_sent(kv_sum, i, bits[i])
    sum_b, third_b = columns_third(*after(second_b, kv_grad))
    share_kv_all = wide(steps_kv[0]) + wide(after(steps_kv[1], third_b[1]))
    share_kv = low(share_kv_all[:weight_rows])
    vector_part = share_kv_all[weight_rows : weight_rows + vector_rows]
    share_query = part_sum(*after(steps_query, kv_grad))
    near_att = swap_core(jnp.stack([att_in, near_att_cross]))
    near_att = jnp.concatenate([att_in, near_att[0], near_att_cross, near_att[1]])
    near_datt = to_strips([d_att[:, strip_q * k : strip_q * (k + 1)] for k in range(4)])
    out_grad = low(left_product(near_att, after(near_datt, d_attended))).reshape(block_shape)
    steps_out = part_sent(out_grad, len(bits) - 1, bits[-1])
    anchors = [own_part, kv_grad]
    for i in range(len(bits) - 2, -1, -1):
        anchor = anchors[min(len(bits) - 2 - i, 1)]
        steps_out = part_sent(part_sum(*after(steps_out, anchor)), i, bits[i])
    share_out = part_sum(*after(steps_out, kv_grad))

    grad_out = jnp.concatenate(gather_grp(share_out), axis=1)
    query_parts = gather_grp(share_query)
    key_parts = gather_grp(share_kv)
    grad_attend = jnp.concatenate(query_parts + [key_parts[k] for k in (0, 2, 1, 3)], axis=1)

    other = wide(swap_core(hone_there))
    d_hone = wide(hone_here[:token_count]) + other[:token_count]
    d_hone_send = low(wide(hone_here[token_count:]) + other[token_count:])
    d_hone_cross = swap_cross(d_hone_send)
    square_sum = square_total(
        [
            wide(s)
            for s in (share_query, share_kv, share_out, sum_a, sum_b, share_down)
        ]
    )
    packed = jnp.concatenate([vector_part, jnp.full((8, HD), square_sum)])
    packed = after(packed, (d_hone_send, d_hone))
    packed = packed + swap_cross(packed)
    packed = packed + swap_core(packed)
    share_vector = packed[:vector_rows].reshape(-1)[:small_count]
    square_sum = packed[vector_rows:] + jnp.sum(share_vector * share_vector)
    for bit in bits:
        square_sum = square_sum + swap_blk(square_sum, bit)
    grad_norm = jnp.sqrt(square_sum[0, 0])
    factor = jnp.minimum(1.0, CLIP_NORM / (grad_norm + 1e-06))
    out_chip = chip_sum(out_part, after(out_came, kv_grad))
    out_far = scatter_far(out_chip)
    factor = after(factor, (out_chip, near_a))

    new_first_attend, new_second_attend, new_attend = adam_step(
        w_attend, factor * wide(grad_attend), first_attend, second_attend, RATE_ATTEND, WEIGHT_DECAY
    )
    new_first_out, new_second_out, new_out = adam_step(
        w_out, factor * wide(grad_out), first_out, second_out, RATE_OUT, WEIGHT_DECAY
    )
    new_first_down, new_second_down, new_down = adam_step(
        w_down, factor * wide(grad_down), first_down, second_down, RATE_DOWN, WEIGHT_DECAY
    )
    own_b = columns_last(*third_b)
    cross_b = after(swap_cross(own_b), new_down)
    near_b = jnp.stack([own_b, cross_b])
    near_b = [near_b, swap_core(near_b)]
    new_first_gate, new_second_gate, new_gate = adam_columns(
        0, ids, factor[None], near_a, near_b, w_gate, first_gate, second_gate, blk_count, RATE_GATE, WEIGHT_DECAY
    )
    new_first_up, new_second_up, new_up = adam_columns(
        1, ids, factor[None], near_a, near_b, w_up, first_up, second_up, blk_count, RATE_GATE, WEIGHT_DECAY
    )
    norm_value_one, norm_back_one = jax.vjp(norm_apply, flat, gain_one)
    d_hone = after(d_hone + wide(after(d_hone_cross, new_gate)), new_gate)
    d_flat_norm, unused_gain = norm_back_one(d_hone)
    grad_tokens = low(d_resid + d_flat_norm)

    new_first_small, new_second_small, new_small = adam_step(
        small_params, factor * share_vector, first_small, second_small, RATE_VECTOR, 0.0
    )

    out_near = after(scatter_near(out_chip, *after(out_far, factor)), (new_gate, new_up))
    out_tokens = low(resid + wide(out_chip[:token_count]) + wide(out_near[0]) + wide(out_near[1]))
    return (
        out_tokens.reshape(rows_here, block_len, D),
        grad_tokens.reshape(rows_here, block_len, D),
        grad_norm,
        new_first_attend,
        new_second_attend,
        new_attend,
        new_first_out,
        new_second_out,
        new_out,
        new_first_gate,
        new_second_gate,
        new_gate,
        new_first_up,
        new_second_up,
        new_up,
        new_first_down,
        new_second_down,
        new_down,
        new_first_small,
        new_second_small,
        new_small,
    )


def solution(mesh):
    placed = (
        P("grp", "blk", None),
        P("grp", "blk", None),
        P("grp", "blk"),
        P("grp", "blk"),
        P("blk", None),
        P("blk", None),
        P("blk", None),
        P("blk", None),
        P("blk", None),
        P("blk"),
        P("blk", None),
        P("blk", None),
        P("blk", None),
        P("blk", None),
        P("blk", None),
        P("blk"),
        P("blk", None),
        P("blk", None),
        P("blk", None),
        P("blk", None),
        P("blk", None),
        P("blk"),
    )
    return jax.shard_map(
        on_device,
        mesh=mesh,
        in_specs=placed,
        out_specs=(
            P("grp", "blk", None),
            P("grp", "blk", None),
            P(),
            P("blk", None),
            P("blk", None),
            P("blk", None),
            P("blk", None),
            P("blk", None),
            P("blk", None),
            P("blk", None),
            P("blk", None),
            P("blk", None),
            P("blk", None),
            P("blk", None),
            P("blk", None),
            P("blk", None),
            P("blk", None),
            P("blk", None),
            P("blk"),
            P("blk"),
            P("blk"),
        ),
        check_vma=False,
    )
```

```python
import functools

import jax
import jax.numpy as jnp
from jax import lax
from jax.experimental import pallas as pl
from jax.experimental.pallas import tpu as pltpu
from jax.sharding import PartitionSpec as P

D = 1536
FF = 8960
H = 12
KVH = 2
HD = 128
STEP = 10
HQD = 1536
KVD = 256


NORM_EPS = 1e-06
ROPE_BASE = 10000.0
CLIP_NORM = 1.0
BETA_FIRST = 0.9
BETA_SECOND = 0.95
ADAM_EPS = 1e-08
WEIGHT_DECAY = 0.1
RATE_ATTEND = 0.06
RATE_OUT = 0.5
RATE_GATE = 0.06
RATE_DOWN = 0.03
RATE_VECTOR = 0.5
NEG_LARGE = -1e30
LOG2E = 1.4426950408889634
VMEM = 48 * 1024 * 1024
SMALL_COST = pl.CostEstimate(flops=1000, bytes_accessed=1000, transcendentals=0)


def norm_apply(values, gain):
    return values * lax.rsqrt(jnp.mean(values * values, axis=-1, keepdims=True) + NORM_EPS) * gain


def swish_product(gate, up_proj):
    return jax.nn.silu(gate) * up_proj


def left_product(left_side, right_side):
    return lax.dot_general(
        left_side, right_side, (((0,), (0,)), ((), ())), preferred_element_type=jnp.float32
    )


def right_transposed(left_side, right_side):
    return lax.dot_general(
        left_side, right_side, (((1,), (1,)), ((), ())), preferred_element_type=jnp.float32
    )


def square_total(arrays):
    return sum((jnp.sum(member * member) for member in arrays))


def adam_step(weight, grad, first, second, rate, decay):
    first_new = BETA_FIRST * first + (1.0 - BETA_FIRST) * grad
    second_new = BETA_SECOND * second + (1.0 - BETA_SECOND) * grad * grad
    first_hat = first_new / (1.0 - BETA_FIRST**STEP)
    second_hat = second_new / (1.0 - BETA_SECOND**STEP)
    weight_new = weight - rate * (first_hat / (jnp.sqrt(second_hat) + ADAM_EPS) + decay * weight)
    return (first_new, second_new, weight_new)


def ring_order(count):
    return list(range(0, count, 2)) + list(range(count - 1, 0, -2))


def halves_of(quarter):
    first = quarter * 16 // 35
    return ((0, first), (first, quarter - first))


def pick_body(blk_count, ids, gate_ref, up_ref, *out_refs):
    quarter = FF // blk_count // 4
    per = blk_count // 4
    for k in range(4):

        @pl.when(ids[0] == k)
        def _(k=k):
            for (at, size), out_ref in zip(halves_of(quarter), out_refs):
                for which, src in enumerate((gate_ref, up_ref)):
                    for bit in range(2):
                        parts = []
                        for high in range(2):
                            for small in range(per):
                                begin = (((high * 2 + bit) * per + small) * 4 + k) * quarter + at
                                parts.append(src[:, begin : begin + size])
                        out_ref[ids[1] ^ bit, which] = jnp.concatenate(parts, axis=1).astype(
                            jnp.bfloat16
                        )


def pick_columns(ids, gate, up, blk_count):
    rows = gate.shape[0]
    step = 48 if rows % 48 == 0 else rows
    widths = [size * blk_count // 2 for at, size in halves_of(FF // blk_count // 4)]
    spec = pl.BlockSpec((step, FF), lambda i, ids: (i, 0))
    return pl.pallas_call(
        functools.partial(pick_body, blk_count),
        grid_spec=pltpu.PrefetchScalarGridSpec(
            num_scalar_prefetch=1,
            grid=(rows // step,),
            in_specs=[spec, spec],
            out_specs=[pl.BlockSpec((2, 2, step, w), lambda i, ids: (0, 0, i, 0)) for w in widths],
        ),
        out_shape=[jax.ShapeDtypeStruct((2, 2, rows, w), jnp.bfloat16) for w in widths],
        compiler_params=pltpu.CompilerParams(vmem_limit_bytes=VMEM),
        cost_estimate=SMALL_COST,
        name="pick_columns",
    )(ids, gate, up)


def adam_body(blk_count, rate, decay, ids, factor_ref, first_ref, first_far_ref, second_ref, second_far_ref, w_ref, m_ref, v_ref, m_out, v_out, w_out):
    per = blk_count // 4
    sizes = [size for at, size in halves_of(FF // blk_count // 4)]
    grads = []
    for near_ref, far_ref in ((first_ref, first_far_ref), (second_ref, second_far_ref)):
        by_grp = []
        for k in range(4):
            away = ids[0] ^ k
            bits_of_k = []
            for bit in range(2):
                near = near_ref[away >> 1, bit].astype(jnp.float32)
                far = far_ref[away >> 1, bit].astype(jnp.float32)
                bits_of_k.append(jnp.where((away & 1) == 1, far, near))
            by_grp.append(bits_of_k)
        grads.append(by_grp)
    parts = []
    for high in range(2):
        for bit in range(2):
            for small in range(per):
                place = high * per + small
                for k in range(4):
                    for part, size in zip(grads, sizes):
                        parts.append(part[k][bit][:, place * size : (place + 1) * size])
    grad = jnp.concatenate(parts, axis=1) * factor_ref[0]
    m, v, w = adam_step(w_ref[...], grad, m_ref[...], v_ref[...], rate, decay)
    m_out[...] = m
    v_out[...] = v
    w_out[...] = w


def adam_columns(which, ids, factor, first, second, w, m, v, blk_count, rate, decay):
    rows = w.shape[0]
    step = 32 if rows % 32 == 0 else rows
    spec = pl.BlockSpec((step, FF), lambda i, ids: (i, 0))
    shape = jax.ShapeDtypeStruct((rows, FF), jnp.float32)
    grads = [
        pl.BlockSpec((2, None, 2, step, g.shape[-1]), lambda i, ids: (0, which, 0, i, 0))
        for g in first + second
    ]
    return pl.pallas_call(
        functools.partial(adam_body, blk_count, rate, decay),
        grid_spec=pltpu.PrefetchScalarGridSpec(
            num_scalar_prefetch=1,
            grid=(rows // step,),
            in_specs=[pl.BlockSpec(memory_space=pltpu.SMEM)] + grads + [spec, spec, spec],
            out_specs=[spec, spec, spec],
        ),
        out_shape=[shape] * 3,
        compiler_params=pltpu.CompilerParams(vmem_limit_bytes=VMEM),
        cost_estimate=SMALL_COST,
        name="adam_columns",
    )(ids, factor, *first, *second, w, m, v)


def nt(a, b, **kw):
    return lax.dot_general(a, b, (((1,), (1,)), ((), ())), preferred_element_type=jnp.float32, **kw)

def tn(a, b, **kw):
    return lax.dot_general(a, b, (((0,), (0,)), ((), ())), preferred_element_type=jnp.float32, **kw)

def stack_heads(ref, kvh, group):
    return jnp.concatenate([ref[:, HD * (kvh * group + i): HD * (kvh * group + i + 1)] for i in range(group)], axis=0)

def hidden_from(seg_key_ref, seg_query_ref, first, chunk, block_len, blk):
    key = first + lax.broadcasted_iota(jnp.int32, (chunk, block_len), 0)
    query = blk * block_len + lax.broadcasted_iota(jnp.int32, (chunk, block_len), 1)
    seg_key = seg_key_ref[pl.ds(first, chunk), :]
    counts = jnp.logical_and(key <= query, seg_key == seg_query_ref[0:1, :])
    return jnp.where(counts, 0.0, NEG_LARGE)

def ring_pair(ref, c, at):
    return jnp.concatenate(
        [ref[c, :, at : at + HD], ref[ref.shape[0] - 1 - c, :, at : at + HD]], axis=0
    )


def attend_body(chunk, ids, q_ref, k_ref, v_ref, seg_key_ref, seg_query_ref, o_ref, lse_ref, m_s, l_s, acc_s):
    block_len = q_ref.shape[0]
    group = H // KVH
    row = pl.program_id(0)
    per = chunk // block_len
    scale = HD ** (-0.5) * LOG2E
    start = ids[1 + row] // per
    stop = ids[0] // per + 1
    for kvh in range(KVH):
        q = stack_heads(q_ref, kvh, group)
        m_s[...] = jnp.full_like(m_s, NEG_LARGE)
        l_s[...] = jnp.zeros_like(l_s)
        acc_s[...] = jnp.zeros_like(acc_s)

        def step(c, carry):
            keys = ring_pair(k_ref, c, HD * kvh)
            vals = ring_pair(v_ref, c, HD * kvh)
            bias = hidden_from(seg_key_ref, seg_query_ref, c * chunk, chunk, block_len, ids[0])
            s = nt(keys, q) * scale + jnp.concatenate([bias] * group, axis=1)
            old = m_s[0:1, :]
            new = jnp.maximum(old, jnp.max(s, axis=0, keepdims=True))
            p = jnp.exp2(s - new)
            fade = jnp.exp2(old - new)
            l_s[0:1, :] = l_s[0:1, :] * fade + jnp.sum(p, axis=0, keepdims=True)
            acc_s[...] = acc_s[...] * fade + tn(vals, p.astype(jnp.bfloat16))
            m_s[0:1, :] = new
            return carry

        lax.fori_loop(start, stop, step, 0)
        total = l_s[0:1, :]
        out = (acc_s[...] * (1.0 / total)).T
        for i in range(group):
            o_ref[:, HD * (kvh * group + i): HD * (kvh * group + i + 1)] = out[block_len * i: block_len * (i + 1), :].astype(jnp.bfloat16)
        lse_ref[kvh] = jnp.broadcast_to(m_s[0:1, :] + jnp.log2(total), (8, group * block_len))

def attend(ids, q, kv, seg_key, seg_query, block_len):
    blk_count, rows = kv.shape[:2]
    group = H // KVH
    chunk = 2 * block_len
    many = group * block_len
    return pl.pallas_call(
        functools.partial(attend_body, chunk),
        grid_spec=pltpu.PrefetchScalarGridSpec(
            num_scalar_prefetch=1, grid=(rows,),
            in_specs=[
                pl.BlockSpec((block_len, HQD), lambda r, ids: (r, 0)),
                pl.BlockSpec((blk_count, None, block_len, KVD), lambda r, ids: (0, r, 0, 0)),
                pl.BlockSpec((blk_count, None, block_len, KVD), lambda r, ids: (0, r, 0, 1)),
                pl.BlockSpec((None, blk_count * block_len, HD), lambda r, ids: (r, 0, 0)),
                pl.BlockSpec((None, 8, block_len), lambda r, ids: (r, 0, 0)),
            ],
            out_specs=[
                pl.BlockSpec((block_len, HQD), lambda r, ids: (r, 0)),
                pl.BlockSpec((None, KVH, 8, many), lambda r, ids: (r, 0, 0, 0)),
            ],
            scratch_shapes=[pltpu.VMEM((8, many), jnp.float32), pltpu.VMEM((8, many), jnp.float32), pltpu.VMEM((HD, many), jnp.float32)]),
        out_shape=[
            jax.ShapeDtypeStruct((rows * block_len, HQD), jnp.bfloat16),
            jax.ShapeDtypeStruct((rows, KVH, 8, many), jnp.float32),
        ],
        compiler_params=pltpu.CompilerParams(vmem_limit_bytes=VMEM),
        cost_estimate=SMALL_COST,
        name="attend",
    )(ids, q, kv, kv, seg_key, seg_query)

def turn_back(u, cosine, sine):
    lane = lax.broadcasted_iota(jnp.int32, u.shape, 1)
    other = pltpu.roll(u, HD // 2, 1)
    return u * cosine + jnp.where(lane < HD // 2, other, -other) * sine

def attend_back_body(chunk, ids, q_ref, k_ref, v_ref, seg_key_ref, seg_query_ref, o_ref, do_ref, lse_ref, cos_ref, sin_ref, dq_ref, dkv_ref, dq_s):
    block_len = q_ref.shape[0]
    group = H // KVH
    row = pl.program_id(0)
    per = chunk // block_len
    plain = HD ** (-0.5)
    scale = plain * LOG2E
    start = ids[1 + row] // per
    stop = ids[0] // per + 1
    dkv_ref[...] = jnp.zeros_like(dkv_ref)
    for kvh in range(KVH):
        q = stack_heads(q_ref, kvh, group)
        do = stack_heads(do_ref, kvh, group)
        o = stack_heads(o_ref, kvh, group)
        both = do.astype(jnp.float32) * o.astype(jnp.float32)
        delta = nt(jnp.ones((8, HD), jnp.float32), both, precision=lax.Precision.HIGHEST)[0:1, :]
        lse = lse_ref[kvh][0:1, :]
        dq_s[...] = jnp.zeros_like(dq_s)

        def step(c, carry):
            keys = ring_pair(k_ref, c, HD * kvh)
            vals = ring_pair(v_ref, c, HD * kvh)
            bias = hidden_from(seg_key_ref, seg_query_ref, c * chunk, chunk, block_len, ids[0])
            s = nt(keys, q) * scale + jnp.concatenate([bias] * group, axis=1)
            p = jnp.exp2(s - lse)
            dp = nt(vals, do)
            ds = (p * (dp - delta)).astype(jnp.bfloat16)
            dk = jnp.dot(ds, q, preferred_element_type=jnp.float32) * plain
            dv = jnp.dot(p.astype(jnp.bfloat16), do, preferred_element_type=jnp.float32)
            for at, part in ((HD * kvh, dk.astype(jnp.bfloat16)), (KVD + HD * kvh, dv.astype(jnp.bfloat16))):
                dkv_ref[c, :, at : at + HD] = part[:block_len]
                dkv_ref[dkv_ref.shape[0] - 1 - c, :, at : at + HD] = part[block_len:]
            dq_s[...] += tn(ds, keys)
            return carry

        lax.fori_loop(start, stop, step, 0)
        cosine, sine = cos_ref[...], sin_ref[...]
        for i in range(group):
            u = dq_s[block_len * i: block_len * (i + 1), :] * plain
            at = HD * (kvh * group + i)
            dq_ref[:, at: at + HD] = turn_back(u, cosine, sine).astype(jnp.bfloat16)

def attend_back(ids, q, kv, seg_key, seg_query, o, do, lse, cosine, sine, block_len):
    blk_count, rows = kv.shape[:2]
    group = H // KVH
    chunk = 2 * block_len
    many = group * block_len
    per_row = pl.BlockSpec((block_len, HQD), lambda r, ids: (r, 0))
    turn = pl.BlockSpec((block_len, HD), lambda r, ids: (r, 0))
    return pl.pallas_call(
        functools.partial(attend_back_body, chunk),
        grid_spec=pltpu.PrefetchScalarGridSpec(
            num_scalar_prefetch=1, grid=(rows,),
            in_specs=[
                per_row,
                pl.BlockSpec((blk_count, None, block_len, KVD), lambda r, ids: (0, r, 0, 0)),
                pl.BlockSpec((blk_count, None, block_len, KVD), lambda r, ids: (0, r, 0, 1)),
                pl.BlockSpec((None, blk_count * block_len, HD), lambda r, ids: (r, 0, 0)),
                pl.BlockSpec((None, 8, block_len), lambda r, ids: (r, 0, 0)),
                per_row, per_row,
                pl.BlockSpec((None, KVH, 8, many), lambda r, ids: (r, 0, 0, 0)),
                turn, turn,
            ],
            out_specs=[per_row, pl.BlockSpec((blk_count, None, block_len, 2 * KVD), lambda r, ids: (0, r, 0, 0))],
            scratch_shapes=[pltpu.VMEM((many, HD), jnp.float32)]),
        out_shape=[
            jax.ShapeDtypeStruct((rows * block_len, HQD), jnp.bfloat16),
            jax.ShapeDtypeStruct((blk_count, rows, block_len, 2 * KVD), jnp.bfloat16),
        ],
        compiler_params=pltpu.CompilerParams(vmem_limit_bytes=VMEM),
        cost_estimate=SMALL_COST,
        name="attend_back",
    )(ids, q, kv, kv, seg_key, seg_query, o, do, lse, cosine, sine)

def nn(a, b):
    return jnp.dot(a, b, preferred_element_type=jnp.float32)


def middle_body(add, order, h_ref, dy_ref, wg_ref, wu_ref, wd_ref, *refs):
    prev_refs = refs[:2] if add else None
    hid_ref, dg_ref, du_ref, dh_ref, dh_far_ref = refs[-5:]
    here = pl.program_id(0) < 4
    h = h_ref[...]
    gate = nn(h, wg_ref[...])
    up = nn(h, wu_ref[...])
    sig = 1.0 / (1.0 + jnp.exp(-gate))
    silu = gate * sig
    hid_ref[...] = (silu * up).astype(jnp.bfloat16)
    dhid = nt(dy_ref[...], wd_ref[...])
    dg = (dhid * up * sig * (1.0 + gate * (1.0 - sig))).astype(jnp.bfloat16)
    du = (dhid * silu).astype(jnp.bfloat16)
    dg_ref[...] = dg
    du_ref[...] = du
    dh = nt(dg, wg_ref[...]) + nt(du, wu_ref[...])
    if add:
        prev = jnp.where(here, prev_refs[0][...].astype(jnp.float32), prev_refs[1][...].astype(jnp.float32))
        dh = dh + prev
    dh = dh.astype(jnp.bfloat16)

    @pl.when(here)
    def _():
        dh_ref[...] = dh

    @pl.when(jnp.logical_not(here))
    def _():
        dh_far_ref[...] = dh


def middle(order, h, dy, gate_up, wd, prev=None):
    count = h.shape[0]
    step = count // order.shape[0]
    wide_here = wd.shape[0]
    row = pl.BlockSpec((step, D), lambda i, order: (i, 0))
    placed = pl.BlockSpec((step, D), lambda i, order: (order[i], 0))
    part = pl.BlockSpec((step, wide_here), lambda i, order: (i, 0))
    part_placed = pl.BlockSpec((step, wide_here), lambda i, order: (order[i], 0))
    once = pl.Buffered(1)
    extra = [] if prev is None else list(prev)
    near = pl.BlockSpec((step, D), lambda i, order: (jnp.minimum(i, 3), 0))
    far = pl.BlockSpec((step, D), lambda i, order: (jnp.maximum(i - 4, 0), 0))
    return pl.pallas_call(
        functools.partial(middle_body, prev is not None),
        grid_spec=pltpu.PrefetchScalarGridSpec(
            num_scalar_prefetch=1,
            grid=(count // step,),
            in_specs=[
                placed,
                row,
                pl.BlockSpec((None, D, wide_here), lambda i, order: (0, 0, 0), pipeline_mode=once),
                pl.BlockSpec((None, D, wide_here), lambda i, order: (1, 0, 0), pipeline_mode=once),
                pl.BlockSpec((wide_here, D), lambda i, order: (0, 0), pipeline_mode=once),
            ]
            + [near, far][: len(extra)],
            out_specs=[part, part_placed, part_placed, near, far],
        ),
        out_shape=[jax.ShapeDtypeStruct((count, wide_here), jnp.bfloat16)] * 3
        + [jax.ShapeDtypeStruct((count // 2, D), jnp.bfloat16)] * 2,
        compiler_params=pltpu.CompilerParams(vmem_limit_bytes=VMEM),
        cost_estimate=SMALL_COST,
        name="middle",
    )(order, h, dy, gate_up, gate_up, wd, *extra)


def two_grads_body(h_ref, a_ref, b_ref, out_ref):
    h = h_ref[...]
    out_ref[0] = tn(h, a_ref[...]).astype(jnp.bfloat16)
    out_ref[1] = tn(h, b_ref[...]).astype(jnp.bfloat16)


def two_grads(h, a, b, step=256):
    count = h.shape[0]
    wide_here = a.shape[1]
    whole = pl.BlockSpec(a.shape, lambda i: (0, 0), pipeline_mode=pl.Buffered(1))
    return pl.pallas_call(
        two_grads_body,
        grid=(D // step,),
        in_specs=[pl.BlockSpec((count, step), lambda i: (0, i)), whole, whole],
        out_specs=pl.BlockSpec((2, step, wide_here), lambda i: (0, i, 0)),
        out_shape=jax.ShapeDtypeStruct((2, D, wide_here), jnp.bfloat16),
        compiler_params=pltpu.CompilerParams(vmem_limit_bytes=VMEM),
        cost_estimate=SMALL_COST,
        name="two_grads",
    )(h, a, b)


def down_grad_body(hid_ref, dy_ref, g_ref):
    g_ref[...] = tn(hid_ref[...], dy_ref[...]).astype(jnp.bfloat16)

def down_grad(hid, dy, step=512):
    T, F = hid.shape
    D = dy.shape[1]
    return pl.pallas_call(down_grad_body, grid=(D // step,),
        in_specs=[pl.BlockSpec((T, F), lambda i: (0, 0), pipeline_mode=pl.Buffered(1)), pl.BlockSpec((T, step), lambda i: (0, i))],
        out_specs=pl.BlockSpec((F, step), lambda i: (0, i)),
        out_shape=jax.ShapeDtypeStruct((F, D), jnp.bfloat16),
        compiler_params=pltpu.CompilerParams(vmem_limit_bytes=VMEM),
        cost_estimate=SMALL_COST,
        name="down_grad")(hid, dy)

def down_body(hid_a_ref, hid_b_ref, wd_a_ref, wd_b_ref, o_ref, o_far_ref):
    out = nn(hid_a_ref[...], wd_a_ref[...]) + nn(hid_b_ref[...], wd_b_ref[...])
    out = out.astype(jnp.bfloat16)
    here = pl.program_id(0) < 4

    @pl.when(here)
    def _():
        o_ref[...] = out

    @pl.when(jnp.logical_not(here))
    def _():
        o_far_ref[...] = out


def down(hid_a, hid_b, wd_a, wd_b, step):
    count = hid_a.shape[0]

    def rows(array):
        return pl.BlockSpec((step, array.shape[1]), lambda i: (i, 0))

    def whole(array):
        return pl.BlockSpec(array.shape, lambda i: (0, 0), pipeline_mode=pl.Buffered(1))

    return pl.pallas_call(
        down_body,
        grid=(count // step,),
        in_specs=[rows(hid_a), rows(hid_b), whole(wd_a), whole(wd_b)],
        out_specs=[
            pl.BlockSpec((step, D), lambda i: (jnp.minimum(i, 3), 0)),
            pl.BlockSpec((step, D), lambda i: (jnp.maximum(i - 4, 0), 0)),
        ],
        out_shape=[jax.ShapeDtypeStruct((count // 2, D), jnp.bfloat16)] * 2,
        compiler_params=pltpu.CompilerParams(vmem_limit_bytes=VMEM),
        cost_estimate=SMALL_COST,
        name="down",
    )(hid_a, hid_b, wd_a, wd_b)


def turn(u, cosine, sine):
    lane = lax.broadcasted_iota(jnp.int32, u.shape, 1)
    other = pltpu.roll(u, HD // 2, 1)
    return u * cosine + jnp.where(lane < HD // 2, -other, other) * sine


def mix_body(
    blk_count, rows, small_count, ids, own_ref, cross_ref, core_ref, ring_ref, freq_ref,
    self_ref, near_ref, far_ref, one_ref, strip_ref, vector_ref,
):
    ring = ring_order(blk_count)
    wide_here = ring_ref.shape[-1]
    pieces = []
    for b in range(blk_count):
        at = ring.index(b)
        strip_ref[rows * b : rows * (b + 1)] = ring_ref[at, :rows]
        left = small_count
        line = rows
        while left > 0:
            size = min(left, wide_here)
            pieces.append(ring_ref[at, line : line + 1, :size].astype(jnp.float32))
            left -= size
            line += 1
    vector = jnp.concatenate(pieces, axis=1)
    vector_ref[...] = vector
    gain = vector[:, :D]
    grp = ids[0]
    strip_q = wide_here - HD
    bias = jnp.zeros((1, wide_here), jnp.float32)
    for k in range(4):
        kv_at = 2 * D + HQD + HD * (k // 2) + KVD * (k % 2)
        part = jnp.concatenate(
            [
                vector[:, 2 * D + strip_q * k : 2 * D + strip_q * (k + 1)],
                vector[:, kv_at : kv_at + HD],
            ],
            axis=1,
        )
        bias = bias + jnp.where(grp == k, part, 0.0)
    count = own_ref.shape[0]
    strip = strip_ref[...]
    for d in range(4):
        source = (own_ref[...], core_ref[0], cross_ref[...], core_ref[1])[d]
        x = source[:, :D].astype(jnp.float32)
        root = lax.rsqrt(jnp.mean(x * x, axis=1, keepdims=True) + NORM_EPS)
        one = (x * root * gain).astype(jnp.bfloat16)
        one_ref[count * d : count * (d + 1)] = one
        mixed = nn(one, strip) + bias
        digits = source[:, D : D + HD].astype(jnp.float32)
        position = 64.0 * digits[:, 0:1] + digits[:, 1:2]
        angles = position * freq_ref[...]
        cosine, sine = jnp.cos(angles), jnp.sin(angles)
        for i in range(wide_here // HD):
            c, s = cosine, sine
            if i == wide_here // HD - 1:
                c = jnp.where(grp % 2 == 1, 1.0, c)
                s = jnp.where(grp % 2 == 1, 0.0, s)
            at = HD * i
            out = turn(mixed[:, at : at + HD], c, s).astype(jnp.bfloat16)
            if d == 0:
                self_ref[:, at : at + HD] = out
            elif d == 1:
                near_ref[:, at : at + HD] = out
            else:
                far_ref[d - 2, :, at : at + HD] = out


def mix(ids, own, cross, core, ring, freq, blk_count, rows, small_count):
    count = own.shape[0]
    wide_here = ring.shape[-1]
    low16 = jnp.bfloat16
    return pl.pallas_call(
        functools.partial(mix_body, blk_count, rows, small_count),
        in_specs=[pl.BlockSpec(memory_space=pltpu.SMEM)] + [pl.BlockSpec(memory_space=pltpu.VMEM)] * 5,
        out_specs=[pl.BlockSpec(memory_space=pltpu.VMEM)] * 6,
        out_shape=[
            jax.ShapeDtypeStruct((count, wide_here), low16),
            jax.ShapeDtypeStruct((count, wide_here), low16),
            jax.ShapeDtypeStruct((2, count, wide_here), low16),
            jax.ShapeDtypeStruct((4 * count, D), low16),
            jax.ShapeDtypeStruct((D, wide_here), low16),
            jax.ShapeDtypeStruct((1, blk_count * small_count), jnp.float32),
        ],
        compiler_params=pltpu.CompilerParams(vmem_limit_bytes=VMEM),
        cost_estimate=SMALL_COST,
        name="mix",
    )(ids, own, cross, core, ring, freq)


def pack_body(ids, self_ref, cross_ref, core_ref, q_ref, kv_ref):
    strip_q = self_ref.shape[1] - HD
    for g in range(4):

        @pl.when(ids[0] == g)
        def _(g=g):
            for k in range(4):
                part = (self_ref[...], core_ref[0], cross_ref[0], core_ref[1])[g ^ k]
                q_ref[:, strip_q * k : strip_q * (k + 1)] = part[:, :strip_q]
                at = (k % 2) * KVD + (k // 2) * HD
                kv_ref[:, at : at + HD] = part[:, strip_q:]


def pack(ids, own, cross, core):
    count = own.shape[0]
    return pl.pallas_call(
        pack_body,
        in_specs=[pl.BlockSpec(memory_space=pltpu.SMEM)] + [pl.BlockSpec(memory_space=pltpu.VMEM)] * 3,
        out_specs=[pl.BlockSpec(memory_space=pltpu.VMEM)] * 2,
        out_shape=[
            jax.ShapeDtypeStruct((count, HQD), jnp.bfloat16),
            jax.ShapeDtypeStruct((count, 2 * KVD), jnp.bfloat16),
        ],
        compiler_params=pltpu.CompilerParams(vmem_limit_bytes=VMEM),
        cost_estimate=SMALL_COST,
        name="pack",
    )(ids, own, cross, core)


def turn_dkv_body(ids, dkv_ref, cos_ref, sin_ref, self_ref, near_ref, far_ref, sum_ref):
    items = []
    sums = [None] * 4
    for k in range(4):
        at = (k % 2) * KVD + (k // 2) * HD
        part = dkv_ref[:, at : at + HD]
        if k % 2 == 0:
            part = turn_back(part.astype(jnp.float32), cos_ref[...], sin_ref[...]).astype(jnp.bfloat16)
        items.append(part)
        sums[(k % 2) * 2 + k // 2] = jnp.sum(part.astype(jnp.float32), axis=0, keepdims=True)
    sum_ref[...] = jnp.concatenate(sums, axis=1)
    for g in range(4):

        @pl.when(ids[0] == g)
        def _(g=g):
            self_ref[...] = items[g]
            near_ref[...] = items[g ^ 1]
            far_ref[0] = items[g ^ 2]
            far_ref[1] = items[g ^ 3]


def turn_dkv(ids, dkv, cosine, sine):
    count = dkv.shape[0]
    return pl.pallas_call(
        turn_dkv_body,
        in_specs=[pl.BlockSpec(memory_space=pltpu.SMEM)] + [pl.BlockSpec(memory_space=pltpu.VMEM)] * 3,
        out_specs=[pl.BlockSpec(memory_space=pltpu.VMEM)] * 4,
        out_shape=[
            jax.ShapeDtypeStruct((count, HD), jnp.bfloat16),
            jax.ShapeDtypeStruct((count, HD), jnp.bfloat16),
            jax.ShapeDtypeStruct((2, count, HD), jnp.bfloat16),
            jax.ShapeDtypeStruct((1, 2 * KVD), jnp.float32),
        ],
        compiler_params=pltpu.CompilerParams(vmem_limit_bytes=VMEM),
        cost_estimate=SMALL_COST,
        name="turn_dkv",
    )(ids, dkv, cosine, sine)


def kv_grad_body(
    blk_count, rows, small_count, self_ref, cross_ref, core_ref, dq_ref, one_ref, own_ref, near_x_ref,
    core_x_ref, strip_ref, gain_two_ref, bias_q_ref, bias_kv_ref, grad_ref, here_ref, there_ref,
):
    count = self_ref.shape[0]
    strip_q = strip_ref.shape[1] - HD
    parts = (self_ref[...], core_ref[0], cross_ref[0], core_ref[1])
    near = jnp.concatenate(parts, axis=0)
    grad = tn(one_ref[...], near)
    gain_one = jnp.zeros((1, D), jnp.float32)
    for d in range(4):
        x = (own_ref[...], core_x_ref[0], near_x_ref[...], core_x_ref[1])[d][:, :D].astype(jnp.float32)
        root = lax.rsqrt(jnp.mean(x * x, axis=1, keepdims=True) + NORM_EPS)
        hone = nt(dq_ref[count * d : count * (d + 1)], strip_ref[:, :strip_q])
        hone = hone + nt(parts[d], strip_ref[:, strip_q:])
        gain_one = gain_one + jnp.sum(hone * x * root, axis=0, keepdims=True)
        out_ref = (here_ref, there_ref)[d % 2]
        out_ref[count * (d // 2) : count * (d // 2 + 1)] = hone.astype(jnp.bfloat16)
    vector = jnp.concatenate([gain_one, gain_two_ref[...], bias_q_ref[...], bias_kv_ref[...]], axis=1)
    extra = grad_ref.shape[1] - rows
    for b in range(blk_count):
        grad_ref[b, :rows] = grad[rows * b : rows * (b + 1)].astype(jnp.bfloat16)
        lines = []
        for line in range(extra):
            size = min(HD, max(small_count - line * HD, 0))
            begin = small_count * b + line * HD
            pieces = [vector[:, begin : begin + size]] if size > 0 else []
            if size < HD:
                pieces.append(jnp.zeros((1, HD - size), jnp.float32))
            lines.append(pieces[0] if len(pieces) == 1 else jnp.concatenate(pieces, axis=1))
        grad_ref[b, rows:] = jnp.concatenate(lines, axis=0).astype(jnp.bfloat16)


def kv_grad_rows(rows, small_count):
    needed = rows + -(-small_count // HD)
    return needed + -needed % 16


def make_kv_grad(blk_count, rows, small_count, own, cross, core, dq, one, x_own, x_cross, x_core, strip, gain_two, bias_q, bias_kv):
    count = own.shape[0]
    height = kv_grad_rows(rows, small_count)
    return pl.pallas_call(
        functools.partial(kv_grad_body, blk_count, rows, small_count),
        in_specs=[pl.BlockSpec(memory_space=pltpu.VMEM)] * 12,
        out_specs=[pl.BlockSpec(memory_space=pltpu.VMEM)] * 3,
        out_shape=[
            jax.ShapeDtypeStruct((blk_count, height, HD), jnp.bfloat16),
            jax.ShapeDtypeStruct((2 * count, D), jnp.bfloat16),
            jax.ShapeDtypeStruct((2 * count, D), jnp.bfloat16),
        ],
        compiler_params=pltpu.CompilerParams(vmem_limit_bytes=VMEM),
        cost_estimate=SMALL_COST,
        name="kv_grad",
    )(own, cross, core, dq, one, x_own, x_cross, x_core, strip, gain_two, bias_q, bias_kv)


CORE = [(0, 1), (1, 0), (2, 3), (3, 2)]
CROSS = [(0, 2), (2, 0), (1, 3), (3, 1)]
DIAG = [(0, 3), (3, 0), (1, 2), (2, 1)]


def low(values):
    return values.astype(jnp.bfloat16)


def wide(values):
    return values.astype(jnp.float32)


def swap_core(values):
    return lax.ppermute(values, "grp", CORE)


def swap_cross(values):
    return lax.ppermute(values, "grp", CROSS)


def swap_diag(values):
    return lax.ppermute(values, "grp", DIAG)


def swap_blk(values, bit):
    count = lax.axis_size("blk")
    return lax.ppermute(values, "blk", [(i, i ^ bit) for i in range(count)])


def blk_bit(bit):
    return (lax.axis_index("blk") & bit) != 0


def bits_of(count):
    out = []
    bit = count // 2
    while bit >= 1:
        out.append(bit)
        bit //= 2
    return out


def gather_bits(values, order):
    done = []
    for bit in order:
        other = swap_blk(values, bit)
        mine = blk_bit(bit)
        axis = sum(1 for d in done if d > bit)
        values = jnp.stack(
            [jnp.where(mine, other, values), jnp.where(mine, values, other)], axis=axis
        )
        done.append(bit)
    return values


def scatter_bits(values, axes, order):
    axes = list(axes)
    for bit in order:
        axis = axes.index(bit)
        mine = blk_bit(bit).astype(jnp.int32)
        keep = lax.dynamic_index_in_dim(values, mine, axis, keepdims=False)
        send = lax.dynamic_index_in_dim(values, 1 - mine, axis, keepdims=False)
        values = low(wide(keep) + wide(swap_blk(send, bit)))
        axes.remove(bit)
    return values


def by_place(parts):
    grp = lax.axis_index("grp")
    core = (grp & 1) != 0
    cross = (grp & 2) != 0
    a, b, c, d = parts
    a, b = jnp.where(core, b, a), jnp.where(core, a, b)
    c, d = jnp.where(core, d, c), jnp.where(core, c, d)
    a, c = jnp.where(cross, c, a), jnp.where(cross, a, c)
    b, d = jnp.where(cross, d, b), jnp.where(cross, b, d)
    return [a, b, c, d]


def gather_near(values):
    cross = swap_cross(values)
    both = swap_core(jnp.stack([values, cross]))
    return [values, both[0], cross, both[1]]


def gather_grp(values):
    return by_place(gather_near(values))


def gather_tokens(values, bit):
    half = values.shape[0] // 2
    cross = swap_cross(values)
    over = swap_blk(values, bit)
    first = swap_blk(cross[:half], bit)
    second = swap_cross(over[half:])
    chip = jnp.concatenate([values, cross, over, first, second])
    return jnp.concatenate([chip, swap_core(chip)])


def angles_of(position):
    half = HD // 2
    freqs = ROPE_BASE ** (-2.0 * jnp.arange(half, dtype=jnp.float32) / HD)
    return position.astype(jnp.float32)[:, None] * freqs[None, :]


def rotate_by(values, cosine, sine):
    half = HD // 2
    first_half = values[..., :half]
    second_half = values[..., half:]
    return jnp.concatenate(
        [first_half * cosine - second_half * sine, second_half * cosine + first_half * sine],
        axis=-1,
    )


def after(values, anchor):
    return lax.optimization_barrier((values, anchor))[0]


def gather_step(values, done, bit):
    other = swap_blk(values, bit)
    mine = blk_bit(bit)
    axis = sum(1 for d in done if d > bit)
    return jnp.stack(
        [jnp.where(mine, other, values), jnp.where(mine, values, other)], axis=axis
    )


def gather_near_stacked(values):
    both = jnp.stack([values, swap_cross(values)])
    return [both, swap_core(both)]


def ring_groups(count):
    return [[g * count + b for b in ring_order(count)] for g in range(4)]


def gather_ring(values):
    count = lax.axis_size("blk")
    return lax.all_gather(values, ("grp", "blk"), axis=0, axis_index_groups=ring_groups(count))


def exchange_near(parts):
    cross = swap_cross(jnp.stack([parts[2], parts[3]]))
    core = swap_core(jnp.stack([parts[1], cross[1]]))
    return [parts[0], core[0], cross[0], core[1]]


def on_device(
    tokens,
    cotangent,
    segment_ids,
    position_ids,
    w_attend,
    w_out,
    w_gate,
    w_up,
    w_down,
    small_params,
    first_attend,
    first_out,
    first_gate,
    first_up,
    first_down,
    first_small,
    second_attend,
    second_out,
    second_gate,
    second_up,
    second_down,
    second_small,
):
    rows_here, block_len = tokens.shape[:2]
    blk_count = lax.axis_size("blk")
    seq_len = block_len * blk_count
    token_count = rows_here * block_len
    grp = lax.axis_index("grp")
    blk = lax.axis_index("blk")
    cross_id, core_id = grp // 2, grp % 2
    strip_heads = H // 4
    strip_q = strip_heads * HD
    bits = bits_of(blk_count)
    team = blk_count // 4
    lows = [bit for bit in bits if bit < team]
    spread = [bits[0]] + lows
    low_shape = (2,) * len(lows)
    in_team = blk_bit(team).astype(jnp.int32)
    weight_rows = w_gate.shape[0]
    ff_block = w_down.shape[0]
    quarter = ff_block // 4
    widths = [size * blk_count // 2 for at, size in halves_of(quarter)]
    chip_rows = 4 * token_count
    half = token_count // 2

    ids = jnp.stack([grp, in_team])
    flat_low = tokens.reshape(token_count, D)
    dy_low = cotangent.reshape(token_count, D)
    positions = position_ids.reshape(token_count)
    kv_at = HQD + HD * cross_id + KVD * core_id
    strip_local = low(
        jnp.concatenate(
            [
                lax.dynamic_slice_in_dim(w_attend, strip_q * grp, strip_q, 1),
                lax.dynamic_slice_in_dim(w_attend, kv_at, HD, 1),
            ],
            axis=1,
        )
    )
    small_count = small_params.shape[0]
    small_send = jnp.concatenate([low(small_params), low(segment_ids.reshape(token_count))])
    strip_wide = strip_q + HD
    small_send = jnp.pad(small_send, (0, -small_send.shape[0] % (16 * strip_wide)))
    strip_local = jnp.concatenate([strip_local, small_send.reshape(-1, strip_wide)])
    ring = ring_order(blk_count)
    strip_ring = gather_ring(strip_local)
    small_ring = strip_ring[:, weight_rows:].reshape(blk_count, -1)[:, small_count : small_count + token_count]
    small_all = jnp.stack([small_ring[ring.index(b)] for b in range(blk_count)])
    digits = low(jnp.stack([positions // 64, positions % 64], axis=1))
    digits = jnp.pad(digits, ((0, 0), (0, HD - 2)))
    token_send = jnp.concatenate([flat_low, digits], axis=1)
    picked_a, picked_b = pick_columns(ids, w_gate, w_up, blk_count)
    got_a = swap_blk(picked_a[1], team)
    dy_cross = swap_cross(after(dy_low, picked_a))
    dy_over = swap_blk(after(dy_low, strip_ring), team)
    token_cross = after(swap_cross(token_send), (picked_a, strip_ring, got_a, dy_cross))

    def place(values, other, done, bit, lead=0):
        mine = blk_bit(bit)
        axis = lead + sum(1 for d in done if d > bit)
        return jnp.stack(
            [jnp.where(mine, other, values), jnp.where(mine, values, other)], axis=axis
        )

    mine_team = blk_bit(team)
    (low_first, size_first), (low_second, size_second) = halves_of(quarter)

    def team_pair(mine, got):
        return jnp.stack(
            [jnp.where(mine_team, got, mine), jnp.where(mine_team, mine, got)], axis=1
        )

    out_local = low(lax.dynamic_slice_in_dim(w_out, strip_q * grp, strip_q, 1))
    out_ring = gather_ring(after(out_local, strip_ring))
    down_here = low(lax.dynamic_slice_in_dim(w_down, quarter * grp, quarter, 0))
    token_core = swap_core(jnp.stack([token_send, token_cross]))
    freqs = ROPE_BASE ** (-2.0 * jnp.arange(HD // 2, dtype=jnp.float32) / HD)
    freqs = jnp.concatenate([freqs, freqs])[None]
    mixed_own, mixed_core, mixed_far, near_one, strip, vector = mix(
        ids, token_send, token_cross, token_core, strip_ring, freqs, blk_count, weight_rows, small_count
    )
    vector = vector[0]
    gain_one = vector[:D]
    gain_two = vector[D : 2 * D]
    seg_all = small_all.astype(jnp.int32)
    seg_all = seg_all.reshape(blk_count, rows_here, block_len)
    seg_key = jnp.broadcast_to(
        seg_all.transpose(1, 0, 2).reshape(rows_here, seq_len)[:, :, None], (rows_here, seq_len, HD)
    )
    seg_query = jnp.broadcast_to(segment_ids[:, None, :], (rows_here, 8, block_len))
    first_blk = jnp.sum((seg_all[:, :, -1] < segment_ids[None, :, 0]).astype(jnp.int32), axis=0)
    attend_ids = jnp.concatenate([blk[None], first_blk])

    mixed_cross = swap_cross(mixed_far)
    mixed_core = swap_core(jnp.stack([mixed_core, mixed_cross[1]]))
    pair_a = team_pair(picked_a[0], after(got_a, mixed_own))
    pair_a_got = swap_blk(pair_a, bits[0])
    mixed_core = after(mixed_core, (pair_a_got, dy_over))
    down_got = swap_blk(after(down_here, mixed_own), bits[0])
    query, packed_kv = pack(ids, mixed_own, mixed_cross, mixed_core)
    key_value = packed_kv.reshape(rows_here, block_len, 2 * KVD)
    kv_all = gather_ring(key_value)

    teams = [
        [g * blk_count + (i | t) for g in range(4) for t in (0, team)]
        for i in range(blk_count)
        if not i & team
    ]
    order = jnp.stack(
        [
            (grp ^ (2 * (i & 1) + (i >> 2))) * 2 + (in_team ^ ((i >> 1) & 1))
            for i in range(8)
        ]
    )

    peers = [[i for i in range(blk_count) if (i & team) == t] for t in (0, team)]

    def lows_of(values, done, lead=0, anchor=None):
        for bit in lows:
            got = swap_blk(values, bit)
            if anchor is not None:
                got = after(got, anchor)
            values = place(values, got, done, bit, lead)
            done = done + [bit]
        return values

    got_b = swap_blk(after(picked_b[1], mixed_own), team)
    pair_a = place(pair_a, after(pair_a_got, packed_kv), [team], bits[0], 1)
    pair_y_got = swap_blk(pair_a, lows[0])
    got_b, down_got = after((got_b, down_got), kv_all)
    kv_all = after(kv_all, (got_b, down_got, pair_y_got))
    down_here = place(down_here, down_got, [], bits[0])
    down_here = lows_of(down_here, [bits[0]]).reshape(2 * blk_count // 4, quarter, D)
    dy_first = swap_blk(dy_cross[:half], team)
    dy_second = swap_cross(dy_over[half:])
    dy_chip = jnp.concatenate([dy_low, dy_cross, dy_over, dy_first, dy_second])
    dy_team = jnp.concatenate([dy_chip, swap_core(dy_chip)])
    pair_b = team_pair(picked_b[0], after(got_b, kv_all))
    pair_b_got = swap_blk(pair_b, bits[0])
    out_ring = after(out_ring, packed_kv)
    out_strip = jnp.concatenate([out_ring[ring.index(b)] for b in range(blk_count)])
    out_cross = swap_cross(out_strip)
    out_core = swap_core(jnp.stack([out_strip, after(out_cross, kv_all)]))
    out_full = jnp.concatenate(by_place([out_strip, out_core[0], out_cross, out_core[1]]), axis=1)

    att_in, lse = attend(attend_ids, query, kv_all, seg_key, seg_query, block_len)
    flat = wide(flat_low)
    resid = flat + jnp.dot(att_in, out_full, preferred_element_type=jnp.float32)
    h_two = low(norm_apply(resid, gain_two))
    pair_a = place(pair_a, after(pair_y_got, h_two), [bits[0], team], lows[0], 1)
    for i in range(1, len(lows)):
        done = [bits[0], team] + lows[:i]
        pair_a = place(pair_a, swap_blk(pair_a, lows[i]), done, lows[i], 1)
    gate_up_a = pair_a.reshape(2, D, -1)
    pair_b_got = after(pair_b_got, h_two)
    down_a = down_here[:, :size_first].reshape(widths[0], D)
    down_b = down_here[:, size_first:].reshape(widths[1], D)
    h_team = lax.all_gather(h_two, ("grp", "blk"), axis=0, tiled=True, axis_index_groups=teams)
    pair_b_got = after(pair_b_got, (h_two, gate_up_a))
    pair_b = place(pair_b, pair_b_got, [team], bits[0], 1)
    h_team = after(h_team, (gate_up_a, pair_b, dy_team))
    hidden_a, d_gate_a, d_up_a, *part_a = middle(order, h_team, dy_team, gate_up_a, down_a)
    gate_up_b = lows_of(pair_b, [bits[0], team], 1, hidden_a).reshape(2, D, -1)
    down_grad_a = down_grad(after(hidden_a, gate_up_b), dy_team)
    down_share_a = lax.psum_scatter(
        down_grad_a, "blk", scatter_dimension=0, axis_index_groups=peers, tiled=True
    )
    column_grad_a = two_grads(h_team, d_gate_a, d_up_a)

    def part_sent(values, axis, bit):
        mine = blk_bit(bit).astype(jnp.int32)
        keep = lax.dynamic_index_in_dim(values, mine, axis, keepdims=False)
        send = lax.dynamic_index_in_dim(values, 1 - mine, axis, keepdims=False)
        return keep, swap_blk(send, bit)

    def part_sum(keep, got):
        return low(wide(keep) + wide(got))

    def columns_first(grad):
        grad = grad.reshape((2, 2, 2) + low_shape + (weight_rows, -1))
        return part_sent(grad, 2 + len(lows), lows[-1])

    def columns_mid(keep, got):
        values = part_sum(keep, got)
        for i in range(len(lows) - 2, -1, -1):
            values = part_sum(*part_sent(values, 3 + i, lows[i]))
        return values

    def columns_third(keep, got):
        values = part_sum(keep, got)
        mine = lax.dynamic_index_in_dim(values, in_team, 1, keepdims=False)
        send = lax.dynamic_index_in_dim(values, 1 - in_team, 1, keepdims=False)
        return values, (mine, swap_blk(send, team))

    def rows_second(keep, got):
        values = part_sum(keep, got)
        for i in range(len(lows) - 2, -1, -1):
            values = part_sum(*part_sent(values, 1 + i, lows[i]))
        return part_sent(values, 0, bits[0])

    def columns_last(mine, got):
        return jnp.stack(
            [jnp.where(mine_team, got, mine), jnp.where(mine_team, mine, got)], axis=1
        )

    first_a = columns_first(column_grad_a)
    hidden_b, d_gate_b, d_up_b, d_here, d_there = middle(
        order, after(h_team, (column_grad_a, down_grad_a)), dy_team, gate_up_b, down_b, part_a
    )

    def chip_sum(values, came):
        return low(wide(values) + wide(came))

    def scatter_far(chip):
        far = chip[3 * token_count :]
        return swap_blk(far[:half], team), swap_cross(far[half:])

    def scatter_near(chip, first, second):
        cross, over = (chip[token_count * i : token_count * (i + 1)] for i in (1, 2))
        cross = jnp.concatenate([low(wide(cross[:half]) + wide(first)), cross[half:]])
        over = jnp.concatenate([over[:half], low(wide(over[half:]) + wide(second))])
        return swap_cross(cross), swap_blk(over, team)

    near_att_cross = swap_cross(after(att_in, hidden_a))
    d_there = after(d_there, (first_a[1], down_share_a, near_att_cross))
    d_came = swap_core(d_there)
    down_grad_b = down_grad(hidden_b, dy_team)
    rows_b = part_sent(
        down_grad_b.reshape((2,) + low_shape + (size_second, D)), len(lows), lows[-1]
    )
    mid_a = columns_mid(*after(first_a, d_came))
    second_a = part_sent(mid_a, 1, bits[0])
    d_chip = chip_sum(d_here, after(d_came, down_grad_b))
    d_far = scatter_far(d_chip)
    column_grad_b = two_grads(h_team, *after((d_gate_b, d_up_b), d_chip))
    first_b = columns_first(column_grad_b)
    d_far = after(d_far, column_grad_b)
    d_cross, d_over = scatter_near(d_chip, *d_far)
    out_part, out_there = down(*after((hidden_a, hidden_b), d_far), down_a, down_b, token_count)
    out_came = swap_core(out_there)
    d_cross, d_over = after((d_cross, d_over), out_part)
    d_htwo = wide(d_chip[:token_count]) + wide(d_cross) + wide(d_over)

    norm_value_two, norm_back_two = jax.vjp(norm_apply, resid, gain_two)
    d_resid_norm, grad_gain_two = norm_back_two(d_htwo)
    d_resid = wide(dy_low) + d_resid_norm
    d_att = low(d_resid)
    rows_b = rows_second(*after(rows_b, d_att))

    d_attended = low(right_transposed(d_att, out_full))
    own_angles = angles_of(positions)
    cosine, sine = jnp.cos(own_angles), jnp.sin(own_angles)
    d_query, dkv = attend_back(
        attend_ids,
        query,
        kv_all,
        seg_key,
        seg_query,
        att_in,
        d_attended,
        lse,
        jnp.concatenate([cosine, cosine], axis=1),
        jnp.concatenate([sine, sine], axis=1),
        block_len,
    )
    dkv = lax.psum_scatter(
        dkv.reshape(blk_count * token_count, 2 * KVD),
        ("grp", "blk"),
        scatter_dimension=0,
        axis_index_groups=ring_groups(blk_count),
        tiled=True,
    )
    down_share_b = part_sum(*after(rows_b, d_query))
    sum_a, third_a = columns_third(*after(second_a, d_att))

    def to_strips(parts):
        return jnp.concatenate(exchange_near(by_place(parts)))

    near_dq = to_strips([d_query[:, strip_q * k : strip_q * (k + 1)] for k in range(4)])
    block_shape = (2,) * len(bits) + (weight_rows, -1)
    query_grad = low(left_product(near_one, near_dq)).reshape(block_shape)
    steps_query = part_sent(query_grad, len(bits) - 1, bits[-1])
    second_b = part_sent(columns_mid(*after(first_b, d_query)), 1, bits[0])
    dkv = after(dkv, down_share_b)
    own_part, core_part, far_part, bias_kv = turn_dkv(
        ids, dkv, jnp.concatenate([cosine, cosine], axis=1), jnp.concatenate([sine, sine], axis=1)
    )
    bias_q = jnp.sum(wide(d_query), axis=0)
    d_key = own_part
    cross_part = swap_cross(far_part)
    near_a = gather_near_stacked(columns_last(*after(third_a, own_part)))
    core_part = swap_core(jnp.stack([core_part, cross_part[1]]))
    kv_grad, hone_here, hone_there = make_kv_grad(
        blk_count,
        weight_rows,
        small_count,
        own_part,
        cross_part,
        core_part,
        near_dq,
        near_one,
        token_send,
        token_cross,
        token_core,
        strip,
        grad_gain_two[None],
        bias_q[None],
        bias_kv,
    )
    vector_rows = -(-small_count // HD)
    kv_grad = kv_grad.reshape((2,) * len(bits) + kv_grad.shape[1:])
    steps_kv = part_sent(kv_grad, len(bits) - 1, bits[-1])
    share_down = after(jnp.concatenate([down_share_a, down_share_b]), dkv)
    grad_down = lax.all_gather(share_down, "grp", axis=0, tiled=True)
    marks = [hone_there]
    for i in range(len(bits) - 2, -1, -1):
        kv_sum = part_sum(*steps_kv)
        steps_kv = part_sent(kv_sum, i, bits[i])
        marks.append(kv_sum)
    for n, i in enumerate(range(len(bits) - 2, -1, -1)):
        steps_query = part_sent(part_sum(*after(steps_query, marks[n + 1])), i, bits[i])
    sum_b, third_b = columns_third(*after(second_b, marks[-1]))
    share_kv_all = wide(steps_kv[0]) + wide(steps_kv[1])
    share_kv = low(share_kv_all[:weight_rows])
    vector_part = share_kv_all[weight_rows : weight_rows + vector_rows]
    share_query = part_sum(*after(steps_query, marks[-1]))
    near_att = swap_core(jnp.stack([att_in, near_att_cross]))
    near_att = jnp.concatenate([att_in, near_att[0], near_att_cross, near_att[1]])
    near_datt = to_strips([d_att[:, strip_q * k : strip_q * (k + 1)] for k in range(4)])
    out_grad = low(left_product(near_att, after(near_datt, d_attended))).reshape(block_shape)
    steps_out = part_sent(out_grad, len(bits) - 1, bits[-1])
    for n, i in enumerate(range(len(bits) - 2, -1, -1)):
        steps_out = part_sent(part_sum(*after(steps_out, marks[n + 1])), i, bits[i])
    share_out = part_sum(*after(steps_out, marks[-1]))

    other = wide(swap_core(hone_there))
    d_hone = wide(hone_here[:token_count]) + other[:token_count]
    d_hone_send = low(wide(hone_here[token_count:]) + other[token_count:])
    d_hone_cross = swap_cross(d_hone_send)
    square_sum = square_total(
        [
            wide(s)
            for s in (share_query, share_kv, share_out, sum_a, sum_b, share_down)
        ]
    )
    packed = jnp.concatenate([vector_part, jnp.full((8, HD), square_sum)])
    packed = after(packed, (d_hone_send, d_hone))
    packed = packed + swap_cross(packed)
    packed = packed + swap_core(packed)
    grad_out = jnp.concatenate(gather_grp(after(share_out, packed)), axis=1)
    query_parts = gather_grp(after(share_query, packed))
    key_parts = gather_grp(after(share_kv, packed))
    grad_attend = jnp.concatenate(query_parts + [key_parts[k] for k in (0, 2, 1, 3)], axis=1)

    share_vector = packed[:vector_rows].reshape(-1)[:small_count]
    square_sum = packed[vector_rows:] + jnp.sum(share_vector * share_vector)
    square_sum = after(square_sum, third_b[1])
    for bit in bits:
        square_sum = square_sum + swap_blk(square_sum, bit)
    grad_norm = jnp.sqrt(square_sum[0, 0])
    factor = jnp.minimum(1.0, CLIP_NORM / (grad_norm + 1e-06))
    out_chip = chip_sum(out_part, after(out_came, marks[1]))
    out_far = scatter_far(out_chip)
    factor = after(factor, (out_chip, near_a))

    new_first_attend, new_second_attend, new_attend = adam_step(
        w_attend, factor * wide(grad_attend), first_attend, second_attend, RATE_ATTEND, WEIGHT_DECAY
    )
    new_first_out, new_second_out, new_out = adam_step(
        w_out, factor * wide(grad_out), first_out, second_out, RATE_OUT, WEIGHT_DECAY
    )
    new_first_down, new_second_down, new_down = adam_step(
        w_down, factor * wide(grad_down), first_down, second_down, RATE_DOWN, WEIGHT_DECAY
    )
    own_b = columns_last(*third_b)
    cross_b = after(swap_cross(own_b), new_down)
    near_b = jnp.stack([own_b, cross_b])
    near_b = [near_b, swap_core(near_b)]
    new_first_gate, new_second_gate, new_gate = adam_columns(
        0, ids, factor[None], near_a, near_b, w_gate, first_gate, second_gate, blk_count, RATE_GATE, WEIGHT_DECAY
    )
    new_first_up, new_second_up, new_up = adam_columns(
        1, ids, factor[None], near_a, near_b, w_up, first_up, second_up, blk_count, RATE_GATE, WEIGHT_DECAY
    )
    norm_value_one, norm_back_one = jax.vjp(norm_apply, flat, gain_one)
    d_hone = after(d_hone + wide(after(d_hone_cross, new_gate)), new_gate)
    d_flat_norm, unused_gain = norm_back_one(d_hone)
    grad_tokens = low(d_resid + d_flat_norm)

    new_first_small, new_second_small, new_small = adam_step(
        small_params, factor * share_vector, first_small, second_small, RATE_VECTOR, 0.0
    )

    out_near = after(scatter_near(out_chip, *after(out_far, factor)), (new_gate, new_up))
    out_tokens = low(resid + wide(out_chip[:token_count]) + wide(out_near[0]) + wide(out_near[1]))
    return (
        out_tokens.reshape(rows_here, block_len, D),
        grad_tokens.reshape(rows_here, block_len, D),
        grad_norm,
        new_first_attend,
        new_second_attend,
        new_attend,
        new_first_out,
        new_second_out,
        new_out,
        new_first_gate,
        new_second_gate,
        new_gate,
        new_first_up,
        new_second_up,
        new_up,
        new_first_down,
        new_second_down,
        new_down,
        new_first_small,
        new_second_small,
        new_small,
    )


def solution(mesh):
    placed = (
        P("grp", "blk", None),
        P("grp", "blk", None),
        P("grp", "blk"),
        P("grp", "blk"),
        P("blk", None),
        P("blk", None),
        P("blk", None),
        P("blk", None),
        P("blk", None),
        P("blk"),
        P("blk", None),
        P("blk", None),
        P("blk", None),
        P("blk", None),
        P("blk", None),
        P("blk"),
        P("blk", None),
        P("blk", None),
        P("blk", None),
        P("blk", None),
        P("blk", None),
        P("blk"),
    )
    return jax.shard_map(
        on_device,
        mesh=mesh,
        in_specs=placed,
        out_specs=(
            P("grp", "blk", None),
            P("grp", "blk", None),
            P(),
            P("blk", None),
            P("blk", None),
            P("blk", None),
            P("blk", None),
            P("blk", None),
            P("blk", None),
            P("blk", None),
            P("blk", None),
            P("blk", None),
            P("blk", None),
            P("blk", None),
            P("blk", None),
            P("blk", None),
            P("blk", None),
            P("blk", None),
            P("blk"),
            P("blk"),
            P("blk"),
        ),
        check_vma=False,
    )
```

```python
import functools

import jax
import jax.numpy as jnp
from jax import lax
from jax.experimental import pallas as pl
from jax.experimental.pallas import tpu as pltpu
from jax.sharding import PartitionSpec as P

D = 1536
FF = 8960
H = 12
KVH = 2
HD = 128
STEP = 10
HQD = 1536
KVD = 256


NORM_EPS = 1e-06
ROPE_BASE = 10000.0
CLIP_NORM = 1.0
BETA_FIRST = 0.9
BETA_SECOND = 0.95
ADAM_EPS = 1e-08
WEIGHT_DECAY = 0.1
RATE_ATTEND = 0.06
RATE_OUT = 0.5
RATE_GATE = 0.06
RATE_DOWN = 0.03
RATE_VECTOR = 0.5
NEG_LARGE = -1e30
LOG2E = 1.4426950408889634
VMEM = 48 * 1024 * 1024
SMALL_COST = pl.CostEstimate(flops=1000, bytes_accessed=1000, transcendentals=0)


def norm_apply(values, gain):
    return values * lax.rsqrt(jnp.mean(values * values, axis=-1, keepdims=True) + NORM_EPS) * gain


def swish_product(gate, up_proj):
    return jax.nn.silu(gate) * up_proj


def left_product(left_side, right_side):
    return lax.dot_general(
        left_side, right_side, (((0,), (0,)), ((), ())), preferred_element_type=jnp.float32
    )


def right_transposed(left_side, right_side):
    return lax.dot_general(
        left_side, right_side, (((1,), (1,)), ((), ())), preferred_element_type=jnp.float32
    )


def square_total(arrays):
    return sum((jnp.sum(member * member) for member in arrays))


def adam_step(weight, grad, first, second, rate, decay):
    first_new = BETA_FIRST * first + (1.0 - BETA_FIRST) * grad
    second_new = BETA_SECOND * second + (1.0 - BETA_SECOND) * grad * grad
    first_hat = first_new / (1.0 - BETA_FIRST**STEP)
    second_hat = second_new / (1.0 - BETA_SECOND**STEP)
    weight_new = weight - rate * (first_hat / (jnp.sqrt(second_hat) + ADAM_EPS) + decay * weight)
    return (first_new, second_new, weight_new)


def ring_order(count):
    return list(range(0, count, 2)) + list(range(count - 1, 0, -2))


def halves_of(quarter):
    first = quarter * 16 // 35
    return ((0, first), (first, quarter - first))


def pick_body(blk_count, ids, gate_ref, up_ref, *out_refs):
    quarter = FF // blk_count // 4
    per = blk_count // 4
    for k in range(4):

        @pl.when(ids[0] == k)
        def _(k=k):
            for (at, size), out_ref in zip(halves_of(quarter), out_refs):
                for which, src in enumerate((gate_ref, up_ref)):
                    for bit in range(2):
                        parts = []
                        for high in range(2):
                            for small in range(per):
                                begin = (((high * 2 + bit) * per + small) * 4 + k) * quarter + at
                                parts.append(src[:, begin : begin + size])
                        out_ref[ids[1] ^ bit, which] = jnp.concatenate(parts, axis=1).astype(
                            jnp.bfloat16
                        )


def pick_columns(ids, gate, up, blk_count):
    rows = gate.shape[0]
    step = 48 if rows % 48 == 0 else rows
    widths = [size * blk_count // 2 for at, size in halves_of(FF // blk_count // 4)]
    spec = pl.BlockSpec((step, FF), lambda i, ids: (i, 0))
    return pl.pallas_call(
        functools.partial(pick_body, blk_count),
        grid_spec=pltpu.PrefetchScalarGridSpec(
            num_scalar_prefetch=1,
            grid=(rows // step,),
            in_specs=[spec, spec],
            out_specs=[pl.BlockSpec((2, 2, step, w), lambda i, ids: (0, 0, i, 0)) for w in widths],
        ),
        out_shape=[jax.ShapeDtypeStruct((2, 2, rows, w), jnp.bfloat16) for w in widths],
        compiler_params=pltpu.CompilerParams(vmem_limit_bytes=VMEM),
        cost_estimate=SMALL_COST,
        name="pick_columns",
    )(ids, gate, up)


def adam_body(blk_count, rate, decay, ids, factor_ref, first_ref, first_far_ref, second_ref, second_far_ref, w_ref, m_ref, v_ref, m_out, v_out, w_out):
    per = blk_count // 4
    sizes = [size for at, size in halves_of(FF // blk_count // 4)]
    grads = []
    for near_ref, far_ref in ((first_ref, first_far_ref), (second_ref, second_far_ref)):
        by_grp = []
        for k in range(4):
            away = ids[0] ^ k
            bits_of_k = []
            for bit in range(2):
                near = near_ref[away >> 1, bit].astype(jnp.float32)
                far = far_ref[away >> 1, bit].astype(jnp.float32)
                bits_of_k.append(jnp.where((away & 1) == 1, far, near))
            by_grp.append(bits_of_k)
        grads.append(by_grp)
    parts = []
    for high in range(2):
        for bit in range(2):
            for small in range(per):
                place = high * per + small
                for k in range(4):
                    for part, size in zip(grads, sizes):
                        parts.append(part[k][bit][:, place * size : (place + 1) * size])
    grad = jnp.concatenate(parts, axis=1) * factor_ref[0]
    m, v, w = adam_step(w_ref[...], grad, m_ref[...], v_ref[...], rate, decay)
    m_out[...] = m
    v_out[...] = v
    w_out[...] = w


def adam_columns(which, ids, factor, first, second, w, m, v, blk_count, rate, decay):
    rows = w.shape[0]
    step = 32 if rows % 32 == 0 else rows
    spec = pl.BlockSpec((step, FF), lambda i, ids: (i, 0))
    shape = jax.ShapeDtypeStruct((rows, FF), jnp.float32)
    grads = [
        pl.BlockSpec((2, None, 2, step, g.shape[-1]), lambda i, ids: (0, which, 0, i, 0))
        for g in first + second
    ]
    return pl.pallas_call(
        functools.partial(adam_body, blk_count, rate, decay),
        grid_spec=pltpu.PrefetchScalarGridSpec(
            num_scalar_prefetch=1,
            grid=(rows // step,),
            in_specs=[pl.BlockSpec(memory_space=pltpu.SMEM)] + grads + [spec, spec, spec],
            out_specs=[spec, spec, spec],
        ),
        out_shape=[shape] * 3,
        compiler_params=pltpu.CompilerParams(vmem_limit_bytes=VMEM),
        cost_estimate=SMALL_COST,
        name="adam_columns",
    )(ids, factor, *first, *second, w, m, v)


def nt(a, b, **kw):
    return lax.dot_general(a, b, (((1,), (1,)), ((), ())), preferred_element_type=jnp.float32, **kw)

def tn(a, b, **kw):
    return lax.dot_general(a, b, (((0,), (0,)), ((), ())), preferred_element_type=jnp.float32, **kw)

def stack_heads(ref, kvh, group):
    return jnp.concatenate([ref[:, HD * (kvh * group + i): HD * (kvh * group + i + 1)] for i in range(group)], axis=0)

def hidden_from(seg_key_ref, seg_query_ref, first, chunk, block_len, blk):
    key = first + lax.broadcasted_iota(jnp.int32, (chunk, block_len), 0)
    query = blk * block_len + lax.broadcasted_iota(jnp.int32, (chunk, block_len), 1)
    seg_key = seg_key_ref[pl.ds(first, chunk), :]
    counts = jnp.logical_and(key <= query, seg_key == seg_query_ref[0:1, :])
    return jnp.where(counts, 0.0, NEG_LARGE)

def ring_pair(ref, c, at):
    return jnp.concatenate(
        [ref[c, :, at : at + HD], ref[ref.shape[0] - 1 - c, :, at : at + HD]], axis=0
    )


def attend_body(chunk, ids, q_ref, k_ref, v_ref, seg_key_ref, seg_query_ref, o_ref, lse_ref, m_s, l_s, acc_s):
    block_len = q_ref.shape[0]
    group = H // KVH
    row = pl.program_id(0)
    per = chunk // block_len
    scale = HD ** (-0.5) * LOG2E
    start = ids[1 + row] // per
    stop = ids[0] // per + 1
    for kvh in range(KVH):
        q = stack_heads(q_ref, kvh, group)
        m_s[...] = jnp.full_like(m_s, NEG_LARGE)
        l_s[...] = jnp.zeros_like(l_s)
        acc_s[...] = jnp.zeros_like(acc_s)

        def step(c, carry):
            keys = ring_pair(k_ref, c, HD * kvh)
            vals = ring_pair(v_ref, c, HD * kvh)
            bias = hidden_from(seg_key_ref, seg_query_ref, c * chunk, chunk, block_len, ids[0])
            s = nt(keys, q) * scale + jnp.concatenate([bias] * group, axis=1)
            old = m_s[0:1, :]
            new = jnp.maximum(old, jnp.max(s, axis=0, keepdims=True))
            p = jnp.exp2(s - new)
            fade = jnp.exp2(old - new)
            l_s[0:1, :] = l_s[0:1, :] * fade + jnp.sum(p, axis=0, keepdims=True)
            acc_s[...] = acc_s[...] * fade + tn(vals, p.astype(jnp.bfloat16))
            m_s[0:1, :] = new
            return carry

        lax.fori_loop(start, stop, step, 0)
        total = l_s[0:1, :]
        out = (acc_s[...] * (1.0 / total)).T
        for i in range(group):
            o_ref[:, HD * (kvh * group + i): HD * (kvh * group + i + 1)] = out[block_len * i: block_len * (i + 1), :].astype(jnp.bfloat16)
        lse_ref[kvh] = jnp.broadcast_to(m_s[0:1, :] + jnp.log2(total), (8, group * block_len))

def attend(ids, q, kv, seg_key, seg_query, block_len):
    blk_count, rows = kv.shape[:2]
    group = H // KVH
    chunk = 2 * block_len
    many = group * block_len
    return pl.pallas_call(
        functools.partial(attend_body, chunk),
        grid_spec=pltpu.PrefetchScalarGridSpec(
            num_scalar_prefetch=1, grid=(rows,),
            in_specs=[
                pl.BlockSpec((block_len, HQD), lambda r, ids: (r, 0)),
                pl.BlockSpec((blk_count, None, block_len, KVD), lambda r, ids: (0, r, 0, 0)),
                pl.BlockSpec((blk_count, None, block_len, KVD), lambda r, ids: (0, r, 0, 1)),
                pl.BlockSpec((None, blk_count * block_len, HD), lambda r, ids: (r, 0, 0)),
                pl.BlockSpec((None, 8, block_len), lambda r, ids: (r, 0, 0)),
            ],
            out_specs=[
                pl.BlockSpec((block_len, HQD), lambda r, ids: (r, 0)),
                pl.BlockSpec((None, KVH, 8, many), lambda r, ids: (r, 0, 0, 0)),
            ],
            scratch_shapes=[pltpu.VMEM((8, many), jnp.float32), pltpu.VMEM((8, many), jnp.float32), pltpu.VMEM((HD, many), jnp.float32)]),
        out_shape=[
            jax.ShapeDtypeStruct((rows * block_len, HQD), jnp.bfloat16),
            jax.ShapeDtypeStruct((rows, KVH, 8, many), jnp.float32),
        ],
        compiler_params=pltpu.CompilerParams(vmem_limit_bytes=VMEM),
        cost_estimate=SMALL_COST,
        name="attend",
    )(ids, q, kv, kv, seg_key, seg_query)

def turn_back(u, cosine, sine):
    lane = lax.broadcasted_iota(jnp.int32, u.shape, 1)
    other = pltpu.roll(u, HD // 2, 1)
    return u * cosine + jnp.where(lane < HD // 2, other, -other) * sine

def attend_back_body(chunk, ids, q_ref, k_ref, v_ref, seg_key_ref, seg_query_ref, o_ref, do_ref, lse_ref, cos_ref, sin_ref, dq_ref, dkv_ref, dq_s):
    block_len = q_ref.shape[0]
    group = H // KVH
    row = pl.program_id(0)
    per = chunk // block_len
    plain = HD ** (-0.5)
    scale = plain * LOG2E
    start = ids[1 + row] // per
    stop = ids[0] // per + 1
    dkv_ref[...] = jnp.zeros_like(dkv_ref)
    for kvh in range(KVH):
        q = stack_heads(q_ref, kvh, group)
        do = stack_heads(do_ref, kvh, group)
        o = stack_heads(o_ref, kvh, group)
        both = do.astype(jnp.float32) * o.astype(jnp.float32)
        delta = nt(jnp.ones((8, HD), jnp.float32), both, precision=lax.Precision.HIGHEST)[0:1, :]
        lse = lse_ref[kvh][0:1, :]
        dq_s[...] = jnp.zeros_like(dq_s)

        def step(c, carry):
            keys = ring_pair(k_ref, c, HD * kvh)
            vals = ring_pair(v_ref, c, HD * kvh)
            bias = hidden_from(seg_key_ref, seg_query_ref, c * chunk, chunk, block_len, ids[0])
            s = nt(keys, q) * scale + jnp.concatenate([bias] * group, axis=1)
            p = jnp.exp2(s - lse)
            dp = nt(vals, do)
            ds = (p * (dp - delta)).astype(jnp.bfloat16)
            dk = jnp.dot(ds, q, preferred_element_type=jnp.float32) * plain
            dv = jnp.dot(p.astype(jnp.bfloat16), do, preferred_element_type=jnp.float32)
            for at, part in ((HD * kvh, dk.astype(jnp.bfloat16)), (KVD + HD * kvh, dv.astype(jnp.bfloat16))):
                dkv_ref[c, :, at : at + HD] = part[:block_len]
                dkv_ref[dkv_ref.shape[0] - 1 - c, :, at : at + HD] = part[block_len:]
            dq_s[...] += tn(ds, keys)
            return carry

        lax.fori_loop(start, stop, step, 0)
        cosine, sine = cos_ref[...], sin_ref[...]
        for i in range(group):
            u = dq_s[block_len * i: block_len * (i + 1), :] * plain
            at = HD * (kvh * group + i)
            dq_ref[:, at: at + HD] = turn_back(u, cosine, sine).astype(jnp.bfloat16)

def attend_back(ids, q, kv, seg_key, seg_query, o, do, lse, cosine, sine, block_len):
    blk_count, rows = kv.shape[:2]
    group = H // KVH
    chunk = 2 * block_len
    many = group * block_len
    per_row = pl.BlockSpec((block_len, HQD), lambda r, ids: (r, 0))
    turn = pl.BlockSpec((block_len, HD), lambda r, ids: (r, 0))
    return pl.pallas_call(
        functools.partial(attend_back_body, chunk),
        grid_spec=pltpu.PrefetchScalarGridSpec(
            num_scalar_prefetch=1, grid=(rows,),
            in_specs=[
                per_row,
                pl.BlockSpec((blk_count, None, block_len, KVD), lambda r, ids: (0, r, 0, 0)),
                pl.BlockSpec((blk_count, None, block_len, KVD), lambda r, ids: (0, r, 0, 1)),
                pl.BlockSpec((None, blk_count * block_len, HD), lambda r, ids: (r, 0, 0)),
                pl.BlockSpec((None, 8, block_len), lambda r, ids: (r, 0, 0)),
                per_row, per_row,
                pl.BlockSpec((None, KVH, 8, many), lambda r, ids: (r, 0, 0, 0)),
                turn, turn,
            ],
            out_specs=[per_row, pl.BlockSpec((blk_count, None, block_len, 2 * KVD), lambda r, ids: (0, r, 0, 0))],
            scratch_shapes=[pltpu.VMEM((many, HD), jnp.float32)]),
        out_shape=[
            jax.ShapeDtypeStruct((rows * block_len, HQD), jnp.bfloat16),
            jax.ShapeDtypeStruct((blk_count, rows, block_len, 2 * KVD), jnp.bfloat16),
        ],
        compiler_params=pltpu.CompilerParams(vmem_limit_bytes=VMEM),
        cost_estimate=SMALL_COST,
        name="attend_back",
    )(ids, q, kv, kv, seg_key, seg_query, o, do, lse, cosine, sine)

def nn(a, b):
    return jnp.dot(a, b, preferred_element_type=jnp.float32)


def middle_body(add, order, h_ref, dy_ref, wg_ref, wu_ref, wd_ref, *refs):
    prev_refs = refs[:2] if add else None
    hid_ref, dg_ref, du_ref, dh_ref, dh_far_ref = refs[-5:]
    here = pl.program_id(0) < 4
    h = h_ref[...]
    gate = nn(h, wg_ref[...])
    up = nn(h, wu_ref[...])
    sig = 1.0 / (1.0 + jnp.exp(-gate))
    silu = gate * sig
    hid_ref[...] = (silu * up).astype(jnp.bfloat16)
    dhid = nt(dy_ref[...], wd_ref[...])
    dg = (dhid * up * sig * (1.0 + gate * (1.0 - sig))).astype(jnp.bfloat16)
    du = (dhid * silu).astype(jnp.bfloat16)
    dg_ref[...] = dg
    du_ref[...] = du
    dh = nt(dg, wg_ref[...]) + nt(du, wu_ref[...])
    if add:
        prev = jnp.where(here, prev_refs[0][...].astype(jnp.float32), prev_refs[1][...].astype(jnp.float32))
        dh = dh + prev
    dh = dh.astype(jnp.bfloat16)

    @pl.when(here)
    def _():
        dh_ref[...] = dh

    @pl.when(jnp.logical_not(here))
    def _():
        dh_far_ref[...] = dh


def middle(order, h, dy, gate_up, wd, prev=None):
    count = h.shape[0]
    step = count // order.shape[0]
    wide_here = wd.shape[0]
    row = pl.BlockSpec((step, D), lambda i, order: (i, 0))
    placed = pl.BlockSpec((step, D), lambda i, order: (order[i], 0))
    part = pl.BlockSpec((step, wide_here), lambda i, order: (i, 0))
    part_placed = pl.BlockSpec((step, wide_here), lambda i, order: (order[i], 0))
    once = pl.Buffered(1)
    extra = [] if prev is None else list(prev)
    near = pl.BlockSpec((step, D), lambda i, order: (jnp.minimum(i, 3), 0))
    far = pl.BlockSpec((step, D), lambda i, order: (jnp.maximum(i - 4, 0), 0))
    return pl.pallas_call(
        functools.partial(middle_body, prev is not None),
        grid_spec=pltpu.PrefetchScalarGridSpec(
            num_scalar_prefetch=1,
            grid=(count // step,),
            in_specs=[
                placed,
                row,
                pl.BlockSpec((None, D, wide_here), lambda i, order: (0, 0, 0), pipeline_mode=once),
                pl.BlockSpec((None, D, wide_here), lambda i, order: (1, 0, 0), pipeline_mode=once),
                pl.BlockSpec((wide_here, D), lambda i, order: (0, 0), pipeline_mode=once),
            ]
            + [near, far][: len(extra)],
            out_specs=[part, part_placed, part_placed, near, far],
        ),
        out_shape=[jax.ShapeDtypeStruct((count, wide_here), jnp.bfloat16)] * 3
        + [jax.ShapeDtypeStruct((count // 2, D), jnp.bfloat16)] * 2,
        compiler_params=pltpu.CompilerParams(vmem_limit_bytes=VMEM),
        cost_estimate=SMALL_COST,
        name="middle",
    )(order, h, dy, gate_up, gate_up, wd, *extra)


def two_grads_body(h_ref, a_ref, b_ref, out_ref):
    h = h_ref[...]
    out_ref[0] = tn(h, a_ref[...]).astype(jnp.bfloat16)
    out_ref[1] = tn(h, b_ref[...]).astype(jnp.bfloat16)


def two_grads(h, a, b, step=256):
    count = h.shape[0]
    wide_here = a.shape[1]
    whole = pl.BlockSpec(a.shape, lambda i: (0, 0), pipeline_mode=pl.Buffered(1))
    return pl.pallas_call(
        two_grads_body,
        grid=(D // step,),
        in_specs=[pl.BlockSpec((count, step), lambda i: (0, i)), whole, whole],
        out_specs=pl.BlockSpec((2, step, wide_here), lambda i: (0, i, 0)),
        out_shape=jax.ShapeDtypeStruct((2, D, wide_here), jnp.bfloat16),
        compiler_params=pltpu.CompilerParams(vmem_limit_bytes=VMEM),
        cost_estimate=SMALL_COST,
        name="two_grads",
    )(h, a, b)


def down_grad_body(hid_ref, dy_ref, g_ref):
    g_ref[...] = tn(hid_ref[...], dy_ref[...]).astype(jnp.bfloat16)

def down_grad(hid, dy, step=512):
    T, F = hid.shape
    D = dy.shape[1]
    return pl.pallas_call(down_grad_body, grid=(D // step,),
        in_specs=[pl.BlockSpec((T, F), lambda i: (0, 0), pipeline_mode=pl.Buffered(1)), pl.BlockSpec((T, step), lambda i: (0, i))],
        out_specs=pl.BlockSpec((F, step), lambda i: (0, i)),
        out_shape=jax.ShapeDtypeStruct((F, D), jnp.bfloat16),
        compiler_params=pltpu.CompilerParams(vmem_limit_bytes=VMEM),
        cost_estimate=SMALL_COST,
        name="down_grad")(hid, dy)

def down_body(hid_a_ref, hid_b_ref, wd_a_ref, wd_b_ref, o_ref, o_far_ref):
    out = nn(hid_a_ref[...], wd_a_ref[...]) + nn(hid_b_ref[...], wd_b_ref[...])
    out = out.astype(jnp.bfloat16)
    here = pl.program_id(0) < 4

    @pl.when(here)
    def _():
        o_ref[...] = out

    @pl.when(jnp.logical_not(here))
    def _():
        o_far_ref[...] = out


def down(hid_a, hid_b, wd_a, wd_b, step):
    count = hid_a.shape[0]

    def rows(array):
        return pl.BlockSpec((step, array.shape[1]), lambda i: (i, 0))

    def whole(array):
        return pl.BlockSpec(array.shape, lambda i: (0, 0), pipeline_mode=pl.Buffered(1))

    return pl.pallas_call(
        down_body,
        grid=(count // step,),
        in_specs=[rows(hid_a), rows(hid_b), whole(wd_a), whole(wd_b)],
        out_specs=[
            pl.BlockSpec((step, D), lambda i: (jnp.minimum(i, 3), 0)),
            pl.BlockSpec((step, D), lambda i: (jnp.maximum(i - 4, 0), 0)),
        ],
        out_shape=[jax.ShapeDtypeStruct((count // 2, D), jnp.bfloat16)] * 2,
        compiler_params=pltpu.CompilerParams(vmem_limit_bytes=VMEM),
        cost_estimate=SMALL_COST,
        name="down",
    )(hid_a, hid_b, wd_a, wd_b)


def turn(u, cosine, sine):
    lane = lax.broadcasted_iota(jnp.int32, u.shape, 1)
    other = pltpu.roll(u, HD // 2, 1)
    return u * cosine + jnp.where(lane < HD // 2, -other, other) * sine


def mix_body(
    blk_count, rows, small_count, ids, own_ref, cross_ref, core_ref, ring_ref, freq_ref,
    self_ref, near_ref, far_ref, one_ref, strip_ref, vector_ref,
):
    ring = ring_order(blk_count)
    wide_here = ring_ref.shape[-1]
    pieces = []
    for b in range(blk_count):
        at = ring.index(b)
        strip_ref[rows * b : rows * (b + 1)] = ring_ref[at, :rows]
        left = small_count
        line = rows
        while left > 0:
            size = min(left, wide_here)
            pieces.append(ring_ref[at, line : line + 1, :size].astype(jnp.float32))
            left -= size
            line += 1
    vector = jnp.concatenate(pieces, axis=1)
    vector_ref[...] = vector
    gain = vector[:, :D]
    grp = ids[0]
    strip_q = wide_here - HD
    bias = jnp.zeros((1, wide_here), jnp.float32)
    for k in range(4):
        kv_at = 2 * D + HQD + HD * (k // 2) + KVD * (k % 2)
        part = jnp.concatenate(
            [
                vector[:, 2 * D + strip_q * k : 2 * D + strip_q * (k + 1)],
                vector[:, kv_at : kv_at + HD],
            ],
            axis=1,
        )
        bias = bias + jnp.where(grp == k, part, 0.0)
    count = own_ref.shape[0]
    strip = strip_ref[...]
    for d in range(4):
        source = (own_ref[...], core_ref[0], cross_ref[...], core_ref[1])[d]
        x = source[:, :D].astype(jnp.float32)
        root = lax.rsqrt(jnp.mean(x * x, axis=1, keepdims=True) + NORM_EPS)
        one = (x * root * gain).astype(jnp.bfloat16)
        one_ref[count * d : count * (d + 1)] = one
        mixed = nn(one, strip) + bias
        digits = source[:, D : D + HD].astype(jnp.float32)
        position = 64.0 * digits[:, 0:1] + digits[:, 1:2]
        angles = position * freq_ref[...]
        cosine, sine = jnp.cos(angles), jnp.sin(angles)
        for i in range(wide_here // HD):
            c, s = cosine, sine
            if i == wide_here // HD - 1:
                c = jnp.where(grp % 2 == 1, 1.0, c)
                s = jnp.where(grp % 2 == 1, 0.0, s)
            at = HD * i
            out = turn(mixed[:, at : at + HD], c, s).astype(jnp.bfloat16)
            if d == 0:
                self_ref[:, at : at + HD] = out
            elif d == 1:
                near_ref[:, at : at + HD] = out
            else:
                far_ref[d - 2, :, at : at + HD] = out


def mix(ids, own, cross, core, ring, freq, blk_count, rows, small_count):
    count = own.shape[0]
    wide_here = ring.shape[-1]
    low16 = jnp.bfloat16
    return pl.pallas_call(
        functools.partial(mix_body, blk_count, rows, small_count),
        in_specs=[pl.BlockSpec(memory_space=pltpu.SMEM)] + [pl.BlockSpec(memory_space=pltpu.VMEM)] * 5,
        out_specs=[pl.BlockSpec(memory_space=pltpu.VMEM)] * 6,
        out_shape=[
            jax.ShapeDtypeStruct((count, wide_here), low16),
            jax.ShapeDtypeStruct((count, wide_here), low16),
            jax.ShapeDtypeStruct((2, count, wide_here), low16),
            jax.ShapeDtypeStruct((4 * count, D), low16),
            jax.ShapeDtypeStruct((D, wide_here), low16),
            jax.ShapeDtypeStruct((1, blk_count * small_count), jnp.float32),
        ],
        compiler_params=pltpu.CompilerParams(vmem_limit_bytes=VMEM),
        cost_estimate=SMALL_COST,
        name="mix",
    )(ids, own, cross, core, ring, freq)


def pack_body(ids, self_ref, cross_ref, core_ref, q_ref, kv_ref):
    strip_q = self_ref.shape[1] - HD
    for g in range(4):

        @pl.when(ids[0] == g)
        def _(g=g):
            for k in range(4):
                part = (self_ref[...], core_ref[0], cross_ref[0], core_ref[1])[g ^ k]
                q_ref[:, strip_q * k : strip_q * (k + 1)] = part[:, :strip_q]
                at = (k % 2) * KVD + (k // 2) * HD
                kv_ref[:, at : at + HD] = part[:, strip_q:]


def pack(ids, own, cross, core):
    count = own.shape[0]
    return pl.pallas_call(
        pack_body,
        in_specs=[pl.BlockSpec(memory_space=pltpu.SMEM)] + [pl.BlockSpec(memory_space=pltpu.VMEM)] * 3,
        out_specs=[pl.BlockSpec(memory_space=pltpu.VMEM)] * 2,
        out_shape=[
            jax.ShapeDtypeStruct((count, HQD), jnp.bfloat16),
            jax.ShapeDtypeStruct((count, 2 * KVD), jnp.bfloat16),
        ],
        compiler_params=pltpu.CompilerParams(vmem_limit_bytes=VMEM),
        cost_estimate=SMALL_COST,
        name="pack",
    )(ids, own, cross, core)


def turn_dkv_body(ids, dkv_ref, cos_ref, sin_ref, self_ref, near_ref, far_ref, sum_ref):
    items = []
    sums = [None] * 4
    for k in range(4):
        at = (k % 2) * KVD + (k // 2) * HD
        part = dkv_ref[:, at : at + HD]
        if k % 2 == 0:
            part = turn_back(part.astype(jnp.float32), cos_ref[...], sin_ref[...]).astype(jnp.bfloat16)
        items.append(part)
        sums[(k % 2) * 2 + k // 2] = jnp.sum(part.astype(jnp.float32), axis=0, keepdims=True)
    sum_ref[...] = jnp.concatenate(sums, axis=1)
    for g in range(4):

        @pl.when(ids[0] == g)
        def _(g=g):
            self_ref[...] = items[g]
            near_ref[...] = items[g ^ 1]
            far_ref[0] = items[g ^ 2]
            far_ref[1] = items[g ^ 3]


def turn_dkv(ids, dkv, cosine, sine):
    count = dkv.shape[0]
    return pl.pallas_call(
        turn_dkv_body,
        in_specs=[pl.BlockSpec(memory_space=pltpu.SMEM)] + [pl.BlockSpec(memory_space=pltpu.VMEM)] * 3,
        out_specs=[pl.BlockSpec(memory_space=pltpu.VMEM)] * 4,
        out_shape=[
            jax.ShapeDtypeStruct((count, HD), jnp.bfloat16),
            jax.ShapeDtypeStruct((count, HD), jnp.bfloat16),
            jax.ShapeDtypeStruct((2, count, HD), jnp.bfloat16),
            jax.ShapeDtypeStruct((1, 2 * KVD), jnp.float32),
        ],
        compiler_params=pltpu.CompilerParams(vmem_limit_bytes=VMEM),
        cost_estimate=SMALL_COST,
        name="turn_dkv",
    )(ids, dkv, cosine, sine)


def kv_grad_body(
    blk_count, rows, small_count, self_ref, cross_ref, core_ref, dq_ref, one_ref, own_ref, near_x_ref,
    core_x_ref, strip_ref, gain_two_ref, bias_q_ref, bias_kv_ref, grad_ref, here_ref, there_ref,
):
    count = self_ref.shape[0]
    strip_q = strip_ref.shape[1] - HD
    parts = (self_ref[...], core_ref[0], cross_ref[0], core_ref[1])
    near = jnp.concatenate(parts, axis=0)
    grad = tn(one_ref[...], near)
    gain_one = jnp.zeros((1, D), jnp.float32)
    for d in range(4):
        x = (own_ref[...], core_x_ref[0], near_x_ref[...], core_x_ref[1])[d][:, :D].astype(jnp.float32)
        root = lax.rsqrt(jnp.mean(x * x, axis=1, keepdims=True) + NORM_EPS)
        hone = nt(dq_ref[count * d : count * (d + 1)], strip_ref[:, :strip_q])
        hone = hone + nt(parts[d], strip_ref[:, strip_q:])
        gain_one = gain_one + jnp.sum(hone * x * root, axis=0, keepdims=True)
        out_ref = (here_ref, there_ref)[d % 2]
        out_ref[count * (d // 2) : count * (d // 2 + 1)] = hone.astype(jnp.bfloat16)
    vector = jnp.concatenate([gain_one, gain_two_ref[...], bias_q_ref[...], bias_kv_ref[...]], axis=1)
    extra = grad_ref.shape[1] - rows
    for b in range(blk_count):
        grad_ref[b, :rows] = grad[rows * b : rows * (b + 1)].astype(jnp.bfloat16)
        lines = []
        for line in range(extra):
            size = min(HD, max(small_count - line * HD, 0))
            begin = small_count * b + line * HD
            pieces = [vector[:, begin : begin + size]] if size > 0 else []
            if size < HD:
                pieces.append(jnp.zeros((1, HD - size), jnp.float32))
            lines.append(pieces[0] if len(pieces) == 1 else jnp.concatenate(pieces, axis=1))
        grad_ref[b, rows:] = jnp.concatenate(lines, axis=0).astype(jnp.bfloat16)


def kv_grad_rows(rows, small_count):
    needed = rows + -(-small_count // HD)
    return needed + -needed % 16


def make_kv_grad(blk_count, rows, small_count, own, cross, core, dq, one, x_own, x_cross, x_core, strip, gain_two, bias_q, bias_kv):
    count = own.shape[0]
    height = kv_grad_rows(rows, small_count)
    return pl.pallas_call(
        functools.partial(kv_grad_body, blk_count, rows, small_count),
        in_specs=[pl.BlockSpec(memory_space=pltpu.VMEM)] * 12,
        out_specs=[pl.BlockSpec(memory_space=pltpu.VMEM)] * 3,
        out_shape=[
            jax.ShapeDtypeStruct((blk_count, height, HD), jnp.bfloat16),
            jax.ShapeDtypeStruct((2 * count, D), jnp.bfloat16),
            jax.ShapeDtypeStruct((2 * count, D), jnp.bfloat16),
        ],
        compiler_params=pltpu.CompilerParams(vmem_limit_bytes=VMEM),
        cost_estimate=SMALL_COST,
        name="kv_grad",
    )(own, cross, core, dq, one, x_own, x_cross, x_core, strip, gain_two, bias_q, bias_kv)


CORE = [(0, 1), (1, 0), (2, 3), (3, 2)]
CROSS = [(0, 2), (2, 0), (1, 3), (3, 1)]
DIAG = [(0, 3), (3, 0), (1, 2), (2, 1)]


def low(values):
    return values.astype(jnp.bfloat16)


def wide(values):
    return values.astype(jnp.float32)


def swap_core(values):
    return lax.ppermute(values, "grp", CORE)


def swap_cross(values):
    return lax.ppermute(values, "grp", CROSS)


def swap_diag(values):
    return lax.ppermute(values, "grp", DIAG)


def swap_blk(values, bit):
    count = lax.axis_size("blk")
    return lax.ppermute(values, "blk", [(i, i ^ bit) for i in range(count)])


def blk_bit(bit):
    return (lax.axis_index("blk") & bit) != 0


def bits_of(count):
    out = []
    bit = count // 2
    while bit >= 1:
        out.append(bit)
        bit //= 2
    return out


def gather_bits(values, order):
    done = []
    for bit in order:
        other = swap_blk(values, bit)
        mine = blk_bit(bit)
        axis = sum(1 for d in done if d > bit)
        values = jnp.stack(
            [jnp.where(mine, other, values), jnp.where(mine, values, other)], axis=axis
        )
        done.append(bit)
    return values


def scatter_bits(values, axes, order):
    axes = list(axes)
    for bit in order:
        axis = axes.index(bit)
        mine = blk_bit(bit).astype(jnp.int32)
        keep = lax.dynamic_index_in_dim(values, mine, axis, keepdims=False)
        send = lax.dynamic_index_in_dim(values, 1 - mine, axis, keepdims=False)
        values = low(wide(keep) + wide(swap_blk(send, bit)))
        axes.remove(bit)
    return values


def by_place(parts):
    grp = lax.axis_index("grp")
    core = (grp & 1) != 0
    cross = (grp & 2) != 0
    a, b, c, d = parts
    a, b = jnp.where(core, b, a), jnp.where(core, a, b)
    c, d = jnp.where(core, d, c), jnp.where(core, c, d)
    a, c = jnp.where(cross, c, a), jnp.where(cross, a, c)
    b, d = jnp.where(cross, d, b), jnp.where(cross, b, d)
    return [a, b, c, d]


def gather_near(values):
    cross = swap_cross(values)
    both = swap_core(jnp.stack([values, cross]))
    return [values, both[0], cross, both[1]]


def gather_grp(values):
    return by_place(gather_near(values))


def gather_tokens(values, bit):
    half = values.shape[0] // 2
    cross = swap_cross(values)
    over = swap_blk(values, bit)
    first = swap_blk(cross[:half], bit)
    second = swap_cross(over[half:])
    chip = jnp.concatenate([values, cross, over, first, second])
    return jnp.concatenate([chip, swap_core(chip)])


def angles_of(position):
    half = HD // 2
    freqs = ROPE_BASE ** (-2.0 * jnp.arange(half, dtype=jnp.float32) / HD)
    return position.astype(jnp.float32)[:, None] * freqs[None, :]


def rotate_by(values, cosine, sine):
    half = HD // 2
    first_half = values[..., :half]
    second_half = values[..., half:]
    return jnp.concatenate(
        [first_half * cosine - second_half * sine, second_half * cosine + first_half * sine],
        axis=-1,
    )


def after(values, anchor):
    return lax.optimization_barrier((values, anchor))[0]


def gather_step(values, done, bit):
    other = swap_blk(values, bit)
    mine = blk_bit(bit)
    axis = sum(1 for d in done if d > bit)
    return jnp.stack(
        [jnp.where(mine, other, values), jnp.where(mine, values, other)], axis=axis
    )


def gather_near_stacked(values):
    both = jnp.stack([values, swap_cross(values)])
    return [both, swap_core(both)]


def ring_groups(count):
    return [[g * count + b for b in ring_order(count)] for g in range(4)]


def gather_ring(values):
    count = lax.axis_size("blk")
    return lax.all_gather(values, ("grp", "blk"), axis=0, axis_index_groups=ring_groups(count))


def exchange_near(parts):
    cross = swap_cross(jnp.stack([parts[2], parts[3]]))
    core = swap_core(jnp.stack([parts[1], cross[1]]))
    return [parts[0], core[0], cross[0], core[1]]


def on_device(
    tokens,
    cotangent,
    segment_ids,
    position_ids,
    w_attend,
    w_out,
    w_gate,
    w_up,
    w_down,
    small_params,
    first_attend,
    first_out,
    first_gate,
    first_up,
    first_down,
    first_small,
    second_attend,
    second_out,
    second_gate,
    second_up,
    second_down,
    second_small,
):
    rows_here, block_len = tokens.shape[:2]
    blk_count = lax.axis_size("blk")
    seq_len = block_len * blk_count
    token_count = rows_here * block_len
    grp = lax.axis_index("grp")
    blk = lax.axis_index("blk")
    cross_id, core_id = grp // 2, grp % 2
    strip_heads = H // 4
    strip_q = strip_heads * HD
    bits = bits_of(blk_count)
    team = blk_count // 4
    lows = [bit for bit in bits if bit < team]
    spread = [bits[0]] + lows
    low_shape = (2,) * len(lows)
    in_team = blk_bit(team).astype(jnp.int32)
    weight_rows = w_gate.shape[0]
    ff_block = w_down.shape[0]
    quarter = ff_block // 4
    widths = [size * blk_count // 2 for at, size in halves_of(quarter)]
    chip_rows = 4 * token_count
    half = token_count // 2

    ids = jnp.stack([grp, in_team])
    flat_low = tokens.reshape(token_count, D)
    dy_low = cotangent.reshape(token_count, D)
    positions = position_ids.reshape(token_count)
    kv_at = HQD + HD * cross_id + KVD * core_id
    strip_local = low(
        jnp.concatenate(
            [
                lax.dynamic_slice_in_dim(w_attend, strip_q * grp, strip_q, 1),
                lax.dynamic_slice_in_dim(w_attend, kv_at, HD, 1),
            ],
            axis=1,
        )
    )
    small_count = small_params.shape[0]
    small_send = jnp.concatenate([low(small_params), low(segment_ids.reshape(token_count))])
    strip_wide = strip_q + HD
    small_send = jnp.pad(small_send, (0, -small_send.shape[0] % (16 * strip_wide)))
    strip_local = jnp.concatenate([strip_local, small_send.reshape(-1, strip_wide)])
    ring = ring_order(blk_count)
    strip_ring = gather_ring(strip_local)
    small_ring = strip_ring[:, weight_rows:].reshape(blk_count, -1)[:, small_count : small_count + token_count]
    small_all = jnp.stack([small_ring[ring.index(b)] for b in range(blk_count)])
    digits = low(jnp.stack([positions // 64, positions % 64], axis=1))
    digits = jnp.pad(digits, ((0, 0), (0, HD - 2)))
    token_send = jnp.concatenate([flat_low, digits], axis=1)
    picked_a, picked_b = pick_columns(ids, w_gate, w_up, blk_count)
    got_a = swap_blk(picked_a[1], team)
    dy_cross = swap_cross(after(dy_low, picked_a))
    dy_over = swap_blk(after(dy_low, strip_ring), team)
    token_cross = after(swap_cross(token_send), (picked_a, strip_ring, got_a, dy_cross))

    def place(values, other, done, bit, lead=0):
        mine = blk_bit(bit)
        axis = lead + sum(1 for d in done if d > bit)
        return jnp.stack(
            [jnp.where(mine, other, values), jnp.where(mine, values, other)], axis=axis
        )

    mine_team = blk_bit(team)
    (low_first, size_first), (low_second, size_second) = halves_of(quarter)

    def team_pair(mine, got):
        return jnp.stack(
            [jnp.where(mine_team, got, mine), jnp.where(mine_team, mine, got)], axis=1
        )

    out_local = low(lax.dynamic_slice_in_dim(w_out, strip_q * grp, strip_q, 1))
    out_ring = gather_ring(after(out_local, strip_ring))
    down_here = low(lax.dynamic_slice_in_dim(w_down, quarter * grp, quarter, 0))
    token_core = swap_core(jnp.stack([token_send, token_cross]))
    freqs = ROPE_BASE ** (-2.0 * jnp.arange(HD // 2, dtype=jnp.float32) / HD)
    freqs = jnp.concatenate([freqs, freqs])[None]
    mixed_own, mixed_core, mixed_far, near_one, strip, vector = mix(
        ids, token_send, token_cross, token_core, strip_ring, freqs, blk_count, weight_rows, small_count
    )
    vector = vector[0]
    gain_one = vector[:D]
    gain_two = vector[D : 2 * D]
    seg_all = small_all.astype(jnp.int32)
    seg_all = seg_all.reshape(blk_count, rows_here, block_len)
    seg_key = jnp.broadcast_to(
        seg_all.transpose(1, 0, 2).reshape(rows_here, seq_len)[:, :, None], (rows_here, seq_len, HD)
    )
    seg_query = jnp.broadcast_to(segment_ids[:, None, :], (rows_here, 8, block_len))
    first_blk = jnp.sum((seg_all[:, :, -1] < segment_ids[None, :, 0]).astype(jnp.int32), axis=0)
    attend_ids = jnp.concatenate([blk[None], first_blk])

    mixed_cross = swap_cross(mixed_far)
    mixed_core = swap_core(jnp.stack([mixed_core, mixed_cross[1]]))
    pair_a = team_pair(picked_a[0], after(got_a, mixed_own))
    pair_a_got = swap_blk(pair_a, bits[0])
    mixed_core = after(mixed_core, (pair_a_got, dy_over))
    down_got = swap_blk(after(down_here, mixed_own), bits[0])
    query, packed_kv = pack(ids, mixed_own, mixed_cross, mixed_core)
    key_value = packed_kv.reshape(rows_here, block_len, 2 * KVD)
    kv_all = gather_ring(key_value)

    teams = [
        [g * blk_count + (i | t) for g in range(4) for t in (0, team)]
        for i in range(blk_count)
        if not i & team
    ]
    order = jnp.stack(
        [
            (grp ^ (2 * (i & 1) + (i >> 2))) * 2 + (in_team ^ ((i >> 1) & 1))
            for i in range(8)
        ]
    )

    peers = [[i for i in range(blk_count) if (i & team) == t] for t in (0, team)]

    def lows_of(values, done, lead=0, anchor=None):
        for bit in lows:
            got = swap_blk(values, bit)
            if anchor is not None:
                got = after(got, anchor)
            values = place(values, got, done, bit, lead)
            done = done + [bit]
        return values

    got_b = swap_blk(after(picked_b[1], mixed_own), team)
    pair_a = place(pair_a, after(pair_a_got, packed_kv), [team], bits[0], 1)
    pair_y_got = swap_blk(pair_a, lows[0])
    got_b, down_got = after((got_b, down_got), kv_all)
    kv_all = after(kv_all, (got_b, down_got, pair_y_got))
    down_here = place(down_here, down_got, [], bits[0])
    down_y_got = swap_blk(down_here, lows[0])
    down_here = place(down_here, down_y_got, [bits[0]], lows[0])
    for n in range(1, len(lows)):
        done = [bits[0]] + lows[:n]
        down_here = place(down_here, swap_blk(down_here, lows[n]), done, lows[n])
    down_here = down_here.reshape(2 * blk_count // 4, quarter, D)
    dy_first = swap_blk(dy_cross[:half], team)
    dy_second = swap_cross(dy_over[half:])
    out_ring = after(out_ring, packed_kv)
    out_strip = jnp.concatenate([out_ring[ring.index(b)] for b in range(blk_count)])
    out_cross = swap_cross(out_strip)
    out_core = swap_core(jnp.stack([out_strip, after(out_cross, kv_all)]))
    out_full = jnp.concatenate(by_place([out_strip, out_core[0], out_cross, out_core[1]]), axis=1)

    att_in, lse = attend(attend_ids, query, kv_all, seg_key, seg_query, block_len)
    pair_b = team_pair(picked_b[0], after(got_b, att_in))
    pair_b_got = swap_blk(pair_b, bits[0])
    flat = wide(flat_low)
    resid = flat + jnp.dot(att_in, out_full, preferred_element_type=jnp.float32)
    h_two = low(norm_apply(resid, gain_two))
    pair_a = place(pair_a, after(pair_y_got, h_two), [bits[0], team], lows[0], 1)
    for i in range(1, len(lows)):
        done = [bits[0], team] + lows[:i]
        pair_a = place(pair_a, swap_blk(pair_a, lows[i]), done, lows[i], 1)
    gate_up_a = pair_a.reshape(2, D, -1)
    pair_b_got = after(pair_b_got, (h_two, down_y_got))
    dy_first, dy_second = after((dy_first, dy_second), pair_b_got)
    dy_chip = jnp.concatenate([dy_low, dy_cross, dy_over, dy_first, dy_second])
    dy_team = jnp.concatenate([dy_chip, swap_core(dy_chip)])
    down_a = down_here[:, :size_first].reshape(widths[0], D)
    down_b = down_here[:, size_first:].reshape(widths[1], D)
    h_team = lax.all_gather(h_two, ("grp", "blk"), axis=0, tiled=True, axis_index_groups=teams)
    pair_b_got = after(pair_b_got, (h_two, gate_up_a))
    pair_b = place(pair_b, pair_b_got, [team], bits[0], 1)
    h_team = after(h_team, (gate_up_a, pair_b, dy_team))
    hidden_a, d_gate_a, d_up_a, *part_a = middle(order, h_team, dy_team, gate_up_a, down_a)
    gate_up_b = lows_of(pair_b, [bits[0], team], 1, hidden_a).reshape(2, D, -1)
    down_grad_a = down_grad(after(hidden_a, gate_up_b), dy_team)
    down_share_a = lax.psum_scatter(
        down_grad_a, "blk", scatter_dimension=0, axis_index_groups=peers, tiled=True
    )
    column_grad_a = two_grads(h_team, d_gate_a, d_up_a)

    def part_sent(values, axis, bit):
        mine = blk_bit(bit).astype(jnp.int32)
        keep = lax.dynamic_index_in_dim(values, mine, axis, keepdims=False)
        send = lax.dynamic_index_in_dim(values, 1 - mine, axis, keepdims=False)
        return keep, swap_blk(send, bit)

    def part_sum(keep, got):
        return low(wide(keep) + wide(got))

    def columns_first(grad):
        grad = grad.reshape((2, 2, 2) + low_shape + (weight_rows, -1))
        return part_sent(grad, 2 + len(lows), lows[-1])

    def columns_mid(keep, got):
        values = part_sum(keep, got)
        for i in range(len(lows) - 2, -1, -1):
            values = part_sum(*part_sent(values, 3 + i, lows[i]))
        return values

    def columns_third(keep, got):
        values = part_sum(keep, got)
        mine = lax.dynamic_index_in_dim(values, in_team, 1, keepdims=False)
        send = lax.dynamic_index_in_dim(values, 1 - in_team, 1, keepdims=False)
        return values, (mine, swap_blk(send, team))

    def rows_second(keep, got):
        values = part_sum(keep, got)
        for i in range(len(lows) - 2, -1, -1):
            values = part_sum(*part_sent(values, 1 + i, lows[i]))
        return part_sent(values, 0, bits[0])

    def columns_last(mine, got):
        return jnp.stack(
            [jnp.where(mine_team, got, mine), jnp.where(mine_team, mine, got)], axis=1
        )

    first_a = columns_first(column_grad_a)
    hidden_b, d_gate_b, d_up_b, d_here, d_there = middle(
        order, after(h_team, (column_grad_a, down_grad_a)), dy_team, gate_up_b, down_b, part_a
    )

    def chip_sum(values, came):
        return low(wide(values) + wide(came))

    def scatter_far(chip):
        far = chip[3 * token_count :]
        return swap_blk(far[:half], team), swap_cross(far[half:])

    def scatter_near(chip, first, second):
        cross, over = (chip[token_count * i : token_count * (i + 1)] for i in (1, 2))
        cross = jnp.concatenate([low(wide(cross[:half]) + wide(first)), cross[half:]])
        over = jnp.concatenate([over[:half], low(wide(over[half:]) + wide(second))])
        return swap_cross(cross), swap_blk(over, team)

    near_att_cross = swap_cross(after(att_in, hidden_a))
    d_there = after(d_there, (first_a[1], down_share_a, near_att_cross))
    d_came = swap_core(d_there)
    down_grad_b = down_grad(hidden_b, dy_team)
    rows_b = part_sent(
        down_grad_b.reshape((2,) + low_shape + (size_second, D)), len(lows), lows[-1]
    )
    mid_a = columns_mid(*after(first_a, d_came))
    second_a = part_sent(mid_a, 1, bits[0])
    d_chip = chip_sum(d_here, after(d_came, down_grad_b))
    d_far = scatter_far(d_chip)
    column_grad_b = two_grads(h_team, *after((d_gate_b, d_up_b), d_chip))
    first_b = columns_first(column_grad_b)
    d_far = after(d_far, column_grad_b)
    d_cross, d_over = scatter_near(d_chip, *d_far)
    out_part, out_there = down(*after((hidden_a, hidden_b), d_far), down_a, down_b, token_count)
    out_came = swap_core(out_there)
    d_cross, d_over = after((d_cross, d_over), out_part)
    d_htwo = wide(d_chip[:token_count]) + wide(d_cross) + wide(d_over)

    norm_value_two, norm_back_two = jax.vjp(norm_apply, resid, gain_two)
    d_resid_norm, grad_gain_two = norm_back_two(d_htwo)
    d_resid = wide(dy_low) + d_resid_norm
    d_att = low(d_resid)
    rows_b = rows_second(*after(rows_b, d_att))

    d_attended = low(right_transposed(d_att, out_full))
    own_angles = angles_of(positions)
    cosine, sine = jnp.cos(own_angles), jnp.sin(own_angles)
    d_query, dkv = attend_back(
        attend_ids,
        query,
        kv_all,
        seg_key,
        seg_query,
        att_in,
        d_attended,
        lse,
        jnp.concatenate([cosine, cosine], axis=1),
        jnp.concatenate([sine, sine], axis=1),
        block_len,
    )
    dkv = lax.psum_scatter(
        dkv.reshape(blk_count * token_count, 2 * KVD),
        ("grp", "blk"),
        scatter_dimension=0,
        axis_index_groups=ring_groups(blk_count),
        tiled=True,
    )
    down_share_b = part_sum(*after(rows_b, d_query))
    sum_a, third_a = columns_third(*after(second_a, d_att))

    def to_strips(parts):
        return jnp.concatenate(exchange_near(by_place(parts)))

    near_dq = to_strips([d_query[:, strip_q * k : strip_q * (k + 1)] for k in range(4)])
    block_shape = (2,) * len(bits) + (weight_rows, -1)
    query_grad = low(left_product(near_one, near_dq)).reshape(block_shape)

    near_att = swap_core(jnp.stack([att_in, near_att_cross]))
    near_att = jnp.concatenate([att_in, near_att[0], near_att_cross, near_att[1]])
    near_datt = to_strips([d_att[:, strip_q * k : strip_q * (k + 1)] for k in range(4)])
    out_grad = low(left_product(near_att, after(near_datt, d_attended))).reshape(block_shape)
    query_out = jnp.concatenate([query_grad, out_grad], axis=-1)
    steps_query = part_sent(query_out, len(bits) - 1, bits[-1])
    second_b = part_sent(columns_mid(*after(first_b, d_query)), 1, bits[0])
    dkv = after(dkv, down_share_b)
    own_part, core_part, far_part, bias_kv = turn_dkv(
        ids, dkv, jnp.concatenate([cosine, cosine], axis=1), jnp.concatenate([sine, sine], axis=1)
    )
    bias_q = jnp.sum(wide(d_query), axis=0)
    d_key = own_part
    cross_part = swap_cross(far_part)
    near_a = gather_near_stacked(columns_last(*after(third_a, own_part)))
    core_part = swap_core(jnp.stack([core_part, cross_part[1]]))
    kv_grad, hone_here, hone_there = make_kv_grad(
        blk_count,
        weight_rows,
        small_count,
        own_part,
        cross_part,
        core_part,
        near_dq,
        near_one,
        token_send,
        token_cross,
        token_core,
        strip,
        grad_gain_two[None],
        bias_q[None],
        bias_kv,
    )
    vector_rows = -(-small_count // HD)
    kv_grad = kv_grad.reshape((2,) * len(bits) + kv_grad.shape[1:])
    steps_kv = part_sent(kv_grad, len(bits) - 1, bits[-1])
    share_down = after(jnp.concatenate([down_share_a, down_share_b]), dkv)
    grad_down = lax.all_gather(share_down, "grp", axis=0, tiled=True)
    marks = [hone_there]
    for i in range(len(bits) - 2, -1, -1):
        kv_sum = part_sum(*steps_kv)
        steps_kv = part_sent(kv_sum, i, bits[i])
        marks.append(kv_sum)
    for n, i in enumerate(range(len(bits) - 2, -1, -1)):
        steps_query = part_sent(part_sum(*after(steps_query, marks[n + 1])), i, bits[i])
    sum_b, third_b = columns_third(*after(second_b, marks[-1]))
    share_kv_all = wide(steps_kv[0]) + wide(steps_kv[1])
    share_kv = low(share_kv_all[:weight_rows])
    vector_part = share_kv_all[weight_rows : weight_rows + vector_rows]
    share_query_out = part_sum(*after(steps_query, marks[-1]))

    other = wide(swap_core(hone_there))
    d_hone = wide(hone_here[:token_count]) + other[:token_count]
    d_hone_send = low(wide(hone_here[token_count:]) + other[token_count:])
    d_hone_cross = swap_cross(d_hone_send)
    square_sum = square_total(
        [
            wide(s)
            for s in (share_query_out, share_kv, sum_a, sum_b, share_down)
        ]
    )
    packed = jnp.concatenate([vector_part, jnp.full((8, HD), square_sum)])
    packed = after(packed, (d_hone_send, d_hone))
    packed = packed + swap_cross(packed)
    packed = packed + swap_core(packed)
    parts = gather_grp(after(jnp.concatenate([share_query_out, share_kv], axis=1), packed))
    grad_out = jnp.concatenate([part[:, strip_q : 2 * strip_q] for part in parts], axis=1)
    grad_attend = jnp.concatenate(
        [part[:, :strip_q] for part in parts] + [parts[k][:, 2 * strip_q :] for k in (0, 2, 1, 3)],
        axis=1,
    )
    share_vector = packed[:vector_rows].reshape(-1)[:small_count]
    square_sum = packed[vector_rows:] + jnp.sum(share_vector * share_vector)
    square_sum = after(square_sum, third_b[1])
    for bit in bits:
        square_sum = square_sum + swap_blk(square_sum, bit)
    grad_norm = jnp.sqrt(square_sum[0, 0])
    factor = jnp.minimum(1.0, CLIP_NORM / (grad_norm + 1e-06))
    out_chip = chip_sum(out_part, after(out_came, marks[1]))
    out_far = scatter_far(out_chip)
    factor = after(factor, (out_chip, near_a))

    new_first_attend, new_second_attend, new_attend = adam_step(
        w_attend, factor * wide(grad_attend), first_attend, second_attend, RATE_ATTEND, WEIGHT_DECAY
    )
    new_first_out, new_second_out, new_out = adam_step(
        w_out, factor * wide(grad_out), first_out, second_out, RATE_OUT, WEIGHT_DECAY
    )
    new_first_down, new_second_down, new_down = adam_step(
        w_down, factor * wide(grad_down), first_down, second_down, RATE_DOWN, WEIGHT_DECAY
    )
    own_b = columns_last(*third_b)
    cross_b = after(swap_cross(own_b), new_down)
    near_b = jnp.stack([own_b, cross_b])
    near_b = [near_b, swap_core(near_b)]
    new_first_gate, new_second_gate, new_gate = adam_columns(
        0, ids, factor[None], near_a, near_b, w_gate, first_gate, second_gate, blk_count, RATE_GATE, WEIGHT_DECAY
    )
    new_first_up, new_second_up, new_up = adam_columns(
        1, ids, factor[None], near_a, near_b, w_up, first_up, second_up, blk_count, RATE_GATE, WEIGHT_DECAY
    )
    norm_value_one, norm_back_one = jax.vjp(norm_apply, flat, gain_one)
    d_hone = after(d_hone + wide(after(d_hone_cross, new_gate)), new_gate)
    d_flat_norm, unused_gain = norm_back_one(d_hone)
    grad_tokens = low(d_resid + d_flat_norm)

    new_first_small, new_second_small, new_small = adam_step(
        small_params, factor * share_vector, first_small, second_small, RATE_VECTOR, 0.0
    )

    out_near = after(scatter_near(out_chip, *after(out_far, factor)), (new_gate, new_up))
    out_tokens = low(resid + wide(out_chip[:token_count]) + wide(out_near[0]) + wide(out_near[1]))
    return (
        out_tokens.reshape(rows_here, block_len, D),
        grad_tokens.reshape(rows_here, block_len, D),
        grad_norm,
        new_first_attend,
        new_second_attend,
        new_attend,
        new_first_out,
        new_second_out,
        new_out,
        new_first_gate,
        new_second_gate,
        new_gate,
        new_first_up,
        new_second_up,
        new_up,
        new_first_down,
        new_second_down,
        new_down,
        new_first_small,
        new_second_small,
        new_small,
    )


def solution(mesh):
    placed = (
        P("grp", "blk", None),
        P("grp", "blk", None),
        P("grp", "blk"),
        P("grp", "blk"),
        P("blk", None),
        P("blk", None),
        P("blk", None),
        P("blk", None),
        P("blk", None),
        P("blk"),
        P("blk", None),
        P("blk", None),
        P("blk", None),
        P("blk", None),
        P("blk", None),
        P("blk"),
        P("blk", None),
        P("blk", None),
        P("blk", None),
        P("blk", None),
        P("blk", None),
        P("blk"),
    )
    return jax.shard_map(
        on_device,
        mesh=mesh,
        in_specs=placed,
        out_specs=(
            P("grp", "blk", None),
            P("grp", "blk", None),
            P(),
            P("blk", None),
            P("blk", None),
            P("blk", None),
            P("blk", None),
            P("blk", None),
            P("blk", None),
            P("blk", None),
            P("blk", None),
            P("blk", None),
            P("blk", None),
            P("blk", None),
            P("blk", None),
            P("blk", None),
            P("blk", None),
            P("blk", None),
            P("blk"),
            P("blk"),
            P("blk"),
        ),
        check_vma=False,
    )
```

```python
import functools

import jax
import jax.numpy as jnp
from jax import lax
from jax.experimental import pallas as pl
from jax.experimental.pallas import tpu as pltpu
from jax.sharding import PartitionSpec as P

D = 1536
FF = 8960
H = 12
KVH = 2
HD = 128
STEP = 10
HQD = 1536
KVD = 256


NORM_EPS = 1e-06
ROPE_BASE = 10000.0
CLIP_NORM = 1.0
BETA_FIRST = 0.9
BETA_SECOND = 0.95
ADAM_EPS = 1e-08
WEIGHT_DECAY = 0.1
RATE_ATTEND = 0.06
RATE_OUT = 0.5
RATE_GATE = 0.06
RATE_DOWN = 0.03
RATE_VECTOR = 0.5
NEG_LARGE = -1e30
LOG2E = 1.4426950408889634
VMEM = 48 * 1024 * 1024
SMALL_COST = pl.CostEstimate(flops=1000, bytes_accessed=1000, transcendentals=0)


def norm_apply(values, gain):
    return values * lax.rsqrt(jnp.mean(values * values, axis=-1, keepdims=True) + NORM_EPS) * gain


def swish_product(gate, up_proj):
    return jax.nn.silu(gate) * up_proj


def left_product(left_side, right_side):
    return lax.dot_general(
        left_side, right_side, (((0,), (0,)), ((), ())), preferred_element_type=jnp.float32
    )


def right_transposed(left_side, right_side):
    return lax.dot_general(
        left_side, right_side, (((1,), (1,)), ((), ())), preferred_element_type=jnp.float32
    )


def square_total(arrays):
    return sum((jnp.sum(member * member) for member in arrays))


def adam_step(weight, grad, first, second, rate, decay):
    first_new = BETA_FIRST * first + (1.0 - BETA_FIRST) * grad
    second_new = BETA_SECOND * second + (1.0 - BETA_SECOND) * grad * grad
    first_hat = first_new / (1.0 - BETA_FIRST**STEP)
    second_hat = second_new / (1.0 - BETA_SECOND**STEP)
    weight_new = weight - rate * (first_hat / (jnp.sqrt(second_hat) + ADAM_EPS) + decay * weight)
    return (first_new, second_new, weight_new)


def ring_order(count):
    return list(range(0, count, 2)) + list(range(count - 1, 0, -2))


def halves_of(quarter):
    first = quarter * 16 // 35
    return ((0, first), (first, quarter - first))


def pick_body(blk_count, ids, gate_ref, up_ref, *out_refs):
    quarter = FF // blk_count // 4
    per = blk_count // 4
    for k in range(4):

        @pl.when(ids[0] == k)
        def _(k=k):
            for (at, size), out_ref in zip(halves_of(quarter), out_refs):
                for which, src in enumerate((gate_ref, up_ref)):
                    for bit in range(2):
                        parts = []
                        for high in range(2):
                            for small in range(per):
                                begin = (((high * 2 + bit) * per + small) * 4 + k) * quarter + at
                                parts.append(src[:, begin : begin + size])
                        out_ref[ids[1] ^ bit, which] = jnp.concatenate(parts, axis=1).astype(
                            jnp.bfloat16
                        )


def pick_columns(ids, gate, up, blk_count):
    rows = gate.shape[0]
    step = 48 if rows % 48 == 0 else rows
    widths = [size * blk_count // 2 for at, size in halves_of(FF // blk_count // 4)]
    spec = pl.BlockSpec((step, FF), lambda i, ids: (i, 0))
    return pl.pallas_call(
        functools.partial(pick_body, blk_count),
        grid_spec=pltpu.PrefetchScalarGridSpec(
            num_scalar_prefetch=1,
            grid=(rows // step,),
            in_specs=[spec, spec],
            out_specs=[pl.BlockSpec((2, 2, step, w), lambda i, ids: (0, 0, i, 0)) for w in widths],
        ),
        out_shape=[jax.ShapeDtypeStruct((2, 2, rows, w), jnp.bfloat16) for w in widths],
        compiler_params=pltpu.CompilerParams(vmem_limit_bytes=VMEM),
        cost_estimate=SMALL_COST,
        name="pick_columns",
    )(ids, gate, up)


def adam_body(blk_count, rate, decay, ids, factor_ref, first_ref, first_far_ref, second_ref, second_far_ref, w_ref, m_ref, v_ref, m_out, v_out, w_out):
    per = blk_count // 4
    sizes = [size for at, size in halves_of(FF // blk_count // 4)]
    grads = []
    for near_ref, far_ref in ((first_ref, first_far_ref), (second_ref, second_far_ref)):
        by_grp = []
        for k in range(4):
            away = ids[0] ^ k
            bits_of_k = []
            for bit in range(2):
                near = near_ref[away >> 1, bit].astype(jnp.float32)
                far = far_ref[away >> 1, bit].astype(jnp.float32)
                bits_of_k.append(jnp.where((away & 1) == 1, far, near))
            by_grp.append(bits_of_k)
        grads.append(by_grp)
    parts = []
    for high in range(2):
        for bit in range(2):
            for small in range(per):
                place = high * per + small
                for k in range(4):
                    for part, size in zip(grads, sizes):
                        parts.append(part[k][bit][:, place * size : (place + 1) * size])
    grad = jnp.concatenate(parts, axis=1) * factor_ref[0]
    m, v, w = adam_step(w_ref[...], grad, m_ref[...], v_ref[...], rate, decay)
    m_out[...] = m
    v_out[...] = v
    w_out[...] = w


def adam_columns(which, ids, factor, first, second, w, m, v, blk_count, rate, decay):
    rows = w.shape[0]
    step = 96 if rows % 96 == 0 else rows
    spec = pl.BlockSpec((step, FF), lambda i, ids: (i, 0))
    shape = jax.ShapeDtypeStruct((rows, FF), jnp.float32)
    grads = [
        pl.BlockSpec((2, None, 2, step, g.shape[-1]), lambda i, ids: (0, which, 0, i, 0))
        for g in first + second
    ]
    return pl.pallas_call(
        functools.partial(adam_body, blk_count, rate, decay),
        grid_spec=pltpu.PrefetchScalarGridSpec(
            num_scalar_prefetch=1,
            grid=(rows // step,),
            in_specs=[pl.BlockSpec(memory_space=pltpu.SMEM)] + grads + [spec, spec, spec],
            out_specs=[spec, spec, spec],
        ),
        out_shape=[shape] * 3,
        compiler_params=pltpu.CompilerParams(vmem_limit_bytes=VMEM),
        cost_estimate=SMALL_COST,
        name="adam_columns",
    )(ids, factor, *first, *second, w, m, v)


def nt(a, b, **kw):
    return lax.dot_general(a, b, (((1,), (1,)), ((), ())), preferred_element_type=jnp.float32, **kw)

def tn(a, b, **kw):
    return lax.dot_general(a, b, (((0,), (0,)), ((), ())), preferred_element_type=jnp.float32, **kw)

def stack_heads(ref, kvh, group):
    return jnp.concatenate([ref[:, HD * (kvh * group + i): HD * (kvh * group + i + 1)] for i in range(group)], axis=0)

def hidden_from(seg_key_ref, seg_query_ref, first, chunk, block_len, blk):
    key = first + lax.broadcasted_iota(jnp.int32, (chunk, block_len), 0)
    query = blk * block_len + lax.broadcasted_iota(jnp.int32, (chunk, block_len), 1)
    seg_key = seg_key_ref[pl.ds(first, chunk), :]
    counts = jnp.logical_and(key <= query, seg_key == seg_query_ref[0:1, :])
    return jnp.where(counts, 0.0, NEG_LARGE)

def ring_pair(ref, c, at):
    return jnp.concatenate(
        [ref[c, :, at : at + HD], ref[ref.shape[0] - 1 - c, :, at : at + HD]], axis=0
    )


def attend_body(chunk, ids, q_ref, k_ref, v_ref, seg_key_ref, seg_query_ref, o_ref, lse_ref, m_s, l_s, acc_s):
    block_len = q_ref.shape[0]
    group = H // KVH
    row = pl.program_id(0)
    per = chunk // block_len
    scale = HD ** (-0.5) * LOG2E
    start = ids[1 + row] // per
    stop = ids[0] // per + 1
    for kvh in range(KVH):
        q = stack_heads(q_ref, kvh, group)
        m_s[...] = jnp.full_like(m_s, NEG_LARGE)
        l_s[...] = jnp.zeros_like(l_s)
        acc_s[...] = jnp.zeros_like(acc_s)

        def step(c, carry):
            keys = ring_pair(k_ref, c, HD * kvh)
            vals = ring_pair(v_ref, c, HD * kvh)
            bias = hidden_from(seg_key_ref, seg_query_ref, c * chunk, chunk, block_len, ids[0])
            s = nt(keys, q) * scale + jnp.concatenate([bias] * group, axis=1)
            old = m_s[0:1, :]
            new = jnp.maximum(old, jnp.max(s, axis=0, keepdims=True))
            p = jnp.exp2(s - new)
            fade = jnp.exp2(old - new)
            l_s[0:1, :] = l_s[0:1, :] * fade + jnp.sum(p, axis=0, keepdims=True)
            acc_s[...] = acc_s[...] * fade + tn(vals, p.astype(jnp.bfloat16))
            m_s[0:1, :] = new
            return carry

        lax.fori_loop(start, stop, step, 0)
        total = l_s[0:1, :]
        out = (acc_s[...] * (1.0 / total)).T
        for i in range(group):
            o_ref[:, HD * (kvh * group + i): HD * (kvh * group + i + 1)] = out[block_len * i: block_len * (i + 1), :].astype(jnp.bfloat16)
        lse_ref[kvh] = jnp.broadcast_to(m_s[0:1, :] + jnp.log2(total), (8, group * block_len))

def attend(ids, q, kv, seg_key, seg_query, block_len):
    blk_count, rows = kv.shape[:2]
    group = H // KVH
    chunk = 2 * block_len
    many = group * block_len
    return pl.pallas_call(
        functools.partial(attend_body, chunk),
        grid_spec=pltpu.PrefetchScalarGridSpec(
            num_scalar_prefetch=1, grid=(rows,),
            in_specs=[
                pl.BlockSpec((block_len, HQD), lambda r, ids: (r, 0)),
                pl.BlockSpec((blk_count, None, block_len, KVD), lambda r, ids: (0, r, 0, 0)),
                pl.BlockSpec((blk_count, None, block_len, KVD), lambda r, ids: (0, r, 0, 1)),
                pl.BlockSpec((None, blk_count * block_len, HD), lambda r, ids: (r, 0, 0)),
                pl.BlockSpec((None, 8, block_len), lambda r, ids: (r, 0, 0)),
            ],
            out_specs=[
                pl.BlockSpec((block_len, HQD), lambda r, ids: (r, 0)),
                pl.BlockSpec((None, KVH, 8, many), lambda r, ids: (r, 0, 0, 0)),
            ],
            scratch_shapes=[pltpu.VMEM((8, many), jnp.float32), pltpu.VMEM((8, many), jnp.float32), pltpu.VMEM((HD, many), jnp.float32)]),
        out_shape=[
            jax.ShapeDtypeStruct((rows * block_len, HQD), jnp.bfloat16),
            jax.ShapeDtypeStruct((rows, KVH, 8, many), jnp.float32),
        ],
        compiler_params=pltpu.CompilerParams(vmem_limit_bytes=VMEM),
        cost_estimate=SMALL_COST,
        name="attend",
    )(ids, q, kv, kv, seg_key, seg_query)

def turn_back(u, cosine, sine):
    lane = lax.broadcasted_iota(jnp.int32, u.shape, 1)
    other = pltpu.roll(u, HD // 2, 1)
    return u * cosine + jnp.where(lane < HD // 2, other, -other) * sine

def attend_back_body(chunk, ids, q_ref, k_ref, v_ref, seg_key_ref, seg_query_ref, o_ref, do_ref, lse_ref, cos_ref, sin_ref, dq_ref, dkv_ref, dq_s):
    block_len = q_ref.shape[0]
    group = H // KVH
    row = pl.program_id(0)
    per = chunk // block_len
    plain = HD ** (-0.5)
    scale = plain * LOG2E
    start = ids[1 + row] // per
    stop = ids[0] // per + 1
    dkv_ref[...] = jnp.zeros_like(dkv_ref)
    for kvh in range(KVH):
        q = stack_heads(q_ref, kvh, group)
        do = stack_heads(do_ref, kvh, group)
        o = stack_heads(o_ref, kvh, group)
        both = do.astype(jnp.float32) * o.astype(jnp.float32)
        delta = nt(jnp.ones((8, HD), jnp.float32), both, precision=lax.Precision.HIGHEST)[0:1, :]
        lse = lse_ref[kvh][0:1, :]
        dq_s[...] = jnp.zeros_like(dq_s)

        def step(c, carry):
            keys = ring_pair(k_ref, c, HD * kvh)
            vals = ring_pair(v_ref, c, HD * kvh)
            bias = hidden_from(seg_key_ref, seg_query_ref, c * chunk, chunk, block_len, ids[0])
            s = nt(keys, q) * scale + jnp.concatenate([bias] * group, axis=1)
            p = jnp.exp2(s - lse)
            dp = nt(vals, do)
            ds = (p * (dp - delta)).astype(jnp.bfloat16)
            dk = jnp.dot(ds, q, preferred_element_type=jnp.float32) * plain
            dv = jnp.dot(p.astype(jnp.bfloat16), do, preferred_element_type=jnp.float32)
            for at, part in ((HD * kvh, dk.astype(jnp.bfloat16)), (KVD + HD * kvh, dv.astype(jnp.bfloat16))):
                dkv_ref[c, :, at : at + HD] = part[:block_len]
                dkv_ref[dkv_ref.shape[0] - 1 - c, :, at : at + HD] = part[block_len:]
            dq_s[...] += tn(ds, keys)
            return carry

        lax.fori_loop(start, stop, step, 0)
        cosine, sine = cos_ref[...], sin_ref[...]
        for i in range(group):
            u = dq_s[block_len * i: block_len * (i + 1), :] * plain
            at = HD * (kvh * group + i)
            dq_ref[:, at: at + HD] = turn_back(u, cosine, sine).astype(jnp.bfloat16)

def attend_back(ids, q, kv, seg_key, seg_query, o, do, lse, cosine, sine, block_len):
    blk_count, rows = kv.shape[:2]
    group = H // KVH
    chunk = 2 * block_len
    many = group * block_len
    per_row = pl.BlockSpec((block_len, HQD), lambda r, ids: (r, 0))
    turn = pl.BlockSpec((block_len, HD), lambda r, ids: (r, 0))
    return pl.pallas_call(
        functools.partial(attend_back_body, chunk),
        grid_spec=pltpu.PrefetchScalarGridSpec(
            num_scalar_prefetch=1, grid=(rows,),
            in_specs=[
                per_row,
                pl.BlockSpec((blk_count, None, block_len, KVD), lambda r, ids: (0, r, 0, 0)),
                pl.BlockSpec((blk_count, None, block_len, KVD), lambda r, ids: (0, r, 0, 1)),
                pl.BlockSpec((None, blk_count * block_len, HD), lambda r, ids: (r, 0, 0)),
                pl.BlockSpec((None, 8, block_len), lambda r, ids: (r, 0, 0)),
                per_row, per_row,
                pl.BlockSpec((None, KVH, 8, many), lambda r, ids: (r, 0, 0, 0)),
                turn, turn,
            ],
            out_specs=[per_row, pl.BlockSpec((blk_count, None, block_len, 2 * KVD), lambda r, ids: (0, r, 0, 0))],
            scratch_shapes=[pltpu.VMEM((many, HD), jnp.float32)]),
        out_shape=[
            jax.ShapeDtypeStruct((rows * block_len, HQD), jnp.bfloat16),
            jax.ShapeDtypeStruct((blk_count, rows, block_len, 2 * KVD), jnp.bfloat16),
        ],
        compiler_params=pltpu.CompilerParams(vmem_limit_bytes=VMEM),
        cost_estimate=SMALL_COST,
        name="attend_back",
    )(ids, q, kv, kv, seg_key, seg_query, o, do, lse, cosine, sine)

def nn(a, b):
    return jnp.dot(a, b, preferred_element_type=jnp.float32)


def middle_body(add, order, h_ref, dy_ref, wg_ref, wu_ref, wd_ref, *refs):
    prev_refs = refs[:2] if add else None
    hid_ref, dg_ref, du_ref, dh_ref, dh_far_ref = refs[-5:]
    here = pl.program_id(0) < 4
    h = h_ref[...]
    gate = nn(h, wg_ref[...])
    up = nn(h, wu_ref[...])
    sig = 1.0 / (1.0 + jnp.exp(-gate))
    silu = gate * sig
    hid_ref[...] = (silu * up).astype(jnp.bfloat16)
    dhid = nt(dy_ref[...], wd_ref[...])
    dg = (dhid * up * sig * (1.0 + gate * (1.0 - sig))).astype(jnp.bfloat16)
    du = (dhid * silu).astype(jnp.bfloat16)
    dg_ref[...] = dg
    du_ref[...] = du
    dh = nt(dg, wg_ref[...]) + nt(du, wu_ref[...])
    if add:
        prev = jnp.where(here, prev_refs[0][...].astype(jnp.float32), prev_refs[1][...].astype(jnp.float32))
        dh = dh + prev
    dh = dh.astype(jnp.bfloat16)

    @pl.when(here)
    def _():
        dh_ref[...] = dh

    @pl.when(jnp.logical_not(here))
    def _():
        dh_far_ref[...] = dh


def middle(order, h, dy, gate_up, wd, prev=None):
    count = h.shape[0]
    step = count // order.shape[0]
    wide_here = wd.shape[0]
    row = pl.BlockSpec((step, D), lambda i, order: (i, 0))
    placed = pl.BlockSpec((step, D), lambda i, order: (order[i], 0))
    part = pl.BlockSpec((step, wide_here), lambda i, order: (i, 0))
    part_placed = pl.BlockSpec((step, wide_here), lambda i, order: (order[i], 0))
    once = pl.Buffered(1)
    extra = [] if prev is None else list(prev)
    near = pl.BlockSpec((step, D), lambda i, order: (jnp.minimum(i, 3), 0))
    far = pl.BlockSpec((step, D), lambda i, order: (jnp.maximum(i - 4, 0), 0))
    return pl.pallas_call(
        functools.partial(middle_body, prev is not None),
        grid_spec=pltpu.PrefetchScalarGridSpec(
            num_scalar_prefetch=1,
            grid=(count // step,),
            in_specs=[
                placed,
                row,
                pl.BlockSpec((None, D, wide_here), lambda i, order: (0, 0, 0), pipeline_mode=once),
                pl.BlockSpec((None, D, wide_here), lambda i, order: (1, 0, 0), pipeline_mode=once),
                pl.BlockSpec((wide_here, D), lambda i, order: (0, 0), pipeline_mode=once),
            ]
            + [near, far][: len(extra)],
            out_specs=[part, part_placed, part_placed, near, far],
        ),
        out_shape=[jax.ShapeDtypeStruct((count, wide_here), jnp.bfloat16)] * 3
        + [jax.ShapeDtypeStruct((count // 2, D), jnp.bfloat16)] * 2,
        compiler_params=pltpu.CompilerParams(vmem_limit_bytes=VMEM),
        cost_estimate=SMALL_COST,
        name="middle",
    )(order, h, dy, gate_up, gate_up, wd, *extra)


def two_grads_body(h_ref, a_ref, b_ref, out_ref):
    h = h_ref[...]
    out_ref[0] = tn(h, a_ref[...]).astype(jnp.bfloat16)
    out_ref[1] = tn(h, b_ref[...]).astype(jnp.bfloat16)


def two_grads(h, a, b, step=256):
    count = h.shape[0]
    wide_here = a.shape[1]
    whole = pl.BlockSpec(a.shape, lambda i: (0, 0), pipeline_mode=pl.Buffered(1))
    return pl.pallas_call(
        two_grads_body,
        grid=(D // step,),
        in_specs=[pl.BlockSpec((count, step), lambda i: (0, i)), whole, whole],
        out_specs=pl.BlockSpec((2, step, wide_here), lambda i: (0, i, 0)),
        out_shape=jax.ShapeDtypeStruct((2, D, wide_here), jnp.bfloat16),
        compiler_params=pltpu.CompilerParams(vmem_limit_bytes=VMEM),
        cost_estimate=SMALL_COST,
        name="two_grads",
    )(h, a, b)


def down_grad_body(hid_ref, dy_ref, g_ref):
    g_ref[...] = tn(hid_ref[...], dy_ref[...]).astype(jnp.bfloat16)

def down_grad(hid, dy, step=512):
    T, F = hid.shape
    D = dy.shape[1]
    return pl.pallas_call(down_grad_body, grid=(D // step,),
        in_specs=[pl.BlockSpec((T, F), lambda i: (0, 0), pipeline_mode=pl.Buffered(1)), pl.BlockSpec((T, step), lambda i: (0, i))],
        out_specs=pl.BlockSpec((F, step), lambda i: (0, i)),
        out_shape=jax.ShapeDtypeStruct((F, D), jnp.bfloat16),
        compiler_params=pltpu.CompilerParams(vmem_limit_bytes=VMEM),
        cost_estimate=SMALL_COST,
        name="down_grad")(hid, dy)

def down_body(hid_a_ref, hid_b_ref, wd_a_ref, wd_b_ref, o_ref, o_far_ref):
    out = nn(hid_a_ref[...], wd_a_ref[...]) + nn(hid_b_ref[...], wd_b_ref[...])
    out = out.astype(jnp.bfloat16)
    here = pl.program_id(0) < 4

    @pl.when(here)
    def _():
        o_ref[...] = out

    @pl.when(jnp.logical_not(here))
    def _():
        o_far_ref[...] = out


def down(hid_a, hid_b, wd_a, wd_b, step):
    count = hid_a.shape[0]

    def rows(array):
        return pl.BlockSpec((step, array.shape[1]), lambda i: (i, 0))

    def whole(array):
        return pl.BlockSpec(array.shape, lambda i: (0, 0), pipeline_mode=pl.Buffered(1))

    return pl.pallas_call(
        down_body,
        grid=(count // step,),
        in_specs=[rows(hid_a), rows(hid_b), whole(wd_a), whole(wd_b)],
        out_specs=[
            pl.BlockSpec((step, D), lambda i: (jnp.minimum(i, 3), 0)),
            pl.BlockSpec((step, D), lambda i: (jnp.maximum(i - 4, 0), 0)),
        ],
        out_shape=[jax.ShapeDtypeStruct((count // 2, D), jnp.bfloat16)] * 2,
        compiler_params=pltpu.CompilerParams(vmem_limit_bytes=VMEM),
        cost_estimate=SMALL_COST,
        name="down",
    )(hid_a, hid_b, wd_a, wd_b)


def turn(u, cosine, sine):
    lane = lax.broadcasted_iota(jnp.int32, u.shape, 1)
    other = pltpu.roll(u, HD // 2, 1)
    return u * cosine + jnp.where(lane < HD // 2, -other, other) * sine


def mix_body(
    blk_count, rows, small_count, ids, own_ref, cross_ref, core_ref, ring_ref, freq_ref,
    self_ref, near_ref, far_ref, one_ref, strip_ref, vector_ref,
):
    ring = ring_order(blk_count)
    wide_here = ring_ref.shape[-1]
    pieces = []
    for b in range(blk_count):
        at = ring.index(b)
        strip_ref[rows * b : rows * (b + 1)] = ring_ref[at, :rows]
        left = small_count
        line = rows
        while left > 0:
            size = min(left, wide_here)
            pieces.append(ring_ref[at, line : line + 1, :size].astype(jnp.float32))
            left -= size
            line += 1
    vector = jnp.concatenate(pieces, axis=1)
    vector_ref[...] = vector
    gain = vector[:, :D]
    grp = ids[0]
    strip_q = wide_here - HD
    bias = jnp.zeros((1, wide_here), jnp.float32)
    for k in range(4):
        kv_at = 2 * D + HQD + HD * (k // 2) + KVD * (k % 2)
        part = jnp.concatenate(
            [
                vector[:, 2 * D + strip_q * k : 2 * D + strip_q * (k + 1)],
                vector[:, kv_at : kv_at + HD],
            ],
            axis=1,
        )
        bias = bias + jnp.where(grp == k, part, 0.0)
    count = own_ref.shape[0]
    strip = strip_ref[...]
    for d in range(4):
        source = (own_ref[...], core_ref[0], cross_ref[...], core_ref[1])[d]
        x = source[:, :D].astype(jnp.float32)
        root = lax.rsqrt(jnp.mean(x * x, axis=1, keepdims=True) + NORM_EPS)
        one = (x * root * gain).astype(jnp.bfloat16)
        one_ref[count * d : count * (d + 1)] = one
        mixed = nn(one, strip) + bias
        digits = source[:, D : D + HD].astype(jnp.float32)
        position = 64.0 * digits[:, 0:1] + digits[:, 1:2]
        angles = position * freq_ref[...]
        cosine, sine = jnp.cos(angles), jnp.sin(angles)
        for i in range(wide_here // HD):
            c, s = cosine, sine
            if i == wide_here // HD - 1:
                c = jnp.where(grp % 2 == 1, 1.0, c)
                s = jnp.where(grp % 2 == 1, 0.0, s)
            at = HD * i
            out = turn(mixed[:, at : at + HD], c, s).astype(jnp.bfloat16)
            if d == 0:
                self_ref[:, at : at + HD] = out
            elif d == 1:
                near_ref[:, at : at + HD] = out
            else:
                far_ref[d - 2, :, at : at + HD] = out


def mix(ids, own, cross, core, ring, freq, blk_count, rows, small_count):
    count = own.shape[0]
    wide_here = ring.shape[-1]
    low16 = jnp.bfloat16
    return pl.pallas_call(
        functools.partial(mix_body, blk_count, rows, small_count),
        in_specs=[pl.BlockSpec(memory_space=pltpu.SMEM)] + [pl.BlockSpec(memory_space=pltpu.VMEM)] * 5,
        out_specs=[pl.BlockSpec(memory_space=pltpu.VMEM)] * 6,
        out_shape=[
            jax.ShapeDtypeStruct((count, wide_here), low16),
            jax.ShapeDtypeStruct((count, wide_here), low16),
            jax.ShapeDtypeStruct((2, count, wide_here), low16),
            jax.ShapeDtypeStruct((4 * count, D), low16),
            jax.ShapeDtypeStruct((D, wide_here), low16),
            jax.ShapeDtypeStruct((1, blk_count * small_count), jnp.float32),
        ],
        compiler_params=pltpu.CompilerParams(vmem_limit_bytes=VMEM),
        cost_estimate=SMALL_COST,
        name="mix",
    )(ids, own, cross, core, ring, freq)


def pack_body(ids, self_ref, cross_ref, core_ref, q_ref, kv_ref):
    strip_q = self_ref.shape[1] - HD
    for g in range(4):

        @pl.when(ids[0] == g)
        def _(g=g):
            for k in range(4):
                part = (self_ref[...], core_ref[0], cross_ref[0], core_ref[1])[g ^ k]
                q_ref[:, strip_q * k : strip_q * (k + 1)] = part[:, :strip_q]
                at = (k % 2) * KVD + (k // 2) * HD
                kv_ref[:, at : at + HD] = part[:, strip_q:]


def pack(ids, own, cross, core):
    count = own.shape[0]
    return pl.pallas_call(
        pack_body,
        in_specs=[pl.BlockSpec(memory_space=pltpu.SMEM)] + [pl.BlockSpec(memory_space=pltpu.VMEM)] * 3,
        out_specs=[pl.BlockSpec(memory_space=pltpu.VMEM)] * 2,
        out_shape=[
            jax.ShapeDtypeStruct((count, HQD), jnp.bfloat16),
            jax.ShapeDtypeStruct((count, 2 * KVD), jnp.bfloat16),
        ],
        compiler_params=pltpu.CompilerParams(vmem_limit_bytes=VMEM),
        cost_estimate=SMALL_COST,
        name="pack",
    )(ids, own, cross, core)


def turn_dkv_body(ids, dkv_ref, cos_ref, sin_ref, self_ref, near_ref, far_ref, sum_ref):
    items = []
    sums = [None] * 4
    for k in range(4):
        at = (k % 2) * KVD + (k // 2) * HD
        part = dkv_ref[:, at : at + HD]
        if k % 2 == 0:
            part = turn_back(part.astype(jnp.float32), cos_ref[...], sin_ref[...]).astype(jnp.bfloat16)
        items.append(part)
        sums[(k % 2) * 2 + k // 2] = jnp.sum(part.astype(jnp.float32), axis=0, keepdims=True)
    sum_ref[...] = jnp.concatenate(sums, axis=1)
    for g in range(4):

        @pl.when(ids[0] == g)
        def _(g=g):
            self_ref[...] = items[g]
            near_ref[...] = items[g ^ 1]
            far_ref[0] = items[g ^ 2]
            far_ref[1] = items[g ^ 3]


def turn_dkv(ids, dkv, cosine, sine):
    count = dkv.shape[0]
    return pl.pallas_call(
        turn_dkv_body,
        in_specs=[pl.BlockSpec(memory_space=pltpu.SMEM)] + [pl.BlockSpec(memory_space=pltpu.VMEM)] * 3,
        out_specs=[pl.BlockSpec(memory_space=pltpu.VMEM)] * 4,
        out_shape=[
            jax.ShapeDtypeStruct((count, HD), jnp.bfloat16),
            jax.ShapeDtypeStruct((count, HD), jnp.bfloat16),
            jax.ShapeDtypeStruct((2, count, HD), jnp.bfloat16),
            jax.ShapeDtypeStruct((1, 2 * KVD), jnp.float32),
        ],
        compiler_params=pltpu.CompilerParams(vmem_limit_bytes=VMEM),
        cost_estimate=SMALL_COST,
        name="turn_dkv",
    )(ids, dkv, cosine, sine)


def kv_grad_body(
    blk_count, rows, small_count, self_ref, cross_ref, core_ref, dq_ref, one_ref, own_ref, near_x_ref,
    core_x_ref, strip_ref, gain_two_ref, bias_q_ref, bias_kv_ref, grad_ref, here_ref, there_ref,
):
    count = self_ref.shape[0]
    strip_q = strip_ref.shape[1] - HD
    parts = (self_ref[...], core_ref[0], cross_ref[0], core_ref[1])
    near = jnp.concatenate(parts, axis=0)
    grad = tn(one_ref[...], near)
    gain_one = jnp.zeros((1, D), jnp.float32)
    for d in range(4):
        x = (own_ref[...], core_x_ref[0], near_x_ref[...], core_x_ref[1])[d][:, :D].astype(jnp.float32)
        root = lax.rsqrt(jnp.mean(x * x, axis=1, keepdims=True) + NORM_EPS)
        hone = nt(dq_ref[count * d : count * (d + 1)], strip_ref[:, :strip_q])
        hone = hone + nt(parts[d], strip_ref[:, strip_q:])
        gain_one = gain_one + jnp.sum(hone * x * root, axis=0, keepdims=True)
        out_ref = (here_ref, there_ref)[d % 2]
        out_ref[count * (d // 2) : count * (d // 2 + 1)] = hone.astype(jnp.bfloat16)
    vector = jnp.concatenate([gain_one, gain_two_ref[...], bias_q_ref[...], bias_kv_ref[...]], axis=1)
    extra = grad_ref.shape[1] - rows
    for b in range(blk_count):
        grad_ref[b, :rows] = grad[rows * b : rows * (b + 1)].astype(jnp.bfloat16)
        lines = []
        for line in range(extra):
            size = min(HD, max(small_count - line * HD, 0))
            begin = small_count * b + line * HD
            pieces = [vector[:, begin : begin + size]] if size > 0 else []
            if size < HD:
                pieces.append(jnp.zeros((1, HD - size), jnp.float32))
            lines.append(pieces[0] if len(pieces) == 1 else jnp.concatenate(pieces, axis=1))
        grad_ref[b, rows:] = jnp.concatenate(lines, axis=0).astype(jnp.bfloat16)


def kv_grad_rows(rows, small_count):
    needed = rows + -(-small_count // HD)
    return needed + -needed % 16


def make_kv_grad(blk_count, rows, small_count, own, cross, core, dq, one, x_own, x_cross, x_core, strip, gain_two, bias_q, bias_kv):
    count = own.shape[0]
    height = kv_grad_rows(rows, small_count)
    return pl.pallas_call(
        functools.partial(kv_grad_body, blk_count, rows, small_count),
        in_specs=[pl.BlockSpec(memory_space=pltpu.VMEM)] * 12,
        out_specs=[pl.BlockSpec(memory_space=pltpu.VMEM)] * 3,
        out_shape=[
            jax.ShapeDtypeStruct((blk_count, height, HD), jnp.bfloat16),
            jax.ShapeDtypeStruct((2 * count, D), jnp.bfloat16),
            jax.ShapeDtypeStruct((2 * count, D), jnp.bfloat16),
        ],
        compiler_params=pltpu.CompilerParams(vmem_limit_bytes=VMEM),
        cost_estimate=SMALL_COST,
        name="kv_grad",
    )(own, cross, core, dq, one, x_own, x_cross, x_core, strip, gain_two, bias_q, bias_kv)


CORE = [(0, 1), (1, 0), (2, 3), (3, 2)]
CROSS = [(0, 2), (2, 0), (1, 3), (3, 1)]
DIAG = [(0, 3), (3, 0), (1, 2), (2, 1)]


def low(values):
    return values.astype(jnp.bfloat16)


def wide(values):
    return values.astype(jnp.float32)


def swap_core(values):
    return lax.ppermute(values, "grp", CORE)


def swap_cross(values):
    return lax.ppermute(values, "grp", CROSS)


def swap_diag(values):
    return lax.ppermute(values, "grp", DIAG)


def swap_blk(values, bit):
    count = lax.axis_size("blk")
    return lax.ppermute(values, "blk", [(i, i ^ bit) for i in range(count)])


def blk_bit(bit):
    return (lax.axis_index("blk") & bit) != 0


def bits_of(count):
    out = []
    bit = count // 2
    while bit >= 1:
        out.append(bit)
        bit //= 2
    return out


def gather_bits(values, order):
    done = []
    for bit in order:
        other = swap_blk(values, bit)
        mine = blk_bit(bit)
        axis = sum(1 for d in done if d > bit)
        values = jnp.stack(
            [jnp.where(mine, other, values), jnp.where(mine, values, other)], axis=axis
        )
        done.append(bit)
    return values


def scatter_bits(values, axes, order):
    axes = list(axes)
    for bit in order:
        axis = axes.index(bit)
        mine = blk_bit(bit).astype(jnp.int32)
        keep = lax.dynamic_index_in_dim(values, mine, axis, keepdims=False)
        send = lax.dynamic_index_in_dim(values, 1 - mine, axis, keepdims=False)
        values = low(wide(keep) + wide(swap_blk(send, bit)))
        axes.remove(bit)
    return values


def by_place(parts):
    grp = lax.axis_index("grp")
    core = (grp & 1) != 0
    cross = (grp & 2) != 0
    a, b, c, d = parts
    a, b = jnp.where(core, b, a), jnp.where(core, a, b)
    c, d = jnp.where(core, d, c), jnp.where(core, c, d)
    a, c = jnp.where(cross, c, a), jnp.where(cross, a, c)
    b, d = jnp.where(cross, d, b), jnp.where(cross, b, d)
    return [a, b, c, d]


def gather_near(values):
    cross = swap_cross(values)
    both = swap_core(jnp.stack([values, cross]))
    return [values, both[0], cross, both[1]]


def gather_grp(values):
    return by_place(gather_near(values))


def gather_tokens(values, bit):
    half = values.shape[0] // 2
    cross = swap_cross(values)
    over = swap_blk(values, bit)
    first = swap_blk(cross[:half], bit)
    second = swap_cross(over[half:])
    chip = jnp.concatenate([values, cross, over, first, second])
    return jnp.concatenate([chip, swap_core(chip)])


def angles_of(position):
    half = HD // 2
    freqs = ROPE_BASE ** (-2.0 * jnp.arange(half, dtype=jnp.float32) / HD)
    return position.astype(jnp.float32)[:, None] * freqs[None, :]


def rotate_by(values, cosine, sine):
    half = HD // 2
    first_half = values[..., :half]
    second_half = values[..., half:]
    return jnp.concatenate(
        [first_half * cosine - second_half * sine, second_half * cosine + first_half * sine],
        axis=-1,
    )


def after(values, anchor):
    return lax.optimization_barrier((values, anchor))[0]


def gather_step(values, done, bit):
    other = swap_blk(values, bit)
    mine = blk_bit(bit)
    axis = sum(1 for d in done if d > bit)
    return jnp.stack(
        [jnp.where(mine, other, values), jnp.where(mine, values, other)], axis=axis
    )


def gather_near_stacked(values):
    both = jnp.stack([values, swap_cross(values)])
    return [both, swap_core(both)]


def ring_groups(count):
    return [[g * count + b for b in ring_order(count)] for g in range(4)]


def gather_ring(values):
    count = lax.axis_size("blk")
    return lax.all_gather(values, ("grp", "blk"), axis=0, axis_index_groups=ring_groups(count))


def exchange_near(parts):
    cross = swap_cross(jnp.stack([parts[2], parts[3]]))
    core = swap_core(jnp.stack([parts[1], cross[1]]))
    return [parts[0], core[0], cross[0], core[1]]


def on_device(
    tokens,
    cotangent,
    segment_ids,
    position_ids,
    w_attend,
    w_out,
    w_gate,
    w_up,
    w_down,
    small_params,
    first_attend,
    first_out,
    first_gate,
    first_up,
    first_down,
    first_small,
    second_attend,
    second_out,
    second_gate,
    second_up,
    second_down,
    second_small,
):
    rows_here, block_len = tokens.shape[:2]
    blk_count = lax.axis_size("blk")
    seq_len = block_len * blk_count
    token_count = rows_here * block_len
    grp = lax.axis_index("grp")
    blk = lax.axis_index("blk")
    cross_id, core_id = grp // 2, grp % 2
    strip_heads = H // 4
    strip_q = strip_heads * HD
    bits = bits_of(blk_count)
    team = blk_count // 4
    lows = [bit for bit in bits if bit < team]
    spread = [bits[0]] + lows
    low_shape = (2,) * len(lows)
    in_team = blk_bit(team).astype(jnp.int32)
    weight_rows = w_gate.shape[0]
    ff_block = w_down.shape[0]
    quarter = ff_block // 4
    widths = [size * blk_count // 2 for at, size in halves_of(quarter)]
    chip_rows = 4 * token_count
    half = token_count // 2

    ids = jnp.stack([grp, in_team])
    flat_low = tokens.reshape(token_count, D)
    dy_low = cotangent.reshape(token_count, D)
    positions = position_ids.reshape(token_count)
    kv_at = HQD + HD * cross_id + KVD * core_id
    strip_local = low(
        jnp.concatenate(
            [
                lax.dynamic_slice_in_dim(w_attend, strip_q * grp, strip_q, 1),
                lax.dynamic_slice_in_dim(w_attend, kv_at, HD, 1),
            ],
            axis=1,
        )
    )
    small_count = small_params.shape[0]
    small_send = jnp.concatenate([low(small_params), low(segment_ids.reshape(token_count))])
    strip_wide = strip_q + HD
    small_send = jnp.pad(small_send, (0, -small_send.shape[0] % (16 * strip_wide)))
    strip_local = jnp.concatenate([strip_local, small_send.reshape(-1, strip_wide)])
    ring = ring_order(blk_count)
    strip_ring = gather_ring(strip_local)
    small_ring = strip_ring[:, weight_rows:].reshape(blk_count, -1)[:, small_count : small_count + token_count]
    small_all = jnp.stack([small_ring[ring.index(b)] for b in range(blk_count)])
    digits = low(jnp.stack([positions // 64, positions % 64], axis=1))
    digits = jnp.pad(digits, ((0, 0), (0, HD - 2)))
    token_send = jnp.concatenate([flat_low, digits], axis=1)
    picked_a, picked_b = pick_columns(ids, w_gate, w_up, blk_count)
    got_a = swap_blk(picked_a[1], team)
    dy_cross = swap_cross(after(dy_low, picked_a))
    dy_over = swap_blk(after(dy_low, strip_ring), team)
    token_cross = after(swap_cross(token_send), (picked_a, strip_ring, got_a, dy_cross))

    def place(values, other, done, bit, lead=0):
        mine = blk_bit(bit)
        axis = lead + sum(1 for d in done if d > bit)
        return jnp.stack(
            [jnp.where(mine, other, values), jnp.where(mine, values, other)], axis=axis
        )

    mine_team = blk_bit(team)
    (low_first, size_first), (low_second, size_second) = halves_of(quarter)

    def team_pair(mine, got):
        return jnp.stack(
            [jnp.where(mine_team, got, mine), jnp.where(mine_team, mine, got)], axis=1
        )

    out_local = low(lax.dynamic_slice_in_dim(w_out, strip_q * grp, strip_q, 1))
    out_ring = gather_ring(after(out_local, strip_ring))
    down_here = low(lax.dynamic_slice_in_dim(w_down, quarter * grp, quarter, 0))
    token_core = swap_core(jnp.stack([token_send, token_cross]))
    freqs = ROPE_BASE ** (-2.0 * jnp.arange(HD // 2, dtype=jnp.float32) / HD)
    freqs = jnp.concatenate([freqs, freqs])[None]
    mixed_own, mixed_core, mixed_far, near_one, strip, vector = mix(
        ids, token_send, token_cross, token_core, strip_ring, freqs, blk_count, weight_rows, small_count
    )
    vector = vector[0]
    gain_one = vector[:D]
    gain_two = vector[D : 2 * D]
    seg_all = small_all.astype(jnp.int32)
    seg_all = seg_all.reshape(blk_count, rows_here, block_len)
    seg_key = jnp.broadcast_to(
        seg_all.transpose(1, 0, 2).reshape(rows_here, seq_len)[:, :, None], (rows_here, seq_len, HD)
    )
    seg_query = jnp.broadcast_to(segment_ids[:, None, :], (rows_here, 8, block_len))
    first_blk = jnp.sum((seg_all[:, :, -1] < segment_ids[None, :, 0]).astype(jnp.int32), axis=0)
    attend_ids = jnp.concatenate([blk[None], first_blk])

    mixed_cross = swap_cross(mixed_far)
    mixed_core = swap_core(jnp.stack([mixed_core, mixed_cross[1]]))
    pair_a = team_pair(picked_a[0], after(got_a, mixed_own))
    pair_a_got = swap_blk(pair_a, bits[0])
    mixed_core = after(mixed_core, (pair_a_got, dy_over))
    down_got = swap_blk(after(down_here, mixed_own), bits[0])
    query, packed_kv = pack(ids, mixed_own, mixed_cross, mixed_core)
    key_value = packed_kv.reshape(rows_here, block_len, 2 * KVD)
    kv_all = gather_ring(key_value)

    teams = [
        [g * blk_count + (i | t) for g in range(4) for t in (0, team)]
        for i in range(blk_count)
        if not i & team
    ]
    order = jnp.stack(
        [
            (grp ^ (2 * (i & 1) + (i >> 2))) * 2 + (in_team ^ ((i >> 1) & 1))
            for i in range(8)
        ]
    )

    peers = [[i for i in range(blk_count) if (i & team) == t] for t in (0, team)]

    def lows_of(values, done, lead=0, anchor=None):
        for bit in lows:
            got = swap_blk(values, bit)
            if anchor is not None:
                got = after(got, anchor)
            values = place(values, got, done, bit, lead)
            done = done + [bit]
        return values

    got_b = swap_blk(after(picked_b[1], mixed_own), team)
    pair_a = place(pair_a, after(pair_a_got, packed_kv), [team], bits[0], 1)
    pair_y_got = swap_blk(pair_a, lows[0])
    got_b, down_got = after((got_b, down_got), kv_all)
    kv_all = after(kv_all, (got_b, down_got, pair_y_got))
    down_here = place(down_here, down_got, [], bits[0])
    down_y_got = swap_blk(down_here, lows[0])
    down_here = place(down_here, down_y_got, [bits[0]], lows[0])
    for n in range(1, len(lows)):
        done = [bits[0]] + lows[:n]
        down_here = place(down_here, swap_blk(down_here, lows[n]), done, lows[n])
    down_here = down_here.reshape(2 * blk_count // 4, quarter, D)
    dy_first = swap_blk(dy_cross[:half], team)
    dy_second = swap_cross(dy_over[half:])
    out_ring = after(out_ring, packed_kv)
    out_strip = jnp.concatenate([out_ring[ring.index(b)] for b in range(blk_count)])
    out_cross = swap_cross(out_strip)
    out_core = swap_core(jnp.stack([out_strip, after(out_cross, kv_all)]))
    out_full = jnp.concatenate(by_place([out_strip, out_core[0], out_cross, out_core[1]]), axis=1)

    att_in, lse = attend(attend_ids, query, kv_all, seg_key, seg_query, block_len)
    pair_b = team_pair(picked_b[0], after(got_b, att_in))
    pair_b_got = swap_blk(pair_b, bits[0])
    flat = wide(flat_low)
    resid = flat + jnp.dot(att_in, out_full, preferred_element_type=jnp.float32)
    h_two = low(norm_apply(resid, gain_two))
    pair_a = place(pair_a, after(pair_y_got, h_two), [bits[0], team], lows[0], 1)
    for i in range(1, len(lows)):
        done = [bits[0], team] + lows[:i]
        pair_a = place(pair_a, swap_blk(pair_a, lows[i]), done, lows[i], 1)
    gate_up_a = pair_a.reshape(2, D, -1)
    pair_b_got = after(pair_b_got, (h_two, down_y_got))
    dy_first, dy_second = after((dy_first, dy_second), pair_b_got)
    dy_chip = jnp.concatenate([dy_low, dy_cross, dy_over, dy_first, dy_second])
    dy_team = jnp.concatenate([dy_chip, swap_core(dy_chip)])
    down_a = down_here[:, :size_first].reshape(widths[0], D)
    down_b = down_here[:, size_first:].reshape(widths[1], D)
    h_team = lax.all_gather(h_two, ("grp", "blk"), axis=0, tiled=True, axis_index_groups=teams)
    pair_b_got = after(pair_b_got, (h_two, gate_up_a))
    pair_b = place(pair_b, pair_b_got, [team], bits[0], 1)
    h_team = after(h_team, (gate_up_a, pair_b, dy_team))
    hidden_a, d_gate_a, d_up_a, *part_a = middle(order, h_team, dy_team, gate_up_a, down_a)
    gate_up_b = lows_of(pair_b, [bits[0], team], 1, hidden_a).reshape(2, D, -1)
    down_grad_a = down_grad(after(hidden_a, gate_up_b), dy_team)
    down_share_a = lax.psum_scatter(
        down_grad_a, "blk", scatter_dimension=0, axis_index_groups=peers, tiled=True
    )
    column_grad_a = two_grads(h_team, d_gate_a, d_up_a)

    def part_sent(values, axis, bit):
        mine = blk_bit(bit).astype(jnp.int32)
        keep = lax.dynamic_index_in_dim(values, mine, axis, keepdims=False)
        send = lax.dynamic_index_in_dim(values, 1 - mine, axis, keepdims=False)
        return keep, swap_blk(send, bit)

    def part_sum(keep, got):
        return low(wide(keep) + wide(got))

    def columns_first(grad):
        grad = grad.reshape((2, 2, 2) + low_shape + (weight_rows, -1))
        return part_sent(grad, 2 + len(lows), lows[-1])

    def columns_mid(keep, got):
        values = part_sum(keep, got)
        for i in range(len(lows) - 2, -1, -1):
            values = part_sum(*part_sent(values, 3 + i, lows[i]))
        return values

    def columns_third(keep, got):
        values = part_sum(keep, got)
        mine = lax.dynamic_index_in_dim(values, in_team, 1, keepdims=False)
        send = lax.dynamic_index_in_dim(values, 1 - in_team, 1, keepdims=False)
        return values, (mine, swap_blk(send, team))

    def rows_second(keep, got):
        values = part_sum(keep, got)
        for i in range(len(lows) - 2, -1, -1):
            values = part_sum(*part_sent(values, 1 + i, lows[i]))
        return part_sent(values, 0, bits[0])

    def columns_last(mine, got):
        return jnp.stack(
            [jnp.where(mine_team, got, mine), jnp.where(mine_team, mine, got)], axis=1
        )

    first_a = columns_first(column_grad_a)
    hidden_b, d_gate_b, d_up_b, d_here, d_there = middle(
        order, after(h_team, (column_grad_a, down_grad_a)), dy_team, gate_up_b, down_b, part_a
    )

    def chip_sum(values, came):
        return low(wide(values) + wide(came))

    def scatter_far(chip):
        far = chip[3 * token_count :]
        return swap_blk(far[:half], team), swap_cross(far[half:])

    def scatter_near(chip, first, second):
        cross, over = (chip[token_count * i : token_count * (i + 1)] for i in (1, 2))
        cross = jnp.concatenate([low(wide(cross[:half]) + wide(first)), cross[half:]])
        over = jnp.concatenate([over[:half], low(wide(over[half:]) + wide(second))])
        return swap_cross(cross), swap_blk(over, team)

    near_att_cross = swap_cross(after(att_in, hidden_a))
    d_there = after(d_there, (first_a[1], down_share_a, near_att_cross))
    d_came = swap_core(d_there)
    down_grad_b = down_grad(hidden_b, dy_team)
    rows_b = part_sent(
        down_grad_b.reshape((2,) + low_shape + (size_second, D)), len(lows), lows[-1]
    )
    mid_a = columns_mid(*after(first_a, d_came))
    second_a = part_sent(mid_a, 1, bits[0])
    d_chip = chip_sum(d_here, after(d_came, down_grad_b))
    d_far = scatter_far(d_chip)
    column_grad_b = two_grads(h_team, *after((d_gate_b, d_up_b), d_chip))
    first_b = columns_first(column_grad_b)
    d_far = after(d_far, column_grad_b)
    d_cross, d_over = scatter_near(d_chip, *d_far)
    out_part, out_there = down(*after((hidden_a, hidden_b), d_far), down_a, down_b, token_count)
    out_came = swap_core(out_there)
    d_cross, d_over = after((d_cross, d_over), out_part)
    d_htwo = wide(d_chip[:token_count]) + wide(d_cross) + wide(d_over)

    norm_value_two, norm_back_two = jax.vjp(norm_apply, resid, gain_two)
    d_resid_norm, grad_gain_two = norm_back_two(d_htwo)
    d_resid = wide(dy_low) + d_resid_norm
    d_att = low(d_resid)
    rows_b = rows_second(*after(rows_b, d_att))

    d_attended = low(right_transposed(d_att, out_full))
    own_angles = angles_of(positions)
    cosine, sine = jnp.cos(own_angles), jnp.sin(own_angles)
    d_query, dkv = attend_back(
        attend_ids,
        query,
        kv_all,
        seg_key,
        seg_query,
        att_in,
        d_attended,
        lse,
        jnp.concatenate([cosine, cosine], axis=1),
        jnp.concatenate([sine, sine], axis=1),
        block_len,
    )
    dkv = lax.psum_scatter(
        dkv.reshape(blk_count * token_count, 2 * KVD),
        ("grp", "blk"),
        scatter_dimension=0,
        axis_index_groups=ring_groups(blk_count),
        tiled=True,
    )
    down_share_b = part_sum(*after(rows_b, d_query))
    sum_a, third_a = columns_third(*after(second_a, d_att))

    def to_strips(parts):
        return jnp.concatenate(exchange_near(by_place(parts)))

    near_dq = to_strips([d_query[:, strip_q * k : strip_q * (k + 1)] for k in range(4)])
    block_shape = (2,) * len(bits) + (weight_rows, -1)
    query_grad = low(left_product(near_one, near_dq)).reshape(block_shape)

    near_att = swap_core(jnp.stack([att_in, near_att_cross]))
    near_att = jnp.concatenate([att_in, near_att[0], near_att_cross, near_att[1]])
    near_datt = to_strips([d_att[:, strip_q * k : strip_q * (k + 1)] for k in range(4)])
    out_grad = low(left_product(near_att, after(near_datt, d_attended))).reshape(block_shape)
    query_out = jnp.concatenate([query_grad, out_grad], axis=-1)
    steps_query = part_sent(query_out, len(bits) - 1, bits[-1])
    second_b = part_sent(columns_mid(*after(first_b, d_query)), 1, bits[0])
    dkv = after(dkv, down_share_b)
    own_part, core_part, far_part, bias_kv = turn_dkv(
        ids, dkv, jnp.concatenate([cosine, cosine], axis=1), jnp.concatenate([sine, sine], axis=1)
    )
    bias_q = jnp.sum(wide(d_query), axis=0)
    d_key = own_part
    cross_part = swap_cross(far_part)
    own_a = columns_last(*after(third_a, own_part))
    core_part = swap_core(jnp.stack([core_part, cross_part[1]]))
    kv_grad, hone_here, hone_there = make_kv_grad(
        blk_count,
        weight_rows,
        small_count,
        own_part,
        cross_part,
        core_part,
        near_dq,
        near_one,
        token_send,
        token_cross,
        token_core,
        strip,
        grad_gain_two[None],
        bias_q[None],
        bias_kv,
    )
    vector_rows = -(-small_count // HD)
    kv_grad = kv_grad.reshape((2,) * len(bits) + kv_grad.shape[1:])
    steps_kv = part_sent(kv_grad, len(bits) - 1, bits[-1])
    share_down = after(jnp.concatenate([down_share_a, down_share_b]), dkv)
    grad_down = lax.all_gather(share_down, "grp", axis=0, tiled=True)
    marks = [hone_there]
    for i in range(len(bits) - 2, -1, -1):
        kv_sum = part_sum(*steps_kv)
        steps_kv = part_sent(kv_sum, i, bits[i])
        marks.append(kv_sum)
    near_a = gather_near_stacked(after(own_a, marks[-1]))
    for n, i in enumerate(range(len(bits) - 2, -1, -1)):
        steps_query = part_sent(part_sum(*after(steps_query, marks[n + 1])), i, bits[i])
    sum_b, third_b = columns_third(*after(second_b, marks[-1]))
    share_kv_all = wide(steps_kv[0]) + wide(steps_kv[1])
    share_kv = low(share_kv_all[:weight_rows])
    vector_part = share_kv_all[weight_rows : weight_rows + vector_rows]
    share_query_out = part_sum(*after(steps_query, marks[-1]))

    other = wide(swap_core(hone_there))
    d_hone = wide(hone_here[:token_count]) + other[:token_count]
    d_hone_send = low(wide(hone_here[token_count:]) + other[token_count:])
    d_hone_cross = swap_cross(d_hone_send)
    square_sum = square_total(
        [
            wide(s)
            for s in (share_query_out, share_kv, sum_a, sum_b, share_down)
        ]
    )
    packed = jnp.concatenate([vector_part, jnp.full((8, HD), square_sum)])
    packed = after(packed, (d_hone_send, d_hone))
    packed = packed + swap_cross(packed)
    packed = packed + swap_core(packed)
    parts = gather_grp(after(jnp.concatenate([share_query_out, share_kv], axis=1), packed))
    grad_out = jnp.concatenate([part[:, strip_q : 2 * strip_q] for part in parts], axis=1)
    grad_attend = jnp.concatenate(
        [part[:, :strip_q] for part in parts] + [parts[k][:, 2 * strip_q :] for k in (0, 2, 1, 3)],
        axis=1,
    )
    share_vector = packed[:vector_rows].reshape(-1)[:small_count]
    square_sum = packed[vector_rows:] + jnp.sum(share_vector * share_vector)
    square_sum = after(square_sum, third_b[1])
    for bit in bits:
        square_sum = square_sum + swap_blk(square_sum, bit)
    grad_norm = jnp.sqrt(square_sum[0, 0])
    factor = jnp.minimum(1.0, CLIP_NORM / (grad_norm + 1e-06))
    out_chip = chip_sum(out_part, after(out_came, marks[1]))
    out_far = scatter_far(out_chip)
    factor = after(factor, (out_chip, near_a))

    new_first_attend, new_second_attend, new_attend = adam_step(
        w_attend, factor * wide(grad_attend), first_attend, second_attend, RATE_ATTEND, WEIGHT_DECAY
    )
    new_first_out, new_second_out, new_out = adam_step(
        w_out, factor * wide(grad_out), first_out, second_out, RATE_OUT, WEIGHT_DECAY
    )
    new_first_down, new_second_down, new_down = adam_step(
        w_down, factor * wide(grad_down), first_down, second_down, RATE_DOWN, WEIGHT_DECAY
    )
    own_b = columns_last(*third_b)
    cross_b = after(swap_cross(own_b), new_down)
    near_b = jnp.stack([own_b, cross_b])
    near_b = [near_b, swap_core(near_b)]
    new_first_gate, new_second_gate, new_gate = adam_columns(
        0, ids, factor[None], near_a, near_b, w_gate, first_gate, second_gate, blk_count, RATE_GATE, WEIGHT_DECAY
    )
    new_first_up, new_second_up, new_up = adam_columns(
        1, ids, factor[None], near_a, near_b, w_up, first_up, second_up, blk_count, RATE_GATE, WEIGHT_DECAY
    )
    norm_value_one, norm_back_one = jax.vjp(norm_apply, flat, gain_one)
    d_hone = after(d_hone + wide(after(d_hone_cross, new_gate)), new_gate)
    d_flat_norm, unused_gain = norm_back_one(d_hone)
    grad_tokens = low(d_resid + d_flat_norm)

    new_first_small, new_second_small, new_small = adam_step(
        small_params, factor * share_vector, first_small, second_small, RATE_VECTOR, 0.0
    )

    out_near = after(scatter_near(out_chip, *after(out_far, factor)), (new_gate, new_up))
    out_tokens = low(resid + wide(out_chip[:token_count]) + wide(out_near[0]) + wide(out_near[1]))
    return (
        out_tokens.reshape(rows_here, block_len, D),
        grad_tokens.reshape(rows_here, block_len, D),
        grad_norm,
        new_first_attend,
        new_second_attend,
        new_attend,
        new_first_out,
        new_second_out,
        new_out,
        new_first_gate,
        new_second_gate,
        new_gate,
        new_first_up,
        new_second_up,
        new_up,
        new_first_down,
        new_second_down,
        new_down,
        new_first_small,
        new_second_small,
        new_small,
    )


def solution(mesh):
    placed = (
        P("grp", "blk", None),
        P("grp", "blk", None),
        P("grp", "blk"),
        P("grp", "blk"),
        P("blk", None),
        P("blk", None),
        P("blk", None),
        P("blk", None),
        P("blk", None),
        P("blk"),
        P("blk", None),
        P("blk", None),
        P("blk", None),
        P("blk", None),
        P("blk", None),
        P("blk"),
        P("blk", None),
        P("blk", None),
        P("blk", None),
        P("blk", None),
        P("blk", None),
        P("blk"),
    )
    return jax.shard_map(
        on_device,
        mesh=mesh,
        in_specs=placed,
        out_specs=(
            P("grp", "blk", None),
            P("grp", "blk", None),
            P(),
            P("blk", None),
            P("blk", None),
            P("blk", None),
            P("blk", None),
            P("blk", None),
            P("blk", None),
            P("blk", None),
            P("blk", None),
            P("blk", None),
            P("blk", None),
            P("blk", None),
            P("blk", None),
            P("blk", None),
            P("blk", None),
            P("blk", None),
            P("blk"),
            P("blk"),
            P("blk"),
        ),
        check_vma=False,
    )
```

```python
import functools

import jax
import jax.numpy as jnp
from jax import lax
from jax.experimental import pallas as pl
from jax.experimental.pallas import tpu as pltpu
from jax.sharding import PartitionSpec as P

D = 1536
FF = 8960
H = 12
KVH = 2
HD = 128
STEP = 10
HQD = 1536
KVD = 256


NORM_EPS = 1e-06
ROPE_BASE = 10000.0
CLIP_NORM = 1.0
BETA_FIRST = 0.9
BETA_SECOND = 0.95
ADAM_EPS = 1e-08
WEIGHT_DECAY = 0.1
RATE_ATTEND = 0.06
RATE_OUT = 0.5
RATE_GATE = 0.06
RATE_DOWN = 0.03
RATE_VECTOR = 0.5
NEG_LARGE = -1e30
LOG2E = 1.4426950408889634
VMEM = 48 * 1024 * 1024
SMALL_COST = pl.CostEstimate(flops=1000, bytes_accessed=1000, transcendentals=0)


def norm_apply(values, gain):
    return values * lax.rsqrt(jnp.mean(values * values, axis=-1, keepdims=True) + NORM_EPS) * gain


def swish_product(gate, up_proj):
    return jax.nn.silu(gate) * up_proj


def left_product(left_side, right_side):
    return lax.dot_general(
        left_side, right_side, (((0,), (0,)), ((), ())), preferred_element_type=jnp.float32
    )


def right_transposed(left_side, right_side):
    return lax.dot_general(
        left_side, right_side, (((1,), (1,)), ((), ())), preferred_element_type=jnp.float32
    )


def square_total(arrays):
    return sum((jnp.sum(member * member) for member in arrays))


def adam_step(weight, grad, first, second, rate, decay):
    first_new = BETA_FIRST * first + (1.0 - BETA_FIRST) * grad
    second_new = BETA_SECOND * second + (1.0 - BETA_SECOND) * grad * grad
    first_hat = first_new / (1.0 - BETA_FIRST**STEP)
    second_hat = second_new / (1.0 - BETA_SECOND**STEP)
    weight_new = weight - rate * (first_hat / (jnp.sqrt(second_hat) + ADAM_EPS) + decay * weight)
    return (first_new, second_new, weight_new)


def ring_order(count):
    return list(range(0, count, 2)) + list(range(count - 1, 0, -2))


def halves_of(quarter):
    first = quarter * 16 // 35
    return ((0, first), (first, quarter - first))


def pick_body(blk_count, ids, gate_ref, up_ref, *out_refs):
    quarter = FF // blk_count // 4
    per = blk_count // 4
    for k in range(4):

        @pl.when(ids[0] == k)
        def _(k=k):
            for (at, size), out_ref in zip(halves_of(quarter), out_refs):
                for which, src in enumerate((gate_ref, up_ref)):
                    for bit in range(2):
                        parts = []
                        for high in range(2):
                            for small in range(per):
                                begin = (((high * 2 + bit) * per + small) * 4 + k) * quarter + at
                                parts.append(src[:, begin : begin + size])
                        out_ref[ids[1] ^ bit, which] = jnp.concatenate(parts, axis=1).astype(
                            jnp.bfloat16
                        )


def pick_columns(ids, gate, up, blk_count):
    rows = gate.shape[0]
    step = 48 if rows % 48 == 0 else rows
    widths = [size * blk_count // 2 for at, size in halves_of(FF // blk_count // 4)]
    spec = pl.BlockSpec((step, FF), lambda i, ids: (i, 0))
    return pl.pallas_call(
        functools.partial(pick_body, blk_count),
        grid_spec=pltpu.PrefetchScalarGridSpec(
            num_scalar_prefetch=1,
            grid=(rows // step,),
            in_specs=[spec, spec],
            out_specs=[pl.BlockSpec((2, 2, step, w), lambda i, ids: (0, 0, i, 0)) for w in widths],
        ),
        out_shape=[jax.ShapeDtypeStruct((2, 2, rows, w), jnp.bfloat16) for w in widths],
        compiler_params=pltpu.CompilerParams(vmem_limit_bytes=VMEM),
        cost_estimate=SMALL_COST,
        name="pick_columns",
    )(ids, gate, up)


def adam_body(blk_count, rate, decay, ids, factor_ref, first_ref, first_far_ref, second_ref, second_far_ref, w_ref, m_ref, v_ref, m_out, v_out, w_out):
    per = blk_count // 4
    sizes = [size for at, size in halves_of(FF // blk_count // 4)]
    grads = []
    for near_ref, far_ref in ((first_ref, first_far_ref), (second_ref, second_far_ref)):
        by_grp = []
        for k in range(4):
            away = ids[0] ^ k
            bits_of_k = []
            for bit in range(2):
                near = near_ref[away >> 1, bit].astype(jnp.float32)
                far = far_ref[away >> 1, bit].astype(jnp.float32)
                bits_of_k.append(jnp.where((away & 1) == 1, far, near))
            by_grp.append(bits_of_k)
        grads.append(by_grp)
    parts = []
    for high in range(2):
        for bit in range(2):
            for small in range(per):
                place = high * per + small
                for k in range(4):
                    for part, size in zip(grads, sizes):
                        parts.append(part[k][bit][:, place * size : (place + 1) * size])
    grad = jnp.concatenate(parts, axis=1) * factor_ref[0]
    m, v, w = adam_step(w_ref[...], grad, m_ref[...], v_ref[...], rate, decay)
    m_out[...] = m
    v_out[...] = v
    w_out[...] = w


def adam_columns(which, ids, factor, first, second, w, m, v, blk_count, rate, decay):
    rows = w.shape[0]
    step = 96 if rows % 96 == 0 else rows
    spec = pl.BlockSpec((step, FF), lambda i, ids: (i, 0))
    shape = jax.ShapeDtypeStruct((rows, FF), jnp.float32)
    grads = [
        pl.BlockSpec((2, None, 2, step, g.shape[-1]), lambda i, ids: (0, which, 0, i, 0))
        for g in first + second
    ]
    return pl.pallas_call(
        functools.partial(adam_body, blk_count, rate, decay),
        grid_spec=pltpu.PrefetchScalarGridSpec(
            num_scalar_prefetch=1,
            grid=(rows // step,),
            in_specs=[pl.BlockSpec(memory_space=pltpu.SMEM)] + grads + [spec, spec, spec],
            out_specs=[spec, spec, spec],
        ),
        out_shape=[shape] * 3,
        compiler_params=pltpu.CompilerParams(vmem_limit_bytes=VMEM),
        cost_estimate=SMALL_COST,
        name="adam_columns",
    )(ids, factor, *first, *second, w, m, v)


def nt(a, b, **kw):
    return lax.dot_general(a, b, (((1,), (1,)), ((), ())), preferred_element_type=jnp.float32, **kw)

def tn(a, b, **kw):
    return lax.dot_general(a, b, (((0,), (0,)), ((), ())), preferred_element_type=jnp.float32, **kw)

def stack_heads(ref, kvh, group):
    return jnp.concatenate([ref[:, HD * (kvh * group + i): HD * (kvh * group + i + 1)] for i in range(group)], axis=0)

def hidden_from(seg_key_ref, seg_query_ref, first, chunk, block_len, blk):
    key = first + lax.broadcasted_iota(jnp.int32, (chunk, block_len), 0)
    query = blk * block_len + lax.broadcasted_iota(jnp.int32, (chunk, block_len), 1)
    seg_key = seg_key_ref[pl.ds(first, chunk), :]
    counts = jnp.logical_and(key <= query, seg_key == seg_query_ref[0:1, :])
    return jnp.where(counts, 0.0, NEG_LARGE)

def ring_pair(ref, c, at):
    return jnp.concatenate(
        [ref[c, :, at : at + HD], ref[ref.shape[0] - 1 - c, :, at : at + HD]], axis=0
    )


def attend_body(chunk, ids, q_ref, k_ref, v_ref, seg_key_ref, seg_query_ref, o_ref, lse_ref, m_s, l_s, acc_s):
    block_len = q_ref.shape[0]
    group = H // KVH
    row = pl.program_id(0)
    per = chunk // block_len
    scale = HD ** (-0.5) * LOG2E
    start = ids[1 + row] // per
    stop = ids[0] // per + 1
    for kvh in range(KVH):
        q = stack_heads(q_ref, kvh, group)
        m_s[...] = jnp.full_like(m_s, NEG_LARGE)
        l_s[...] = jnp.zeros_like(l_s)
        acc_s[...] = jnp.zeros_like(acc_s)

        def step(c, carry):
            keys = ring_pair(k_ref, c, HD * kvh)
            vals = ring_pair(v_ref, c, HD * kvh)
            bias = hidden_from(seg_key_ref, seg_query_ref, c * chunk, chunk, block_len, ids[0])
            s = nt(keys, q) * scale + jnp.concatenate([bias] * group, axis=1)
            old = m_s[0:1, :]
            new = jnp.maximum(old, jnp.max(s, axis=0, keepdims=True))
            p = jnp.exp2(s - new)
            fade = jnp.exp2(old - new)
            l_s[0:1, :] = l_s[0:1, :] * fade + jnp.sum(p, axis=0, keepdims=True)
            acc_s[...] = acc_s[...] * fade + tn(vals, p.astype(jnp.bfloat16))
            m_s[0:1, :] = new
            return carry

        lax.fori_loop(start, stop, step, 0)
        total = l_s[0:1, :]
        out = (acc_s[...] * (1.0 / total)).T
        for i in range(group):
            o_ref[:, HD * (kvh * group + i): HD * (kvh * group + i + 1)] = out[block_len * i: block_len * (i + 1), :].astype(jnp.bfloat16)
        lse_ref[kvh] = jnp.broadcast_to(m_s[0:1, :] + jnp.log2(total), (8, group * block_len))

def attend(ids, q, kv, seg_key, seg_query, block_len):
    blk_count, rows = kv.shape[:2]
    group = H // KVH
    chunk = 2 * block_len
    many = group * block_len
    return pl.pallas_call(
        functools.partial(attend_body, chunk),
        grid_spec=pltpu.PrefetchScalarGridSpec(
            num_scalar_prefetch=1, grid=(rows,),
            in_specs=[
                pl.BlockSpec((block_len, HQD), lambda r, ids: (r, 0)),
                pl.BlockSpec((blk_count, None, block_len, KVD), lambda r, ids: (0, r, 0, 0)),
                pl.BlockSpec((blk_count, None, block_len, KVD), lambda r, ids: (0, r, 0, 1)),
                pl.BlockSpec((None, blk_count * block_len, HD), lambda r, ids: (r, 0, 0)),
                pl.BlockSpec((None, 8, block_len), lambda r, ids: (r, 0, 0)),
            ],
            out_specs=[
                pl.BlockSpec((block_len, HQD), lambda r, ids: (r, 0)),
                pl.BlockSpec((None, KVH, 8, many), lambda r, ids: (r, 0, 0, 0)),
            ],
            scratch_shapes=[pltpu.VMEM((8, many), jnp.float32), pltpu.VMEM((8, many), jnp.float32), pltpu.VMEM((HD, many), jnp.float32)]),
        out_shape=[
            jax.ShapeDtypeStruct((rows * block_len, HQD), jnp.bfloat16),
            jax.ShapeDtypeStruct((rows, KVH, 8, many), jnp.float32),
        ],
        compiler_params=pltpu.CompilerParams(vmem_limit_bytes=VMEM),
        cost_estimate=SMALL_COST,
        name="attend",
    )(ids, q, kv, kv, seg_key, seg_query)

def turn_back(u, cosine, sine):
    lane = lax.broadcasted_iota(jnp.int32, u.shape, 1)
    other = pltpu.roll(u, HD // 2, 1)
    return u * cosine + jnp.where(lane < HD // 2, other, -other) * sine

def attend_back_body(chunk, ids, q_ref, k_ref, v_ref, seg_key_ref, seg_query_ref, o_ref, do_ref, lse_ref, cos_ref, sin_ref, dq_ref, dkv_ref, dq_s):
    block_len = q_ref.shape[0]
    group = H // KVH
    row = pl.program_id(0)
    per = chunk // block_len
    plain = HD ** (-0.5)
    scale = plain * LOG2E
    start = ids[1 + row] // per
    stop = ids[0] // per + 1
    dkv_ref[...] = jnp.zeros_like(dkv_ref)
    for kvh in range(KVH):
        q = stack_heads(q_ref, kvh, group)
        do = stack_heads(do_ref, kvh, group)
        o = stack_heads(o_ref, kvh, group)
        both = do.astype(jnp.float32) * o.astype(jnp.float32)
        delta = nt(jnp.ones((8, HD), jnp.float32), both, precision=lax.Precision.HIGHEST)[0:1, :]
        lse = lse_ref[kvh][0:1, :]
        dq_s[...] = jnp.zeros_like(dq_s)

        def step(c, carry):
            keys = ring_pair(k_ref, c, HD * kvh)
            vals = ring_pair(v_ref, c, HD * kvh)
            bias = hidden_from(seg_key_ref, seg_query_ref, c * chunk, chunk, block_len, ids[0])
            s = nt(keys, q) * scale + jnp.concatenate([bias] * group, axis=1)
            p = jnp.exp2(s - lse)
            dp = nt(vals, do)
            ds = (p * (dp - delta)).astype(jnp.bfloat16)
            dk = jnp.dot(ds, q, preferred_element_type=jnp.float32) * plain
            dv = jnp.dot(p.astype(jnp.bfloat16), do, preferred_element_type=jnp.float32)
            for at, part in ((HD * kvh, dk.astype(jnp.bfloat16)), (KVD + HD * kvh, dv.astype(jnp.bfloat16))):
                dkv_ref[c, :, at : at + HD] = part[:block_len]
                dkv_ref[dkv_ref.shape[0] - 1 - c, :, at : at + HD] = part[block_len:]
            dq_s[...] += tn(ds, keys)
            return carry

        lax.fori_loop(start, stop, step, 0)
        cosine, sine = cos_ref[...], sin_ref[...]
        for i in range(group):
            u = dq_s[block_len * i: block_len * (i + 1), :] * plain
            at = HD * (kvh * group + i)
            dq_ref[:, at: at + HD] = turn_back(u, cosine, sine).astype(jnp.bfloat16)

def attend_back(ids, q, kv, seg_key, seg_query, o, do, lse, cosine, sine, block_len):
    blk_count, rows = kv.shape[:2]
    group = H // KVH
    chunk = 2 * block_len
    many = group * block_len
    per_row = pl.BlockSpec((block_len, HQD), lambda r, ids: (r, 0))
    turn = pl.BlockSpec((block_len, HD), lambda r, ids: (r, 0))
    return pl.pallas_call(
        functools.partial(attend_back_body, chunk),
        grid_spec=pltpu.PrefetchScalarGridSpec(
            num_scalar_prefetch=1, grid=(rows,),
            in_specs=[
                per_row,
                pl.BlockSpec((blk_count, None, block_len, KVD), lambda r, ids: (0, r, 0, 0)),
                pl.BlockSpec((blk_count, None, block_len, KVD), lambda r, ids: (0, r, 0, 1)),
                pl.BlockSpec((None, blk_count * block_len, HD), lambda r, ids: (r, 0, 0)),
                pl.BlockSpec((None, 8, block_len), lambda r, ids: (r, 0, 0)),
                per_row, per_row,
                pl.BlockSpec((None, KVH, 8, many), lambda r, ids: (r, 0, 0, 0)),
                turn, turn,
            ],
            out_specs=[per_row, pl.BlockSpec((blk_count, None, block_len, 2 * KVD), lambda r, ids: (0, r, 0, 0))],
            scratch_shapes=[pltpu.VMEM((many, HD), jnp.float32)]),
        out_shape=[
            jax.ShapeDtypeStruct((rows * block_len, HQD), jnp.bfloat16),
            jax.ShapeDtypeStruct((blk_count, rows, block_len, 2 * KVD), jnp.bfloat16),
        ],
        compiler_params=pltpu.CompilerParams(vmem_limit_bytes=VMEM),
        cost_estimate=SMALL_COST,
        name="attend_back",
    )(ids, q, kv, kv, seg_key, seg_query, o, do, lse, cosine, sine)

def nn(a, b):
    return jnp.dot(a, b, preferred_element_type=jnp.float32)


def middle_body(add, order, h_ref, dy_ref, wg_ref, wu_ref, wd_ref, *refs):
    prev_refs = refs[:2] if add else None
    hid_ref, dg_ref, du_ref, dh_ref, dh_far_ref = refs[-5:]
    here = pl.program_id(0) < 4
    h = h_ref[...]
    gate = nn(h, wg_ref[...])
    up = nn(h, wu_ref[...])
    sig = 1.0 / (1.0 + jnp.exp(-gate))
    silu = gate * sig
    hid_ref[...] = (silu * up).astype(jnp.bfloat16)
    dhid = nt(dy_ref[...], wd_ref[...])
    dg = (dhid * up * sig * (1.0 + gate * (1.0 - sig))).astype(jnp.bfloat16)
    du = (dhid * silu).astype(jnp.bfloat16)
    dg_ref[...] = dg
    du_ref[...] = du
    dh = nt(dg, wg_ref[...]) + nt(du, wu_ref[...])
    if add:
        prev = jnp.where(here, prev_refs[0][...].astype(jnp.float32), prev_refs[1][...].astype(jnp.float32))
        dh = dh + prev
    dh = dh.astype(jnp.bfloat16)

    @pl.when(here)
    def _():
        dh_ref[...] = dh

    @pl.when(jnp.logical_not(here))
    def _():
        dh_far_ref[...] = dh


def middle(order, h, dy, gate_up, wd, prev=None):
    count = h.shape[0]
    step = count // order.shape[0]
    wide_here = wd.shape[0]
    row = pl.BlockSpec((step, D), lambda i, order: (i, 0))
    placed = pl.BlockSpec((step, D), lambda i, order: (order[i], 0))
    part = pl.BlockSpec((step, wide_here), lambda i, order: (i, 0))
    part_placed = pl.BlockSpec((step, wide_here), lambda i, order: (order[i], 0))
    once = pl.Buffered(1)
    extra = [] if prev is None else list(prev)
    near = pl.BlockSpec((step, D), lambda i, order: (jnp.minimum(i, 3), 0))
    far = pl.BlockSpec((step, D), lambda i, order: (jnp.maximum(i - 4, 0), 0))
    return pl.pallas_call(
        functools.partial(middle_body, prev is not None),
        grid_spec=pltpu.PrefetchScalarGridSpec(
            num_scalar_prefetch=1,
            grid=(count // step,),
            in_specs=[
                placed,
                row,
                pl.BlockSpec((None, D, wide_here), lambda i, order: (0, 0, 0), pipeline_mode=once),
                pl.BlockSpec((None, D, wide_here), lambda i, order: (1, 0, 0), pipeline_mode=once),
                pl.BlockSpec((wide_here, D), lambda i, order: (0, 0), pipeline_mode=once),
            ]
            + [near, far][: len(extra)],
            out_specs=[part, part_placed, part_placed, near, far],
        ),
        out_shape=[jax.ShapeDtypeStruct((count, wide_here), jnp.bfloat16)] * 3
        + [jax.ShapeDtypeStruct((count // 2, D), jnp.bfloat16)] * 2,
        compiler_params=pltpu.CompilerParams(vmem_limit_bytes=VMEM),
        cost_estimate=SMALL_COST,
        name="middle",
    )(order, h, dy, gate_up, gate_up, wd, *extra)


def two_grads_body(h_ref, a_ref, b_ref, out_ref):
    h = h_ref[...]
    out_ref[0] = tn(h, a_ref[...]).astype(jnp.bfloat16)
    out_ref[1] = tn(h, b_ref[...]).astype(jnp.bfloat16)


def two_grads(h, a, b, step=256):
    count = h.shape[0]
    wide_here = a.shape[1]
    whole = pl.BlockSpec(a.shape, lambda i: (0, 0), pipeline_mode=pl.Buffered(1))
    return pl.pallas_call(
        two_grads_body,
        grid=(D // step,),
        in_specs=[pl.BlockSpec((count, step), lambda i: (0, i)), whole, whole],
        out_specs=pl.BlockSpec((2, step, wide_here), lambda i: (0, i, 0)),
        out_shape=jax.ShapeDtypeStruct((2, D, wide_here), jnp.bfloat16),
        compiler_params=pltpu.CompilerParams(vmem_limit_bytes=VMEM),
        cost_estimate=SMALL_COST,
        name="two_grads",
    )(h, a, b)


def down_grad_body(hid_ref, dy_ref, g_ref):
    g_ref[...] = tn(hid_ref[...], dy_ref[...]).astype(jnp.bfloat16)

def down_grad(hid, dy, step=512):
    T, F = hid.shape
    D = dy.shape[1]
    return pl.pallas_call(down_grad_body, grid=(D // step,),
        in_specs=[pl.BlockSpec((T, F), lambda i: (0, 0), pipeline_mode=pl.Buffered(1)), pl.BlockSpec((T, step), lambda i: (0, i))],
        out_specs=pl.BlockSpec((F, step), lambda i: (0, i)),
        out_shape=jax.ShapeDtypeStruct((F, D), jnp.bfloat16),
        compiler_params=pltpu.CompilerParams(vmem_limit_bytes=VMEM),
        cost_estimate=SMALL_COST,
        name="down_grad")(hid, dy)

def down_body(hid_a_ref, hid_b_ref, wd_a_ref, wd_b_ref, o_ref, o_far_ref):
    out = nn(hid_a_ref[...], wd_a_ref[...]) + nn(hid_b_ref[...], wd_b_ref[...])
    out = out.astype(jnp.bfloat16)
    here = pl.program_id(0) < 4

    @pl.when(here)
    def _():
        o_ref[...] = out

    @pl.when(jnp.logical_not(here))
    def _():
        o_far_ref[...] = out


def down(hid_a, hid_b, wd_a, wd_b, step):
    count = hid_a.shape[0]

    def rows(array):
        return pl.BlockSpec((step, array.shape[1]), lambda i: (i, 0))

    def whole(array):
        return pl.BlockSpec(array.shape, lambda i: (0, 0), pipeline_mode=pl.Buffered(1))

    return pl.pallas_call(
        down_body,
        grid=(count // step,),
        in_specs=[rows(hid_a), rows(hid_b), whole(wd_a), whole(wd_b)],
        out_specs=[
            pl.BlockSpec((step, D), lambda i: (jnp.minimum(i, 3), 0)),
            pl.BlockSpec((step, D), lambda i: (jnp.maximum(i - 4, 0), 0)),
        ],
        out_shape=[jax.ShapeDtypeStruct((count // 2, D), jnp.bfloat16)] * 2,
        compiler_params=pltpu.CompilerParams(vmem_limit_bytes=VMEM),
        cost_estimate=SMALL_COST,
        name="down",
    )(hid_a, hid_b, wd_a, wd_b)


def turn(u, cosine, sine):
    lane = lax.broadcasted_iota(jnp.int32, u.shape, 1)
    other = pltpu.roll(u, HD // 2, 1)
    return u * cosine + jnp.where(lane < HD // 2, -other, other) * sine


def mix_body(
    blk_count, rows, small_count, ids, own_ref, cross_ref, core_ref, ring_ref, freq_ref,
    self_ref, near_ref, far_ref, one_ref, strip_ref, vector_ref,
):
    ring = ring_order(blk_count)
    wide_here = ring_ref.shape[-1]
    pieces = []
    for b in range(blk_count):
        at = ring.index(b)
        strip_ref[rows * b : rows * (b + 1)] = ring_ref[at, :rows]
        left = small_count
        line = rows
        while left > 0:
            size = min(left, wide_here)
            pieces.append(ring_ref[at, line : line + 1, :size].astype(jnp.float32))
            left -= size
            line += 1
    vector = jnp.concatenate(pieces, axis=1)
    vector_ref[...] = vector
    gain = vector[:, :D]
    grp = ids[0]
    strip_q = wide_here - HD
    bias = jnp.zeros((1, wide_here), jnp.float32)
    for k in range(4):
        kv_at = 2 * D + HQD + HD * (k // 2) + KVD * (k % 2)
        part = jnp.concatenate(
            [
                vector[:, 2 * D + strip_q * k : 2 * D + strip_q * (k + 1)],
                vector[:, kv_at : kv_at + HD],
            ],
            axis=1,
        )
        bias = bias + jnp.where(grp == k, part, 0.0)
    count = own_ref.shape[0]
    strip = strip_ref[...]
    for d in range(4):
        source = (own_ref[...], core_ref[0], cross_ref[...], core_ref[1])[d]
        x = source[:, :D].astype(jnp.float32)
        root = lax.rsqrt(jnp.mean(x * x, axis=1, keepdims=True) + NORM_EPS)
        one = (x * root * gain).astype(jnp.bfloat16)
        one_ref[count * d : count * (d + 1)] = one
        mixed = nn(one, strip) + bias
        digits = source[:, D : D + HD].astype(jnp.float32)
        position = 64.0 * digits[:, 0:1] + digits[:, 1:2]
        angles = position * freq_ref[...]
        cosine, sine = jnp.cos(angles), jnp.sin(angles)
        for i in range(wide_here // HD):
            c, s = cosine, sine
            if i == wide_here // HD - 1:
                c = jnp.where(grp % 2 == 1, 1.0, c)
                s = jnp.where(grp % 2 == 1, 0.0, s)
            at = HD * i
            out = turn(mixed[:, at : at + HD], c, s).astype(jnp.bfloat16)
            if d == 0:
                self_ref[:, at : at + HD] = out
            elif d == 1:
                near_ref[:, at : at + HD] = out
            else:
                far_ref[d - 2, :, at : at + HD] = out


def mix(ids, own, cross, core, ring, freq, blk_count, rows, small_count):
    count = own.shape[0]
    wide_here = ring.shape[-1]
    low16 = jnp.bfloat16
    return pl.pallas_call(
        functools.partial(mix_body, blk_count, rows, small_count),
        in_specs=[pl.BlockSpec(memory_space=pltpu.SMEM)] + [pl.BlockSpec(memory_space=pltpu.VMEM)] * 5,
        out_specs=[pl.BlockSpec(memory_space=pltpu.VMEM)] * 6,
        out_shape=[
            jax.ShapeDtypeStruct((count, wide_here), low16),
            jax.ShapeDtypeStruct((count, wide_here), low16),
            jax.ShapeDtypeStruct((2, count, wide_here), low16),
            jax.ShapeDtypeStruct((4 * count, D), low16),
            jax.ShapeDtypeStruct((D, wide_here), low16),
            jax.ShapeDtypeStruct((1, blk_count * small_count), jnp.float32),
        ],
        compiler_params=pltpu.CompilerParams(vmem_limit_bytes=VMEM),
        cost_estimate=SMALL_COST,
        name="mix",
    )(ids, own, cross, core, ring, freq)


def pack_body(ids, self_ref, cross_ref, core_ref, q_ref, kv_ref):
    strip_q = self_ref.shape[1] - HD
    for g in range(4):

        @pl.when(ids[0] == g)
        def _(g=g):
            for k in range(4):
                part = (self_ref[...], core_ref[0], cross_ref[0], core_ref[1])[g ^ k]
                q_ref[:, strip_q * k : strip_q * (k + 1)] = part[:, :strip_q]
                at = (k % 2) * KVD + (k // 2) * HD
                kv_ref[:, at : at + HD] = part[:, strip_q:]


def pack(ids, own, cross, core):
    count = own.shape[0]
    return pl.pallas_call(
        pack_body,
        in_specs=[pl.BlockSpec(memory_space=pltpu.SMEM)] + [pl.BlockSpec(memory_space=pltpu.VMEM)] * 3,
        out_specs=[pl.BlockSpec(memory_space=pltpu.VMEM)] * 2,
        out_shape=[
            jax.ShapeDtypeStruct((count, HQD), jnp.bfloat16),
            jax.ShapeDtypeStruct((count, 2 * KVD), jnp.bfloat16),
        ],
        compiler_params=pltpu.CompilerParams(vmem_limit_bytes=VMEM),
        cost_estimate=SMALL_COST,
        name="pack",
    )(ids, own, cross, core)


def turn_dkv_body(ids, dkv_ref, cos_ref, sin_ref, self_ref, near_ref, far_ref, sum_ref):
    items = []
    sums = [None] * 4
    for k in range(4):
        at = (k % 2) * KVD + (k // 2) * HD
        part = dkv_ref[:, at : at + HD]
        if k % 2 == 0:
            part = turn_back(part.astype(jnp.float32), cos_ref[...], sin_ref[...]).astype(jnp.bfloat16)
        items.append(part)
        sums[(k % 2) * 2 + k // 2] = jnp.sum(part.astype(jnp.float32), axis=0, keepdims=True)
    sum_ref[...] = jnp.concatenate(sums, axis=1)
    for g in range(4):

        @pl.when(ids[0] == g)
        def _(g=g):
            self_ref[...] = items[g]
            near_ref[...] = items[g ^ 1]
            far_ref[0] = items[g ^ 2]
            far_ref[1] = items[g ^ 3]


def turn_dkv(ids, dkv, cosine, sine):
    count = dkv.shape[0]
    return pl.pallas_call(
        turn_dkv_body,
        in_specs=[pl.BlockSpec(memory_space=pltpu.SMEM)] + [pl.BlockSpec(memory_space=pltpu.VMEM)] * 3,
        out_specs=[pl.BlockSpec(memory_space=pltpu.VMEM)] * 4,
        out_shape=[
            jax.ShapeDtypeStruct((count, HD), jnp.bfloat16),
            jax.ShapeDtypeStruct((count, HD), jnp.bfloat16),
            jax.ShapeDtypeStruct((2, count, HD), jnp.bfloat16),
            jax.ShapeDtypeStruct((1, 2 * KVD), jnp.float32),
        ],
        compiler_params=pltpu.CompilerParams(vmem_limit_bytes=VMEM),
        cost_estimate=SMALL_COST,
        name="turn_dkv",
    )(ids, dkv, cosine, sine)


def kv_grad_body(
    blk_count, rows, small_count, self_ref, cross_ref, core_ref, dq_ref, one_ref, own_ref, near_x_ref,
    core_x_ref, strip_ref, gain_two_ref, bias_q_ref, bias_kv_ref, grad_ref, here_ref, there_ref,
):
    count = self_ref.shape[0]
    strip_q = strip_ref.shape[1] - HD
    parts = (self_ref[...], core_ref[0], cross_ref[0], core_ref[1])
    near = jnp.concatenate(parts, axis=0)
    grad = tn(one_ref[...], near)
    gain_one = jnp.zeros((1, D), jnp.float32)
    for d in range(4):
        x = (own_ref[...], core_x_ref[0], near_x_ref[...], core_x_ref[1])[d][:, :D].astype(jnp.float32)
        root = lax.rsqrt(jnp.mean(x * x, axis=1, keepdims=True) + NORM_EPS)
        hone = nt(dq_ref[count * d : count * (d + 1)], strip_ref[:, :strip_q])
        hone = hone + nt(parts[d], strip_ref[:, strip_q:])
        gain_one = gain_one + jnp.sum(hone * x * root, axis=0, keepdims=True)
        out_ref = (here_ref, there_ref)[d % 2]
        out_ref[count * (d // 2) : count * (d // 2 + 1)] = hone.astype(jnp.bfloat16)
    vector = jnp.concatenate([gain_one, gain_two_ref[...], bias_q_ref[...], bias_kv_ref[...]], axis=1)
    extra = grad_ref.shape[1] - rows
    for b in range(blk_count):
        grad_ref[b, :rows] = grad[rows * b : rows * (b + 1)].astype(jnp.bfloat16)
        lines = []
        for line in range(extra):
            size = min(HD, max(small_count - line * HD, 0))
            begin = small_count * b + line * HD
            pieces = [vector[:, begin : begin + size]] if size > 0 else []
            if size < HD:
                pieces.append(jnp.zeros((1, HD - size), jnp.float32))
            lines.append(pieces[0] if len(pieces) == 1 else jnp.concatenate(pieces, axis=1))
        grad_ref[b, rows:] = jnp.concatenate(lines, axis=0).astype(jnp.bfloat16)


def kv_grad_rows(rows, small_count):
    needed = rows + -(-small_count // HD)
    return needed + -needed % 16


def make_kv_grad(blk_count, rows, small_count, own, cross, core, dq, one, x_own, x_cross, x_core, strip, gain_two, bias_q, bias_kv):
    count = own.shape[0]
    height = kv_grad_rows(rows, small_count)
    return pl.pallas_call(
        functools.partial(kv_grad_body, blk_count, rows, small_count),
        in_specs=[pl.BlockSpec(memory_space=pltpu.VMEM)] * 12,
        out_specs=[pl.BlockSpec(memory_space=pltpu.VMEM)] * 3,
        out_shape=[
            jax.ShapeDtypeStruct((blk_count, height, HD), jnp.bfloat16),
            jax.ShapeDtypeStruct((2 * count, D), jnp.bfloat16),
            jax.ShapeDtypeStruct((2 * count, D), jnp.bfloat16),
        ],
        compiler_params=pltpu.CompilerParams(vmem_limit_bytes=VMEM),
        cost_estimate=SMALL_COST,
        name="kv_grad",
    )(own, cross, core, dq, one, x_own, x_cross, x_core, strip, gain_two, bias_q, bias_kv)


CORE = [(0, 1), (1, 0), (2, 3), (3, 2)]
CROSS = [(0, 2), (2, 0), (1, 3), (3, 1)]
DIAG = [(0, 3), (3, 0), (1, 2), (2, 1)]


def low(values):
    return values.astype(jnp.bfloat16)


def wide(values):
    return values.astype(jnp.float32)


def swap_core(values):
    return lax.ppermute(values, "grp", CORE)


def swap_cross(values):
    return lax.ppermute(values, "grp", CROSS)


def swap_diag(values):
    return lax.ppermute(values, "grp", DIAG)


def swap_blk(values, bit):
    count = lax.axis_size("blk")
    return lax.ppermute(values, "blk", [(i, i ^ bit) for i in range(count)])


def blk_bit(bit):
    return (lax.axis_index("blk") & bit) != 0


def bits_of(count):
    out = []
    bit = count // 2
    while bit >= 1:
        out.append(bit)
        bit //= 2
    return out


def gather_bits(values, order):
    done = []
    for bit in order:
        other = swap_blk(values, bit)
        mine = blk_bit(bit)
        axis = sum(1 for d in done if d > bit)
        values = jnp.stack(
            [jnp.where(mine, other, values), jnp.where(mine, values, other)], axis=axis
        )
        done.append(bit)
    return values


def scatter_bits(values, axes, order):
    axes = list(axes)
    for bit in order:
        axis = axes.index(bit)
        mine = blk_bit(bit).astype(jnp.int32)
        keep = lax.dynamic_index_in_dim(values, mine, axis, keepdims=False)
        send = lax.dynamic_index_in_dim(values, 1 - mine, axis, keepdims=False)
        values = low(wide(keep) + wide(swap_blk(send, bit)))
        axes.remove(bit)
    return values


def by_place(parts):
    grp = lax.axis_index("grp")
    core = (grp & 1) != 0
    cross = (grp & 2) != 0
    a, b, c, d = parts
    a, b = jnp.where(core, b, a), jnp.where(core, a, b)
    c, d = jnp.where(core, d, c), jnp.where(core, c, d)
    a, c = jnp.where(cross, c, a), jnp.where(cross, a, c)
    b, d = jnp.where(cross, d, b), jnp.where(cross, b, d)
    return [a, b, c, d]


def gather_near(values):
    cross = swap_cross(values)
    both = swap_core(jnp.stack([values, cross]))
    return [values, both[0], cross, both[1]]


def gather_grp(values):
    return by_place(gather_near(values))


def gather_tokens(values, bit):
    half = values.shape[0] // 2
    cross = swap_cross(values)
    over = swap_blk(values, bit)
    first = swap_blk(cross[:half], bit)
    second = swap_cross(over[half:])
    chip = jnp.concatenate([values, cross, over, first, second])
    return jnp.concatenate([chip, swap_core(chip)])


def angles_of(position):
    half = HD // 2
    freqs = ROPE_BASE ** (-2.0 * jnp.arange(half, dtype=jnp.float32) / HD)
    return position.astype(jnp.float32)[:, None] * freqs[None, :]


def rotate_by(values, cosine, sine):
    half = HD // 2
    first_half = values[..., :half]
    second_half = values[..., half:]
    return jnp.concatenate(
        [first_half * cosine - second_half * sine, second_half * cosine + first_half * sine],
        axis=-1,
    )


def after(values, anchor):
    return lax.optimization_barrier((values, anchor))[0]


def gather_step(values, done, bit):
    other = swap_blk(values, bit)
    mine = blk_bit(bit)
    axis = sum(1 for d in done if d > bit)
    return jnp.stack(
        [jnp.where(mine, other, values), jnp.where(mine, values, other)], axis=axis
    )


def gather_near_stacked(values):
    both = jnp.stack([values, swap_cross(values)])
    return [both, swap_core(both)]


def ring_groups(count):
    return [[g * count + b for b in ring_order(count)] for g in range(4)]


def gather_ring(values):
    count = lax.axis_size("blk")
    return lax.all_gather(values, ("grp", "blk"), axis=0, axis_index_groups=ring_groups(count))


def exchange_near(parts):
    cross = swap_cross(jnp.stack([parts[2], parts[3]]))
    core = swap_core(jnp.stack([parts[1], cross[1]]))
    return [parts[0], core[0], cross[0], core[1]]


def on_device(
    tokens,
    cotangent,
    segment_ids,
    position_ids,
    w_attend,
    w_out,
    w_gate,
    w_up,
    w_down,
    small_params,
    first_attend,
    first_out,
    first_gate,
    first_up,
    first_down,
    first_small,
    second_attend,
    second_out,
    second_gate,
    second_up,
    second_down,
    second_small,
):
    rows_here, block_len = tokens.shape[:2]
    blk_count = lax.axis_size("blk")
    seq_len = block_len * blk_count
    token_count = rows_here * block_len
    grp = lax.axis_index("grp")
    blk = lax.axis_index("blk")
    cross_id, core_id = grp // 2, grp % 2
    strip_heads = H // 4
    strip_q = strip_heads * HD
    bits = bits_of(blk_count)
    team = blk_count // 4
    lows = [bit for bit in bits if bit < team]
    spread = [bits[0]] + lows
    low_shape = (2,) * len(lows)
    in_team = blk_bit(team).astype(jnp.int32)
    weight_rows = w_gate.shape[0]
    ff_block = w_down.shape[0]
    quarter = ff_block // 4
    widths = [size * blk_count // 2 for at, size in halves_of(quarter)]
    chip_rows = 4 * token_count
    half = token_count // 2

    ids = jnp.stack([grp, in_team])
    flat_low = tokens.reshape(token_count, D)
    dy_low = cotangent.reshape(token_count, D)
    positions = position_ids.reshape(token_count)
    kv_at = HQD + HD * cross_id + KVD * core_id
    strip_local = low(
        jnp.concatenate(
            [
                lax.dynamic_slice_in_dim(w_attend, strip_q * grp, strip_q, 1),
                lax.dynamic_slice_in_dim(w_attend, kv_at, HD, 1),
            ],
            axis=1,
        )
    )
    small_count = small_params.shape[0]
    small_send = jnp.concatenate([low(small_params), low(segment_ids.reshape(token_count))])
    strip_wide = strip_q + HD
    small_send = jnp.pad(small_send, (0, -small_send.shape[0] % (16 * strip_wide)))
    strip_local = jnp.concatenate([strip_local, small_send.reshape(-1, strip_wide)])
    ring = ring_order(blk_count)
    strip_ring = gather_ring(strip_local)
    small_ring = strip_ring[:, weight_rows:].reshape(blk_count, -1)[:, small_count : small_count + token_count]
    small_all = jnp.stack([small_ring[ring.index(b)] for b in range(blk_count)])
    digits = low(jnp.stack([positions // 64, positions % 64], axis=1))
    digits = jnp.pad(digits, ((0, 0), (0, HD - 2)))
    token_send = jnp.concatenate([flat_low, digits], axis=1)
    picked_a, picked_b = pick_columns(ids, w_gate, w_up, blk_count)
    got_a = swap_blk(picked_a[1], team)
    dy_cross = swap_cross(after(dy_low, picked_a))
    dy_over = swap_blk(after(dy_low, strip_ring), team)
    token_cross = after(swap_cross(token_send), (picked_a, strip_ring, got_a, dy_cross))

    def place(values, other, done, bit, lead=0):
        mine = blk_bit(bit)
        axis = lead + sum(1 for d in done if d > bit)
        return jnp.stack(
            [jnp.where(mine, other, values), jnp.where(mine, values, other)], axis=axis
        )

    mine_team = blk_bit(team)
    (low_first, size_first), (low_second, size_second) = halves_of(quarter)

    def team_pair(mine, got):
        return jnp.stack(
            [jnp.where(mine_team, got, mine), jnp.where(mine_team, mine, got)], axis=1
        )

    out_local = low(lax.dynamic_slice_in_dim(w_out, strip_q * grp, strip_q, 1))
    out_ring = gather_ring(after(out_local, strip_ring))
    down_here = low(lax.dynamic_slice_in_dim(w_down, quarter * grp, quarter, 0))
    token_core = swap_core(jnp.stack([token_send, token_cross]))
    freqs = ROPE_BASE ** (-2.0 * jnp.arange(HD // 2, dtype=jnp.float32) / HD)
    freqs = jnp.concatenate([freqs, freqs])[None]
    mixed_own, mixed_core, mixed_far, near_one, strip, vector = mix(
        ids, token_send, token_cross, token_core, strip_ring, freqs, blk_count, weight_rows, small_count
    )
    vector = vector[0]
    gain_one = vector[:D]
    gain_two = vector[D : 2 * D]
    seg_all = small_all.astype(jnp.int32)
    seg_all = seg_all.reshape(blk_count, rows_here, block_len)
    seg_key = jnp.broadcast_to(
        seg_all.transpose(1, 0, 2).reshape(rows_here, seq_len)[:, :, None], (rows_here, seq_len, HD)
    )
    seg_query = jnp.broadcast_to(segment_ids[:, None, :], (rows_here, 8, block_len))
    first_blk = jnp.sum((seg_all[:, :, -1] < segment_ids[None, :, 0]).astype(jnp.int32), axis=0)
    attend_ids = jnp.concatenate([blk[None], first_blk])

    mixed_cross = swap_cross(mixed_far)
    mixed_core = swap_core(jnp.stack([mixed_core, mixed_cross[1]]))
    pair_a = team_pair(picked_a[0], after(got_a, mixed_own))
    pair_a_got = swap_blk(pair_a, bits[0])
    mixed_core = after(mixed_core, (pair_a_got, dy_over))
    down_got = swap_blk(after(down_here, mixed_own), bits[0])
    query, packed_kv = pack(ids, mixed_own, mixed_cross, mixed_core)
    key_value = packed_kv.reshape(rows_here, block_len, 2 * KVD)
    kv_all = gather_ring(key_value)

    teams = [
        [g * blk_count + (i | t) for g in range(4) for t in (0, team)]
        for i in range(blk_count)
        if not i & team
    ]
    order = jnp.stack(
        [
            (grp ^ (2 * (i & 1) + (i >> 2))) * 2 + (in_team ^ ((i >> 1) & 1))
            for i in range(8)
        ]
    )

    peers = [[i for i in range(blk_count) if (i & team) == t] for t in (0, team)]

    def lows_of(values, done, lead=0, anchor=None):
        for bit in lows:
            got = swap_blk(values, bit)
            if anchor is not None:
                got = after(got, anchor)
            values = place(values, got, done, bit, lead)
            done = done + [bit]
        return values

    got_b = swap_blk(after(picked_b[1], mixed_own), team)
    pair_a = place(pair_a, after(pair_a_got, packed_kv), [team], bits[0], 1)
    pair_y_got = swap_blk(pair_a, lows[0])
    got_b, down_got = after((got_b, down_got), kv_all)
    kv_all = after(kv_all, (got_b, down_got, pair_y_got))
    down_here = place(down_here, down_got, [], bits[0])
    down_y_got = swap_blk(down_here, lows[0])
    down_here = place(down_here, down_y_got, [bits[0]], lows[0])
    for n in range(1, len(lows)):
        done = [bits[0]] + lows[:n]
        down_here = place(down_here, swap_blk(down_here, lows[n]), done, lows[n])
    down_here = down_here.reshape(2 * blk_count // 4, quarter, D)
    dy_first = swap_blk(dy_cross[:half], team)
    dy_second = swap_cross(dy_over[half:])
    out_ring = after(out_ring, packed_kv)
    out_strip = jnp.concatenate([out_ring[ring.index(b)] for b in range(blk_count)])
    out_cross = swap_cross(out_strip)
    out_core = swap_core(jnp.stack([out_strip, after(out_cross, kv_all)]))
    out_full = jnp.concatenate(by_place([out_strip, out_core[0], out_cross, out_core[1]]), axis=1)

    att_in, lse = attend(attend_ids, query, kv_all, seg_key, seg_query, block_len)
    pair_b = team_pair(picked_b[0], after(got_b, att_in))
    pair_b_got = swap_blk(pair_b, bits[0])
    flat = wide(flat_low)
    resid = flat + jnp.dot(att_in, out_full, preferred_element_type=jnp.float32)
    h_two = low(norm_apply(resid, gain_two))
    pair_a = place(pair_a, after(pair_y_got, h_two), [bits[0], team], lows[0], 1)
    for i in range(1, len(lows)):
        done = [bits[0], team] + lows[:i]
        pair_a = place(pair_a, swap_blk(pair_a, lows[i]), done, lows[i], 1)
    gate_up_a = pair_a.reshape(2, D, -1)
    pair_b_got = after(pair_b_got, (h_two, down_y_got))
    dy_first, dy_second = after((dy_first, dy_second), pair_b_got)
    dy_chip = jnp.concatenate([dy_low, dy_cross, dy_over, dy_first, dy_second])
    dy_team = jnp.concatenate([dy_chip, swap_core(dy_chip)])
    down_a = down_here[:, :size_first].reshape(widths[0], D)
    down_b = down_here[:, size_first:].reshape(widths[1], D)
    h_team = lax.all_gather(h_two, ("grp", "blk"), axis=0, tiled=True, axis_index_groups=teams)
    pair_b_got = after(pair_b_got, (h_two, gate_up_a))
    pair_b = place(pair_b, pair_b_got, [team], bits[0], 1)
    h_team = after(h_team, (gate_up_a, pair_b, dy_team))
    hidden_a, d_gate_a, d_up_a, *part_a = middle(order, h_team, dy_team, gate_up_a, down_a)
    gate_up_b = lows_of(pair_b, [bits[0], team], 1, hidden_a).reshape(2, D, -1)
    down_grad_a = down_grad(after(hidden_a, gate_up_b), dy_team)
    down_share_a = lax.psum_scatter(
        down_grad_a, "blk", scatter_dimension=0, axis_index_groups=peers, tiled=True
    )
    column_grad_a = two_grads(h_team, d_gate_a, d_up_a)

    def part_sent(values, axis, bit):
        mine = blk_bit(bit).astype(jnp.int32)
        keep = lax.dynamic_index_in_dim(values, mine, axis, keepdims=False)
        send = lax.dynamic_index_in_dim(values, 1 - mine, axis, keepdims=False)
        return keep, swap_blk(send, bit)

    def part_sum(keep, got):
        return low(wide(keep) + wide(got))

    def columns_first(grad):
        grad = grad.reshape((2, 2, 2) + low_shape + (weight_rows, -1))
        return part_sent(grad, 2 + len(lows), lows[-1])

    def columns_mid(keep, got):
        values = part_sum(keep, got)
        for i in range(len(lows) - 2, -1, -1):
            values = part_sum(*part_sent(values, 3 + i, lows[i]))
        return values

    def columns_third(keep, got):
        values = part_sum(keep, got)
        mine = lax.dynamic_index_in_dim(values, in_team, 1, keepdims=False)
        send = lax.dynamic_index_in_dim(values, 1 - in_team, 1, keepdims=False)
        return values, (mine, swap_blk(send, team))

    def rows_second(keep, got):
        values = part_sum(keep, got)
        for i in range(len(lows) - 2, -1, -1):
            values = part_sum(*part_sent(values, 1 + i, lows[i]))
        return part_sent(values, 0, bits[0])

    def columns_last(mine, got):
        return jnp.stack(
            [jnp.where(mine_team, got, mine), jnp.where(mine_team, mine, got)], axis=1
        )

    first_a = columns_first(column_grad_a)
    hidden_b, d_gate_b, d_up_b, d_here, d_there = middle(
        order, after(h_team, (column_grad_a, down_grad_a)), dy_team, gate_up_b, down_b, part_a
    )

    def chip_sum(values, came):
        return low(wide(values) + wide(came))

    def scatter_far(chip):
        far = chip[3 * token_count :]
        return swap_blk(far[:half], team), swap_cross(far[half:])

    def scatter_near(chip, first, second):
        cross, over = (chip[token_count * i : token_count * (i + 1)] for i in (1, 2))
        cross = jnp.concatenate([low(wide(cross[:half]) + wide(first)), cross[half:]])
        over = jnp.concatenate([over[:half], low(wide(over[half:]) + wide(second))])
        return swap_cross(cross), swap_blk(over, team)

    near_att_cross = swap_cross(after(att_in, hidden_a))
    d_there = after(d_there, (first_a[1], down_share_a, near_att_cross))
    d_came = swap_core(d_there)
    down_grad_b = down_grad(hidden_b, dy_team)
    rows_b = part_sent(
        down_grad_b.reshape((2,) + low_shape + (size_second, D)), len(lows), lows[-1]
    )
    mid_a = columns_mid(*after(first_a, d_came))
    second_a = part_sent(mid_a, 1, bits[0])
    d_chip = chip_sum(d_here, after(d_came, down_grad_b))
    d_far = scatter_far(d_chip)
    column_grad_b = two_grads(h_team, *after((d_gate_b, d_up_b), d_chip))
    first_b = columns_first(column_grad_b)
    d_far = after(d_far, column_grad_b)
    d_cross, d_over = scatter_near(d_chip, *d_far)
    out_part, out_there = down(*after((hidden_a, hidden_b), d_far), down_a, down_b, token_count)
    out_came = swap_core(out_there)
    d_cross, d_over = after((d_cross, d_over), out_part)
    d_htwo = wide(d_chip[:token_count]) + wide(d_cross) + wide(d_over)

    norm_value_two, norm_back_two = jax.vjp(norm_apply, resid, gain_two)
    d_resid_norm, grad_gain_two = norm_back_two(d_htwo)
    d_resid = wide(dy_low) + d_resid_norm
    d_att = low(d_resid)
    rows_b = rows_second(*after(rows_b, d_att))

    d_attended = low(right_transposed(d_att, out_full))
    own_angles = angles_of(positions)
    cosine, sine = jnp.cos(own_angles), jnp.sin(own_angles)
    d_query, dkv = attend_back(
        attend_ids,
        query,
        kv_all,
        seg_key,
        seg_query,
        att_in,
        d_attended,
        lse,
        jnp.concatenate([cosine, cosine], axis=1),
        jnp.concatenate([sine, sine], axis=1),
        block_len,
    )
    dkv = lax.psum_scatter(
        dkv.reshape(blk_count * token_count, 2 * KVD),
        ("grp", "blk"),
        scatter_dimension=0,
        axis_index_groups=ring_groups(blk_count),
        tiled=True,
    )
    down_share_b = part_sum(*after(rows_b, d_query))
    sum_a, third_a = columns_third(*after(second_a, d_att))

    def to_strips(parts):
        return jnp.concatenate(exchange_near(by_place(parts)))

    near_dq = to_strips([d_query[:, strip_q * k : strip_q * (k + 1)] for k in range(4)])
    block_shape = (2,) * len(bits) + (weight_rows, -1)
    query_grad = low(left_product(near_one, near_dq)).reshape(block_shape)

    near_att = swap_core(jnp.stack([att_in, near_att_cross]))
    near_att = jnp.concatenate([att_in, near_att[0], near_att_cross, near_att[1]])
    near_datt = to_strips([d_att[:, strip_q * k : strip_q * (k + 1)] for k in range(4)])
    out_grad = low(left_product(near_att, after(near_datt, d_attended))).reshape(block_shape)
    query_out = jnp.concatenate([query_grad, out_grad], axis=-1)
    steps_query = part_sent(query_out, len(bits) - 1, bits[-1])
    second_b = part_sent(columns_mid(*after(first_b, d_query)), 1, bits[0])
    dkv = after(dkv, down_share_b)
    own_part, core_part, far_part, bias_kv = turn_dkv(
        ids, dkv, jnp.concatenate([cosine, cosine], axis=1), jnp.concatenate([sine, sine], axis=1)
    )
    bias_q = jnp.sum(wide(d_query), axis=0)
    d_key = own_part
    cross_part = swap_cross(far_part)
    own_a = columns_last(*after(third_a, own_part))
    core_part = swap_core(jnp.stack([core_part, cross_part[1]]))
    kv_grad, hone_here, hone_there = make_kv_grad(
        blk_count,
        weight_rows,
        small_count,
        own_part,
        cross_part,
        core_part,
        near_dq,
        near_one,
        token_send,
        token_cross,
        token_core,
        strip,
        grad_gain_two[None],
        bias_q[None],
        bias_kv,
    )
    vector_rows = -(-small_count // HD)
    kv_grad = kv_grad.reshape((2,) * len(bits) + kv_grad.shape[1:])
    steps_kv = part_sent(kv_grad, len(bits) - 1, bits[-1])
    share_down = after(jnp.concatenate([down_share_a, down_share_b]), dkv)
    grad_down = lax.all_gather(share_down, "grp", axis=0, tiled=True)
    marks = [hone_there]
    for i in range(len(bits) - 2, -1, -1):
        kv_sum = part_sum(*steps_kv)
        steps_kv = part_sent(kv_sum, i, bits[i])
        marks.append(kv_sum)
    cross_a = swap_cross(after(own_a, marks[-1]))
    for n, i in enumerate(range(len(bits) - 2, -1, -1)):
        steps_query = part_sent(part_sum(*after(steps_query, marks[n + 1])), i, bits[i])
    sum_b, third_b = columns_third(*after(second_b, marks[-1]))
    share_kv_all = wide(steps_kv[0]) + wide(steps_kv[1])
    share_kv = low(share_kv_all[:weight_rows])
    vector_part = share_kv_all[weight_rows : weight_rows + vector_rows]
    share_query_out = part_sum(*after(steps_query, marks[-1]))

    other = wide(swap_core(hone_there))
    d_hone = wide(hone_here[:token_count]) + other[:token_count]
    d_hone_send = low(wide(hone_here[token_count:]) + other[token_count:])
    d_hone_cross = swap_cross(d_hone_send)
    square_sum = square_total(
        [
            wide(s)
            for s in (share_query_out, share_kv, sum_a, sum_b, share_down)
        ]
    )
    packed = jnp.concatenate([vector_part, jnp.full((8, HD), square_sum)])
    packed = after(packed, (d_hone_send, d_hone))
    packed = packed + swap_cross(packed)
    packed = packed + swap_core(packed)
    share_rest = after(jnp.concatenate([share_query_out, share_kv], axis=1), packed)
    cross_rest = swap_cross(share_rest)
    share_vector = packed[:vector_rows].reshape(-1)[:small_count]
    square_sum = packed[vector_rows:] + jnp.sum(share_vector * share_vector)
    square_sum = after(square_sum, third_b[1])
    for bit in bits:
        square_sum = square_sum + swap_blk(square_sum, bit)
    grad_norm = jnp.sqrt(square_sum[0, 0])
    factor = jnp.minimum(1.0, CLIP_NORM / (grad_norm + 1e-06))
    out_chip = chip_sum(out_part, after(out_came, marks[1]))
    out_far = scatter_far(out_chip)
    factor = after(factor, out_chip)

    new_first_down, new_second_down, new_down = adam_step(
        w_down, factor * wide(grad_down), first_down, second_down, RATE_DOWN, WEIGHT_DECAY
    )
    cross_rest = after(cross_rest, new_down)
    core_rest = swap_core(jnp.stack([share_rest, cross_rest]))
    parts = by_place([share_rest, core_rest[0], cross_rest, core_rest[1]])
    grad_out = jnp.concatenate([part[:, strip_q : 2 * strip_q] for part in parts], axis=1)
    grad_attend = jnp.concatenate(
        [part[:, :strip_q] for part in parts] + [parts[k][:, 2 * strip_q :] for k in (0, 2, 1, 3)],
        axis=1,
    )
    new_first_attend, new_second_attend, new_attend = adam_step(
        w_attend, factor * wide(grad_attend), first_attend, second_attend, RATE_ATTEND, WEIGHT_DECAY
    )
    new_first_out, new_second_out, new_out = adam_step(
        w_out, factor * wide(grad_out), first_out, second_out, RATE_OUT, WEIGHT_DECAY
    )
    near_a = jnp.stack([own_a, after(cross_a, new_down)])
    near_a = [near_a, swap_core(near_a)]
    own_b = columns_last(*third_b)
    cross_b = after(swap_cross(own_b), new_down)
    near_b = jnp.stack([own_b, cross_b])
    near_b = [near_b, swap_core(near_b)]
    new_first_gate, new_second_gate, new_gate = adam_columns(
        0, ids, factor[None], near_a, near_b, w_gate, first_gate, second_gate, blk_count, RATE_GATE, WEIGHT_DECAY
    )
    new_first_up, new_second_up, new_up = adam_columns(
        1, ids, factor[None], near_a, near_b, w_up, first_up, second_up, blk_count, RATE_GATE, WEIGHT_DECAY
    )
    norm_value_one, norm_back_one = jax.vjp(norm_apply, flat, gain_one)
    d_hone = after(d_hone + wide(after(d_hone_cross, new_gate)), new_gate)
    d_flat_norm, unused_gain = norm_back_one(d_hone)
    grad_tokens = low(d_resid + d_flat_norm)

    new_first_small, new_second_small, new_small = adam_step(
        small_params, factor * share_vector, first_small, second_small, RATE_VECTOR, 0.0
    )

    out_near = after(scatter_near(out_chip, *after(out_far, factor)), (new_gate, new_up))
    out_tokens = low(resid + wide(out_chip[:token_count]) + wide(out_near[0]) + wide(out_near[1]))
    return (
        out_tokens.reshape(rows_here, block_len, D),
        grad_tokens.reshape(rows_here, block_len, D),
        grad_norm,
        new_first_attend,
        new_second_attend,
        new_attend,
        new_first_out,
        new_second_out,
        new_out,
        new_first_gate,
        new_second_gate,
        new_gate,
        new_first_up,
        new_second_up,
        new_up,
        new_first_down,
        new_second_down,
        new_down,
        new_first_small,
        new_second_small,
        new_small,
    )


def solution(mesh):
    placed = (
        P("grp", "blk", None),
        P("grp", "blk", None),
        P("grp", "blk"),
        P("grp", "blk"),
        P("blk", None),
        P("blk", None),
        P("blk", None),
        P("blk", None),
        P("blk", None),
        P("blk"),
        P("blk", None),
        P("blk", None),
        P("blk", None),
        P("blk", None),
        P("blk", None),
        P("blk"),
        P("blk", None),
        P("blk", None),
        P("blk", None),
        P("blk", None),
        P("blk", None),
        P("blk"),
    )
    return jax.shard_map(
        on_device,
        mesh=mesh,
        in_specs=placed,
        out_specs=(
            P("grp", "blk", None),
            P("grp", "blk", None),
            P(),
            P("blk", None),
            P("blk", None),
            P("blk", None),
            P("blk", None),
            P("blk", None),
            P("blk", None),
            P("blk", None),
            P("blk", None),
            P("blk", None),
            P("blk", None),
            P("blk", None),
            P("blk", None),
            P("blk", None),
            P("blk", None),
            P("blk", None),
            P("blk"),
            P("blk"),
            P("blk"),
        ),
        check_vma=False,
    )
```
